32 devices in a mesh: experts: 4 (over y, x), context: 2 (over core), dp: 4 (over z).
Axes of the slice: x: 2, y: 2, z: 4, core: 2. Of those that a mesh axis runs over, the one named last changes fastest.
Arguments:
- hidden: bfloat16 [16, 1024, 2048], P(('experts', 'dp'), 'context'), may hold values from -6 to 6
- cotangent: bfloat16 [16, 1024, 2048], P(('experts', 'dp'), 'context'), may hold values from -6 to 6
- segments: int32 [16, 1024], P(('experts', 'dp'), 'context'), may hold values from 0 to 1023, as said below
- padding: int32 [16, 1024], P(('experts', 'dp'), 'context'), may hold values 0 or 1
- routes: int32 [16, 1024, 4], P(('experts', 'dp'), 'context'), may hold values from 0 to 7, all different within a row
- order: int32 [16, 2, 512], P(('experts', 'dp'), 'context'), may hold values from 0 to 511, each once within a row
- norm1_gain: bfloat16 [2048], P('dp'), may hold values from 0.5 to 1.5
- w_query: bfloat16 [2048, 2048], P('dp'), may hold values from -0.125 to 0.125
- w_key: bfloat16 [2048, 2048], P('dp'), may hold values from -0.125 to 0.125
- w_value: bfloat16 [2048, 2048], P('dp'), may hold values from -0.125 to 0.125
- w_out: bfloat16 [2048, 2048], P('dp'), may hold values from -1 to 1
- norm2_gain: bfloat16 [2048], P('dp'), may hold values from 0.5 to 1.5
- router: bfloat16 [2048, 8], P('dp'), may hold values from -0.0625 to 0.0625
- shared_gate_vec: bfloat16 [2048], P('dp'), may hold values from -0.125 to 0.125
- shared_w_gate: bfloat16 [2048, 5632], P('dp', 'experts'), may hold values from -0.125 to 0.125
- shared_w_up: bfloat16 [2048, 5632], P('dp', 'experts'), may hold values from -0.125 to 0.125
- shared_w_down: bfloat16 [5632, 2048], P(('experts', 'dp')), may hold values from -0.15625 to 0.15625
- expert_w_gate: bfloat16 [8, 2048, 1408], P(('experts', 'context'), 'dp'), may hold values from -0.125 to 0.125
- expert_w_up: bfloat16 [8, 2048, 1408], P(('experts', 'context'), 'dp'), may hold values from -0.125 to 0.125
- expert_w_down: bfloat16 [8, 1408, 2048], P(('experts', 'context'), None, 'dp'), may hold values from -0.625 to 0.625
Outputs:
- output: bfloat16 [16, 1024, 2048], P(('experts', 'dp'), 'context')
- input_grad: bfloat16 [16, 1024, 2048], P(('experts', 'dp'), 'context')
- grad_norm1_gain: float32 [2048], P(('experts', 'context', 'dp'))
- grad_w_query: float32 [2048, 2048], P(('experts', 'context', 'dp'))
- grad_w_key: float32 [2048, 2048], P(('experts', 'context', 'dp'))
- grad_w_value: float32 [2048, 2048], P(('experts', 'context', 'dp'))
- grad_w_out: float32 [2048, 2048], P(('experts', 'context', 'dp'))
- grad_norm2_gain: float32 [2048], P(('experts', 'context', 'dp'))
- grad_router: float32 [2048, 8], P(('experts', 'context', 'dp'))
- grad_shared_gate_vec: float32 [2048], P(('experts', 'context', 'dp'))
- grad_shared_w_gate: float32 [2048, 5632], P(('context', 'dp'), 'experts')
- grad_shared_w_up: float32 [2048, 5632], P(('context', 'dp'), 'experts')
- grad_shared_w_down: float32 [5632, 2048], P('experts', ('context', 'dp'))
- grad_expert_w_gate: float32 [8, 2048, 1408], P(('experts', 'context'), 'dp')
- grad_expert_w_up: float32 [8, 2048, 1408], P(('experts', 'context'), 'dp')
- grad_expert_w_down: float32 [8, 1408, 2048], P(('experts', 'context'), None, 'dp')
The draws below stay inside these ranges and needn't reach their ends.
Inputs may be any that keep to these rules, and one draw needn't show every extreme that they name: `segments`: along a sequence segment numbers never fall; the last token of every sequence has number 1024 - 1. `routes`: each token names 4 different experts. `order`: each row is a permutation of the 512 ranks of a block.
All inputs are finite; a program needn't handle non-finite values. No bound on the sum of `padding` on one device may be relied on, other than what follows from the above.
Results may differ from the reference program's by a relative error of at most 0.015.
Values may be sent and summed in bfloat16 or wider, within the bound.
A program may use at most 576 MiB of HBM per device.

```python
from functools import partial
import jax
import jax.numpy as jnp
from jax import lax

D = 2048
HEADS = 16
HEAD_DIM = 128
FF = 1408
SFF = 5632
TOP = 4
SEQ_LEN = 1024
TOK_DEV = 512
BATCH = 16
EXPERTS = 8
CAP = 288
N_CONTEXT = 2


def draw_segments(key, part):
    key = jax.random.fold_in(key, 11)
    key_start, key_stop, key_rate, key_flags = jax.random.split(key, 4)
    begin = jax.random.randint(key_start, (BATCH, 1), 1, TOK_DEV)
    finish = jax.random.randint(key_stop, (BATCH, 1), SEQ_LEN - TOK_DEV + 1, SEQ_LEN)
    spacing = jax.random.randint(key_rate, (BATCH, 1), 3, 48)
    boundary_flags = jax.random.randint(key_flags, (BATCH, SEQ_LEN), 0, 1 << 20) % spacing == 0
    places = jnp.arange(SEQ_LEN, dtype=jnp.int32)[None, :]
    outside = (places < begin) | (places > finish)
    starts = boundary_flags & outside | (places == begin) | (places == finish)
    starts = starts & (places > 0)
    counted = jnp.cumsum(starts.astype(jnp.int32), axis=1).astype(jnp.int32)
    return (counted + (SEQ_LEN - 1 - counted[:, -1:])).astype(jnp.int32)


def place_ends(array, stream_key, least, high):
    index_at = [jax.random.randint(jax.random.fold_in(stream_key, axis), (), 0, length) for axis, length in enumerate(array.shape)]
    main_axis = array.shape.index(max(array.shape))
    beside = index_at[:main_axis] + [(index_at[main_axis] + 1) % array.shape[main_axis]] + index_at[main_axis + 1:]
    return array.at[tuple(index_at)].set(least).at[tuple(beside)].set(high)


def steps_of(rng, shape, pieces, low, high):
    loudness, own = 1.0, jax.random.fold_in(rng, 6)
    for axis_at, blocks in pieces:
        draws = jnp.exp(jax.random.uniform(jax.random.fold_in(own, axis_at), (blocks,), jnp.float32, low / len(pieces), high / len(pieces)))
        loudness = loudness * jnp.repeat(draws, shape[axis_at] // blocks).reshape([-1 if axis == axis_at else 1 for axis in range(len(shape))])
    return loudness


def choose_distinct(own_key, rows, number_of, top, lift):
    ranking = jax.random.permutation(jax.random.fold_in(own_key, 1), number_of)
    pull = ranking
    for power in range(3):
        pull = pull * pull // number_of
    pull = pull * lift // number_of
    chance = jax.random.randint(jax.random.fold_in(own_key, 2), (rows, number_of), 0, 4096) + pull
    holders = jax.random.permutation(jax.random.fold_in(own_key, 3), rows)[jnp.arange(number_of) % rows]
    chance = jnp.where(jnp.arange(rows)[:, None] == holders[None, :], 1 << 14, chance)
    score = chance * number_of + jnp.arange(number_of)
    return lax.top_k(score.astype(jnp.int32), top)[1].astype(jnp.int32)


def bell_draw(rng, extent, scale, limit, shards=(), held_as=jnp.bfloat16):
    entries = scale * jax.random.normal(rng, extent, jnp.float32)
    if shards:
        entries = entries * steps_of(rng, extent, shards, -0.22, 0.18)
    return jnp.clip(entries, -limit, limit).astype(held_as)


def setup_inputs(seed: int = 0) -> dict:
    key_list = jax.random.split(jax.random.key(seed), 21)
    hidden = bell_draw(key_list[0], (BATCH, SEQ_LEN, D), 1.0, 6.0, ((0, 16), (1, 2)))
    cotangent = bell_draw(key_list[1], (BATCH, SEQ_LEN, D), 1.0, 6.0, ((0, 16), (1, 2)))
    segments = draw_segments(jax.random.fold_in(key_list[20], 71), 0)
    padding = place_ends((jax.random.randint(key_list[3], (BATCH, SEQ_LEN), 0, 8) < 7).astype(jnp.int32), jax.random.fold_in(key_list[3], 1), 0, 1)
    routes = choose_distinct(key_list[4], BATCH * SEQ_LEN, EXPERTS, TOP, 4096).reshape((BATCH, SEQ_LEN, TOP))
    order = jax.vmap(lambda own: jax.random.permutation(own, TOK_DEV))(jax.random.split(key_list[5], BATCH * N_CONTEXT)).reshape((BATCH, N_CONTEXT, TOK_DEV)).astype(jnp.int32)
    norm1_gain = jnp.clip(1.0 + 0.1 * jax.random.normal(key_list[6], (D,), jnp.float32), 0.5, 1.5).astype(jnp.bfloat16)
    w_query = bell_draw(key_list[7], (D, D), D ** -0.5, 0.125, ((0, 4),))
    w_key = bell_draw(key_list[8], (D, D), D ** -0.5, 0.125, ((0, 4),))
    w_value = bell_draw(key_list[9], (D, D), D ** -0.5, 0.125, ((0, 4),))
    w_out = bell_draw(key_list[10], (D, D), (D // 64) ** -0.5, 1.0, ((0, 4),))
    norm2_gain = jnp.clip(1.0 + 0.1 * jax.random.normal(key_list[11], (D,), jnp.float32), 0.5, 1.5).astype(jnp.bfloat16)
    router = bell_draw(key_list[12], (D, EXPERTS), (4 * D) ** -0.5, 0.0625, ((0, 4),))
    shared_gate_vec = bell_draw(key_list[13], (D,), D ** -0.5, 0.125, ((0, 4),))
    shared_w_gate = bell_draw(key_list[14], (D, SFF), D ** -0.5, 0.125, ((0, 4), (1, 4)))
    shared_w_up = bell_draw(key_list[15], (D, SFF), D ** -0.5, 0.125, ((0, 4), (1, 4)))
    shared_w_down = bell_draw(key_list[16], (SFF, D), (SFF // 4) ** -0.5, 0.15625, ((0, 16),))
    expert_w_gate = bell_draw(key_list[17], (EXPERTS, D, FF), D ** -0.5, 0.125, ((0, 8), (1, 4)))
    expert_w_up = bell_draw(key_list[18], (EXPERTS, D, FF), D ** -0.5, 0.125, ((0, 8), (1, 4)))
    expert_w_down = bell_draw(key_list[19], (EXPERTS, FF, D), (max(1, FF * 4 // (EXPERTS * EXPERTS))) ** -0.5, 0.625, ((0, 8), (2, 4)))
    return dict(hidden=hidden, cotangent=cotangent, segments=segments, padding=padding, routes=routes, order=order, norm1_gain=norm1_gain, w_query=w_query, w_key=w_key, w_value=w_value, w_out=w_out, norm2_gain=norm2_gain, router=router, shared_gate_vec=shared_gate_vec, shared_w_gate=shared_w_gate, shared_w_up=shared_w_up, shared_w_down=shared_w_down, expert_w_gate=expert_w_gate, expert_w_up=expert_w_up, expert_w_down=expert_w_down)


EPS = 1e-06
NEG = -1e+30
HIGH = lax.Precision.HIGHEST

@jax.custom_vjp
def low(v):
    return lax.optimization_barrier(v.astype(jnp.bfloat16)).astype(jnp.float32)

@jax.custom_vjp
def low_back(v):
    return v

def low_keep(v):
    return (low(v), None)

def low_pass(kept, grad):
    return (grad,)

def back_keep(v):
    return (v, None)

def back_low(kept, grad):
    return (low(grad),)
low.defvjp(low_keep, low_pass)
low_back.defvjp(back_keep, back_low)

def matmul(left, right):
    return jnp.dot(left, right, precision=HIGH)

def rms_norm(values_in, gain_vec):
    return values_in * lax.rsqrt(lax.optimization_barrier(jnp.mean(values_in * values_in, axis=-1, keepdims=True)) + EPS) * gain_vec

def block_slots(route_row, priority, expert_count):
    matches = (route_row[:, None] == jnp.arange(expert_count, dtype=jnp.int32)[None, :]).astype(jnp.int32)
    ordered = jnp.zeros_like(matches).at[priority].set(matches)
    before = jnp.cumsum(ordered, axis=0) - ordered
    return lax.optimization_barrier(jnp.sum(before[priority] * matches, axis=1)).astype(jnp.int32)

def fill_slots(source_rows, target, kept_rows):
    empty_slots = jnp.zeros((EXPERTS * CAP, D), dtype=source_rows.dtype)
    return empty_slots.at[target].add(jnp.where(kept_rows[:, None], source_rows, 0.0))

def take_rows(table_rows, target):
    return table_rows[target]

def one_head(packed, allowed):
    query_h, key_h, value_h = packed
    raw_scores = low_back(matmul(query_h, key_h.T))
    logits = jnp.where(allowed, raw_scores * HEAD_DIM ** (-0.5), NEG)
    exp_scores = jnp.exp(logits - lax.optimization_barrier(jnp.max(logits, axis=1, keepdims=True)))
    attn_probs = exp_scores / lax.optimization_barrier(jnp.sum(exp_scores, axis=1, keepdims=True))
    return matmul(low(attn_probs), value_h)

def sequence_forward(params, packed):
    hidden_seq, segment_seq, padding_seq, route_seq, order_seq = packed
    gain_one, query_w, key_w, value_w, out_w, gain_two, router_w, gate_vec, sh_gate, sh_up, sh_down, ex_gate, ex_up, ex_down = params
    normed_one = low(rms_norm(hidden_seq, gain_one))
    queries = low_back(low(matmul(normed_one, query_w)))
    keys_seq = low_back(low(matmul(normed_one, key_w)))
    values_seq = low_back(low(matmul(normed_one, value_w)))
    places = jnp.arange(SEQ_LEN, dtype=jnp.int32)
    allowed = (places[None, :] <= places[:, None]) & (segment_seq[None, :] == segment_seq[:, None]) & ((padding_seq[None, :] > 0) | (places[None, :] == places[:, None]))
    head_q = queries.reshape(SEQ_LEN, HEADS, HEAD_DIM).transpose(1, 0, 2)
    head_k = keys_seq.reshape(SEQ_LEN, HEADS, HEAD_DIM).transpose(1, 0, 2)
    head_v = values_seq.reshape(SEQ_LEN, HEADS, HEAD_DIM).transpose(1, 0, 2)
    attended = lax.map(jax.checkpoint(partial(one_head, allowed=allowed)), (head_q, head_k, head_v))
    attended = low_back(low(attended.transpose(1, 0, 2).reshape(SEQ_LEN, D)))
    residual = hidden_seq + low_back(matmul(attended, out_w))
    normed_two = low(rms_norm(residual, gain_two))
    router_logits = low_back(matmul(normed_two, router_w))
    router_exp = jnp.exp(router_logits - lax.optimization_barrier(jnp.max(router_logits, axis=1, keepdims=True)))
    router_probs = router_exp / lax.optimization_barrier(jnp.sum(router_exp, axis=1, keepdims=True))
    route_gates = jnp.take_along_axis(router_probs, route_seq, axis=1)
    shared_gate = jax.nn.sigmoid(low_back(matmul(normed_two, gate_vec)))
    gate_pre = low_back(matmul(normed_two, sh_gate))
    up_pre = low_back(matmul(normed_two, sh_up))
    shared_hidden = low(gate_pre * jax.nn.sigmoid(gate_pre) * up_pre)
    shared_out = low_back(matmul(shared_hidden, sh_down))
    priority = (order_seq[:, :, None] * TOP + jnp.arange(TOP, dtype=jnp.int32)[None, None, :]).reshape(N_CONTEXT, TOK_DEV * TOP)
    block_routes = route_seq.reshape(N_CONTEXT, TOK_DEV * TOP)
    slot_index = jax.vmap(partial(block_slots, expert_count=EXPERTS))(block_routes, priority)
    kept_rows = slot_index < CAP
    target = block_routes * CAP + jnp.minimum(slot_index, CAP - 1)
    source_rows = jnp.repeat(normed_two.reshape(N_CONTEXT, TOK_DEV, D), TOP, axis=1)
    buffers = low_back(jax.vmap(fill_slots)(source_rows, target, kept_rows))
    expert_rows = buffers.reshape(N_CONTEXT, EXPERTS, CAP, D).transpose(1, 0, 2, 3).reshape(EXPERTS, N_CONTEXT * CAP, D)
    gate_e = low_back(jnp.einsum('erd,edf->erf', expert_rows, ex_gate, precision=HIGH))
    up_e = low_back(jnp.einsum('erd,edf->erf', expert_rows, ex_up, precision=HIGH))
    hidden_e = low(gate_e * jax.nn.sigmoid(gate_e) * up_e)
    result_e = low(low_back(jnp.einsum('erf,efd->erd', hidden_e, ex_down, precision=HIGH)))
    result_blocks = result_e.reshape(EXPERTS, N_CONTEXT, CAP, D).transpose(1, 0, 2, 3).reshape(N_CONTEXT, EXPERTS * CAP, D)
    picked = jax.vmap(take_rows)(result_blocks, target)
    picked = jnp.where(kept_rows[:, :, None], picked, 0.0)
    weighted = picked * route_gates.reshape(N_CONTEXT, TOK_DEV * TOP)[:, :, None]
    routed = lax.optimization_barrier(jnp.sum(weighted.reshape(SEQ_LEN, TOP, D), axis=1))
    return residual + shared_gate[:, None] * shared_out + routed

def reference(hidden, cotangent, segments, padding, routes, order, norm1_gain, w_query, w_key, w_value, w_out, norm2_gain, router, shared_gate_vec, shared_w_gate, shared_w_up, shared_w_down, expert_w_gate, expert_w_up, expert_w_down):
    params = tuple((weight_arr.astype(jnp.float32) for weight_arr in (norm1_gain, w_query, w_key, w_value, w_out, norm2_gain, router, shared_gate_vec, shared_w_gate, shared_w_up, shared_w_down, expert_w_gate, expert_w_up, expert_w_down)))

    def forward(params_in, hidden_in):
        return lax.map(jax.checkpoint(partial(sequence_forward, params_in)), (hidden_in, segments, padding, routes, order))
    result, pullback = jax.vjp(forward, params, hidden.astype(jnp.float32))
    weight_grads, input_grad = pullback(cotangent.astype(jnp.float32))
    return (result.astype(jnp.bfloat16), input_grad.astype(jnp.bfloat16), weight_grads[0], weight_grads[1], weight_grads[2], weight_grads[3], weight_grads[4], weight_grads[5], weight_grads[6], weight_grads[7], weight_grads[8], weight_grads[9], weight_grads[10], weight_grads[11], weight_grads[12], weight_grads[13])
```

```python
from functools import partial

import jax
import jax.numpy as jnp
from jax import lax
from jax.experimental import pallas as pl
from jax.experimental.pallas import tpu as pltpu
from jax.sharding import PartitionSpec as P

HEADS = 16
HEAD_DIM = 128
TOP = 4


EPS = 1e-06
NEG = -1e30


def silu_grad(pre_act):
    logistic = jax.nn.sigmoid(pre_act)
    return logistic * (1.0 + pre_act * (1.0 - logistic))


def block_slots(route_row, priority, expert_count):
    matches = (route_row[:, None] == jnp.arange(expert_count, dtype=jnp.int32)[None, :]).astype(
        jnp.int32
    )
    ordered = jnp.zeros_like(matches).at[priority].set(matches)
    before = jnp.cumsum(ordered, axis=0) - ordered
    return jnp.sum(before[priority] * matches, axis=1)


def norm_back(values_in, inv_rms, gain_vec, gradient):
    weighted = gradient * gain_vec
    inner_sum = jnp.mean(weighted * values_in, axis=1, keepdims=True)
    d_value = inv_rms * weighted - values_in * inv_rms**3 * inner_sum
    d_gain = jnp.sum(gradient * values_in * inv_rms, axis=0)
    return (d_value, d_gain)


def attend_head(packed, allowed, scale_factor):
    query_h, key_h, value_h = packed
    raw_scores = jnp.einsum("th,lh->tl", query_h, key_h, preferred_element_type=jnp.float32)
    logits = jnp.where(allowed, raw_scores * scale_factor, NEG)
    row_max = jnp.max(logits, axis=1, keepdims=True)
    exp_scores = jnp.exp(logits - row_max)
    row_total = jnp.sum(exp_scores, axis=1, keepdims=True)
    attn_probs = (exp_scores / row_total).astype(jnp.bfloat16)
    head_out = jnp.dot(attn_probs, value_h, preferred_element_type=jnp.float32).astype(jnp.bfloat16)
    return (head_out, row_max + jnp.log(row_total))


def attend_back(packed, allowed, scale_factor):
    query_h, key_h, value_h, out_grad, log_total = packed
    raw_scores = jnp.einsum("th,lh->tl", query_h, key_h, preferred_element_type=jnp.float32)
    logits = jnp.where(allowed, raw_scores * scale_factor, NEG)
    attn_probs = jnp.exp(logits - log_total)
    prob_grad = jnp.einsum("th,lh->tl", out_grad, value_h, preferred_element_type=jnp.float32)
    inner_sum = jnp.sum(attn_probs * prob_grad, axis=1, keepdims=True)
    score_grad = (attn_probs * (prob_grad - inner_sum) * scale_factor).astype(jnp.bfloat16)
    query_grad = jnp.dot(score_grad, key_h, preferred_element_type=jnp.float32)
    key_grad = jnp.einsum("tl,th->lh", score_grad, query_h, preferred_element_type=jnp.float32)
    value_grad = jnp.einsum(
        "tl,th->lh", attn_probs.astype(jnp.bfloat16), out_grad, preferred_element_type=jnp.float32
    )
    return (query_grad, key_grad, value_grad)


def local_general(
    hidden,
    cotangent,
    segments,
    padding,
    routes,
    order,
    norm1_gain,
    w_query,
    w_key,
    w_value,
    w_out,
    norm2_gain,
    router,
    shared_gate_vec,
    shared_w_gate,
    shared_w_up,
    shared_w_down,
    expert_w_gate,
    expert_w_up,
    expert_w_down,
):
    fetched = (
        lax.all_gather(norm1_gain, "dp", axis=0, tiled=True),
        lax.all_gather(w_query, "dp", axis=0, tiled=True),
        lax.all_gather(w_key, "dp", axis=0, tiled=True),
        lax.all_gather(w_value, "dp", axis=0, tiled=True),
        lax.all_gather(w_out, "dp", axis=0, tiled=True),
        lax.all_gather(norm2_gain, "dp", axis=0, tiled=True),
        lax.all_gather(router, "dp", axis=0, tiled=True),
        lax.all_gather(shared_gate_vec, "dp", axis=0, tiled=True),
        lax.all_gather(shared_w_gate, "dp", axis=0, tiled=True),
        lax.all_gather(shared_w_up, "dp", axis=0, tiled=True),
        lax.all_gather(shared_w_down, "dp", axis=0, tiled=True),
        lax.all_gather(expert_w_gate, "dp", axis=1, tiled=True),
        lax.all_gather(expert_w_up, "dp", axis=1, tiled=True),
        lax.all_gather(expert_w_down, "dp", axis=2, tiled=True),
    )
    (
        gain_one,
        query_w,
        key_w,
        value_w,
        out_w,
        gain_two,
        router_full,
        gate_vec,
        sh_gate,
        sh_up,
        sh_down,
        ex_gate,
        ex_up,
        ex_down,
    ) = fetched
    sh_gate, sh_up, sh_down = (
        lax.all_gather(sh_gate, "experts", axis=1, tiled=True),
        lax.all_gather(sh_up, "experts", axis=1, tiled=True),
        lax.all_gather(sh_down, "experts", axis=0, tiled=True),
    )
    tokens_here = hidden.shape[1]
    model_width = hidden.shape[2]
    x_rows = hidden[0].astype(jnp.float32)
    cot_rows = cotangent[0].astype(jnp.float32)
    inv_one = lax.rsqrt(jnp.mean(x_rows * x_rows, axis=1, keepdims=True) + EPS)
    g_one = gain_one.astype(jnp.float32)
    normed_one = (x_rows * inv_one * g_one).astype(jnp.bfloat16)
    queries = jnp.dot(normed_one, query_w, preferred_element_type=jnp.float32).astype(jnp.bfloat16)
    keys_own = jnp.dot(normed_one, key_w, preferred_element_type=jnp.float32).astype(jnp.bfloat16)
    values_own = jnp.dot(normed_one, value_w, preferred_element_type=jnp.float32).astype(
        jnp.bfloat16
    )
    own_codes = jnp.where(padding[0] > 0, segments[0] + 1, 0)
    code_parts = jnp.stack([own_codes // 64, own_codes % 64]).astype(jnp.bfloat16)
    keys_all, values_all, parts_all = (
        lax.all_gather(keys_own, "context", axis=0, tiled=True),
        lax.all_gather(values_own, "context", axis=0, tiled=True),
        lax.all_gather(code_parts, "context", axis=1, tiled=True),
    )
    key_codes = parts_all[0].astype(jnp.int32) * 64 + parts_all[1].astype(jnp.int32)
    seq_total = keys_all.shape[0]
    query_pos = lax.axis_index("context") * tokens_here + jnp.arange(tokens_here, dtype=jnp.int32)
    key_pos = jnp.arange(seq_total, dtype=jnp.int32)
    same_doc = key_codes[None, :] == (segments[0] + 1)[:, None]
    allowed = (key_pos[None, :] <= query_pos[:, None]) & (
        same_doc | (key_pos[None, :] == query_pos[:, None])
    )
    scale_factor = HEAD_DIM ** (-0.5)

    def to_heads(rows_in):
        return rows_in.reshape(rows_in.shape[0], HEADS, HEAD_DIM).transpose(1, 0, 2)

    def from_heads(heads_in):
        return heads_in.transpose(1, 0, 2).reshape(heads_in.shape[1], model_width)

    head_q = to_heads(queries)
    head_k = to_heads(keys_all)
    head_v = to_heads(values_all)
    head_out, log_total = lax.map(
        partial(attend_head, allowed=allowed, scale_factor=scale_factor), (head_q, head_k, head_v)
    )
    attended = from_heads(head_out)
    residual = x_rows + jnp.dot(attended, out_w, preferred_element_type=jnp.float32)
    inv_two = lax.rsqrt(jnp.mean(residual * residual, axis=1, keepdims=True) + EPS)
    g_two = gain_two.astype(jnp.float32)
    normed_two = (residual * inv_two * g_two).astype(jnp.bfloat16)
    router_logits = jnp.dot(normed_two, router_full, preferred_element_type=jnp.float32)
    router_exp = jnp.exp(router_logits - jnp.max(router_logits, axis=1, keepdims=True))
    router_probs = router_exp / jnp.sum(router_exp, axis=1, keepdims=True)
    route_gates = jnp.take_along_axis(router_probs, routes[0], axis=1)
    shared_gate = jax.nn.sigmoid(jnp.dot(normed_two, gate_vec, preferred_element_type=jnp.float32))
    shared_scaled = (shared_gate[:, None] * cot_rows).astype(jnp.bfloat16)
    rows_group, grads_group = (normed_two, shared_scaled)
    gate_pre = jnp.dot(rows_group, sh_gate, preferred_element_type=jnp.float32)
    up_pre = jnp.dot(rows_group, sh_up, preferred_element_type=jnp.float32)
    gate_act = gate_pre * jax.nn.sigmoid(gate_pre)
    shared_hidden = (gate_act * up_pre).astype(jnp.bfloat16)
    shared_part = jnp.dot(shared_hidden, sh_down, preferred_element_type=jnp.float32)
    experts_all = router_full.shape[1]
    capacity = (9 * tokens_here * TOP + 8 * experts_all - 1) // (8 * experts_all)
    priority = (order[0, 0][:, None] * TOP + jnp.arange(TOP, dtype=jnp.int32)[None, :]).reshape(-1)
    flat_routes = routes[0].reshape(-1)
    slot_index = block_slots(flat_routes, priority, experts_all)
    kept_rows = slot_index < capacity
    target = flat_routes * capacity + jnp.minimum(slot_index, capacity - 1)
    row_gates = route_gates.reshape(-1)
    cot_repeated = jnp.repeat(cot_rows, TOP, axis=0)
    source_rows = jnp.repeat(normed_two, TOP, axis=0)
    source_grads = (cot_repeated * row_gates[:, None]).astype(jnp.bfloat16)
    empty_slots = jnp.zeros((experts_all * capacity, model_width), jnp.bfloat16)
    send_rows = empty_slots.at[target].add(
        jnp.where(kept_rows[:, None], source_rows, jnp.zeros_like(source_rows))
    )
    send_grads = empty_slots.at[target].add(
        jnp.where(kept_rows[:, None], source_grads, jnp.zeros_like(source_grads))
    )
    recv_rows, recv_grads = (
        lax.all_to_all(
            send_rows.reshape(experts_all, capacity, model_width),
            ("experts", "context"),
            split_axis=0,
            concat_axis=0,
            tiled=True,
        ),
        lax.all_to_all(
            send_grads.reshape(experts_all, capacity, model_width),
            ("experts", "context"),
            split_axis=0,
            concat_axis=0,
            tiled=True,
        ),
    )
    local_count = ex_gate.shape[0]
    sources = experts_all // local_count

    def to_local(buffer_in):
        return (
            buffer_in.reshape(sources, local_count, capacity, model_width)
            .transpose(1, 0, 2, 3)
            .reshape(local_count, sources * capacity, model_width)
        )

    def to_owner(buffer_in):
        return (
            buffer_in.reshape(local_count, sources, capacity, model_width)
            .transpose(1, 0, 2, 3)
            .reshape(experts_all, capacity, model_width)
        )

    expert_rows = to_local(recv_rows)
    expert_grads_in = to_local(recv_grads)
    gate_e = jnp.einsum("erd,edf->erf", expert_rows, ex_gate, preferred_element_type=jnp.float32)
    up_e = jnp.einsum("erd,edf->erf", expert_rows, ex_up, preferred_element_type=jnp.float32)
    act_e = gate_e * jax.nn.sigmoid(gate_e)
    hidden_e = (act_e * up_e).astype(jnp.bfloat16)
    result_e = jnp.einsum(
        "erf,efd->erd", hidden_e, ex_down, preferred_element_type=jnp.float32
    ).astype(jnp.bfloat16)
    returned = lax.all_to_all(
        to_owner(result_e), ("experts", "context"), split_axis=0, concat_axis=0, tiled=True
    )
    picked = returned.reshape(experts_all * capacity, model_width)[target]
    picked = jnp.where(kept_rows[:, None], picked, jnp.zeros_like(picked)).astype(jnp.float32)
    routed = jnp.sum((picked * row_gates[:, None]).reshape(tokens_here, TOP, model_width), axis=1)
    output = (residual + shared_gate[:, None] * shared_part + routed).astype(jnp.bfloat16)
    gate_grads = jnp.sum(picked * cot_repeated, axis=1).reshape(tokens_here, TOP)
    hidden_grad_e = jnp.einsum(
        "erd,efd->erf", expert_grads_in, ex_down, preferred_element_type=jnp.float32
    )
    gate_grad_e = (hidden_grad_e * up_e * silu_grad(gate_e)).astype(jnp.bfloat16)
    up_grad_e = (hidden_grad_e * act_e).astype(jnp.bfloat16)
    grad_ex_down = jnp.einsum(
        "erf,erd->efd", hidden_e, expert_grads_in, preferred_element_type=jnp.float32
    )
    grad_ex_gate = jnp.einsum(
        "erd,erf->edf", expert_rows, gate_grad_e, preferred_element_type=jnp.float32
    )
    grad_ex_up = jnp.einsum(
        "erd,erf->edf", expert_rows, up_grad_e, preferred_element_type=jnp.float32
    )
    expert_sums = (
        lax.psum_scatter(grad_ex_gate, "dp", scatter_dimension=1, tiled=True),
        lax.psum_scatter(grad_ex_up, "dp", scatter_dimension=1, tiled=True),
        lax.psum_scatter(grad_ex_down, "dp", scatter_dimension=2, tiled=True),
    )
    rows_grad_e = jnp.einsum(
        "erf,edf->erd", gate_grad_e, ex_gate, preferred_element_type=jnp.float32
    )
    rows_grad_e = (
        rows_grad_e
        + jnp.einsum("erf,edf->erd", up_grad_e, ex_up, preferred_element_type=jnp.float32)
    ).astype(jnp.bfloat16)
    returned_grads = lax.all_to_all(
        to_owner(rows_grad_e), ("experts", "context"), split_axis=0, concat_axis=0, tiled=True
    )
    routed_grad = returned_grads.reshape(experts_all * capacity, model_width)[target]
    routed_grad = jnp.where(kept_rows[:, None], routed_grad, jnp.zeros_like(routed_grad)).astype(
        jnp.float32
    )
    norm_grad = jnp.sum(routed_grad.reshape(tokens_here, TOP, model_width), axis=1)
    choose = (
        routes[0][:, :, None] == jnp.arange(experts_all, dtype=jnp.int32)[None, None, :]
    ).astype(jnp.float32)
    probs_grad = jnp.einsum("tk,tke->te", gate_grads, choose)
    logit_grad = (
        router_probs * (probs_grad - jnp.sum(router_probs * probs_grad, axis=1, keepdims=True))
    ).astype(jnp.bfloat16)
    grad_router = jnp.dot(normed_two.T, logit_grad, preferred_element_type=jnp.float32)
    gate_logit_grad = (
        jnp.sum(cot_rows * shared_part, axis=1) * shared_gate * (1.0 - shared_gate)
    ).astype(jnp.bfloat16)
    grad_gate_vec = jnp.dot(gate_logit_grad, normed_two, preferred_element_type=jnp.float32)
    norm_grad = norm_grad + jnp.dot(logit_grad, router_full.T, preferred_element_type=jnp.float32)
    norm_grad = (
        norm_grad
        + gate_logit_grad.astype(jnp.float32)[:, None] * gate_vec.astype(jnp.float32)[None, :]
    )
    shared_hgrad = jnp.dot(grads_group, sh_down.T, preferred_element_type=jnp.float32)
    gate_grad_s = (shared_hgrad * up_pre * silu_grad(gate_pre)).astype(jnp.bfloat16)
    up_grad_s = (shared_hgrad * gate_act).astype(jnp.bfloat16)
    shared_rows_grad = jnp.dot(gate_grad_s, sh_gate.T, preferred_element_type=jnp.float32)
    shared_rows_grad = shared_rows_grad + jnp.dot(
        up_grad_s, sh_up.T, preferred_element_type=jnp.float32
    )
    groups = lax.axis_size("experts")
    parts_cd = lax.axis_size(("context", "dp"))
    rows_count = rows_group.shape[0]
    arr_gate = jnp.einsum(
        "td,tes->eds",
        rows_group,
        gate_grad_s.reshape(rows_count, groups, -1),
        preferred_element_type=jnp.float32,
    ).reshape(groups * model_width, -1)
    arr_up = jnp.einsum(
        "td,tes->eds",
        rows_group,
        up_grad_s.reshape(rows_count, groups, -1),
        preferred_element_type=jnp.float32,
    ).reshape(groups * model_width, -1)
    arr_down = jnp.einsum(
        "tes,tcd->ecsd",
        shared_hidden.reshape(rows_count, groups, -1),
        grads_group.reshape(rows_count, parts_cd, -1),
        preferred_element_type=jnp.float32,
    ).reshape(-1, model_width // parts_cd)
    sums_gate, sums_up, sums_down = (
        lax.psum_scatter(arr_gate, ("experts", "context", "dp"), scatter_dimension=0, tiled=True),
        lax.psum_scatter(arr_up, ("experts", "context", "dp"), scatter_dimension=0, tiled=True),
        lax.psum_scatter(arr_down, ("experts", "context", "dp"), scatter_dimension=0, tiled=True),
    )
    norm_grad = norm_grad + shared_rows_grad
    residual_grad, grad_gain_two = norm_back(residual, inv_two, g_two, norm_grad)
    residual_grad = residual_grad + cot_rows
    low_residual = residual_grad.astype(jnp.bfloat16)
    grad_out_w = jnp.dot(attended.T, low_residual, preferred_element_type=jnp.float32)
    attended_grad = jnp.dot(low_residual, out_w.T, preferred_element_type=jnp.float32).astype(
        jnp.bfloat16
    )
    head_q_grad, head_k_grad, head_v_grad = lax.map(
        partial(attend_back, allowed=allowed, scale_factor=scale_factor),
        (head_q, head_k, head_v, to_heads(attended_grad), log_total),
    )
    key_sum, value_sum = (
        lax.psum_scatter(from_heads(head_k_grad), "context", scatter_dimension=0, tiled=True),
        lax.psum_scatter(from_heads(head_v_grad), "context", scatter_dimension=0, tiled=True),
    )
    query_low = from_heads(head_q_grad).astype(jnp.bfloat16)
    key_low = key_sum.astype(jnp.bfloat16)
    value_low = value_sum.astype(jnp.bfloat16)
    grad_query = jnp.dot(normed_one.T, query_low, preferred_element_type=jnp.float32)
    grad_key = jnp.dot(normed_one.T, key_low, preferred_element_type=jnp.float32)
    grad_value = jnp.dot(normed_one.T, value_low, preferred_element_type=jnp.float32)
    normed_grad = jnp.dot(query_low, query_w.T, preferred_element_type=jnp.float32)
    normed_grad = normed_grad + jnp.dot(key_low, key_w.T, preferred_element_type=jnp.float32)
    normed_grad = normed_grad + jnp.dot(value_low, value_w.T, preferred_element_type=jnp.float32)
    input_part, grad_gain_one = norm_back(x_rows, inv_one, g_one, normed_grad)
    input_grad = (residual_grad + input_part).astype(jnp.bfloat16)
    dense = (
        lax.psum_scatter(
            grad_gain_one, ("experts", "context", "dp"), scatter_dimension=0, tiled=True
        ),
        lax.psum_scatter(grad_query, ("experts", "context", "dp"), scatter_dimension=0, tiled=True),
        lax.psum_scatter(grad_key, ("experts", "context", "dp"), scatter_dimension=0, tiled=True),
        lax.psum_scatter(grad_value, ("experts", "context", "dp"), scatter_dimension=0, tiled=True),
        lax.psum_scatter(grad_out_w, ("experts", "context", "dp"), scatter_dimension=0, tiled=True),
        lax.psum_scatter(
            grad_gain_two, ("experts", "context", "dp"), scatter_dimension=0, tiled=True
        ),
        lax.psum_scatter(
            grad_router, ("experts", "context", "dp"), scatter_dimension=0, tiled=True
        ),
        lax.psum_scatter(
            grad_gate_vec, ("experts", "context", "dp"), scatter_dimension=0, tiled=True
        ),
    )
    return (
        output[None],
        input_grad[None],
        dense[0],
        dense[1],
        dense[2],
        dense[3],
        dense[4],
        dense[5],
        dense[6],
        dense[7],
        sums_gate,
        sums_up,
        sums_down,
        expert_sums[0],
        expert_sums[1],
        expert_sums[2],
    )

PLANE = ("experts", "context")


def attention_probs(q_blk, k_part, q_code, k_code, first_row, scale_factor):
    scores = lax.dot_general(
        q_blk, k_part, (((1,), (1,)), ((), ())), preferred_element_type=jnp.float32
    )
    row = first_row + lax.broadcasted_iota(jnp.int32, scores.shape, 0)
    col = lax.broadcasted_iota(jnp.int32, scores.shape, 1)
    allowed = ((col < row) & (k_code == q_code)) | (col == row)
    logits = jnp.where(allowed, scores * scale_factor, NEG)
    exp_scores = jnp.exp(logits - jnp.max(logits, axis=1, keepdims=True))
    return exp_scores * (1.0 / jnp.sum(exp_scores, axis=1, keepdims=True))


def attend_kernel(heads, step, qkv_ref, q_code_ref, k_code_ref, out_ref):
    seq_len = qkv_ref.shape[0]
    width = heads * HEAD_DIM
    for head in range(heads):
        at = head * HEAD_DIM
        for first in range(0, seq_len, step):
            upto = first + step
            probs = attention_probs(
                qkv_ref[first:upto, at : at + HEAD_DIM],
                qkv_ref[0:upto, width + at : width + at + HEAD_DIM],
                q_code_ref[first:upto, :],
                k_code_ref[0, :, 0:upto],
                first,
                HEAD_DIM**-0.5,
            )
            out_ref[first:upto, at : at + HEAD_DIM] = jnp.dot(
                probs.astype(jnp.bfloat16),
                qkv_ref[0:upto, 2 * width + at : 2 * width + at + HEAD_DIM],
                preferred_element_type=jnp.float32,
            ).astype(jnp.bfloat16)


def attend_back_kernel(
    heads, step, qkv_ref, grad_ref, q_code_ref, k_code_ref, out_ref, key_acc, value_acc
):
    seq_len = qkv_ref.shape[0]
    width = heads * HEAD_DIM
    for head in range(heads):
        at = head * HEAD_DIM
        key_at, value_at = width + at, 2 * width + at
        key_acc[...] = jnp.zeros_like(key_acc)
        value_acc[...] = jnp.zeros_like(value_acc)
        for first in range(0, seq_len, step):
            upto = first + step
            q_blk = qkv_ref[first:upto, at : at + HEAD_DIM]
            k_part = qkv_ref[0:upto, key_at : key_at + HEAD_DIM]
            v_part = qkv_ref[0:upto, value_at : value_at + HEAD_DIM]
            g_blk = grad_ref[first:upto, at : at + HEAD_DIM]
            probs = attention_probs(
                q_blk,
                k_part,
                q_code_ref[first:upto, :],
                k_code_ref[0, :, 0:upto],
                first,
                HEAD_DIM**-0.5,
            )
            prob_grad = lax.dot_general(
                g_blk, v_part, (((1,), (1,)), ((), ())), preferred_element_type=jnp.float32
            )
            inner = jnp.sum(probs * prob_grad, axis=1, keepdims=True)
            score_grad = (probs * (prob_grad - inner) * HEAD_DIM**-0.5).astype(jnp.bfloat16)
            out_ref[first:upto, at : at + HEAD_DIM] = jnp.dot(
                score_grad, k_part, preferred_element_type=jnp.float32
            ).astype(jnp.bfloat16)
            key_acc[0:upto, :] += lax.dot_general(
                score_grad, q_blk, (((0,), (0,)), ((), ())), preferred_element_type=jnp.float32
            )
            value_acc[0:upto, :] += lax.dot_general(
                probs.astype(jnp.bfloat16),
                g_blk,
                (((0,), (0,)), ((), ())),
                preferred_element_type=jnp.float32,
            )
        out_ref[:, key_at : key_at + HEAD_DIM] = key_acc[...].astype(jnp.bfloat16)
        out_ref[:, value_at : value_at + HEAD_DIM] = value_acc[...].astype(jnp.bfloat16)


def attention_call(qkv, grads, q_codes, k_codes, seq_len):
    rows, triple = qkv.shape
    width = triple // 3
    heads = width // HEAD_DIM
    step = min(256, seq_len)
    specs = [pl.BlockSpec((seq_len, triple), lambda s: (s, 0))]
    operands = [qkv]
    if grads is not None:
        specs.append(pl.BlockSpec((seq_len, width), lambda s: (s, 0)))
        operands.append(grads)
    specs += [
        pl.BlockSpec((seq_len, 1), lambda s: (s, 0)),
        pl.BlockSpec((1, 1, seq_len), lambda s: (s, 0, 0)),
    ]
    operands += [q_codes, k_codes]
    out_width = width if grads is None else triple
    body = attend_kernel if grads is None else attend_back_kernel
    passes = 2 if grads is None else 5
    area = rows * seq_len * heads
    return pl.pallas_call(
        partial(body, heads, step),
        grid=(rows // seq_len,),
        in_specs=specs,
        out_specs=pl.BlockSpec((seq_len, out_width), lambda s: (s, 0)),
        out_shape=jax.ShapeDtypeStruct((rows, out_width), jnp.bfloat16),
        scratch_shapes=[]
        if grads is None
        else [pltpu.VMEM((seq_len, HEAD_DIM), jnp.float32)] * 2,
        compiler_params=pltpu.CompilerParams(vmem_limit_bytes=48 * 2**20),
        cost_estimate=pl.CostEstimate(
            flops=2 * passes * area * HEAD_DIM,
            bytes_accessed=2 * rows * (triple + out_width),
            transcendentals=area,
        ),
    )(*operands)


def mm(left, right, dims=((1,), (0,))):
    return lax.dot_general(left, right, (dims, ((), ())), preferred_element_type=jnp.float32)


def low(values):
    return values.astype(jnp.bfloat16)


def local_plane(
    hidden,
    cotangent,
    segments,
    padding,
    routes,
    order,
    norm1_gain,
    w_query,
    w_key,
    w_value,
    w_out,
    norm2_gain,
    router,
    shared_gate_vec,
    shared_w_gate,
    shared_w_up,
    shared_w_down,
    expert_w_gate,
    expert_w_up,
    expert_w_down,
):
    plane = lax.axis_size(PLANE)
    groups = lax.axis_size("experts")
    halves = lax.axis_size("context")
    depth = lax.axis_size("dp")
    me = lax.axis_index(PLANE)
    core = lax.axis_index("context")
    tokens, width = hidden.shape[1], hidden.shape[2]
    all_tokens = plane * tokens
    seq_len = halves * tokens
    experts_all = router.shape[1]
    head_cols = width // plane
    shard = width // depth

    small = jnp.concatenate(
        [
            norm1_gain[None],
            norm2_gain[None],
            shared_gate_vec[None],
            jnp.zeros((5, shard), jnp.bfloat16),
            router.T,
        ]
    )
    small = lax.all_gather(small, "dp", axis=0, tiled=False)
    small = small.transpose(1, 0, 2).reshape(-1, width)
    g_one = small[0].astype(jnp.float32)
    g_two = small[1].astype(jnp.float32)
    gate_vec = small[2]
    router_t = small[8:]
    token_info = jnp.concatenate(
        [segments + 1, jnp.where(padding > 0, segments + 1, 0), order[0], routes[0].T]
    )
    info_rows = token_info.shape[0]
    token_info = jnp.concatenate([token_info, jnp.zeros((8 - info_rows, tokens), jnp.int32)])
    info_all = lax.all_gather(token_info, PLANE, axis=0, tiled=False)

    hidden_all = lax.all_gather(hidden[0], PLANE, axis=0, tiled=True)
    w_qkv_part = jnp.concatenate(
        [
            lax.dynamic_slice(w, (0, me * head_cols), (shard, head_cols))
            for w in (w_query, w_key, w_value)
        ],
        axis=1,
    )
    w_qkv = lax.all_gather(w_qkv_part, "dp", axis=0, tiled=True)
    out_rows = shard // plane
    w_out_part = lax.dynamic_slice(w_out, (me * out_rows, 0), (out_rows, width))
    w_out_part = lax.all_gather(w_out_part, "dp", axis=0, tiled=False)
    w_out_full = lax.all_gather(w_out_part, PLANE, axis=0, tiled=False)
    w_out_full = w_out_full.transpose(1, 0, 2, 3).reshape(width, width)

    def normed(values, gain):
        values = values.astype(jnp.float32)
        inv = lax.rsqrt(jnp.mean(values * values, axis=1, keepdims=True) + EPS)
        return values, inv, low(values * inv * gain)

    _, _, n1_all = normed(hidden_all, g_one)
    x_rows, inv_one, _ = normed(hidden[0], g_one)
    cot_rows = cotangent[0].astype(jnp.float32)
    qkv = low(mm(n1_all, w_qkv))
    q_codes = info_all[:, 0].reshape(all_tokens, 1)
    k_codes = info_all[:, 1].reshape(all_tokens // seq_len, 1, seq_len)
    attended_cols = attention_call(qkv, None, q_codes, k_codes, seq_len)

    def to_tokens(cols):
        got = lax.all_to_all(
            cols.reshape(plane, tokens, head_cols), PLANE, split_axis=0, concat_axis=0, tiled=True
        )
        return got.transpose(1, 0, 2).reshape(tokens, width)

    def to_columns(rows_in):
        send = rows_in.reshape(tokens, plane, head_cols).transpose(1, 0, 2)
        got = lax.all_to_all(send, PLANE, split_axis=0, concat_axis=0, tiled=True)
        return got.reshape(all_tokens, head_cols)

    attended = to_tokens(attended_cols)
    residual = x_rows + mm(attended, w_out_full)
    residual, inv_two, n2 = normed(residual, g_two)

    n2_all = lax.all_gather(n2, PLANE, axis=0, tiled=True)
    cot_all = lax.all_gather(cotangent[0], PLANE, axis=0, tiled=True)
    units = shared_w_gate.shape[1]
    part = units // (depth * halves)
    pick = lambda w: lax.dynamic_index_in_dim(
        w.reshape(w.shape[0], depth, halves, part), core, axis=2, keepdims=False
    ).reshape(w.shape[0], depth * part)
    sh_gate = lax.all_gather(pick(shared_w_gate), "dp", axis=0, tiled=True)
    sh_up = lax.all_gather(pick(shared_w_up), "dp", axis=0, tiled=True)
    sh_down = lax.all_gather(
        lax.dynamic_slice(shared_w_down, (core * part, 0), (part, width)), "dp", axis=0, tiled=True
    )
    ex_gate = lax.all_gather(expert_w_gate[0], "dp", axis=0, tiled=True)
    ex_up = lax.all_gather(expert_w_up[0], "dp", axis=0, tiled=True)
    ex_down = lax.all_gather(expert_w_down[0], "dp", axis=1, tiled=True)

    def router_of(rows_in):
        z = mm(rows_in, router_t, ((1,), (1,)))
        e = jnp.exp(z - jnp.max(z, axis=1, keepdims=True))
        return e / jnp.sum(e, axis=1, keepdims=True)

    def shared_gate_of(rows_in):
        return jax.nn.sigmoid(mm(rows_in, gate_vec[:, None]))

    probs_all = router_of(n2_all)
    sg_all = shared_gate_of(n2_all)
    expert_gate = lax.dynamic_slice(probs_all, (0, me), (all_tokens, 1))

    capacity = (9 * tokens * TOP + 8 * experts_all - 1) // (8 * experts_all)
    order_all = info_all[:, 2]
    routed_here = jnp.any(info_all[:, 3 : 3 + TOP] == me, axis=1)
    earlier = (order_all[:, None, :] < order_all[:, :, None]) & routed_here[:, None, :]
    slots = jnp.sum(earlier.astype(jnp.int32), axis=2)
    slots = jnp.where(routed_here, slots, capacity)
    chosen = slots[:, None, :] == jnp.arange(capacity, dtype=jnp.int32)[None, :, None]
    onehot = chosen.astype(jnp.bfloat16)

    def rows_of(values):
        got = jnp.einsum(
            "bst,btd->bsd",
            onehot,
            values.reshape(plane, tokens, width),
            preferred_element_type=jnp.float32,
        )
        return got.reshape(plane * capacity, width)

    def back_to_tokens(values):
        got = jnp.einsum(
            "bst,bsd->btd",
            onehot,
            values.reshape(plane, capacity, width),
            preferred_element_type=jnp.float32,
        )
        return got.reshape(all_tokens, width)

    slot_gates = jnp.sum(
        jnp.where(chosen, expert_gate.reshape(plane, 1, tokens), 0.0), axis=2
    ).reshape(plane * capacity, 1)
    expert_rows = low(rows_of(n2_all))
    row_cots = low(rows_of(cot_all))
    row_grads = low(row_cots.astype(jnp.float32) * slot_gates)

    shared_grads = low(sg_all * cot_all.astype(jnp.float32))
    gate_pre = mm(n2_all, sh_gate)
    up_pre = mm(n2_all, sh_up)
    gate_act = gate_pre * jax.nn.sigmoid(gate_pre)
    shared_hidden = low(gate_act * up_pre)
    shared_part = mm(shared_hidden, sh_down)
    cot_dot_shared = jnp.sum(shared_part * cot_all.astype(jnp.float32), axis=1)
    shared_hgrad = mm(shared_grads, sh_down, ((1,), (1,)))
    gate_grad_s = low(shared_hgrad * up_pre * silu_grad(gate_pre))
    up_grad_s = low(shared_hgrad * gate_act)

    def shared_scatter(grad):
        halved = lax.all_to_all(
            low(grad).reshape(halves, width // halves, depth * part),
            "context",
            split_axis=0,
            concat_axis=0,
            tiled=True,
        )
        rows_out = width // (halves * depth)
        halved = (
            halved.reshape(halves, depth, rows_out, depth * part)
            .transpose(1, 2, 0, 3)
            .reshape(depth * rows_out, units)
        )
        total = lax.psum_scatter(halved, "dp", scatter_dimension=0, tiled=True)
        total = total.reshape(rows_out, halves, depth, part).transpose(0, 2, 1, 3)
        return total.reshape(rows_out, units).astype(jnp.float32)

    grad_sh_gate = shared_scatter(mm(n2_all, gate_grad_s, ((0,), (0,))))
    grad_sh_up = shared_scatter(mm(n2_all, up_grad_s, ((0,), (0,))))
    grad_sh_down = shared_scatter(mm(shared_grads, shared_hidden, ((0,), (0,)))).T

    gate_e = mm(expert_rows, ex_gate)
    up_e = mm(expert_rows, ex_up)
    act_e = gate_e * jax.nn.sigmoid(gate_e)
    hidden_e = low(act_e * up_e)
    result_e = low(mm(hidden_e, ex_down))
    row_dots = jnp.sum(result_e.astype(jnp.float32) * row_cots.astype(jnp.float32), axis=1)
    gate_dots = jnp.sum(
        jnp.where(chosen, row_dots.reshape(plane, capacity, 1), 0.0), axis=1
    )
    hgrad_e = mm(row_grads, ex_down, ((1,), (1,)))
    gate_grad_e = low(hgrad_e * up_e * silu_grad(gate_e))
    up_grad_e = low(hgrad_e * act_e)

    def expert_scatter(grad, dim):
        return lax.psum_scatter(low(grad), "dp", scatter_dimension=dim, tiled=True).astype(
            jnp.float32
        )[None]

    grad_ex_down = expert_scatter(mm(hidden_e, row_grads, ((0,), (0,))), 1)
    grad_ex_gate = expert_scatter(mm(expert_rows, gate_grad_e, ((0,), (0,))), 0)
    grad_ex_up = expert_scatter(mm(expert_rows, up_grad_e, ((0,), (0,))), 0)
    rows_grad = low(
        mm(gate_grad_e, ex_gate, ((1,), (1,))) + mm(up_grad_e, ex_up, ((1,), (1,)))
    )

    out_part = low(sg_all * shared_part + expert_gate * back_to_tokens(result_e))
    out_sum = lax.psum_scatter(out_part, PLANE, scatter_dimension=0, tiled=True)
    output = low(residual + out_sum.astype(jnp.float32))
    n2_grad_part = low(
        mm(gate_grad_s, sh_gate, ((1,), (1,)))
        + mm(up_grad_s, sh_up, ((1,), (1,)))
        + back_to_tokens(rows_grad)
    )
    n2_grad = lax.psum_scatter(n2_grad_part, PLANE, scatter_dimension=0, tiled=True).astype(
        jnp.float32
    )

    dots = jnp.stack([gate_dots, cot_dot_shared.reshape(plane, tokens)], axis=1)
    dots = lax.all_to_all(dots, PLANE, split_axis=0, concat_axis=0, tiled=True)
    probs_grad = dots[:, 0].T
    probs = router_of(n2)
    sg = shared_gate_of(n2)
    logit_grad = low(probs * (probs_grad - jnp.sum(probs * probs_grad, axis=1, keepdims=True)))
    sg_logit_grad = low(jnp.sum(dots[:, 1], axis=0)[:, None] * sg * (1.0 - sg))
    small_grads = mm(n2, jnp.concatenate([logit_grad, sg_logit_grad], axis=1), ((0,), (0,)))
    n2_grad = (
        n2_grad
        + mm(logit_grad, router_t)
        + sg_logit_grad.astype(jnp.float32) * gate_vec.astype(jnp.float32)[None]
    )
    residual_grad, grad_gain_two = norm_back(residual, inv_two, g_two, n2_grad)
    residual_grad = residual_grad + cot_rows
    low_residual = low(residual_grad)

    grad_out = low(mm(attended, low_residual, ((0,), (0,))))
    grad_out = lax.psum_scatter(grad_out, PLANE, scatter_dimension=0, tiled=True)
    grad_out = lax.psum_scatter(grad_out, "dp", scatter_dimension=0, tiled=True).astype(jnp.float32)
    attended_grad = to_columns(low(mm(low_residual, w_out_full, ((1,), (1,)))))
    qkv_grad = attention_call(qkv, attended_grad, q_codes, k_codes, seq_len)
    n1_grad = low(mm(qkv_grad, w_qkv, ((1,), (1,))))
    n1_grad = lax.psum_scatter(n1_grad, PLANE, scatter_dimension=0, tiled=True).astype(jnp.float32)
    grad_qkv = low(mm(n1_all, qkv_grad, ((0,), (0,))))
    fine = shard // plane
    grad_qkv = (
        grad_qkv.reshape(plane, depth, fine, 3 * head_cols)
        .transpose(1, 0, 2, 3)
        .reshape(width, 3 * head_cols)
    )
    grad_qkv = lax.psum_scatter(grad_qkv, "dp", scatter_dimension=0, tiled=True)
    grad_qkv = lax.all_to_all(
        grad_qkv.reshape(plane, fine, 3 * head_cols),
        PLANE,
        split_axis=0,
        concat_axis=0,
        tiled=True,
    )
    grad_qkv = (
        grad_qkv.reshape(plane, fine, 3, head_cols)
        .transpose(2, 1, 0, 3)
        .reshape(3, fine, width)
        .astype(jnp.float32)
    )
    input_part, grad_gain_one = norm_back(x_rows, inv_one, g_one, n1_grad)
    input_grad = low(residual_grad + input_part)
    small_grads = jnp.concatenate(
        [small_grads, grad_gain_two[:, None], grad_gain_one[:, None]], axis=1
    )
    small_grads = lax.psum_scatter(
        small_grads, ("experts", "context", "dp"), scatter_dimension=0, tiled=True
    )
    return (
        output[None],
        input_grad[None],
        small_grads[:, experts_all + 2],
        grad_qkv[0],
        grad_qkv[1],
        grad_qkv[2],
        grad_out,
        small_grads[:, experts_all + 1],
        small_grads[:, :experts_all],
        small_grads[:, experts_all],
        grad_sh_gate,
        grad_sh_up,
        grad_sh_down,
        grad_ex_gate,
        grad_ex_up,
        grad_ex_down,
    )


def solution(mesh):
    in_specs = (
        P(("experts", "dp"), "context", None),
        P(("experts", "dp"), "context", None),
        P(("experts", "dp"), "context"),
        P(("experts", "dp"), "context"),
        P(("experts", "dp"), "context", None),
        P(("experts", "dp"), "context", None),
        P("dp"),
        P("dp", None),
        P("dp", None),
        P("dp", None),
        P("dp", None),
        P("dp"),
        P("dp", None),
        P("dp"),
        P("dp", "experts"),
        P("dp", "experts"),
        P(("experts", "dp"), None),
        P(("experts", "context"), "dp", None),
        P(("experts", "context"), "dp", None),
        P(("experts", "context"), None, "dp"),
    )
    out_specs = (
        P(("experts", "dp"), "context", None),
        P(("experts", "dp"), "context", None),
        P(("experts", "context", "dp")),
        P(("experts", "context", "dp"), None),
        P(("experts", "context", "dp"), None),
        P(("experts", "context", "dp"), None),
        P(("experts", "context", "dp"), None),
        P(("experts", "context", "dp")),
        P(("experts", "context", "dp"), None),
        P(("experts", "context", "dp")),
        P(("context", "dp"), "experts"),
        P(("context", "dp"), "experts"),
        P("experts", ("context", "dp")),
        P(("experts", "context"), "dp", None),
        P(("experts", "context"), "dp", None),
        P(("experts", "context"), None, "dp"),
    )
    plane = mesh.shape["experts"] * mesh.shape["context"]

    def run(*args):
        one_each = args[12].shape[1] == plane and HEADS % plane == 0
        local = local_plane if one_each else local_general
        return jax.shard_map(
            local, mesh=mesh, in_specs=in_specs, out_specs=out_specs, check_vma=False
        )(*args)

    return run
```

```python
from functools import partial

import jax
import jax.numpy as jnp
from jax import lax
from jax.experimental import pallas as pl
from jax.experimental.pallas import tpu as pltpu
from jax.sharding import PartitionSpec as P

EXP, CTX, DP = "experts", "context", "dp"
PLANE = (EXP, CTX)
HEADS = 16
HEAD_DIM = 128
TOP = 4


EPS = 1e-06
NEG = -1e30


def silu_grad(pre_act):
    logistic = jax.nn.sigmoid(pre_act)
    return logistic * (1.0 + pre_act * (1.0 - logistic))


def block_slots(route_row, priority, expert_count):
    matches = (route_row[:, None] == jnp.arange(expert_count, dtype=jnp.int32)[None, :]).astype(
        jnp.int32
    )
    ordered = jnp.zeros_like(matches).at[priority].set(matches)
    before = jnp.cumsum(ordered, axis=0) - ordered
    return jnp.sum(before[priority] * matches, axis=1)


def norm_back(values_in, inv_rms, gain_vec, gradient):
    weighted = gradient * gain_vec
    inner_sum = jnp.mean(weighted * values_in, axis=1, keepdims=True)
    d_value = inv_rms * weighted - values_in * inv_rms**3 * inner_sum
    d_gain = jnp.sum(gradient * values_in * inv_rms, axis=0)
    return (d_value, d_gain)


def attend_head(packed, allowed, scale_factor):
    query_h, key_h, value_h = packed
    raw_scores = jnp.einsum("th,lh->tl", query_h, key_h, preferred_element_type=jnp.float32)
    logits = jnp.where(allowed, raw_scores * scale_factor, NEG)
    row_max = jnp.max(logits, axis=1, keepdims=True)
    exp_scores = jnp.exp(logits - row_max)
    row_total = jnp.sum(exp_scores, axis=1, keepdims=True)
    attn_probs = (exp_scores / row_total).astype(jnp.bfloat16)
    head_out = jnp.dot(attn_probs, value_h, preferred_element_type=jnp.float32).astype(jnp.bfloat16)
    return (head_out, row_max + jnp.log(row_total))


def attend_back(packed, allowed, scale_factor):
    query_h, key_h, value_h, out_grad, log_total = packed
    raw_scores = jnp.einsum("th,lh->tl", query_h, key_h, preferred_element_type=jnp.float32)
    logits = jnp.where(allowed, raw_scores * scale_factor, NEG)
    attn_probs = jnp.exp(logits - log_total)
    prob_grad = jnp.einsum("th,lh->tl", out_grad, value_h, preferred_element_type=jnp.float32)
    inner_sum = jnp.sum(attn_probs * prob_grad, axis=1, keepdims=True)
    score_grad = (attn_probs * (prob_grad - inner_sum) * scale_factor).astype(jnp.bfloat16)
    query_grad = jnp.dot(score_grad, key_h, preferred_element_type=jnp.float32)
    key_grad = jnp.einsum("tl,th->lh", score_grad, query_h, preferred_element_type=jnp.float32)
    value_grad = jnp.einsum(
        "tl,th->lh", attn_probs.astype(jnp.bfloat16), out_grad, preferred_element_type=jnp.float32
    )
    return (query_grad, key_grad, value_grad)


def local_general(
    hidden,
    cotangent,
    segments,
    padding,
    routes,
    order,
    norm1_gain,
    w_query,
    w_key,
    w_value,
    w_out,
    norm2_gain,
    router,
    shared_gate_vec,
    shared_w_gate,
    shared_w_up,
    shared_w_down,
    expert_w_gate,
    expert_w_up,
    expert_w_down,
):
    fetched = (
        lax.all_gather(norm1_gain, DP, axis=0, tiled=True),
        lax.all_gather(w_query, DP, axis=0, tiled=True),
        lax.all_gather(w_key, DP, axis=0, tiled=True),
        lax.all_gather(w_value, DP, axis=0, tiled=True),
        lax.all_gather(w_out, DP, axis=0, tiled=True),
        lax.all_gather(norm2_gain, DP, axis=0, tiled=True),
        lax.all_gather(router, DP, axis=0, tiled=True),
        lax.all_gather(shared_gate_vec, DP, axis=0, tiled=True),
        lax.all_gather(shared_w_gate, DP, axis=0, tiled=True),
        lax.all_gather(shared_w_up, DP, axis=0, tiled=True),
        lax.all_gather(shared_w_down, DP, axis=0, tiled=True),
        lax.all_gather(expert_w_gate, DP, axis=1, tiled=True),
        lax.all_gather(expert_w_up, DP, axis=1, tiled=True),
        lax.all_gather(expert_w_down, DP, axis=2, tiled=True),
    )
    (
        gain_one,
        query_w,
        key_w,
        value_w,
        out_w,
        gain_two,
        router_full,
        gate_vec,
        sh_gate,
        sh_up,
        sh_down,
        ex_gate,
        ex_up,
        ex_down,
    ) = fetched
    sh_gate, sh_up, sh_down = (
        lax.all_gather(sh_gate, EXP, axis=1, tiled=True),
        lax.all_gather(sh_up, EXP, axis=1, tiled=True),
        lax.all_gather(sh_down, EXP, axis=0, tiled=True),
    )
    tokens_here = hidden.shape[1]
    model_width = hidden.shape[2]
    x_rows = hidden[0].astype(jnp.float32)
    cot_rows = cotangent[0].astype(jnp.float32)
    inv_one = lax.rsqrt(jnp.mean(x_rows * x_rows, axis=1, keepdims=True) + EPS)
    g_one = gain_one.astype(jnp.float32)
    normed_one = (x_rows * inv_one * g_one).astype(jnp.bfloat16)
    queries = jnp.dot(normed_one, query_w, preferred_element_type=jnp.float32).astype(jnp.bfloat16)
    keys_own = jnp.dot(normed_one, key_w, preferred_element_type=jnp.float32).astype(jnp.bfloat16)
    values_own = jnp.dot(normed_one, value_w, preferred_element_type=jnp.float32).astype(
        jnp.bfloat16
    )
    own_codes = jnp.where(padding[0] > 0, segments[0] + 1, 0)
    code_parts = jnp.stack([own_codes // 64, own_codes % 64]).astype(jnp.bfloat16)
    keys_all, values_all, parts_all = (
        lax.all_gather(keys_own, CTX, axis=0, tiled=True),
        lax.all_gather(values_own, CTX, axis=0, tiled=True),
        lax.all_gather(code_parts, CTX, axis=1, tiled=True),
    )
    key_codes = parts_all[0].astype(jnp.int32) * 64 + parts_all[1].astype(jnp.int32)
    seq_total = keys_all.shape[0]
    query_pos = lax.axis_index(CTX) * tokens_here + jnp.arange(tokens_here, dtype=jnp.int32)
    key_pos = jnp.arange(seq_total, dtype=jnp.int32)
    same_doc = key_codes[None, :] == (segments[0] + 1)[:, None]
    allowed = (key_pos[None, :] <= query_pos[:, None]) & (
        same_doc | (key_pos[None, :] == query_pos[:, None])
    )
    scale_factor = HEAD_DIM ** (-0.5)

    def to_heads(rows_in):
        return rows_in.reshape(rows_in.shape[0], HEADS, HEAD_DIM).transpose(1, 0, 2)

    def from_heads(heads_in):
        return heads_in.transpose(1, 0, 2).reshape(heads_in.shape[1], model_width)

    head_q = to_heads(queries)
    head_k = to_heads(keys_all)
    head_v = to_heads(values_all)
    head_out, log_total = lax.map(
        partial(attend_head, allowed=allowed, scale_factor=scale_factor), (head_q, head_k, head_v)
    )
    attended = from_heads(head_out)
    residual = x_rows + jnp.dot(attended, out_w, preferred_element_type=jnp.float32)
    inv_two = lax.rsqrt(jnp.mean(residual * residual, axis=1, keepdims=True) + EPS)
    g_two = gain_two.astype(jnp.float32)
    normed_two = (residual * inv_two * g_two).astype(jnp.bfloat16)
    router_logits = jnp.dot(normed_two, router_full, preferred_element_type=jnp.float32)
    router_exp = jnp.exp(router_logits - jnp.max(router_logits, axis=1, keepdims=True))
    router_probs = router_exp / jnp.sum(router_exp, axis=1, keepdims=True)
    route_gates = jnp.take_along_axis(router_probs, routes[0], axis=1)
    shared_gate = jax.nn.sigmoid(jnp.dot(normed_two, gate_vec, preferred_element_type=jnp.float32))
    shared_scaled = (shared_gate[:, None] * cot_rows).astype(jnp.bfloat16)
    rows_group, grads_group = (normed_two, shared_scaled)
    gate_pre = jnp.dot(rows_group, sh_gate, preferred_element_type=jnp.float32)
    up_pre = jnp.dot(rows_group, sh_up, preferred_element_type=jnp.float32)
    gate_act = gate_pre * jax.nn.sigmoid(gate_pre)
    shared_hidden = (gate_act * up_pre).astype(jnp.bfloat16)
    shared_part = jnp.dot(shared_hidden, sh_down, preferred_element_type=jnp.float32)
    experts_all = router_full.shape[1]
    capacity = (9 * tokens_here * TOP + 8 * experts_all - 1) // (8 * experts_all)
    priority = (order[0, 0][:, None] * TOP + jnp.arange(TOP, dtype=jnp.int32)[None, :]).reshape(-1)
    flat_routes = routes[0].reshape(-1)
    slot_index = block_slots(flat_routes, priority, experts_all)
    kept_rows = slot_index < capacity
    target = flat_routes * capacity + jnp.minimum(slot_index, capacity - 1)
    row_gates = route_gates.reshape(-1)
    cot_repeated = jnp.repeat(cot_rows, TOP, axis=0)
    source_rows = jnp.repeat(normed_two, TOP, axis=0)
    source_grads = (cot_repeated * row_gates[:, None]).astype(jnp.bfloat16)
    empty_slots = jnp.zeros((experts_all * capacity, model_width), jnp.bfloat16)
    send_rows = empty_slots.at[target].add(
        jnp.where(kept_rows[:, None], source_rows, jnp.zeros_like(source_rows))
    )
    send_grads = empty_slots.at[target].add(
        jnp.where(kept_rows[:, None], source_grads, jnp.zeros_like(source_grads))
    )
    recv_rows, recv_grads = (
        lax.all_to_all(
            send_rows.reshape(experts_all, capacity, model_width),
            (EXP, CTX),
            split_axis=0,
            concat_axis=0,
            tiled=True,
        ),
        lax.all_to_all(
            send_grads.reshape(experts_all, capacity, model_width),
            (EXP, CTX),
            split_axis=0,
            concat_axis=0,
            tiled=True,
        ),
    )
    local_count = ex_gate.shape[0]
    sources = experts_all // local_count

    def to_local(buffer_in):
        return (
            buffer_in.reshape(sources, local_count, capacity, model_width)
            .transpose(1, 0, 2, 3)
            .reshape(local_count, sources * capacity, model_width)
        )

    def to_owner(buffer_in):
        return (
            buffer_in.reshape(local_count, sources, capacity, model_width)
            .transpose(1, 0, 2, 3)
            .reshape(experts_all, capacity, model_width)
        )

    expert_rows = to_local(recv_rows)
    expert_grads_in = to_local(recv_grads)
    gate_e = jnp.einsum("erd,edf->erf", expert_rows, ex_gate, preferred_element_type=jnp.float32)
    up_e = jnp.einsum("erd,edf->erf", expert_rows, ex_up, preferred_element_type=jnp.float32)
    act_e = gate_e * jax.nn.sigmoid(gate_e)
    hidden_e = (act_e * up_e).astype(jnp.bfloat16)
    result_e = jnp.einsum(
        "erf,efd->erd", hidden_e, ex_down, preferred_element_type=jnp.float32
    ).astype(jnp.bfloat16)
    returned = lax.all_to_all(
        to_owner(result_e), (EXP, CTX), split_axis=0, concat_axis=0, tiled=True
    )
    picked = returned.reshape(experts_all * capacity, model_width)[target]
    picked = jnp.where(kept_rows[:, None], picked, jnp.zeros_like(picked)).astype(jnp.float32)
    routed = jnp.sum((picked * row_gates[:, None]).reshape(tokens_here, TOP, model_width), axis=1)
    output = (residual + shared_gate[:, None] * shared_part + routed).astype(jnp.bfloat16)
    gate_grads = jnp.sum(picked * cot_repeated, axis=1).reshape(tokens_here, TOP)
    hidden_grad_e = jnp.einsum(
        "erd,efd->erf", expert_grads_in, ex_down, preferred_element_type=jnp.float32
    )
    gate_grad_e = (hidden_grad_e * up_e * silu_grad(gate_e)).astype(jnp.bfloat16)
    up_grad_e = (hidden_grad_e * act_e).astype(jnp.bfloat16)
    grad_ex_down = jnp.einsum(
        "erf,erd->efd", hidden_e, expert_grads_in, preferred_element_type=jnp.float32
    )
    grad_ex_gate = jnp.einsum(
        "erd,erf->edf", expert_rows, gate_grad_e, preferred_element_type=jnp.float32
    )
    grad_ex_up = jnp.einsum(
        "erd,erf->edf", expert_rows, up_grad_e, preferred_element_type=jnp.float32
    )
    expert_sums = (
        lax.psum_scatter(grad_ex_gate, DP, scatter_dimension=1, tiled=True),
        lax.psum_scatter(grad_ex_up, DP, scatter_dimension=1, tiled=True),
        lax.psum_scatter(grad_ex_down, DP, scatter_dimension=2, tiled=True),
    )
    rows_grad_e = jnp.einsum(
        "erf,edf->erd", gate_grad_e, ex_gate, preferred_element_type=jnp.float32
    )
    rows_grad_e = (
        rows_grad_e
        + jnp.einsum("erf,edf->erd", up_grad_e, ex_up, preferred_element_type=jnp.float32)
    ).astype(jnp.bfloat16)
    returned_grads = lax.all_to_all(
        to_owner(rows_grad_e), (EXP, CTX), split_axis=0, concat_axis=0, tiled=True
    )
    routed_grad = returned_grads.reshape(experts_all * capacity, model_width)[target]
    routed_grad = jnp.where(kept_rows[:, None], routed_grad, jnp.zeros_like(routed_grad)).astype(
        jnp.float32
    )
    norm_grad = jnp.sum(routed_grad.reshape(tokens_here, TOP, model_width), axis=1)
    choose = (
        routes[0][:, :, None] == jnp.arange(experts_all, dtype=jnp.int32)[None, None, :]
    ).astype(jnp.float32)
    probs_grad = jnp.einsum("tk,tke->te", gate_grads, choose)
    logit_grad = (
        router_probs * (probs_grad - jnp.sum(router_probs * probs_grad, axis=1, keepdims=True))
    ).astype(jnp.bfloat16)
    grad_router = jnp.dot(normed_two.T, logit_grad, preferred_element_type=jnp.float32)
    gate_logit_grad = (
        jnp.sum(cot_rows * shared_part, axis=1) * shared_gate * (1.0 - shared_gate)
    ).astype(jnp.bfloat16)
    grad_gate_vec = jnp.dot(gate_logit_grad, normed_two, preferred_element_type=jnp.float32)
    norm_grad = norm_grad + jnp.dot(logit_grad, router_full.T, preferred_element_type=jnp.float32)
    norm_grad = (
        norm_grad
        + gate_logit_grad.astype(jnp.float32)[:, None] * gate_vec.astype(jnp.float32)[None, :]
    )
    shared_hgrad = jnp.dot(grads_group, sh_down.T, preferred_element_type=jnp.float32)
    gate_grad_s = (shared_hgrad * up_pre * silu_grad(gate_pre)).astype(jnp.bfloat16)
    up_grad_s = (shared_hgrad * gate_act).astype(jnp.bfloat16)
    shared_rows_grad = jnp.dot(gate_grad_s, sh_gate.T, preferred_element_type=jnp.float32)
    shared_rows_grad = shared_rows_grad + jnp.dot(
        up_grad_s, sh_up.T, preferred_element_type=jnp.float32
    )
    groups = lax.axis_size(EXP)
    parts_cd = lax.axis_size((CTX, DP))
    rows_count = rows_group.shape[0]
    arr_gate = jnp.einsum(
        "td,tes->eds",
        rows_group,
        gate_grad_s.reshape(rows_count, groups, -1),
        preferred_element_type=jnp.float32,
    ).reshape(groups * model_width, -1)
    arr_up = jnp.einsum(
        "td,tes->eds",
        rows_group,
        up_grad_s.reshape(rows_count, groups, -1),
        preferred_element_type=jnp.float32,
    ).reshape(groups * model_width, -1)
    arr_down = jnp.einsum(
        "tes,tcd->ecsd",
        shared_hidden.reshape(rows_count, groups, -1),
        grads_group.reshape(rows_count, parts_cd, -1),
        preferred_element_type=jnp.float32,
    ).reshape(-1, model_width // parts_cd)
    sums_gate, sums_up, sums_down = (
        lax.psum_scatter(arr_gate, (EXP, CTX, DP), scatter_dimension=0, tiled=True),
        lax.psum_scatter(arr_up, (EXP, CTX, DP), scatter_dimension=0, tiled=True),
        lax.psum_scatter(arr_down, (EXP, CTX, DP), scatter_dimension=0, tiled=True),
    )
    norm_grad = norm_grad + shared_rows_grad
    residual_grad, grad_gain_two = norm_back(residual, inv_two, g_two, norm_grad)
    residual_grad = residual_grad + cot_rows
    low_residual = residual_grad.astype(jnp.bfloat16)
    grad_out_w = jnp.dot(attended.T, low_residual, preferred_element_type=jnp.float32)
    attended_grad = jnp.dot(low_residual, out_w.T, preferred_element_type=jnp.float32).astype(
        jnp.bfloat16
    )
    head_q_grad, head_k_grad, head_v_grad = lax.map(
        partial(attend_back, allowed=allowed, scale_factor=scale_factor),
        (head_q, head_k, head_v, to_heads(attended_grad), log_total),
    )
    key_sum, value_sum = (
        lax.psum_scatter(from_heads(head_k_grad), CTX, scatter_dimension=0, tiled=True),
        lax.psum_scatter(from_heads(head_v_grad), CTX, scatter_dimension=0, tiled=True),
    )
    query_low = from_heads(head_q_grad).astype(jnp.bfloat16)
    key_low = key_sum.astype(jnp.bfloat16)
    value_low = value_sum.astype(jnp.bfloat16)
    grad_query = jnp.dot(normed_one.T, query_low, preferred_element_type=jnp.float32)
    grad_key = jnp.dot(normed_one.T, key_low, preferred_element_type=jnp.float32)
    grad_value = jnp.dot(normed_one.T, value_low, preferred_element_type=jnp.float32)
    normed_grad = jnp.dot(query_low, query_w.T, preferred_element_type=jnp.float32)
    normed_grad = normed_grad + jnp.dot(key_low, key_w.T, preferred_element_type=jnp.float32)
    normed_grad = normed_grad + jnp.dot(value_low, value_w.T, preferred_element_type=jnp.float32)
    input_part, grad_gain_one = norm_back(x_rows, inv_one, g_one, normed_grad)
    input_grad = (residual_grad + input_part).astype(jnp.bfloat16)
    dense = (
        lax.psum_scatter(
            grad_gain_one, (EXP, CTX, DP), scatter_dimension=0, tiled=True
        ),
        lax.psum_scatter(grad_query, (EXP, CTX, DP), scatter_dimension=0, tiled=True),
        lax.psum_scatter(grad_key, (EXP, CTX, DP), scatter_dimension=0, tiled=True),
        lax.psum_scatter(grad_value, (EXP, CTX, DP), scatter_dimension=0, tiled=True),
        lax.psum_scatter(grad_out_w, (EXP, CTX, DP), scatter_dimension=0, tiled=True),
        lax.psum_scatter(
            grad_gain_two, (EXP, CTX, DP), scatter_dimension=0, tiled=True
        ),
        lax.psum_scatter(
            grad_router, (EXP, CTX, DP), scatter_dimension=0, tiled=True
        ),
        lax.psum_scatter(
            grad_gate_vec, (EXP, CTX, DP), scatter_dimension=0, tiled=True
        ),
    )
    return (
        output[None],
        input_grad[None],
        dense[0],
        dense[1],
        dense[2],
        dense[3],
        dense[4],
        dense[5],
        dense[6],
        dense[7],
        sums_gate,
        sums_up,
        sums_down,
        expert_sums[0],
        expert_sums[1],
        expert_sums[2],
    )

def attention_probs(q_blk, k_part, q_code, k_code, first_row, scale_factor):
    scores = lax.dot_general(
        q_blk, k_part, (((1,), (1,)), ((), ())), preferred_element_type=jnp.float32
    )
    row = first_row + lax.broadcasted_iota(jnp.int32, scores.shape, 0)
    col = lax.broadcasted_iota(jnp.int32, scores.shape, 1)
    allowed = ((col < row) & (k_code == q_code)) | (col == row)
    logits = jnp.where(allowed, scores * scale_factor, NEG)
    exp_scores = jnp.exp(logits - jnp.max(logits, axis=1, keepdims=True))
    return exp_scores * (1.0 / jnp.sum(exp_scores, axis=1, keepdims=True))


def attend_kernel(heads, step, qkv_ref, q_code_ref, k_code_ref, out_ref):
    seq_len = qkv_ref.shape[0]
    width = heads * HEAD_DIM
    for head in range(heads):
        at = head * HEAD_DIM
        for first in range(0, seq_len, step):
            upto = first + step
            probs = attention_probs(
                qkv_ref[first:upto, at : at + HEAD_DIM],
                qkv_ref[0:upto, width + at : width + at + HEAD_DIM],
                q_code_ref[first:upto, :],
                k_code_ref[0, :, 0:upto],
                first,
                HEAD_DIM**-0.5,
            )
            out_ref[first:upto, at : at + HEAD_DIM] = jnp.dot(
                probs.astype(jnp.bfloat16),
                qkv_ref[0:upto, 2 * width + at : 2 * width + at + HEAD_DIM],
                preferred_element_type=jnp.float32,
            ).astype(jnp.bfloat16)


def attend_back_kernel(
    heads, step, qkv_ref, grad_ref, q_code_ref, k_code_ref, out_ref, key_acc, value_acc
):
    seq_len = qkv_ref.shape[0]
    width = heads * HEAD_DIM
    for head in range(heads):
        at = head * HEAD_DIM
        key_at, value_at = width + at, 2 * width + at
        key_acc[...] = jnp.zeros_like(key_acc)
        value_acc[...] = jnp.zeros_like(value_acc)
        for first in range(0, seq_len, step):
            upto = first + step
            q_blk = qkv_ref[first:upto, at : at + HEAD_DIM]
            k_part = qkv_ref[0:upto, key_at : key_at + HEAD_DIM]
            v_part = qkv_ref[0:upto, value_at : value_at + HEAD_DIM]
            g_blk = grad_ref[first:upto, at : at + HEAD_DIM]
            probs = attention_probs(
                q_blk,
                k_part,
                q_code_ref[first:upto, :],
                k_code_ref[0, :, 0:upto],
                first,
                HEAD_DIM**-0.5,
            )
            prob_grad = lax.dot_general(
                g_blk, v_part, (((1,), (1,)), ((), ())), preferred_element_type=jnp.float32
            )
            inner = jnp.sum(probs * prob_grad, axis=1, keepdims=True)
            score_grad = (probs * (prob_grad - inner) * HEAD_DIM**-0.5).astype(jnp.bfloat16)
            out_ref[first:upto, at : at + HEAD_DIM] = jnp.dot(
                score_grad, k_part, preferred_element_type=jnp.float32
            ).astype(jnp.bfloat16)
            key_acc[0:upto, :] += lax.dot_general(
                score_grad, q_blk, (((0,), (0,)), ((), ())), preferred_element_type=jnp.float32
            )
            value_acc[0:upto, :] += lax.dot_general(
                probs.astype(jnp.bfloat16),
                g_blk,
                (((0,), (0,)), ((), ())),
                preferred_element_type=jnp.float32,
            )
        out_ref[:, key_at : key_at + HEAD_DIM] = key_acc[...].astype(jnp.bfloat16)
        out_ref[:, value_at : value_at + HEAD_DIM] = value_acc[...].astype(jnp.bfloat16)


def attention_call(qkv, grads, q_codes, k_codes, seq_len):
    rows, triple = qkv.shape
    width = triple // 3
    heads = width // HEAD_DIM
    step = min(256, seq_len)
    specs = [pl.BlockSpec((seq_len, triple), lambda s: (s, 0))]
    operands = [qkv]
    if grads is not None:
        specs.append(pl.BlockSpec((seq_len, width), lambda s: (s, 0)))
        operands.append(grads)
    specs += [
        pl.BlockSpec((seq_len, 1), lambda s: (s, 0)),
        pl.BlockSpec((1, 1, seq_len), lambda s: (s, 0, 0)),
    ]
    operands += [q_codes, k_codes]
    out_width = width if grads is None else triple
    body = attend_kernel if grads is None else attend_back_kernel
    passes = 2 if grads is None else 5
    area = rows * seq_len * heads
    return pl.pallas_call(
        partial(body, heads, step),
        grid=(rows // seq_len,),
        in_specs=specs,
        out_specs=pl.BlockSpec((seq_len, out_width), lambda s: (s, 0)),
        out_shape=jax.ShapeDtypeStruct((rows, out_width), jnp.bfloat16),
        scratch_shapes=[]
        if grads is None
        else [pltpu.VMEM((seq_len, HEAD_DIM), jnp.float32)] * 2,
        compiler_params=pltpu.CompilerParams(vmem_limit_bytes=48 * 2**20),
        cost_estimate=pl.CostEstimate(
            flops=2 * passes * area * HEAD_DIM,
            bytes_accessed=2 * rows * (triple + out_width),
            transcendentals=area,
        ),
    )(*operands)


MESH_ID = pl.DeviceIdType.MESH


def other_in_pair(index, bit):
    return index + bit - 2 * bit * (lax.div(index, bit) % 2)


def plane_places():
    at = lax.axis_index(EXP)
    core = lax.axis_index(CTX)
    across, along = other_in_pair(at, 1), other_in_pair(at, 2)
    return at, core, across, along, other_in_pair(along, 1)


def greet(across, along, core):
    barrier = pltpu.get_barrier_semaphore()
    for target in ({EXP: across}, {EXP: along}, {CTX: 1 - core}):
        pl.semaphore_signal(barrier, inc=1, device_id=target, device_id_type=MESH_ID)
    pl.semaphore_wait(barrier, 3)


def plane_gather_kernel(with_info, relative, *refs):
    if with_info:
        own_ref, info_ref, all_ref, info_all_ref, send_sem, recv_sem, local_sem = refs
    else:
        own_ref, all_ref, send_sem, recv_sem, local_sem = refs
    at, core, across, along, far = plane_places()
    rows = own_ref.shape[0]
    half = rows // 2
    top, bottom, whole = pl.ds(0, half), pl.ds(half, half), pl.ds(0, rows)
    greet(across, along, core)
    started = []
    twin_id = {CTX: 1 - core}

    def slot_of(place, shift, for_twin):
        if relative:
            return shift + 4 * for_twin
        return place * 2 + core

    def send(number, src, dst, target):
        copy = pltpu.make_async_remote_copy(
            src_ref=src,
            dst_ref=dst,
            send_sem=send_sem.at[number],
            recv_sem=recv_sem.at[number],
            device_id=target,
            device_id_type=MESH_ID,
        )
        copy.start()
        started.append(copy)
        return copy

    def piece(place, shift, part, for_twin=0):
        return all_ref.at[slot_of(place, shift, for_twin), part]

    x_top = send(0, own_ref.at[top], piece(at, 1, top), {EXP: across})
    y_bottom = send(1, own_ref.at[bottom], piece(at, 2, bottom), {EXP: along})
    x_bottom = send(2, own_ref.at[bottom], piece(at, 1, bottom), {EXP: across})
    y_top = send(3, own_ref.at[top], piece(at, 2, top), {EXP: along})
    twins = [send(4, own_ref, piece(at, 0, whole, 1), twin_id)]
    heres = [pltpu.make_async_copy(own_ref, piece(at, 0, whole), local_sem.at[0])]
    heres[0].start()
    if with_info:
        info_at = lambda place: info_all_ref.at[place * 2 + core]
        heres.append(pltpu.make_async_copy(info_ref, info_at(at), local_sem.at[1]))
        heres[1].start()
        info_x = send(13, info_ref, info_at(at), {EXP: across})
        info_y = send(14, info_ref, info_at(at), {EXP: along})
        twins.append(send(15, info_ref, info_at(at), twin_id))
        info_x.wait_recv()
        info_far = send(16, info_at(across), info_at(across), {EXP: along})
        twins.append(send(17, info_at(across), info_at(across), twin_id))
        info_y.wait_recv()
        twins.append(send(18, info_at(along), info_at(along), twin_id))
        info_far.wait_recv()
        twins.append(send(19, info_at(far), info_at(far), twin_id))

    def hand_on(number, place, shift, part):
        src = piece(place, shift, part)
        twins.append(send(number, src, piece(place, shift, part, 1), twin_id))

    x_top.wait_recv()
    far_top = send(5, piece(across, 1, top), piece(across, 3, top), {EXP: along})
    hand_on(6, across, 1, top)
    y_bottom.wait_recv()
    far_bottom = send(7, piece(along, 2, bottom), piece(along, 3, bottom), {EXP: across})
    hand_on(8, along, 2, bottom)
    x_bottom.wait_recv()
    hand_on(9, across, 1, bottom)
    y_top.wait_recv()
    hand_on(10, along, 2, top)
    far_top.wait_recv()
    hand_on(11, far, 3, top)
    far_bottom.wait_recv()
    hand_on(12, far, 3, bottom)
    for copy in twins:
        copy.wait_recv()
    for copy in started:
        copy.wait_send()
    for copy in heres:
        copy.wait()


def plane_gather(own, info, relative, number):
    plane = lax.axis_size(PLANE)
    operands = [own] if info is None else [own, info]
    outs = [jax.ShapeDtypeStruct((plane, *v.shape), v.dtype) for v in operands]
    anywhere = pl.BlockSpec(memory_space=pl.ANY)
    return pl.pallas_call(
        partial(plane_gather_kernel, info is not None, relative),
        out_shape=outs,
        in_specs=[anywhere] * len(operands),
        out_specs=[anywhere] * len(operands),
        scratch_shapes=[
            pltpu.SemaphoreType.DMA((20,)),
            pltpu.SemaphoreType.DMA((20,)),
            pltpu.SemaphoreType.DMA((2,)),
        ],
        compiler_params=pltpu.CompilerParams(collective_id=number, has_side_effects=True),
        cost_estimate=pl.CostEstimate(
            flops=0, bytes_accessed=100 * own.size, transcendentals=0
        ),
    )(*operands)


def plane_scatter_kernel(
    relative,
    part_ref,
    out_ref,
    own,
    twin_got,
    x_got,
    y_got,
    x_last,
    y_last,
    send_sem,
    recv_sem,
    local_sem,
):
    at, core, across, along, far = plane_places()
    rows = part_ref.shape[1]
    half = rows // 2
    step = 64
    greet(across, along, core)
    started = []

    def send(number, src, dst, target):
        copy = pltpu.make_async_remote_copy(
            src_ref=src,
            dst_ref=dst,
            send_sem=send_sem.at[number],
            recv_sem=recv_sem.at[number],
            device_id=target,
            device_id_type=MESH_ID,
        )
        copy.start()
        started.append(copy)
        return copy

    twins, heres = [], []
    for j, (label, shift) in enumerate(((far, 3), (across, 1), (along, 2), (at, 0))):
        theirs = shift + 4 if relative else label * 2 + 1 - core
        ours = shift if relative else label * 2 + core
        twins.append(send(j, part_ref.at[theirs], twin_got.at[j], {CTX: 1 - core}))
        here = pltpu.make_async_copy(part_ref.at[ours], own.at[j], local_sem.at[j])
        here.start()
        heres.append(here)

    def add_rows(target, t_first, count, source, s_first):
        @pl.loop(0, count // step)
        def _(i):
            into = pl.ds(pl.multiple_of(t_first + i * step, step), step)
            take = pl.ds(pl.multiple_of(s_first + i * step, step), step)
            total = target[into].astype(jnp.float32) + source[take].astype(jnp.float32)
            target[into] = total.astype(target.dtype)

    top, bottom = pl.ds(0, half), pl.ds(half, half)
    x_sent, y_sent = [], []
    for j in range(4):
        twins[j].wait_recv()
        heres[j].wait()
        add_rows(own.at[j], 0, rows, twin_got.at[j], 0)
        if j < 2:
            x_sent.append(send(4 + j, own.at[j, top], x_got.at[j], {EXP: across}))
        if j == 0 or j == 2:
            y_sent.append(send(6 + j // 2, own.at[j, bottom], y_got.at[j // 2], {EXP: along}))
    x_sent[0].wait_recv()
    add_rows(own.at[2], 0, half, x_got.at[0], 0)
    last_y = send(8, own.at[2, top], y_last, {EXP: along})
    y_sent[0].wait_recv()
    add_rows(own.at[1], half, half, y_got.at[0], 0)
    last_x = send(9, own.at[1, bottom], x_last, {EXP: across})

    def finish(first, near, later):
        @pl.loop(0, half // step)
        def _(i):
            take = pl.ds(pl.multiple_of(i * step, step), step)
            into = pl.ds(pl.multiple_of(first + i * step, step), step)
            out_ref[into] = (
                own[3, into].astype(jnp.float32)
                + near[1, take].astype(jnp.float32)
                + later[take].astype(jnp.float32)
            ).astype(out_ref.dtype)

    x_sent[1].wait_recv()
    last_y.wait_recv()
    finish(0, x_got, y_last)
    y_sent[1].wait_recv()
    last_x.wait_recv()
    finish(half, y_got, x_last)
    for copy in started:
        copy.wait_send()


def plane_scatter(parts, relative, number, out_type):
    plane, rows, cols = parts.shape
    half = rows // 2
    vmem = lambda *shape: pltpu.VMEM(shape, parts.dtype)
    return pl.pallas_call(
        partial(plane_scatter_kernel, relative),
        out_shape=jax.ShapeDtypeStruct((rows, cols), out_type),
        in_specs=[pl.BlockSpec(memory_space=pl.ANY)],
        out_specs=pl.BlockSpec(memory_space=pltpu.VMEM),
        scratch_shapes=[
            vmem(4, rows, cols),
            vmem(4, rows, cols),
            vmem(2, half, cols),
            vmem(2, half, cols),
            vmem(half, cols),
            vmem(half, cols),
            pltpu.SemaphoreType.DMA((10,)),
            pltpu.SemaphoreType.DMA((10,)),
            pltpu.SemaphoreType.DMA((4,)),
        ],
        compiler_params=pltpu.CompilerParams(
            collective_id=number, has_side_effects=True, vmem_limit_bytes=44 * 2**20
        ),
        cost_estimate=pl.CostEstimate(
            flops=0, bytes_accessed=100 * rows * cols, transcendentals=0
        ),
    )(parts)


def swap(values, bits):
    return lax.ppermute(values, EXP, [(i, i ^ bits) for i in range(4)])


def twin(values):
    return lax.ppermute(values, CTX, [(0, 1), (1, 0)])


def hop_sum(ours, theirs):
    got = twin(theirs)
    sums = [
        low(ours[k].astype(jnp.float32) + got[k].astype(jnp.float32)) for k in range(4)
    ]
    total = sums[0].astype(jnp.float32)
    for k in (1, 2, 3):
        total = total + swap(sums[k], k).astype(jnp.float32)
    return total


def mm(left, right, dims=((1,), (0,))):
    return lax.dot_general(left, right, (dims, ((), ())), preferred_element_type=jnp.float32)


def low(values):
    return values.astype(jnp.bfloat16)


def local_plane(
    hidden,
    cotangent,
    segments,
    padding,
    routes,
    order,
    norm1_gain,
    w_query,
    w_key,
    w_value,
    w_out,
    norm2_gain,
    router,
    shared_gate_vec,
    shared_w_gate,
    shared_w_up,
    shared_w_down,
    expert_w_gate,
    expert_w_up,
    expert_w_down,
):
    plane = lax.axis_size(PLANE)
    groups = lax.axis_size(EXP)
    halves = lax.axis_size(CTX)
    depth = lax.axis_size(DP)
    me = lax.axis_index(PLANE)
    core = lax.axis_index(CTX)
    tokens, width = hidden.shape[1], hidden.shape[2]
    all_tokens = plane * tokens
    seq_len = halves * tokens
    experts_all = router.shape[1]
    head_cols = width // plane
    shard = width // depth

    token_info = jnp.concatenate(
        [segments + 1, jnp.where(padding > 0, segments + 1, 0), order[0], routes[0].T]
    )
    info_rows = token_info.shape[0]
    token_info = jnp.concatenate([token_info, jnp.zeros((8 - info_rows, tokens), jnp.int32)])

    hidden_all, info_all = plane_gather(hidden[0], token_info, False, 0)
    hidden_all = hidden_all.reshape(all_tokens, width)
    place = lax.axis_index(EXP)
    away = [(place ^ k) * 2 + (core ^ j) for j in (0, 1) for k in range(4)]
    away = jnp.stack(away)
    cot_own, _ = lax.optimization_barrier((cotangent[0], info_all))
    cot_near = jnp.stack([cot_own, swap(cot_own, 1), swap(cot_own, 2), swap(cot_own, 3)])
    cot_all = jnp.concatenate([cot_near, twin(cot_near)]).reshape(all_tokens, width)
    w_qkv_part = jnp.concatenate(
        [
            lax.dynamic_slice(w, (0, me * head_cols), (shard, head_cols))
            for w in (w_query, w_key, w_value)
        ]
        + [router, norm1_gain[:, None], norm2_gain[:, None], shared_gate_vec[:, None]]
        + [jnp.zeros((shard, 128 - experts_all - 3), jnp.bfloat16)],
        axis=1,
    )
    w_qkv = lax.all_gather(w_qkv_part, DP, axis=0, tiled=True)
    small = w_qkv[:, 3 * head_cols :].T
    w_qkv = w_qkv[:, : 3 * head_cols]
    router_t = small[:experts_all]
    g_one = small[experts_all].astype(jnp.float32)
    g_two = small[experts_all + 1].astype(jnp.float32)
    gate_vec = small[experts_all + 2]
    out_rows = shard // plane
    w_out_part = lax.dynamic_slice(w_out, (me * out_rows, 0), (out_rows, width))
    w_out_part = lax.all_gather(w_out_part, DP, axis=0, tiled=False)
    pieces = [w_out_part] + [swap(w_out_part, k) for k in (1, 2, 3)]
    w_out_near = jnp.zeros((depth, groups, 1, out_rows, width), jnp.bfloat16)
    for k in range(4):
        w_out_near = lax.dynamic_update_slice(
            w_out_near, pieces[k][:, None, None], (0, place ^ k, 0, 0, 0)
        )
    w_out_far = twin(w_out_near)
    w_out_full = jnp.where(
        core == 0,
        jnp.concatenate([w_out_near, w_out_far], axis=2),
        jnp.concatenate([w_out_far, w_out_near], axis=2),
    ).reshape(width, width)

    def normed(values, gain):
        values = values.astype(jnp.float32)
        inv = lax.rsqrt(jnp.mean(values * values, axis=1, keepdims=True) + EPS)
        return values, inv, low(values * inv * gain)

    _, _, n1_all = normed(hidden_all, g_one)
    x_rows, inv_one, _ = normed(hidden[0], g_one)
    cot_rows = cotangent[0].astype(jnp.float32)
    qkv = low(mm(n1_all, w_qkv))
    q_codes = info_all[:, 0].reshape(all_tokens, 1)
    k_codes = info_all[:, 1].reshape(all_tokens // seq_len, 1, seq_len)
    attended_cols = attention_call(qkv, None, q_codes, k_codes, seq_len)

    def to_tokens(cols):
        got = lax.all_to_all(
            cols.reshape(plane, tokens, head_cols), PLANE, split_axis=0, concat_axis=0, tiled=True
        )
        return got.transpose(1, 0, 2).reshape(tokens, width)

    def to_columns(rows_in):
        send = rows_in.reshape(tokens, plane, head_cols).transpose(1, 0, 2)
        got = lax.all_to_all(send, PLANE, split_axis=0, concat_axis=0, tiled=True)
        return got.reshape(all_tokens, head_cols)

    attended = to_tokens(attended_cols)
    residual = x_rows + mm(attended, w_out_full)
    residual, inv_two, n2 = normed(residual, g_two)

    n2, cot_all = lax.optimization_barrier((n2, cot_all))
    n2_all = plane_gather(n2, None, True, 2)[0].reshape(all_tokens, width)
    units = shared_w_gate.shape[1]
    part = units // (depth * halves)
    pick = lambda w: lax.dynamic_index_in_dim(
        w.reshape(w.shape[0], depth, halves, part), core, axis=2, keepdims=False
    ).reshape(w.shape[0], depth * part)
    sh_gate = lax.all_gather(pick(shared_w_gate), DP, axis=0, tiled=True)
    sh_up = lax.all_gather(pick(shared_w_up), DP, axis=0, tiled=True)
    sh_down = lax.all_gather(
        lax.dynamic_slice(shared_w_down, (core * part, 0), (part, width)), DP, axis=0, tiled=True
    )
    ex_gate = lax.all_gather(expert_w_gate[0], DP, axis=0, tiled=True)
    ex_up = lax.all_gather(expert_w_up[0], DP, axis=0, tiled=True)
    ex_down = lax.all_gather(expert_w_down[0], DP, axis=1, tiled=True)

    small_w = jnp.concatenate([router_t, gate_vec[None]])

    def gates_of(rows_in):
        both = mm(rows_in, small_w, ((1,), (1,)))
        z = both[:, :experts_all]
        e = jnp.exp(z - jnp.max(z, axis=1, keepdims=True))
        return e / jnp.sum(e, axis=1, keepdims=True), jax.nn.sigmoid(both[:, experts_all:])

    probs_all, sg_all = gates_of(n2_all)
    expert_gate = lax.dynamic_slice(probs_all, (0, me), (all_tokens, 1))

    capacity = (9 * tokens * TOP + 8 * experts_all - 1) // (8 * experts_all)
    info_away = info_all[away]
    order_all = info_away[:, 2]
    routed_here = jnp.any(info_away[:, 3 : 3 + TOP] == me, axis=1)
    earlier = (order_all[:, None, :] < order_all[:, :, None]) & routed_here[:, None, :]
    slots = jnp.sum(earlier.astype(jnp.int32), axis=2)
    slots = jnp.where(routed_here, slots, capacity)
    chosen = slots[:, None, :] == jnp.arange(capacity, dtype=jnp.int32)[None, :, None]
    onehot = chosen.astype(jnp.bfloat16)

    def rows_of(values):
        got = lax.dot_general(
            onehot,
            values.reshape(plane, tokens, width),
            (((2,), (1,)), ((0,), (0,))),
            preferred_element_type=jnp.float32,
        )
        return got.reshape(plane * capacity, width)

    def back_to_tokens(values):
        got = lax.dot_general(
            onehot,
            values.reshape(plane, capacity, width),
            (((1,), (1,)), ((0,), (0,))),
            preferred_element_type=jnp.float32,
        )
        return got.reshape(all_tokens, width)

    slot_gates = jnp.sum(
        jnp.where(chosen, expert_gate.reshape(plane, 1, tokens), 0.0), axis=2
    ).reshape(plane * capacity, 1)
    expert_rows = low(rows_of(n2_all))
    row_cots = low(rows_of(cot_all))
    row_grads = low(row_cots.astype(jnp.float32) * slot_gates)

    shared_grads = low(sg_all * cot_all.astype(jnp.float32))
    gate_pre = mm(n2_all, sh_gate)
    up_pre = mm(n2_all, sh_up)
    gate_act = gate_pre * jax.nn.sigmoid(gate_pre)
    shared_hidden = low(gate_act * up_pre)
    shared_part = mm(shared_hidden, sh_down)
    cot_dot_shared = jnp.sum(shared_part * cot_all.astype(jnp.float32), axis=1)
    shared_hgrad = mm(shared_grads, sh_down, ((1,), (1,)))
    gate_grad_s = low(shared_hgrad * up_pre * silu_grad(gate_pre))
    up_grad_s = low(shared_hgrad * gate_act)

    rows_out = width // (halves * depth)

    def own_units(grad):
        grad = low(grad).reshape(depth * part, halves, depth, rows_out).transpose(2, 0, 1, 3)
        return grad.reshape(depth * depth * part, halves * rows_out)

    def shared_scatter(grad):
        total = lax.psum_scatter(grad, DP, scatter_dimension=0, tiled=True)
        total = total.reshape(depth * part, halves, rows_out)
        keep = lax.dynamic_index_in_dim(total, core, axis=1, keepdims=False)
        give = lax.dynamic_index_in_dim(total, 1 - core, axis=1, keepdims=False)
        both = jnp.stack([keep, twin(give)]).reshape(halves, depth, part, rows_out)
        both = jnp.where(core == 0, both, both[::-1]).transpose(1, 0, 2, 3)
        return both.reshape(units, rows_out).astype(jnp.float32)

    grad_sh_gate = own_units(mm(gate_grad_s, n2_all, ((0,), (0,))))
    grad_sh_up = own_units(mm(up_grad_s, n2_all, ((0,), (0,))))
    grad_sh_down = own_units(mm(shared_hidden, shared_grads, ((0,), (0,))))

    gate_e = mm(expert_rows, ex_gate)
    up_e = mm(expert_rows, ex_up)
    act_e = gate_e * jax.nn.sigmoid(gate_e)
    hidden_e = low(act_e * up_e)
    result_e = low(mm(hidden_e, ex_down))
    row_dots = jnp.sum(result_e.astype(jnp.float32) * row_cots.astype(jnp.float32), axis=1)
    gate_dots = jnp.sum(
        jnp.where(chosen, row_dots.reshape(plane, capacity, 1), 0.0), axis=1
    )
    hgrad_e = mm(row_grads, ex_down, ((1,), (1,)))
    gate_grad_e = low(hgrad_e * up_e * silu_grad(gate_e))
    up_grad_e = low(hgrad_e * act_e)

    def expert_scatter(grad, dim):
        return lax.psum_scatter(grad, DP, scatter_dimension=dim, tiled=True).astype(
            jnp.float32
        )[None]

    grad_ex_down = low(mm(hidden_e, row_grads, ((0,), (0,))))
    grad_ex_gate = low(mm(expert_rows, gate_grad_e, ((0,), (0,))))
    grad_ex_up = low(mm(expert_rows, up_grad_e, ((0,), (0,))))
    rows_grad = low(
        mm(gate_grad_e, ex_gate, ((1,), (1,))) + mm(up_grad_e, ex_up, ((1,), (1,)))
    )

    out_part = low(sg_all * shared_part + expert_gate * back_to_tokens(result_e))
    out_part = out_part.reshape(plane, tokens, width)
    output = low(residual + hop_sum(out_part[:4], out_part[4:]))
    n2_grad_part = low(
        mm(gate_grad_s, sh_gate, ((1,), (1,)))
        + mm(up_grad_s, sh_up, ((1,), (1,)))
        + back_to_tokens(rows_grad)
    )
    grads = (grad_sh_gate, grad_sh_up, grad_sh_down, grad_ex_down, grad_ex_gate, grad_ex_up)
    n2_grad_part, grads = lax.optimization_barrier((n2_grad_part, grads))
    grad_sh_gate, grad_sh_up, grad_sh_down = [shared_scatter(v) for v in grads[:3]]
    grad_sh_gate, grad_sh_up = grad_sh_gate.T, grad_sh_up.T
    grad_ex_down = expert_scatter(grads[3], 1)
    grad_ex_gate, grad_ex_up = [expert_scatter(v, 0) for v in grads[4:]]
    n2_grad = plane_scatter(n2_grad_part.reshape(plane, tokens, width), True, 3, jnp.float32)

    dots = jnp.stack([gate_dots, cot_dot_shared.reshape(plane, tokens)], axis=1)
    back = jnp.arange(plane, dtype=jnp.int32) ^ me
    dots = dots[(back // 2) + 4 * (back % 2)]
    dots = lax.all_to_all(dots, PLANE, split_axis=0, concat_axis=0, tiled=True)
    probs_grad = dots[:, 0].T
    probs, sg = gates_of(n2)
    logit_grad = low(probs * (probs_grad - jnp.sum(probs * probs_grad, axis=1, keepdims=True)))
    sg_logit_grad = low(jnp.sum(dots[:, 1], axis=0)[:, None] * sg * (1.0 - sg))
    small_grads = mm(n2, jnp.concatenate([logit_grad, sg_logit_grad], axis=1), ((0,), (0,)))
    n2_grad = (
        n2_grad
        + mm(logit_grad, router_t)
        + sg_logit_grad.astype(jnp.float32) * gate_vec.astype(jnp.float32)[None]
    )
    residual_grad, grad_gain_two = norm_back(residual, inv_two, g_two, n2_grad)
    residual_grad = residual_grad + cot_rows
    low_residual = low(residual_grad)

    small_grads = jnp.concatenate([small_grads, grad_gain_two[:, None]], axis=1).T
    small_grads = jnp.pad(small_grads, ((0, 14 - experts_all), (0, 0)))
    small_grads = small_grads.reshape(16, plane, width // plane).transpose(1, 0, 2)
    small_grads = jnp.sum(
        lax.all_to_all(small_grads, PLANE, split_axis=0, concat_axis=0, tiled=True), axis=0
    )
    small_grads = small_grads.reshape(16, depth, shard // plane).transpose(1, 0, 2)
    small_grads = jnp.sum(
        lax.all_to_all(small_grads, DP, split_axis=0, concat_axis=0, tiled=True), axis=0
    )
    grad_out = low(mm(attended, low_residual, ((0,), (0,))))
    grad_out = grad_out.reshape(groups, halves, width // plane, width)
    block_of = lambda k, c: lax.dynamic_slice(
        grad_out, (place ^ k, c, 0, 0), (1, 1, width // plane, width)
    )[0, 0]
    grad_out = low(
        hop_sum(
            [block_of(k, core) for k in range(4)],
            jnp.stack([block_of(k, 1 - core) for k in range(4)]),
        )
    )
    grad_out = lax.psum_scatter(grad_out, DP, scatter_dimension=0, tiled=True).astype(jnp.float32)
    attended_grad = to_columns(low(mm(low_residual, w_out_full, ((1,), (1,)))))
    qkv_grad = attention_call(qkv, attended_grad, q_codes, k_codes, seq_len)
    n1_grad = low(mm(qkv_grad, w_qkv, ((1,), (1,))))
    n1_grad = plane_scatter(n1_grad.reshape(plane, tokens, width), False, 1, jnp.float32)
    grad_qkv = low(mm(n1_all, qkv_grad, ((0,), (0,))))
    fine = shard // plane
    grad_qkv = (
        grad_qkv.reshape(plane, depth, fine, 3 * head_cols)
        .transpose(1, 0, 2, 3)
        .reshape(width, 3 * head_cols)
    )
    grad_qkv = lax.psum_scatter(grad_qkv, DP, scatter_dimension=0, tiled=True)
    w_rows = (
        w_qkv.reshape(plane, depth, fine, 3 * head_cols)
        .transpose(1, 0, 2, 3)
        .reshape(depth, plane * fine, 3 * head_cols)
    )
    w_rows = lax.dynamic_index_in_dim(w_rows, lax.axis_index(DP), axis=0, keepdims=False)
    gain_dots = jnp.sum(grad_qkv.astype(jnp.float32) * w_rows.astype(jnp.float32), axis=1)
    gain_dots = lax.all_to_all(
        gain_dots.reshape(plane, 1, fine), PLANE, split_axis=0, concat_axis=0, tiled=True
    )
    my_gain = lax.dynamic_slice(
        g_one, ((me * depth + lax.axis_index(DP)) * fine,), (fine,)
    )
    grad_gain_one = jnp.sum(gain_dots[:, 0], axis=0) / my_gain
    grad_qkv = lax.all_to_all(
        grad_qkv.reshape(plane, fine, 3 * head_cols),
        PLANE,
        split_axis=0,
        concat_axis=0,
        tiled=True,
    )
    grad_qkv = (
        grad_qkv.reshape(plane, fine, 3, head_cols)
        .transpose(2, 1, 0, 3)
        .reshape(3, fine, width)
        .astype(jnp.float32)
    )
    input_part, _ = norm_back(x_rows, inv_one, g_one, n1_grad)
    input_grad = low(residual_grad + input_part)
    return (
        output[None],
        input_grad[None],
        grad_gain_one,
        grad_qkv[0],
        grad_qkv[1],
        grad_qkv[2],
        grad_out,
        small_grads[experts_all + 1],
        small_grads[:experts_all].T,
        small_grads[experts_all],
        grad_sh_gate,
        grad_sh_up,
        grad_sh_down,
        grad_ex_gate,
        grad_ex_up,
        grad_ex_down,
    )


def solution(mesh):
    in_specs = (
        P((EXP, DP), CTX, None),
        P((EXP, DP), CTX, None),
        P((EXP, DP), CTX),
        P((EXP, DP), CTX),
        P((EXP, DP), CTX, None),
        P((EXP, DP), CTX, None),
        P(DP),
        P(DP, None),
        P(DP, None),
        P(DP, None),
        P(DP, None),
        P(DP),
        P(DP, None),
        P(DP),
        P(DP, EXP),
        P(DP, EXP),
        P((EXP, DP), None),
        P((EXP, CTX), DP, None),
        P((EXP, CTX), DP, None),
        P((EXP, CTX), None, DP),
    )
    out_specs = (
        P((EXP, DP), CTX, None),
        P((EXP, DP), CTX, None),
        P((EXP, CTX, DP)),
        P((EXP, CTX, DP), None),
        P((EXP, CTX, DP), None),
        P((EXP, CTX, DP), None),
        P((EXP, CTX, DP), None),
        P((EXP, CTX, DP)),
        P((EXP, CTX, DP), None),
        P((EXP, CTX, DP)),
        P((CTX, DP), EXP),
        P((CTX, DP), EXP),
        P(EXP, (CTX, DP)),
        P((EXP, CTX), DP, None),
        P((EXP, CTX), DP, None),
        P((EXP, CTX), None, DP),
    )
    plane = mesh.shape[EXP] * mesh.shape[CTX]

    def run(*args):
        square = mesh.shape[EXP] == 4 and mesh.shape[CTX] == 2
        one_each = square and args[12].shape[1] == plane
        local = local_plane if one_each else local_general
        return jax.shard_map(
            local, mesh=mesh, in_specs=in_specs, out_specs=out_specs, check_vma=False
        )(*args)

    return run
```

```python
from functools import partial

import jax
import jax.numpy as jnp
from jax import lax
from jax.experimental import pallas as pl
from jax.experimental.pallas import tpu as pltpu
from jax.sharding import PartitionSpec as P

EXP, CTX, DP = "experts", "context", "dp"
PLANE = (EXP, CTX)
HEADS = 16
HEAD_DIM = 128
TOP = 4


EPS = 1e-06
NEG = -1e30


def silu_grad(pre_act):
    logistic = jax.nn.sigmoid(pre_act)
    return logistic * (1.0 + pre_act * (1.0 - logistic))


def block_slots(route_row, priority, expert_count):
    matches = (route_row[:, None] == jnp.arange(expert_count, dtype=jnp.int32)[None, :]).astype(
        jnp.int32
    )
    ordered = jnp.zeros_like(matches).at[priority].set(matches)
    before = jnp.cumsum(ordered, axis=0) - ordered
    return jnp.sum(before[priority] * matches, axis=1)


def norm_back(values_in, inv_rms, gain_vec, gradient):
    weighted = gradient * gain_vec
    inner_sum = jnp.mean(weighted * values_in, axis=1, keepdims=True)
    d_value = inv_rms * weighted - values_in * inv_rms**3 * inner_sum
    d_gain = jnp.sum(gradient * values_in * inv_rms, axis=0)
    return (d_value, d_gain)


def attend_head(packed, allowed, scale_factor):
    query_h, key_h, value_h = packed
    raw_scores = jnp.einsum("th,lh->tl", query_h, key_h, preferred_element_type=jnp.float32)
    logits = jnp.where(allowed, raw_scores * scale_factor, NEG)
    row_max = jnp.max(logits, axis=1, keepdims=True)
    exp_scores = jnp.exp(logits - row_max)
    row_total = jnp.sum(exp_scores, axis=1, keepdims=True)
    attn_probs = (exp_scores / row_total).astype(jnp.bfloat16)
    head_out = jnp.dot(attn_probs, value_h, preferred_element_type=jnp.float32).astype(jnp.bfloat16)
    return (head_out, row_max + jnp.log(row_total))


def attend_back(packed, allowed, scale_factor):
    query_h, key_h, value_h, out_grad, log_total = packed
    raw_scores = jnp.einsum("th,lh->tl", query_h, key_h, preferred_element_type=jnp.float32)
    logits = jnp.where(allowed, raw_scores * scale_factor, NEG)
    attn_probs = jnp.exp(logits - log_total)
    prob_grad = jnp.einsum("th,lh->tl", out_grad, value_h, preferred_element_type=jnp.float32)
    inner_sum = jnp.sum(attn_probs * prob_grad, axis=1, keepdims=True)
    score_grad = (attn_probs * (prob_grad - inner_sum) * scale_factor).astype(jnp.bfloat16)
    query_grad = jnp.dot(score_grad, key_h, preferred_element_type=jnp.float32)
    key_grad = jnp.einsum("tl,th->lh", score_grad, query_h, preferred_element_type=jnp.float32)
    value_grad = jnp.einsum(
        "tl,th->lh", attn_probs.astype(jnp.bfloat16), out_grad, preferred_element_type=jnp.float32
    )
    return (query_grad, key_grad, value_grad)


def local_general(
    hidden,
    cotangent,
    segments,
    padding,
    routes,
    order,
    norm1_gain,
    w_query,
    w_key,
    w_value,
    w_out,
    norm2_gain,
    router,
    shared_gate_vec,
    shared_w_gate,
    shared_w_up,
    shared_w_down,
    expert_w_gate,
    expert_w_up,
    expert_w_down,
):
    fetched = (
        lax.all_gather(norm1_gain, DP, axis=0, tiled=True),
        lax.all_gather(w_query, DP, axis=0, tiled=True),
        lax.all_gather(w_key, DP, axis=0, tiled=True),
        lax.all_gather(w_value, DP, axis=0, tiled=True),
        lax.all_gather(w_out, DP, axis=0, tiled=True),
        lax.all_gather(norm2_gain, DP, axis=0, tiled=True),
        lax.all_gather(router, DP, axis=0, tiled=True),
        lax.all_gather(shared_gate_vec, DP, axis=0, tiled=True),
        lax.all_gather(shared_w_gate, DP, axis=0, tiled=True),
        lax.all_gather(shared_w_up, DP, axis=0, tiled=True),
        lax.all_gather(shared_w_down, DP, axis=0, tiled=True),
        lax.all_gather(expert_w_gate, DP, axis=1, tiled=True),
        lax.all_gather(expert_w_up, DP, axis=1, tiled=True),
        lax.all_gather(expert_w_down, DP, axis=2, tiled=True),
    )
    (
        gain_one,
        query_w,
        key_w,
        value_w,
        out_w,
        gain_two,
        router_full,
        gate_vec,
        sh_gate,
        sh_up,
        sh_down,
        ex_gate,
        ex_up,
        ex_down,
    ) = fetched
    sh_gate, sh_up, sh_down = (
        lax.all_gather(sh_gate, EXP, axis=1, tiled=True),
        lax.all_gather(sh_up, EXP, axis=1, tiled=True),
        lax.all_gather(sh_down, EXP, axis=0, tiled=True),
    )
    tokens_here = hidden.shape[1]
    model_width = hidden.shape[2]
    x_rows = hidden[0].astype(jnp.float32)
    cot_rows = cotangent[0].astype(jnp.float32)
    inv_one = lax.rsqrt(jnp.mean(x_rows * x_rows, axis=1, keepdims=True) + EPS)
    g_one = gain_one.astype(jnp.float32)
    normed_one = (x_rows * inv_one * g_one).astype(jnp.bfloat16)
    queries = jnp.dot(normed_one, query_w, preferred_element_type=jnp.float32).astype(jnp.bfloat16)
    keys_own = jnp.dot(normed_one, key_w, preferred_element_type=jnp.float32).astype(jnp.bfloat16)
    values_own = jnp.dot(normed_one, value_w, preferred_element_type=jnp.float32).astype(
        jnp.bfloat16
    )
    own_codes = jnp.where(padding[0] > 0, segments[0] + 1, 0)
    code_parts = jnp.stack([own_codes // 64, own_codes % 64]).astype(jnp.bfloat16)
    keys_all, values_all, parts_all = (
        lax.all_gather(keys_own, CTX, axis=0, tiled=True),
        lax.all_gather(values_own, CTX, axis=0, tiled=True),
        lax.all_gather(code_parts, CTX, axis=1, tiled=True),
    )
    key_codes = parts_all[0].astype(jnp.int32) * 64 + parts_all[1].astype(jnp.int32)
    seq_total = keys_all.shape[0]
    query_pos = lax.axis_index(CTX) * tokens_here + jnp.arange(tokens_here, dtype=jnp.int32)
    key_pos = jnp.arange(seq_total, dtype=jnp.int32)
    same_doc = key_codes[None, :] == (segments[0] + 1)[:, None]
    allowed = (key_pos[None, :] <= query_pos[:, None]) & (
        same_doc | (key_pos[None, :] == query_pos[:, None])
    )
    scale_factor = HEAD_DIM ** (-0.5)

    def to_heads(rows_in):
        return rows_in.reshape(rows_in.shape[0], HEADS, HEAD_DIM).transpose(1, 0, 2)

    def from_heads(heads_in):
        return heads_in.transpose(1, 0, 2).reshape(heads_in.shape[1], model_width)

    head_q = to_heads(queries)
    head_k = to_heads(keys_all)
    head_v = to_heads(values_all)
    head_out, log_total = lax.map(
        partial(attend_head, allowed=allowed, scale_factor=scale_factor), (head_q, head_k, head_v)
    )
    attended = from_heads(head_out)
    residual = x_rows + jnp.dot(attended, out_w, preferred_element_type=jnp.float32)
    inv_two = lax.rsqrt(jnp.mean(residual * residual, axis=1, keepdims=True) + EPS)
    g_two = gain_two.astype(jnp.float32)
    normed_two = (residual * inv_two * g_two).astype(jnp.bfloat16)
    router_logits = jnp.dot(normed_two, router_full, preferred_element_type=jnp.float32)
    router_exp = jnp.exp(router_logits - jnp.max(router_logits, axis=1, keepdims=True))
    router_probs = router_exp / jnp.sum(router_exp, axis=1, keepdims=True)
    route_gates = jnp.take_along_axis(router_probs, routes[0], axis=1)
    shared_gate = jax.nn.sigmoid(jnp.dot(normed_two, gate_vec, preferred_element_type=jnp.float32))
    shared_scaled = (shared_gate[:, None] * cot_rows).astype(jnp.bfloat16)
    rows_group, grads_group = (normed_two, shared_scaled)
    gate_pre = jnp.dot(rows_group, sh_gate, preferred_element_type=jnp.float32)
    up_pre = jnp.dot(rows_group, sh_up, preferred_element_type=jnp.float32)
    gate_act = gate_pre * jax.nn.sigmoid(gate_pre)
    shared_hidden = (gate_act * up_pre).astype(jnp.bfloat16)
    shared_part = jnp.dot(shared_hidden, sh_down, preferred_element_type=jnp.float32)
    experts_all = router_full.shape[1]
    capacity = (9 * tokens_here * TOP + 8 * experts_all - 1) // (8 * experts_all)
    priority = (order[0, 0][:, None] * TOP + jnp.arange(TOP, dtype=jnp.int32)[None, :]).reshape(-1)
    flat_routes = routes[0].reshape(-1)
    slot_index = block_slots(flat_routes, priority, experts_all)
    kept_rows = slot_index < capacity
    target = flat_routes * capacity + jnp.minimum(slot_index, capacity - 1)
    row_gates = route_gates.reshape(-1)
    cot_repeated = jnp.repeat(cot_rows, TOP, axis=0)
    source_rows = jnp.repeat(normed_two, TOP, axis=0)
    source_grads = (cot_repeated * row_gates[:, None]).astype(jnp.bfloat16)
    empty_slots = jnp.zeros((experts_all * capacity, model_width), jnp.bfloat16)
    send_rows = empty_slots.at[target].add(
        jnp.where(kept_rows[:, None], source_rows, jnp.zeros_like(source_rows))
    )
    send_grads = empty_slots.at[target].add(
        jnp.where(kept_rows[:, None], source_grads, jnp.zeros_like(source_grads))
    )
    recv_rows, recv_grads = (
        lax.all_to_all(
            send_rows.reshape(experts_all, capacity, model_width),
            (EXP, CTX),
            split_axis=0,
            concat_axis=0,
            tiled=True,
        ),
        lax.all_to_all(
            send_grads.reshape(experts_all, capacity, model_width),
            (EXP, CTX),
            split_axis=0,
            concat_axis=0,
            tiled=True,
        ),
    )
    local_count = ex_gate.shape[0]
    sources = experts_all // local_count

    def to_local(buffer_in):
        return (
            buffer_in.reshape(sources, local_count, capacity, model_width)
            .transpose(1, 0, 2, 3)
            .reshape(local_count, sources * capacity, model_width)
        )

    def to_owner(buffer_in):
        return (
            buffer_in.reshape(local_count, sources, capacity, model_width)
            .transpose(1, 0, 2, 3)
            .reshape(experts_all, capacity, model_width)
        )

    expert_rows = to_local(recv_rows)
    expert_grads_in = to_local(recv_grads)
    gate_e = jnp.einsum("erd,edf->erf", expert_rows, ex_gate, preferred_element_type=jnp.float32)
    up_e = jnp.einsum("erd,edf->erf", expert_rows, ex_up, preferred_element_type=jnp.float32)
    act_e = gate_e * jax.nn.sigmoid(gate_e)
    hidden_e = (act_e * up_e).astype(jnp.bfloat16)
    result_e = jnp.einsum(
        "erf,efd->erd", hidden_e, ex_down, preferred_element_type=jnp.float32
    ).astype(jnp.bfloat16)
    returned = lax.all_to_all(
        to_owner(result_e), (EXP, CTX), split_axis=0, concat_axis=0, tiled=True
    )
    picked = returned.reshape(experts_all * capacity, model_width)[target]
    picked = jnp.where(kept_rows[:, None], picked, jnp.zeros_like(picked)).astype(jnp.float32)
    routed = jnp.sum((picked * row_gates[:, None]).reshape(tokens_here, TOP, model_width), axis=1)
    output = (residual + shared_gate[:, None] * shared_part + routed).astype(jnp.bfloat16)
    gate_grads = jnp.sum(picked * cot_repeated, axis=1).reshape(tokens_here, TOP)
    hidden_grad_e = jnp.einsum(
        "erd,efd->erf", expert_grads_in, ex_down, preferred_element_type=jnp.float32
    )
    gate_grad_e = (hidden_grad_e * up_e * silu_grad(gate_e)).astype(jnp.bfloat16)
    up_grad_e = (hidden_grad_e * act_e).astype(jnp.bfloat16)
    grad_ex_down = jnp.einsum(
        "erf,erd->efd", hidden_e, expert_grads_in, preferred_element_type=jnp.float32
    )
    grad_ex_gate = jnp.einsum(
        "erd,erf->edf", expert_rows, gate_grad_e, preferred_element_type=jnp.float32
    )
    grad_ex_up = jnp.einsum(
        "erd,erf->edf", expert_rows, up_grad_e, preferred_element_type=jnp.float32
    )
    expert_sums = (
        lax.psum_scatter(grad_ex_gate, DP, scatter_dimension=1, tiled=True),
        lax.psum_scatter(grad_ex_up, DP, scatter_dimension=1, tiled=True),
        lax.psum_scatter(grad_ex_down, DP, scatter_dimension=2, tiled=True),
    )
    rows_grad_e = jnp.einsum(
        "erf,edf->erd", gate_grad_e, ex_gate, preferred_element_type=jnp.float32
    )
    rows_grad_e = (
        rows_grad_e
        + jnp.einsum("erf,edf->erd", up_grad_e, ex_up, preferred_element_type=jnp.float32)
    ).astype(jnp.bfloat16)
    returned_grads = lax.all_to_all(
        to_owner(rows_grad_e), (EXP, CTX), split_axis=0, concat_axis=0, tiled=True
    )
    routed_grad = returned_grads.reshape(experts_all * capacity, model_width)[target]
    routed_grad = jnp.where(kept_rows[:, None], routed_grad, jnp.zeros_like(routed_grad)).astype(
        jnp.float32
    )
    norm_grad = jnp.sum(routed_grad.reshape(tokens_here, TOP, model_width), axis=1)
    choose = (
        routes[0][:, :, None] == jnp.arange(experts_all, dtype=jnp.int32)[None, None, :]
    ).astype(jnp.float32)
    probs_grad = jnp.einsum("tk,tke->te", gate_grads, choose)
    logit_grad = (
        router_probs * (probs_grad - jnp.sum(router_probs * probs_grad, axis=1, keepdims=True))
    ).astype(jnp.bfloat16)
    grad_router = jnp.dot(normed_two.T, logit_grad, preferred_element_type=jnp.float32)
    gate_logit_grad = (
        jnp.sum(cot_rows * shared_part, axis=1) * shared_gate * (1.0 - shared_gate)
    ).astype(jnp.bfloat16)
    grad_gate_vec = jnp.dot(gate_logit_grad, normed_two, preferred_element_type=jnp.float32)
    norm_grad = norm_grad + jnp.dot(logit_grad, router_full.T, preferred_element_type=jnp.float32)
    norm_grad = (
        norm_grad
        + gate_logit_grad.astype(jnp.float32)[:, None] * gate_vec.astype(jnp.float32)[None, :]
    )
    shared_hgrad = jnp.dot(grads_group, sh_down.T, preferred_element_type=jnp.float32)
    gate_grad_s = (shared_hgrad * up_pre * silu_grad(gate_pre)).astype(jnp.bfloat16)
    up_grad_s = (shared_hgrad * gate_act).astype(jnp.bfloat16)
    shared_rows_grad = jnp.dot(gate_grad_s, sh_gate.T, preferred_element_type=jnp.float32)
    shared_rows_grad = shared_rows_grad + jnp.dot(
        up_grad_s, sh_up.T, preferred_element_type=jnp.float32
    )
    groups = lax.axis_size(EXP)
    parts_cd = lax.axis_size((CTX, DP))
    rows_count = rows_group.shape[0]
    arr_gate = jnp.einsum(
        "td,tes->eds",
        rows_group,
        gate_grad_s.reshape(rows_count, groups, -1),
        preferred_element_type=jnp.float32,
    ).reshape(groups * model_width, -1)
    arr_up = jnp.einsum(
        "td,tes->eds",
        rows_group,
        up_grad_s.reshape(rows_count, groups, -1),
        preferred_element_type=jnp.float32,
    ).reshape(groups * model_width, -1)
    arr_down = jnp.einsum(
        "tes,tcd->ecsd",
        shared_hidden.reshape(rows_count, groups, -1),
        grads_group.reshape(rows_count, parts_cd, -1),
        preferred_element_type=jnp.float32,
    ).reshape(-1, model_width // parts_cd)
    sums_gate, sums_up, sums_down = (
        lax.psum_scatter(arr_gate, (EXP, CTX, DP), scatter_dimension=0, tiled=True),
        lax.psum_scatter(arr_up, (EXP, CTX, DP), scatter_dimension=0, tiled=True),
        lax.psum_scatter(arr_down, (EXP, CTX, DP), scatter_dimension=0, tiled=True),
    )
    norm_grad = norm_grad + shared_rows_grad
    residual_grad, grad_gain_two = norm_back(residual, inv_two, g_two, norm_grad)
    residual_grad = residual_grad + cot_rows
    low_residual = residual_grad.astype(jnp.bfloat16)
    grad_out_w = jnp.dot(attended.T, low_residual, preferred_element_type=jnp.float32)
    attended_grad = jnp.dot(low_residual, out_w.T, preferred_element_type=jnp.float32).astype(
        jnp.bfloat16
    )
    head_q_grad, head_k_grad, head_v_grad = lax.map(
        partial(attend_back, allowed=allowed, scale_factor=scale_factor),
        (head_q, head_k, head_v, to_heads(attended_grad), log_total),
    )
    key_sum, value_sum = (
        lax.psum_scatter(from_heads(head_k_grad), CTX, scatter_dimension=0, tiled=True),
        lax.psum_scatter(from_heads(head_v_grad), CTX, scatter_dimension=0, tiled=True),
    )
    query_low = from_heads(head_q_grad).astype(jnp.bfloat16)
    key_low = key_sum.astype(jnp.bfloat16)
    value_low = value_sum.astype(jnp.bfloat16)
    grad_query = jnp.dot(normed_one.T, query_low, preferred_element_type=jnp.float32)
    grad_key = jnp.dot(normed_one.T, key_low, preferred_element_type=jnp.float32)
    grad_value = jnp.dot(normed_one.T, value_low, preferred_element_type=jnp.float32)
    normed_grad = jnp.dot(query_low, query_w.T, preferred_element_type=jnp.float32)
    normed_grad = normed_grad + jnp.dot(key_low, key_w.T, preferred_element_type=jnp.float32)
    normed_grad = normed_grad + jnp.dot(value_low, value_w.T, preferred_element_type=jnp.float32)
    input_part, grad_gain_one = norm_back(x_rows, inv_one, g_one, normed_grad)
    input_grad = (residual_grad + input_part).astype(jnp.bfloat16)
    dense = (
        lax.psum_scatter(
            grad_gain_one, (EXP, CTX, DP), scatter_dimension=0, tiled=True
        ),
        lax.psum_scatter(grad_query, (EXP, CTX, DP), scatter_dimension=0, tiled=True),
        lax.psum_scatter(grad_key, (EXP, CTX, DP), scatter_dimension=0, tiled=True),
        lax.psum_scatter(grad_value, (EXP, CTX, DP), scatter_dimension=0, tiled=True),
        lax.psum_scatter(grad_out_w, (EXP, CTX, DP), scatter_dimension=0, tiled=True),
        lax.psum_scatter(
            grad_gain_two, (EXP, CTX, DP), scatter_dimension=0, tiled=True
        ),
        lax.psum_scatter(
            grad_router, (EXP, CTX, DP), scatter_dimension=0, tiled=True
        ),
        lax.psum_scatter(
            grad_gate_vec, (EXP, CTX, DP), scatter_dimension=0, tiled=True
        ),
    )
    return (
        output[None],
        input_grad[None],
        dense[0],
        dense[1],
        dense[2],
        dense[3],
        dense[4],
        dense[5],
        dense[6],
        dense[7],
        sums_gate,
        sums_up,
        sums_down,
        expert_sums[0],
        expert_sums[1],
        expert_sums[2],
    )

def attention_probs(q_blk, k_part, q_code, k_code, first_row, scale_factor):
    scores = lax.dot_general(
        q_blk, k_part, (((1,), (1,)), ((), ())), preferred_element_type=jnp.float32
    )
    row = first_row + lax.broadcasted_iota(jnp.int32, scores.shape, 0)
    col = lax.broadcasted_iota(jnp.int32, scores.shape, 1)
    allowed = ((col < row) & (k_code == q_code)) | (col == row)
    logits = jnp.where(allowed, scores * scale_factor, NEG)
    exp_scores = jnp.exp(logits - jnp.max(logits, axis=1, keepdims=True))
    return exp_scores * (1.0 / jnp.sum(exp_scores, axis=1, keepdims=True))


def attend_kernel(heads, step, qkv_ref, q_code_ref, k_code_ref, out_ref):
    seq_len = qkv_ref.shape[0]
    width = heads * HEAD_DIM
    for head in range(heads):
        at = head * HEAD_DIM
        for first in range(0, seq_len, step):
            upto = first + step
            probs = attention_probs(
                qkv_ref[first:upto, at : at + HEAD_DIM],
                qkv_ref[0:upto, width + at : width + at + HEAD_DIM],
                q_code_ref[first:upto, :],
                k_code_ref[0, :, 0:upto],
                first,
                HEAD_DIM**-0.5,
            )
            out_ref[first:upto, at : at + HEAD_DIM] = jnp.dot(
                probs.astype(jnp.bfloat16),
                qkv_ref[0:upto, 2 * width + at : 2 * width + at + HEAD_DIM],
                preferred_element_type=jnp.float32,
            ).astype(jnp.bfloat16)


def attend_back_kernel(
    heads, step, qkv_ref, grad_ref, q_code_ref, k_code_ref, out_ref, key_acc, value_acc
):
    seq_len = qkv_ref.shape[0]
    width = heads * HEAD_DIM
    for head in range(heads):
        at = head * HEAD_DIM
        key_at, value_at = width + at, 2 * width + at
        key_acc[...] = jnp.zeros_like(key_acc)
        value_acc[...] = jnp.zeros_like(value_acc)
        for first in range(0, seq_len, step):
            upto = first + step
            q_blk = qkv_ref[first:upto, at : at + HEAD_DIM]
            k_part = qkv_ref[0:upto, key_at : key_at + HEAD_DIM]
            v_part = qkv_ref[0:upto, value_at : value_at + HEAD_DIM]
            g_blk = grad_ref[first:upto, at : at + HEAD_DIM]
            probs = attention_probs(
                q_blk,
                k_part,
                q_code_ref[first:upto, :],
                k_code_ref[0, :, 0:upto],
                first,
                HEAD_DIM**-0.5,
            )
            prob_grad = lax.dot_general(
                g_blk, v_part, (((1,), (1,)), ((), ())), preferred_element_type=jnp.float32
            )
            inner = jnp.sum(probs * prob_grad, axis=1, keepdims=True)
            score_grad = (probs * (prob_grad - inner) * HEAD_DIM**-0.5).astype(jnp.bfloat16)
            out_ref[first:upto, at : at + HEAD_DIM] = jnp.dot(
                score_grad, k_part, preferred_element_type=jnp.float32
            ).astype(jnp.bfloat16)
            key_acc[0:upto, :] += lax.dot_general(
                score_grad, q_blk, (((0,), (0,)), ((), ())), preferred_element_type=jnp.float32
            )
            value_acc[0:upto, :] += lax.dot_general(
                probs.astype(jnp.bfloat16),
                g_blk,
                (((0,), (0,)), ((), ())),
                preferred_element_type=jnp.float32,
            )
        out_ref[:, key_at : key_at + HEAD_DIM] = key_acc[...].astype(jnp.bfloat16)
        out_ref[:, value_at : value_at + HEAD_DIM] = value_acc[...].astype(jnp.bfloat16)


def attention_call(qkv, grads, q_codes, k_codes, seq_len):
    rows, triple = qkv.shape
    width = triple // 3
    heads = width // HEAD_DIM
    step = min(256, seq_len)
    specs = [pl.BlockSpec((seq_len, triple), lambda s: (s, 0))]
    operands = [qkv]
    if grads is not None:
        specs.append(pl.BlockSpec((seq_len, width), lambda s: (s, 0)))
        operands.append(grads)
    specs += [
        pl.BlockSpec((seq_len, 1), lambda s: (s, 0)),
        pl.BlockSpec((1, 1, seq_len), lambda s: (s, 0, 0)),
    ]
    operands += [q_codes, k_codes]
    out_width = width if grads is None else triple
    body = attend_kernel if grads is None else attend_back_kernel
    passes = 2 if grads is None else 5
    area = rows * seq_len * heads
    return pl.pallas_call(
        partial(body, heads, step),
        grid=(rows // seq_len,),
        in_specs=specs,
        out_specs=pl.BlockSpec((seq_len, out_width), lambda s: (s, 0)),
        out_shape=jax.ShapeDtypeStruct((rows, out_width), jnp.bfloat16),
        scratch_shapes=[]
        if grads is None
        else [pltpu.VMEM((seq_len, HEAD_DIM), jnp.float32)] * 2,
        compiler_params=pltpu.CompilerParams(vmem_limit_bytes=48 * 2**20),
        cost_estimate=pl.CostEstimate(
            flops=2 * passes * area * HEAD_DIM,
            bytes_accessed=2 * rows * (triple + out_width),
            transcendentals=area,
        ),
    )(*operands)


MESH_ID = pl.DeviceIdType.MESH


def other_in_pair(index, bit):
    return index + bit - 2 * bit * (lax.div(index, bit) % 2)


def plane_places():
    at = lax.axis_index(EXP)
    core = lax.axis_index(CTX)
    across, along = other_in_pair(at, 1), other_in_pair(at, 2)
    return at, core, across, along, other_in_pair(along, 1)


def greet(across, along, core):
    barrier = pltpu.get_barrier_semaphore()
    for target in ({EXP: across}, {EXP: along}, {CTX: 1 - core}):
        pl.semaphore_signal(barrier, inc=1, device_id=target, device_id_type=MESH_ID)
    pl.semaphore_wait(barrier, 3)


def plane_gather_kernel(with_info, relative, *refs):
    if with_info:
        own_ref, info_ref, all_ref, info_all_ref, send_sem, recv_sem, local_sem = refs
    else:
        own_ref, all_ref, send_sem, recv_sem, local_sem = refs
    at, core, across, along, far = plane_places()
    rows = own_ref.shape[0]
    half = rows // 2
    top, bottom, whole = pl.ds(0, half), pl.ds(half, half), pl.ds(0, rows)
    greet(across, along, core)
    started = []
    twin_id = {CTX: 1 - core}

    def slot_of(place, shift, for_twin):
        if relative:
            return shift + 4 * for_twin
        return place * 2 + core

    def send(number, src, dst, target):
        copy = pltpu.make_async_remote_copy(
            src_ref=src,
            dst_ref=dst,
            send_sem=send_sem.at[number],
            recv_sem=recv_sem.at[number],
            device_id=target,
            device_id_type=MESH_ID,
        )
        copy.start()
        started.append(copy)
        return copy

    def piece(place, shift, part, for_twin=0):
        return all_ref.at[slot_of(place, shift, for_twin), part]

    x_top = send(0, own_ref.at[top], piece(at, 1, top), {EXP: across})
    y_bottom = send(1, own_ref.at[bottom], piece(at, 2, bottom), {EXP: along})
    x_bottom = send(2, own_ref.at[bottom], piece(at, 1, bottom), {EXP: across})
    y_top = send(3, own_ref.at[top], piece(at, 2, top), {EXP: along})
    twins = [send(4, own_ref, piece(at, 0, whole, 1), twin_id)]
    heres = [pltpu.make_async_copy(own_ref, piece(at, 0, whole), local_sem.at[0])]
    heres[0].start()
    if with_info:
        info_at = lambda place: info_all_ref.at[place * 2 + core]
        heres.append(pltpu.make_async_copy(info_ref, info_at(at), local_sem.at[1]))
        heres[1].start()
        info_x = send(13, info_ref, info_at(at), {EXP: across})
        info_y = send(14, info_ref, info_at(at), {EXP: along})
        twins.append(send(15, info_ref, info_at(at), twin_id))
        info_x.wait_recv()
        info_far = send(16, info_at(across), info_at(across), {EXP: along})
        twins.append(send(17, info_at(across), info_at(across), twin_id))
        info_y.wait_recv()
        twins.append(send(18, info_at(along), info_at(along), twin_id))
        info_far.wait_recv()
        twins.append(send(19, info_at(far), info_at(far), twin_id))

    def hand_on(number, place, shift, part):
        src = piece(place, shift, part)
        twins.append(send(number, src, piece(place, shift, part, 1), twin_id))

    x_top.wait_recv()
    far_top = send(5, piece(across, 1, top), piece(across, 3, top), {EXP: along})
    hand_on(6, across, 1, top)
    y_bottom.wait_recv()
    far_bottom = send(7, piece(along, 2, bottom), piece(along, 3, bottom), {EXP: across})
    hand_on(8, along, 2, bottom)
    x_bottom.wait_recv()
    hand_on(9, across, 1, bottom)
    y_top.wait_recv()
    hand_on(10, along, 2, top)
    far_top.wait_recv()
    hand_on(11, far, 3, top)
    far_bottom.wait_recv()
    hand_on(12, far, 3, bottom)
    for copy in twins:
        copy.wait_recv()
    for copy in started:
        copy.wait_send()
    for copy in heres:
        copy.wait()


def plane_gather(own, info, relative, number):
    plane = lax.axis_size(PLANE)
    operands = [own] if info is None else [own, info]
    outs = [jax.ShapeDtypeStruct((plane, *v.shape), v.dtype) for v in operands]
    anywhere = pl.BlockSpec(memory_space=pl.ANY)
    return pl.pallas_call(
        partial(plane_gather_kernel, info is not None, relative),
        out_shape=outs,
        in_specs=[anywhere] * len(operands),
        out_specs=[anywhere] * len(operands),
        scratch_shapes=[
            pltpu.SemaphoreType.DMA((20,)),
            pltpu.SemaphoreType.DMA((20,)),
            pltpu.SemaphoreType.DMA((2,)),
        ],
        compiler_params=pltpu.CompilerParams(collective_id=number, has_side_effects=True),
        cost_estimate=pl.CostEstimate(
            flops=0, bytes_accessed=100 * own.size, transcendentals=0
        ),
    )(*operands)


def plane_scatter_kernel(
    relative,
    part_ref,
    out_ref,
    own,
    twin_got,
    x_got,
    y_got,
    x_last,
    y_last,
    send_sem,
    recv_sem,
    local_sem,
):
    at, core, across, along, far = plane_places()
    rows = part_ref.shape[1]
    half = rows // 2
    step = 64
    greet(across, along, core)
    started = []

    def send(number, src, dst, target):
        copy = pltpu.make_async_remote_copy(
            src_ref=src,
            dst_ref=dst,
            send_sem=send_sem.at[number],
            recv_sem=recv_sem.at[number],
            device_id=target,
            device_id_type=MESH_ID,
        )
        copy.start()
        started.append(copy)
        return copy

    twins, heres = [], []
    for j, (label, shift) in enumerate(((far, 3), (across, 1), (along, 2), (at, 0))):
        theirs = shift + 4 if relative else label * 2 + 1 - core
        ours = shift if relative else label * 2 + core
        twins.append(send(j, part_ref.at[theirs], twin_got.at[j], {CTX: 1 - core}))
        here = pltpu.make_async_copy(part_ref.at[ours], own.at[j], local_sem.at[j])
        here.start()
        heres.append(here)

    def add_rows(target, t_first, count, source, s_first):
        @pl.loop(0, count // step)
        def _(i):
            into = pl.ds(pl.multiple_of(t_first + i * step, step), step)
            take = pl.ds(pl.multiple_of(s_first + i * step, step), step)
            total = target[into].astype(jnp.float32) + source[take].astype(jnp.float32)
            target[into] = total.astype(target.dtype)

    top, bottom = pl.ds(0, half), pl.ds(half, half)
    x_sent, y_sent = [], []
    for j in range(4):
        twins[j].wait_recv()
        heres[j].wait()
        add_rows(own.at[j], 0, rows, twin_got.at[j], 0)
        if j < 2:
            x_sent.append(send(4 + j, own.at[j, top], x_got.at[j], {EXP: across}))
        if j == 0 or j == 2:
            y_sent.append(send(6 + j // 2, own.at[j, bottom], y_got.at[j // 2], {EXP: along}))
    x_sent[0].wait_recv()
    add_rows(own.at[2], 0, half, x_got.at[0], 0)
    last_y = send(8, own.at[2, top], y_last, {EXP: along})
    y_sent[0].wait_recv()
    add_rows(own.at[1], half, half, y_got.at[0], 0)
    last_x = send(9, own.at[1, bottom], x_last, {EXP: across})

    def finish(first, near, later):
        @pl.loop(0, half // step)
        def _(i):
            take = pl.ds(pl.multiple_of(i * step, step), step)
            into = pl.ds(pl.multiple_of(first + i * step, step), step)
            out_ref[into] = (
                own[3, into].astype(jnp.float32)
                + near[1, take].astype(jnp.float32)
                + later[take].astype(jnp.float32)
            ).astype(out_ref.dtype)

    x_sent[1].wait_recv()
    last_y.wait_recv()
    finish(0, x_got, y_last)
    y_sent[1].wait_recv()
    last_x.wait_recv()
    finish(half, y_got, x_last)
    for copy in started:
        copy.wait_send()


def plane_scatter(parts, relative, number, out_type):
    plane, rows, cols = parts.shape
    half = rows // 2
    vmem = lambda *shape: pltpu.VMEM(shape, parts.dtype)
    return pl.pallas_call(
        partial(plane_scatter_kernel, relative),
        out_shape=jax.ShapeDtypeStruct((rows, cols), out_type),
        in_specs=[pl.BlockSpec(memory_space=pl.ANY)],
        out_specs=pl.BlockSpec(memory_space=pltpu.VMEM),
        scratch_shapes=[
            vmem(4, rows, cols),
            vmem(4, rows, cols),
            vmem(2, half, cols),
            vmem(2, half, cols),
            vmem(half, cols),
            vmem(half, cols),
            pltpu.SemaphoreType.DMA((10,)),
            pltpu.SemaphoreType.DMA((10,)),
            pltpu.SemaphoreType.DMA((4,)),
        ],
        compiler_params=pltpu.CompilerParams(
            collective_id=number, has_side_effects=True, vmem_limit_bytes=44 * 2**20
        ),
        cost_estimate=pl.CostEstimate(
            flops=0, bytes_accessed=100 * rows * cols, transcendentals=0
        ),
    )(parts)


def after(values, others):
    return lax.optimization_barrier((values, others))[0]


def swap(values, bits):
    return lax.ppermute(values, EXP, [(i, i ^ bits) for i in range(4)])


def twin(values):
    return lax.ppermute(values, CTX, [(0, 1), (1, 0)])


def twin_sums(ours, theirs):
    got = twin(theirs)
    return [low(ours[k].astype(jnp.float32) + got[k].astype(jnp.float32)) for k in range(4)]


def hop_sum(sums, later):
    total = sums[0].astype(jnp.float32)
    for k in (1, 2, 3):
        total = total + after(swap(sums[k], k), later).astype(jnp.float32)
    return total


def mm(left, right, dims=((1,), (0,))):
    return lax.dot_general(left, right, (dims, ((), ())), preferred_element_type=jnp.float32)


def low(values):
    return values.astype(jnp.bfloat16)


def local_plane(
    hidden,
    cotangent,
    segments,
    padding,
    routes,
    order,
    norm1_gain,
    w_query,
    w_key,
    w_value,
    w_out,
    norm2_gain,
    router,
    shared_gate_vec,
    shared_w_gate,
    shared_w_up,
    shared_w_down,
    expert_w_gate,
    expert_w_up,
    expert_w_down,
):
    plane = lax.axis_size(PLANE)
    groups = lax.axis_size(EXP)
    halves = lax.axis_size(CTX)
    depth = lax.axis_size(DP)
    me = lax.axis_index(PLANE)
    core = lax.axis_index(CTX)
    tokens, width = hidden.shape[1], hidden.shape[2]
    all_tokens = plane * tokens
    seq_len = halves * tokens
    experts_all = router.shape[1]
    head_cols = width // plane
    shard = width // depth

    token_info = jnp.concatenate(
        [segments + 1, jnp.where(padding > 0, segments + 1, 0), order[0], routes[0].T]
    )
    info_rows = token_info.shape[0]
    token_info = jnp.concatenate([token_info, jnp.zeros((8 - info_rows, tokens), jnp.int32)])

    hidden_all, info_all = plane_gather(hidden[0], token_info, False, 0)
    hidden_all = hidden_all.reshape(all_tokens, width)
    place = lax.axis_index(EXP)
    away = [(place ^ k) * 2 + (core ^ j) for j in (0, 1) for k in range(4)]
    away = jnp.stack(away)
    w_qkv_part = jnp.concatenate(
        [
            lax.dynamic_slice(w, (0, me * head_cols), (shard, head_cols))
            for w in (w_query, w_key, w_value)
        ]
        + [router, norm1_gain[:, None], norm2_gain[:, None], shared_gate_vec[:, None]]
        + [jnp.zeros((shard, 128 - experts_all - 3), jnp.bfloat16)],
        axis=1,
    )
    w_qkv = lax.all_gather(w_qkv_part, DP, axis=0, tiled=True)
    small = w_qkv[:, 3 * head_cols :].T
    w_qkv = w_qkv[:, : 3 * head_cols]
    router_t = small[:experts_all]
    g_one = small[experts_all].astype(jnp.float32)
    g_two = small[experts_all + 1].astype(jnp.float32)
    gate_vec = small[experts_all + 2]
    out_rows = shard // plane
    w_out_part = lax.dynamic_slice(w_out, (me * out_rows, 0), (out_rows, width))
    w_out_part = lax.all_gather(w_out_part, DP, axis=0, tiled=False)
    w_out_part = after(w_out_part, info_all)
    w_out_got = [swap(w_out_part, k) for k in (1, 2, 3)]

    def normed(values, gain):
        values = values.astype(jnp.float32)
        inv = lax.rsqrt(jnp.mean(values * values, axis=1, keepdims=True) + EPS)
        return values, inv, low(values * inv * gain)

    _, _, n1_all = normed(hidden_all, g_one)
    qkv = low(mm(n1_all, w_qkv))
    q_codes = info_all[:, 0].reshape(all_tokens, 1)
    k_codes = info_all[:, 1].reshape(all_tokens // seq_len, 1, seq_len)
    attended_cols = attention_call(qkv, None, q_codes, k_codes, seq_len)
    pieces = [w_out_part] + [after(v, qkv) for v in w_out_got]
    w_out_near = jnp.zeros((depth, groups, 1, out_rows, width), jnp.bfloat16)
    for k in range(4):
        w_out_near = lax.dynamic_update_slice(
            w_out_near, pieces[k][:, None, None], (0, place ^ k, 0, 0, 0)
        )
    w_out_far = twin(w_out_near)
    w_out_full = jnp.where(
        core == 0,
        jnp.concatenate([w_out_near, w_out_far], axis=2),
        jnp.concatenate([w_out_far, w_out_near], axis=2),
    ).reshape(width, width)

    x_rows, inv_one, _ = normed(hidden[0], g_one)
    cot_rows = cotangent[0].astype(jnp.float32)

    def to_tokens(cols):
        got = lax.all_to_all(
            cols.reshape(plane, tokens, head_cols), PLANE, split_axis=0, concat_axis=0, tiled=True
        )
        return got.transpose(1, 0, 2).reshape(tokens, width)

    def to_columns(rows_in):
        send = rows_in.reshape(tokens, plane, head_cols).transpose(1, 0, 2)
        got = lax.all_to_all(send, PLANE, split_axis=0, concat_axis=0, tiled=True)
        return got.reshape(all_tokens, head_cols)

    attended = to_tokens(attended_cols)
    residual = x_rows + mm(attended, w_out_full)
    residual, inv_two, n2 = normed(residual, g_two)

    units = shared_w_gate.shape[1]
    part = units // (depth * halves)
    pick = lambda w: lax.dynamic_index_in_dim(
        w.reshape(w.shape[0], depth, halves, part), core, axis=2, keepdims=False
    ).reshape(w.shape[0], depth * part)
    sh_gate = lax.all_gather(pick(shared_w_gate), DP, axis=0, tiled=True)
    sh_up = lax.all_gather(pick(shared_w_up), DP, axis=0, tiled=True)
    sh_down = lax.all_gather(
        lax.dynamic_slice(shared_w_down, (core * part, 0), (part, width)), DP, axis=0, tiled=True
    )
    n2 = after(n2, (sh_gate, sh_up))
    n2_all = plane_gather(n2, None, True, 2)[0].reshape(all_tokens, width)
    cot_own = after(cotangent[0], n2_all)
    cot_got = [swap(cot_own, k) for k in (1, 2, 3)]
    ex_gate = lax.all_gather(after(expert_w_gate[0], info_all), DP, axis=0, tiled=True)
    ex_up = lax.all_gather(after(expert_w_up[0], info_all), DP, axis=0, tiled=True)
    ex_down = lax.all_gather(after(expert_w_down[0], info_all), DP, axis=1, tiled=True)

    small_w = jnp.concatenate([router_t, gate_vec[None]])

    def gates_of(rows_in):
        both = mm(rows_in, small_w, ((1,), (1,)))
        z = both[:, :experts_all]
        e = jnp.exp(z - jnp.max(z, axis=1, keepdims=True))
        return e / jnp.sum(e, axis=1, keepdims=True), jax.nn.sigmoid(both[:, experts_all:])

    probs_all, sg_all = gates_of(n2_all)
    expert_gate = lax.dynamic_slice(probs_all, (0, me), (all_tokens, 1))

    capacity = (9 * tokens * TOP + 8 * experts_all - 1) // (8 * experts_all)
    info_away = info_all[away]
    order_all = info_away[:, 2]
    routed_here = jnp.any(info_away[:, 3 : 3 + TOP] == me, axis=1)
    earlier = (order_all[:, None, :] < order_all[:, :, None]) & routed_here[:, None, :]
    slots = jnp.sum(earlier.astype(jnp.int32), axis=2)
    slots = jnp.where(routed_here, slots, capacity)
    chosen = slots[:, None, :] == jnp.arange(capacity, dtype=jnp.int32)[None, :, None]
    onehot = chosen.astype(jnp.bfloat16)

    def rows_of(values):
        got = lax.dot_general(
            onehot,
            values.reshape(plane, tokens, width),
            (((2,), (1,)), ((0,), (0,))),
            preferred_element_type=jnp.float32,
        )
        return got.reshape(plane * capacity, width)

    def back_to_tokens(values):
        got = lax.dot_general(
            onehot,
            values.reshape(plane, capacity, width),
            (((1,), (1,)), ((0,), (0,))),
            preferred_element_type=jnp.float32,
        )
        return got.reshape(all_tokens, width)

    slot_gates = jnp.sum(
        jnp.where(chosen, expert_gate.reshape(plane, 1, tokens), 0.0), axis=2
    ).reshape(plane * capacity, 1)
    expert_rows = low(rows_of(n2_all))
    gate_e = mm(expert_rows, ex_gate)
    up_e = mm(expert_rows, ex_up)
    act_e = gate_e * jax.nn.sigmoid(gate_e)
    hidden_e = low(act_e * up_e)
    cot_near = jnp.concatenate([cot_own] + [after(v, hidden_e) for v in cot_got])
    cot_all = jnp.concatenate([cot_near, twin(cot_near)])
    row_cots = low(rows_of(cot_all))
    row_grads = low(row_cots.astype(jnp.float32) * slot_gates)

    shared_grads = low(sg_all * cot_all.astype(jnp.float32))
    gate_pre = mm(n2_all, sh_gate)
    up_pre = mm(n2_all, sh_up)
    gate_act = gate_pre * jax.nn.sigmoid(gate_pre)
    shared_hidden = low(gate_act * up_pre)
    shared_part = mm(shared_hidden, sh_down)
    cot_dot_shared = jnp.sum(shared_part * cot_all.astype(jnp.float32), axis=1)
    shared_hgrad = mm(shared_grads, sh_down, ((1,), (1,)))
    gate_grad_s = low(shared_hgrad * up_pre * silu_grad(gate_pre))
    up_grad_s = low(shared_hgrad * gate_act)

    rows_out = width // (halves * depth)

    def own_units(grad):
        grad = low(grad)
        cut = lambda c, z: grad[:, (c * depth + z) * rows_out : (c * depth + z + 1) * rows_out]
        return jnp.concatenate(
            [
                jnp.concatenate([cut(c, z) for c in range(halves)], axis=1)
                for z in range(depth)
            ]
        )

    def shared_scatter(grad):
        total = grad.reshape(depth * part, halves, rows_out)
        keep = lax.dynamic_index_in_dim(total, core, axis=1, keepdims=False)
        give = lax.dynamic_index_in_dim(total, 1 - core, axis=1, keepdims=False)
        both = jnp.stack([keep, twin(give)]).reshape(halves, depth, part, rows_out)
        both = jnp.where(core == 0, both, both[::-1]).transpose(1, 0, 2, 3)
        return both.reshape(units, rows_out).astype(jnp.float32)

    grad_sh_gate = own_units(mm(gate_grad_s, n2_all, ((0,), (0,))))
    grad_sh_up = own_units(mm(up_grad_s, n2_all, ((0,), (0,))))
    grad_sh_down = own_units(mm(shared_hidden, shared_grads, ((0,), (0,))))

    result_e = low(mm(hidden_e, ex_down))
    row_dots = jnp.sum(result_e.astype(jnp.float32) * row_cots.astype(jnp.float32), axis=1)
    gate_dots = jnp.sum(
        jnp.where(chosen, row_dots.reshape(plane, capacity, 1), 0.0), axis=1
    )
    hgrad_e = mm(row_grads, ex_down, ((1,), (1,)))
    gate_grad_e = low(hgrad_e * up_e * silu_grad(gate_e))
    up_grad_e = low(hgrad_e * act_e)

    grad_ex_down = low(mm(hidden_e, row_grads, ((0,), (0,))))
    grad_ex_gate = low(mm(expert_rows, gate_grad_e, ((0,), (0,))))
    grad_ex_up = low(mm(expert_rows, up_grad_e, ((0,), (0,))))
    rows_grad = low(
        mm(gate_grad_e, ex_gate, ((1,), (1,))) + mm(up_grad_e, ex_up, ((1,), (1,)))
    )

    out_part = low(sg_all * shared_part + expert_gate * back_to_tokens(result_e))
    n2_grad_part = low(
        mm(gate_grad_s, sh_gate, ((1,), (1,)))
        + mm(up_grad_s, sh_up, ((1,), (1,)))
        + back_to_tokens(rows_grad)
    )
    grads = (grad_sh_gate, grad_sh_up, grad_sh_down, grad_ex_down, grad_ex_gate, grad_ex_up)
    grads_made = grads
    grads = [
        lax.psum_scatter(v, DP, scatter_dimension=dim, tiled=True)
        for v, dim in zip(grads, (0, 0, 0, 1, 0, 0))
    ]
    n2_grad_part = after(n2_grad_part, (grads_made, out_part, grads[:3]))
    n2_grad = plane_scatter(n2_grad_part.reshape(plane, tokens, width), True, 3, jnp.float32)

    dots = jnp.stack([gate_dots, cot_dot_shared.reshape(plane, tokens)], axis=1)
    back = jnp.arange(plane, dtype=jnp.int32) ^ me
    dots = dots[(back // 2) + 4 * (back % 2)]
    dots = lax.all_to_all(dots, PLANE, split_axis=0, concat_axis=0, tiled=True)
    probs_grad = dots[:, 0].T
    probs, sg = gates_of(n2)
    logit_grad = low(probs * (probs_grad - jnp.sum(probs * probs_grad, axis=1, keepdims=True)))
    sg_logit_grad = low(jnp.sum(dots[:, 1], axis=0)[:, None] * sg * (1.0 - sg))
    small_grads = mm(n2, jnp.concatenate([logit_grad, sg_logit_grad], axis=1), ((0,), (0,)))
    n2_grad = (
        n2_grad
        + mm(logit_grad, router_t)
        + sg_logit_grad.astype(jnp.float32) * gate_vec.astype(jnp.float32)[None]
    )
    residual_grad, grad_gain_two = norm_back(residual, inv_two, g_two, n2_grad)
    residual_grad = residual_grad + cot_rows
    low_residual = low(residual_grad)

    small_grads = jnp.concatenate([small_grads, grad_gain_two[:, None]], axis=1).T
    small_grads = jnp.pad(small_grads, ((0, 14 - experts_all), (0, 0)))
    small_grads = small_grads.reshape(16, plane, width // plane).transpose(1, 0, 2)
    small_grads = jnp.sum(
        lax.all_to_all(small_grads, PLANE, split_axis=0, concat_axis=0, tiled=True), axis=0
    )
    small_grads = small_grads.reshape(16, depth, shard // plane).transpose(1, 0, 2)
    small_grads = jnp.sum(
        lax.all_to_all(small_grads, DP, split_axis=0, concat_axis=0, tiled=True), axis=0
    )
    grad_out = low(mm(attended, low_residual, ((0,), (0,))))
    grad_out = grad_out.reshape(groups, halves, width // plane, width)
    block_of = lambda k, c: lax.dynamic_slice(
        grad_out, (place ^ k, c, 0, 0), (1, 1, width // plane, width)
    )[0, 0]
    attended_grad = to_columns(low(mm(low_residual, w_out_full, ((1,), (1,)))))
    out_part = after(out_part, n2_grad).reshape(plane, tokens, width)
    out_sums = twin_sums(out_part[:4], out_part[4:])
    attended_grad = after(attended_grad, (out_sums, grads[3]))
    qkv_grad = attention_call(qkv, attended_grad, q_codes, k_codes, seq_len)
    out_grad_sums = twin_sums(
        [block_of(k, core) for k in range(4)],
        jnp.stack([block_of(k, 1 - core) for k in range(4)]),
    )
    grad_qkv = low(mm(n1_all, qkv_grad, ((0,), (0,))))
    n1_grad = low(mm(qkv_grad, w_qkv, ((1,), (1,))))
    grad_out = low(hop_sum(out_grad_sums, n1_grad))
    grad_out = lax.psum_scatter(grad_out, DP, scatter_dimension=0, tiled=True)
    n1_grad = after(n1_grad, (grad_qkv, out_grad_sums, grads[4]))
    n1_grad = plane_scatter(n1_grad.reshape(plane, tokens, width), False, 1, jnp.float32)
    output = low(residual + hop_sum(out_sums, n1_grad))
    grad_sh_gate, grad_sh_up, grad_sh_down = [
        shared_scatter(after(v, n1_grad)) for v in grads[:3]
    ]
    grad_sh_gate, grad_sh_up = grad_sh_gate.T, grad_sh_up.T
    fine = shard // plane
    grad_qkv = (
        grad_qkv.reshape(plane, depth, fine, 3 * head_cols)
        .transpose(1, 0, 2, 3)
        .reshape(width, 3 * head_cols)
    )
    grad_qkv = lax.psum_scatter(grad_qkv, DP, scatter_dimension=0, tiled=True)
    w_rows = (
        w_qkv.reshape(plane, depth, fine, 3 * head_cols)
        .transpose(1, 0, 2, 3)
        .reshape(depth, plane * fine, 3 * head_cols)
    )
    w_rows = lax.dynamic_index_in_dim(w_rows, lax.axis_index(DP), axis=0, keepdims=False)
    gain_dots = jnp.sum(grad_qkv.astype(jnp.float32) * w_rows.astype(jnp.float32), axis=1)
    gain_dots = lax.all_to_all(
        gain_dots.reshape(plane, 1, fine), PLANE, split_axis=0, concat_axis=0, tiled=True
    )
    my_gain = lax.dynamic_slice(
        g_one, ((me * depth + lax.axis_index(DP)) * fine,), (fine,)
    )
    grad_gain_one = jnp.sum(gain_dots[:, 0], axis=0) / my_gain
    grad_qkv = lax.all_to_all(
        grad_qkv.reshape(plane, fine, 3 * head_cols),
        PLANE,
        split_axis=0,
        concat_axis=0,
        tiled=True,
    )
    grad_qkv = (
        grad_qkv.reshape(plane, fine, 3, head_cols)
        .transpose(2, 1, 0, 3)
        .reshape(3, fine, width)
        .astype(jnp.float32)
    )
    grad_out = after(grad_out, n1_grad).astype(jnp.float32)
    grad_ex_down, grad_ex_gate, grad_ex_up = [
        after(v, n1_grad).astype(jnp.float32)[None] for v in grads[3:]
    ]
    input_part, _ = norm_back(x_rows, inv_one, g_one, n1_grad)
    input_grad = low(residual_grad + input_part)
    return (
        output[None],
        input_grad[None],
        grad_gain_one,
        grad_qkv[0],
        grad_qkv[1],
        grad_qkv[2],
        grad_out,
        small_grads[experts_all + 1],
        small_grads[:experts_all].T,
        small_grads[experts_all],
        grad_sh_gate,
        grad_sh_up,
        grad_sh_down,
        grad_ex_gate,
        grad_ex_up,
        grad_ex_down,
    )


def solution(mesh):
    in_specs = (
        P((EXP, DP), CTX, None),
        P((EXP, DP), CTX, None),
        P((EXP, DP), CTX),
        P((EXP, DP), CTX),
        P((EXP, DP), CTX, None),
        P((EXP, DP), CTX, None),
        P(DP),
        P(DP, None),
        P(DP, None),
        P(DP, None),
        P(DP, None),
        P(DP),
        P(DP, None),
        P(DP),
        P(DP, EXP),
        P(DP, EXP),
        P((EXP, DP), None),
        P((EXP, CTX), DP, None),
        P((EXP, CTX), DP, None),
        P((EXP, CTX), None, DP),
    )
    out_specs = (
        P((EXP, DP), CTX, None),
        P((EXP, DP), CTX, None),
        P((EXP, CTX, DP)),
        P((EXP, CTX, DP), None),
        P((EXP, CTX, DP), None),
        P((EXP, CTX, DP), None),
        P((EXP, CTX, DP), None),
        P((EXP, CTX, DP)),
        P((EXP, CTX, DP), None),
        P((EXP, CTX, DP)),
        P((CTX, DP), EXP),
        P((CTX, DP), EXP),
        P(EXP, (CTX, DP)),
        P((EXP, CTX), DP, None),
        P((EXP, CTX), DP, None),
        P((EXP, CTX), None, DP),
    )
    plane = mesh.shape[EXP] * mesh.shape[CTX]

    def run(*args):
        square = mesh.shape[EXP] == 4 and mesh.shape[CTX] == 2
        one_each = square and args[12].shape[1] == plane
        local = local_plane if one_each else local_general
        return jax.shard_map(
            local, mesh=mesh, in_specs=in_specs, out_specs=out_specs, check_vma=False
        )(*args)

    return run
```

```python
from functools import partial

import jax
import jax.numpy as jnp
from jax import lax
from jax.experimental import pallas as pl
from jax.experimental.pallas import tpu as pltpu
from jax.sharding import PartitionSpec as P

EXP, CTX, DP = "experts", "context", "dp"
PLANE = (EXP, CTX)
HEADS = 16
HEAD_DIM = 128
TOP = 4


EPS = 1e-06
NEG = -1e30


def silu_grad(pre_act):
    logistic = jax.nn.sigmoid(pre_act)
    return logistic * (1.0 + pre_act * (1.0 - logistic))


def block_slots(route_row, priority, expert_count):
    matches = (route_row[:, None] == jnp.arange(expert_count, dtype=jnp.int32)[None, :]).astype(
        jnp.int32
    )
    ordered = jnp.zeros_like(matches).at[priority].set(matches)
    before = jnp.cumsum(ordered, axis=0) - ordered
    return jnp.sum(before[priority] * matches, axis=1)


def norm_back(values_in, inv_rms, gain_vec, gradient):
    weighted = gradient * gain_vec
    inner_sum = jnp.mean(weighted * values_in, axis=1, keepdims=True)
    d_value = inv_rms * weighted - values_in * inv_rms**3 * inner_sum
    d_gain = jnp.sum(gradient * values_in * inv_rms, axis=0)
    return (d_value, d_gain)


def attend_head(packed, allowed, scale_factor):
    query_h, key_h, value_h = packed
    raw_scores = jnp.einsum("th,lh->tl", query_h, key_h, preferred_element_type=jnp.float32)
    logits = jnp.where(allowed, raw_scores * scale_factor, NEG)
    row_max = jnp.max(logits, axis=1, keepdims=True)
    exp_scores = jnp.exp(logits - row_max)
    row_total = jnp.sum(exp_scores, axis=1, keepdims=True)
    attn_probs = (exp_scores / row_total).astype(jnp.bfloat16)
    head_out = jnp.dot(attn_probs, value_h, preferred_element_type=jnp.float32).astype(jnp.bfloat16)
    return (head_out, row_max + jnp.log(row_total))


def attend_back(packed, allowed, scale_factor):
    query_h, key_h, value_h, out_grad, log_total = packed
    raw_scores = jnp.einsum("th,lh->tl", query_h, key_h, preferred_element_type=jnp.float32)
    logits = jnp.where(allowed, raw_scores * scale_factor, NEG)
    attn_probs = jnp.exp(logits - log_total)
    prob_grad = jnp.einsum("th,lh->tl", out_grad, value_h, preferred_element_type=jnp.float32)
    inner_sum = jnp.sum(attn_probs * prob_grad, axis=1, keepdims=True)
    score_grad = (attn_probs * (prob_grad - inner_sum) * scale_factor).astype(jnp.bfloat16)
    query_grad = jnp.dot(score_grad, key_h, preferred_element_type=jnp.float32)
    key_grad = jnp.einsum("tl,th->lh", score_grad, query_h, preferred_element_type=jnp.float32)
    value_grad = jnp.einsum(
        "tl,th->lh", attn_probs.astype(jnp.bfloat16), out_grad, preferred_element_type=jnp.float32
    )
    return (query_grad, key_grad, value_grad)


def local_general(
    hidden,
    cotangent,
    segments,
    padding,
    routes,
    order,
    norm1_gain,
    w_query,
    w_key,
    w_value,
    w_out,
    norm2_gain,
    router,
    shared_gate_vec,
    shared_w_gate,
    shared_w_up,
    shared_w_down,
    expert_w_gate,
    expert_w_up,
    expert_w_down,
):
    fetched = (
        lax.all_gather(norm1_gain, DP, axis=0, tiled=True),
        lax.all_gather(w_query, DP, axis=0, tiled=True),
        lax.all_gather(w_key, DP, axis=0, tiled=True),
        lax.all_gather(w_value, DP, axis=0, tiled=True),
        lax.all_gather(w_out, DP, axis=0, tiled=True),
        lax.all_gather(norm2_gain, DP, axis=0, tiled=True),
        lax.all_gather(router, DP, axis=0, tiled=True),
        lax.all_gather(shared_gate_vec, DP, axis=0, tiled=True),
        lax.all_gather(shared_w_gate, DP, axis=0, tiled=True),
        lax.all_gather(shared_w_up, DP, axis=0, tiled=True),
        lax.all_gather(shared_w_down, DP, axis=0, tiled=True),
        lax.all_gather(expert_w_gate, DP, axis=1, tiled=True),
        lax.all_gather(expert_w_up, DP, axis=1, tiled=True),
        lax.all_gather(expert_w_down, DP, axis=2, tiled=True),
    )
    (
        gain_one,
        query_w,
        key_w,
        value_w,
        out_w,
        gain_two,
        router_full,
        gate_vec,
        sh_gate,
        sh_up,
        sh_down,
        ex_gate,
        ex_up,
        ex_down,
    ) = fetched
    sh_gate, sh_up, sh_down = (
        lax.all_gather(sh_gate, EXP, axis=1, tiled=True),
        lax.all_gather(sh_up, EXP, axis=1, tiled=True),
        lax.all_gather(sh_down, EXP, axis=0, tiled=True),
    )
    tokens_here = hidden.shape[1]
    model_width = hidden.shape[2]
    x_rows = hidden[0].astype(jnp.float32)
    cot_rows = cotangent[0].astype(jnp.float32)
    inv_one = lax.rsqrt(jnp.mean(x_rows * x_rows, axis=1, keepdims=True) + EPS)
    g_one = gain_one.astype(jnp.float32)
    normed_one = (x_rows * inv_one * g_one).astype(jnp.bfloat16)
    queries = jnp.dot(normed_one, query_w, preferred_element_type=jnp.float32).astype(jnp.bfloat16)
    keys_own = jnp.dot(normed_one, key_w, preferred_element_type=jnp.float32).astype(jnp.bfloat16)
    values_own = jnp.dot(normed_one, value_w, preferred_element_type=jnp.float32).astype(
        jnp.bfloat16
    )
    own_codes = jnp.where(padding[0] > 0, segments[0] + 1, 0)
    code_parts = jnp.stack([own_codes // 64, own_codes % 64]).astype(jnp.bfloat16)
    keys_all, values_all, parts_all = (
        lax.all_gather(keys_own, CTX, axis=0, tiled=True),
        lax.all_gather(values_own, CTX, axis=0, tiled=True),
        lax.all_gather(code_parts, CTX, axis=1, tiled=True),
    )
    key_codes = parts_all[0].astype(jnp.int32) * 64 + parts_all[1].astype(jnp.int32)
    seq_total = keys_all.shape[0]
    query_pos = lax.axis_index(CTX) * tokens_here + jnp.arange(tokens_here, dtype=jnp.int32)
    key_pos = jnp.arange(seq_total, dtype=jnp.int32)
    same_doc = key_codes[None, :] == (segments[0] + 1)[:, None]
    allowed = (key_pos[None, :] <= query_pos[:, None]) & (
        same_doc | (key_pos[None, :] == query_pos[:, None])
    )
    scale_factor = HEAD_DIM ** (-0.5)

    def to_heads(rows_in):
        return rows_in.reshape(rows_in.shape[0], HEADS, HEAD_DIM).transpose(1, 0, 2)

    def from_heads(heads_in):
        return heads_in.transpose(1, 0, 2).reshape(heads_in.shape[1], model_width)

    head_q = to_heads(queries)
    head_k = to_heads(keys_all)
    head_v = to_heads(values_all)
    head_out, log_total = lax.map(
        partial(attend_head, allowed=allowed, scale_factor=scale_factor), (head_q, head_k, head_v)
    )
    attended = from_heads(head_out)
    residual = x_rows + jnp.dot(attended, out_w, preferred_element_type=jnp.float32)
    inv_two = lax.rsqrt(jnp.mean(residual * residual, axis=1, keepdims=True) + EPS)
    g_two = gain_two.astype(jnp.float32)
    normed_two = (residual * inv_two * g_two).astype(jnp.bfloat16)
    router_logits = jnp.dot(normed_two, router_full, preferred_element_type=jnp.float32)
    router_exp = jnp.exp(router_logits - jnp.max(router_logits, axis=1, keepdims=True))
    router_probs = router_exp / jnp.sum(router_exp, axis=1, keepdims=True)
    route_gates = jnp.take_along_axis(router_probs, routes[0], axis=1)
    shared_gate = jax.nn.sigmoid(jnp.dot(normed_two, gate_vec, preferred_element_type=jnp.float32))
    shared_scaled = (shared_gate[:, None] * cot_rows).astype(jnp.bfloat16)
    rows_group, grads_group = (normed_two, shared_scaled)
    gate_pre = jnp.dot(rows_group, sh_gate, preferred_element_type=jnp.float32)
    up_pre = jnp.dot(rows_group, sh_up, preferred_element_type=jnp.float32)
    gate_act = gate_pre * jax.nn.sigmoid(gate_pre)
    shared_hidden = (gate_act * up_pre).astype(jnp.bfloat16)
    shared_part = jnp.dot(shared_hidden, sh_down, preferred_element_type=jnp.float32)
    experts_all = router_full.shape[1]
    capacity = (9 * tokens_here * TOP + 8 * experts_all - 1) // (8 * experts_all)
    priority = (order[0, 0][:, None] * TOP + jnp.arange(TOP, dtype=jnp.int32)[None, :]).reshape(-1)
    flat_routes = routes[0].reshape(-1)
    slot_index = block_slots(flat_routes, priority, experts_all)
    kept_rows = slot_index < capacity
    target = flat_routes * capacity + jnp.minimum(slot_index, capacity - 1)
    row_gates = route_gates.reshape(-1)
    cot_repeated = jnp.repeat(cot_rows, TOP, axis=0)
    source_rows = jnp.repeat(normed_two, TOP, axis=0)
    source_grads = (cot_repeated * row_gates[:, None]).astype(jnp.bfloat16)
    empty_slots = jnp.zeros((experts_all * capacity, model_width), jnp.bfloat16)
    send_rows = empty_slots.at[target].add(
        jnp.where(kept_rows[:, None], source_rows, jnp.zeros_like(source_rows))
    )
    send_grads = empty_slots.at[target].add(
        jnp.where(kept_rows[:, None], source_grads, jnp.zeros_like(source_grads))
    )
    recv_rows, recv_grads = (
        lax.all_to_all(
            send_rows.reshape(experts_all, capacity, model_width),
            (EXP, CTX),
            split_axis=0,
            concat_axis=0,
            tiled=True,
        ),
        lax.all_to_all(
            send_grads.reshape(experts_all, capacity, model_width),
            (EXP, CTX),
            split_axis=0,
            concat_axis=0,
            tiled=True,
        ),
    )
    local_count = ex_gate.shape[0]
    sources = experts_all // local_count

    def to_local(buffer_in):
        return (
            buffer_in.reshape(sources, local_count, capacity, model_width)
            .transpose(1, 0, 2, 3)
            .reshape(local_count, sources * capacity, model_width)
        )

    def to_owner(buffer_in):
        return (
            buffer_in.reshape(local_count, sources, capacity, model_width)
            .transpose(1, 0, 2, 3)
            .reshape(experts_all, capacity, model_width)
        )

    expert_rows = to_local(recv_rows)
    expert_grads_in = to_local(recv_grads)
    gate_e = jnp.einsum("erd,edf->erf", expert_rows, ex_gate, preferred_element_type=jnp.float32)
    up_e = jnp.einsum("erd,edf->erf", expert_rows, ex_up, preferred_element_type=jnp.float32)
    act_e = gate_e * jax.nn.sigmoid(gate_e)
    hidden_e = (act_e * up_e).astype(jnp.bfloat16)
    result_e = jnp.einsum(
        "erf,efd->erd", hidden_e, ex_down, preferred_element_type=jnp.float32
    ).astype(jnp.bfloat16)
    returned = lax.all_to_all(
        to_owner(result_e), (EXP, CTX), split_axis=0, concat_axis=0, tiled=True
    )
    picked = returned.reshape(experts_all * capacity, model_width)[target]
    picked = jnp.where(kept_rows[:, None], picked, jnp.zeros_like(picked)).astype(jnp.float32)
    routed = jnp.sum((picked * row_gates[:, None]).reshape(tokens_here, TOP, model_width), axis=1)
    output = (residual + shared_gate[:, None] * shared_part + routed).astype(jnp.bfloat16)
    gate_grads = jnp.sum(picked * cot_repeated, axis=1).reshape(tokens_here, TOP)
    hidden_grad_e = jnp.einsum(
        "erd,efd->erf", expert_grads_in, ex_down, preferred_element_type=jnp.float32
    )
    gate_grad_e = (hidden_grad_e * up_e * silu_grad(gate_e)).astype(jnp.bfloat16)
    up_grad_e = (hidden_grad_e * act_e).astype(jnp.bfloat16)
    grad_ex_down = jnp.einsum(
        "erf,erd->efd", hidden_e, expert_grads_in, preferred_element_type=jnp.float32
    )
    grad_ex_gate = jnp.einsum(
        "erd,erf->edf", expert_rows, gate_grad_e, preferred_element_type=jnp.float32
    )
    grad_ex_up = jnp.einsum(
        "erd,erf->edf", expert_rows, up_grad_e, preferred_element_type=jnp.float32
    )
    expert_sums = (
        lax.psum_scatter(grad_ex_gate, DP, scatter_dimension=1, tiled=True),
        lax.psum_scatter(grad_ex_up, DP, scatter_dimension=1, tiled=True),
        lax.psum_scatter(grad_ex_down, DP, scatter_dimension=2, tiled=True),
    )
    rows_grad_e = jnp.einsum(
        "erf,edf->erd", gate_grad_e, ex_gate, preferred_element_type=jnp.float32
    )
    rows_grad_e = (
        rows_grad_e
        + jnp.einsum("erf,edf->erd", up_grad_e, ex_up, preferred_element_type=jnp.float32)
    ).astype(jnp.bfloat16)
    returned_grads = lax.all_to_all(
        to_owner(rows_grad_e), (EXP, CTX), split_axis=0, concat_axis=0, tiled=True
    )
    routed_grad = returned_grads.reshape(experts_all * capacity, model_width)[target]
    routed_grad = jnp.where(kept_rows[:, None], routed_grad, jnp.zeros_like(routed_grad)).astype(
        jnp.float32
    )
    norm_grad = jnp.sum(routed_grad.reshape(tokens_here, TOP, model_width), axis=1)
    choose = (
        routes[0][:, :, None] == jnp.arange(experts_all, dtype=jnp.int32)[None, None, :]
    ).astype(jnp.float32)
    probs_grad = jnp.einsum("tk,tke->te", gate_grads, choose)
    logit_grad = (
        router_probs * (probs_grad - jnp.sum(router_probs * probs_grad, axis=1, keepdims=True))
    ).astype(jnp.bfloat16)
    grad_router = jnp.dot(normed_two.T, logit_grad, preferred_element_type=jnp.float32)
    gate_logit_grad = (
        jnp.sum(cot_rows * shared_part, axis=1) * shared_gate * (1.0 - shared_gate)
    ).astype(jnp.bfloat16)
    grad_gate_vec = jnp.dot(gate_logit_grad, normed_two, preferred_element_type=jnp.float32)
    norm_grad = norm_grad + jnp.dot(logit_grad, router_full.T, preferred_element_type=jnp.float32)
    norm_grad = (
        norm_grad
        + gate_logit_grad.astype(jnp.float32)[:, None] * gate_vec.astype(jnp.float32)[None, :]
    )
    shared_hgrad = jnp.dot(grads_group, sh_down.T, preferred_element_type=jnp.float32)
    gate_grad_s = (shared_hgrad * up_pre * silu_grad(gate_pre)).astype(jnp.bfloat16)
    up_grad_s = (shared_hgrad * gate_act).astype(jnp.bfloat16)
    shared_rows_grad = jnp.dot(gate_grad_s, sh_gate.T, preferred_element_type=jnp.float32)
    shared_rows_grad = shared_rows_grad + jnp.dot(
        up_grad_s, sh_up.T, preferred_element_type=jnp.float32
    )
    groups = lax.axis_size(EXP)
    parts_cd = lax.axis_size((CTX, DP))
    rows_count = rows_group.shape[0]
    arr_gate = jnp.einsum(
        "td,tes->eds",
        rows_group,
        gate_grad_s.reshape(rows_count, groups, -1),
        preferred_element_type=jnp.float32,
    ).reshape(groups * model_width, -1)
    arr_up = jnp.einsum(
        "td,tes->eds",
        rows_group,
        up_grad_s.reshape(rows_count, groups, -1),
        preferred_element_type=jnp.float32,
    ).reshape(groups * model_width, -1)
    arr_down = jnp.einsum(
        "tes,tcd->ecsd",
        shared_hidden.reshape(rows_count, groups, -1),
        grads_group.reshape(rows_count, parts_cd, -1),
        preferred_element_type=jnp.float32,
    ).reshape(-1, model_width // parts_cd)
    sums_gate, sums_up, sums_down = (
        lax.psum_scatter(arr_gate, (EXP, CTX, DP), scatter_dimension=0, tiled=True),
        lax.psum_scatter(arr_up, (EXP, CTX, DP), scatter_dimension=0, tiled=True),
        lax.psum_scatter(arr_down, (EXP, CTX, DP), scatter_dimension=0, tiled=True),
    )
    norm_grad = norm_grad + shared_rows_grad
    residual_grad, grad_gain_two = norm_back(residual, inv_two, g_two, norm_grad)
    residual_grad = residual_grad + cot_rows
    low_residual = residual_grad.astype(jnp.bfloat16)
    grad_out_w = jnp.dot(attended.T, low_residual, preferred_element_type=jnp.float32)
    attended_grad = jnp.dot(low_residual, out_w.T, preferred_element_type=jnp.float32).astype(
        jnp.bfloat16
    )
    head_q_grad, head_k_grad, head_v_grad = lax.map(
        partial(attend_back, allowed=allowed, scale_factor=scale_factor),
        (head_q, head_k, head_v, to_heads(attended_grad), log_total),
    )
    key_sum, value_sum = (
        lax.psum_scatter(from_heads(head_k_grad), CTX, scatter_dimension=0, tiled=True),
        lax.psum_scatter(from_heads(head_v_grad), CTX, scatter_dimension=0, tiled=True),
    )
    query_low = from_heads(head_q_grad).astype(jnp.bfloat16)
    key_low = key_sum.astype(jnp.bfloat16)
    value_low = value_sum.astype(jnp.bfloat16)
    grad_query = jnp.dot(normed_one.T, query_low, preferred_element_type=jnp.float32)
    grad_key = jnp.dot(normed_one.T, key_low, preferred_element_type=jnp.float32)
    grad_value = jnp.dot(normed_one.T, value_low, preferred_element_type=jnp.float32)
    normed_grad = jnp.dot(query_low, query_w.T, preferred_element_type=jnp.float32)
    normed_grad = normed_grad + jnp.dot(key_low, key_w.T, preferred_element_type=jnp.float32)
    normed_grad = normed_grad + jnp.dot(value_low, value_w.T, preferred_element_type=jnp.float32)
    input_part, grad_gain_one = norm_back(x_rows, inv_one, g_one, normed_grad)
    input_grad = (residual_grad + input_part).astype(jnp.bfloat16)
    dense = (
        lax.psum_scatter(
            grad_gain_one, (EXP, CTX, DP), scatter_dimension=0, tiled=True
        ),
        lax.psum_scatter(grad_query, (EXP, CTX, DP), scatter_dimension=0, tiled=True),
        lax.psum_scatter(grad_key, (EXP, CTX, DP), scatter_dimension=0, tiled=True),
        lax.psum_scatter(grad_value, (EXP, CTX, DP), scatter_dimension=0, tiled=True),
        lax.psum_scatter(grad_out_w, (EXP, CTX, DP), scatter_dimension=0, tiled=True),
        lax.psum_scatter(
            grad_gain_two, (EXP, CTX, DP), scatter_dimension=0, tiled=True
        ),
        lax.psum_scatter(
            grad_router, (EXP, CTX, DP), scatter_dimension=0, tiled=True
        ),
        lax.psum_scatter(
            grad_gate_vec, (EXP, CTX, DP), scatter_dimension=0, tiled=True
        ),
    )
    return (
        output[None],
        input_grad[None],
        dense[0],
        dense[1],
        dense[2],
        dense[3],
        dense[4],
        dense[5],
        dense[6],
        dense[7],
        sums_gate,
        sums_up,
        sums_down,
        expert_sums[0],
        expert_sums[1],
        expert_sums[2],
    )

def attention_probs(q_blk, k_part, q_code, k_code, first_row, scale_factor):
    scores = lax.dot_general(
        q_blk, k_part, (((1,), (1,)), ((), ())), preferred_element_type=jnp.float32
    )
    row = first_row + lax.broadcasted_iota(jnp.int32, scores.shape, 0)
    col = lax.broadcasted_iota(jnp.int32, scores.shape, 1)
    allowed = ((col < row) & (k_code == q_code)) | (col == row)
    logits = jnp.where(allowed, scores * scale_factor, NEG)
    exp_scores = jnp.exp(logits - jnp.max(logits, axis=1, keepdims=True))
    return exp_scores * (1.0 / jnp.sum(exp_scores, axis=1, keepdims=True))


def attend_kernel(heads, step, qkv_ref, q_code_ref, k_code_ref, out_ref):
    seq_len = qkv_ref.shape[0]
    width = heads * HEAD_DIM
    for head in range(heads):
        at = head * HEAD_DIM
        for first in range(0, seq_len, step):
            upto = first + step
            probs = attention_probs(
                qkv_ref[first:upto, at : at + HEAD_DIM],
                qkv_ref[0:upto, width + at : width + at + HEAD_DIM],
                q_code_ref[first:upto, :],
                k_code_ref[0, :, 0:upto],
                first,
                HEAD_DIM**-0.5,
            )
            out_ref[first:upto, at : at + HEAD_DIM] = jnp.dot(
                probs.astype(jnp.bfloat16),
                qkv_ref[0:upto, 2 * width + at : 2 * width + at + HEAD_DIM],
                preferred_element_type=jnp.float32,
            ).astype(jnp.bfloat16)


def attend_back_kernel(
    heads, step, qkv_ref, grad_ref, q_code_ref, k_code_ref, out_ref, key_acc, value_acc
):
    seq_len = qkv_ref.shape[0]
    width = heads * HEAD_DIM
    for head in range(heads):
        at = head * HEAD_DIM
        key_at, value_at = width + at, 2 * width + at
        key_acc[...] = jnp.zeros_like(key_acc)
        value_acc[...] = jnp.zeros_like(value_acc)
        for first in range(0, seq_len, step):
            upto = first + step
            q_blk = qkv_ref[first:upto, at : at + HEAD_DIM]
            k_part = qkv_ref[0:upto, key_at : key_at + HEAD_DIM]
            v_part = qkv_ref[0:upto, value_at : value_at + HEAD_DIM]
            g_blk = grad_ref[first:upto, at : at + HEAD_DIM]
            probs = attention_probs(
                q_blk,
                k_part,
                q_code_ref[first:upto, :],
                k_code_ref[0, :, 0:upto],
                first,
                HEAD_DIM**-0.5,
            )
            prob_grad = lax.dot_general(
                g_blk, v_part, (((1,), (1,)), ((), ())), preferred_element_type=jnp.float32
            )
            inner = jnp.sum(probs * prob_grad, axis=1, keepdims=True)
            score_grad = (probs * (prob_grad - inner) * HEAD_DIM**-0.5).astype(jnp.bfloat16)
            out_ref[first:upto, at : at + HEAD_DIM] = jnp.dot(
                score_grad, k_part, preferred_element_type=jnp.float32
            ).astype(jnp.bfloat16)
            key_acc[0:upto, :] += lax.dot_general(
                score_grad, q_blk, (((0,), (0,)), ((), ())), preferred_element_type=jnp.float32
            )
            value_acc[0:upto, :] += lax.dot_general(
                probs.astype(jnp.bfloat16),
                g_blk,
                (((0,), (0,)), ((), ())),
                preferred_element_type=jnp.float32,
            )
        out_ref[:, key_at : key_at + HEAD_DIM] = key_acc[...].astype(jnp.bfloat16)
        out_ref[:, value_at : value_at + HEAD_DIM] = value_acc[...].astype(jnp.bfloat16)


def attention_call(qkv, grads, q_codes, k_codes, seq_len):
    rows, triple = qkv.shape
    width = triple // 3
    heads = width // HEAD_DIM
    step = min(256, seq_len)
    specs = [pl.BlockSpec((seq_len, triple), lambda s: (s, 0))]
    operands = [qkv]
    if grads is not None:
        specs.append(pl.BlockSpec((seq_len, width), lambda s: (s, 0)))
        operands.append(grads)
    specs += [
        pl.BlockSpec((seq_len, 1), lambda s: (s, 0)),
        pl.BlockSpec((1, 1, seq_len), lambda s: (s, 0, 0)),
    ]
    operands += [q_codes, k_codes]
    out_width = width if grads is None else triple
    body = attend_kernel if grads is None else attend_back_kernel
    passes = 2 if grads is None else 5
    area = rows * seq_len * heads
    return pl.pallas_call(
        partial(body, heads, step),
        grid=(rows // seq_len,),
        in_specs=specs,
        out_specs=pl.BlockSpec((seq_len, out_width), lambda s: (s, 0)),
        out_shape=jax.ShapeDtypeStruct((rows, out_width), jnp.bfloat16),
        scratch_shapes=[]
        if grads is None
        else [pltpu.VMEM((seq_len, HEAD_DIM), jnp.float32)] * 2,
        compiler_params=pltpu.CompilerParams(vmem_limit_bytes=48 * 2**20),
        cost_estimate=pl.CostEstimate(
            flops=2 * passes * area * HEAD_DIM,
            bytes_accessed=2 * rows * (triple + out_width),
            transcendentals=area,
        ),
    )(*operands)


MESH_ID = pl.DeviceIdType.MESH


def other_in_pair(index, bit):
    return index + bit - 2 * bit * (lax.div(index, bit) % 2)


def plane_places():
    at = lax.axis_index(EXP)
    core = lax.axis_index(CTX)
    across, along = other_in_pair(at, 1), other_in_pair(at, 2)
    return at, core, across, along, other_in_pair(along, 1)


def greet(across, along, core):
    barrier = pltpu.get_barrier_semaphore()
    for target in ({EXP: across}, {EXP: along}, {CTX: 1 - core}):
        pl.semaphore_signal(barrier, inc=1, device_id=target, device_id_type=MESH_ID)
    pl.semaphore_wait(barrier, 3)


def plane_gather_kernel(with_info, relative, *refs):
    if with_info:
        own_ref, info_ref, all_ref, info_all_ref, send_sem, recv_sem, local_sem = refs
    else:
        own_ref, all_ref, send_sem, recv_sem, local_sem = refs
    at, core, across, along, far = plane_places()
    rows = own_ref.shape[0]
    half = rows // 2
    top, bottom, whole = pl.ds(0, half), pl.ds(half, half), pl.ds(0, rows)
    greet(across, along, core)
    started = []
    twin_id = {CTX: 1 - core}

    def slot_of(place, shift, for_twin):
        if relative:
            return shift + 4 * for_twin
        return place * 2 + core

    def send(number, src, dst, target):
        copy = pltpu.make_async_remote_copy(
            src_ref=src,
            dst_ref=dst,
            send_sem=send_sem.at[number],
            recv_sem=recv_sem.at[number],
            device_id=target,
            device_id_type=MESH_ID,
        )
        copy.start()
        started.append(copy)
        return copy

    def piece(place, shift, part, for_twin=0):
        return all_ref.at[slot_of(place, shift, for_twin), part]

    x_top = send(0, own_ref.at[top], piece(at, 1, top), {EXP: across})
    y_bottom = send(1, own_ref.at[bottom], piece(at, 2, bottom), {EXP: along})
    x_bottom = send(2, own_ref.at[bottom], piece(at, 1, bottom), {EXP: across})
    y_top = send(3, own_ref.at[top], piece(at, 2, top), {EXP: along})
    twins = [send(4, own_ref, piece(at, 0, whole, 1), twin_id)]
    heres = [pltpu.make_async_copy(own_ref, piece(at, 0, whole), local_sem.at[0])]
    heres[0].start()
    if with_info:
        info_at = lambda place: info_all_ref.at[place * 2 + core]
        heres.append(pltpu.make_async_copy(info_ref, info_at(at), local_sem.at[1]))
        heres[1].start()
        info_x = send(13, info_ref, info_at(at), {EXP: across})
        info_y = send(14, info_ref, info_at(at), {EXP: along})
        twins.append(send(15, info_ref, info_at(at), twin_id))
        info_x.wait_recv()
        info_far = send(16, info_at(across), info_at(across), {EXP: along})
        twins.append(send(17, info_at(across), info_at(across), twin_id))
        info_y.wait_recv()
        twins.append(send(18, info_at(along), info_at(along), twin_id))
        info_far.wait_recv()
        twins.append(send(19, info_at(far), info_at(far), twin_id))

    def hand_on(number, place, shift, part):
        src = piece(place, shift, part)
        twins.append(send(number, src, piece(place, shift, part, 1), twin_id))

    x_top.wait_recv()
    far_top = send(5, piece(across, 1, top), piece(across, 3, top), {EXP: along})
    hand_on(6, across, 1, top)
    y_bottom.wait_recv()
    far_bottom = send(7, piece(along, 2, bottom), piece(along, 3, bottom), {EXP: across})
    hand_on(8, along, 2, bottom)
    x_bottom.wait_recv()
    hand_on(9, across, 1, bottom)
    y_top.wait_recv()
    hand_on(10, along, 2, top)
    far_top.wait_recv()
    hand_on(11, far, 3, top)
    far_bottom.wait_recv()
    hand_on(12, far, 3, bottom)
    for copy in twins:
        copy.wait_recv()
    for copy in started:
        copy.wait_send()
    for copy in heres:
        copy.wait()


def plane_gather(own, info, relative, number):
    plane = lax.axis_size(PLANE)
    operands = [own] if info is None else [own, info]
    outs = [jax.ShapeDtypeStruct((plane, *v.shape), v.dtype) for v in operands]
    anywhere = pl.BlockSpec(memory_space=pl.ANY)
    return pl.pallas_call(
        partial(plane_gather_kernel, info is not None, relative),
        out_shape=outs,
        in_specs=[anywhere] * len(operands),
        out_specs=[anywhere] * len(operands),
        scratch_shapes=[
            pltpu.SemaphoreType.DMA((20,)),
            pltpu.SemaphoreType.DMA((20,)),
            pltpu.SemaphoreType.DMA((2,)),
        ],
        compiler_params=pltpu.CompilerParams(collective_id=number, has_side_effects=True),
        cost_estimate=pl.CostEstimate(
            flops=0, bytes_accessed=own.size, transcendentals=0
        ),
    )(*operands)


def plane_scatter_kernel(relative, with_extra, *refs):
    if with_extra:
        part_ref, extra_ref, out_ref, *refs = refs
        extra_out, refs = refs[:4], refs[4:]
        extra_own, extra_got, extra_sems, refs = refs[0], refs[1], refs[2:5], refs[5:]
    else:
        part_ref, out_ref, *refs = refs
    own, twin_got, x_got, y_got, x_last, y_last, send_sem, recv_sem, local_sem = refs
    at, core, across, along, far = plane_places()
    rows = part_ref.shape[1]
    half = rows // 2
    step = 64
    greet(across, along, core)
    started = []

    def send(number, src, dst, target):
        copy = pltpu.make_async_remote_copy(
            src_ref=src,
            dst_ref=dst,
            send_sem=send_sem.at[number],
            recv_sem=recv_sem.at[number],
            device_id=target,
            device_id_type=MESH_ID,
        )
        copy.start()
        started.append(copy)
        return copy

    twins, heres = [], []
    for j, (label, shift) in enumerate(((far, 3), (across, 1), (along, 2), (at, 0))):
        theirs = shift + 4 if relative else label * 2 + 1 - core
        ours = shift if relative else label * 2 + core
        twins.append(send(j, part_ref.at[theirs], twin_got.at[j], {CTX: 1 - core}))
        here = pltpu.make_async_copy(part_ref.at[ours], own.at[j], local_sem.at[j])
        here.start()
        heres.append(here)

    def add_rows(target, t_first, count, source, s_first):
        @pl.loop(0, count // step)
        def _(i):
            into = pl.ds(pl.multiple_of(t_first + i * step, step), step)
            take = pl.ds(pl.multiple_of(s_first + i * step, step), step)
            total = target[into].astype(jnp.float32) + source[take].astype(jnp.float32)
            target[into] = total.astype(target.dtype)

    top, bottom = pl.ds(0, half), pl.ds(half, half)
    x_sent, y_sent = [], []
    for j in range(4):
        twins[j].wait_recv()
        heres[j].wait()
        add_rows(own.at[j], 0, rows, twin_got.at[j], 0)
        if j < 2:
            x_sent.append(send(4 + j, own.at[j, top], x_got.at[j], {EXP: across}))
        if j == 0 or j == 2:
            y_sent.append(send(6 + j // 2, own.at[j, bottom], y_got.at[j // 2], {EXP: along}))
    if with_extra:
        extra_here, extra_twin, extra_done = [], [], []
        for k in range(4):
            copy = pltpu.make_async_remote_copy(
                src_ref=extra_ref.at[k + 4],
                dst_ref=extra_got.at[k],
                send_sem=extra_sems[0].at[k],
                recv_sem=extra_sems[1].at[k],
                device_id={CTX: 1 - core},
                device_id_type=MESH_ID,
            )
            copy.start()
            started.append(copy)
            extra_twin.append(copy)
            here = pltpu.make_async_copy(extra_ref.at[k], extra_own.at[k], extra_sems[2].at[k])
            here.start()
            extra_here.append(here)
        for k in range(4):
            extra_twin[k].wait_recv()
            extra_here[k].wait()
            add_rows(extra_own.at[k], 0, rows, extra_got.at[k], 0)
            here = pltpu.make_async_copy(extra_own.at[k], extra_out[k], extra_sems[2].at[k])
            here.start()
            extra_done.append(here)
    x_sent[0].wait_recv()
    add_rows(own.at[2], 0, half, x_got.at[0], 0)
    last_y = send(8, own.at[2, top], y_last, {EXP: along})
    y_sent[0].wait_recv()
    add_rows(own.at[1], half, half, y_got.at[0], 0)
    last_x = send(9, own.at[1, bottom], x_last, {EXP: across})

    def finish(first, near, later):
        @pl.loop(0, half // step)
        def _(i):
            take = pl.ds(pl.multiple_of(i * step, step), step)
            into = pl.ds(pl.multiple_of(first + i * step, step), step)
            out_ref[into] = (
                own[3, into].astype(jnp.float32)
                + near[1, take].astype(jnp.float32)
                + later[take].astype(jnp.float32)
            ).astype(out_ref.dtype)

    x_sent[1].wait_recv()
    last_y.wait_recv()
    finish(0, x_got, y_last)
    y_sent[1].wait_recv()
    last_x.wait_recv()
    finish(half, y_got, x_last)
    if with_extra:
        for copy in extra_done:
            copy.wait()
    for copy in started:
        copy.wait_send()


def plane_scatter(parts, relative, number, out_type, extra=None):
    plane, rows, cols = parts.shape
    operands, extra_scratch = [parts], []
    out_shape = [jax.ShapeDtypeStruct((rows, cols), out_type)]
    out_specs = [pl.BlockSpec(memory_space=pltpu.VMEM)]
    anywhere = pl.BlockSpec(memory_space=pl.ANY)
    if extra is not None:
        operands.append(extra)
        out_shape += [jax.ShapeDtypeStruct((rows, cols), extra.dtype)] * 4
        out_specs += [anywhere] * 4
        extra_scratch = [pltpu.VMEM((4, rows, cols), extra.dtype)] * 2
        extra_scratch += [pltpu.SemaphoreType.DMA((4,))] * 3
    half = rows // 2
    vmem = lambda *shape: pltpu.VMEM(shape, parts.dtype)
    return pl.pallas_call(
        partial(plane_scatter_kernel, relative, extra is not None),
        out_shape=out_shape,
        in_specs=[anywhere] * len(operands),
        out_specs=out_specs,
        scratch_shapes=extra_scratch
        + [
            vmem(4, rows, cols),
            vmem(4, rows, cols),
            vmem(2, half, cols),
            vmem(2, half, cols),
            vmem(half, cols),
            vmem(half, cols),
            pltpu.SemaphoreType.DMA((10,)),
            pltpu.SemaphoreType.DMA((10,)),
            pltpu.SemaphoreType.DMA((4,)),
        ],
        compiler_params=pltpu.CompilerParams(
            collective_id=number,
            has_side_effects=True,
            vmem_limit_bytes=(36 if extra is None else 54) * 2**20,
        ),
        cost_estimate=pl.CostEstimate(
            flops=0, bytes_accessed=rows * cols, transcendentals=0
        ),
    )(*operands)


def after(values, others):
    return lax.optimization_barrier((values, others))[0]


def swap(values, bits):
    return lax.ppermute(values, EXP, [(i, i ^ bits) for i in range(4)])


def twin(values):
    return lax.ppermute(values, CTX, [(0, 1), (1, 0)])


def twin_sums(ours, theirs):
    got = twin(theirs)
    return [low(ours[k].astype(jnp.float32) + got[k].astype(jnp.float32)) for k in range(4)]


def hop_sum(sums, later):
    total = sums[0].astype(jnp.float32)
    for k in (1, 2, 3):
        total = total + after(swap(sums[k], k), later).astype(jnp.float32)
    return total


def mm(left, right, dims=((1,), (0,))):
    return lax.dot_general(left, right, (dims, ((), ())), preferred_element_type=jnp.float32)


def low(values):
    return values.astype(jnp.bfloat16)


def local_plane(
    hidden,
    cotangent,
    segments,
    padding,
    routes,
    order,
    norm1_gain,
    w_query,
    w_key,
    w_value,
    w_out,
    norm2_gain,
    router,
    shared_gate_vec,
    shared_w_gate,
    shared_w_up,
    shared_w_down,
    expert_w_gate,
    expert_w_up,
    expert_w_down,
):
    plane = lax.axis_size(PLANE)
    groups = lax.axis_size(EXP)
    halves = lax.axis_size(CTX)
    depth = lax.axis_size(DP)
    me = lax.axis_index(PLANE)
    core = lax.axis_index(CTX)
    tokens, width = hidden.shape[1], hidden.shape[2]
    all_tokens = plane * tokens
    seq_len = halves * tokens
    experts_all = router.shape[1]
    head_cols = width // plane
    shard = width // depth

    token_info = jnp.concatenate(
        [segments + 1, jnp.where(padding > 0, segments + 1, 0), order[0], routes[0].T]
    )
    info_rows = token_info.shape[0]
    token_info = jnp.concatenate([token_info, jnp.zeros((8 - info_rows, tokens), jnp.int32)])

    hidden_all, info_all = plane_gather(hidden[0], token_info, False, 0)
    hidden_all = hidden_all.reshape(all_tokens, width)
    place = lax.axis_index(EXP)
    away = [(place ^ k) * 2 + (core ^ j) for j in (0, 1) for k in range(4)]
    away = jnp.stack(away)
    w_qkv_part = jnp.concatenate(
        [
            lax.dynamic_slice(w, (0, me * head_cols), (shard, head_cols))
            for w in (w_query, w_key, w_value)
        ]
        + [router, norm1_gain[:, None], norm2_gain[:, None], shared_gate_vec[:, None]]
        + [jnp.zeros((shard, 128 - experts_all - 3), jnp.bfloat16)],
        axis=1,
    )
    w_qkv = lax.all_gather(w_qkv_part, DP, axis=0, tiled=True)
    small = w_qkv[:, 3 * head_cols :].T
    w_qkv = w_qkv[:, : 3 * head_cols]
    router_t = small[:experts_all]
    g_one = small[experts_all].astype(jnp.float32)
    g_two = small[experts_all + 1].astype(jnp.float32)
    gate_vec = small[experts_all + 2]
    out_rows = shard // plane
    w_out_part = lax.dynamic_slice(w_out, (me * out_rows, 0), (out_rows, width))
    w_out_part = lax.all_gather(w_out_part, DP, axis=0, tiled=False)
    w_out_part = after(w_out_part, info_all)
    w_out_got = [swap(w_out_part, k) for k in (1, 2, 3)]

    def normed(values, gain):
        values = values.astype(jnp.float32)
        inv = lax.rsqrt(jnp.mean(values * values, axis=1, keepdims=True) + EPS)
        return values, inv, low(values * inv * gain)

    _, _, n1_all = normed(hidden_all, g_one)
    qkv = low(mm(n1_all, w_qkv))
    q_codes = info_all[:, 0].reshape(all_tokens, 1)
    k_codes = info_all[:, 1].reshape(all_tokens // seq_len, 1, seq_len)
    attended_cols = attention_call(qkv, None, q_codes, k_codes, seq_len)
    pieces = [w_out_part] + [after(v, qkv) for v in w_out_got]
    w_out_near = jnp.zeros((depth, groups, 1, out_rows, width), jnp.bfloat16)
    for k in range(4):
        w_out_near = lax.dynamic_update_slice(
            w_out_near, pieces[k][:, None, None], (0, place ^ k, 0, 0, 0)
        )
    w_out_far = twin(w_out_near)
    w_out_full = jnp.where(
        core == 0,
        jnp.concatenate([w_out_near, w_out_far], axis=2),
        jnp.concatenate([w_out_far, w_out_near], axis=2),
    ).reshape(width, width)

    x_rows, inv_one, _ = normed(hidden[0], g_one)
    cot_rows = cotangent[0].astype(jnp.float32)

    def to_tokens(cols):
        got = lax.all_to_all(
            cols.reshape(plane, tokens, head_cols), PLANE, split_axis=0, concat_axis=0, tiled=True
        )
        return got.transpose(1, 0, 2).reshape(tokens, width)

    def to_columns(rows_in):
        send = rows_in.reshape(tokens, plane, head_cols).transpose(1, 0, 2)
        got = lax.all_to_all(send, PLANE, split_axis=0, concat_axis=0, tiled=True)
        return got.reshape(all_tokens, head_cols)

    attended = to_tokens(attended_cols)
    residual = x_rows + mm(attended, w_out_full)
    residual, inv_two, n2 = normed(residual, g_two)

    units = shared_w_gate.shape[1]
    part = units // (depth * halves)
    pick = lambda w: lax.dynamic_index_in_dim(
        w.reshape(w.shape[0], depth, halves, part), core, axis=2, keepdims=False
    ).reshape(w.shape[0], depth * part)
    sh_gate = lax.all_gather(pick(shared_w_gate), DP, axis=0, tiled=True)
    sh_up = lax.all_gather(pick(shared_w_up), DP, axis=0, tiled=True)
    sh_down = lax.all_gather(
        lax.dynamic_slice(shared_w_down, (core * part, 0), (part, width)), DP, axis=0, tiled=True
    )
    n2 = after(n2, (sh_gate, sh_up))
    n2_all = plane_gather(n2, None, True, 2)[0].reshape(all_tokens, width)
    cot_own = after(cotangent[0], n2_all)
    cot_got = [swap(cot_own, k) for k in (1, 2, 3)]
    ex_gate = lax.all_gather(after(expert_w_gate[0], info_all), DP, axis=0, tiled=True)
    ex_up = lax.all_gather(after(expert_w_up[0], info_all), DP, axis=0, tiled=True)
    ex_down = lax.all_gather(after(expert_w_down[0], info_all), DP, axis=1, tiled=True)

    small_w = jnp.concatenate([router_t, gate_vec[None]])

    def gates_of(rows_in):
        both = mm(rows_in, small_w, ((1,), (1,)))
        z = both[:, :experts_all]
        e = jnp.exp(z - jnp.max(z, axis=1, keepdims=True))
        return e / jnp.sum(e, axis=1, keepdims=True), jax.nn.sigmoid(both[:, experts_all:])

    probs_all, sg_all = gates_of(n2_all)
    expert_gate = lax.dynamic_slice(probs_all, (0, me), (all_tokens, 1))

    capacity = (9 * tokens * TOP + 8 * experts_all - 1) // (8 * experts_all)
    info_away = info_all[away]
    order_all = info_away[:, 2]
    routed_here = jnp.any(info_away[:, 3 : 3 + TOP] == me, axis=1)
    earlier = (order_all[:, None, :] < order_all[:, :, None]) & routed_here[:, None, :]
    slots = jnp.sum(earlier.astype(jnp.int32), axis=2)
    slots = jnp.where(routed_here, slots, capacity)
    chosen = slots[:, None, :] == jnp.arange(capacity, dtype=jnp.int32)[None, :, None]
    onehot = chosen.astype(jnp.bfloat16)

    def rows_of(values):
        got = lax.dot_general(
            onehot,
            values.reshape(plane, tokens, width),
            (((2,), (1,)), ((0,), (0,))),
            preferred_element_type=jnp.float32,
        )
        return got.reshape(plane * capacity, width)

    def back_to_tokens(values):
        got = lax.dot_general(
            onehot,
            values.reshape(plane, capacity, width),
            (((1,), (1,)), ((0,), (0,))),
            preferred_element_type=jnp.float32,
        )
        return got.reshape(all_tokens, width)

    slot_gates = jnp.sum(
        jnp.where(chosen, expert_gate.reshape(plane, 1, tokens), 0.0), axis=2
    ).reshape(plane * capacity, 1)
    expert_rows = low(rows_of(n2_all))
    gate_pre = mm(n2_all, sh_gate)
    up_pre = mm(n2_all, sh_up)
    gate_act = gate_pre * jax.nn.sigmoid(gate_pre)
    shared_hidden = low(gate_act * up_pre)
    expert_rows = after(expert_rows, (shared_hidden, sh_down))
    gate_e = mm(expert_rows, ex_gate)
    up_e = mm(expert_rows, ex_up)
    act_e = gate_e * jax.nn.sigmoid(gate_e)
    hidden_e = low(act_e * up_e)
    cot_near = jnp.concatenate([cot_own] + [after(v, hidden_e) for v in cot_got])
    cot_all = jnp.concatenate([cot_near, twin(cot_near)])
    row_cots = low(rows_of(cot_all))
    row_grads = low(row_cots.astype(jnp.float32) * slot_gates)

    shared_grads = low(sg_all * cot_all.astype(jnp.float32))
    shared_part = mm(shared_hidden, sh_down)
    cot_dot_shared = jnp.sum(shared_part * cot_all.astype(jnp.float32), axis=1)
    shared_hgrad = mm(shared_grads, sh_down, ((1,), (1,)))
    gate_grad_s = low(shared_hgrad * up_pre * silu_grad(gate_pre))
    up_grad_s = low(shared_hgrad * gate_act)

    rows_out = width // (halves * depth)

    def shared_scatter(first, second):
        keep = jnp.where(core == 0, first, second)
        got = twin(jnp.where(core == 0, second, first))
        both = jnp.where(core == 0, jnp.stack([keep, got]), jnp.stack([got, keep]))
        both = both.reshape(halves, depth, part, rows_out).transpose(1, 0, 2, 3)
        return both.reshape(units, rows_out).astype(jnp.float32)

    grad_sh_gate = low(mm(gate_grad_s, n2_all, ((0,), (0,))))
    grad_sh_up = low(mm(up_grad_s, n2_all, ((0,), (0,))))
    grad_sh_down = low(mm(shared_hidden, shared_grads, ((0,), (0,))))

    result_e = low(mm(hidden_e, ex_down))
    row_dots = jnp.sum(result_e.astype(jnp.float32) * row_cots.astype(jnp.float32), axis=1)
    gate_dots = jnp.sum(
        jnp.where(chosen, row_dots.reshape(plane, capacity, 1), 0.0), axis=1
    )
    hgrad_e = mm(row_grads, ex_down, ((1,), (1,)))
    gate_grad_e = low(hgrad_e * up_e * silu_grad(gate_e))
    up_grad_e = low(hgrad_e * act_e)

    grad_ex_down = low(mm(hidden_e, row_grads, ((0,), (0,))))
    grad_ex_gate = low(mm(expert_rows, gate_grad_e, ((0,), (0,))))
    grad_ex_up = low(mm(expert_rows, up_grad_e, ((0,), (0,))))
    scatter = lambda v, dim: lax.psum_scatter(v, DP, scatter_dimension=dim, tiled=True)
    side = width // halves
    shared_sums = [
        [scatter(v[:, c * side : (c + 1) * side], 1) for c in range(halves)]
        for v in (grad_sh_gate, grad_sh_up, grad_sh_down)
    ]
    grads_made = (grad_ex_down, grad_ex_gate, grad_ex_up)
    grads = [scatter(v, dim) for v, dim in zip(grads_made, (1, 0, 0))]
    result_e, gate_grad_s = after((result_e, gate_grad_s), grads_made)
    rows_grad = low(
        mm(gate_grad_e, ex_gate, ((1,), (1,))) + mm(up_grad_e, ex_up, ((1,), (1,)))
    )

    out_part = low(sg_all * shared_part + expert_gate * back_to_tokens(result_e))
    n2_grad_part = low(
        mm(gate_grad_s, sh_gate, ((1,), (1,)))
        + mm(up_grad_s, sh_up, ((1,), (1,)))
        + back_to_tokens(rows_grad)
    )
    n2_grad_part = after(n2_grad_part, (out_part, shared_sums))
    n2_grad, *out_sums = plane_scatter(
        n2_grad_part.reshape(plane, tokens, width),
        True,
        3,
        jnp.float32,
        out_part.reshape(plane, tokens, width),
    )

    dots = jnp.stack([gate_dots, cot_dot_shared.reshape(plane, tokens)], axis=1)
    back = jnp.arange(plane, dtype=jnp.int32) ^ me
    dots = dots[(back // 2) + 4 * (back % 2)]
    dots = lax.all_to_all(dots, PLANE, split_axis=0, concat_axis=0, tiled=True)
    probs_grad = dots[:, 0].T
    probs, sg = gates_of(n2)
    logit_grad = low(probs * (probs_grad - jnp.sum(probs * probs_grad, axis=1, keepdims=True)))
    sg_logit_grad = low(jnp.sum(dots[:, 1], axis=0)[:, None] * sg * (1.0 - sg))
    small_grads = mm(n2, jnp.concatenate([logit_grad, sg_logit_grad], axis=1), ((0,), (0,)))
    n2_grad = (
        n2_grad
        + mm(logit_grad, router_t)
        + sg_logit_grad.astype(jnp.float32) * gate_vec.astype(jnp.float32)[None]
    )
    residual_grad, grad_gain_two = norm_back(residual, inv_two, g_two, n2_grad)
    residual_grad = residual_grad + cot_rows
    low_residual = low(residual_grad)

    small_grads = jnp.concatenate([small_grads, grad_gain_two[:, None]], axis=1).T
    small_grads = jnp.pad(small_grads, ((0, 14 - experts_all), (0, 0)))
    small_grads = small_grads.reshape(16, plane, width // plane).transpose(1, 0, 2)
    small_grads = jnp.sum(
        lax.all_to_all(small_grads, PLANE, split_axis=0, concat_axis=0, tiled=True), axis=0
    )
    small_grads = small_grads.reshape(16, depth, shard // plane).transpose(1, 0, 2)
    small_grads = jnp.sum(
        lax.all_to_all(small_grads, DP, split_axis=0, concat_axis=0, tiled=True), axis=0
    )
    grad_out = low(mm(attended, low_residual, ((0,), (0,))))
    grad_out = grad_out.reshape(groups, halves, width // plane, width)
    block_of = lambda k, c: lax.dynamic_slice(
        grad_out, (place ^ k, c, 0, 0), (1, 1, width // plane, width)
    )[0, 0]
    attended_grad = to_columns(low(mm(low_residual, w_out_full, ((1,), (1,)))))
    out_grad_sums = twin_sums(
        [block_of(k, core) for k in range(4)],
        jnp.stack([block_of(k, 1 - core) for k in range(4)]),
    )
    attended_grad = after(attended_grad, (out_grad_sums, grads[0]))
    qkv_grad = attention_call(qkv, attended_grad, q_codes, k_codes, seq_len)
    grad_qkv = low(mm(n1_all, qkv_grad, ((0,), (0,))))
    n1_grad = low(mm(qkv_grad, w_qkv, ((1,), (1,))))
    grad_out = low(hop_sum(out_grad_sums, (n1_grad, grad_qkv)))
    n1_grad = after(n1_grad, (grad_qkv, grad_out, grads[1]))
    grad_out = lax.psum_scatter(grad_out, DP, scatter_dimension=0, tiled=True)
    n1_grad = plane_scatter(n1_grad.reshape(plane, tokens, width), False, 1, jnp.float32)[0]
    output = low(residual + hop_sum(out_sums, n1_grad))
    grad_sh_gate, grad_sh_up, grad_sh_down = [
        shared_scatter(*after(v, n1_grad)) for v in shared_sums
    ]
    grad_sh_gate, grad_sh_up = grad_sh_gate.T, grad_sh_up.T
    fine = shard // plane
    grad_qkv = (
        grad_qkv.reshape(plane, depth, fine, 3 * head_cols)
        .transpose(1, 0, 2, 3)
        .reshape(width, 3 * head_cols)
    )
    grad_qkv = lax.psum_scatter(grad_qkv, DP, scatter_dimension=0, tiled=True)
    w_rows = (
        w_qkv.reshape(plane, depth, fine, 3 * head_cols)
        .transpose(1, 0, 2, 3)
        .reshape(depth, plane * fine, 3 * head_cols)
    )
    w_rows = lax.dynamic_index_in_dim(w_rows, lax.axis_index(DP), axis=0, keepdims=False)
    gain_dots = jnp.sum(grad_qkv.astype(jnp.float32) * w_rows.astype(jnp.float32), axis=1)
    gain_dots = lax.all_to_all(
        gain_dots.reshape(plane, 1, fine), PLANE, split_axis=0, concat_axis=0, tiled=True
    )
    my_gain = lax.dynamic_slice(
        g_one, ((me * depth + lax.axis_index(DP)) * fine,), (fine,)
    )
    grad_gain_one = jnp.sum(gain_dots[:, 0], axis=0) / my_gain
    grad_qkv = lax.all_to_all(
        grad_qkv.reshape(plane, fine, 3 * head_cols),
        PLANE,
        split_axis=0,
        concat_axis=0,
        tiled=True,
    )
    grad_qkv = (
        grad_qkv.reshape(plane, fine, 3, head_cols)
        .transpose(2, 1, 0, 3)
        .reshape(3, fine, width)
        .astype(jnp.float32)
    )
    grad_out = after(grad_out, n1_grad).astype(jnp.float32)
    grad_ex_down, grad_ex_gate, grad_ex_up = [
        after(v, n1_grad).astype(jnp.float32)[None] for v in grads
    ]
    input_part, _ = norm_back(x_rows, inv_one, g_one, n1_grad)
    input_grad = low(residual_grad + input_part)
    return (
        output[None],
        input_grad[None],
        grad_gain_one,
        grad_qkv[0],
        grad_qkv[1],
        grad_qkv[2],
        grad_out,
        small_grads[experts_all + 1],
        small_grads[:experts_all].T,
        small_grads[experts_all],
        grad_sh_gate,
        grad_sh_up,
        grad_sh_down,
        grad_ex_gate,
        grad_ex_up,
        grad_ex_down,
    )


def solution(mesh):
    in_specs = (
        P((EXP, DP), CTX, None),
        P((EXP, DP), CTX, None),
        P((EXP, DP), CTX),
        P((EXP, DP), CTX),
        P((EXP, DP), CTX, None),
        P((EXP, DP), CTX, None),
        P(DP),
        P(DP, None),
        P(DP, None),
        P(DP, None),
        P(DP, None),
        P(DP),
        P(DP, None),
        P(DP),
        P(DP, EXP),
        P(DP, EXP),
        P((EXP, DP), None),
        P((EXP, CTX), DP, None),
        P((EXP, CTX), DP, None),
        P((EXP, CTX), None, DP),
    )
    out_specs = (
        P((EXP, DP), CTX, None),
        P((EXP, DP), CTX, None),
        P((EXP, CTX, DP)),
        P((EXP, CTX, DP), None),
        P((EXP, CTX, DP), None),
        P((EXP, CTX, DP), None),
        P((EXP, CTX, DP), None),
        P((EXP, CTX, DP)),
        P((EXP, CTX, DP), None),
        P((EXP, CTX, DP)),
        P((CTX, DP), EXP),
        P((CTX, DP), EXP),
        P(EXP, (CTX, DP)),
        P((EXP, CTX), DP, None),
        P((EXP, CTX), DP, None),
        P((EXP, CTX), None, DP),
    )
    plane = mesh.shape[EXP] * mesh.shape[CTX]

    def run(*args):
        square = mesh.shape[EXP] == 4 and mesh.shape[CTX] == 2
        one_each = square and args[12].shape[1] == plane
        local = local_plane if one_each else local_general
        return jax.shard_map(
            local, mesh=mesh, in_specs=in_specs, out_specs=out_specs, check_vma=False
        )(*args)

    return run
```

```python
from functools import partial

import jax
import jax.numpy as jnp
from jax import lax
from jax.experimental import pallas as pl
from jax.experimental.pallas import tpu as pltpu
from jax.sharding import PartitionSpec as P

EXP, CTX, DP = "experts", "context", "dp"
PLANE = (EXP, CTX)
HEADS = 16
HEAD_DIM = 128
TOP = 4


EPS = 1e-06
NEG = -1e30


def silu_grad(pre_act):
    logistic = jax.nn.sigmoid(pre_act)
    return logistic * (1.0 + pre_act * (1.0 - logistic))


def block_slots(route_row, priority, expert_count):
    matches = (route_row[:, None] == jnp.arange(expert_count, dtype=jnp.int32)[None, :]).astype(
        jnp.int32
    )
    ordered = jnp.zeros_like(matches).at[priority].set(matches)
    before = jnp.cumsum(ordered, axis=0) - ordered
    return jnp.sum(before[priority] * matches, axis=1)


def norm_back(values_in, inv_rms, gain_vec, gradient):
    weighted = gradient * gain_vec
    inner_sum = jnp.mean(weighted * values_in, axis=1, keepdims=True)
    d_value = inv_rms * weighted - values_in * inv_rms**3 * inner_sum
    d_gain = jnp.sum(gradient * values_in * inv_rms, axis=0)
    return (d_value, d_gain)


def attend_head(packed, allowed, scale_factor):
    query_h, key_h, value_h = packed
    raw_scores = jnp.einsum("th,lh->tl", query_h, key_h, preferred_element_type=jnp.float32)
    logits = jnp.where(allowed, raw_scores * scale_factor, NEG)
    row_max = jnp.max(logits, axis=1, keepdims=True)
    exp_scores = jnp.exp(logits - row_max)
    row_total = jnp.sum(exp_scores, axis=1, keepdims=True)
    attn_probs = (exp_scores / row_total).astype(jnp.bfloat16)
    head_out = jnp.dot(attn_probs, value_h, preferred_element_type=jnp.float32).astype(jnp.bfloat16)
    return (head_out, row_max + jnp.log(row_total))


def attend_back(packed, allowed, scale_factor):
    query_h, key_h, value_h, out_grad, log_total = packed
    raw_scores = jnp.einsum("th,lh->tl", query_h, key_h, preferred_element_type=jnp.float32)
    logits = jnp.where(allowed, raw_scores * scale_factor, NEG)
    attn_probs = jnp.exp(logits - log_total)
    prob_grad = jnp.einsum("th,lh->tl", out_grad, value_h, preferred_element_type=jnp.float32)
    inner_sum = jnp.sum(attn_probs * prob_grad, axis=1, keepdims=True)
    score_grad = (attn_probs * (prob_grad - inner_sum) * scale_factor).astype(jnp.bfloat16)
    query_grad = jnp.dot(score_grad, key_h, preferred_element_type=jnp.float32)
    key_grad = jnp.einsum("tl,th->lh", score_grad, query_h, preferred_element_type=jnp.float32)
    value_grad = jnp.einsum(
        "tl,th->lh", attn_probs.astype(jnp.bfloat16), out_grad, preferred_element_type=jnp.float32
    )
    return (query_grad, key_grad, value_grad)


def local_general(
    hidden,
    cotangent,
    segments,
    padding,
    routes,
    order,
    norm1_gain,
    w_query,
    w_key,
    w_value,
    w_out,
    norm2_gain,
    router,
    shared_gate_vec,
    shared_w_gate,
    shared_w_up,
    shared_w_down,
    expert_w_gate,
    expert_w_up,
    expert_w_down,
):
    fetched = (
        lax.all_gather(norm1_gain, DP, axis=0, tiled=True),
        lax.all_gather(w_query, DP, axis=0, tiled=True),
        lax.all_gather(w_key, DP, axis=0, tiled=True),
        lax.all_gather(w_value, DP, axis=0, tiled=True),
        lax.all_gather(w_out, DP, axis=0, tiled=True),
        lax.all_gather(norm2_gain, DP, axis=0, tiled=True),
        lax.all_gather(router, DP, axis=0, tiled=True),
        lax.all_gather(shared_gate_vec, DP, axis=0, tiled=True),
        lax.all_gather(shared_w_gate, DP, axis=0, tiled=True),
        lax.all_gather(shared_w_up, DP, axis=0, tiled=True),
        lax.all_gather(shared_w_down, DP, axis=0, tiled=True),
        lax.all_gather(expert_w_gate, DP, axis=1, tiled=True),
        lax.all_gather(expert_w_up, DP, axis=1, tiled=True),
        lax.all_gather(expert_w_down, DP, axis=2, tiled=True),
    )
    (
        gain_one,
        query_w,
        key_w,
        value_w,
        out_w,
        gain_two,
        router_full,
        gate_vec,
        sh_gate,
        sh_up,
        sh_down,
        ex_gate,
        ex_up,
        ex_down,
    ) = fetched
    sh_gate, sh_up, sh_down = (
        lax.all_gather(sh_gate, EXP, axis=1, tiled=True),
        lax.all_gather(sh_up, EXP, axis=1, tiled=True),
        lax.all_gather(sh_down, EXP, axis=0, tiled=True),
    )
    tokens_here = hidden.shape[1]
    model_width = hidden.shape[2]
    x_rows = hidden[0].astype(jnp.float32)
    cot_rows = cotangent[0].astype(jnp.float32)
    inv_one = lax.rsqrt(jnp.mean(x_rows * x_rows, axis=1, keepdims=True) + EPS)
    g_one = gain_one.astype(jnp.float32)
    normed_one = (x_rows * inv_one * g_one).astype(jnp.bfloat16)
    queries = jnp.dot(normed_one, query_w, preferred_element_type=jnp.float32).astype(jnp.bfloat16)
    keys_own = jnp.dot(normed_one, key_w, preferred_element_type=jnp.float32).astype(jnp.bfloat16)
    values_own = jnp.dot(normed_one, value_w, preferred_element_type=jnp.float32).astype(
        jnp.bfloat16
    )
    own_codes = jnp.where(padding[0] > 0, segments[0] + 1, 0)
    code_parts = jnp.stack([own_codes // 64, own_codes % 64]).astype(jnp.bfloat16)
    keys_all, values_all, parts_all = (
        lax.all_gather(keys_own, CTX, axis=0, tiled=True),
        lax.all_gather(values_own, CTX, axis=0, tiled=True),
        lax.all_gather(code_parts, CTX, axis=1, tiled=True),
    )
    key_codes = parts_all[0].astype(jnp.int32) * 64 + parts_all[1].astype(jnp.int32)
    seq_total = keys_all.shape[0]
    query_pos = lax.axis_index(CTX) * tokens_here + jnp.arange(tokens_here, dtype=jnp.int32)
    key_pos = jnp.arange(seq_total, dtype=jnp.int32)
    same_doc = key_codes[None, :] == (segments[0] + 1)[:, None]
    allowed = (key_pos[None, :] <= query_pos[:, None]) & (
        same_doc | (key_pos[None, :] == query_pos[:, None])
    )
    scale_factor = HEAD_DIM ** (-0.5)

    def to_heads(rows_in):
        return rows_in.reshape(rows_in.shape[0], HEADS, HEAD_DIM).transpose(1, 0, 2)

    def from_heads(heads_in):
        return heads_in.transpose(1, 0, 2).reshape(heads_in.shape[1], model_width)

    head_q = to_heads(queries)
    head_k = to_heads(keys_all)
    head_v = to_heads(values_all)
    head_out, log_total = lax.map(
        partial(attend_head, allowed=allowed, scale_factor=scale_factor), (head_q, head_k, head_v)
    )
    attended = from_heads(head_out)
    residual = x_rows + jnp.dot(attended, out_w, preferred_element_type=jnp.float32)
    inv_two = lax.rsqrt(jnp.mean(residual * residual, axis=1, keepdims=True) + EPS)
    g_two = gain_two.astype(jnp.float32)
    normed_two = (residual * inv_two * g_two).astype(jnp.bfloat16)
    router_logits = jnp.dot(normed_two, router_full, preferred_element_type=jnp.float32)
    router_exp = jnp.exp(router_logits - jnp.max(router_logits, axis=1, keepdims=True))
    router_probs = router_exp / jnp.sum(router_exp, axis=1, keepdims=True)
    route_gates = jnp.take_along_axis(router_probs, routes[0], axis=1)
    shared_gate = jax.nn.sigmoid(jnp.dot(normed_two, gate_vec, preferred_element_type=jnp.float32))
    shared_scaled = (shared_gate[:, None] * cot_rows).astype(jnp.bfloat16)
    rows_group, grads_group = (normed_two, shared_scaled)
    gate_pre = jnp.dot(rows_group, sh_gate, preferred_element_type=jnp.float32)
    up_pre = jnp.dot(rows_group, sh_up, preferred_element_type=jnp.float32)
    gate_act = gate_pre * jax.nn.sigmoid(gate_pre)
    shared_hidden = (gate_act * up_pre).astype(jnp.bfloat16)
    shared_part = jnp.dot(shared_hidden, sh_down, preferred_element_type=jnp.float32)
    experts_all = router_full.shape[1]
    capacity = (9 * tokens_here * TOP + 8 * experts_all - 1) // (8 * experts_all)
    priority = (order[0, 0][:, None] * TOP + jnp.arange(TOP, dtype=jnp.int32)[None, :]).reshape(-1)
    flat_routes = routes[0].reshape(-1)
    slot_index = block_slots(flat_routes, priority, experts_all)
    kept_rows = slot_index < capacity
    target = flat_routes * capacity + jnp.minimum(slot_index, capacity - 1)
    row_gates = route_gates.reshape(-1)
    cot_repeated = jnp.repeat(cot_rows, TOP, axis=0)
    source_rows = jnp.repeat(normed_two, TOP, axis=0)
    source_grads = (cot_repeated * row_gates[:, None]).astype(jnp.bfloat16)
    empty_slots = jnp.zeros((experts_all * capacity, model_width), jnp.bfloat16)
    send_rows = empty_slots.at[target].add(
        jnp.where(kept_rows[:, None], source_rows, jnp.zeros_like(source_rows))
    )
    send_grads = empty_slots.at[target].add(
        jnp.where(kept_rows[:, None], source_grads, jnp.zeros_like(source_grads))
    )
    recv_rows, recv_grads = (
        lax.all_to_all(
            send_rows.reshape(experts_all, capacity, model_width),
            (EXP, CTX),
            split_axis=0,
            concat_axis=0,
            tiled=True,
        ),
        lax.all_to_all(
            send_grads.reshape(experts_all, capacity, model_width),
            (EXP, CTX),
            split_axis=0,
            concat_axis=0,
            tiled=True,
        ),
    )
    local_count = ex_gate.shape[0]
    sources = experts_all // local_count

    def to_local(buffer_in):
        return (
            buffer_in.reshape(sources, local_count, capacity, model_width)
            .transpose(1, 0, 2, 3)
            .reshape(local_count, sources * capacity, model_width)
        )

    def to_owner(buffer_in):
        return (
            buffer_in.reshape(local_count, sources, capacity, model_width)
            .transpose(1, 0, 2, 3)
            .reshape(experts_all, capacity, model_width)
        )

    expert_rows = to_local(recv_rows)
    expert_grads_in = to_local(recv_grads)
    gate_e = jnp.einsum("erd,edf->erf", expert_rows, ex_gate, preferred_element_type=jnp.float32)
    up_e = jnp.einsum("erd,edf->erf", expert_rows, ex_up, preferred_element_type=jnp.float32)
    act_e = gate_e * jax.nn.sigmoid(gate_e)
    hidden_e = (act_e * up_e).astype(jnp.bfloat16)
    result_e = jnp.einsum(
        "erf,efd->erd", hidden_e, ex_down, preferred_element_type=jnp.float32
    ).astype(jnp.bfloat16)
    returned = lax.all_to_all(
        to_owner(result_e), (EXP, CTX), split_axis=0, concat_axis=0, tiled=True
    )
    picked = returned.reshape(experts_all * capacity, model_width)[target]
    picked = jnp.where(kept_rows[:, None], picked, jnp.zeros_like(picked)).astype(jnp.float32)
    routed = jnp.sum((picked * row_gates[:, None]).reshape(tokens_here, TOP, model_width), axis=1)
    output = (residual + shared_gate[:, None] * shared_part + routed).astype(jnp.bfloat16)
    gate_grads = jnp.sum(picked * cot_repeated, axis=1).reshape(tokens_here, TOP)
    hidden_grad_e = jnp.einsum(
        "erd,efd->erf", expert_grads_in, ex_down, preferred_element_type=jnp.float32
    )
    gate_grad_e = (hidden_grad_e * up_e * silu_grad(gate_e)).astype(jnp.bfloat16)
    up_grad_e = (hidden_grad_e * act_e).astype(jnp.bfloat16)
    grad_ex_down = jnp.einsum(
        "erf,erd->efd", hidden_e, expert_grads_in, preferred_element_type=jnp.float32
    )
    grad_ex_gate = jnp.einsum(
        "erd,erf->edf", expert_rows, gate_grad_e, preferred_element_type=jnp.float32
    )
    grad_ex_up = jnp.einsum(
        "erd,erf->edf", expert_rows, up_grad_e, preferred_element_type=jnp.float32
    )
    expert_sums = (
        lax.psum_scatter(grad_ex_gate, DP, scatter_dimension=1, tiled=True),
        lax.psum_scatter(grad_ex_up, DP, scatter_dimension=1, tiled=True),
        lax.psum_scatter(grad_ex_down, DP, scatter_dimension=2, tiled=True),
    )
    rows_grad_e = jnp.einsum(
        "erf,edf->erd", gate_grad_e, ex_gate, preferred_element_type=jnp.float32
    )
    rows_grad_e = (
        rows_grad_e
        + jnp.einsum("erf,edf->erd", up_grad_e, ex_up, preferred_element_type=jnp.float32)
    ).astype(jnp.bfloat16)
    returned_grads = lax.all_to_all(
        to_owner(rows_grad_e), (EXP, CTX), split_axis=0, concat_axis=0, tiled=True
    )
    routed_grad = returned_grads.reshape(experts_all * capacity, model_width)[target]
    routed_grad = jnp.where(kept_rows[:, None], routed_grad, jnp.zeros_like(routed_grad)).astype(
        jnp.float32
    )
    norm_grad = jnp.sum(routed_grad.reshape(tokens_here, TOP, model_width), axis=1)
    choose = (
        routes[0][:, :, None] == jnp.arange(experts_all, dtype=jnp.int32)[None, None, :]
    ).astype(jnp.float32)
    probs_grad = jnp.einsum("tk,tke->te", gate_grads, choose)
    logit_grad = (
        router_probs * (probs_grad - jnp.sum(router_probs * probs_grad, axis=1, keepdims=True))
    ).astype(jnp.bfloat16)
    grad_router = jnp.dot(normed_two.T, logit_grad, preferred_element_type=jnp.float32)
    gate_logit_grad = (
        jnp.sum(cot_rows * shared_part, axis=1) * shared_gate * (1.0 - shared_gate)
    ).astype(jnp.bfloat16)
    grad_gate_vec = jnp.dot(gate_logit_grad, normed_two, preferred_element_type=jnp.float32)
    norm_grad = norm_grad + jnp.dot(logit_grad, router_full.T, preferred_element_type=jnp.float32)
    norm_grad = (
        norm_grad
        + gate_logit_grad.astype(jnp.float32)[:, None] * gate_vec.astype(jnp.float32)[None, :]
    )
    shared_hgrad = jnp.dot(grads_group, sh_down.T, preferred_element_type=jnp.float32)
    gate_grad_s = (shared_hgrad * up_pre * silu_grad(gate_pre)).astype(jnp.bfloat16)
    up_grad_s = (shared_hgrad * gate_act).astype(jnp.bfloat16)
    shared_rows_grad = jnp.dot(gate_grad_s, sh_gate.T, preferred_element_type=jnp.float32)
    shared_rows_grad = shared_rows_grad + jnp.dot(
        up_grad_s, sh_up.T, preferred_element_type=jnp.float32
    )
    groups = lax.axis_size(EXP)
    parts_cd = lax.axis_size((CTX, DP))
    rows_count = rows_group.shape[0]
    arr_gate = jnp.einsum(
        "td,tes->eds",
        rows_group,
        gate_grad_s.reshape(rows_count, groups, -1),
        preferred_element_type=jnp.float32,
    ).reshape(groups * model_width, -1)
    arr_up = jnp.einsum(
        "td,tes->eds",
        rows_group,
        up_grad_s.reshape(rows_count, groups, -1),
        preferred_element_type=jnp.float32,
    ).reshape(groups * model_width, -1)
    arr_down = jnp.einsum(
        "tes,tcd->ecsd",
        shared_hidden.reshape(rows_count, groups, -1),
        grads_group.reshape(rows_count, parts_cd, -1),
        preferred_element_type=jnp.float32,
    ).reshape(-1, model_width // parts_cd)
    sums_gate, sums_up, sums_down = (
        lax.psum_scatter(arr_gate, (EXP, CTX, DP), scatter_dimension=0, tiled=True),
        lax.psum_scatter(arr_up, (EXP, CTX, DP), scatter_dimension=0, tiled=True),
        lax.psum_scatter(arr_down, (EXP, CTX, DP), scatter_dimension=0, tiled=True),
    )
    norm_grad = norm_grad + shared_rows_grad
    residual_grad, grad_gain_two = norm_back(residual, inv_two, g_two, norm_grad)
    residual_grad = residual_grad + cot_rows
    low_residual = residual_grad.astype(jnp.bfloat16)
    grad_out_w = jnp.dot(attended.T, low_residual, preferred_element_type=jnp.float32)
    attended_grad = jnp.dot(low_residual, out_w.T, preferred_element_type=jnp.float32).astype(
        jnp.bfloat16
    )
    head_q_grad, head_k_grad, head_v_grad = lax.map(
        partial(attend_back, allowed=allowed, scale_factor=scale_factor),
        (head_q, head_k, head_v, to_heads(attended_grad), log_total),
    )
    key_sum, value_sum = (
        lax.psum_scatter(from_heads(head_k_grad), CTX, scatter_dimension=0, tiled=True),
        lax.psum_scatter(from_heads(head_v_grad), CTX, scatter_dimension=0, tiled=True),
    )
    query_low = from_heads(head_q_grad).astype(jnp.bfloat16)
    key_low = key_sum.astype(jnp.bfloat16)
    value_low = value_sum.astype(jnp.bfloat16)
    grad_query = jnp.dot(normed_one.T, query_low, preferred_element_type=jnp.float32)
    grad_key = jnp.dot(normed_one.T, key_low, preferred_element_type=jnp.float32)
    grad_value = jnp.dot(normed_one.T, value_low, preferred_element_type=jnp.float32)
    normed_grad = jnp.dot(query_low, query_w.T, preferred_element_type=jnp.float32)
    normed_grad = normed_grad + jnp.dot(key_low, key_w.T, preferred_element_type=jnp.float32)
    normed_grad = normed_grad + jnp.dot(value_low, value_w.T, preferred_element_type=jnp.float32)
    input_part, grad_gain_one = norm_back(x_rows, inv_one, g_one, normed_grad)
    input_grad = (residual_grad + input_part).astype(jnp.bfloat16)
    dense = (
        lax.psum_scatter(
            grad_gain_one, (EXP, CTX, DP), scatter_dimension=0, tiled=True
        ),
        lax.psum_scatter(grad_query, (EXP, CTX, DP), scatter_dimension=0, tiled=True),
        lax.psum_scatter(grad_key, (EXP, CTX, DP), scatter_dimension=0, tiled=True),
        lax.psum_scatter(grad_value, (EXP, CTX, DP), scatter_dimension=0, tiled=True),
        lax.psum_scatter(grad_out_w, (EXP, CTX, DP), scatter_dimension=0, tiled=True),
        lax.psum_scatter(
            grad_gain_two, (EXP, CTX, DP), scatter_dimension=0, tiled=True
        ),
        lax.psum_scatter(
            grad_router, (EXP, CTX, DP), scatter_dimension=0, tiled=True
        ),
        lax.psum_scatter(
            grad_gate_vec, (EXP, CTX, DP), scatter_dimension=0, tiled=True
        ),
    )
    return (
        output[None],
        input_grad[None],
        dense[0],
        dense[1],
        dense[2],
        dense[3],
        dense[4],
        dense[5],
        dense[6],
        dense[7],
        sums_gate,
        sums_up,
        sums_down,
        expert_sums[0],
        expert_sums[1],
        expert_sums[2],
    )

def attention_probs(q_blk, k_part, q_code, k_code, first_row, scale_factor):
    scores = lax.dot_general(
        q_blk, k_part, (((1,), (1,)), ((), ())), preferred_element_type=jnp.float32
    )
    row = first_row + lax.broadcasted_iota(jnp.int32, scores.shape, 0)
    col = lax.broadcasted_iota(jnp.int32, scores.shape, 1)
    allowed = ((col < row) & (k_code == q_code)) | (col == row)
    logits = jnp.where(allowed, scores * scale_factor, NEG)
    exp_scores = jnp.exp(logits - jnp.max(logits, axis=1, keepdims=True))
    return exp_scores * (1.0 / jnp.sum(exp_scores, axis=1, keepdims=True))


def attend_kernel(heads, step, qkv_ref, q_code_ref, k_code_ref, out_ref):
    seq_len = qkv_ref.shape[0]
    width = heads * HEAD_DIM
    for head in range(heads):
        at = head * HEAD_DIM
        for first in range(0, seq_len, step):
            upto = first + step
            probs = attention_probs(
                qkv_ref[first:upto, at : at + HEAD_DIM],
                qkv_ref[0:upto, width + at : width + at + HEAD_DIM],
                q_code_ref[first:upto, :],
                k_code_ref[0, :, 0:upto],
                first,
                HEAD_DIM**-0.5,
            )
            out_ref[first:upto, at : at + HEAD_DIM] = jnp.dot(
                probs.astype(jnp.bfloat16),
                qkv_ref[0:upto, 2 * width + at : 2 * width + at + HEAD_DIM],
                preferred_element_type=jnp.float32,
            ).astype(jnp.bfloat16)


def attend_back_kernel(
    heads, step, qkv_ref, grad_ref, q_code_ref, k_code_ref, out_ref, key_acc, value_acc
):
    seq_len = qkv_ref.shape[0]
    width = heads * HEAD_DIM
    for head in range(heads):
        at = head * HEAD_DIM
        key_at, value_at = width + at, 2 * width + at
        key_acc[...] = jnp.zeros_like(key_acc)
        value_acc[...] = jnp.zeros_like(value_acc)
        for first in range(0, seq_len, step):
            upto = first + step
            q_blk = qkv_ref[first:upto, at : at + HEAD_DIM]
            k_part = qkv_ref[0:upto, key_at : key_at + HEAD_DIM]
            v_part = qkv_ref[0:upto, value_at : value_at + HEAD_DIM]
            g_blk = grad_ref[first:upto, at : at + HEAD_DIM]
            probs = attention_probs(
                q_blk,
                k_part,
                q_code_ref[first:upto, :],
                k_code_ref[0, :, 0:upto],
                first,
                HEAD_DIM**-0.5,
            )
            prob_grad = lax.dot_general(
                g_blk, v_part, (((1,), (1,)), ((), ())), preferred_element_type=jnp.float32
            )
            inner = jnp.sum(probs * prob_grad, axis=1, keepdims=True)
            score_grad = (probs * (prob_grad - inner) * HEAD_DIM**-0.5).astype(jnp.bfloat16)
            out_ref[first:upto, at : at + HEAD_DIM] = jnp.dot(
                score_grad, k_part, preferred_element_type=jnp.float32
            ).astype(jnp.bfloat16)
            key_acc[0:upto, :] += lax.dot_general(
                score_grad, q_blk, (((0,), (0,)), ((), ())), preferred_element_type=jnp.float32
            )
            value_acc[0:upto, :] += lax.dot_general(
                probs.astype(jnp.bfloat16),
                g_blk,
                (((0,), (0,)), ((), ())),
                preferred_element_type=jnp.float32,
            )
        out_ref[:, key_at : key_at + HEAD_DIM] = key_acc[...].astype(jnp.bfloat16)
        out_ref[:, value_at : value_at + HEAD_DIM] = value_acc[...].astype(jnp.bfloat16)


def attention_call(qkv, grads, q_codes, k_codes, seq_len):
    rows, triple = qkv.shape
    width = triple // 3
    heads = width // HEAD_DIM
    step = min(256, seq_len)
    specs = [pl.BlockSpec((seq_len, triple), lambda s: (s, 0))]
    operands = [qkv]
    if grads is not None:
        specs.append(pl.BlockSpec((seq_len, width), lambda s: (s, 0)))
        operands.append(grads)
    specs += [
        pl.BlockSpec((seq_len, 1), lambda s: (s, 0)),
        pl.BlockSpec((1, 1, seq_len), lambda s: (s, 0, 0)),
    ]
    operands += [q_codes, k_codes]
    out_width = width if grads is None else triple
    body = attend_kernel if grads is None else attend_back_kernel
    passes = 2 if grads is None else 5
    area = rows * seq_len * heads
    return pl.pallas_call(
        partial(body, heads, step),
        grid=(rows // seq_len,),
        in_specs=specs,
        out_specs=pl.BlockSpec((seq_len, out_width), lambda s: (s, 0)),
        out_shape=jax.ShapeDtypeStruct((rows, out_width), jnp.bfloat16),
        scratch_shapes=[]
        if grads is None
        else [pltpu.VMEM((seq_len, HEAD_DIM), jnp.float32)] * 2,
        compiler_params=pltpu.CompilerParams(vmem_limit_bytes=48 * 2**20),
        cost_estimate=pl.CostEstimate(
            flops=2 * passes * area * HEAD_DIM,
            bytes_accessed=2 * rows * (triple + out_width),
            transcendentals=area,
        ),
    )(*operands)


MESH_ID = pl.DeviceIdType.MESH


def other_in_pair(index, bit):
    return index + bit - 2 * bit * (lax.div(index, bit) % 2)


def plane_places():
    at = lax.axis_index(EXP)
    core = lax.axis_index(CTX)
    across, along = other_in_pair(at, 1), other_in_pair(at, 2)
    return at, core, across, along, other_in_pair(along, 1)


def greet(across, along, core):
    barrier = pltpu.get_barrier_semaphore()
    for target in ({EXP: across}, {EXP: along}, {CTX: 1 - core}):
        pl.semaphore_signal(barrier, inc=1, device_id=target, device_id_type=MESH_ID)
    pl.semaphore_wait(barrier, 3)


def plane_gather_kernel(with_info, relative, *refs):
    if with_info:
        own_ref, info_ref, all_ref, info_all_ref, send_sem, recv_sem, local_sem = refs
    else:
        own_ref, all_ref, send_sem, recv_sem, local_sem = refs
    at, core, across, along, far = plane_places()
    rows = own_ref.shape[0]
    half = rows // 2
    top, bottom, whole = pl.ds(0, half), pl.ds(half, half), pl.ds(0, rows)
    greet(across, along, core)
    started = []
    twin_id = {CTX: 1 - core}

    def slot_of(place, shift, for_twin):
        if relative:
            return shift + 4 * for_twin
        return place * 2 + core

    def send(number, src, dst, target):
        copy = pltpu.make_async_remote_copy(
            src_ref=src,
            dst_ref=dst,
            send_sem=send_sem.at[number],
            recv_sem=recv_sem.at[number],
            device_id=target,
            device_id_type=MESH_ID,
        )
        copy.start()
        started.append(copy)
        return copy

    def piece(place, shift, part, for_twin=0):
        return all_ref.at[slot_of(place, shift, for_twin), part]

    x_top = send(0, own_ref.at[top], piece(at, 1, top), {EXP: across})
    y_bottom = send(1, own_ref.at[bottom], piece(at, 2, bottom), {EXP: along})
    x_bottom = send(2, own_ref.at[bottom], piece(at, 1, bottom), {EXP: across})
    y_top = send(3, own_ref.at[top], piece(at, 2, top), {EXP: along})
    twins = [send(4, own_ref, piece(at, 0, whole, 1), twin_id)]
    heres = [pltpu.make_async_copy(own_ref, piece(at, 0, whole), local_sem.at[0])]
    heres[0].start()
    if with_info:
        info_at = lambda place: info_all_ref.at[place * 2 + core]
        heres.append(pltpu.make_async_copy(info_ref, info_at(at), local_sem.at[1]))
        heres[1].start()
        info_x = send(13, info_ref, info_at(at), {EXP: across})
        info_y = send(14, info_ref, info_at(at), {EXP: along})
        twins.append(send(15, info_ref, info_at(at), twin_id))
        info_x.wait_recv()
        info_far = send(16, info_at(across), info_at(across), {EXP: along})
        twins.append(send(17, info_at(across), info_at(across), twin_id))
        info_y.wait_recv()
        twins.append(send(18, info_at(along), info_at(along), twin_id))
        info_far.wait_recv()
        twins.append(send(19, info_at(far), info_at(far), twin_id))

    def hand_on(number, place, shift, part):
        src = piece(place, shift, part)
        twins.append(send(number, src, piece(place, shift, part, 1), twin_id))

    x_top.wait_recv()
    far_top = send(5, piece(across, 1, top), piece(across, 3, top), {EXP: along})
    hand_on(6, across, 1, top)
    y_bottom.wait_recv()
    far_bottom = send(7, piece(along, 2, bottom), piece(along, 3, bottom), {EXP: across})
    hand_on(8, along, 2, bottom)
    x_bottom.wait_recv()
    hand_on(9, across, 1, bottom)
    y_top.wait_recv()
    hand_on(10, along, 2, top)
    far_top.wait_recv()
    hand_on(11, far, 3, top)
    far_bottom.wait_recv()
    hand_on(12, far, 3, bottom)
    for copy in twins:
        copy.wait_recv()
    for copy in started:
        copy.wait_send()
    for copy in heres:
        copy.wait()


def plane_gather(own, info, relative, number):
    plane = lax.axis_size(PLANE)
    operands = [own] if info is None else [own, info]
    outs = [jax.ShapeDtypeStruct((plane, *v.shape), v.dtype) for v in operands]
    anywhere = pl.BlockSpec(memory_space=pl.ANY)
    return pl.pallas_call(
        partial(plane_gather_kernel, info is not None, relative),
        out_shape=outs,
        in_specs=[anywhere] * len(operands),
        out_specs=[anywhere] * len(operands),
        scratch_shapes=[
            pltpu.SemaphoreType.DMA((20,)),
            pltpu.SemaphoreType.DMA((20,)),
            pltpu.SemaphoreType.DMA((2,)),
        ],
        compiler_params=pltpu.CompilerParams(collective_id=number, has_side_effects=True),
        cost_estimate=pl.CostEstimate(
            flops=0, bytes_accessed=own.size, transcendentals=0
        ),
    )(*operands)


def plane_scatter_kernel(relative, with_extra, *refs):
    if with_extra:
        part_ref, extra_ref, out_ref, *refs = refs
        extra_out, refs = refs[:4], refs[4:]
        extra_own, extra_got, extra_sems, refs = refs[0], refs[1], refs[2:5], refs[5:]
    else:
        part_ref, out_ref, *refs = refs
    own, twin_got, x_got, y_got, x_last, y_last, send_sem, recv_sem, local_sem = refs
    at, core, across, along, far = plane_places()
    rows = part_ref.shape[1]
    half = rows // 2
    step = 64
    greet(across, along, core)
    started = []

    def send(number, src, dst, target):
        copy = pltpu.make_async_remote_copy(
            src_ref=src,
            dst_ref=dst,
            send_sem=send_sem.at[number],
            recv_sem=recv_sem.at[number],
            device_id=target,
            device_id_type=MESH_ID,
        )
        copy.start()
        started.append(copy)
        return copy

    twins, heres = [], []
    for j, (label, shift) in enumerate(((far, 3), (across, 1), (along, 2), (at, 0))):
        theirs = shift + 4 if relative else label * 2 + 1 - core
        ours = shift if relative else label * 2 + core
        twins.append(send(j, part_ref.at[theirs], twin_got.at[j], {CTX: 1 - core}))
        here = pltpu.make_async_copy(part_ref.at[ours], own.at[j], local_sem.at[j])
        here.start()
        heres.append(here)

    def add_rows(target, t_first, count, source, s_first):
        @pl.loop(0, count // step)
        def _(i):
            into = pl.ds(pl.multiple_of(t_first + i * step, step), step)
            take = pl.ds(pl.multiple_of(s_first + i * step, step), step)
            total = target[into].astype(jnp.float32) + source[take].astype(jnp.float32)
            target[into] = total.astype(target.dtype)

    top, bottom = pl.ds(0, half), pl.ds(half, half)
    x_sent, y_sent = [], []
    for j in range(4):
        twins[j].wait_recv()
        heres[j].wait()
        add_rows(own.at[j], 0, rows, twin_got.at[j], 0)
        if j < 2:
            x_sent.append(send(4 + j, own.at[j, top], x_got.at[j], {EXP: across}))
        if j == 0 or j == 2:
            y_sent.append(send(6 + j // 2, own.at[j, bottom], y_got.at[j // 2], {EXP: along}))
    if with_extra:
        extra_here, extra_twin, extra_done = [], [], []
        for k in range(4):
            copy = pltpu.make_async_remote_copy(
                src_ref=extra_ref.at[k + 4],
                dst_ref=extra_got.at[k],
                send_sem=extra_sems[0].at[k],
                recv_sem=extra_sems[1].at[k],
                device_id={CTX: 1 - core},
                device_id_type=MESH_ID,
            )
            copy.start()
            started.append(copy)
            extra_twin.append(copy)
            here = pltpu.make_async_copy(extra_ref.at[k], extra_own.at[k], extra_sems[2].at[k])
            here.start()
            extra_here.append(here)
        for k in range(4):
            extra_twin[k].wait_recv()
            extra_here[k].wait()
            add_rows(extra_own.at[k], 0, rows, extra_got.at[k], 0)
            here = pltpu.make_async_copy(extra_own.at[k], extra_out[k], extra_sems[2].at[k])
            here.start()
            extra_done.append(here)
    x_sent[0].wait_recv()
    add_rows(own.at[2], 0, half, x_got.at[0], 0)
    last_y = send(8, own.at[2, top], y_last, {EXP: along})
    y_sent[0].wait_recv()
    add_rows(own.at[1], half, half, y_got.at[0], 0)
    last_x = send(9, own.at[1, bottom], x_last, {EXP: across})

    def finish(first, near, later):
        @pl.loop(0, half // step)
        def _(i):
            take = pl.ds(pl.multiple_of(i * step, step), step)
            into = pl.ds(pl.multiple_of(first + i * step, step), step)
            out_ref[into] = (
                own[3, into].astype(jnp.float32)
                + near[1, take].astype(jnp.float32)
                + later[take].astype(jnp.float32)
            ).astype(out_ref.dtype)

    x_sent[1].wait_recv()
    last_y.wait_recv()
    finish(0, x_got, y_last)
    y_sent[1].wait_recv()
    last_x.wait_recv()
    finish(half, y_got, x_last)
    if with_extra:
        for copy in extra_done:
            copy.wait()
    for copy in started:
        copy.wait_send()


def plane_scatter(parts, relative, number, out_type, extra=None):
    plane, rows, cols = parts.shape
    operands, extra_scratch = [parts], []
    out_shape = [jax.ShapeDtypeStruct((rows, cols), out_type)]
    out_specs = [pl.BlockSpec(memory_space=pltpu.VMEM)]
    anywhere = pl.BlockSpec(memory_space=pl.ANY)
    if extra is not None:
        operands.append(extra)
        out_shape += [jax.ShapeDtypeStruct((rows, cols), extra.dtype)] * 4
        out_specs += [anywhere] * 4
        extra_scratch = [pltpu.VMEM((4, rows, cols), extra.dtype)] * 2
        extra_scratch += [pltpu.SemaphoreType.DMA((4,))] * 3
    half = rows // 2
    vmem = lambda *shape: pltpu.VMEM(shape, parts.dtype)
    return pl.pallas_call(
        partial(plane_scatter_kernel, relative, extra is not None),
        out_shape=out_shape,
        in_specs=[anywhere] * len(operands),
        out_specs=out_specs,
        scratch_shapes=extra_scratch
        + [
            vmem(4, rows, cols),
            vmem(4, rows, cols),
            vmem(2, half, cols),
            vmem(2, half, cols),
            vmem(half, cols),
            vmem(half, cols),
            pltpu.SemaphoreType.DMA((10,)),
            pltpu.SemaphoreType.DMA((10,)),
            pltpu.SemaphoreType.DMA((4,)),
        ],
        compiler_params=pltpu.CompilerParams(
            collective_id=number,
            has_side_effects=True,
            vmem_limit_bytes=(36 if extra is None else 54) * 2**20,
        ),
        cost_estimate=pl.CostEstimate(
            flops=0, bytes_accessed=rows * cols, transcendentals=0
        ),
    )(*operands)


def chosen_rows(slots, capacity):
    lanes = lax.broadcasted_iota(jnp.int32, (slots.shape[0], capacity), 1)
    return (slots == lanes).astype(jnp.bfloat16)


def output_kernel(
    half,
    hidden_ref,
    down_ref,
    rows_ref,
    slot_ref,
    sg_ref,
    gate_ref,
    cot_ref,
    near_ref,
    dots_ref,
    given,
    got,
    send_sem,
    recv_sem,
):
    step_at = pl.program_id(0)
    is_far = step_at < half
    slot = lax.rem(step_at, half)
    twin_id = {CTX: 1 - lax.axis_index(CTX)}

    @pl.when(step_at == 0)
    def _():
        barrier = pltpu.get_barrier_semaphore()
        pl.semaphore_signal(barrier, inc=1, device_id=twin_id, device_id_type=MESH_ID)
        pl.semaphore_wait(barrier, 1)

    def block_copy(k):
        return pltpu.make_async_remote_copy(
            src_ref=given.at[k],
            dst_ref=got.at[k],
            send_sem=send_sem.at[k],
            recv_sem=recv_sem.at[k],
            device_id=twin_id,
            device_id_type=MESH_ID,
        )

    @pl.when(jnp.logical_not(is_far))
    def _():
        block_copy(slot).wait_recv()

    chosen = chosen_rows(slot_ref[...], rows_ref.shape[1])
    width = down_ref.shape[1]
    step = 512
    gate_dot, shared_dot = 0.0, 0.0
    for first in range(0, width, step):
        cols = pl.ds(first, step)
        shared = mm(hidden_ref[...], down_ref[:, cols], ((0,), (0,)))
        picked = mm(chosen, rows_ref[0, :, cols])
        cot = cot_ref[:, cols].astype(jnp.float32)
        gate_dot += jnp.sum(picked * cot, axis=1, keepdims=True)
        shared_dot += jnp.sum(shared * cot, axis=1, keepdims=True)
        total = sg_ref[...] * shared + gate_ref[...] * picked

        @pl.when(is_far)
        def _():
            given[slot, :, cols] = low(total)

        @pl.when(jnp.logical_not(is_far))
        def _():
            near_ref[0, :, cols] = low(total + got[slot, :, cols].astype(jnp.float32))

    lanes = lax.broadcasted_iota(jnp.int32, dots_ref.shape, 1)
    dots_ref[...] = jnp.where(lanes == 0, gate_dot, jnp.where(lanes == 1, shared_dot, 0.0))

    @pl.when(is_far)
    def _():
        block_copy(slot).start()

    @pl.when(step_at == 2 * half - 1)
    def _():
        for k in range(half):
            block_copy(k).wait_send()


def output_parts(hidden, down, rows, slots, sg, gates, cot):
    blocks, capacity, width = rows.shape
    units, count = hidden.shape
    tokens, half = count // blocks, blocks // 2
    at = lambda i: lax.rem(i + half, blocks)
    column = pl.BlockSpec((tokens, 1), lambda i: (at(i), 0))
    return pl.pallas_call(
        partial(output_kernel, half),
        grid=(blocks,),
        in_specs=[
            pl.BlockSpec((units, tokens), lambda i: (0, at(i))),
            pl.BlockSpec((units, width), lambda i: (0, 0)),
            pl.BlockSpec((1, capacity, width), lambda i: (at(i), 0, 0)),
            column,
            column,
            column,
            pl.BlockSpec((tokens, width), lambda i: (at(i), 0)),
        ],
        out_specs=[
            pl.BlockSpec((1, tokens, width), lambda i: (jnp.maximum(i - half, 0), 0, 0)),
            pl.BlockSpec((tokens, 128), lambda i: (at(i), 0)),
        ],
        out_shape=[
            jax.ShapeDtypeStruct((half, tokens, width), jnp.bfloat16),
            jax.ShapeDtypeStruct((count, 128), jnp.float32),
        ],
        scratch_shapes=[
            pltpu.VMEM((half, tokens, width), jnp.bfloat16),
            pltpu.VMEM((half, tokens, width), jnp.bfloat16),
            pltpu.SemaphoreType.DMA((half,)),
            pltpu.SemaphoreType.DMA((half,)),
        ],
        compiler_params=pltpu.CompilerParams(
            collective_id=4, has_side_effects=True, vmem_limit_bytes=56 * 2**20
        ),
        cost_estimate=pl.CostEstimate(
            flops=2 * count * width * (units + capacity),
            bytes_accessed=6 * count * width,
            transcendentals=0,
        ),
    )(hidden, down, rows, slots, sg, gates, cot)


def n2_grad_kernel(dgate_ref, dup_ref, gate_ref, up_ref, rows_ref, slot_ref, out_ref):
    chosen = chosen_rows(slot_ref[...], rows_ref.shape[1])
    step = 512
    for first in range(0, gate_ref.shape[1], step):
        cols = pl.ds(first, step)
        total = mm(dgate_ref[...], gate_ref[:, cols], ((0,), (0,)))
        total += mm(dup_ref[...], up_ref[:, cols], ((0,), (0,)))
        out_ref[0, :, cols] = low(total + mm(chosen, rows_ref[0, :, cols]))


def n2_grad_parts(dgate, dup, gate_w, up_w, rows, slots):
    blocks, capacity, width = rows.shape
    units, count = dgate.shape
    tokens = count // blocks
    by_units = pl.BlockSpec((units, tokens), lambda i: (0, i))
    whole = pl.BlockSpec((units, width), lambda i: (0, 0))
    return pl.pallas_call(
        n2_grad_kernel,
        grid=(blocks,),
        in_specs=[
            by_units,
            by_units,
            whole,
            whole,
            pl.BlockSpec((1, capacity, width), lambda i: (i, 0, 0)),
            pl.BlockSpec((tokens, 1), lambda i: (i, 0)),
        ],
        out_specs=pl.BlockSpec((1, tokens, width), lambda i: (i, 0, 0)),
        out_shape=jax.ShapeDtypeStruct((blocks, tokens, width), jnp.bfloat16),
        compiler_params=pltpu.CompilerParams(vmem_limit_bytes=48 * 2**20),
        cost_estimate=pl.CostEstimate(
            flops=2 * count * width * (2 * units + capacity),
            bytes_accessed=4 * count * width,
            transcendentals=0,
        ),
    )(dgate, dup, gate_w, up_w, rows, slots)


def unit_grad_kernel(left_ref, right_ref, out_ref):
    out_ref[0] = low(mm(left_ref[...], right_ref[...]))


def unit_grads(left, right, depth, halves):
    units, count = left.shape
    width = right.shape[1]
    cols = width // (depth * halves)
    return pl.pallas_call(
        unit_grad_kernel,
        grid=(depth * halves,),
        in_specs=[
            pl.BlockSpec((units, count), lambda i: (0, 0)),
            pl.BlockSpec((count, cols), lambda i: (0, i)),
        ],
        out_specs=pl.BlockSpec((1, units, cols), lambda i: (lax.rem(i, depth), 0, i // depth)),
        out_shape=jax.ShapeDtypeStruct((depth, units, halves * cols), jnp.bfloat16),
        compiler_params=pltpu.CompilerParams(vmem_limit_bytes=48 * 2**20),
        cost_estimate=pl.CostEstimate(
            flops=2 * units * count * width,
            bytes_accessed=2 * (units * count + count * width + units * width),
            transcendentals=0,
        ),
    )(left, right)


def after(values, others):
    return lax.optimization_barrier((values, others))[0]


def swap(values, bits):
    return lax.ppermute(values, EXP, [(i, i ^ bits) for i in range(4)])


def twin(values):
    return lax.ppermute(values, CTX, [(0, 1), (1, 0)])


def twin_sums(ours, theirs):
    got = twin(theirs)
    return [low(ours[k].astype(jnp.float32) + got[k].astype(jnp.float32)) for k in range(4)]


def hops(sums):
    return [sums[0]] + [swap(sums[k], k) for k in (1, 2, 3)]


def sum_up(parts):
    return sum(v.astype(jnp.float32) for v in parts)


def mm(left, right, dims=((1,), (0,))):
    return lax.dot_general(left, right, (dims, ((), ())), preferred_element_type=jnp.float32)


def low(values):
    return values.astype(jnp.bfloat16)


def local_plane(
    hidden,
    cotangent,
    segments,
    padding,
    routes,
    order,
    norm1_gain,
    w_query,
    w_key,
    w_value,
    w_out,
    norm2_gain,
    router,
    shared_gate_vec,
    shared_w_gate,
    shared_w_up,
    shared_w_down,
    expert_w_gate,
    expert_w_up,
    expert_w_down,
):
    plane = lax.axis_size(PLANE)
    groups = lax.axis_size(EXP)
    halves = lax.axis_size(CTX)
    depth = lax.axis_size(DP)
    me = lax.axis_index(PLANE)
    core = lax.axis_index(CTX)
    tokens, width = hidden.shape[1], hidden.shape[2]
    all_tokens = plane * tokens
    seq_len = halves * tokens
    experts_all = router.shape[1]
    head_cols = width // plane
    shard = width // depth

    token_info = jnp.concatenate(
        [segments + 1, jnp.where(padding > 0, segments + 1, 0), order[0], routes[0].T]
    )
    info_rows = token_info.shape[0]
    token_info = jnp.concatenate([token_info, jnp.zeros((8 - info_rows, tokens), jnp.int32)])

    hidden_all, info_all = plane_gather(hidden[0], token_info, False, 0)
    hidden_all = hidden_all.reshape(all_tokens, width)
    place = lax.axis_index(EXP)
    away = [(place ^ k) * 2 + (core ^ j) for j in (0, 1) for k in range(4)]
    away = jnp.stack(away)
    w_qkv_part = jnp.concatenate(
        [
            lax.dynamic_slice(w, (0, me * head_cols), (shard, head_cols))
            for w in (w_query, w_key, w_value)
        ]
        + [router, norm1_gain[:, None], norm2_gain[:, None], shared_gate_vec[:, None]]
        + [jnp.zeros((shard, 128 - experts_all - 3), jnp.bfloat16)],
        axis=1,
    )
    w_qkv = lax.all_gather(w_qkv_part, DP, axis=0, tiled=True)
    small = w_qkv[:, 3 * head_cols :].T
    w_qkv = w_qkv[:, : 3 * head_cols]
    router_t = small[:experts_all]
    g_one = small[experts_all].astype(jnp.float32)
    g_two = small[experts_all + 1].astype(jnp.float32)
    gate_vec = small[experts_all + 2]
    out_rows = shard // plane
    w_out_part = lax.dynamic_slice(w_out, (me * out_rows, 0), (out_rows, width))
    w_out_part = lax.all_gather(w_out_part, DP, axis=0, tiled=False)
    w_out_part = after(w_out_part, info_all)
    w_out_got = [swap(w_out_part, k) for k in (1, 2, 3)]

    def normed(values, gain):
        values = values.astype(jnp.float32)
        inv = lax.rsqrt(jnp.mean(values * values, axis=1, keepdims=True) + EPS)
        return values, inv, low(values * inv * gain)

    _, _, n1_all = normed(hidden_all, g_one)
    qkv = low(mm(n1_all, w_qkv))
    q_codes = info_all[:, 0].reshape(all_tokens, 1)
    k_codes = info_all[:, 1].reshape(all_tokens // seq_len, 1, seq_len)
    attended_cols = attention_call(qkv, None, q_codes, k_codes, seq_len)
    pieces = [w_out_part] + [after(v, qkv) for v in w_out_got]
    w_out_near = jnp.zeros((depth, groups, 1, out_rows, width), jnp.bfloat16)
    for k in range(4):
        w_out_near = lax.dynamic_update_slice(
            w_out_near, pieces[k][:, None, None], (0, place ^ k, 0, 0, 0)
        )
    w_out_far = twin(w_out_near)
    w_out_full = jnp.where(
        core == 0,
        jnp.concatenate([w_out_near, w_out_far], axis=2),
        jnp.concatenate([w_out_far, w_out_near], axis=2),
    ).reshape(width, width)

    x_rows, inv_one, _ = normed(hidden[0], g_one)
    cot_rows = cotangent[0].astype(jnp.float32)

    def to_tokens(cols):
        got = lax.all_to_all(
            cols.reshape(plane, tokens, head_cols), PLANE, split_axis=0, concat_axis=0, tiled=True
        )
        return got.transpose(1, 0, 2).reshape(tokens, width)

    def to_columns(rows_in):
        send = rows_in.reshape(tokens, plane, head_cols).transpose(1, 0, 2)
        got = lax.all_to_all(send, PLANE, split_axis=0, concat_axis=0, tiled=True)
        return got.reshape(all_tokens, head_cols)

    attended = to_tokens(attended_cols)
    residual = x_rows + mm(attended, w_out_full)
    residual, inv_two, n2 = normed(residual, g_two)

    units = shared_w_gate.shape[1]
    part = units // (depth * halves)
    pick = lambda w: lax.dynamic_index_in_dim(
        w.reshape(w.shape[0], depth, halves, part), core, axis=2, keepdims=False
    ).reshape(w.shape[0], depth * part)
    sh_gate = lax.all_gather(pick(shared_w_gate), DP, axis=0, tiled=True)
    sh_up = lax.all_gather(pick(shared_w_up), DP, axis=0, tiled=True)
    sh_gate_t, sh_up_t = sh_gate.T, sh_up.T
    sh_down = lax.all_gather(
        lax.dynamic_slice(shared_w_down, (core * part, 0), (part, width)), DP, axis=0, tiled=True
    )
    n2 = after(n2, (sh_gate, sh_up))
    n2_all = plane_gather(n2, None, True, 2)[0].reshape(all_tokens, width)
    cot_own = after(cotangent[0], n2_all)
    cot_got = [swap(cot_own, k) for k in (1, 2, 3)]
    ex_gate = lax.all_gather(after(expert_w_gate[0], info_all), DP, axis=0, tiled=True)
    ex_up = lax.all_gather(after(expert_w_up[0], info_all), DP, axis=0, tiled=True)
    ex_down = lax.all_gather(after(expert_w_down[0], info_all), DP, axis=1, tiled=True)

    small_w = jnp.concatenate([router_t, gate_vec[None]])

    def gates_of(rows_in):
        both = mm(rows_in, small_w, ((1,), (1,)))
        z = both[:, :experts_all]
        e = jnp.exp(z - jnp.max(z, axis=1, keepdims=True))
        return e / jnp.sum(e, axis=1, keepdims=True), jax.nn.sigmoid(both[:, experts_all:])

    probs_all, sg_all = gates_of(n2_all)
    expert_gate = lax.dynamic_slice(probs_all, (0, me), (all_tokens, 1))

    capacity = (9 * tokens * TOP + 8 * experts_all - 1) // (8 * experts_all)
    info_away = info_all[away]
    order_all = info_away[:, 2]
    routed_here = jnp.any(info_away[:, 3 : 3 + TOP] == me, axis=1)
    earlier = (order_all[:, None, :] < order_all[:, :, None]) & routed_here[:, None, :]
    slots = jnp.sum(earlier.astype(jnp.int32), axis=2)
    slots = jnp.where(routed_here, slots, capacity)
    chosen = slots[:, None, :] == jnp.arange(capacity, dtype=jnp.int32)[None, :, None]
    onehot = chosen.astype(jnp.bfloat16)

    def rows_of(values):
        got = lax.dot_general(
            onehot,
            values.reshape(plane, tokens, width),
            (((2,), (1,)), ((0,), (0,))),
            preferred_element_type=jnp.float32,
        )
        return got.reshape(plane * capacity, width)

    slot_gates = jnp.sum(
        jnp.where(chosen, expert_gate.reshape(plane, 1, tokens), 0.0), axis=2
    ).reshape(plane * capacity, 1)
    expert_rows = low(rows_of(n2_all))
    gate_pre = mm(sh_gate_t, n2_all, ((1,), (1,)))
    up_pre = mm(sh_up_t, n2_all, ((1,), (1,)))
    gate_act = gate_pre * jax.nn.sigmoid(gate_pre)
    shared_hidden = low(gate_act * up_pre)
    expert_rows = after(expert_rows, (shared_hidden, sh_down))
    gate_e = mm(expert_rows, ex_gate)
    up_e = mm(expert_rows, ex_up)
    act_e = gate_e * jax.nn.sigmoid(gate_e)
    hidden_e = low(act_e * up_e)
    cot_near = jnp.concatenate([cot_own] + [after(v, gate_e) for v in cot_got])
    cot_all = jnp.concatenate([cot_near, twin(cot_near)])
    row_cots = low(rows_of(cot_all))
    row_grads = low(row_cots.astype(jnp.float32) * slot_gates)

    shared_grads = low(sg_all * cot_all.astype(jnp.float32))
    shared_hgrad = mm(sh_down, shared_grads, ((1,), (1,)))
    gate_grad_s = low(shared_hgrad * up_pre * silu_grad(gate_pre))
    up_grad_s = low(shared_hgrad * gate_act)
    rows_out = width // (halves * depth)

    def shared_scatter(total):
        first, second = total[:, :rows_out], total[:, rows_out:]
        keep = jnp.where(core == 0, first, second)
        got = twin(jnp.where(core == 0, second, first))
        both = jnp.where(core == 0, jnp.stack([keep, got]), jnp.stack([got, keep]))
        both = both.reshape(halves, depth, part, rows_out).transpose(1, 0, 2, 3)
        return both.reshape(units, rows_out).astype(jnp.float32)

    scatter = lambda v, dim: lax.psum_scatter(v, DP, scatter_dimension=dim, tiled=True)
    shared_sums = [
        scatter(
            unit_grads(left, right, depth, halves).reshape(depth * depth * part, -1), 0
        )
        for left, right in (
            (shared_hidden, shared_grads),
            (gate_grad_s, n2_all),
            (up_grad_s, n2_all),
        )
    ]
    result_e = low(mm(hidden_e, ex_down))
    hgrad_e = mm(row_grads, ex_down, ((1,), (1,)))
    gate_grad_e = low(hgrad_e * up_e * silu_grad(gate_e))
    up_grad_e = low(hgrad_e * act_e)

    grad_ex_down = low(mm(hidden_e, row_grads, ((0,), (0,))))
    grad_ex_gate = low(mm(expert_rows, gate_grad_e, ((0,), (0,))))
    grad_ex_up = low(mm(expert_rows, up_grad_e, ((0,), (0,))))
    grads_made = (grad_ex_down, grad_ex_gate, grad_ex_up)
    grads = [scatter(v, dim) for v, dim in zip(grads_made, (1, 0, 0))]
    slots = slots.reshape(all_tokens, 1)
    out_near, dots = output_parts(
        shared_hidden,
        sh_down,
        result_e.reshape(plane, capacity, width),
        after(slots, grads_made),
        sg_all,
        expert_gate,
        cot_all,
    )
    out_sums = [out_near[k] for k in range(4)]
    rows_grad = low(
        mm(gate_grad_e, ex_gate, ((1,), (1,))) + mm(up_grad_e, ex_up, ((1,), (1,)))
    )

    n2_grad_part = n2_grad_parts(
        gate_grad_s,
        up_grad_s,
        sh_gate_t,
        sh_up_t,
        rows_grad.reshape(plane, capacity, width),
        after(slots, out_sums),
    )
    out_got = hops(out_sums)
    n2_grad_part, out_got, _ = lax.optimization_barrier((n2_grad_part, out_got, shared_sums))
    output = low(residual + sum_up(out_got))
    n2_grad = plane_scatter(n2_grad_part, True, 3, jnp.float32)[0]

    dots = dots.reshape(plane, tokens, 128)[:, :, :2].transpose(0, 2, 1)
    back = jnp.arange(plane, dtype=jnp.int32) ^ me
    dots = dots[(back // 2) + 4 * (back % 2)]
    dots = lax.all_to_all(dots, PLANE, split_axis=0, concat_axis=0, tiled=True)
    probs_grad = dots[:, 0].T
    probs, sg = gates_of(n2)
    logit_grad = low(probs * (probs_grad - jnp.sum(probs * probs_grad, axis=1, keepdims=True)))
    sg_logit_grad = low(jnp.sum(dots[:, 1], axis=0)[:, None] * sg * (1.0 - sg))
    small_grads = mm(n2, jnp.concatenate([logit_grad, sg_logit_grad], axis=1), ((0,), (0,)))
    n2_grad = (
        n2_grad
        + mm(logit_grad, router_t)
        + sg_logit_grad.astype(jnp.float32) * gate_vec.astype(jnp.float32)[None]
    )
    residual_grad, grad_gain_two = norm_back(residual, inv_two, g_two, n2_grad)
    residual_grad = residual_grad + cot_rows
    low_residual = low(residual_grad)

    small_grads = jnp.concatenate([small_grads, grad_gain_two[:, None]], axis=1).T
    small_grads = jnp.pad(small_grads, ((0, 14 - experts_all), (0, 0)))
    small_grads = small_grads.reshape(16, plane, width // plane).transpose(1, 0, 2)
    small_grads = jnp.sum(
        lax.all_to_all(small_grads, PLANE, split_axis=0, concat_axis=0, tiled=True), axis=0
    )
    small_grads = small_grads.reshape(16, depth, shard // plane).transpose(1, 0, 2)
    small_grads = jnp.sum(
        lax.all_to_all(small_grads, DP, split_axis=0, concat_axis=0, tiled=True), axis=0
    )
    grad_out = low(mm(attended, low_residual, ((0,), (0,))))
    grad_out = grad_out.reshape(groups, halves, width // plane, width)
    block_of = lambda k, c: lax.dynamic_slice(
        grad_out, (place ^ k, c, 0, 0), (1, 1, width // plane, width)
    )[0, 0]
    attended_grad = to_columns(low(mm(low_residual, w_out_full, ((1,), (1,)))))
    out_grad_sums = twin_sums(
        [block_of(k, core) for k in range(4)],
        jnp.stack([block_of(k, 1 - core) for k in range(4)]),
    )
    attended_grad = after(attended_grad, (out_grad_sums, grads[0]))
    qkv_grad = attention_call(qkv, attended_grad, q_codes, k_codes, seq_len)
    grad_qkv = low(mm(n1_all, qkv_grad, ((0,), (0,))))
    n1_grad = low(mm(qkv_grad, w_qkv, ((1,), (1,))))
    out_grad_got = hops(out_grad_sums)
    grad_out = low(sum_up(after(out_grad_got, (n1_grad, grad_qkv))))
    n1_grad = after(n1_grad, (grad_qkv, grad_out, grads[1]))
    grad_out = lax.psum_scatter(grad_out, DP, scatter_dimension=0, tiled=True)
    n1_grad = plane_scatter(n1_grad.reshape(plane, tokens, width), False, 1, jnp.float32)[0]
    grad_sh_down, grad_sh_gate, grad_sh_up = [
        shared_scatter(after(v, n1_grad)) for v in shared_sums
    ]
    grad_sh_gate, grad_sh_up = grad_sh_gate.T, grad_sh_up.T
    fine = shard // plane
    grad_qkv = (
        grad_qkv.reshape(plane, depth, fine, 3 * head_cols)
        .transpose(1, 0, 2, 3)
        .reshape(width, 3 * head_cols)
    )
    grad_qkv = lax.psum_scatter(grad_qkv, DP, scatter_dimension=0, tiled=True)
    w_rows = (
        w_qkv.reshape(plane, depth, fine, 3 * head_cols)
        .transpose(1, 0, 2, 3)
        .reshape(depth, plane * fine, 3 * head_cols)
    )
    w_rows = lax.dynamic_index_in_dim(w_rows, lax.axis_index(DP), axis=0, keepdims=False)
    gain_dots = jnp.sum(grad_qkv.astype(jnp.float32) * w_rows.astype(jnp.float32), axis=1)
    gain_dots = lax.all_to_all(
        gain_dots.reshape(plane, 1, fine), PLANE, split_axis=0, concat_axis=0, tiled=True
    )
    my_gain = lax.dynamic_slice(
        g_one, ((me * depth + lax.axis_index(DP)) * fine,), (fine,)
    )
    grad_gain_one = jnp.sum(gain_dots[:, 0], axis=0) / my_gain
    grad_qkv = lax.all_to_all(
        grad_qkv.reshape(plane, fine, 3 * head_cols),
        PLANE,
        split_axis=0,
        concat_axis=0,
        tiled=True,
    )
    grad_qkv = (
        grad_qkv.reshape(plane, fine, 3, head_cols)
        .transpose(2, 1, 0, 3)
        .reshape(3, fine, width)
        .astype(jnp.float32)
    )
    grad_out = after(grad_out, n1_grad).astype(jnp.float32)
    grad_ex_down, grad_ex_gate, grad_ex_up = [
        after(v, n1_grad).astype(jnp.float32)[None] for v in grads
    ]
    input_part, _ = norm_back(x_rows, inv_one, g_one, n1_grad)
    input_grad = low(residual_grad + input_part)
    return (
        output[None],
        input_grad[None],
        grad_gain_one,
        grad_qkv[0],
        grad_qkv[1],
        grad_qkv[2],
        grad_out,
        small_grads[experts_all + 1],
        small_grads[:experts_all].T,
        small_grads[experts_all],
        grad_sh_gate,
        grad_sh_up,
        grad_sh_down,
        grad_ex_gate,
        grad_ex_up,
        grad_ex_down,
    )


def solution(mesh):
    in_specs = (
        P((EXP, DP), CTX, None),
        P((EXP, DP), CTX, None),
        P((EXP, DP), CTX),
        P((EXP, DP), CTX),
        P((EXP, DP), CTX, None),
        P((EXP, DP), CTX, None),
        P(DP),
        P(DP, None),
        P(DP, None),
        P(DP, None),
        P(DP, None),
        P(DP),
        P(DP, None),
        P(DP),
        P(DP, EXP),
        P(DP, EXP),
        P((EXP, DP), None),
        P((EXP, CTX), DP, None),
        P((EXP, CTX), DP, None),
        P((EXP, CTX), None, DP),
    )
    out_specs = (
        P((EXP, DP), CTX, None),
        P((EXP, DP), CTX, None),
        P((EXP, CTX, DP)),
        P((EXP, CTX, DP), None),
        P((EXP, CTX, DP), None),
        P((EXP, CTX, DP), None),
        P((EXP, CTX, DP), None),
        P((EXP, CTX, DP)),
        P((EXP, CTX, DP), None),
        P((EXP, CTX, DP)),
        P((CTX, DP), EXP),
        P((CTX, DP), EXP),
        P(EXP, (CTX, DP)),
        P((EXP, CTX), DP, None),
        P((EXP, CTX), DP, None),
        P((EXP, CTX), None, DP),
    )
    plane = mesh.shape[EXP] * mesh.shape[CTX]

    def run(*args):
        square = mesh.shape[EXP] == 4 and mesh.shape[CTX] == 2
        one_each = square and args[12].shape[1] == plane
        local = local_plane if one_each else local_general
        return jax.shard_map(
            local, mesh=mesh, in_specs=in_specs, out_specs=out_specs, check_vma=False
        )(*args)

    return run
```

```python
from functools import partial

import jax
import jax.numpy as jnp
from jax import lax
from jax.experimental import pallas as pl
from jax.experimental.pallas import tpu as pltpu
from jax.sharding import PartitionSpec as P

EXP, CTX, DP = "experts", "context", "dp"
PLANE = (EXP, CTX)
HEADS = 16
HEAD_DIM = 128
TOP = 4


EPS = 1e-06
NEG = -1e30


def silu_grad(pre_act):
    logistic = jax.nn.sigmoid(pre_act)
    return logistic * (1.0 + pre_act * (1.0 - logistic))


def block_slots(route_row, priority, expert_count):
    matches = (route_row[:, None] == jnp.arange(expert_count, dtype=jnp.int32)[None, :]).astype(
        jnp.int32
    )
    ordered = jnp.zeros_like(matches).at[priority].set(matches)
    before = jnp.cumsum(ordered, axis=0) - ordered
    return jnp.sum(before[priority] * matches, axis=1)


def norm_back(values_in, inv_rms, gain_vec, gradient):
    weighted = gradient * gain_vec
    inner_sum = jnp.mean(weighted * values_in, axis=1, keepdims=True)
    d_value = inv_rms * weighted - values_in * inv_rms**3 * inner_sum
    d_gain = jnp.sum(gradient * values_in * inv_rms, axis=0)
    return (d_value, d_gain)


def attend_head(packed, allowed, scale_factor):
    query_h, key_h, value_h = packed
    raw_scores = jnp.einsum("th,lh->tl", query_h, key_h, preferred_element_type=jnp.float32)
    logits = jnp.where(allowed, raw_scores * scale_factor, NEG)
    row_max = jnp.max(logits, axis=1, keepdims=True)
    exp_scores = jnp.exp(logits - row_max)
    row_total = jnp.sum(exp_scores, axis=1, keepdims=True)
    attn_probs = (exp_scores / row_total).astype(jnp.bfloat16)
    head_out = jnp.dot(attn_probs, value_h, preferred_element_type=jnp.float32).astype(jnp.bfloat16)
    return (head_out, row_max + jnp.log(row_total))


def attend_back(packed, allowed, scale_factor):
    query_h, key_h, value_h, out_grad, log_total = packed
    raw_scores = jnp.einsum("th,lh->tl", query_h, key_h, preferred_element_type=jnp.float32)
    logits = jnp.where(allowed, raw_scores * scale_factor, NEG)
    attn_probs = jnp.exp(logits - log_total)
    prob_grad = jnp.einsum("th,lh->tl", out_grad, value_h, preferred_element_type=jnp.float32)
    inner_sum = jnp.sum(attn_probs * prob_grad, axis=1, keepdims=True)
    score_grad = (attn_probs * (prob_grad - inner_sum) * scale_factor).astype(jnp.bfloat16)
    query_grad = jnp.dot(score_grad, key_h, preferred_element_type=jnp.float32)
    key_grad = jnp.einsum("tl,th->lh", score_grad, query_h, preferred_element_type=jnp.float32)
    value_grad = jnp.einsum(
        "tl,th->lh", attn_probs.astype(jnp.bfloat16), out_grad, preferred_element_type=jnp.float32
    )
    return (query_grad, key_grad, value_grad)


def local_general(
    hidden,
    cotangent,
    segments,
    padding,
    routes,
    order,
    norm1_gain,
    w_query,
    w_key,
    w_value,
    w_out,
    norm2_gain,
    router,
    shared_gate_vec,
    shared_w_gate,
    shared_w_up,
    shared_w_down,
    expert_w_gate,
    expert_w_up,
    expert_w_down,
):
    fetched = (
        lax.all_gather(norm1_gain, DP, axis=0, tiled=True),
        lax.all_gather(w_query, DP, axis=0, tiled=True),
        lax.all_gather(w_key, DP, axis=0, tiled=True),
        lax.all_gather(w_value, DP, axis=0, tiled=True),
        lax.all_gather(w_out, DP, axis=0, tiled=True),
        lax.all_gather(norm2_gain, DP, axis=0, tiled=True),
        lax.all_gather(router, DP, axis=0, tiled=True),
        lax.all_gather(shared_gate_vec, DP, axis=0, tiled=True),
        lax.all_gather(shared_w_gate, DP, axis=0, tiled=True),
        lax.all_gather(shared_w_up, DP, axis=0, tiled=True),
        lax.all_gather(shared_w_down, DP, axis=0, tiled=True),
        lax.all_gather(expert_w_gate, DP, axis=1, tiled=True),
        lax.all_gather(expert_w_up, DP, axis=1, tiled=True),
        lax.all_gather(expert_w_down, DP, axis=2, tiled=True),
    )
    (
        gain_one,
        query_w,
        key_w,
        value_w,
        out_w,
        gain_two,
        router_full,
        gate_vec,
        sh_gate,
        sh_up,
        sh_down,
        ex_gate,
        ex_up,
        ex_down,
    ) = fetched
    sh_gate, sh_up, sh_down = (
        lax.all_gather(sh_gate, EXP, axis=1, tiled=True),
        lax.all_gather(sh_up, EXP, axis=1, tiled=True),
        lax.all_gather(sh_down, EXP, axis=0, tiled=True),
    )
    tokens_here = hidden.shape[1]
    model_width = hidden.shape[2]
    x_rows = hidden[0].astype(jnp.float32)
    cot_rows = cotangent[0].astype(jnp.float32)
    inv_one = lax.rsqrt(jnp.mean(x_rows * x_rows, axis=1, keepdims=True) + EPS)
    g_one = gain_one.astype(jnp.float32)
    normed_one = (x_rows * inv_one * g_one).astype(jnp.bfloat16)
    queries = jnp.dot(normed_one, query_w, preferred_element_type=jnp.float32).astype(jnp.bfloat16)
    keys_own = jnp.dot(normed_one, key_w, preferred_element_type=jnp.float32).astype(jnp.bfloat16)
    values_own = jnp.dot(normed_one, value_w, preferred_element_type=jnp.float32).astype(
        jnp.bfloat16
    )
    own_codes = jnp.where(padding[0] > 0, segments[0] + 1, 0)
    code_parts = jnp.stack([own_codes // 64, own_codes % 64]).astype(jnp.bfloat16)
    keys_all, values_all, parts_all = (
        lax.all_gather(keys_own, CTX, axis=0, tiled=True),
        lax.all_gather(values_own, CTX, axis=0, tiled=True),
        lax.all_gather(code_parts, CTX, axis=1, tiled=True),
    )
    key_codes = parts_all[0].astype(jnp.int32) * 64 + parts_all[1].astype(jnp.int32)
    seq_total = keys_all.shape[0]
    query_pos = lax.axis_index(CTX) * tokens_here + jnp.arange(tokens_here, dtype=jnp.int32)
    key_pos = jnp.arange(seq_total, dtype=jnp.int32)
    same_doc = key_codes[None, :] == (segments[0] + 1)[:, None]
    allowed = (key_pos[None, :] <= query_pos[:, None]) & (
        same_doc | (key_pos[None, :] == query_pos[:, None])
    )
    scale_factor = HEAD_DIM ** (-0.5)

    def to_heads(rows_in):
        return rows_in.reshape(rows_in.shape[0], HEADS, HEAD_DIM).transpose(1, 0, 2)

    def from_heads(heads_in):
        return heads_in.transpose(1, 0, 2).reshape(heads_in.shape[1], model_width)

    head_q = to_heads(queries)
    head_k = to_heads(keys_all)
    head_v = to_heads(values_all)
    head_out, log_total = lax.map(
        partial(attend_head, allowed=allowed, scale_factor=scale_factor), (head_q, head_k, head_v)
    )
    attended = from_heads(head_out)
    residual = x_rows + jnp.dot(attended, out_w, preferred_element_type=jnp.float32)
    inv_two = lax.rsqrt(jnp.mean(residual * residual, axis=1, keepdims=True) + EPS)
    g_two = gain_two.astype(jnp.float32)
    normed_two = (residual * inv_two * g_two).astype(jnp.bfloat16)
    router_logits = jnp.dot(normed_two, router_full, preferred_element_type=jnp.float32)
    router_exp = jnp.exp(router_logits - jnp.max(router_logits, axis=1, keepdims=True))
    router_probs = router_exp / jnp.sum(router_exp, axis=1, keepdims=True)
    route_gates = jnp.take_along_axis(router_probs, routes[0], axis=1)
    shared_gate = jax.nn.sigmoid(jnp.dot(normed_two, gate_vec, preferred_element_type=jnp.float32))
    shared_scaled = (shared_gate[:, None] * cot_rows).astype(jnp.bfloat16)
    rows_group, grads_group = (normed_two, shared_scaled)
    gate_pre = jnp.dot(rows_group, sh_gate, preferred_element_type=jnp.float32)
    up_pre = jnp.dot(rows_group, sh_up, preferred_element_type=jnp.float32)
    gate_act = gate_pre * jax.nn.sigmoid(gate_pre)
    shared_hidden = (gate_act * up_pre).astype(jnp.bfloat16)
    shared_part = jnp.dot(shared_hidden, sh_down, preferred_element_type=jnp.float32)
    experts_all = router_full.shape[1]
    capacity = (9 * tokens_here * TOP + 8 * experts_all - 1) // (8 * experts_all)
    priority = (order[0, 0][:, None] * TOP + jnp.arange(TOP, dtype=jnp.int32)[None, :]).reshape(-1)
    flat_routes = routes[0].reshape(-1)
    slot_index = block_slots(flat_routes, priority, experts_all)
    kept_rows = slot_index < capacity
    target = flat_routes * capacity + jnp.minimum(slot_index, capacity - 1)
    row_gates = route_gates.reshape(-1)
    cot_repeated = jnp.repeat(cot_rows, TOP, axis=0)
    source_rows = jnp.repeat(normed_two, TOP, axis=0)
    source_grads = (cot_repeated * row_gates[:, None]).astype(jnp.bfloat16)
    empty_slots = jnp.zeros((experts_all * capacity, model_width), jnp.bfloat16)
    send_rows = empty_slots.at[target].add(
        jnp.where(kept_rows[:, None], source_rows, jnp.zeros_like(source_rows))
    )
    send_grads = empty_slots.at[target].add(
        jnp.where(kept_rows[:, None], source_grads, jnp.zeros_like(source_grads))
    )
    recv_rows, recv_grads = (
        lax.all_to_all(
            send_rows.reshape(experts_all, capacity, model_width),
            (EXP, CTX),
            split_axis=0,
            concat_axis=0,
            tiled=True,
        ),
        lax.all_to_all(
            send_grads.reshape(experts_all, capacity, model_width),
            (EXP, CTX),
            split_axis=0,
            concat_axis=0,
            tiled=True,
        ),
    )
    local_count = ex_gate.shape[0]
    sources = experts_all // local_count

    def to_local(buffer_in):
        return (
            buffer_in.reshape(sources, local_count, capacity, model_width)
            .transpose(1, 0, 2, 3)
            .reshape(local_count, sources * capacity, model_width)
        )

    def to_owner(buffer_in):
        return (
            buffer_in.reshape(local_count, sources, capacity, model_width)
            .transpose(1, 0, 2, 3)
            .reshape(experts_all, capacity, model_width)
        )

    expert_rows = to_local(recv_rows)
    expert_grads_in = to_local(recv_grads)
    gate_e = jnp.einsum("erd,edf->erf", expert_rows, ex_gate, preferred_element_type=jnp.float32)
    up_e = jnp.einsum("erd,edf->erf", expert_rows, ex_up, preferred_element_type=jnp.float32)
    act_e = gate_e * jax.nn.sigmoid(gate_e)
    hidden_e = (act_e * up_e).astype(jnp.bfloat16)
    result_e = jnp.einsum(
        "erf,efd->erd", hidden_e, ex_down, preferred_element_type=jnp.float32
    ).astype(jnp.bfloat16)
    returned = lax.all_to_all(
        to_owner(result_e), (EXP, CTX), split_axis=0, concat_axis=0, tiled=True
    )
    picked = returned.reshape(experts_all * capacity, model_width)[target]
    picked = jnp.where(kept_rows[:, None], picked, jnp.zeros_like(picked)).astype(jnp.float32)
    routed = jnp.sum((picked * row_gates[:, None]).reshape(tokens_here, TOP, model_width), axis=1)
    output = (residual + shared_gate[:, None] * shared_part + routed).astype(jnp.bfloat16)
    gate_grads = jnp.sum(picked * cot_repeated, axis=1).reshape(tokens_here, TOP)
    hidden_grad_e = jnp.einsum(
        "erd,efd->erf", expert_grads_in, ex_down, preferred_element_type=jnp.float32
    )
    gate_grad_e = (hidden_grad_e * up_e * silu_grad(gate_e)).astype(jnp.bfloat16)
    up_grad_e = (hidden_grad_e * act_e).astype(jnp.bfloat16)
    grad_ex_down = jnp.einsum(
        "erf,erd->efd", hidden_e, expert_grads_in, preferred_element_type=jnp.float32
    )
    grad_ex_gate = jnp.einsum(
        "erd,erf->edf", expert_rows, gate_grad_e, preferred_element_type=jnp.float32
    )
    grad_ex_up = jnp.einsum(
        "erd,erf->edf", expert_rows, up_grad_e, preferred_element_type=jnp.float32
    )
    expert_sums = (
        lax.psum_scatter(grad_ex_gate, DP, scatter_dimension=1, tiled=True),
        lax.psum_scatter(grad_ex_up, DP, scatter_dimension=1, tiled=True),
        lax.psum_scatter(grad_ex_down, DP, scatter_dimension=2, tiled=True),
    )
    rows_grad_e = jnp.einsum(
        "erf,edf->erd", gate_grad_e, ex_gate, preferred_element_type=jnp.float32
    )
    rows_grad_e = (
        rows_grad_e
        + jnp.einsum("erf,edf->erd", up_grad_e, ex_up, preferred_element_type=jnp.float32)
    ).astype(jnp.bfloat16)
    returned_grads = lax.all_to_all(
        to_owner(rows_grad_e), (EXP, CTX), split_axis=0, concat_axis=0, tiled=True
    )
    routed_grad = returned_grads.reshape(experts_all * capacity, model_width)[target]
    routed_grad = jnp.where(kept_rows[:, None], routed_grad, jnp.zeros_like(routed_grad)).astype(
        jnp.float32
    )
    norm_grad = jnp.sum(routed_grad.reshape(tokens_here, TOP, model_width), axis=1)
    choose = (
        routes[0][:, :, None] == jnp.arange(experts_all, dtype=jnp.int32)[None, None, :]
    ).astype(jnp.float32)
    probs_grad = jnp.einsum("tk,tke->te", gate_grads, choose)
    logit_grad = (
        router_probs * (probs_grad - jnp.sum(router_probs * probs_grad, axis=1, keepdims=True))
    ).astype(jnp.bfloat16)
    grad_router = jnp.dot(normed_two.T, logit_grad, preferred_element_type=jnp.float32)
    gate_logit_grad = (
        jnp.sum(cot_rows * shared_part, axis=1) * shared_gate * (1.0 - shared_gate)
    ).astype(jnp.bfloat16)
    grad_gate_vec = jnp.dot(gate_logit_grad, normed_two, preferred_element_type=jnp.float32)
    norm_grad = norm_grad + jnp.dot(logit_grad, router_full.T, preferred_element_type=jnp.float32)
    norm_grad = (
        norm_grad
        + gate_logit_grad.astype(jnp.float32)[:, None] * gate_vec.astype(jnp.float32)[None, :]
    )
    shared_hgrad = jnp.dot(grads_group, sh_down.T, preferred_element_type=jnp.float32)
    gate_grad_s = (shared_hgrad * up_pre * silu_grad(gate_pre)).astype(jnp.bfloat16)
    up_grad_s = (shared_hgrad * gate_act).astype(jnp.bfloat16)
    shared_rows_grad = jnp.dot(gate_grad_s, sh_gate.T, preferred_element_type=jnp.float32)
    shared_rows_grad = shared_rows_grad + jnp.dot(
        up_grad_s, sh_up.T, preferred_element_type=jnp.float32
    )
    groups = lax.axis_size(EXP)
    parts_cd = lax.axis_size((CTX, DP))
    rows_count = rows_group.shape[0]
    arr_gate = jnp.einsum(
        "td,tes->eds",
        rows_group,
        gate_grad_s.reshape(rows_count, groups, -1),
        preferred_element_type=jnp.float32,
    ).reshape(groups * model_width, -1)
    arr_up = jnp.einsum(
        "td,tes->eds",
        rows_group,
        up_grad_s.reshape(rows_count, groups, -1),
        preferred_element_type=jnp.float32,
    ).reshape(groups * model_width, -1)
    arr_down = jnp.einsum(
        "tes,tcd->ecsd",
        shared_hidden.reshape(rows_count, groups, -1),
        grads_group.reshape(rows_count, parts_cd, -1),
        preferred_element_type=jnp.float32,
    ).reshape(-1, model_width // parts_cd)
    sums_gate, sums_up, sums_down = (
        lax.psum_scatter(arr_gate, (EXP, CTX, DP), scatter_dimension=0, tiled=True),
        lax.psum_scatter(arr_up, (EXP, CTX, DP), scatter_dimension=0, tiled=True),
        lax.psum_scatter(arr_down, (EXP, CTX, DP), scatter_dimension=0, tiled=True),
    )
    norm_grad = norm_grad + shared_rows_grad
    residual_grad, grad_gain_two = norm_back(residual, inv_two, g_two, norm_grad)
    residual_grad = residual_grad + cot_rows
    low_residual = residual_grad.astype(jnp.bfloat16)
    grad_out_w = jnp.dot(attended.T, low_residual, preferred_element_type=jnp.float32)
    attended_grad = jnp.dot(low_residual, out_w.T, preferred_element_type=jnp.float32).astype(
        jnp.bfloat16
    )
    head_q_grad, head_k_grad, head_v_grad = lax.map(
        partial(attend_back, allowed=allowed, scale_factor=scale_factor),
        (head_q, head_k, head_v, to_heads(attended_grad), log_total),
    )
    key_sum, value_sum = (
        lax.psum_scatter(from_heads(head_k_grad), CTX, scatter_dimension=0, tiled=True),
        lax.psum_scatter(from_heads(head_v_grad), CTX, scatter_dimension=0, tiled=True),
    )
    query_low = from_heads(head_q_grad).astype(jnp.bfloat16)
    key_low = key_sum.astype(jnp.bfloat16)
    value_low = value_sum.astype(jnp.bfloat16)
    grad_query = jnp.dot(normed_one.T, query_low, preferred_element_type=jnp.float32)
    grad_key = jnp.dot(normed_one.T, key_low, preferred_element_type=jnp.float32)
    grad_value = jnp.dot(normed_one.T, value_low, preferred_element_type=jnp.float32)
    normed_grad = jnp.dot(query_low, query_w.T, preferred_element_type=jnp.float32)
    normed_grad = normed_grad + jnp.dot(key_low, key_w.T, preferred_element_type=jnp.float32)
    normed_grad = normed_grad + jnp.dot(value_low, value_w.T, preferred_element_type=jnp.float32)
    input_part, grad_gain_one = norm_back(x_rows, inv_one, g_one, normed_grad)
    input_grad = (residual_grad + input_part).astype(jnp.bfloat16)
    dense = (
        lax.psum_scatter(
            grad_gain_one, (EXP, CTX, DP), scatter_dimension=0, tiled=True
        ),
        lax.psum_scatter(grad_query, (EXP, CTX, DP), scatter_dimension=0, tiled=True),
        lax.psum_scatter(grad_key, (EXP, CTX, DP), scatter_dimension=0, tiled=True),
        lax.psum_scatter(grad_value, (EXP, CTX, DP), scatter_dimension=0, tiled=True),
        lax.psum_scatter(grad_out_w, (EXP, CTX, DP), scatter_dimension=0, tiled=True),
        lax.psum_scatter(
            grad_gain_two, (EXP, CTX, DP), scatter_dimension=0, tiled=True
        ),
        lax.psum_scatter(
            grad_router, (EXP, CTX, DP), scatter_dimension=0, tiled=True
        ),
        lax.psum_scatter(
            grad_gate_vec, (EXP, CTX, DP), scatter_dimension=0, tiled=True
        ),
    )
    return (
        output[None],
        input_grad[None],
        dense[0],
        dense[1],
        dense[2],
        dense[3],
        dense[4],
        dense[5],
        dense[6],
        dense[7],
        sums_gate,
        sums_up,
        sums_down,
        expert_sums[0],
        expert_sums[1],
        expert_sums[2],
    )

def attention_probs(q_blk, k_part, q_code, k_code, first_row, scale_factor):
    scores = lax.dot_general(
        q_blk, k_part, (((1,), (1,)), ((), ())), preferred_element_type=jnp.float32
    )
    row = first_row + lax.broadcasted_iota(jnp.int32, scores.shape, 0)
    col = lax.broadcasted_iota(jnp.int32, scores.shape, 1)
    allowed = ((col < row) & (k_code == q_code)) | (col == row)
    logits = jnp.where(allowed, scores * scale_factor, NEG)
    exp_scores = jnp.exp(logits - jnp.max(logits, axis=1, keepdims=True))
    return exp_scores * (1.0 / jnp.sum(exp_scores, axis=1, keepdims=True))


def attend_kernel(heads, step, qkv_ref, q_code_ref, k_code_ref, out_ref):
    seq_len = qkv_ref.shape[0]
    width = heads * HEAD_DIM
    for head in range(heads):
        at = head * HEAD_DIM
        for first in range(0, seq_len, step):
            upto = first + step
            probs = attention_probs(
                qkv_ref[first:upto, at : at + HEAD_DIM],
                qkv_ref[0:upto, width + at : width + at + HEAD_DIM],
                q_code_ref[first:upto, :],
                k_code_ref[0, :, 0:upto],
                first,
                HEAD_DIM**-0.5,
            )
            out_ref[first:upto, at : at + HEAD_DIM] = jnp.dot(
                probs.astype(jnp.bfloat16),
                qkv_ref[0:upto, 2 * width + at : 2 * width + at + HEAD_DIM],
                preferred_element_type=jnp.float32,
            ).astype(jnp.bfloat16)


def attend_back_kernel(
    heads, step, qkv_ref, grad_ref, q_code_ref, k_code_ref, out_ref, key_acc, value_acc
):
    seq_len = qkv_ref.shape[0]
    width = heads * HEAD_DIM
    for head in range(heads):
        at = head * HEAD_DIM
        key_at, value_at = width + at, 2 * width + at
        key_acc[...] = jnp.zeros_like(key_acc)
        value_acc[...] = jnp.zeros_like(value_acc)
        for first in range(0, seq_len, step):
            upto = first + step
            q_blk = qkv_ref[first:upto, at : at + HEAD_DIM]
            k_part = qkv_ref[0:upto, key_at : key_at + HEAD_DIM]
            v_part = qkv_ref[0:upto, value_at : value_at + HEAD_DIM]
            g_blk = grad_ref[first:upto, at : at + HEAD_DIM]
            probs = attention_probs(
                q_blk,
                k_part,
                q_code_ref[first:upto, :],
                k_code_ref[0, :, 0:upto],
                first,
                HEAD_DIM**-0.5,
            )
            prob_grad = lax.dot_general(
                g_blk, v_part, (((1,), (1,)), ((), ())), preferred_element_type=jnp.float32
            )
            inner = jnp.sum(probs * prob_grad, axis=1, keepdims=True)
            score_grad = (probs * (prob_grad - inner) * HEAD_DIM**-0.5).astype(jnp.bfloat16)
            out_ref[first:upto, at : at + HEAD_DIM] = jnp.dot(
                score_grad, k_part, preferred_element_type=jnp.float32
            ).astype(jnp.bfloat16)
            key_acc[0:upto, :] += lax.dot_general(
                score_grad, q_blk, (((0,), (0,)), ((), ())), preferred_element_type=jnp.float32
            )
            value_acc[0:upto, :] += lax.dot_general(
                probs.astype(jnp.bfloat16),
                g_blk,
                (((0,), (0,)), ((), ())),
                preferred_element_type=jnp.float32,
            )
        out_ref[:, key_at : key_at + HEAD_DIM] = key_acc[...].astype(jnp.bfloat16)
        out_ref[:, value_at : value_at + HEAD_DIM] = value_acc[...].astype(jnp.bfloat16)


def attention_call(qkv, grads, q_codes, k_codes, seq_len):
    rows, triple = qkv.shape
    width = triple // 3
    heads = width // HEAD_DIM
    step = min(256, seq_len)
    specs = [pl.BlockSpec((seq_len, triple), lambda s: (s, 0))]
    operands = [qkv]
    if grads is not None:
        specs.append(pl.BlockSpec((seq_len, width), lambda s: (s, 0)))
        operands.append(grads)
    specs += [
        pl.BlockSpec((seq_len, 1), lambda s: (s, 0)),
        pl.BlockSpec((1, 1, seq_len), lambda s: (s, 0, 0)),
    ]
    operands += [q_codes, k_codes]
    out_width = width if grads is None else triple
    body = attend_kernel if grads is None else attend_back_kernel
    passes = 2 if grads is None else 5
    area = rows * seq_len * heads
    return pl.pallas_call(
        partial(body, heads, step),
        grid=(rows // seq_len,),
        in_specs=specs,
        out_specs=pl.BlockSpec((seq_len, out_width), lambda s: (s, 0)),
        out_shape=jax.ShapeDtypeStruct((rows, out_width), jnp.bfloat16),
        scratch_shapes=[]
        if grads is None
        else [pltpu.VMEM((seq_len, HEAD_DIM), jnp.float32)] * 2,
        compiler_params=pltpu.CompilerParams(vmem_limit_bytes=48 * 2**20),
        cost_estimate=pl.CostEstimate(
            flops=2 * passes * area * HEAD_DIM,
            bytes_accessed=2 * rows * (triple + out_width),
            transcendentals=area,
        ),
    )(*operands)


MESH_ID = pl.DeviceIdType.MESH


def other_in_pair(index, bit):
    return index + bit - 2 * bit * (lax.div(index, bit) % 2)


def plane_places():
    at = lax.axis_index(EXP)
    core = lax.axis_index(CTX)
    across, along = other_in_pair(at, 1), other_in_pair(at, 2)
    return at, core, across, along, other_in_pair(along, 1)


def greet(across, along, core):
    barrier = pltpu.get_barrier_semaphore()
    for target in ({EXP: across}, {EXP: along}, {CTX: 1 - core}):
        pl.semaphore_signal(barrier, inc=1, device_id=target, device_id_type=MESH_ID)
    pl.semaphore_wait(barrier, 3)


def plane_gather_kernel(with_info, relative, *refs):
    if with_info:
        own_ref, info_ref, all_ref, info_all_ref, send_sem, recv_sem, local_sem = refs
    else:
        own_ref, all_ref, send_sem, recv_sem, local_sem = refs
    at, core, across, along, far = plane_places()
    rows = own_ref.shape[0]
    half = rows // 2
    top, bottom, whole = pl.ds(0, half), pl.ds(half, half), pl.ds(0, rows)
    greet(across, along, core)
    started = []
    twin_id = {CTX: 1 - core}

    def slot_of(place, shift, for_twin):
        if relative:
            return shift + 4 * for_twin
        return place * 2 + core

    def send(number, src, dst, target):
        copy = pltpu.make_async_remote_copy(
            src_ref=src,
            dst_ref=dst,
            send_sem=send_sem.at[number],
            recv_sem=recv_sem.at[number],
            device_id=target,
            device_id_type=MESH_ID,
        )
        copy.start()
        started.append(copy)
        return copy

    def piece(place, shift, part, for_twin=0):
        return all_ref.at[slot_of(place, shift, for_twin), part]

    x_top = send(0, own_ref.at[top], piece(at, 1, top), {EXP: across})
    y_bottom = send(1, own_ref.at[bottom], piece(at, 2, bottom), {EXP: along})
    x_bottom = send(2, own_ref.at[bottom], piece(at, 1, bottom), {EXP: across})
    y_top = send(3, own_ref.at[top], piece(at, 2, top), {EXP: along})
    twins = [send(4, own_ref, piece(at, 0, whole, 1), twin_id)]
    heres = [pltpu.make_async_copy(own_ref, piece(at, 0, whole), local_sem.at[0])]
    heres[0].start()
    if with_info:
        info_at = lambda place: info_all_ref.at[place * 2 + core]
        heres.append(pltpu.make_async_copy(info_ref, info_at(at), local_sem.at[1]))
        heres[1].start()
        info_x = send(13, info_ref, info_at(at), {EXP: across})
        info_y = send(14, info_ref, info_at(at), {EXP: along})
        twins.append(send(15, info_ref, info_at(at), twin_id))
        info_x.wait_recv()
        info_far = send(16, info_at(across), info_at(across), {EXP: along})
        twins.append(send(17, info_at(across), info_at(across), twin_id))
        info_y.wait_recv()
        twins.append(send(18, info_at(along), info_at(along), twin_id))
        info_far.wait_recv()
        twins.append(send(19, info_at(far), info_at(far), twin_id))

    def hand_on(number, place, shift, part):
        src = piece(place, shift, part)
        twins.append(send(number, src, piece(place, shift, part, 1), twin_id))

    x_top.wait_recv()
    far_top = send(5, piece(across, 1, top), piece(across, 3, top), {EXP: along})
    hand_on(6, across, 1, top)
    y_bottom.wait_recv()
    far_bottom = send(7, piece(along, 2, bottom), piece(along, 3, bottom), {EXP: across})
    hand_on(8, along, 2, bottom)
    x_bottom.wait_recv()
    hand_on(9, across, 1, bottom)
    y_top.wait_recv()
    hand_on(10, along, 2, top)
    far_top.wait_recv()
    hand_on(11, far, 3, top)
    far_bottom.wait_recv()
    hand_on(12, far, 3, bottom)
    for copy in twins:
        copy.wait_recv()
    for copy in started:
        copy.wait_send()
    for copy in heres:
        copy.wait()


def plane_gather(own, info, relative, number):
    plane = lax.axis_size(PLANE)
    operands = [own] if info is None else [own, info]
    outs = [jax.ShapeDtypeStruct((plane, *v.shape), v.dtype) for v in operands]
    anywhere = pl.BlockSpec(memory_space=pl.ANY)
    return pl.pallas_call(
        partial(plane_gather_kernel, info is not None, relative),
        out_shape=outs,
        in_specs=[anywhere] * len(operands),
        out_specs=[anywhere] * len(operands),
        scratch_shapes=[
            pltpu.SemaphoreType.DMA((20,)),
            pltpu.SemaphoreType.DMA((20,)),
            pltpu.SemaphoreType.DMA((2,)),
        ],
        compiler_params=pltpu.CompilerParams(collective_id=number, has_side_effects=True),
        cost_estimate=pl.CostEstimate(
            flops=0, bytes_accessed=own.size, transcendentals=0
        ),
    )(*operands)


def plane_scatter_kernel(relative, with_extra, *refs):
    if with_extra:
        part_ref, extra_ref, out_ref, *refs = refs
        extra_out, refs = refs[:4], refs[4:]
        extra_own, extra_got, extra_sems, refs = refs[0], refs[1], refs[2:5], refs[5:]
    else:
        part_ref, out_ref, *refs = refs
    own, twin_got, x_got, y_got, x_last, y_last, send_sem, recv_sem, local_sem = refs
    at, core, across, along, far = plane_places()
    rows = part_ref.shape[1]
    half = rows // 2
    step = 64
    greet(across, along, core)
    started = []

    def send(number, src, dst, target):
        copy = pltpu.make_async_remote_copy(
            src_ref=src,
            dst_ref=dst,
            send_sem=send_sem.at[number],
            recv_sem=recv_sem.at[number],
            device_id=target,
            device_id_type=MESH_ID,
        )
        copy.start()
        started.append(copy)
        return copy

    twins, heres = [], []
    for j, (label, shift) in enumerate(((far, 3), (across, 1), (along, 2), (at, 0))):
        theirs = shift + 4 if relative else label * 2 + 1 - core
        ours = shift if relative else label * 2 + core
        twins.append(send(j, part_ref.at[theirs], twin_got.at[j], {CTX: 1 - core}))
        here = pltpu.make_async_copy(part_ref.at[ours], own.at[j], local_sem.at[j])
        here.start()
        heres.append(here)

    def add_rows(target, t_first, count, source, s_first):
        @pl.loop(0, count // step)
        def _(i):
            into = pl.ds(pl.multiple_of(t_first + i * step, step), step)
            take = pl.ds(pl.multiple_of(s_first + i * step, step), step)
            total = target[into].astype(jnp.float32) + source[take].astype(jnp.float32)
            target[into] = total.astype(target.dtype)

    top, bottom = pl.ds(0, half), pl.ds(half, half)
    x_sent, y_sent = [], []
    for j in range(4):
        twins[j].wait_recv()
        heres[j].wait()
        add_rows(own.at[j], 0, rows, twin_got.at[j], 0)
        if j < 2:
            x_sent.append(send(4 + j, own.at[j, top], x_got.at[j], {EXP: across}))
        if j == 0 or j == 2:
            y_sent.append(send(6 + j // 2, own.at[j, bottom], y_got.at[j // 2], {EXP: along}))
    if with_extra:
        extra_here, extra_twin, extra_done = [], [], []
        for k in range(4):
            copy = pltpu.make_async_remote_copy(
                src_ref=extra_ref.at[k + 4],
                dst_ref=extra_got.at[k],
                send_sem=extra_sems[0].at[k],
                recv_sem=extra_sems[1].at[k],
                device_id={CTX: 1 - core},
                device_id_type=MESH_ID,
            )
            copy.start()
            started.append(copy)
            extra_twin.append(copy)
            here = pltpu.make_async_copy(extra_ref.at[k], extra_own.at[k], extra_sems[2].at[k])
            here.start()
            extra_here.append(here)
        for k in range(4):
            extra_twin[k].wait_recv()
            extra_here[k].wait()
            add_rows(extra_own.at[k], 0, rows, extra_got.at[k], 0)
            here = pltpu.make_async_copy(extra_own.at[k], extra_out[k], extra_sems[2].at[k])
            here.start()
            extra_done.append(here)
    x_sent[0].wait_recv()
    add_rows(own.at[2], 0, half, x_got.at[0], 0)
    last_y = send(8, own.at[2, top], y_last, {EXP: along})
    y_sent[0].wait_recv()
    add_rows(own.at[1], half, half, y_got.at[0], 0)
    last_x = send(9, own.at[1, bottom], x_last, {EXP: across})

    def finish(first, near, later):
        @pl.loop(0, half // step)
        def _(i):
            take = pl.ds(pl.multiple_of(i * step, step), step)
            into = pl.ds(pl.multiple_of(first + i * step, step), step)
            out_ref[into] = (
                own[3, into].astype(jnp.float32)
                + near[1, take].astype(jnp.float32)
                + later[take].astype(jnp.float32)
            ).astype(out_ref.dtype)

    x_sent[1].wait_recv()
    last_y.wait_recv()
    finish(0, x_got, y_last)
    y_sent[1].wait_recv()
    last_x.wait_recv()
    finish(half, y_got, x_last)
    if with_extra:
        for copy in extra_done:
            copy.wait()
    for copy in started:
        copy.wait_send()


def plane_scatter(parts, relative, number, out_type, extra=None):
    plane, rows, cols = parts.shape
    operands, extra_scratch = [parts], []
    out_shape = [jax.ShapeDtypeStruct((rows, cols), out_type)]
    out_specs = [pl.BlockSpec(memory_space=pltpu.VMEM)]
    anywhere = pl.BlockSpec(memory_space=pl.ANY)
    if extra is not None:
        operands.append(extra)
        out_shape += [jax.ShapeDtypeStruct((rows, cols), extra.dtype)] * 4
        out_specs += [anywhere] * 4
        extra_scratch = [pltpu.VMEM((4, rows, cols), extra.dtype)] * 2
        extra_scratch += [pltpu.SemaphoreType.DMA((4,))] * 3
    half = rows // 2
    vmem = lambda *shape: pltpu.VMEM(shape, parts.dtype)
    return pl.pallas_call(
        partial(plane_scatter_kernel, relative, extra is not None),
        out_shape=out_shape,
        in_specs=[anywhere] * len(operands),
        out_specs=out_specs,
        scratch_shapes=extra_scratch
        + [
            vmem(4, rows, cols),
            vmem(4, rows, cols),
            vmem(2, half, cols),
            vmem(2, half, cols),
            vmem(half, cols),
            vmem(half, cols),
            pltpu.SemaphoreType.DMA((10,)),
            pltpu.SemaphoreType.DMA((10,)),
            pltpu.SemaphoreType.DMA((4,)),
        ],
        compiler_params=pltpu.CompilerParams(
            collective_id=number,
            has_side_effects=True,
            vmem_limit_bytes=(36 if extra is None else 54) * 2**20,
        ),
        cost_estimate=pl.CostEstimate(
            flops=0, bytes_accessed=rows * cols, transcendentals=0
        ),
    )(*operands)


def norm_qkv_kernel(hidden_ref, gain_ref, w_ref, norm_ref, qkv_ref):
    values = hidden_ref[...].astype(jnp.float32)
    inv = lax.rsqrt(jnp.mean(values * values, axis=1, keepdims=True) + EPS)
    norm_ref[...] = low(values * inv * gain_ref[...])
    qkv_ref[...] = low(mm(norm_ref[...], w_ref[...]))


def norm_qkv(hidden, gain, w, block):
    rows, width = hidden.shape
    cols = w.shape[1]
    return pl.pallas_call(
        norm_qkv_kernel,
        grid=(rows // block,),
        in_specs=[
            pl.BlockSpec((block, width), lambda i: (i, 0)),
            pl.BlockSpec((1, width), lambda i: (0, 0)),
            pl.BlockSpec((width, cols), lambda i: (0, 0)),
        ],
        out_specs=[
            pl.BlockSpec((block, width), lambda i: (i, 0)),
            pl.BlockSpec((block, cols), lambda i: (i, 0)),
        ],
        out_shape=[
            jax.ShapeDtypeStruct((rows, width), jnp.bfloat16),
            jax.ShapeDtypeStruct((rows, cols), jnp.bfloat16),
        ],
        compiler_params=pltpu.CompilerParams(vmem_limit_bytes=48 * 2**20),
        cost_estimate=pl.CostEstimate(
            flops=2 * rows * width * cols,
            bytes_accessed=4 * rows * width,
            transcendentals=0,
        ),
    )(hidden, gain, w)


def chosen_rows(slots, capacity):
    lanes = lax.broadcasted_iota(jnp.int32, (slots.shape[0], capacity), 1)
    return (slots == lanes).astype(jnp.bfloat16)


def output_kernel(
    half,
    hidden_ref,
    down_ref,
    rows_ref,
    slot_ref,
    sg_ref,
    gate_ref,
    cot_ref,
    near_ref,
    dots_ref,
    given,
    got,
    send_sem,
    recv_sem,
):
    step_at = pl.program_id(0)
    is_far = step_at < half
    slot = lax.rem(step_at, half)
    twin_id = {CTX: 1 - lax.axis_index(CTX)}

    @pl.when(step_at == 0)
    def _():
        barrier = pltpu.get_barrier_semaphore()
        pl.semaphore_signal(barrier, inc=1, device_id=twin_id, device_id_type=MESH_ID)
        pl.semaphore_wait(barrier, 1)

    def block_copy(k):
        return pltpu.make_async_remote_copy(
            src_ref=given.at[k],
            dst_ref=got.at[k],
            send_sem=send_sem.at[k],
            recv_sem=recv_sem.at[k],
            device_id=twin_id,
            device_id_type=MESH_ID,
        )

    def make(store):
        chosen = chosen_rows(slot_ref[...], rows_ref.shape[1])
        hidden = hidden_ref[...].T
        tokens, width = cot_ref.shape
        step, lanes = 512, 128
        gate_dot = jnp.zeros((tokens, lanes), jnp.float32)
        shared_dot = jnp.zeros((tokens, lanes), jnp.float32)
        for first in range(0, width, step):
            cols = pl.ds(first, step)
            shared = mm(hidden, down_ref[:, cols])
            picked = mm(chosen, rows_ref[0, :, cols])
            cot = cot_ref[:, cols].astype(jnp.float32)
            gate_part, shared_part = picked * cot, shared * cot
            for at in range(0, step, lanes):
                gate_dot += gate_part[:, at : at + lanes]
                shared_dot += shared_part[:, at : at + lanes]
            store(cols, sg_ref[...] * shared + gate_ref[...] * picked)
        lane = lax.broadcasted_iota(jnp.int32, dots_ref.shape, 1)
        gate_dot = jnp.sum(gate_dot, axis=1, keepdims=True)
        shared_dot = jnp.sum(shared_dot, axis=1, keepdims=True)
        dots_ref[...] = jnp.where(lane == 0, gate_dot, jnp.where(lane == 1, shared_dot, 0.0))

    @pl.when(is_far)
    def _():
        def store(cols, total):
            given[slot, :, cols] = low(total)

        make(store)
        block_copy(slot).start()

    @pl.when(jnp.logical_not(is_far))
    def _():
        block_copy(slot).wait_recv()

        def store(cols, total):
            near_ref[0, :, cols] = low(total + got[slot, :, cols].astype(jnp.float32))

        make(store)

    @pl.when(step_at == 2 * half - 1)
    def _():
        for k in range(half):
            block_copy(k).wait_send()


def output_parts(hidden, down, rows, slots, sg, gates, cot):
    blocks, capacity, width = rows.shape
    units, count = hidden.shape
    tokens, half = count // blocks, blocks // 2
    at = lambda i: lax.rem(i + half, blocks)
    column = pl.BlockSpec((tokens, 1), lambda i: (at(i), 0))
    return pl.pallas_call(
        partial(output_kernel, half),
        grid=(blocks,),
        in_specs=[
            pl.BlockSpec((units, tokens), lambda i: (0, at(i))),
            pl.BlockSpec((units, width), lambda i: (0, 0)),
            pl.BlockSpec((1, capacity, width), lambda i: (at(i), 0, 0)),
            column,
            column,
            column,
            pl.BlockSpec((tokens, width), lambda i: (at(i), 0)),
        ],
        out_specs=[
            pl.BlockSpec((1, tokens, width), lambda i: (jnp.maximum(i - half, 0), 0, 0)),
            pl.BlockSpec((tokens, 128), lambda i: (at(i), 0)),
        ],
        out_shape=[
            jax.ShapeDtypeStruct((half, tokens, width), jnp.bfloat16),
            jax.ShapeDtypeStruct((count, 128), jnp.float32),
        ],
        scratch_shapes=[
            pltpu.VMEM((half, tokens, width), jnp.bfloat16),
            pltpu.VMEM((half, tokens, width), jnp.bfloat16),
            pltpu.SemaphoreType.DMA((half,)),
            pltpu.SemaphoreType.DMA((half,)),
        ],
        compiler_params=pltpu.CompilerParams(
            collective_id=4, has_side_effects=True, vmem_limit_bytes=56 * 2**20
        ),
        cost_estimate=pl.CostEstimate(
            flops=2 * count * width * (units + capacity),
            bytes_accessed=6 * count * width,
            transcendentals=0,
        ),
    )(hidden, down, rows, slots, sg, gates, cot)


def n2_grad_kernel(dgate_ref, dup_ref, gate_ref, up_ref, rows_ref, slot_ref, out_ref):
    chosen = chosen_rows(slot_ref[...], rows_ref.shape[1])
    step = 512
    for first in range(0, gate_ref.shape[1], step):
        cols = pl.ds(first, step)
        total = mm(dgate_ref[...], gate_ref[:, cols], ((0,), (0,)))
        total += mm(dup_ref[...], up_ref[:, cols], ((0,), (0,)))
        out_ref[0, :, cols] = low(total + mm(chosen, rows_ref[0, :, cols]))


def n2_grad_parts(dgate, dup, gate_w, up_w, rows, slots):
    blocks, capacity, width = rows.shape
    units, count = dgate.shape
    tokens = count // blocks
    by_units = pl.BlockSpec((units, tokens), lambda i: (0, i))
    whole = pl.BlockSpec((units, width), lambda i: (0, 0))
    return pl.pallas_call(
        n2_grad_kernel,
        grid=(blocks,),
        in_specs=[
            by_units,
            by_units,
            whole,
            whole,
            pl.BlockSpec((1, capacity, width), lambda i: (i, 0, 0)),
            pl.BlockSpec((tokens, 1), lambda i: (i, 0)),
        ],
        out_specs=pl.BlockSpec((1, tokens, width), lambda i: (i, 0, 0)),
        out_shape=jax.ShapeDtypeStruct((blocks, tokens, width), jnp.bfloat16),
        compiler_params=pltpu.CompilerParams(vmem_limit_bytes=48 * 2**20),
        cost_estimate=pl.CostEstimate(
            flops=2 * count * width * (2 * units + capacity),
            bytes_accessed=4 * count * width,
            transcendentals=0,
        ),
    )(dgate, dup, gate_w, up_w, rows, slots)


def unit_grad_kernel(left_ref, right_ref, out_ref):
    out_ref[0] = low(mm(left_ref[...], right_ref[...]))


def unit_grads(left, right, depth, halves):
    units, count = left.shape
    width = right.shape[1]
    cols = width // (depth * halves)
    return pl.pallas_call(
        unit_grad_kernel,
        grid=(depth * halves,),
        in_specs=[
            pl.BlockSpec((units, count), lambda i: (0, 0)),
            pl.BlockSpec((count, cols), lambda i: (0, i)),
        ],
        out_specs=pl.BlockSpec((1, units, cols), lambda i: (lax.rem(i, depth), 0, i // depth)),
        out_shape=jax.ShapeDtypeStruct((depth, units, halves * cols), jnp.bfloat16),
        compiler_params=pltpu.CompilerParams(vmem_limit_bytes=48 * 2**20),
        cost_estimate=pl.CostEstimate(
            flops=2 * units * count * width,
            bytes_accessed=2 * (units * count + count * width + units * width),
            transcendentals=0,
        ),
    )(left, right)


def after(values, others):
    return lax.optimization_barrier((values, others))[0]


def swap(values, bits):
    return lax.ppermute(values, EXP, [(i, i ^ bits) for i in range(4)])


def twin(values):
    return lax.ppermute(values, CTX, [(0, 1), (1, 0)])


def twin_sums(ours, theirs):
    got = twin(theirs)
    return [low(ours[k].astype(jnp.float32) + got[k].astype(jnp.float32)) for k in range(4)]


def hops(sums):
    return [sums[0]] + [swap(sums[k], k) for k in (1, 2, 3)]


def sum_up(parts):
    return sum(v.astype(jnp.float32) for v in parts)


def mm(left, right, dims=((1,), (0,))):
    return lax.dot_general(left, right, (dims, ((), ())), preferred_element_type=jnp.float32)


def low(values):
    return values.astype(jnp.bfloat16)


def local_plane(
    hidden,
    cotangent,
    segments,
    padding,
    routes,
    order,
    norm1_gain,
    w_query,
    w_key,
    w_value,
    w_out,
    norm2_gain,
    router,
    shared_gate_vec,
    shared_w_gate,
    shared_w_up,
    shared_w_down,
    expert_w_gate,
    expert_w_up,
    expert_w_down,
):
    plane = lax.axis_size(PLANE)
    groups = lax.axis_size(EXP)
    halves = lax.axis_size(CTX)
    depth = lax.axis_size(DP)
    me = lax.axis_index(PLANE)
    core = lax.axis_index(CTX)
    tokens, width = hidden.shape[1], hidden.shape[2]
    all_tokens = plane * tokens
    seq_len = halves * tokens
    experts_all = router.shape[1]
    head_cols = width // plane
    shard = width // depth

    token_info = jnp.concatenate(
        [segments + 1, jnp.where(padding > 0, segments + 1, 0), order[0], routes[0].T]
    )
    info_rows = token_info.shape[0]
    token_info = jnp.concatenate([token_info, jnp.zeros((8 - info_rows, tokens), jnp.int32)])

    hidden_all, info_all = plane_gather(hidden[0], token_info, False, 0)
    hidden_all = hidden_all.reshape(all_tokens, width)
    place = lax.axis_index(EXP)
    away = [(place ^ k) * 2 + (core ^ j) for j in (0, 1) for k in range(4)]
    away = jnp.stack(away)
    w_qkv_part = jnp.concatenate(
        [
            lax.dynamic_slice(w, (0, me * head_cols), (shard, head_cols))
            for w in (w_query, w_key, w_value)
        ]
        + [router, norm1_gain[:, None], norm2_gain[:, None], shared_gate_vec[:, None]]
        + [jnp.zeros((shard, 128 - experts_all - 3), jnp.bfloat16)],
        axis=1,
    )
    w_qkv = lax.all_gather(w_qkv_part, DP, axis=0, tiled=True)
    small = w_qkv[:, 3 * head_cols :].T
    w_qkv = w_qkv[:, : 3 * head_cols]
    router_t = small[:experts_all]
    g_one = small[experts_all].astype(jnp.float32)
    g_two = small[experts_all + 1].astype(jnp.float32)
    gate_vec = small[experts_all + 2]
    out_rows = shard // plane
    w_out_part = lax.dynamic_slice(w_out, (me * out_rows, 0), (out_rows, width))
    w_out_part = lax.all_gather(w_out_part, DP, axis=0, tiled=False)
    w_out_part = after(w_out_part, info_all)
    w_out_got = [swap(w_out_part, k) for k in (1, 2, 3)]

    def normed(values, gain):
        values = values.astype(jnp.float32)
        inv = lax.rsqrt(jnp.mean(values * values, axis=1, keepdims=True) + EPS)
        return values, inv, low(values * inv * gain)

    n1_all, qkv = norm_qkv(hidden_all, g_one[None], w_qkv, tokens)
    q_codes = info_all[:, 0].reshape(all_tokens, 1)
    k_codes = info_all[:, 1].reshape(all_tokens // seq_len, 1, seq_len)
    attended_cols = attention_call(qkv, None, q_codes, k_codes, seq_len)
    pieces = [w_out_part] + [after(v, attended_cols) for v in w_out_got]
    w_out_near = jnp.zeros((depth, groups, 1, out_rows, width), jnp.bfloat16)
    for k in range(4):
        w_out_near = lax.dynamic_update_slice(
            w_out_near, pieces[k][:, None, None], (0, place ^ k, 0, 0, 0)
        )
    w_out_far = twin(w_out_near)
    w_out_full = jnp.where(
        core == 0,
        jnp.concatenate([w_out_near, w_out_far], axis=2),
        jnp.concatenate([w_out_far, w_out_near], axis=2),
    ).reshape(width, width)

    x_rows, inv_one, _ = normed(hidden[0], g_one)
    cot_rows = cotangent[0].astype(jnp.float32)

    def to_tokens(cols):
        got = lax.all_to_all(
            cols.reshape(plane, tokens, head_cols), PLANE, split_axis=0, concat_axis=0, tiled=True
        )
        return got.transpose(1, 0, 2).reshape(tokens, width)

    def to_columns(rows_in):
        send = rows_in.reshape(tokens, plane, head_cols).transpose(1, 0, 2)
        got = lax.all_to_all(send, PLANE, split_axis=0, concat_axis=0, tiled=True)
        return got.reshape(all_tokens, head_cols)

    attended = to_tokens(attended_cols)
    residual = x_rows + mm(attended, w_out_full)
    residual, inv_two, n2 = normed(residual, g_two)

    units = shared_w_gate.shape[1]
    part = units // (depth * halves)
    pick = lambda w: lax.dynamic_index_in_dim(
        w.reshape(w.shape[0], depth, halves, part), core, axis=2, keepdims=False
    ).reshape(w.shape[0], depth * part)
    sh_gate = lax.all_gather(pick(shared_w_gate), DP, axis=0, tiled=True)
    sh_up = lax.all_gather(pick(shared_w_up), DP, axis=0, tiled=True)
    sh_gate_t, sh_up_t = sh_gate.T, sh_up.T
    sh_down = lax.all_gather(
        lax.dynamic_slice(shared_w_down, (core * part, 0), (part, width)), DP, axis=0, tiled=True
    )
    n2 = after(n2, (sh_gate, sh_up))
    n2_all = plane_gather(n2, None, True, 2)[0].reshape(all_tokens, width)
    cot_own = after(cotangent[0], n2_all)
    cot_got = [swap(cot_own, k) for k in (1, 2, 3)]
    ex_gate = lax.all_gather(after(expert_w_gate[0], info_all), DP, axis=0, tiled=True)
    ex_up = jnp.broadcast_to(after(expert_w_up, info_all), (depth, *expert_w_up.shape[1:]))
    ex_up = lax.all_to_all(ex_up, DP, split_axis=0, concat_axis=0, tiled=True)
    ex_up = ex_up.reshape(width, -1)
    ex_down = lax.all_gather(after(expert_w_down[0], info_all), DP, axis=1, tiled=True)

    small_w = jnp.concatenate([router_t, gate_vec[None]])

    def gates_of(rows_in):
        both = mm(rows_in, small_w, ((1,), (1,)))
        z = both[:, :experts_all]
        e = jnp.exp(z - jnp.max(z, axis=1, keepdims=True))
        return e / jnp.sum(e, axis=1, keepdims=True), jax.nn.sigmoid(both[:, experts_all:])

    probs_all, sg_all = gates_of(n2_all)
    expert_gate = lax.dynamic_slice(probs_all, (0, me), (all_tokens, 1))

    capacity = (9 * tokens * TOP + 8 * experts_all - 1) // (8 * experts_all)
    info_away = info_all[away]
    order_all = info_away[:, 2]
    routed_here = jnp.any(info_away[:, 3 : 3 + TOP] == me, axis=1)
    earlier = (order_all[:, None, :] < order_all[:, :, None]) & routed_here[:, None, :]
    slots = jnp.sum(earlier.astype(jnp.int32), axis=2)
    slots = jnp.where(routed_here, slots, capacity)
    chosen = slots[:, None, :] == jnp.arange(capacity, dtype=jnp.int32)[None, :, None]
    onehot = chosen.astype(jnp.bfloat16)

    def rows_of(values):
        got = lax.dot_general(
            onehot,
            values.reshape(plane, tokens, width),
            (((2,), (1,)), ((0,), (0,))),
            preferred_element_type=jnp.float32,
        )
        return got.reshape(plane * capacity, width)

    slot_gates = jnp.sum(
        jnp.where(chosen, expert_gate.reshape(plane, 1, tokens), 0.0), axis=2
    ).reshape(plane * capacity, 1)
    expert_rows = low(rows_of(n2_all))
    gate_pre = mm(sh_gate_t, n2_all, ((1,), (1,)))
    up_pre = mm(sh_up_t, n2_all, ((1,), (1,)))
    gate_act = gate_pre * jax.nn.sigmoid(gate_pre)
    shared_hidden = low(gate_act * up_pre)
    expert_rows = after(expert_rows, (shared_hidden, sh_down))
    gate_e = mm(expert_rows, ex_gate)
    up_e = mm(expert_rows, ex_up)
    act_e = gate_e * jax.nn.sigmoid(gate_e)
    hidden_e = low(act_e * up_e)
    cot_near = jnp.concatenate([cot_own] + [after(v, gate_e) for v in cot_got])
    cot_all = jnp.concatenate([cot_near, twin(cot_near)])
    row_cots = low(rows_of(cot_all))
    row_grads = low(row_cots.astype(jnp.float32) * slot_gates)

    shared_grads = low(sg_all * cot_all.astype(jnp.float32))
    shared_hgrad = mm(sh_down, shared_grads, ((1,), (1,)))
    gate_grad_s = low(shared_hgrad * up_pre * silu_grad(gate_pre))
    up_grad_s = low(shared_hgrad * gate_act)
    rows_out = width // (halves * depth)

    def shared_scatter(total):
        first, second = total[:, :rows_out], total[:, rows_out:]
        keep = jnp.where(core == 0, first, second)
        got = twin(jnp.where(core == 0, second, first))
        both = jnp.where(core == 0, jnp.stack([keep, got]), jnp.stack([got, keep]))
        both = both.reshape(halves, depth, part, rows_out).transpose(1, 0, 2, 3)
        return both.reshape(units, rows_out).astype(jnp.float32)

    scatter = lambda v, dim: lax.psum_scatter(v, DP, scatter_dimension=dim, tiled=True)
    shared_sums = [
        scatter(
            unit_grads(left, right, depth, halves).reshape(depth * depth * part, -1), 0
        )
        for left, right in (
            (shared_hidden, shared_grads),
            (gate_grad_s, n2_all),
            (up_grad_s, n2_all),
        )
    ]
    result_e = low(mm(hidden_e, ex_down))
    hgrad_e = mm(row_grads, ex_down, ((1,), (1,)))
    gate_grad_e = low(hgrad_e * up_e * silu_grad(gate_e))
    up_grad_e = low(hgrad_e * act_e)

    grad_ex_down = low(mm(hidden_e, row_grads, ((0,), (0,))))
    grad_ex_gate = low(mm(expert_rows, gate_grad_e, ((0,), (0,))))
    grad_ex_up = low(mm(expert_rows, up_grad_e, ((0,), (0,))))
    grads_made = (grad_ex_down, grad_ex_gate, grad_ex_up)
    grads = [scatter(v, dim) for v, dim in zip(grads_made, (1, 0, 0))]
    slots = slots.reshape(all_tokens, 1)
    out_near, dots = output_parts(
        shared_hidden,
        sh_down,
        result_e.reshape(plane, capacity, width),
        after(slots, grads_made),
        sg_all,
        expert_gate,
        cot_all,
    )
    out_sums = [out_near[k] for k in range(4)]
    rows_grad = low(
        mm(gate_grad_e, ex_gate, ((1,), (1,))) + mm(up_grad_e, ex_up, ((1,), (1,)))
    )

    n2_grad_part = n2_grad_parts(
        gate_grad_s,
        up_grad_s,
        sh_gate_t,
        sh_up_t,
        rows_grad.reshape(plane, capacity, width),
        after(slots, out_sums),
    )
    out_got = hops(out_sums)
    n2_grad_part, out_got, _ = lax.optimization_barrier((n2_grad_part, out_got, shared_sums))
    output = low(residual + sum_up(out_got))
    n2_grad = plane_scatter(n2_grad_part, True, 3, jnp.float32)[0]

    dots = dots.reshape(plane, tokens, 128)[:, :, :2].transpose(0, 2, 1)
    back = jnp.arange(plane, dtype=jnp.int32) ^ me
    dots = dots[(back // 2) + 4 * (back % 2)]
    dots = lax.all_to_all(dots, PLANE, split_axis=0, concat_axis=0, tiled=True)
    probs_grad = dots[:, 0].T
    probs, sg = gates_of(n2)
    logit_grad = low(probs * (probs_grad - jnp.sum(probs * probs_grad, axis=1, keepdims=True)))
    sg_logit_grad = low(jnp.sum(dots[:, 1], axis=0)[:, None] * sg * (1.0 - sg))
    small_grads = mm(n2, jnp.concatenate([logit_grad, sg_logit_grad], axis=1), ((0,), (0,)))
    n2_grad = (
        n2_grad
        + mm(logit_grad, router_t)
        + sg_logit_grad.astype(jnp.float32) * gate_vec.astype(jnp.float32)[None]
    )
    residual_grad, grad_gain_two = norm_back(residual, inv_two, g_two, n2_grad)
    residual_grad = residual_grad + cot_rows
    low_residual = low(residual_grad)

    small_grads = jnp.concatenate([small_grads, grad_gain_two[:, None]], axis=1).T
    small_grads = jnp.pad(small_grads, ((0, 14 - experts_all), (0, 0)))
    small_grads = small_grads.reshape(16, plane, width // plane).transpose(1, 0, 2)
    small_grads = jnp.sum(
        lax.all_to_all(small_grads, PLANE, split_axis=0, concat_axis=0, tiled=True), axis=0
    )
    small_grads = small_grads.reshape(16, depth, shard // plane).transpose(1, 0, 2)
    small_grads = jnp.sum(
        lax.all_to_all(small_grads, DP, split_axis=0, concat_axis=0, tiled=True), axis=0
    )
    grad_out = low(mm(attended, low_residual, ((0,), (0,))))
    grad_out = grad_out.reshape(groups, halves, width // plane, width)
    block_of = lambda k, c: lax.dynamic_slice(
        grad_out, (place ^ k, c, 0, 0), (1, 1, width // plane, width)
    )[0, 0]
    attended_grad = to_columns(low(mm(low_residual, w_out_full, ((1,), (1,)))))
    out_grad_sums = twin_sums(
        [block_of(k, core) for k in range(4)],
        jnp.stack([block_of(k, 1 - core) for k in range(4)]),
    )
    grad_sh_down, grad_sh_gate, grad_sh_up = [
        shared_scatter(after(v, low_residual)) for v in shared_sums
    ]
    grad_sh_gate, grad_sh_up = grad_sh_gate.T, grad_sh_up.T
    attended_grad = after(
        attended_grad,
        (out_grad_sums, grads[0], small_grads, grad_sh_down, grad_sh_gate, grad_sh_up),
    )
    qkv_grad = attention_call(qkv, attended_grad, q_codes, k_codes, seq_len)
    qkv_grad, grad_out = lax.optimization_barrier((qkv_grad, hops(out_grad_sums)))
    grad_out = low(sum_up(grad_out))
    grad_qkv = low(mm(n1_all, qkv_grad, ((0,), (0,))))
    fine = shard // plane
    grad_qkv = (
        grad_qkv.reshape(plane, depth, fine, 3 * head_cols)
        .transpose(1, 0, 2, 3)
        .reshape(width, 3 * head_cols)
    )
    n1_grad = low(mm(after(qkv_grad, grad_qkv), w_qkv, ((1,), (1,))))
    grad_ex_down, grad_ex_gate = [v.astype(jnp.float32)[None] for v in grads[:2]]
    n1_grad = after(n1_grad, (grad_qkv, grad_out, grad_ex_down, grad_ex_gate))
    grad_out = lax.psum_scatter(grad_out, DP, scatter_dimension=0, tiled=True)
    n1_grad = plane_scatter(n1_grad.reshape(plane, tokens, width), False, 1, jnp.float32)[0]
    grad_qkv = lax.psum_scatter(grad_qkv, DP, scatter_dimension=0, tiled=True)
    w_rows = (
        w_qkv.reshape(plane, depth, fine, 3 * head_cols)
        .transpose(1, 0, 2, 3)
        .reshape(depth, plane * fine, 3 * head_cols)
    )
    w_rows = lax.dynamic_index_in_dim(w_rows, lax.axis_index(DP), axis=0, keepdims=False)
    gain_dots = jnp.sum(grad_qkv.astype(jnp.float32) * w_rows.astype(jnp.float32), axis=1)
    gain_dots = lax.all_to_all(
        gain_dots.reshape(plane, 1, fine), PLANE, split_axis=0, concat_axis=0, tiled=True
    )
    my_gain = lax.dynamic_slice(
        g_one, ((me * depth + lax.axis_index(DP)) * fine,), (fine,)
    )
    grad_gain_one = jnp.sum(gain_dots[:, 0], axis=0) / my_gain
    grad_qkv = lax.all_to_all(
        grad_qkv.reshape(plane, fine, 3 * head_cols),
        PLANE,
        split_axis=0,
        concat_axis=0,
        tiled=True,
    )
    grad_qkv = (
        grad_qkv.reshape(plane, fine, 3, head_cols)
        .transpose(2, 1, 0, 3)
        .reshape(3, fine, width)
        .astype(jnp.float32)
    )
    grad_out = after(grad_out, n1_grad).astype(jnp.float32)
    grad_ex_up = after(grads[2], n1_grad).astype(jnp.float32)[None]
    input_part, _ = norm_back(x_rows, inv_one, g_one, n1_grad)
    input_grad = low(residual_grad + input_part)
    return (
        output[None],
        input_grad[None],
        grad_gain_one,
        grad_qkv[0],
        grad_qkv[1],
        grad_qkv[2],
        grad_out,
        small_grads[experts_all + 1],
        small_grads[:experts_all].T,
        small_grads[experts_all],
        grad_sh_gate,
        grad_sh_up,
        grad_sh_down,
        grad_ex_gate,
        grad_ex_up,
        grad_ex_down,
    )


def solution(mesh):
    in_specs = (
        P((EXP, DP), CTX, None),
        P((EXP, DP), CTX, None),
        P((EXP, DP), CTX),
        P((EXP, DP), CTX),
        P((EXP, DP), CTX, None),
        P((EXP, DP), CTX, None),
        P(DP),
        P(DP, None),
        P(DP, None),
        P(DP, None),
        P(DP, None),
        P(DP),
        P(DP, None),
        P(DP),
        P(DP, EXP),
        P(DP, EXP),
        P((EXP, DP), None),
        P((EXP, CTX), DP, None),
        P((EXP, CTX), DP, None),
        P((EXP, CTX), None, DP),
    )
    out_specs = (
        P((EXP, DP), CTX, None),
        P((EXP, DP), CTX, None),
        P((EXP, CTX, DP)),
        P((EXP, CTX, DP), None),
        P((EXP, CTX, DP), None),
        P((EXP, CTX, DP), None),
        P((EXP, CTX, DP), None),
        P((EXP, CTX, DP)),
        P((EXP, CTX, DP), None),
        P((EXP, CTX, DP)),
        P((CTX, DP), EXP),
        P((CTX, DP), EXP),
        P(EXP, (CTX, DP)),
        P((EXP, CTX), DP, None),
        P((EXP, CTX), DP, None),
        P((EXP, CTX), None, DP),
    )
    plane = mesh.shape[EXP] * mesh.shape[CTX]

    def run(*args):
        square = mesh.shape[EXP] == 4 and mesh.shape[CTX] == 2
        one_each = square and args[12].shape[1] == plane
        local = local_plane if one_each else local_general
        return jax.shard_map(
            local, mesh=mesh, in_specs=in_specs, out_specs=out_specs, check_vma=False
        )(*args)

    return run
```

```python
from functools import partial

import jax
import jax.numpy as jnp
from jax import lax
from jax.experimental import pallas as pl
from jax.experimental.pallas import tpu as pltpu
from jax.sharding import PartitionSpec as P

EXP, CTX, DP = "experts", "context", "dp"
PLANE = (EXP, CTX)
HEADS = 16
HEAD_DIM = 128
TOP = 4


EPS = 1e-06
NEG = -1e30


def silu_grad(pre_act):
    logistic = jax.nn.sigmoid(pre_act)
    return logistic * (1.0 + pre_act * (1.0 - logistic))


def block_slots(route_row, priority, expert_count):
    matches = (route_row[:, None] == jnp.arange(expert_count, dtype=jnp.int32)[None, :]).astype(
        jnp.int32
    )
    ordered = jnp.zeros_like(matches).at[priority].set(matches)
    before = jnp.cumsum(ordered, axis=0) - ordered
    return jnp.sum(before[priority] * matches, axis=1)


def norm_back(values_in, inv_rms, gain_vec, gradient):
    weighted = gradient * gain_vec
    inner_sum = jnp.mean(weighted * values_in, axis=1, keepdims=True)
    d_value = inv_rms * weighted - values_in * inv_rms**3 * inner_sum
    d_gain = jnp.sum(gradient * values_in * inv_rms, axis=0)
    return (d_value, d_gain)


def attend_head(packed, allowed, scale_factor):
    query_h, key_h, value_h = packed
    raw_scores = jnp.einsum("th,lh->tl", query_h, key_h, preferred_element_type=jnp.float32)
    logits = jnp.where(allowed, raw_scores * scale_factor, NEG)
    row_max = jnp.max(logits, axis=1, keepdims=True)
    exp_scores = jnp.exp(logits - row_max)
    row_total = jnp.sum(exp_scores, axis=1, keepdims=True)
    attn_probs = (exp_scores / row_total).astype(jnp.bfloat16)
    head_out = jnp.dot(attn_probs, value_h, preferred_element_type=jnp.float32).astype(jnp.bfloat16)
    return (head_out, row_max + jnp.log(row_total))


def attend_back(packed, allowed, scale_factor):
    query_h, key_h, value_h, out_grad, log_total = packed
    raw_scores = jnp.einsum("th,lh->tl", query_h, key_h, preferred_element_type=jnp.float32)
    logits = jnp.where(allowed, raw_scores * scale_factor, NEG)
    attn_probs = jnp.exp(logits - log_total)
    prob_grad = jnp.einsum("th,lh->tl", out_grad, value_h, preferred_element_type=jnp.float32)
    inner_sum = jnp.sum(attn_probs * prob_grad, axis=1, keepdims=True)
    score_grad = (attn_probs * (prob_grad - inner_sum) * scale_factor).astype(jnp.bfloat16)
    query_grad = jnp.dot(score_grad, key_h, preferred_element_type=jnp.float32)
    key_grad = jnp.einsum("tl,th->lh", score_grad, query_h, preferred_element_type=jnp.float32)
    value_grad = jnp.einsum(
        "tl,th->lh", attn_probs.astype(jnp.bfloat16), out_grad, preferred_element_type=jnp.float32
    )
    return (query_grad, key_grad, value_grad)


def local_general(
    hidden,
    cotangent,
    segments,
    padding,
    routes,
    order,
    norm1_gain,
    w_query,
    w_key,
    w_value,
    w_out,
    norm2_gain,
    router,
    shared_gate_vec,
    shared_w_gate,
    shared_w_up,
    shared_w_down,
    expert_w_gate,
    expert_w_up,
    expert_w_down,
):
    fetched = (
        lax.all_gather(norm1_gain, DP, axis=0, tiled=True),
        lax.all_gather(w_query, DP, axis=0, tiled=True),
        lax.all_gather(w_key, DP, axis=0, tiled=True),
        lax.all_gather(w_value, DP, axis=0, tiled=True),
        lax.all_gather(w_out, DP, axis=0, tiled=True),
        lax.all_gather(norm2_gain, DP, axis=0, tiled=True),
        lax.all_gather(router, DP, axis=0, tiled=True),
        lax.all_gather(shared_gate_vec, DP, axis=0, tiled=True),
        lax.all_gather(shared_w_gate, DP, axis=0, tiled=True),
        lax.all_gather(shared_w_up, DP, axis=0, tiled=True),
        lax.all_gather(shared_w_down, DP, axis=0, tiled=True),
        lax.all_gather(expert_w_gate, DP, axis=1, tiled=True),
        lax.all_gather(expert_w_up, DP, axis=1, tiled=True),
        lax.all_gather(expert_w_down, DP, axis=2, tiled=True),
    )
    (
        gain_one,
        query_w,
        key_w,
        value_w,
        out_w,
        gain_two,
        router_full,
        gate_vec,
        sh_gate,
        sh_up,
        sh_down,
        ex_gate,
        ex_up,
        ex_down,
    ) = fetched
    sh_gate, sh_up, sh_down = (
        lax.all_gather(sh_gate, EXP, axis=1, tiled=True),
        lax.all_gather(sh_up, EXP, axis=1, tiled=True),
        lax.all_gather(sh_down, EXP, axis=0, tiled=True),
    )
    tokens_here = hidden.shape[1]
    model_width = hidden.shape[2]
    x_rows = hidden[0].astype(jnp.float32)
    cot_rows = cotangent[0].astype(jnp.float32)
    inv_one = lax.rsqrt(jnp.mean(x_rows * x_rows, axis=1, keepdims=True) + EPS)
    g_one = gain_one.astype(jnp.float32)
    normed_one = (x_rows * inv_one * g_one).astype(jnp.bfloat16)
    queries = jnp.dot(normed_one, query_w, preferred_element_type=jnp.float32).astype(jnp.bfloat16)
    keys_own = jnp.dot(normed_one, key_w, preferred_element_type=jnp.float32).astype(jnp.bfloat16)
    values_own = jnp.dot(normed_one, value_w, preferred_element_type=jnp.float32).astype(
        jnp.bfloat16
    )
    own_codes = jnp.where(padding[0] > 0, segments[0] + 1, 0)
    code_parts = jnp.stack([own_codes // 64, own_codes % 64]).astype(jnp.bfloat16)
    keys_all, values_all, parts_all = (
        lax.all_gather(keys_own, CTX, axis=0, tiled=True),
        lax.all_gather(values_own, CTX, axis=0, tiled=True),
        lax.all_gather(code_parts, CTX, axis=1, tiled=True),
    )
    key_codes = parts_all[0].astype(jnp.int32) * 64 + parts_all[1].astype(jnp.int32)
    seq_total = keys_all.shape[0]
    query_pos = lax.axis_index(CTX) * tokens_here + jnp.arange(tokens_here, dtype=jnp.int32)
    key_pos = jnp.arange(seq_total, dtype=jnp.int32)
    same_doc = key_codes[None, :] == (segments[0] + 1)[:, None]
    allowed = (key_pos[None, :] <= query_pos[:, None]) & (
        same_doc | (key_pos[None, :] == query_pos[:, None])
    )
    scale_factor = HEAD_DIM ** (-0.5)

    def to_heads(rows_in):
        return rows_in.reshape(rows_in.shape[0], HEADS, HEAD_DIM).transpose(1, 0, 2)

    def from_heads(heads_in):
        return heads_in.transpose(1, 0, 2).reshape(heads_in.shape[1], model_width)

    head_q = to_heads(queries)
    head_k = to_heads(keys_all)
    head_v = to_heads(values_all)
    head_out, log_total = lax.map(
        partial(attend_head, allowed=allowed, scale_factor=scale_factor), (head_q, head_k, head_v)
    )
    attended = from_heads(head_out)
    residual = x_rows + jnp.dot(attended, out_w, preferred_element_type=jnp.float32)
    inv_two = lax.rsqrt(jnp.mean(residual * residual, axis=1, keepdims=True) + EPS)
    g_two = gain_two.astype(jnp.float32)
    normed_two = (residual * inv_two * g_two).astype(jnp.bfloat16)
    router_logits = jnp.dot(normed_two, router_full, preferred_element_type=jnp.float32)
    router_exp = jnp.exp(router_logits - jnp.max(router_logits, axis=1, keepdims=True))
    router_probs = router_exp / jnp.sum(router_exp, axis=1, keepdims=True)
    route_gates = jnp.take_along_axis(router_probs, routes[0], axis=1)
    shared_gate = jax.nn.sigmoid(jnp.dot(normed_two, gate_vec, preferred_element_type=jnp.float32))
    shared_scaled = (shared_gate[:, None] * cot_rows).astype(jnp.bfloat16)
    rows_group, grads_group = (normed_two, shared_scaled)
    gate_pre = jnp.dot(rows_group, sh_gate, preferred_element_type=jnp.float32)
    up_pre = jnp.dot(rows_group, sh_up, preferred_element_type=jnp.float32)
    gate_act = gate_pre * jax.nn.sigmoid(gate_pre)
    shared_hidden = (gate_act * up_pre).astype(jnp.bfloat16)
    shared_part = jnp.dot(shared_hidden, sh_down, preferred_element_type=jnp.float32)
    experts_all = router_full.shape[1]
    capacity = (9 * tokens_here * TOP + 8 * experts_all - 1) // (8 * experts_all)
    priority = (order[0, 0][:, None] * TOP + jnp.arange(TOP, dtype=jnp.int32)[None, :]).reshape(-1)
    flat_routes = routes[0].reshape(-1)
    slot_index = block_slots(flat_routes, priority, experts_all)
    kept_rows = slot_index < capacity
    target = flat_routes * capacity + jnp.minimum(slot_index, capacity - 1)
    row_gates = route_gates.reshape(-1)
    cot_repeated = jnp.repeat(cot_rows, TOP, axis=0)
    source_rows = jnp.repeat(normed_two, TOP, axis=0)
    source_grads = (cot_repeated * row_gates[:, None]).astype(jnp.bfloat16)
    empty_slots = jnp.zeros((experts_all * capacity, model_width), jnp.bfloat16)
    send_rows = empty_slots.at[target].add(
        jnp.where(kept_rows[:, None], source_rows, jnp.zeros_like(source_rows))
    )
    send_grads = empty_slots.at[target].add(
        jnp.where(kept_rows[:, None], source_grads, jnp.zeros_like(source_grads))
    )
    recv_rows, recv_grads = (
        lax.all_to_all(
            send_rows.reshape(experts_all, capacity, model_width),
            (EXP, CTX),
            split_axis=0,
            concat_axis=0,
            tiled=True,
        ),
        lax.all_to_all(
            send_grads.reshape(experts_all, capacity, model_width),
            (EXP, CTX),
            split_axis=0,
            concat_axis=0,
            tiled=True,
        ),
    )
    local_count = ex_gate.shape[0]
    sources = experts_all // local_count

    def to_local(buffer_in):
        return (
            buffer_in.reshape(sources, local_count, capacity, model_width)
            .transpose(1, 0, 2, 3)
            .reshape(local_count, sources * capacity, model_width)
        )

    def to_owner(buffer_in):
        return (
            buffer_in.reshape(local_count, sources, capacity, model_width)
            .transpose(1, 0, 2, 3)
            .reshape(experts_all, capacity, model_width)
        )

    expert_rows = to_local(recv_rows)
    expert_grads_in = to_local(recv_grads)
    gate_e = jnp.einsum("erd,edf->erf", expert_rows, ex_gate, preferred_element_type=jnp.float32)
    up_e = jnp.einsum("erd,edf->erf", expert_rows, ex_up, preferred_element_type=jnp.float32)
    act_e = gate_e * jax.nn.sigmoid(gate_e)
    hidden_e = (act_e * up_e).astype(jnp.bfloat16)
    result_e = jnp.einsum(
        "erf,efd->erd", hidden_e, ex_down, preferred_element_type=jnp.float32
    ).astype(jnp.bfloat16)
    returned = lax.all_to_all(
        to_owner(result_e), (EXP, CTX), split_axis=0, concat_axis=0, tiled=True
    )
    picked = returned.reshape(experts_all * capacity, model_width)[target]
    picked = jnp.where(kept_rows[:, None], picked, jnp.zeros_like(picked)).astype(jnp.float32)
    routed = jnp.sum((picked * row_gates[:, None]).reshape(tokens_here, TOP, model_width), axis=1)
    output = (residual + shared_gate[:, None] * shared_part + routed).astype(jnp.bfloat16)
    gate_grads = jnp.sum(picked * cot_repeated, axis=1).reshape(tokens_here, TOP)
    hidden_grad_e = jnp.einsum(
        "erd,efd->erf", expert_grads_in, ex_down, preferred_element_type=jnp.float32
    )
    gate_grad_e = (hidden_grad_e * up_e * silu_grad(gate_e)).astype(jnp.bfloat16)
    up_grad_e = (hidden_grad_e * act_e).astype(jnp.bfloat16)
    grad_ex_down = jnp.einsum(
        "erf,erd->efd", hidden_e, expert_grads_in, preferred_element_type=jnp.float32
    )
    grad_ex_gate = jnp.einsum(
        "erd,erf->edf", expert_rows, gate_grad_e, preferred_element_type=jnp.float32
    )
    grad_ex_up = jnp.einsum(
        "erd,erf->edf", expert_rows, up_grad_e, preferred_element_type=jnp.float32
    )
    expert_sums = (
        lax.psum_scatter(grad_ex_gate, DP, scatter_dimension=1, tiled=True),
        lax.psum_scatter(grad_ex_up, DP, scatter_dimension=1, tiled=True),
        lax.psum_scatter(grad_ex_down, DP, scatter_dimension=2, tiled=True),
    )
    rows_grad_e = jnp.einsum(
        "erf,edf->erd", gate_grad_e, ex_gate, preferred_element_type=jnp.float32
    )
    rows_grad_e = (
        rows_grad_e
        + jnp.einsum("erf,edf->erd", up_grad_e, ex_up, preferred_element_type=jnp.float32)
    ).astype(jnp.bfloat16)
    returned_grads = lax.all_to_all(
        to_owner(rows_grad_e), (EXP, CTX), split_axis=0, concat_axis=0, tiled=True
    )
    routed_grad = returned_grads.reshape(experts_all * capacity, model_width)[target]
    routed_grad = jnp.where(kept_rows[:, None], routed_grad, jnp.zeros_like(routed_grad)).astype(
        jnp.float32
    )
    norm_grad = jnp.sum(routed_grad.reshape(tokens_here, TOP, model_width), axis=1)
    choose = (
        routes[0][:, :, None] == jnp.arange(experts_all, dtype=jnp.int32)[None, None, :]
    ).astype(jnp.float32)
    probs_grad = jnp.einsum("tk,tke->te", gate_grads, choose)
    logit_grad = (
        router_probs * (probs_grad - jnp.sum(router_probs * probs_grad, axis=1, keepdims=True))
    ).astype(jnp.bfloat16)
    grad_router = jnp.dot(normed_two.T, logit_grad, preferred_element_type=jnp.float32)
    gate_logit_grad = (
        jnp.sum(cot_rows * shared_part, axis=1) * shared_gate * (1.0 - shared_gate)
    ).astype(jnp.bfloat16)
    grad_gate_vec = jnp.dot(gate_logit_grad, normed_two, preferred_element_type=jnp.float32)
    norm_grad = norm_grad + jnp.dot(logit_grad, router_full.T, preferred_element_type=jnp.float32)
    norm_grad = (
        norm_grad
        + gate_logit_grad.astype(jnp.float32)[:, None] * gate_vec.astype(jnp.float32)[None, :]
    )
    shared_hgrad = jnp.dot(grads_group, sh_down.T, preferred_element_type=jnp.float32)
    gate_grad_s = (shared_hgrad * up_pre * silu_grad(gate_pre)).astype(jnp.bfloat16)
    up_grad_s = (shared_hgrad * gate_act).astype(jnp.bfloat16)
    shared_rows_grad = jnp.dot(gate_grad_s, sh_gate.T, preferred_element_type=jnp.float32)
    shared_rows_grad = shared_rows_grad + jnp.dot(
        up_grad_s, sh_up.T, preferred_element_type=jnp.float32
    )
    groups = lax.axis_size(EXP)
    parts_cd = lax.axis_size((CTX, DP))
    rows_count = rows_group.shape[0]
    arr_gate = jnp.einsum(
        "td,tes->eds",
        rows_group,
        gate_grad_s.reshape(rows_count, groups, -1),
        preferred_element_type=jnp.float32,
    ).reshape(groups * model_width, -1)
    arr_up = jnp.einsum(
        "td,tes->eds",
        rows_group,
        up_grad_s.reshape(rows_count, groups, -1),
        preferred_element_type=jnp.float32,
    ).reshape(groups * model_width, -1)
    arr_down = jnp.einsum(
        "tes,tcd->ecsd",
        shared_hidden.reshape(rows_count, groups, -1),
        grads_group.reshape(rows_count, parts_cd, -1),
        preferred_element_type=jnp.float32,
    ).reshape(-1, model_width // parts_cd)
    sums_gate, sums_up, sums_down = (
        lax.psum_scatter(arr_gate, (EXP, CTX, DP), scatter_dimension=0, tiled=True),
        lax.psum_scatter(arr_up, (EXP, CTX, DP), scatter_dimension=0, tiled=True),
        lax.psum_scatter(arr_down, (EXP, CTX, DP), scatter_dimension=0, tiled=True),
    )
    norm_grad = norm_grad + shared_rows_grad
    residual_grad, grad_gain_two = norm_back(residual, inv_two, g_two, norm_grad)
    residual_grad = residual_grad + cot_rows
    low_residual = residual_grad.astype(jnp.bfloat16)
    grad_out_w = jnp.dot(attended.T, low_residual, preferred_element_type=jnp.float32)
    attended_grad = jnp.dot(low_residual, out_w.T, preferred_element_type=jnp.float32).astype(
        jnp.bfloat16
    )
    head_q_grad, head_k_grad, head_v_grad = lax.map(
        partial(attend_back, allowed=allowed, scale_factor=scale_factor),
        (head_q, head_k, head_v, to_heads(attended_grad), log_total),
    )
    key_sum, value_sum = (
        lax.psum_scatter(from_heads(head_k_grad), CTX, scatter_dimension=0, tiled=True),
        lax.psum_scatter(from_heads(head_v_grad), CTX, scatter_dimension=0, tiled=True),
    )
    query_low = from_heads(head_q_grad).astype(jnp.bfloat16)
    key_low = key_sum.astype(jnp.bfloat16)
    value_low = value_sum.astype(jnp.bfloat16)
    grad_query = jnp.dot(normed_one.T, query_low, preferred_element_type=jnp.float32)
    grad_key = jnp.dot(normed_one.T, key_low, preferred_element_type=jnp.float32)
    grad_value = jnp.dot(normed_one.T, value_low, preferred_element_type=jnp.float32)
    normed_grad = jnp.dot(query_low, query_w.T, preferred_element_type=jnp.float32)
    normed_grad = normed_grad + jnp.dot(key_low, key_w.T, preferred_element_type=jnp.float32)
    normed_grad = normed_grad + jnp.dot(value_low, value_w.T, preferred_element_type=jnp.float32)
    input_part, grad_gain_one = norm_back(x_rows, inv_one, g_one, normed_grad)
    input_grad = (residual_grad + input_part).astype(jnp.bfloat16)
    dense = (
        lax.psum_scatter(
            grad_gain_one, (EXP, CTX, DP), scatter_dimension=0, tiled=True
        ),
        lax.psum_scatter(grad_query, (EXP, CTX, DP), scatter_dimension=0, tiled=True),
        lax.psum_scatter(grad_key, (EXP, CTX, DP), scatter_dimension=0, tiled=True),
        lax.psum_scatter(grad_value, (EXP, CTX, DP), scatter_dimension=0, tiled=True),
        lax.psum_scatter(grad_out_w, (EXP, CTX, DP), scatter_dimension=0, tiled=True),
        lax.psum_scatter(
            grad_gain_two, (EXP, CTX, DP), scatter_dimension=0, tiled=True
        ),
        lax.psum_scatter(
            grad_router, (EXP, CTX, DP), scatter_dimension=0, tiled=True
        ),
        lax.psum_scatter(
            grad_gate_vec, (EXP, CTX, DP), scatter_dimension=0, tiled=True
        ),
    )
    return (
        output[None],
        input_grad[None],
        dense[0],
        dense[1],
        dense[2],
        dense[3],
        dense[4],
        dense[5],
        dense[6],
        dense[7],
        sums_gate,
        sums_up,
        sums_down,
        expert_sums[0],
        expert_sums[1],
        expert_sums[2],
    )

def attention_probs(q_blk, k_part, q_code, k_code, first_row, scale_factor):
    scores = lax.dot_general(
        q_blk, k_part, (((1,), (1,)), ((), ())), preferred_element_type=jnp.float32
    )
    row = first_row + lax.broadcasted_iota(jnp.int32, scores.shape, 0)
    col = lax.broadcasted_iota(jnp.int32, scores.shape, 1)
    allowed = ((col < row) & (k_code == q_code)) | (col == row)
    logits = jnp.where(allowed, scores * scale_factor, NEG)
    exp_scores = jnp.exp(logits - jnp.max(logits, axis=1, keepdims=True))
    return exp_scores * (1.0 / jnp.sum(exp_scores, axis=1, keepdims=True))


def attend_kernel(heads, step, qkv_ref, q_code_ref, k_code_ref, out_ref):
    seq_len = qkv_ref.shape[0]
    width = heads * HEAD_DIM
    for head in range(heads):
        at = head * HEAD_DIM
        for first in range(0, seq_len, step):
            upto = first + step
            probs = attention_probs(
                qkv_ref[first:upto, at : at + HEAD_DIM],
                qkv_ref[0:upto, width + at : width + at + HEAD_DIM],
                q_code_ref[first:upto, :],
                k_code_ref[0, :, 0:upto],
                first,
                HEAD_DIM**-0.5,
            )
            out_ref[first:upto, at : at + HEAD_DIM] = jnp.dot(
                probs.astype(jnp.bfloat16),
                qkv_ref[0:upto, 2 * width + at : 2 * width + at + HEAD_DIM],
                preferred_element_type=jnp.float32,
            ).astype(jnp.bfloat16)


def attend_back_kernel(
    heads, step, qkv_ref, grad_ref, q_code_ref, k_code_ref, out_ref, key_acc, value_acc
):
    seq_len = qkv_ref.shape[0]
    width = heads * HEAD_DIM
    for head in range(heads):
        at = head * HEAD_DIM
        key_at, value_at = width + at, 2 * width + at
        key_acc[...] = jnp.zeros_like(key_acc)
        value_acc[...] = jnp.zeros_like(value_acc)
        for first in range(0, seq_len, step):
            upto = first + step
            q_blk = qkv_ref[first:upto, at : at + HEAD_DIM]
            k_part = qkv_ref[0:upto, key_at : key_at + HEAD_DIM]
            v_part = qkv_ref[0:upto, value_at : value_at + HEAD_DIM]
            g_blk = grad_ref[first:upto, at : at + HEAD_DIM]
            probs = attention_probs(
                q_blk,
                k_part,
                q_code_ref[first:upto, :],
                k_code_ref[0, :, 0:upto],
                first,
                HEAD_DIM**-0.5,
            )
            prob_grad = lax.dot_general(
                g_blk, v_part, (((1,), (1,)), ((), ())), preferred_element_type=jnp.float32
            )
            inner = jnp.sum(probs * prob_grad, axis=1, keepdims=True)
            score_grad = (probs * (prob_grad - inner) * HEAD_DIM**-0.5).astype(jnp.bfloat16)
            out_ref[first:upto, at : at + HEAD_DIM] = jnp.dot(
                score_grad, k_part, preferred_element_type=jnp.float32
            ).astype(jnp.bfloat16)
            key_acc[0:upto, :] += lax.dot_general(
                score_grad, q_blk, (((0,), (0,)), ((), ())), preferred_element_type=jnp.float32
            )
            value_acc[0:upto, :] += lax.dot_general(
                probs.astype(jnp.bfloat16),
                g_blk,
                (((0,), (0,)), ((), ())),
                preferred_element_type=jnp.float32,
            )
        out_ref[:, key_at : key_at + HEAD_DIM] = key_acc[...].astype(jnp.bfloat16)
        out_ref[:, value_at : value_at + HEAD_DIM] = value_acc[...].astype(jnp.bfloat16)


def attention_call(qkv, grads, q_codes, k_codes, seq_len):
    rows, triple = qkv.shape
    width = triple // 3
    heads = width // HEAD_DIM
    step = min(256, seq_len)
    specs = [pl.BlockSpec((seq_len, triple), lambda s: (s, 0))]
    operands = [qkv]
    if grads is not None:
        specs.append(pl.BlockSpec((seq_len, width), lambda s: (s, 0)))
        operands.append(grads)
    specs += [
        pl.BlockSpec((seq_len, 1), lambda s: (s, 0)),
        pl.BlockSpec((1, 1, seq_len), lambda s: (s, 0, 0)),
    ]
    operands += [q_codes, k_codes]
    out_width = width if grads is None else triple
    body = attend_kernel if grads is None else attend_back_kernel
    passes = 2 if grads is None else 5
    area = rows * seq_len * heads
    return pl.pallas_call(
        partial(body, heads, step),
        grid=(rows // seq_len,),
        in_specs=specs,
        out_specs=pl.BlockSpec((seq_len, out_width), lambda s: (s, 0)),
        out_shape=jax.ShapeDtypeStruct((rows, out_width), jnp.bfloat16),
        scratch_shapes=[]
        if grads is None
        else [pltpu.VMEM((seq_len, HEAD_DIM), jnp.float32)] * 2,
        compiler_params=pltpu.CompilerParams(vmem_limit_bytes=48 * 2**20),
        cost_estimate=pl.CostEstimate(
            flops=2 * passes * area * HEAD_DIM,
            bytes_accessed=2 * rows * (triple + out_width),
            transcendentals=area,
        ),
    )(*operands)


MESH_ID = pl.DeviceIdType.MESH


def other_in_pair(index, bit):
    return index + bit - 2 * bit * (lax.div(index, bit) % 2)


def plane_places():
    at = lax.axis_index(EXP)
    core = lax.axis_index(CTX)
    across, along = other_in_pair(at, 1), other_in_pair(at, 2)
    return at, core, across, along, other_in_pair(along, 1)


def greet(across, along, core):
    barrier = pltpu.get_barrier_semaphore()
    for target in ({EXP: across}, {EXP: along}, {CTX: 1 - core}):
        pl.semaphore_signal(barrier, inc=1, device_id=target, device_id_type=MESH_ID)
    pl.semaphore_wait(barrier, 3)


def plane_gather_kernel(with_info, relative, *refs):
    if with_info:
        own_ref, info_ref, all_ref, info_all_ref, send_sem, recv_sem, local_sem = refs
    else:
        own_ref, all_ref, send_sem, recv_sem, local_sem = refs
    at, core, across, along, far = plane_places()
    rows = own_ref.shape[0]
    half = rows // 2
    top, bottom, whole = pl.ds(0, half), pl.ds(half, half), pl.ds(0, rows)
    greet(across, along, core)
    started = []
    twin_id = {CTX: 1 - core}

    def slot_of(place, shift, for_twin):
        if relative:
            return shift + 4 * for_twin
        return place * 2 + core

    def send(number, src, dst, target):
        copy = pltpu.make_async_remote_copy(
            src_ref=src,
            dst_ref=dst,
            send_sem=send_sem.at[number],
            recv_sem=recv_sem.at[number],
            device_id=target,
            device_id_type=MESH_ID,
        )
        copy.start()
        started.append(copy)
        return copy

    def piece(place, shift, part, for_twin=0):
        return all_ref.at[slot_of(place, shift, for_twin), part]

    x_top = send(0, own_ref.at[top], piece(at, 1, top), {EXP: across})
    y_bottom = send(1, own_ref.at[bottom], piece(at, 2, bottom), {EXP: along})
    x_bottom = send(2, own_ref.at[bottom], piece(at, 1, bottom), {EXP: across})
    y_top = send(3, own_ref.at[top], piece(at, 2, top), {EXP: along})
    twins = [send(4, own_ref, piece(at, 0, whole, 1), twin_id)]
    heres = [pltpu.make_async_copy(own_ref, piece(at, 0, whole), local_sem.at[0])]
    heres[0].start()
    if with_info:
        info_at = lambda place: info_all_ref.at[place * 2 + core]
        heres.append(pltpu.make_async_copy(info_ref, info_at(at), local_sem.at[1]))
        heres[1].start()
        info_x = send(13, info_ref, info_at(at), {EXP: across})
        info_y = send(14, info_ref, info_at(at), {EXP: along})
        twins.append(send(15, info_ref, info_at(at), twin_id))
        info_x.wait_recv()
        info_far = send(16, info_at(across), info_at(across), {EXP: along})
        twins.append(send(17, info_at(across), info_at(across), twin_id))
        info_y.wait_recv()
        twins.append(send(18, info_at(along), info_at(along), twin_id))
        info_far.wait_recv()
        twins.append(send(19, info_at(far), info_at(far), twin_id))

    def hand_on(number, place, shift, part):
        src = piece(place, shift, part)
        twins.append(send(number, src, piece(place, shift, part, 1), twin_id))

    x_top.wait_recv()
    far_top = send(5, piece(across, 1, top), piece(across, 3, top), {EXP: along})
    hand_on(6, across, 1, top)
    y_bottom.wait_recv()
    far_bottom = send(7, piece(along, 2, bottom), piece(along, 3, bottom), {EXP: across})
    hand_on(8, along, 2, bottom)
    x_bottom.wait_recv()
    hand_on(9, across, 1, bottom)
    y_top.wait_recv()
    hand_on(10, along, 2, top)
    far_top.wait_recv()
    hand_on(11, far, 3, top)
    far_bottom.wait_recv()
    hand_on(12, far, 3, bottom)
    for copy in twins:
        copy.wait_recv()
    for copy in started:
        copy.wait_send()
    for copy in heres:
        copy.wait()


def plane_gather(own, info, relative, number):
    plane = lax.axis_size(PLANE)
    operands = [own] if info is None else [own, info]
    outs = [jax.ShapeDtypeStruct((plane, *v.shape), v.dtype) for v in operands]
    anywhere = pl.BlockSpec(memory_space=pl.ANY)
    return pl.pallas_call(
        partial(plane_gather_kernel, info is not None, relative),
        out_shape=outs,
        in_specs=[anywhere] * len(operands),
        out_specs=[anywhere] * len(operands),
        scratch_shapes=[
            pltpu.SemaphoreType.DMA((20,)),
            pltpu.SemaphoreType.DMA((20,)),
            pltpu.SemaphoreType.DMA((2,)),
        ],
        compiler_params=pltpu.CompilerParams(collective_id=number, has_side_effects=True),
        cost_estimate=pl.CostEstimate(
            flops=0, bytes_accessed=own.size, transcendentals=0
        ),
    )(*operands)


def plane_scatter_kernel(relative, with_extra, *refs):
    if with_extra:
        part_ref, extra_ref, out_ref, *refs = refs
        extra_out, refs = refs[:4], refs[4:]
        extra_own, extra_got, extra_sems, refs = refs[0], refs[1], refs[2:5], refs[5:]
    else:
        part_ref, out_ref, *refs = refs
    own, twin_got, x_got, y_got, x_last, y_last, send_sem, recv_sem, local_sem = refs
    at, core, across, along, far = plane_places()
    rows = part_ref.shape[1]
    half = rows // 2
    step = 64
    greet(across, along, core)
    started = []

    def send(number, src, dst, target):
        copy = pltpu.make_async_remote_copy(
            src_ref=src,
            dst_ref=dst,
            send_sem=send_sem.at[number],
            recv_sem=recv_sem.at[number],
            device_id=target,
            device_id_type=MESH_ID,
        )
        copy.start()
        started.append(copy)
        return copy

    twins, heres = [], []
    for j, (label, shift) in enumerate(((far, 3), (across, 1), (along, 2), (at, 0))):
        theirs = shift + 4 if relative else label * 2 + 1 - core
        ours = shift if relative else label * 2 + core
        twins.append(send(j, part_ref.at[theirs], twin_got.at[j], {CTX: 1 - core}))
        here = pltpu.make_async_copy(part_ref.at[ours], own.at[j], local_sem.at[j])
        here.start()
        heres.append(here)

    def add_rows(target, t_first, count, source, s_first):
        @pl.loop(0, count // step)
        def _(i):
            into = pl.ds(pl.multiple_of(t_first + i * step, step), step)
            take = pl.ds(pl.multiple_of(s_first + i * step, step), step)
            total = target[into].astype(jnp.float32) + source[take].astype(jnp.float32)
            target[into] = total.astype(target.dtype)

    top, bottom = pl.ds(0, half), pl.ds(half, half)
    x_sent, y_sent = [], []
    for j in range(4):
        twins[j].wait_recv()
        heres[j].wait()
        add_rows(own.at[j], 0, rows, twin_got.at[j], 0)
        if j < 2:
            x_sent.append(send(4 + j, own.at[j, top], x_got.at[j], {EXP: across}))
        if j == 0 or j == 2:
            y_sent.append(send(6 + j // 2, own.at[j, bottom], y_got.at[j // 2], {EXP: along}))
    if with_extra:
        extra_here, extra_twin, extra_done = [], [], []
        for k in range(4):
            copy = pltpu.make_async_remote_copy(
                src_ref=extra_ref.at[k + 4],
                dst_ref=extra_got.at[k],
                send_sem=extra_sems[0].at[k],
                recv_sem=extra_sems[1].at[k],
                device_id={CTX: 1 - core},
                device_id_type=MESH_ID,
            )
            copy.start()
            started.append(copy)
            extra_twin.append(copy)
            here = pltpu.make_async_copy(extra_ref.at[k], extra_own.at[k], extra_sems[2].at[k])
            here.start()
            extra_here.append(here)
        for k in range(4):
            extra_twin[k].wait_recv()
            extra_here[k].wait()
            add_rows(extra_own.at[k], 0, rows, extra_got.at[k], 0)
            here = pltpu.make_async_copy(extra_own.at[k], extra_out[k], extra_sems[2].at[k])
            here.start()
            extra_done.append(here)
    x_sent[0].wait_recv()
    add_rows(own.at[2], 0, half, x_got.at[0], 0)
    last_y = send(8, own.at[2, top], y_last, {EXP: along})
    y_sent[0].wait_recv()
    add_rows(own.at[1], half, half, y_got.at[0], 0)
    last_x = send(9, own.at[1, bottom], x_last, {EXP: across})

    def finish(first, near, later):
        @pl.loop(0, half // step)
        def _(i):
            take = pl.ds(pl.multiple_of(i * step, step), step)
            into = pl.ds(pl.multiple_of(first + i * step, step), step)
            out_ref[into] = (
                own[3, into].astype(jnp.float32)
                + near[1, take].astype(jnp.float32)
                + later[take].astype(jnp.float32)
            ).astype(out_ref.dtype)

    x_sent[1].wait_recv()
    last_y.wait_recv()
    finish(0, x_got, y_last)
    y_sent[1].wait_recv()
    last_x.wait_recv()
    finish(half, y_got, x_last)
    if with_extra:
        for copy in extra_done:
            copy.wait()
    for copy in started:
        copy.wait_send()


def plane_scatter(parts, relative, number, out_type, extra=None):
    plane, rows, cols = parts.shape
    operands, extra_scratch = [parts], []
    out_shape = [jax.ShapeDtypeStruct((rows, cols), out_type)]
    out_specs = [pl.BlockSpec(memory_space=pltpu.VMEM)]
    anywhere = pl.BlockSpec(memory_space=pl.ANY)
    if extra is not None:
        operands.append(extra)
        out_shape += [jax.ShapeDtypeStruct((rows, cols), extra.dtype)] * 4
        out_specs += [anywhere] * 4
        extra_scratch = [pltpu.VMEM((4, rows, cols), extra.dtype)] * 2
        extra_scratch += [pltpu.SemaphoreType.DMA((4,))] * 3
    half = rows // 2
    vmem = lambda *shape: pltpu.VMEM(shape, parts.dtype)
    return pl.pallas_call(
        partial(plane_scatter_kernel, relative, extra is not None),
        out_shape=out_shape,
        in_specs=[anywhere] * len(operands),
        out_specs=out_specs,
        scratch_shapes=extra_scratch
        + [
            vmem(4, rows, cols),
            vmem(4, rows, cols),
            vmem(2, half, cols),
            vmem(2, half, cols),
            vmem(half, cols),
            vmem(half, cols),
            pltpu.SemaphoreType.DMA((10,)),
            pltpu.SemaphoreType.DMA((10,)),
            pltpu.SemaphoreType.DMA((4,)),
        ],
        compiler_params=pltpu.CompilerParams(
            collective_id=number,
            has_side_effects=True,
            vmem_limit_bytes=(36 if extra is None else 54) * 2**20,
        ),
        cost_estimate=pl.CostEstimate(
            flops=0, bytes_accessed=rows * cols, transcendentals=0
        ),
    )(*operands)


def norm_qkv_kernel(hidden_ref, gain_ref, w_ref, norm_ref, qkv_ref):
    values = hidden_ref[...].astype(jnp.float32)
    inv = lax.rsqrt(jnp.mean(values * values, axis=1, keepdims=True) + EPS)
    norm_ref[...] = low(values * inv * gain_ref[...])
    qkv_ref[...] = low(mm(norm_ref[...], w_ref[...]))


def norm_qkv(hidden, gain, w, block):
    rows, width = hidden.shape
    cols = w.shape[1]
    return pl.pallas_call(
        norm_qkv_kernel,
        grid=(rows // block,),
        in_specs=[
            pl.BlockSpec((block, width), lambda i: (i, 0)),
            pl.BlockSpec((1, width), lambda i: (0, 0)),
            pl.BlockSpec((width, cols), lambda i: (0, 0)),
        ],
        out_specs=[
            pl.BlockSpec((block, width), lambda i: (i, 0)),
            pl.BlockSpec((block, cols), lambda i: (i, 0)),
        ],
        out_shape=[
            jax.ShapeDtypeStruct((rows, width), jnp.bfloat16),
            jax.ShapeDtypeStruct((rows, cols), jnp.bfloat16),
        ],
        compiler_params=pltpu.CompilerParams(vmem_limit_bytes=48 * 2**20),
        cost_estimate=pl.CostEstimate(
            flops=2 * rows * width * cols,
            bytes_accessed=4 * rows * width,
            transcendentals=0,
        ),
    )(hidden, gain, w)


def chosen_rows(slots, capacity):
    lanes = lax.broadcasted_iota(jnp.int32, (slots.shape[0], capacity), 1)
    return (slots == lanes).astype(jnp.bfloat16)


def output_kernel(
    half,
    hidden_ref,
    down_ref,
    rows_ref,
    slot_ref,
    sg_ref,
    gate_ref,
    cot_ref,
    near_ref,
    dots_ref,
    given,
    got,
    send_sem,
    recv_sem,
):
    step_at = pl.program_id(0)
    is_far = step_at < half
    slot = lax.rem(step_at, half)
    twin_id = {CTX: 1 - lax.axis_index(CTX)}

    @pl.when(step_at == 0)
    def _():
        barrier = pltpu.get_barrier_semaphore()
        pl.semaphore_signal(barrier, inc=1, device_id=twin_id, device_id_type=MESH_ID)
        pl.semaphore_wait(barrier, 1)

    def block_copy(k):
        return pltpu.make_async_remote_copy(
            src_ref=given.at[k],
            dst_ref=got.at[k],
            send_sem=send_sem.at[k],
            recv_sem=recv_sem.at[k],
            device_id=twin_id,
            device_id_type=MESH_ID,
        )

    def make(store):
        chosen = chosen_rows(slot_ref[...], rows_ref.shape[1])
        hidden = hidden_ref[...].T
        tokens, width = cot_ref.shape
        step, lanes = 512, 128
        gate_dot = jnp.zeros((tokens, lanes), jnp.float32)
        shared_dot = jnp.zeros((tokens, lanes), jnp.float32)
        for first in range(0, width, step):
            cols = pl.ds(first, step)
            shared = mm(hidden, down_ref[:, cols])
            picked = mm(chosen, rows_ref[0, :, cols])
            cot = cot_ref[:, cols].astype(jnp.float32)
            gate_part, shared_part = picked * cot, shared * cot
            for at in range(0, step, lanes):
                gate_dot += gate_part[:, at : at + lanes]
                shared_dot += shared_part[:, at : at + lanes]
            store(cols, sg_ref[...] * shared + gate_ref[...] * picked)
        lane = lax.broadcasted_iota(jnp.int32, dots_ref.shape, 1)
        gate_dot = jnp.sum(gate_dot, axis=1, keepdims=True)
        shared_dot = jnp.sum(shared_dot, axis=1, keepdims=True)
        dots_ref[...] = jnp.where(lane == 0, gate_dot, jnp.where(lane == 1, shared_dot, 0.0))

    @pl.when(is_far)
    def _():
        def store(cols, total):
            given[slot, :, cols] = low(total)

        make(store)
        block_copy(slot).start()

    @pl.when(jnp.logical_not(is_far))
    def _():
        block_copy(slot).wait_recv()

        def store(cols, total):
            near_ref[0, :, cols] = low(total + got[slot, :, cols].astype(jnp.float32))

        make(store)

    @pl.when(step_at == 2 * half - 1)
    def _():
        for k in range(half):
            block_copy(k).wait_send()


def output_parts(hidden, down, rows, slots, sg, gates, cot):
    blocks, capacity, width = rows.shape
    units, count = hidden.shape
    tokens, half = count // blocks, blocks // 2
    at = lambda i: lax.rem(i + half, blocks)
    column = pl.BlockSpec((tokens, 1), lambda i: (at(i), 0))
    return pl.pallas_call(
        partial(output_kernel, half),
        grid=(blocks,),
        in_specs=[
            pl.BlockSpec((units, tokens), lambda i: (0, at(i))),
            pl.BlockSpec((units, width), lambda i: (0, 0)),
            pl.BlockSpec((1, capacity, width), lambda i: (at(i), 0, 0)),
            column,
            column,
            column,
            pl.BlockSpec((tokens, width), lambda i: (at(i), 0)),
        ],
        out_specs=[
            pl.BlockSpec((1, tokens, width), lambda i: (jnp.maximum(i - half, 0), 0, 0)),
            pl.BlockSpec((tokens, 128), lambda i: (at(i), 0)),
        ],
        out_shape=[
            jax.ShapeDtypeStruct((half, tokens, width), jnp.bfloat16),
            jax.ShapeDtypeStruct((count, 128), jnp.float32),
        ],
        scratch_shapes=[
            pltpu.VMEM((half, tokens, width), jnp.bfloat16),
            pltpu.VMEM((half, tokens, width), jnp.bfloat16),
            pltpu.SemaphoreType.DMA((half,)),
            pltpu.SemaphoreType.DMA((half,)),
        ],
        compiler_params=pltpu.CompilerParams(
            collective_id=4, has_side_effects=True, vmem_limit_bytes=56 * 2**20
        ),
        cost_estimate=pl.CostEstimate(
            flops=2 * count * width * (units + capacity),
            bytes_accessed=6 * count * width,
            transcendentals=0,
        ),
    )(hidden, down, rows, slots, sg, gates, cot)


def scatter_step(compute, out_ref, scratch):
    given, total, x_got, y_got, x_last, y_last, send_sem, recv_sem = scratch
    at, core, across, along, far = plane_places()
    step_at = pl.program_id(0)
    row = step_at // 2
    is_twin = step_at % 2 == 0
    rows = total.shape[1]
    half = rows // 2
    top, bottom = pl.ds(0, half), pl.ds(half, half)

    def copy_of(number, src, dst, target):
        return pltpu.make_async_remote_copy(
            src_ref=src,
            dst_ref=dst,
            send_sem=send_sem.at[number],
            recv_sem=recv_sem.at[number],
            device_id=target,
            device_id_type=MESH_ID,
        )

    def twin_copy(k):
        return copy_of(k, given.at[k % 2], total.at[k], {CTX: 1 - core})

    far_x = copy_of(4, total.at[0, top], x_got.at[0], {EXP: across})
    far_y = copy_of(5, total.at[0, bottom], y_got.at[0], {EXP: along})
    own_x = copy_of(6, total.at[1, top], x_got.at[1], {EXP: across})
    own_y = copy_of(7, total.at[2, bottom], y_got.at[1], {EXP: along})
    last_y = copy_of(8, total.at[2, top], y_last, {EXP: along})
    last_x = copy_of(9, total.at[1, bottom], x_last, {EXP: across})

    @pl.when(step_at == 0)
    def _():
        greet(across, along, core)

    @pl.when(is_twin)
    def _():
        @pl.when(row >= 2)
        def _():
            twin_copy(row - 2).wait_send()

        def store(cols, values):
            given[row % 2, :, cols] = low(values)

        compute(store)
        twin_copy(row).start()

    @pl.when(jnp.logical_not(is_twin))
    def _():
        twin_copy(row).wait_recv()

        def store(cols, values):
            total[row, :, cols] = low(values + total[row, :, cols].astype(jnp.float32))

        compute(store)

    @pl.when(step_at == 1)
    def _():
        far_x.start()
        far_y.start()

    @pl.when(step_at == 3)
    def _():
        own_x.start()

    @pl.when(step_at == 5)
    def _():
        own_y.start()

    @pl.when(step_at == 7)
    def _():
        def add_half(k, first, got):
            @pl.loop(0, half // 64)
            def _(i):
                take = pl.ds(pl.multiple_of(i * 64, 64), 64)
                into = pl.ds(pl.multiple_of(first + i * 64, 64), 64)
                total[k, into] = low(
                    total[k, into].astype(jnp.float32) + got[0, take].astype(jnp.float32)
                )

        def finish(first, near, later):
            @pl.loop(0, half // 64)
            def _(i):
                take = pl.ds(pl.multiple_of(i * 64, 64), 64)
                into = pl.ds(pl.multiple_of(first + i * 64, 64), 64)
                out_ref[into] = (
                    total[3, into].astype(jnp.float32)
                    + near[1, take].astype(jnp.float32)
                    + later[take].astype(jnp.float32)
                )

        far_x.wait_recv()
        add_half(2, 0, x_got)
        last_y.start()
        far_y.wait_recv()
        add_half(1, half, y_got)
        last_x.start()
        own_x.wait_recv()
        last_y.wait_recv()
        finish(0, x_got, y_last)
        own_y.wait_recv()
        last_x.wait_recv()
        finish(half, y_got, x_last)
        for copy in (twin_copy(2), twin_copy(3), far_x, far_y, own_x, own_y, last_y, last_x):
            copy.wait_send()


def step_slot(i):
    row = i // 2
    shift = jnp.where(row == 0, 3, jnp.where(row == 3, 0, row))
    return shift + 4 * (1 - i % 2)


def scatter_scratch(tokens, width):
    vmem = lambda *shape: pltpu.VMEM(shape, jnp.bfloat16)
    return [
        vmem(2, tokens, width),
        vmem(4, tokens, width),
        vmem(2, tokens // 2, width),
        vmem(2, tokens // 2, width),
        vmem(tokens // 2, width),
        vmem(tokens // 2, width),
        pltpu.SemaphoreType.DMA((10,)),
        pltpu.SemaphoreType.DMA((10,)),
    ]


def n2_grad_kernel(dgate_ref, dup_ref, gate_ref, up_ref, rows_ref, slot_ref, out_ref, *scratch):
    def compute(store):
        chosen = chosen_rows(slot_ref[...], rows_ref.shape[1])
        dgate, dup = dgate_ref[...].T, dup_ref[...].T
        step = 512
        for first in range(0, gate_ref.shape[1], step):
            cols = pl.ds(first, step)
            total = mm(dgate, gate_ref[:, cols]) + mm(dup, up_ref[:, cols])
            store(cols, total + mm(chosen, rows_ref[0, :, cols]))

    scatter_step(compute, out_ref, scratch)


def n2_grad_sum(dgate, dup, gate_w, up_w, rows, slots):
    blocks, capacity, width = rows.shape
    units, count = dgate.shape
    tokens = count // blocks
    by_units = pl.BlockSpec((units, tokens), lambda i: (0, step_slot(i)))
    whole = pl.BlockSpec((units, width), lambda i: (0, 0), pipeline_mode=pl.Buffered(1))
    return pl.pallas_call(
        n2_grad_kernel,
        grid=(blocks,),
        in_specs=[
            by_units,
            by_units,
            whole,
            whole,
            pl.BlockSpec((1, capacity, width), lambda i: (step_slot(i), 0, 0)),
            pl.BlockSpec((tokens, 1), lambda i: (step_slot(i), 0)),
        ],
        out_specs=pl.BlockSpec((tokens, width), lambda i: (0, 0)),
        out_shape=jax.ShapeDtypeStruct((tokens, width), jnp.float32),
        scratch_shapes=scatter_scratch(tokens, width),
        compiler_params=pltpu.CompilerParams(
            collective_id=3, has_side_effects=True, vmem_limit_bytes=56 * 2**20
        ),
        cost_estimate=pl.CostEstimate(
            flops=2 * count * width * (2 * units + capacity),
            bytes_accessed=4 * count * width,
            transcendentals=0,
        ),
    )(dgate, dup, gate_w, up_w, rows, slots)


def unit_grad_kernel(left_ref, right_ref, out_ref):
    out_ref[0] = low(mm(left_ref[...], right_ref[...]))


def unit_grads(left, right, depth, halves):
    units, count = left.shape
    width = right.shape[1]
    cols = width // (depth * halves)
    return pl.pallas_call(
        unit_grad_kernel,
        grid=(depth * halves,),
        in_specs=[
            pl.BlockSpec((units, count), lambda i: (0, 0)),
            pl.BlockSpec((count, cols), lambda i: (0, i)),
        ],
        out_specs=pl.BlockSpec((1, units, cols), lambda i: (lax.rem(i, depth), 0, i // depth)),
        out_shape=jax.ShapeDtypeStruct((depth, units, halves * cols), jnp.bfloat16),
        compiler_params=pltpu.CompilerParams(vmem_limit_bytes=48 * 2**20),
        cost_estimate=pl.CostEstimate(
            flops=2 * units * count * width,
            bytes_accessed=2 * (units * count + count * width + units * width),
            transcendentals=0,
        ),
    )(left, right)


def after(values, others):
    return lax.optimization_barrier((values, others))[0]


def swap(values, bits):
    return lax.ppermute(values, EXP, [(i, i ^ bits) for i in range(4)])


def twin(values):
    return lax.ppermute(values, CTX, [(0, 1), (1, 0)])


def twin_sums(ours, theirs):
    got = twin(theirs)
    return [low(ours[k].astype(jnp.float32) + got[k].astype(jnp.float32)) for k in range(4)]


def hops(sums):
    return [sums[0]] + [swap(sums[k], k) for k in (1, 2, 3)]


def sum_up(parts):
    return sum(v.astype(jnp.float32) for v in parts)


def mm(left, right, dims=((1,), (0,))):
    return lax.dot_general(left, right, (dims, ((), ())), preferred_element_type=jnp.float32)


def low(values):
    return values.astype(jnp.bfloat16)


def local_plane(
    hidden,
    cotangent,
    segments,
    padding,
    routes,
    order,
    norm1_gain,
    w_query,
    w_key,
    w_value,
    w_out,
    norm2_gain,
    router,
    shared_gate_vec,
    shared_w_gate,
    shared_w_up,
    shared_w_down,
    expert_w_gate,
    expert_w_up,
    expert_w_down,
):
    plane = lax.axis_size(PLANE)
    groups = lax.axis_size(EXP)
    halves = lax.axis_size(CTX)
    depth = lax.axis_size(DP)
    me = lax.axis_index(PLANE)
    core = lax.axis_index(CTX)
    tokens, width = hidden.shape[1], hidden.shape[2]
    all_tokens = plane * tokens
    seq_len = halves * tokens
    experts_all = router.shape[1]
    head_cols = width // plane
    shard = width // depth

    token_info = jnp.concatenate(
        [segments + 1, jnp.where(padding > 0, segments + 1, 0), order[0], routes[0].T]
    )
    info_rows = token_info.shape[0]
    token_info = jnp.concatenate([token_info, jnp.zeros((8 - info_rows, tokens), jnp.int32)])

    hidden_all, info_all = plane_gather(hidden[0], token_info, False, 0)
    hidden_all = hidden_all.reshape(all_tokens, width)
    place = lax.axis_index(EXP)
    away = [(place ^ k) * 2 + (core ^ j) for j in (0, 1) for k in range(4)]
    away = jnp.stack(away)
    w_qkv_part = jnp.concatenate(
        [
            lax.dynamic_slice(w, (0, me * head_cols), (shard, head_cols))
            for w in (w_query, w_key, w_value)
        ]
        + [router, norm1_gain[:, None], norm2_gain[:, None], shared_gate_vec[:, None]]
        + [jnp.zeros((shard, 128 - experts_all - 3), jnp.bfloat16)],
        axis=1,
    )
    w_qkv = lax.all_gather(w_qkv_part, DP, axis=0, tiled=True)
    small = w_qkv[:, 3 * head_cols :].T
    w_qkv = w_qkv[:, : 3 * head_cols]
    router_t = small[:experts_all]
    g_one = small[experts_all].astype(jnp.float32)
    g_two = small[experts_all + 1].astype(jnp.float32)
    gate_vec = small[experts_all + 2]
    out_rows = shard // plane
    w_out_part = lax.dynamic_slice(w_out, (me * out_rows, 0), (out_rows, width))
    w_out_part = lax.all_gather(w_out_part, DP, axis=0, tiled=False)
    w_out_part = after(w_out_part, info_all)
    w_out_got = [swap(w_out_part, k) for k in (1, 2, 3)]

    def normed(values, gain):
        values = values.astype(jnp.float32)
        inv = lax.rsqrt(jnp.mean(values * values, axis=1, keepdims=True) + EPS)
        return values, inv, low(values * inv * gain)

    n1_all, qkv = norm_qkv(hidden_all, g_one[None], w_qkv, tokens)
    q_codes = info_all[:, 0].reshape(all_tokens, 1)
    k_codes = info_all[:, 1].reshape(all_tokens // seq_len, 1, seq_len)
    attended_cols = attention_call(qkv, None, q_codes, k_codes, seq_len)
    pieces = [w_out_part] + [after(v, attended_cols) for v in w_out_got]
    w_out_near = jnp.zeros((depth, groups, 1, out_rows, width), jnp.bfloat16)
    for k in range(4):
        w_out_near = lax.dynamic_update_slice(
            w_out_near, pieces[k][:, None, None], (0, place ^ k, 0, 0, 0)
        )
    w_out_far = twin(w_out_near)
    w_out_full = jnp.where(
        core == 0,
        jnp.concatenate([w_out_near, w_out_far], axis=2),
        jnp.concatenate([w_out_far, w_out_near], axis=2),
    ).reshape(width, width)

    x_rows, inv_one, _ = normed(hidden[0], g_one)
    cot_rows = cotangent[0].astype(jnp.float32)

    def to_tokens(cols):
        got = lax.all_to_all(
            cols.reshape(plane, tokens, head_cols), PLANE, split_axis=0, concat_axis=0, tiled=True
        )
        return got.transpose(1, 0, 2).reshape(tokens, width)

    def to_columns(rows_in):
        send = rows_in.reshape(tokens, plane, head_cols).transpose(1, 0, 2)
        got = lax.all_to_all(send, PLANE, split_axis=0, concat_axis=0, tiled=True)
        return got.reshape(all_tokens, head_cols)

    attended = to_tokens(attended_cols)
    residual = x_rows + mm(attended, w_out_full)
    residual, inv_two, n2 = normed(residual, g_two)

    units = shared_w_gate.shape[1]
    part = units // (depth * halves)
    pick = lambda w: lax.dynamic_index_in_dim(
        w.reshape(w.shape[0], depth, halves, part), core, axis=2, keepdims=False
    ).reshape(w.shape[0], depth * part)
    sh_gate = lax.all_gather(pick(shared_w_gate), DP, axis=0, tiled=True)
    sh_up = lax.all_gather(pick(shared_w_up), DP, axis=0, tiled=True)
    sh_gate_t, sh_up_t = sh_gate.T, sh_up.T
    sh_down = lax.all_gather(
        lax.dynamic_slice(shared_w_down, (core * part, 0), (part, width)), DP, axis=0, tiled=True
    )
    n2 = after(n2, (sh_gate, sh_up))
    n2_all = plane_gather(n2, None, True, 2)[0].reshape(all_tokens, width)
    cot_own = after(cotangent[0], n2_all)
    cot_got = [swap(cot_own, k) for k in (1, 2, 3)]
    ex_gate = lax.all_gather(after(expert_w_gate[0], info_all), DP, axis=0, tiled=True)
    ex_up = lax.all_gather(after(expert_w_up[0], info_all), DP, axis=0, tiled=True)
    ex_down = lax.all_gather(after(expert_w_down[0], info_all), DP, axis=1, tiled=True)

    small_w = jnp.concatenate([router_t, gate_vec[None]])

    def gates_of(rows_in):
        both = mm(rows_in, small_w, ((1,), (1,)))
        z = both[:, :experts_all]
        e = jnp.exp(z - jnp.max(z, axis=1, keepdims=True))
        return e / jnp.sum(e, axis=1, keepdims=True), jax.nn.sigmoid(both[:, experts_all:])

    probs_all, sg_all = gates_of(n2_all)
    expert_gate = lax.dynamic_slice(probs_all, (0, me), (all_tokens, 1))

    capacity = (9 * tokens * TOP + 8 * experts_all - 1) // (8 * experts_all)
    info_away = info_all[away]
    order_all = info_away[:, 2]
    routed_here = jnp.any(info_away[:, 3 : 3 + TOP] == me, axis=1)
    earlier = (order_all[:, None, :] < order_all[:, :, None]) & routed_here[:, None, :]
    slots = jnp.sum(earlier.astype(jnp.int32), axis=2)
    slots = jnp.where(routed_here, slots, capacity)
    chosen = slots[:, None, :] == jnp.arange(capacity, dtype=jnp.int32)[None, :, None]
    onehot = chosen.astype(jnp.bfloat16)

    def rows_of(values):
        got = lax.dot_general(
            onehot,
            values.reshape(plane, tokens, width),
            (((2,), (1,)), ((0,), (0,))),
            preferred_element_type=jnp.float32,
        )
        return got.reshape(plane * capacity, width)

    slot_gates = jnp.sum(
        jnp.where(chosen, expert_gate.reshape(plane, 1, tokens), 0.0), axis=2
    ).reshape(plane * capacity, 1)
    expert_rows = low(rows_of(n2_all))
    gate_pre = mm(sh_gate_t, n2_all, ((1,), (1,)))
    up_pre = mm(sh_up_t, n2_all, ((1,), (1,)))
    gate_act = gate_pre * jax.nn.sigmoid(gate_pre)
    shared_hidden = low(gate_act * up_pre)
    expert_rows = after(expert_rows, (shared_hidden, sh_down))
    gate_e = mm(expert_rows, ex_gate)
    up_e = mm(expert_rows, ex_up)
    act_e = gate_e * jax.nn.sigmoid(gate_e)
    hidden_e = low(act_e * up_e)
    cot_near = jnp.concatenate([cot_own] + [after(v, gate_e) for v in cot_got])
    cot_all = jnp.concatenate([cot_near, twin(cot_near)])
    row_cots = low(rows_of(cot_all))
    row_grads = low(row_cots.astype(jnp.float32) * slot_gates)

    shared_grads = low(sg_all * cot_all.astype(jnp.float32))
    shared_hgrad = mm(sh_down, shared_grads, ((1,), (1,)))
    gate_grad_s = low(shared_hgrad * up_pre * silu_grad(gate_pre))
    up_grad_s = low(shared_hgrad * gate_act)
    rows_out = width // (halves * depth)

    def shared_scatter(total):
        first, second = total[:, :rows_out], total[:, rows_out:]
        keep = jnp.where(core == 0, first, second)
        got = twin(jnp.where(core == 0, second, first))
        both = jnp.where(core == 0, jnp.stack([keep, got]), jnp.stack([got, keep]))
        both = both.reshape(halves, depth, part, rows_out).transpose(1, 0, 2, 3)
        return both.reshape(units, rows_out).astype(jnp.float32)

    scatter = lambda v, dim: lax.psum_scatter(v, DP, scatter_dimension=dim, tiled=True)
    level = lax.axis_index(DP)
    made = [
        unit_grads(left, right, depth, halves)
        for left, right in (
            (shared_hidden, shared_grads),
            (gate_grad_s, n2_all),
            (up_grad_s, n2_all),
        )
    ]
    for_level = lambda k: jnp.concatenate(
        [lax.dynamic_index_in_dim(v, level ^ k, axis=0, keepdims=False) for v in made]
    )
    shared_sums = [for_level(0)] + [
        lax.ppermute(for_level(k), DP, [(i, i ^ k) for i in range(4)]) for k in (1, 2, 3)
    ]
    result_e = low(mm(hidden_e, ex_down))
    hgrad_e = mm(row_grads, ex_down, ((1,), (1,)))
    gate_grad_e = low(hgrad_e * up_e * silu_grad(gate_e))
    up_grad_e = low(hgrad_e * act_e)

    grad_ex_down = low(mm(hidden_e, row_grads, ((0,), (0,))))
    grad_ex_gate = low(mm(expert_rows, gate_grad_e, ((0,), (0,))))
    grad_ex_up = low(mm(expert_rows, up_grad_e, ((0,), (0,))))
    grads_made = (grad_ex_down, grad_ex_gate, grad_ex_up)
    grads = [scatter(v, dim) for v, dim in zip(grads_made, (1, 0, 0))]
    slots = slots.reshape(all_tokens, 1)
    out_near, dots = output_parts(
        shared_hidden,
        sh_down,
        result_e.reshape(plane, capacity, width),
        after(slots, grads_made),
        sg_all,
        expert_gate,
        cot_all,
    )
    rows_grad = low(
        mm(gate_grad_e, ex_gate, ((1,), (1,))) + mm(up_grad_e, ex_up, ((1,), (1,)))
    )

    n2_grad = n2_grad_sum(
        gate_grad_s,
        up_grad_s,
        sh_gate_t,
        sh_up_t,
        rows_grad.reshape(plane, capacity, width),
        slots,
    )
    out_near = after(out_near, n2_grad)
    out_got = hops([out_near[k] for k in range(4)])

    dots = dots.reshape(plane, tokens, 128)[:, :, :2].transpose(0, 2, 1)
    back = jnp.arange(plane, dtype=jnp.int32) ^ me
    dots = dots[(back // 2) + 4 * (back % 2)]
    dots = lax.all_to_all(dots, PLANE, split_axis=0, concat_axis=0, tiled=True)
    probs_grad = dots[:, 0].T
    probs, sg = gates_of(n2)
    logit_grad = low(probs * (probs_grad - jnp.sum(probs * probs_grad, axis=1, keepdims=True)))
    sg_logit_grad = low(jnp.sum(dots[:, 1], axis=0)[:, None] * sg * (1.0 - sg))
    small_grads = mm(n2, jnp.concatenate([logit_grad, sg_logit_grad], axis=1), ((0,), (0,)))
    n2_grad = (
        n2_grad
        + mm(logit_grad, router_t)
        + sg_logit_grad.astype(jnp.float32) * gate_vec.astype(jnp.float32)[None]
    )
    residual_grad, grad_gain_two = norm_back(residual, inv_two, g_two, n2_grad)
    residual_grad = residual_grad + cot_rows
    low_residual = low(residual_grad)

    small_grads = jnp.concatenate([small_grads, grad_gain_two[:, None]], axis=1).T
    small_grads = jnp.pad(small_grads, ((0, 14 - experts_all), (0, 0)))
    small_grads = small_grads.reshape(16, plane, width // plane).transpose(1, 0, 2)
    small_grads = jnp.sum(
        lax.all_to_all(small_grads, PLANE, split_axis=0, concat_axis=0, tiled=True), axis=0
    )
    small_grads = small_grads.reshape(16, depth, shard // plane).transpose(1, 0, 2)
    small_grads = jnp.sum(
        lax.all_to_all(small_grads, DP, split_axis=0, concat_axis=0, tiled=True), axis=0
    )
    grad_out = low(mm(attended, low_residual, ((0,), (0,))))
    grad_out = grad_out.reshape(groups, halves, width // plane, width)
    block_of = lambda k, c: lax.dynamic_slice(
        grad_out, (place ^ k, c, 0, 0), (1, 1, width // plane, width)
    )[0, 0]
    attended_grad = to_columns(low(mm(low_residual, w_out_full, ((1,), (1,)))))
    out_grad_sums = twin_sums(
        [block_of(k, core) for k in range(4)],
        jnp.stack([block_of(k, 1 - core) for k in range(4)]),
    )
    shared_sums = low(sum_up(after(shared_sums, low_residual)))
    grad_sh_down, grad_sh_gate, grad_sh_up = [
        shared_scatter(v) for v in shared_sums.reshape(3, units // halves, -1)
    ]
    grad_sh_gate, grad_sh_up = grad_sh_gate.T, grad_sh_up.T
    attended_grad = after(
        attended_grad,
        (out_grad_sums, grads[0], small_grads, grad_sh_down, grad_sh_gate, grad_sh_up),
    )
    qkv_grad = attention_call(qkv, attended_grad, q_codes, k_codes, seq_len)
    qkv_grad, grad_out = lax.optimization_barrier((qkv_grad, hops(out_grad_sums)))
    grad_out = low(sum_up(grad_out))
    grad_qkv = low(mm(n1_all, qkv_grad, ((0,), (0,))))
    fine = shard // plane
    grad_qkv = (
        grad_qkv.reshape(plane, depth, fine, 3 * head_cols)
        .transpose(1, 0, 2, 3)
        .reshape(width, 3 * head_cols)
    )
    n1_grad = low(mm(after(qkv_grad, grad_qkv), w_qkv, ((1,), (1,))))
    grad_ex_down, grad_ex_gate = [v.astype(jnp.float32)[None] for v in grads[:2]]
    n1_grad = after(n1_grad, (grad_qkv, grad_out, grad_ex_down, grad_ex_gate))
    grad_out = lax.psum_scatter(grad_out, DP, scatter_dimension=0, tiled=True)
    n1_grad = plane_scatter(n1_grad.reshape(plane, tokens, width), False, 1, jnp.float32)[0]
    grad_qkv = lax.psum_scatter(grad_qkv, DP, scatter_dimension=0, tiled=True)
    w_rows = (
        w_qkv.reshape(plane, depth, fine, 3 * head_cols)
        .transpose(1, 0, 2, 3)
        .reshape(depth, plane * fine, 3 * head_cols)
    )
    w_rows = lax.dynamic_index_in_dim(w_rows, lax.axis_index(DP), axis=0, keepdims=False)
    gain_dots = jnp.sum(grad_qkv.astype(jnp.float32) * w_rows.astype(jnp.float32), axis=1)
    gain_dots = lax.all_to_all(
        gain_dots.reshape(plane, 1, fine), PLANE, split_axis=0, concat_axis=0, tiled=True
    )
    my_gain = lax.dynamic_slice(
        g_one, ((me * depth + lax.axis_index(DP)) * fine,), (fine,)
    )
    grad_gain_one = jnp.sum(gain_dots[:, 0], axis=0) / my_gain
    grad_qkv = lax.all_to_all(
        grad_qkv.reshape(plane, fine, 3 * head_cols),
        PLANE,
        split_axis=0,
        concat_axis=0,
        tiled=True,
    )
    grad_qkv = (
        grad_qkv.reshape(plane, fine, 3, head_cols)
        .transpose(2, 1, 0, 3)
        .reshape(3, fine, width)
        .astype(jnp.float32)
    )
    grad_out = after(grad_out, n1_grad).astype(jnp.float32)
    grad_ex_up = after(grads[2], n1_grad).astype(jnp.float32)[None]
    output = low(residual + sum_up(after(out_got, n1_grad)))
    input_part, _ = norm_back(x_rows, inv_one, g_one, n1_grad)
    input_grad = low(residual_grad + input_part)
    return (
        output[None],
        input_grad[None],
        grad_gain_one,
        grad_qkv[0],
        grad_qkv[1],
        grad_qkv[2],
        grad_out,
        small_grads[experts_all + 1],
        small_grads[:experts_all].T,
        small_grads[experts_all],
        grad_sh_gate,
        grad_sh_up,
        grad_sh_down,
        grad_ex_gate,
        grad_ex_up,
        grad_ex_down,
    )


def solution(mesh):
    in_specs = (
        P((EXP, DP), CTX, None),
        P((EXP, DP), CTX, None),
        P((EXP, DP), CTX),
        P((EXP, DP), CTX),
        P((EXP, DP), CTX, None),
        P((EXP, DP), CTX, None),
        P(DP),
        P(DP, None),
        P(DP, None),
        P(DP, None),
        P(DP, None),
        P(DP),
        P(DP, None),
        P(DP),
        P(DP, EXP),
        P(DP, EXP),
        P((EXP, DP), None),
        P((EXP, CTX), DP, None),
        P((EXP, CTX), DP, None),
        P((EXP, CTX), None, DP),
    )
    out_specs = (
        P((EXP, DP), CTX, None),
        P((EXP, DP), CTX, None),
        P((EXP, CTX, DP)),
        P((EXP, CTX, DP), None),
        P((EXP, CTX, DP), None),
        P((EXP, CTX, DP), None),
        P((EXP, CTX, DP), None),
        P((EXP, CTX, DP)),
        P((EXP, CTX, DP), None),
        P((EXP, CTX, DP)),
        P((CTX, DP), EXP),
        P((CTX, DP), EXP),
        P(EXP, (CTX, DP)),
        P((EXP, CTX), DP, None),
        P((EXP, CTX), DP, None),
        P((EXP, CTX), None, DP),
    )
    plane = mesh.shape[EXP] * mesh.shape[CTX]

    def run(*args):
        square = mesh.shape[EXP] == 4 and mesh.shape[CTX] == 2 and mesh.shape[DP] == 4
        one_each = square and args[12].shape[1] == plane
        local = local_plane if one_each else local_general
        return jax.shard_map(
            local, mesh=mesh, in_specs=in_specs, out_specs=out_specs, check_vma=False
        )(*args)

    return run
```

```python
from functools import partial

import jax
import jax.numpy as jnp
from jax import lax
from jax.experimental import pallas as pl
from jax.experimental.pallas import tpu as pltpu
from jax.sharding import PartitionSpec as P

EXP, CTX, DP = "experts", "context", "dp"
PLANE = (EXP, CTX)
HEADS = 16
HEAD_DIM = 128
TOP = 4


EPS = 1e-06
NEG = -1e30


def silu_grad(pre_act):
    logistic = jax.nn.sigmoid(pre_act)
    return logistic * (1.0 + pre_act * (1.0 - logistic))


def block_slots(route_row, priority, expert_count):
    matches = (route_row[:, None] == jnp.arange(expert_count, dtype=jnp.int32)[None, :]).astype(
        jnp.int32
    )
    ordered = jnp.zeros_like(matches).at[priority].set(matches)
    before = jnp.cumsum(ordered, axis=0) - ordered
    return jnp.sum(before[priority] * matches, axis=1)


def norm_back(values_in, inv_rms, gain_vec, gradient):
    weighted = gradient * gain_vec
    inner_sum = jnp.mean(weighted * values_in, axis=1, keepdims=True)
    d_value = inv_rms * weighted - values_in * inv_rms**3 * inner_sum
    d_gain = jnp.sum(gradient * values_in * inv_rms, axis=0)
    return (d_value, d_gain)


def attend_head(packed, allowed, scale_factor):
    query_h, key_h, value_h = packed
    raw_scores = jnp.einsum("th,lh->tl", query_h, key_h, preferred_element_type=jnp.float32)
    logits = jnp.where(allowed, raw_scores * scale_factor, NEG)
    row_max = jnp.max(logits, axis=1, keepdims=True)
    exp_scores = jnp.exp(logits - row_max)
    row_total = jnp.sum(exp_scores, axis=1, keepdims=True)
    attn_probs = (exp_scores / row_total).astype(jnp.bfloat16)
    head_out = jnp.dot(attn_probs, value_h, preferred_element_type=jnp.float32).astype(jnp.bfloat16)
    return (head_out, row_max + jnp.log(row_total))


def attend_back(packed, allowed, scale_factor):
    query_h, key_h, value_h, out_grad, log_total = packed
    raw_scores = jnp.einsum("th,lh->tl", query_h, key_h, preferred_element_type=jnp.float32)
    logits = jnp.where(allowed, raw_scores * scale_factor, NEG)
    attn_probs = jnp.exp(logits - log_total)
    prob_grad = jnp.einsum("th,lh->tl", out_grad, value_h, preferred_element_type=jnp.float32)
    inner_sum = jnp.sum(attn_probs * prob_grad, axis=1, keepdims=True)
    score_grad = (attn_probs * (prob_grad - inner_sum) * scale_factor).astype(jnp.bfloat16)
    query_grad = jnp.dot(score_grad, key_h, preferred_element_type=jnp.float32)
    key_grad = jnp.einsum("tl,th->lh", score_grad, query_h, preferred_element_type=jnp.float32)
    value_grad = jnp.einsum(
        "tl,th->lh", attn_probs.astype(jnp.bfloat16), out_grad, preferred_element_type=jnp.float32
    )
    return (query_grad, key_grad, value_grad)


def local_general(
    hidden,
    cotangent,
    segments,
    padding,
    routes,
    order,
    norm1_gain,
    w_query,
    w_key,
    w_value,
    w_out,
    norm2_gain,
    router,
    shared_gate_vec,
    shared_w_gate,
    shared_w_up,
    shared_w_down,
    expert_w_gate,
    expert_w_up,
    expert_w_down,
):
    fetched = (
        lax.all_gather(norm1_gain, DP, axis=0, tiled=True),
        lax.all_gather(w_query, DP, axis=0, tiled=True),
        lax.all_gather(w_key, DP, axis=0, tiled=True),
        lax.all_gather(w_value, DP, axis=0, tiled=True),
        lax.all_gather(w_out, DP, axis=0, tiled=True),
        lax.all_gather(norm2_gain, DP, axis=0, tiled=True),
        lax.all_gather(router, DP, axis=0, tiled=True),
        lax.all_gather(shared_gate_vec, DP, axis=0, tiled=True),
        lax.all_gather(shared_w_gate, DP, axis=0, tiled=True),
        lax.all_gather(shared_w_up, DP, axis=0, tiled=True),
        lax.all_gather(shared_w_down, DP, axis=0, tiled=True),
        lax.all_gather(expert_w_gate, DP, axis=1, tiled=True),
        lax.all_gather(expert_w_up, DP, axis=1, tiled=True),
        lax.all_gather(expert_w_down, DP, axis=2, tiled=True),
    )
    (
        gain_one,
        query_w,
        key_w,
        value_w,
        out_w,
        gain_two,
        router_full,
        gate_vec,
        sh_gate,
        sh_up,
        sh_down,
        ex_gate,
        ex_up,
        ex_down,
    ) = fetched
    sh_gate, sh_up, sh_down = (
        lax.all_gather(sh_gate, EXP, axis=1, tiled=True),
        lax.all_gather(sh_up, EXP, axis=1, tiled=True),
        lax.all_gather(sh_down, EXP, axis=0, tiled=True),
    )
    tokens_here = hidden.shape[1]
    model_width = hidden.shape[2]
    x_rows = hidden[0].astype(jnp.float32)
    cot_rows = cotangent[0].astype(jnp.float32)
    inv_one = lax.rsqrt(jnp.mean(x_rows * x_rows, axis=1, keepdims=True) + EPS)
    g_one = gain_one.astype(jnp.float32)
    normed_one = (x_rows * inv_one * g_one).astype(jnp.bfloat16)
    queries = jnp.dot(normed_one, query_w, preferred_element_type=jnp.float32).astype(jnp.bfloat16)
    keys_own = jnp.dot(normed_one, key_w, preferred_element_type=jnp.float32).astype(jnp.bfloat16)
    values_own = jnp.dot(normed_one, value_w, preferred_element_type=jnp.float32).astype(
        jnp.bfloat16
    )
    own_codes = jnp.where(padding[0] > 0, segments[0] + 1, 0)
    code_parts = jnp.stack([own_codes // 64, own_codes % 64]).astype(jnp.bfloat16)
    keys_all, values_all, parts_all = (
        lax.all_gather(keys_own, CTX, axis=0, tiled=True),
        lax.all_gather(values_own, CTX, axis=0, tiled=True),
        lax.all_gather(code_parts, CTX, axis=1, tiled=True),
    )
    key_codes = parts_all[0].astype(jnp.int32) * 64 + parts_all[1].astype(jnp.int32)
    seq_total = keys_all.shape[0]
    query_pos = lax.axis_index(CTX) * tokens_here + jnp.arange(tokens_here, dtype=jnp.int32)
    key_pos = jnp.arange(seq_total, dtype=jnp.int32)
    same_doc = key_codes[None, :] == (segments[0] + 1)[:, None]
    allowed = (key_pos[None, :] <= query_pos[:, None]) & (
        same_doc | (key_pos[None, :] == query_pos[:, None])
    )
    scale_factor = HEAD_DIM ** (-0.5)

    def to_heads(rows_in):
        return rows_in.reshape(rows_in.shape[0], HEADS, HEAD_DIM).transpose(1, 0, 2)

    def from_heads(heads_in):
        return heads_in.transpose(1, 0, 2).reshape(heads_in.shape[1], model_width)

    head_q = to_heads(queries)
    head_k = to_heads(keys_all)
    head_v = to_heads(values_all)
    head_out, log_total = lax.map(
        partial(attend_head, allowed=allowed, scale_factor=scale_factor), (head_q, head_k, head_v)
    )
    attended = from_heads(head_out)
    residual = x_rows + jnp.dot(attended, out_w, preferred_element_type=jnp.float32)
    inv_two = lax.rsqrt(jnp.mean(residual * residual, axis=1, keepdims=True) + EPS)
    g_two = gain_two.astype(jnp.float32)
    normed_two = (residual * inv_two * g_two).astype(jnp.bfloat16)
    router_logits = jnp.dot(normed_two, router_full, preferred_element_type=jnp.float32)
    router_exp = jnp.exp(router_logits - jnp.max(router_logits, axis=1, keepdims=True))
    router_probs = router_exp / jnp.sum(router_exp, axis=1, keepdims=True)
    route_gates = jnp.take_along_axis(router_probs, routes[0], axis=1)
    shared_gate = jax.nn.sigmoid(jnp.dot(normed_two, gate_vec, preferred_element_type=jnp.float32))
    shared_scaled = (shared_gate[:, None] * cot_rows).astype(jnp.bfloat16)
    rows_group, grads_group = (normed_two, shared_scaled)
    gate_pre = jnp.dot(rows_group, sh_gate, preferred_element_type=jnp.float32)
    up_pre = jnp.dot(rows_group, sh_up, preferred_element_type=jnp.float32)
    gate_act = gate_pre * jax.nn.sigmoid(gate_pre)
    shared_hidden = (gate_act * up_pre).astype(jnp.bfloat16)
    shared_part = jnp.dot(shared_hidden, sh_down, preferred_element_type=jnp.float32)
    experts_all = router_full.shape[1]
    capacity = (9 * tokens_here * TOP + 8 * experts_all - 1) // (8 * experts_all)
    priority = (order[0, 0][:, None] * TOP + jnp.arange(TOP, dtype=jnp.int32)[None, :]).reshape(-1)
    flat_routes = routes[0].reshape(-1)
    slot_index = block_slots(flat_routes, priority, experts_all)
    kept_rows = slot_index < capacity
    target = flat_routes * capacity + jnp.minimum(slot_index, capacity - 1)
    row_gates = route_gates.reshape(-1)
    cot_repeated = jnp.repeat(cot_rows, TOP, axis=0)
    source_rows = jnp.repeat(normed_two, TOP, axis=0)
    source_grads = (cot_repeated * row_gates[:, None]).astype(jnp.bfloat16)
    empty_slots = jnp.zeros((experts_all * capacity, model_width), jnp.bfloat16)
    send_rows = empty_slots.at[target].add(
        jnp.where(kept_rows[:, None], source_rows, jnp.zeros_like(source_rows))
    )
    send_grads = empty_slots.at[target].add(
        jnp.where(kept_rows[:, None], source_grads, jnp.zeros_like(source_grads))
    )
    recv_rows, recv_grads = (
        lax.all_to_all(
            send_rows.reshape(experts_all, capacity, model_width),
            (EXP, CTX),
            split_axis=0,
            concat_axis=0,
            tiled=True,
        ),
        lax.all_to_all(
            send_grads.reshape(experts_all, capacity, model_width),
            (EXP, CTX),
            split_axis=0,
            concat_axis=0,
            tiled=True,
        ),
    )
    local_count = ex_gate.shape[0]
    sources = experts_all // local_count

    def to_local(buffer_in):
        return (
            buffer_in.reshape(sources, local_count, capacity, model_width)
            .transpose(1, 0, 2, 3)
            .reshape(local_count, sources * capacity, model_width)
        )

    def to_owner(buffer_in):
        return (
            buffer_in.reshape(local_count, sources, capacity, model_width)
            .transpose(1, 0, 2, 3)
            .reshape(experts_all, capacity, model_width)
        )

    expert_rows = to_local(recv_rows)
    expert_grads_in = to_local(recv_grads)
    gate_e = jnp.einsum("erd,edf->erf", expert_rows, ex_gate, preferred_element_type=jnp.float32)
    up_e = jnp.einsum("erd,edf->erf", expert_rows, ex_up, preferred_element_type=jnp.float32)
    act_e = gate_e * jax.nn.sigmoid(gate_e)
    hidden_e = (act_e * up_e).astype(jnp.bfloat16)
    result_e = jnp.einsum(
        "erf,efd->erd", hidden_e, ex_down, preferred_element_type=jnp.float32
    ).astype(jnp.bfloat16)
    returned = lax.all_to_all(
        to_owner(result_e), (EXP, CTX), split_axis=0, concat_axis=0, tiled=True
    )
    picked = returned.reshape(experts_all * capacity, model_width)[target]
    picked = jnp.where(kept_rows[:, None], picked, jnp.zeros_like(picked)).astype(jnp.float32)
    routed = jnp.sum((picked * row_gates[:, None]).reshape(tokens_here, TOP, model_width), axis=1)
    output = (residual + shared_gate[:, None] * shared_part + routed).astype(jnp.bfloat16)
    gate_grads = jnp.sum(picked * cot_repeated, axis=1).reshape(tokens_here, TOP)
    hidden_grad_e = jnp.einsum(
        "erd,efd->erf", expert_grads_in, ex_down, preferred_element_type=jnp.float32
    )
    gate_grad_e = (hidden_grad_e * up_e * silu_grad(gate_e)).astype(jnp.bfloat16)
    up_grad_e = (hidden_grad_e * act_e).astype(jnp.bfloat16)
    grad_ex_down = jnp.einsum(
        "erf,erd->efd", hidden_e, expert_grads_in, preferred_element_type=jnp.float32
    )
    grad_ex_gate = jnp.einsum(
        "erd,erf->edf", expert_rows, gate_grad_e, preferred_element_type=jnp.float32
    )
    grad_ex_up = jnp.einsum(
        "erd,erf->edf", expert_rows, up_grad_e, preferred_element_type=jnp.float32
    )
    expert_sums = (
        lax.psum_scatter(grad_ex_gate, DP, scatter_dimension=1, tiled=True),
        lax.psum_scatter(grad_ex_up, DP, scatter_dimension=1, tiled=True),
        lax.psum_scatter(grad_ex_down, DP, scatter_dimension=2, tiled=True),
    )
    rows_grad_e = jnp.einsum(
        "erf,edf->erd", gate_grad_e, ex_gate, preferred_element_type=jnp.float32
    )
    rows_grad_e = (
        rows_grad_e
        + jnp.einsum("erf,edf->erd", up_grad_e, ex_up, preferred_element_type=jnp.float32)
    ).astype(jnp.bfloat16)
    returned_grads = lax.all_to_all(
        to_owner(rows_grad_e), (EXP, CTX), split_axis=0, concat_axis=0, tiled=True
    )
    routed_grad = returned_grads.reshape(experts_all * capacity, model_width)[target]
    routed_grad = jnp.where(kept_rows[:, None], routed_grad, jnp.zeros_like(routed_grad)).astype(
        jnp.float32
    )
    norm_grad = jnp.sum(routed_grad.reshape(tokens_here, TOP, model_width), axis=1)
    choose = (
        routes[0][:, :, None] == jnp.arange(experts_all, dtype=jnp.int32)[None, None, :]
    ).astype(jnp.float32)
    probs_grad = jnp.einsum("tk,tke->te", gate_grads, choose)
    logit_grad = (
        router_probs * (probs_grad - jnp.sum(router_probs * probs_grad, axis=1, keepdims=True))
    ).astype(jnp.bfloat16)
    grad_router = jnp.dot(normed_two.T, logit_grad, preferred_element_type=jnp.float32)
    gate_logit_grad = (
        jnp.sum(cot_rows * shared_part, axis=1) * shared_gate * (1.0 - shared_gate)
    ).astype(jnp.bfloat16)
    grad_gate_vec = jnp.dot(gate_logit_grad, normed_two, preferred_element_type=jnp.float32)
    norm_grad = norm_grad + jnp.dot(logit_grad, router_full.T, preferred_element_type=jnp.float32)
    norm_grad = (
        norm_grad
        + gate_logit_grad.astype(jnp.float32)[:, None] * gate_vec.astype(jnp.float32)[None, :]
    )
    shared_hgrad = jnp.dot(grads_group, sh_down.T, preferred_element_type=jnp.float32)
    gate_grad_s = (shared_hgrad * up_pre * silu_grad(gate_pre)).astype(jnp.bfloat16)
    up_grad_s = (shared_hgrad * gate_act).astype(jnp.bfloat16)
    shared_rows_grad = jnp.dot(gate_grad_s, sh_gate.T, preferred_element_type=jnp.float32)
    shared_rows_grad = shared_rows_grad + jnp.dot(
        up_grad_s, sh_up.T, preferred_element_type=jnp.float32
    )
    groups = lax.axis_size(EXP)
    parts_cd = lax.axis_size((CTX, DP))
    rows_count = rows_group.shape[0]
    arr_gate = jnp.einsum(
        "td,tes->eds",
        rows_group,
        gate_grad_s.reshape(rows_count, groups, -1),
        preferred_element_type=jnp.float32,
    ).reshape(groups * model_width, -1)
    arr_up = jnp.einsum(
        "td,tes->eds",
        rows_group,
        up_grad_s.reshape(rows_count, groups, -1),
        preferred_element_type=jnp.float32,
    ).reshape(groups * model_width, -1)
    arr_down = jnp.einsum(
        "tes,tcd->ecsd",
        shared_hidden.reshape(rows_count, groups, -1),
        grads_group.reshape(rows_count, parts_cd, -1),
        preferred_element_type=jnp.float32,
    ).reshape(-1, model_width // parts_cd)
    sums_gate, sums_up, sums_down = (
        lax.psum_scatter(arr_gate, (EXP, CTX, DP), scatter_dimension=0, tiled=True),
        lax.psum_scatter(arr_up, (EXP, CTX, DP), scatter_dimension=0, tiled=True),
        lax.psum_scatter(arr_down, (EXP, CTX, DP), scatter_dimension=0, tiled=True),
    )
    norm_grad = norm_grad + shared_rows_grad
    residual_grad, grad_gain_two = norm_back(residual, inv_two, g_two, norm_grad)
    residual_grad = residual_grad + cot_rows
    low_residual = residual_grad.astype(jnp.bfloat16)
    grad_out_w = jnp.dot(attended.T, low_residual, preferred_element_type=jnp.float32)
    attended_grad = jnp.dot(low_residual, out_w.T, preferred_element_type=jnp.float32).astype(
        jnp.bfloat16
    )
    head_q_grad, head_k_grad, head_v_grad = lax.map(
        partial(attend_back, allowed=allowed, scale_factor=scale_factor),
        (head_q, head_k, head_v, to_heads(attended_grad), log_total),
    )
    key_sum, value_sum = (
        lax.psum_scatter(from_heads(head_k_grad), CTX, scatter_dimension=0, tiled=True),
        lax.psum_scatter(from_heads(head_v_grad), CTX, scatter_dimension=0, tiled=True),
    )
    query_low = from_heads(head_q_grad).astype(jnp.bfloat16)
    key_low = key_sum.astype(jnp.bfloat16)
    value_low = value_sum.astype(jnp.bfloat16)
    grad_query = jnp.dot(normed_one.T, query_low, preferred_element_type=jnp.float32)
    grad_key = jnp.dot(normed_one.T, key_low, preferred_element_type=jnp.float32)
    grad_value = jnp.dot(normed_one.T, value_low, preferred_element_type=jnp.float32)
    normed_grad = jnp.dot(query_low, query_w.T, preferred_element_type=jnp.float32)
    normed_grad = normed_grad + jnp.dot(key_low, key_w.T, preferred_element_type=jnp.float32)
    normed_grad = normed_grad + jnp.dot(value_low, value_w.T, preferred_element_type=jnp.float32)
    input_part, grad_gain_one = norm_back(x_rows, inv_one, g_one, normed_grad)
    input_grad = (residual_grad + input_part).astype(jnp.bfloat16)
    dense = (
        lax.psum_scatter(
            grad_gain_one, (EXP, CTX, DP), scatter_dimension=0, tiled=True
        ),
        lax.psum_scatter(grad_query, (EXP, CTX, DP), scatter_dimension=0, tiled=True),
        lax.psum_scatter(grad_key, (EXP, CTX, DP), scatter_dimension=0, tiled=True),
        lax.psum_scatter(grad_value, (EXP, CTX, DP), scatter_dimension=0, tiled=True),
        lax.psum_scatter(grad_out_w, (EXP, CTX, DP), scatter_dimension=0, tiled=True),
        lax.psum_scatter(
            grad_gain_two, (EXP, CTX, DP), scatter_dimension=0, tiled=True
        ),
        lax.psum_scatter(
            grad_router, (EXP, CTX, DP), scatter_dimension=0, tiled=True
        ),
        lax.psum_scatter(
            grad_gate_vec, (EXP, CTX, DP), scatter_dimension=0, tiled=True
        ),
    )
    return (
        output[None],
        input_grad[None],
        dense[0],
        dense[1],
        dense[2],
        dense[3],
        dense[4],
        dense[5],
        dense[6],
        dense[7],
        sums_gate,
        sums_up,
        sums_down,
        expert_sums[0],
        expert_sums[1],
        expert_sums[2],
    )

def attention_probs(q_blk, k_part, q_code, k_code, first_row, scale_factor):
    scores = lax.dot_general(
        q_blk, k_part, (((1,), (1,)), ((), ())), preferred_element_type=jnp.float32
    )
    row = first_row + lax.broadcasted_iota(jnp.int32, scores.shape, 0)
    col = lax.broadcasted_iota(jnp.int32, scores.shape, 1)
    allowed = ((col < row) & (k_code == q_code)) | (col == row)
    logits = jnp.where(allowed, scores * scale_factor, NEG)
    exp_scores = jnp.exp(logits - jnp.max(logits, axis=1, keepdims=True))
    return exp_scores * (1.0 / jnp.sum(exp_scores, axis=1, keepdims=True))


def attend_kernel(heads, step, qkv_ref, q_code_ref, k_code_ref, out_ref):
    seq_len = qkv_ref.shape[0]
    width = heads * HEAD_DIM
    for head in range(heads):
        at = head * HEAD_DIM
        for first in range(0, seq_len, step):
            upto = first + step
            probs = attention_probs(
                qkv_ref[first:upto, at : at + HEAD_DIM],
                qkv_ref[0:upto, width + at : width + at + HEAD_DIM],
                q_code_ref[first:upto, :],
                k_code_ref[0, :, 0:upto],
                first,
                HEAD_DIM**-0.5,
            )
            out_ref[first:upto, at : at + HEAD_DIM] = jnp.dot(
                probs.astype(jnp.bfloat16),
                qkv_ref[0:upto, 2 * width + at : 2 * width + at + HEAD_DIM],
                preferred_element_type=jnp.float32,
            ).astype(jnp.bfloat16)


def attend_back_kernel(
    heads, step, qkv_ref, grad_ref, q_code_ref, k_code_ref, out_ref, key_acc, value_acc
):
    seq_len = qkv_ref.shape[0]
    width = heads * HEAD_DIM
    for head in range(heads):
        at = head * HEAD_DIM
        key_at, value_at = width + at, 2 * width + at
        key_acc[...] = jnp.zeros_like(key_acc)
        value_acc[...] = jnp.zeros_like(value_acc)
        for first in range(0, seq_len, step):
            upto = first + step
            q_blk = qkv_ref[first:upto, at : at + HEAD_DIM]
            k_part = qkv_ref[0:upto, key_at : key_at + HEAD_DIM]
            v_part = qkv_ref[0:upto, value_at : value_at + HEAD_DIM]
            g_blk = grad_ref[first:upto, at : at + HEAD_DIM]
            probs = attention_probs(
                q_blk,
                k_part,
                q_code_ref[first:upto, :],
                k_code_ref[0, :, 0:upto],
                first,
                HEAD_DIM**-0.5,
            )
            prob_grad = lax.dot_general(
                g_blk, v_part, (((1,), (1,)), ((), ())), preferred_element_type=jnp.float32
            )
            inner = jnp.sum(probs * prob_grad, axis=1, keepdims=True)
            score_grad = (probs * (prob_grad - inner) * HEAD_DIM**-0.5).astype(jnp.bfloat16)
            out_ref[first:upto, at : at + HEAD_DIM] = jnp.dot(
                score_grad, k_part, preferred_element_type=jnp.float32
            ).astype(jnp.bfloat16)
            key_acc[0:upto, :] += lax.dot_general(
                score_grad, q_blk, (((0,), (0,)), ((), ())), preferred_element_type=jnp.float32
            )
            value_acc[0:upto, :] += lax.dot_general(
                probs.astype(jnp.bfloat16),
                g_blk,
                (((0,), (0,)), ((), ())),
                preferred_element_type=jnp.float32,
            )
        out_ref[:, key_at : key_at + HEAD_DIM] = key_acc[...].astype(jnp.bfloat16)
        out_ref[:, value_at : value_at + HEAD_DIM] = value_acc[...].astype(jnp.bfloat16)


def attention_call(qkv, grads, q_codes, k_codes, seq_len):
    rows, triple = qkv.shape
    width = triple // 3
    heads = width // HEAD_DIM
    step = min(256, seq_len)
    specs = [pl.BlockSpec((seq_len, triple), lambda s: (s, 0))]
    operands = [qkv]
    if grads is not None:
        specs.append(pl.BlockSpec((seq_len, width), lambda s: (s, 0)))
        operands.append(grads)
    specs += [
        pl.BlockSpec((seq_len, 1), lambda s: (s, 0)),
        pl.BlockSpec((1, 1, seq_len), lambda s: (s, 0, 0)),
    ]
    operands += [q_codes, k_codes]
    out_width = width if grads is None else triple
    body = attend_kernel if grads is None else attend_back_kernel
    passes = 2 if grads is None else 5
    area = rows * seq_len * heads
    return pl.pallas_call(
        partial(body, heads, step),
        grid=(rows // seq_len,),
        in_specs=specs,
        out_specs=pl.BlockSpec((seq_len, out_width), lambda s: (s, 0)),
        out_shape=jax.ShapeDtypeStruct((rows, out_width), jnp.bfloat16),
        scratch_shapes=[]
        if grads is None
        else [pltpu.VMEM((seq_len, HEAD_DIM), jnp.float32)] * 2,
        compiler_params=pltpu.CompilerParams(vmem_limit_bytes=48 * 2**20),
        cost_estimate=pl.CostEstimate(
            flops=2 * passes * area * HEAD_DIM,
            bytes_accessed=2 * rows * (triple + out_width),
            transcendentals=area,
        ),
    )(*operands)


MESH_ID = pl.DeviceIdType.MESH


def other_in_pair(index, bit):
    return index + bit - 2 * bit * (lax.div(index, bit) % 2)


def plane_places():
    at = lax.axis_index(EXP)
    core = lax.axis_index(CTX)
    across, along = other_in_pair(at, 1), other_in_pair(at, 2)
    return at, core, across, along, other_in_pair(along, 1)


def greet(across, along, core):
    barrier = pltpu.get_barrier_semaphore()
    for target in ({EXP: across}, {EXP: along}, {CTX: 1 - core}):
        pl.semaphore_signal(barrier, inc=1, device_id=target, device_id_type=MESH_ID)
    pl.semaphore_wait(barrier, 3)


def plane_gather_kernel(with_info, relative, *refs):
    if with_info:
        own_ref, info_ref, all_ref, info_all_ref, send_sem, recv_sem, local_sem = refs
    else:
        own_ref, all_ref, send_sem, recv_sem, local_sem = refs
    at, core, across, along, far = plane_places()
    rows = own_ref.shape[0]
    half = rows // 2
    top, bottom, whole = pl.ds(0, half), pl.ds(half, half), pl.ds(0, rows)
    greet(across, along, core)
    started = []
    twin_id = {CTX: 1 - core}

    def slot_of(place, shift, for_twin):
        if relative:
            return shift + 4 * for_twin
        return place * 2 + core

    def send(number, src, dst, target):
        copy = pltpu.make_async_remote_copy(
            src_ref=src,
            dst_ref=dst,
            send_sem=send_sem.at[number],
            recv_sem=recv_sem.at[number],
            device_id=target,
            device_id_type=MESH_ID,
        )
        copy.start()
        started.append(copy)
        return copy

    def piece(place, shift, part, for_twin=0):
        return all_ref.at[slot_of(place, shift, for_twin), part]

    x_top = send(0, own_ref.at[top], piece(at, 1, top), {EXP: across})
    y_bottom = send(1, own_ref.at[bottom], piece(at, 2, bottom), {EXP: along})
    x_bottom = send(2, own_ref.at[bottom], piece(at, 1, bottom), {EXP: across})
    y_top = send(3, own_ref.at[top], piece(at, 2, top), {EXP: along})
    twins = [send(4, own_ref, piece(at, 0, whole, 1), twin_id)]
    heres = [pltpu.make_async_copy(own_ref, piece(at, 0, whole), local_sem.at[0])]
    heres[0].start()
    if with_info:
        info_at = lambda place: info_all_ref.at[place * 2 + core]
        heres.append(pltpu.make_async_copy(info_ref, info_at(at), local_sem.at[1]))
        heres[1].start()
        info_x = send(13, info_ref, info_at(at), {EXP: across})
        info_y = send(14, info_ref, info_at(at), {EXP: along})
        twins.append(send(15, info_ref, info_at(at), twin_id))
        info_x.wait_recv()
        info_far = send(16, info_at(across), info_at(across), {EXP: along})
        twins.append(send(17, info_at(across), info_at(across), twin_id))
        info_y.wait_recv()
        twins.append(send(18, info_at(along), info_at(along), twin_id))
        info_far.wait_recv()
        twins.append(send(19, info_at(far), info_at(far), twin_id))

    def hand_on(number, place, shift, part):
        src = piece(place, shift, part)
        twins.append(send(number, src, piece(place, shift, part, 1), twin_id))

    x_top.wait_recv()
    far_top = send(5, piece(across, 1, top), piece(across, 3, top), {EXP: along})
    hand_on(6, across, 1, top)
    y_bottom.wait_recv()
    far_bottom = send(7, piece(along, 2, bottom), piece(along, 3, bottom), {EXP: across})
    hand_on(8, along, 2, bottom)
    x_bottom.wait_recv()
    hand_on(9, across, 1, bottom)
    y_top.wait_recv()
    hand_on(10, along, 2, top)
    far_top.wait_recv()
    hand_on(11, far, 3, top)
    far_bottom.wait_recv()
    hand_on(12, far, 3, bottom)
    for copy in twins:
        copy.wait_recv()
    for copy in started:
        copy.wait_send()
    for copy in heres:
        copy.wait()


def plane_gather(own, info, relative, number):
    plane = lax.axis_size(PLANE)
    operands = [own] if info is None else [own, info]
    outs = [jax.ShapeDtypeStruct((plane, *v.shape), v.dtype) for v in operands]
    anywhere = pl.BlockSpec(memory_space=pl.ANY)
    return pl.pallas_call(
        partial(plane_gather_kernel, info is not None, relative),
        out_shape=outs,
        in_specs=[anywhere] * len(operands),
        out_specs=[anywhere] * len(operands),
        scratch_shapes=[
            pltpu.SemaphoreType.DMA((20,)),
            pltpu.SemaphoreType.DMA((20,)),
            pltpu.SemaphoreType.DMA((2,)),
        ],
        compiler_params=pltpu.CompilerParams(collective_id=number, has_side_effects=True),
        cost_estimate=pl.CostEstimate(
            flops=0, bytes_accessed=own.size, transcendentals=0
        ),
    )(*operands)


def plane_scatter_kernel(relative, with_extra, *refs):
    if with_extra:
        part_ref, extra_ref, out_ref, *refs = refs
        extra_out, refs = refs[:4], refs[4:]
        extra_own, extra_got, extra_sems, refs = refs[0], refs[1], refs[2:5], refs[5:]
    else:
        part_ref, out_ref, *refs = refs
    own, twin_got, x_got, y_got, x_last, y_last, send_sem, recv_sem, local_sem = refs
    at, core, across, along, far = plane_places()
    rows = part_ref.shape[1]
    half = rows // 2
    step = 64
    greet(across, along, core)
    started = []

    def send(number, src, dst, target):
        copy = pltpu.make_async_remote_copy(
            src_ref=src,
            dst_ref=dst,
            send_sem=send_sem.at[number],
            recv_sem=recv_sem.at[number],
            device_id=target,
            device_id_type=MESH_ID,
        )
        copy.start()
        started.append(copy)
        return copy

    twins, heres = [], []
    for j, (label, shift) in enumerate(((far, 3), (across, 1), (along, 2), (at, 0))):
        theirs = shift + 4 if relative else label * 2 + 1 - core
        ours = shift if relative else label * 2 + core
        twins.append(send(j, part_ref.at[theirs], twin_got.at[j], {CTX: 1 - core}))
        here = pltpu.make_async_copy(part_ref.at[ours], own.at[j], local_sem.at[j])
        here.start()
        heres.append(here)

    def add_rows(target, t_first, count, source, s_first):
        @pl.loop(0, count // step)
        def _(i):
            into = pl.ds(pl.multiple_of(t_first + i * step, step), step)
            take = pl.ds(pl.multiple_of(s_first + i * step, step), step)
            total = target[into].astype(jnp.float32) + source[take].astype(jnp.float32)
            target[into] = total.astype(target.dtype)

    top, bottom = pl.ds(0, half), pl.ds(half, half)
    x_sent, y_sent = [], []
    for j in range(4):
        twins[j].wait_recv()
        heres[j].wait()
        add_rows(own.at[j], 0, rows, twin_got.at[j], 0)
        if j < 2:
            x_sent.append(send(4 + j, own.at[j, top], x_got.at[j], {EXP: across}))
        if j == 0 or j == 2:
            y_sent.append(send(6 + j // 2, own.at[j, bottom], y_got.at[j // 2], {EXP: along}))
    if with_extra:
        extra_here, extra_twin, extra_done = [], [], []
        for k in range(4):
            copy = pltpu.make_async_remote_copy(
                src_ref=extra_ref.at[k + 4],
                dst_ref=extra_got.at[k],
                send_sem=extra_sems[0].at[k],
                recv_sem=extra_sems[1].at[k],
                device_id={CTX: 1 - core},
                device_id_type=MESH_ID,
            )
            copy.start()
            started.append(copy)
            extra_twin.append(copy)
            here = pltpu.make_async_copy(extra_ref.at[k], extra_own.at[k], extra_sems[2].at[k])
            here.start()
            extra_here.append(here)
        for k in range(4):
            extra_twin[k].wait_recv()
            extra_here[k].wait()
            add_rows(extra_own.at[k], 0, rows, extra_got.at[k], 0)
            here = pltpu.make_async_copy(extra_own.at[k], extra_out[k], extra_sems[2].at[k])
            here.start()
            extra_done.append(here)
    x_sent[0].wait_recv()
    add_rows(own.at[2], 0, half, x_got.at[0], 0)
    last_y = send(8, own.at[2, top], y_last, {EXP: along})
    y_sent[0].wait_recv()
    add_rows(own.at[1], half, half, y_got.at[0], 0)
    last_x = send(9, own.at[1, bottom], x_last, {EXP: across})

    def finish(first, near, later):
        @pl.loop(0, half // step)
        def _(i):
            take = pl.ds(pl.multiple_of(i * step, step), step)
            into = pl.ds(pl.multiple_of(first + i * step, step), step)
            out_ref[into] = (
                own[3, into].astype(jnp.float32)
                + near[1, take].astype(jnp.float32)
                + later[take].astype(jnp.float32)
            ).astype(out_ref.dtype)

    x_sent[1].wait_recv()
    last_y.wait_recv()
    finish(0, x_got, y_last)
    y_sent[1].wait_recv()
    last_x.wait_recv()
    finish(half, y_got, x_last)
    if with_extra:
        for copy in extra_done:
            copy.wait()
    for copy in started:
        copy.wait_send()


def plane_scatter(parts, relative, number, out_type, extra=None):
    plane, rows, cols = parts.shape
    operands, extra_scratch = [parts], []
    out_shape = [jax.ShapeDtypeStruct((rows, cols), out_type)]
    out_specs = [pl.BlockSpec(memory_space=pltpu.VMEM)]
    anywhere = pl.BlockSpec(memory_space=pl.ANY)
    if extra is not None:
        operands.append(extra)
        out_shape += [jax.ShapeDtypeStruct((rows, cols), extra.dtype)] * 4
        out_specs += [anywhere] * 4
        extra_scratch = [pltpu.VMEM((4, rows, cols), extra.dtype)] * 2
        extra_scratch += [pltpu.SemaphoreType.DMA((4,))] * 3
    half = rows // 2
    vmem = lambda *shape: pltpu.VMEM(shape, parts.dtype)
    return pl.pallas_call(
        partial(plane_scatter_kernel, relative, extra is not None),
        out_shape=out_shape,
        in_specs=[anywhere] * len(operands),
        out_specs=out_specs,
        scratch_shapes=extra_scratch
        + [
            vmem(4, rows, cols),
            vmem(4, rows, cols),
            vmem(2, half, cols),
            vmem(2, half, cols),
            vmem(half, cols),
            vmem(half, cols),
            pltpu.SemaphoreType.DMA((10,)),
            pltpu.SemaphoreType.DMA((10,)),
            pltpu.SemaphoreType.DMA((4,)),
        ],
        compiler_params=pltpu.CompilerParams(
            collective_id=number,
            has_side_effects=True,
            vmem_limit_bytes=(36 if extra is None else 54) * 2**20,
        ),
        cost_estimate=pl.CostEstimate(
            flops=0, bytes_accessed=rows * cols, transcendentals=0
        ),
    )(*operands)


def norm_qkv_kernel(hidden_ref, gain_ref, w_ref, norm_ref, qkv_ref):
    values = hidden_ref[...].astype(jnp.float32)
    inv = lax.rsqrt(jnp.mean(values * values, axis=1, keepdims=True) + EPS)
    norm_ref[...] = low(values * inv * gain_ref[...])
    qkv_ref[...] = low(mm(norm_ref[...], w_ref[...]))


def norm_qkv(hidden, gain, w, block):
    rows, width = hidden.shape
    cols = w.shape[1]
    return pl.pallas_call(
        norm_qkv_kernel,
        grid=(rows // block,),
        in_specs=[
            pl.BlockSpec((block, width), lambda i: (i, 0)),
            pl.BlockSpec((1, width), lambda i: (0, 0)),
            pl.BlockSpec((width, cols), lambda i: (0, 0)),
        ],
        out_specs=[
            pl.BlockSpec((block, width), lambda i: (i, 0)),
            pl.BlockSpec((block, cols), lambda i: (i, 0)),
        ],
        out_shape=[
            jax.ShapeDtypeStruct((rows, width), jnp.bfloat16),
            jax.ShapeDtypeStruct((rows, cols), jnp.bfloat16),
        ],
        compiler_params=pltpu.CompilerParams(vmem_limit_bytes=48 * 2**20),
        cost_estimate=pl.CostEstimate(
            flops=2 * rows * width * cols,
            bytes_accessed=4 * rows * width,
            transcendentals=0,
        ),
    )(hidden, gain, w)


def chosen_rows(slots, capacity):
    lanes = lax.broadcasted_iota(jnp.int32, (slots.shape[0], capacity), 1)
    return (slots == lanes).astype(jnp.bfloat16)


def output_kernel(
    half,
    hidden_ref,
    down_ref,
    rows_ref,
    slot_ref,
    sg_ref,
    gate_ref,
    cot_ref,
    near_ref,
    dots_ref,
    given,
    got,
    send_sem,
    recv_sem,
):
    step_at = pl.program_id(0)
    is_far = step_at < half
    slot = lax.rem(step_at, half)
    twin_id = {CTX: 1 - lax.axis_index(CTX)}

    @pl.when(step_at == 0)
    def _():
        barrier = pltpu.get_barrier_semaphore()
        pl.semaphore_signal(barrier, inc=1, device_id=twin_id, device_id_type=MESH_ID)
        pl.semaphore_wait(barrier, 1)

    def block_copy(k):
        return pltpu.make_async_remote_copy(
            src_ref=given.at[k],
            dst_ref=got.at[k],
            send_sem=send_sem.at[k],
            recv_sem=recv_sem.at[k],
            device_id=twin_id,
            device_id_type=MESH_ID,
        )

    def make(store):
        chosen = chosen_rows(slot_ref[...], rows_ref.shape[1])
        hidden = hidden_ref[...].T
        tokens, width = cot_ref.shape
        step, lanes = 512, 128
        gate_dot = jnp.zeros((tokens, lanes), jnp.float32)
        shared_dot = jnp.zeros((tokens, lanes), jnp.float32)
        for first in range(0, width, step):
            cols = pl.ds(first, step)
            shared = mm(hidden, down_ref[:, cols])
            picked = mm(chosen, rows_ref[0, :, cols])
            cot = cot_ref[:, cols].astype(jnp.float32)
            gate_part, shared_part = picked * cot, shared * cot
            for at in range(0, step, lanes):
                gate_dot += gate_part[:, at : at + lanes]
                shared_dot += shared_part[:, at : at + lanes]
            store(cols, sg_ref[...] * shared + gate_ref[...] * picked)
        lane = lax.broadcasted_iota(jnp.int32, dots_ref.shape, 1)
        gate_dot = jnp.sum(gate_dot, axis=1, keepdims=True)
        shared_dot = jnp.sum(shared_dot, axis=1, keepdims=True)
        dots_ref[...] = jnp.where(lane == 0, gate_dot, jnp.where(lane == 1, shared_dot, 0.0))

    @pl.when(is_far)
    def _():
        def store(cols, total):
            given[slot, :, cols] = low(total)

        make(store)
        block_copy(slot).start()

    @pl.when(jnp.logical_not(is_far))
    def _():
        block_copy(slot).wait_recv()

        def store(cols, total):
            near_ref[0, :, cols] = low(total + got[slot, :, cols].astype(jnp.float32))

        make(store)

    @pl.when(step_at == 2 * half - 1)
    def _():
        for k in range(half):
            block_copy(k).wait_send()


def output_parts(hidden, down, rows, slots, sg, gates, cot):
    blocks, capacity, width = rows.shape
    units, count = hidden.shape
    tokens, half = count // blocks, blocks // 2
    at = lambda i: lax.rem(i + half, blocks)
    column = pl.BlockSpec((tokens, 1), lambda i: (at(i), 0))
    return pl.pallas_call(
        partial(output_kernel, half),
        grid=(blocks,),
        in_specs=[
            pl.BlockSpec((units, tokens), lambda i: (0, at(i))),
            pl.BlockSpec((units, width), lambda i: (0, 0)),
            pl.BlockSpec((1, capacity, width), lambda i: (at(i), 0, 0)),
            column,
            column,
            column,
            pl.BlockSpec((tokens, width), lambda i: (at(i), 0)),
        ],
        out_specs=[
            pl.BlockSpec((1, tokens, width), lambda i: (jnp.maximum(i - half, 0), 0, 0)),
            pl.BlockSpec((tokens, 128), lambda i: (at(i), 0)),
        ],
        out_shape=[
            jax.ShapeDtypeStruct((half, tokens, width), jnp.bfloat16),
            jax.ShapeDtypeStruct((count, 128), jnp.float32),
        ],
        scratch_shapes=[
            pltpu.VMEM((half, tokens, width), jnp.bfloat16),
            pltpu.VMEM((half, tokens, width), jnp.bfloat16),
            pltpu.SemaphoreType.DMA((half,)),
            pltpu.SemaphoreType.DMA((half,)),
        ],
        compiler_params=pltpu.CompilerParams(
            collective_id=4, has_side_effects=True, vmem_limit_bytes=56 * 2**20
        ),
        cost_estimate=pl.CostEstimate(
            flops=2 * count * width * (units + capacity),
            bytes_accessed=6 * count * width,
            transcendentals=0,
        ),
    )(hidden, down, rows, slots, sg, gates, cot)


def scatter_step(compute, out_ref, scratch):
    given, total, x_got, y_got, x_last, y_last, send_sem, recv_sem = scratch
    at, core, across, along, far = plane_places()
    step_at = pl.program_id(0)
    row = step_at // 2
    is_twin = step_at % 2 == 0
    rows = total.shape[1]
    half = rows // 2
    top, bottom = pl.ds(0, half), pl.ds(half, half)

    def copy_of(number, src, dst, target):
        return pltpu.make_async_remote_copy(
            src_ref=src,
            dst_ref=dst,
            send_sem=send_sem.at[number],
            recv_sem=recv_sem.at[number],
            device_id=target,
            device_id_type=MESH_ID,
        )

    def twin_copy(k):
        return copy_of(k, given.at[k % 2], total.at[k], {CTX: 1 - core})

    far_x = copy_of(4, total.at[0, top], x_got.at[0], {EXP: across})
    far_y = copy_of(5, total.at[0, bottom], y_got.at[0], {EXP: along})
    own_x = copy_of(6, total.at[1, top], x_got.at[1], {EXP: across})
    own_y = copy_of(7, total.at[2, bottom], y_got.at[1], {EXP: along})
    last_y = copy_of(8, total.at[2, top], y_last, {EXP: along})
    last_x = copy_of(9, total.at[1, bottom], x_last, {EXP: across})

    @pl.when(step_at == 0)
    def _():
        greet(across, along, core)

    @pl.when(is_twin)
    def _():
        @pl.when(row >= 2)
        def _():
            twin_copy(row - 2).wait_send()

        def store(cols, values):
            given[row % 2, :, cols] = low(values)

        compute(store)
        twin_copy(row).start()

    @pl.when(jnp.logical_not(is_twin))
    def _():
        twin_copy(row).wait_recv()

        def store(cols, values):
            total[row, :, cols] = low(values + total[row, :, cols].astype(jnp.float32))

        compute(store)

    @pl.when(step_at == 1)
    def _():
        far_x.start()
        far_y.start()

    @pl.when(step_at == 3)
    def _():
        own_x.start()

    @pl.when(step_at == 5)
    def _():
        own_y.start()

    @pl.when(step_at == 7)
    def _():
        def add_half(k, first, got):
            @pl.loop(0, half // 64)
            def _(i):
                take = pl.ds(pl.multiple_of(i * 64, 64), 64)
                into = pl.ds(pl.multiple_of(first + i * 64, 64), 64)
                total[k, into] = low(
                    total[k, into].astype(jnp.float32) + got[0, take].astype(jnp.float32)
                )

        def finish(first, near, later):
            @pl.loop(0, half // 64)
            def _(i):
                take = pl.ds(pl.multiple_of(i * 64, 64), 64)
                into = pl.ds(pl.multiple_of(first + i * 64, 64), 64)
                out_ref[into] = (
                    total[3, into].astype(jnp.float32)
                    + near[1, take].astype(jnp.float32)
                    + later[take].astype(jnp.float32)
                )

        far_x.wait_recv()
        add_half(2, 0, x_got)
        last_y.start()
        far_y.wait_recv()
        add_half(1, half, y_got)
        last_x.start()
        own_x.wait_recv()
        last_y.wait_recv()
        finish(0, x_got, y_last)
        own_y.wait_recv()
        last_x.wait_recv()
        finish(half, y_got, x_last)
        for copy in (twin_copy(2), twin_copy(3), far_x, far_y, own_x, own_y, last_y, last_x):
            copy.wait_send()


def step_slot(i):
    row = i // 2
    shift = jnp.where(row == 0, 3, jnp.where(row == 3, 0, row))
    return shift + 4 * (1 - i % 2)


def scatter_scratch(tokens, width):
    vmem = lambda *shape: pltpu.VMEM(shape, jnp.bfloat16)
    return [
        vmem(2, tokens, width),
        vmem(4, tokens, width),
        vmem(2, tokens // 2, width),
        vmem(2, tokens // 2, width),
        vmem(tokens // 2, width),
        vmem(tokens // 2, width),
        pltpu.SemaphoreType.DMA((10,)),
        pltpu.SemaphoreType.DMA((10,)),
    ]


def n2_grad_kernel(dgate_ref, dup_ref, gate_ref, up_ref, rows_ref, slot_ref, out_ref, *scratch):
    def compute(store):
        chosen = chosen_rows(slot_ref[...], rows_ref.shape[1])
        dgate, dup = dgate_ref[...].T, dup_ref[...].T
        step = 512
        for first in range(0, gate_ref.shape[1], step):
            cols = pl.ds(first, step)
            total = mm(dgate, gate_ref[:, cols]) + mm(dup, up_ref[:, cols])
            store(cols, total + mm(chosen, rows_ref[0, :, cols]))

    scatter_step(compute, out_ref, scratch)


def n2_grad_sum(dgate, dup, gate_w, up_w, rows, slots):
    blocks, capacity, width = rows.shape
    units, count = dgate.shape
    tokens = count // blocks
    by_units = pl.BlockSpec((units, tokens), lambda i: (0, step_slot(i)))
    whole = pl.BlockSpec((units, width), lambda i: (0, 0), pipeline_mode=pl.Buffered(1))
    return pl.pallas_call(
        n2_grad_kernel,
        grid=(blocks,),
        in_specs=[
            by_units,
            by_units,
            whole,
            whole,
            pl.BlockSpec((1, capacity, width), lambda i: (step_slot(i), 0, 0)),
            pl.BlockSpec((tokens, 1), lambda i: (step_slot(i), 0)),
        ],
        out_specs=pl.BlockSpec((tokens, width), lambda i: (0, 0)),
        out_shape=jax.ShapeDtypeStruct((tokens, width), jnp.float32),
        scratch_shapes=scatter_scratch(tokens, width),
        compiler_params=pltpu.CompilerParams(
            collective_id=3, has_side_effects=True, vmem_limit_bytes=56 * 2**20
        ),
        cost_estimate=pl.CostEstimate(
            flops=2 * count * width * (2 * units + capacity),
            bytes_accessed=4 * count * width,
            transcendentals=0,
        ),
    )(dgate, dup, gate_w, up_w, rows, slots)


def unit_grad_kernel(hid_ref, dgate_ref, dup_ref, cot_ref, n2_ref, out_ref):
    units = hid_ref.shape[0]
    out_ref[0, :units] = low(mm(hid_ref[...], cot_ref[...]))
    out_ref[0, units : 2 * units] = low(mm(dgate_ref[...], n2_ref[...]))
    out_ref[0, 2 * units :] = low(mm(dup_ref[...], n2_ref[...]))


def unit_grads(hidden, dgate, dup, cots, n2, depth, halves):
    units, count = hidden.shape
    width = n2.shape[1]
    cols = width // (depth * halves)
    whole = pl.BlockSpec((units, count), lambda i: (0, 0), pipeline_mode=pl.Buffered(1))
    strip = pl.BlockSpec((count, cols), lambda i: (0, i))
    return pl.pallas_call(
        unit_grad_kernel,
        grid=(depth * halves,),
        in_specs=[whole, whole, whole, strip, strip],
        out_specs=pl.BlockSpec(
            (1, 3 * units, cols), lambda i: (lax.rem(i, depth), 0, i // depth)
        ),
        out_shape=jax.ShapeDtypeStruct((depth, 3 * units, halves * cols), jnp.bfloat16),
        compiler_params=pltpu.CompilerParams(vmem_limit_bytes=48 * 2**20),
        cost_estimate=pl.CostEstimate(
            flops=6 * units * count * width,
            bytes_accessed=2 * (3 * units * count + 2 * count * width + 3 * units * width),
            transcendentals=0,
        ),
    )(hidden, dgate, dup, cots, n2)


def after(values, others):
    return lax.optimization_barrier((values, others))[0]


def swap(values, bits):
    return lax.ppermute(values, EXP, [(i, i ^ bits) for i in range(4)])


def twin(values):
    return lax.ppermute(values, CTX, [(0, 1), (1, 0)])


def twin_sums(ours, theirs):
    got = twin(theirs)
    return [low(ours[k].astype(jnp.float32) + got[k].astype(jnp.float32)) for k in range(4)]


def hops(sums):
    return [sums[0]] + [swap(sums[k], k) for k in (1, 2, 3)]


def sum_up(parts):
    return sum(v.astype(jnp.float32) for v in parts)


def mm(left, right, dims=((1,), (0,))):
    return lax.dot_general(left, right, (dims, ((), ())), preferred_element_type=jnp.float32)


def low(values):
    return values.astype(jnp.bfloat16)


def local_plane(
    hidden,
    cotangent,
    segments,
    padding,
    routes,
    order,
    norm1_gain,
    w_query,
    w_key,
    w_value,
    w_out,
    norm2_gain,
    router,
    shared_gate_vec,
    shared_w_gate,
    shared_w_up,
    shared_w_down,
    expert_w_gate,
    expert_w_up,
    expert_w_down,
):
    plane = lax.axis_size(PLANE)
    groups = lax.axis_size(EXP)
    halves = lax.axis_size(CTX)
    depth = lax.axis_size(DP)
    me = lax.axis_index(PLANE)
    core = lax.axis_index(CTX)
    tokens, width = hidden.shape[1], hidden.shape[2]
    all_tokens = plane * tokens
    seq_len = halves * tokens
    experts_all = router.shape[1]
    head_cols = width // plane
    shard = width // depth

    token_info = jnp.concatenate(
        [segments + 1, jnp.where(padding > 0, segments + 1, 0), order[0], routes[0].T]
    )
    info_rows = token_info.shape[0]
    token_info = jnp.concatenate([token_info, jnp.zeros((8 - info_rows, tokens), jnp.int32)])

    hidden_all, info_all = plane_gather(hidden[0], token_info, False, 0)
    hidden_all = hidden_all.reshape(all_tokens, width)
    place = lax.axis_index(EXP)
    away = [(place ^ k) * 2 + (core ^ j) for j in (0, 1) for k in range(4)]
    away = jnp.stack(away)
    out_rows = shard // plane
    w_out_part = lax.dynamic_slice(w_out, (me * out_rows, 0), (out_rows, width))
    w_qkv_part = jnp.concatenate(
        [
            lax.dynamic_slice(w, (0, me * head_cols), (shard, head_cols))
            for w in (w_query, w_key, w_value)
        ]
        + [router, norm1_gain[:, None], norm2_gain[:, None], shared_gate_vec[:, None]]
        + [jnp.zeros((shard, 128 - experts_all - 3), jnp.bfloat16)]
        + [w_out_part.reshape(shard, -1)],
        axis=1,
    )
    w_qkv = lax.all_gather(w_qkv_part, DP, axis=0, tiled=True)
    w_out_part = w_qkv[:, 3 * head_cols + 128 :].reshape(depth, out_rows, width)
    small = w_qkv[:, 3 * head_cols : 3 * head_cols + 128].T
    w_qkv = w_qkv[:, : 3 * head_cols]
    router_t = small[:experts_all]
    g_one = small[experts_all].astype(jnp.float32)
    g_two = small[experts_all + 1].astype(jnp.float32)
    gate_vec = small[experts_all + 2]
    w_out_part = after(w_out_part, info_all)
    w_out_got = [swap(w_out_part, k) for k in (1, 2, 3)]

    def normed(values, gain):
        values = values.astype(jnp.float32)
        inv = lax.rsqrt(jnp.mean(values * values, axis=1, keepdims=True) + EPS)
        return values, inv, low(values * inv * gain)

    n1_all, qkv = norm_qkv(hidden_all, g_one[None], w_qkv, tokens)
    q_codes = info_all[:, 0].reshape(all_tokens, 1)
    k_codes = info_all[:, 1].reshape(all_tokens // seq_len, 1, seq_len)
    attended_cols = attention_call(qkv, None, q_codes, k_codes, seq_len)
    pieces = [w_out_part] + [after(v, attended_cols) for v in w_out_got]
    w_out_near = jnp.zeros((depth, groups, 1, out_rows, width), jnp.bfloat16)
    for k in range(4):
        w_out_near = lax.dynamic_update_slice(
            w_out_near, pieces[k][:, None, None], (0, place ^ k, 0, 0, 0)
        )
    w_out_far = twin(w_out_near)
    w_out_full = jnp.where(
        core == 0,
        jnp.concatenate([w_out_near, w_out_far], axis=2),
        jnp.concatenate([w_out_far, w_out_near], axis=2),
    ).reshape(width, width)

    x_rows, inv_one, _ = normed(hidden[0], g_one)
    cot_rows = cotangent[0].astype(jnp.float32)

    def to_tokens(cols):
        got = lax.all_to_all(
            cols.reshape(plane, tokens, head_cols), PLANE, split_axis=0, concat_axis=0, tiled=True
        )
        return got.transpose(1, 0, 2).reshape(tokens, width)

    def to_columns(rows_in):
        send = rows_in.reshape(tokens, plane, head_cols).transpose(1, 0, 2)
        got = lax.all_to_all(send, PLANE, split_axis=0, concat_axis=0, tiled=True)
        return got.reshape(all_tokens, head_cols)

    attended = to_tokens(attended_cols)
    residual = x_rows + mm(attended, w_out_full)
    residual, inv_two, n2 = normed(residual, g_two)

    units = shared_w_gate.shape[1]
    part = units // (depth * halves)
    pick = lambda w: lax.dynamic_index_in_dim(
        w.reshape(w.shape[0], depth, halves, part), core, axis=2, keepdims=False
    ).reshape(w.shape[0], depth * part)
    sh_gate_up = jnp.concatenate([pick(shared_w_gate), pick(shared_w_up)], axis=1)
    sh_gate_up = lax.all_gather(sh_gate_up, DP, axis=0, tiled=True)
    sh_gate_t, sh_up_t = sh_gate_up[:, : depth * part].T, sh_gate_up[:, depth * part :].T
    sh_down = lax.all_gather(
        lax.dynamic_slice(shared_w_down, (core * part, 0), (part, width)), DP, axis=0, tiled=True
    )
    n2 = after(n2, sh_gate_up)
    n2_all = plane_gather(n2, None, True, 2)[0].reshape(all_tokens, width)
    cot_own = after(cotangent[0], n2_all)
    cot_got = [swap(cot_own, k) for k in (1, 2, 3)]
    ex_gate = lax.all_gather(after(expert_w_gate[0], info_all), DP, axis=0, tiled=True)
    ex_up = lax.all_gather(after(expert_w_up[0], info_all), DP, axis=0, tiled=True)
    ex_down = lax.all_gather(after(expert_w_down[0], info_all), DP, axis=1, tiled=True)

    small_w = jnp.concatenate([router_t, gate_vec[None]])

    def gates_of(rows_in):
        both = mm(rows_in, small_w, ((1,), (1,)))
        z = both[:, :experts_all]
        e = jnp.exp(z - jnp.max(z, axis=1, keepdims=True))
        return e / jnp.sum(e, axis=1, keepdims=True), jax.nn.sigmoid(both[:, experts_all:])

    probs_all, sg_all = gates_of(n2_all)
    expert_gate = lax.dynamic_slice(probs_all, (0, me), (all_tokens, 1))

    capacity = (9 * tokens * TOP + 8 * experts_all - 1) // (8 * experts_all)
    info_away = info_all[away]
    order_all = info_away[:, 2]
    routed_here = jnp.any(info_away[:, 3 : 3 + TOP] == me, axis=1)
    earlier = (order_all[:, None, :] < order_all[:, :, None]) & routed_here[:, None, :]
    slots = jnp.sum(earlier.astype(jnp.int32), axis=2)
    slots = jnp.where(routed_here, slots, capacity)
    chosen = slots[:, None, :] == jnp.arange(capacity, dtype=jnp.int32)[None, :, None]
    onehot = chosen.astype(jnp.bfloat16)

    def rows_of(values):
        got = lax.dot_general(
            onehot,
            values.reshape(plane, tokens, width),
            (((2,), (1,)), ((0,), (0,))),
            preferred_element_type=jnp.float32,
        )
        return got.reshape(plane * capacity, width)

    slot_gates = jnp.sum(
        jnp.where(chosen, expert_gate.reshape(plane, 1, tokens), 0.0), axis=2
    ).reshape(plane * capacity, 1)
    expert_rows = low(rows_of(n2_all))
    gate_pre = mm(sh_gate_t, n2_all, ((1,), (1,)))
    up_pre = mm(sh_up_t, n2_all, ((1,), (1,)))
    gate_act = gate_pre * jax.nn.sigmoid(gate_pre)
    shared_hidden = low(gate_act * up_pre)
    expert_rows = after(expert_rows, (shared_hidden, sh_down))
    gate_e = mm(expert_rows, ex_gate)
    up_e = mm(expert_rows, ex_up)
    act_e = gate_e * jax.nn.sigmoid(gate_e)
    hidden_e = low(act_e * up_e)
    cot_near = jnp.concatenate([cot_own] + [after(v, gate_e) for v in cot_got])
    cot_all = jnp.concatenate([cot_near, twin(cot_near)])
    row_cots = low(rows_of(cot_all))
    row_grads = low(row_cots.astype(jnp.float32) * slot_gates)

    shared_grads = low(sg_all * cot_all.astype(jnp.float32))
    shared_hgrad = mm(sh_down, shared_grads, ((1,), (1,)))
    gate_grad_s = low(shared_hgrad * up_pre * silu_grad(gate_pre))
    up_grad_s = low(shared_hgrad * gate_act)
    rows_out = width // (halves * depth)

    def shared_scatter(total):
        first, second = total[:, :rows_out], total[:, rows_out:]
        keep = jnp.where(core == 0, first, second)
        got = twin(jnp.where(core == 0, second, first))
        both = jnp.where(core == 0, jnp.stack([keep, got]), jnp.stack([got, keep]))
        both = both.reshape(halves, depth, part, rows_out).transpose(1, 0, 2, 3)
        return both.reshape(units, rows_out).astype(jnp.float32)

    scatter = lambda v, dim: lax.psum_scatter(v, DP, scatter_dimension=dim, tiled=True)
    shared_sums = unit_grads(
        shared_hidden, gate_grad_s, up_grad_s, shared_grads, n2_all, depth, halves
    )
    shared_sums = scatter(shared_sums.reshape(3 * depth * depth * part, -1), 0)
    result_e = low(mm(hidden_e, ex_down))
    hgrad_e = mm(row_grads, ex_down, ((1,), (1,)))
    gate_grad_e = low(hgrad_e * up_e * silu_grad(gate_e))
    up_grad_e = low(hgrad_e * act_e)

    grad_ex_down = low(mm(hidden_e, row_grads, ((0,), (0,))))
    grad_ex_gate = low(mm(expert_rows, gate_grad_e, ((0,), (0,))))
    grad_ex_up = low(mm(expert_rows, up_grad_e, ((0,), (0,))))
    grads_made = (grad_ex_down, grad_ex_gate, grad_ex_up)
    grads = [scatter(v, dim) for v, dim in zip(grads_made, (1, 0, 0))]
    slots = slots.reshape(all_tokens, 1)
    out_near, dots = output_parts(
        shared_hidden,
        sh_down,
        result_e.reshape(plane, capacity, width),
        after(slots, grads_made),
        sg_all,
        expert_gate,
        cot_all,
    )
    rows_grad = low(
        mm(gate_grad_e, ex_gate, ((1,), (1,))) + mm(up_grad_e, ex_up, ((1,), (1,)))
    )

    out_got = [swap(out_near[k], k) for k in (1, 2)]
    slots, out_got, _ = lax.optimization_barrier((slots, out_got, shared_sums))
    n2_grad = n2_grad_sum(
        gate_grad_s,
        up_grad_s,
        sh_gate_t,
        sh_up_t,
        rows_grad.reshape(plane, capacity, width),
        slots,
    )
    out_far = swap(after(out_near[3], n2_grad), 3)

    dots = dots.reshape(plane, tokens, 128)[:, :, :2].transpose(0, 2, 1)
    back = jnp.arange(plane, dtype=jnp.int32) ^ me
    dots = dots[(back // 2) + 4 * (back % 2)]
    dots = lax.all_to_all(dots, PLANE, split_axis=0, concat_axis=0, tiled=True)
    probs_grad = dots[:, 0].T
    probs, sg = gates_of(n2)
    logit_grad = low(probs * (probs_grad - jnp.sum(probs * probs_grad, axis=1, keepdims=True)))
    sg_logit_grad = low(jnp.sum(dots[:, 1], axis=0)[:, None] * sg * (1.0 - sg))
    n2_grad = (
        n2_grad
        + mm(logit_grad, router_t)
        + sg_logit_grad.astype(jnp.float32) * gate_vec.astype(jnp.float32)[None]
    )
    residual_grad, grad_gain_two = norm_back(residual, inv_two, g_two, n2_grad)
    residual_grad = residual_grad + cot_rows
    low_residual = low(residual_grad)

    attended_grad = low(mm(low_residual, w_out_full, ((1,), (1,))))
    low_residual = after(low_residual, attended_grad)
    out_got = after(out_got, attended_grad)
    output = residual + out_near[0].astype(jnp.float32) + sum_up(out_got)
    attended_grad = to_columns(attended_grad)
    grad_out = low(mm(attended, low_residual, ((0,), (0,))))
    grad_out = grad_out.reshape(groups, halves, width // plane, width)
    block_of = lambda k, c: lax.dynamic_slice(
        grad_out, (place ^ k, c, 0, 0), (1, 1, width // plane, width)
    )[0, 0]
    out_grad_sums = twin_sums(
        [block_of(k, core) for k in range(4)],
        jnp.stack([block_of(k, 1 - core) for k in range(4)]),
    )
    attended_grad = after(attended_grad, (out_grad_sums, output, grads[0]))
    qkv_grad = attention_call(qkv, attended_grad, q_codes, k_codes, seq_len)
    grad_qkv = low(mm(n1_all, qkv_grad, ((0,), (0,))))
    fine = shard // plane
    grad_qkv = (
        grad_qkv.reshape(plane, depth, fine, 3 * head_cols)
        .transpose(1, 0, 2, 3)
        .reshape(width, 3 * head_cols)
    )
    qkv_grad, grad_out, _ = lax.optimization_barrier((qkv_grad, hops(out_grad_sums), grad_qkv))
    grad_out = low(sum_up(grad_out))
    n1_grad = low(mm(qkv_grad, w_qkv, ((1,), (1,))))
    n1_grad, out_far, _ = lax.optimization_barrier(
        (n1_grad, out_far, (grad_qkv, grad_out, grads[1]))
    )
    output = low(output + out_far.astype(jnp.float32))
    n1_grad = plane_scatter(n1_grad.reshape(plane, tokens, width), False, 1, jnp.float32)[0]
    grad_qkv = lax.psum_scatter(grad_qkv, DP, scatter_dimension=0, tiled=True)
    qkv_sum = grad_qkv
    w_rows = (
        w_qkv.reshape(plane, depth, fine, 3 * head_cols)
        .transpose(1, 0, 2, 3)
        .reshape(depth, plane * fine, 3 * head_cols)
    )
    w_rows = lax.dynamic_index_in_dim(w_rows, lax.axis_index(DP), axis=0, keepdims=False)
    gain_dots = jnp.sum(grad_qkv.astype(jnp.float32) * w_rows.astype(jnp.float32), axis=1)
    gain_dots = lax.all_to_all(
        gain_dots.reshape(plane, 1, fine), PLANE, split_axis=0, concat_axis=0, tiled=True
    )
    my_gain = lax.dynamic_slice(
        g_one, ((me * depth + lax.axis_index(DP)) * fine,), (fine,)
    )
    grad_gain_one = jnp.sum(gain_dots[:, 0], axis=0) / my_gain
    grad_qkv = lax.all_to_all(
        grad_qkv.reshape(plane, fine, 3 * head_cols),
        PLANE,
        split_axis=0,
        concat_axis=0,
        tiled=True,
    )
    grad_qkv = (
        grad_qkv.reshape(plane, fine, 3, head_cols)
        .transpose(2, 1, 0, 3)
        .reshape(3, fine, width)
        .astype(jnp.float32)
    )
    grad_ex_down, grad_ex_gate, grad_ex_up = [
        v.astype(jnp.float32)[None] for v in after(grads, n1_grad)
    ]
    grad_out = scatter(after(grad_out, (n1_grad, qkv_sum)), 0).astype(jnp.float32)
    shared_sums = after(shared_sums, (n1_grad, qkv_sum))
    grad_sh_down, grad_sh_gate, grad_sh_up = [
        shared_scatter(v)
        for v in shared_sums.reshape(3, units // halves, -1)
    ]
    grad_sh_gate, grad_sh_up = grad_sh_gate.T, grad_sh_up.T
    dz_all = jnp.concatenate([logit_grad, sg_logit_grad], axis=1)
    dz_all = after(dz_all, (n1_grad, qkv_sum))
    small_grads = mm(n2, dz_all, ((0,), (0,)))
    small_grads = jnp.concatenate([small_grads, grad_gain_two[:, None]], axis=1).T
    small_grads = jnp.pad(small_grads, ((0, 14 - experts_all), (0, 0)))
    small_grads = small_grads.reshape(16, plane, width // plane).transpose(1, 0, 2)
    small_grads = jnp.sum(
        lax.all_to_all(small_grads, PLANE, split_axis=0, concat_axis=0, tiled=True), axis=0
    )
    small_grads = small_grads.reshape(16, depth, shard // plane).transpose(1, 0, 2)
    small_grads = jnp.sum(
        lax.all_to_all(small_grads, DP, split_axis=0, concat_axis=0, tiled=True), axis=0
    )
    input_part, _ = norm_back(x_rows, inv_one, g_one, n1_grad)
    input_grad = low(residual_grad + input_part)
    return (
        output[None],
        input_grad[None],
        grad_gain_one,
        grad_qkv[0],
        grad_qkv[1],
        grad_qkv[2],
        grad_out,
        small_grads[experts_all + 1],
        small_grads[:experts_all].T,
        small_grads[experts_all],
        grad_sh_gate,
        grad_sh_up,
        grad_sh_down,
        grad_ex_gate,
        grad_ex_up,
        grad_ex_down,
    )


def solution(mesh):
    in_specs = (
        P((EXP, DP), CTX, None),
        P((EXP, DP), CTX, None),
        P((EXP, DP), CTX),
        P((EXP, DP), CTX),
        P((EXP, DP), CTX, None),
        P((EXP, DP), CTX, None),
        P(DP),
        P(DP, None),
        P(DP, None),
        P(DP, None),
        P(DP, None),
        P(DP),
        P(DP, None),
        P(DP),
        P(DP, EXP),
        P(DP, EXP),
        P((EXP, DP), None),
        P((EXP, CTX), DP, None),
        P((EXP, CTX), DP, None),
        P((EXP, CTX), None, DP),
    )
    out_specs = (
        P((EXP, DP), CTX, None),
        P((EXP, DP), CTX, None),
        P((EXP, CTX, DP)),
        P((EXP, CTX, DP), None),
        P((EXP, CTX, DP), None),
        P((EXP, CTX, DP), None),
        P((EXP, CTX, DP), None),
        P((EXP, CTX, DP)),
        P((EXP, CTX, DP), None),
        P((EXP, CTX, DP)),
        P((CTX, DP), EXP),
        P((CTX, DP), EXP),
        P(EXP, (CTX, DP)),
        P((EXP, CTX), DP, None),
        P((EXP, CTX), DP, None),
        P((EXP, CTX), None, DP),
    )
    plane = mesh.shape[EXP] * mesh.shape[CTX]

    def run(*args):
        square = mesh.shape[EXP] == 4 and mesh.shape[CTX] == 2 and mesh.shape[DP] == 4
        one_each = square and args[12].shape[1] == plane
        local = local_plane if one_each else local_general
        return jax.shard_map(
            local, mesh=mesh, in_specs=in_specs, out_specs=out_specs, check_vma=False
        )(*args)

    return run
```

```python
from functools import partial

import jax
import jax.numpy as jnp
from jax import lax
from jax.experimental import pallas as pl
from jax.experimental.pallas import tpu as pltpu
from jax.sharding import PartitionSpec as P

EXP, CTX, DP = "experts", "context", "dp"
PLANE = (EXP, CTX)
HEADS = 16
HEAD_DIM = 128
TOP = 4


EPS = 1e-06
NEG = -1e30


def silu_grad(pre_act):
    logistic = jax.nn.sigmoid(pre_act)
    return logistic * (1.0 + pre_act * (1.0 - logistic))


def block_slots(route_row, priority, expert_count):
    matches = (route_row[:, None] == jnp.arange(expert_count, dtype=jnp.int32)[None, :]).astype(
        jnp.int32
    )
    ordered = jnp.zeros_like(matches).at[priority].set(matches)
    before = jnp.cumsum(ordered, axis=0) - ordered
    return jnp.sum(before[priority] * matches, axis=1)


def norm_back(values_in, inv_rms, gain_vec, gradient):
    weighted = gradient * gain_vec
    inner_sum = jnp.mean(weighted * values_in, axis=1, keepdims=True)
    d_value = inv_rms * weighted - values_in * inv_rms**3 * inner_sum
    d_gain = jnp.sum(gradient * values_in * inv_rms, axis=0)
    return (d_value, d_gain)


def attend_head(packed, allowed, scale_factor):
    query_h, key_h, value_h = packed
    raw_scores = jnp.einsum("th,lh->tl", query_h, key_h, preferred_element_type=jnp.float32)
    logits = jnp.where(allowed, raw_scores * scale_factor, NEG)
    row_max = jnp.max(logits, axis=1, keepdims=True)
    exp_scores = jnp.exp(logits - row_max)
    row_total = jnp.sum(exp_scores, axis=1, keepdims=True)
    attn_probs = (exp_scores / row_total).astype(jnp.bfloat16)
    head_out = jnp.dot(attn_probs, value_h, preferred_element_type=jnp.float32).astype(jnp.bfloat16)
    return (head_out, row_max + jnp.log(row_total))


def attend_back(packed, allowed, scale_factor):
    query_h, key_h, value_h, out_grad, log_total = packed
    raw_scores = jnp.einsum("th,lh->tl", query_h, key_h, preferred_element_type=jnp.float32)
    logits = jnp.where(allowed, raw_scores * scale_factor, NEG)
    attn_probs = jnp.exp(logits - log_total)
    prob_grad = jnp.einsum("th,lh->tl", out_grad, value_h, preferred_element_type=jnp.float32)
    inner_sum = jnp.sum(attn_probs * prob_grad, axis=1, keepdims=True)
    score_grad = (attn_probs * (prob_grad - inner_sum) * scale_factor).astype(jnp.bfloat16)
    query_grad = jnp.dot(score_grad, key_h, preferred_element_type=jnp.float32)
    key_grad = jnp.einsum("tl,th->lh", score_grad, query_h, preferred_element_type=jnp.float32)
    value_grad = jnp.einsum(
        "tl,th->lh", attn_probs.astype(jnp.bfloat16), out_grad, preferred_element_type=jnp.float32
    )
    return (query_grad, key_grad, value_grad)


def local_general(
    hidden,
    cotangent,
    segments,
    padding,
    routes,
    order,
    norm1_gain,
    w_query,
    w_key,
    w_value,
    w_out,
    norm2_gain,
    router,
    shared_gate_vec,
    shared_w_gate,
    shared_w_up,
    shared_w_down,
    expert_w_gate,
    expert_w_up,
    expert_w_down,
):
    fetched = (
        lax.all_gather(norm1_gain, DP, axis=0, tiled=True),
        lax.all_gather(w_query, DP, axis=0, tiled=True),
        lax.all_gather(w_key, DP, axis=0, tiled=True),
        lax.all_gather(w_value, DP, axis=0, tiled=True),
        lax.all_gather(w_out, DP, axis=0, tiled=True),
        lax.all_gather(norm2_gain, DP, axis=0, tiled=True),
        lax.all_gather(router, DP, axis=0, tiled=True),
        lax.all_gather(shared_gate_vec, DP, axis=0, tiled=True),
        lax.all_gather(shared_w_gate, DP, axis=0, tiled=True),
        lax.all_gather(shared_w_up, DP, axis=0, tiled=True),
        lax.all_gather(shared_w_down, DP, axis=0, tiled=True),
        lax.all_gather(expert_w_gate, DP, axis=1, tiled=True),
        lax.all_gather(expert_w_up, DP, axis=1, tiled=True),
        lax.all_gather(expert_w_down, DP, axis=2, tiled=True),
    )
    (
        gain_one,
        query_w,
        key_w,
        value_w,
        out_w,
        gain_two,
        router_full,
        gate_vec,
        sh_gate,
        sh_up,
        sh_down,
        ex_gate,
        ex_up,
        ex_down,
    ) = fetched
    sh_gate, sh_up, sh_down = (
        lax.all_gather(sh_gate, EXP, axis=1, tiled=True),
        lax.all_gather(sh_up, EXP, axis=1, tiled=True),
        lax.all_gather(sh_down, EXP, axis=0, tiled=True),
    )
    tokens_here = hidden.shape[1]
    model_width = hidden.shape[2]
    x_rows = hidden[0].astype(jnp.float32)
    cot_rows = cotangent[0].astype(jnp.float32)
    inv_one = lax.rsqrt(jnp.mean(x_rows * x_rows, axis=1, keepdims=True) + EPS)
    g_one = gain_one.astype(jnp.float32)
    normed_one = (x_rows * inv_one * g_one).astype(jnp.bfloat16)
    queries = jnp.dot(normed_one, query_w, preferred_element_type=jnp.float32).astype(jnp.bfloat16)
    keys_own = jnp.dot(normed_one, key_w, preferred_element_type=jnp.float32).astype(jnp.bfloat16)
    values_own = jnp.dot(normed_one, value_w, preferred_element_type=jnp.float32).astype(
        jnp.bfloat16
    )
    own_codes = jnp.where(padding[0] > 0, segments[0] + 1, 0)
    code_parts = jnp.stack([own_codes // 64, own_codes % 64]).astype(jnp.bfloat16)
    keys_all, values_all, parts_all = (
        lax.all_gather(keys_own, CTX, axis=0, tiled=True),
        lax.all_gather(values_own, CTX, axis=0, tiled=True),
        lax.all_gather(code_parts, CTX, axis=1, tiled=True),
    )
    key_codes = parts_all[0].astype(jnp.int32) * 64 + parts_all[1].astype(jnp.int32)
    seq_total = keys_all.shape[0]
    query_pos = lax.axis_index(CTX) * tokens_here + jnp.arange(tokens_here, dtype=jnp.int32)
    key_pos = jnp.arange(seq_total, dtype=jnp.int32)
    same_doc = key_codes[None, :] == (segments[0] + 1)[:, None]
    allowed = (key_pos[None, :] <= query_pos[:, None]) & (
        same_doc | (key_pos[None, :] == query_pos[:, None])
    )
    scale_factor = HEAD_DIM ** (-0.5)

    def to_heads(rows_in):
        return rows_in.reshape(rows_in.shape[0], HEADS, HEAD_DIM).transpose(1, 0, 2)

    def from_heads(heads_in):
        return heads_in.transpose(1, 0, 2).reshape(heads_in.shape[1], model_width)

    head_q = to_heads(queries)
    head_k = to_heads(keys_all)
    head_v = to_heads(values_all)
    head_out, log_total = lax.map(
        partial(attend_head, allowed=allowed, scale_factor=scale_factor), (head_q, head_k, head_v)
    )
    attended = from_heads(head_out)
    residual = x_rows + jnp.dot(attended, out_w, preferred_element_type=jnp.float32)
    inv_two = lax.rsqrt(jnp.mean(residual * residual, axis=1, keepdims=True) + EPS)
    g_two = gain_two.astype(jnp.float32)
    normed_two = (residual * inv_two * g_two).astype(jnp.bfloat16)
    router_logits = jnp.dot(normed_two, router_full, preferred_element_type=jnp.float32)
    router_exp = jnp.exp(router_logits - jnp.max(router_logits, axis=1, keepdims=True))
    router_probs = router_exp / jnp.sum(router_exp, axis=1, keepdims=True)
    route_gates = jnp.take_along_axis(router_probs, routes[0], axis=1)
    shared_gate = jax.nn.sigmoid(jnp.dot(normed_two, gate_vec, preferred_element_type=jnp.float32))
    shared_scaled = (shared_gate[:, None] * cot_rows).astype(jnp.bfloat16)
    rows_group, grads_group = (normed_two, shared_scaled)
    gate_pre = jnp.dot(rows_group, sh_gate, preferred_element_type=jnp.float32)
    up_pre = jnp.dot(rows_group, sh_up, preferred_element_type=jnp.float32)
    gate_act = gate_pre * jax.nn.sigmoid(gate_pre)
    shared_hidden = (gate_act * up_pre).astype(jnp.bfloat16)
    shared_part = jnp.dot(shared_hidden, sh_down, preferred_element_type=jnp.float32)
    experts_all = router_full.shape[1]
    capacity = (9 * tokens_here * TOP + 8 * experts_all - 1) // (8 * experts_all)
    priority = (order[0, 0][:, None] * TOP + jnp.arange(TOP, dtype=jnp.int32)[None, :]).reshape(-1)
    flat_routes = routes[0].reshape(-1)
    slot_index = block_slots(flat_routes, priority, experts_all)
    kept_rows = slot_index < capacity
    target = flat_routes * capacity + jnp.minimum(slot_index, capacity - 1)
    row_gates = route_gates.reshape(-1)
    cot_repeated = jnp.repeat(cot_rows, TOP, axis=0)
    source_rows = jnp.repeat(normed_two, TOP, axis=0)
    source_grads = (cot_repeated * row_gates[:, None]).astype(jnp.bfloat16)
    empty_slots = jnp.zeros((experts_all * capacity, model_width), jnp.bfloat16)
    send_rows = empty_slots.at[target].add(
        jnp.where(kept_rows[:, None], source_rows, jnp.zeros_like(source_rows))
    )
    send_grads = empty_slots.at[target].add(
        jnp.where(kept_rows[:, None], source_grads, jnp.zeros_like(source_grads))
    )
    recv_rows, recv_grads = (
        lax.all_to_all(
            send_rows.reshape(experts_all, capacity, model_width),
            (EXP, CTX),
            split_axis=0,
            concat_axis=0,
            tiled=True,
        ),
        lax.all_to_all(
            send_grads.reshape(experts_all, capacity, model_width),
            (EXP, CTX),
            split_axis=0,
            concat_axis=0,
            tiled=True,
        ),
    )
    local_count = ex_gate.shape[0]
    sources = experts_all // local_count

    def to_local(buffer_in):
        return (
            buffer_in.reshape(sources, local_count, capacity, model_width)
            .transpose(1, 0, 2, 3)
            .reshape(local_count, sources * capacity, model_width)
        )

    def to_owner(buffer_in):
        return (
            buffer_in.reshape(local_count, sources, capacity, model_width)
            .transpose(1, 0, 2, 3)
            .reshape(experts_all, capacity, model_width)
        )

    expert_rows = to_local(recv_rows)
    expert_grads_in = to_local(recv_grads)
    gate_e = jnp.einsum("erd,edf->erf", expert_rows, ex_gate, preferred_element_type=jnp.float32)
    up_e = jnp.einsum("erd,edf->erf", expert_rows, ex_up, preferred_element_type=jnp.float32)
    act_e = gate_e * jax.nn.sigmoid(gate_e)
    hidden_e = (act_e * up_e).astype(jnp.bfloat16)
    result_e = jnp.einsum(
        "erf,efd->erd", hidden_e, ex_down, preferred_element_type=jnp.float32
    ).astype(jnp.bfloat16)
    returned = lax.all_to_all(
        to_owner(result_e), (EXP, CTX), split_axis=0, concat_axis=0, tiled=True
    )
    picked = returned.reshape(experts_all * capacity, model_width)[target]
    picked = jnp.where(kept_rows[:, None], picked, jnp.zeros_like(picked)).astype(jnp.float32)
    routed = jnp.sum((picked * row_gates[:, None]).reshape(tokens_here, TOP, model_width), axis=1)
    output = (residual + shared_gate[:, None] * shared_part + routed).astype(jnp.bfloat16)
    gate_grads = jnp.sum(picked * cot_repeated, axis=1).reshape(tokens_here, TOP)
    hidden_grad_e = jnp.einsum(
        "erd,efd->erf", expert_grads_in, ex_down, preferred_element_type=jnp.float32
    )
    gate_grad_e = (hidden_grad_e * up_e * silu_grad(gate_e)).astype(jnp.bfloat16)
    up_grad_e = (hidden_grad_e * act_e).astype(jnp.bfloat16)
    grad_ex_down = jnp.einsum(
        "erf,erd->efd", hidden_e, expert_grads_in, preferred_element_type=jnp.float32
    )
    grad_ex_gate = jnp.einsum(
        "erd,erf->edf", expert_rows, gate_grad_e, preferred_element_type=jnp.float32
    )
    grad_ex_up = jnp.einsum(
        "erd,erf->edf", expert_rows, up_grad_e, preferred_element_type=jnp.float32
    )
    expert_sums = (
        lax.psum_scatter(grad_ex_gate, DP, scatter_dimension=1, tiled=True),
        lax.psum_scatter(grad_ex_up, DP, scatter_dimension=1, tiled=True),
        lax.psum_scatter(grad_ex_down, DP, scatter_dimension=2, tiled=True),
    )
    rows_grad_e = jnp.einsum(
        "erf,edf->erd", gate_grad_e, ex_gate, preferred_element_type=jnp.float32
    )
    rows_grad_e = (
        rows_grad_e
        + jnp.einsum("erf,edf->erd", up_grad_e, ex_up, preferred_element_type=jnp.float32)
    ).astype(jnp.bfloat16)
    returned_grads = lax.all_to_all(
        to_owner(rows_grad_e), (EXP, CTX), split_axis=0, concat_axis=0, tiled=True
    )
    routed_grad = returned_grads.reshape(experts_all * capacity, model_width)[target]
    routed_grad = jnp.where(kept_rows[:, None], routed_grad, jnp.zeros_like(routed_grad)).astype(
        jnp.float32
    )
    norm_grad = jnp.sum(routed_grad.reshape(tokens_here, TOP, model_width), axis=1)
    choose = (
        routes[0][:, :, None] == jnp.arange(experts_all, dtype=jnp.int32)[None, None, :]
    ).astype(jnp.float32)
    probs_grad = jnp.einsum("tk,tke->te", gate_grads, choose)
    logit_grad = (
        router_probs * (probs_grad - jnp.sum(router_probs * probs_grad, axis=1, keepdims=True))
    ).astype(jnp.bfloat16)
    grad_router = jnp.dot(normed_two.T, logit_grad, preferred_element_type=jnp.float32)
    gate_logit_grad = (
        jnp.sum(cot_rows * shared_part, axis=1) * shared_gate * (1.0 - shared_gate)
    ).astype(jnp.bfloat16)
    grad_gate_vec = jnp.dot(gate_logit_grad, normed_two, preferred_element_type=jnp.float32)
    norm_grad = norm_grad + jnp.dot(logit_grad, router_full.T, preferred_element_type=jnp.float32)
    norm_grad = (
        norm_grad
        + gate_logit_grad.astype(jnp.float32)[:, None] * gate_vec.astype(jnp.float32)[None, :]
    )
    shared_hgrad = jnp.dot(grads_group, sh_down.T, preferred_element_type=jnp.float32)
    gate_grad_s = (shared_hgrad * up_pre * silu_grad(gate_pre)).astype(jnp.bfloat16)
    up_grad_s = (shared_hgrad * gate_act).astype(jnp.bfloat16)
    shared_rows_grad = jnp.dot(gate_grad_s, sh_gate.T, preferred_element_type=jnp.float32)
    shared_rows_grad = shared_rows_grad + jnp.dot(
        up_grad_s, sh_up.T, preferred_element_type=jnp.float32
    )
    groups = lax.axis_size(EXP)
    parts_cd = lax.axis_size((CTX, DP))
    rows_count = rows_group.shape[0]
    arr_gate = jnp.einsum(
        "td,tes->eds",
        rows_group,
        gate_grad_s.reshape(rows_count, groups, -1),
        preferred_element_type=jnp.float32,
    ).reshape(groups * model_width, -1)
    arr_up = jnp.einsum(
        "td,tes->eds",
        rows_group,
        up_grad_s.reshape(rows_count, groups, -1),
        preferred_element_type=jnp.float32,
    ).reshape(groups * model_width, -1)
    arr_down = jnp.einsum(
        "tes,tcd->ecsd",
        shared_hidden.reshape(rows_count, groups, -1),
        grads_group.reshape(rows_count, parts_cd, -1),
        preferred_element_type=jnp.float32,
    ).reshape(-1, model_width // parts_cd)
    sums_gate, sums_up, sums_down = (
        lax.psum_scatter(arr_gate, (EXP, CTX, DP), scatter_dimension=0, tiled=True),
        lax.psum_scatter(arr_up, (EXP, CTX, DP), scatter_dimension=0, tiled=True),
        lax.psum_scatter(arr_down, (EXP, CTX, DP), scatter_dimension=0, tiled=True),
    )
    norm_grad = norm_grad + shared_rows_grad
    residual_grad, grad_gain_two = norm_back(residual, inv_two, g_two, norm_grad)
    residual_grad = residual_grad + cot_rows
    low_residual = residual_grad.astype(jnp.bfloat16)
    grad_out_w = jnp.dot(attended.T, low_residual, preferred_element_type=jnp.float32)
    attended_grad = jnp.dot(low_residual, out_w.T, preferred_element_type=jnp.float32).astype(
        jnp.bfloat16
    )
    head_q_grad, head_k_grad, head_v_grad = lax.map(
        partial(attend_back, allowed=allowed, scale_factor=scale_factor),
        (head_q, head_k, head_v, to_heads(attended_grad), log_total),
    )
    key_sum, value_sum = (
        lax.psum_scatter(from_heads(head_k_grad), CTX, scatter_dimension=0, tiled=True),
        lax.psum_scatter(from_heads(head_v_grad), CTX, scatter_dimension=0, tiled=True),
    )
    query_low = from_heads(head_q_grad).astype(jnp.bfloat16)
    key_low = key_sum.astype(jnp.bfloat16)
    value_low = value_sum.astype(jnp.bfloat16)
    grad_query = jnp.dot(normed_one.T, query_low, preferred_element_type=jnp.float32)
    grad_key = jnp.dot(normed_one.T, key_low, preferred_element_type=jnp.float32)
    grad_value = jnp.dot(normed_one.T, value_low, preferred_element_type=jnp.float32)
    normed_grad = jnp.dot(query_low, query_w.T, preferred_element_type=jnp.float32)
    normed_grad = normed_grad + jnp.dot(key_low, key_w.T, preferred_element_type=jnp.float32)
    normed_grad = normed_grad + jnp.dot(value_low, value_w.T, preferred_element_type=jnp.float32)
    input_part, grad_gain_one = norm_back(x_rows, inv_one, g_one, normed_grad)
    input_grad = (residual_grad + input_part).astype(jnp.bfloat16)
    dense = (
        lax.psum_scatter(
            grad_gain_one, (EXP, CTX, DP), scatter_dimension=0, tiled=True
        ),
        lax.psum_scatter(grad_query, (EXP, CTX, DP), scatter_dimension=0, tiled=True),
        lax.psum_scatter(grad_key, (EXP, CTX, DP), scatter_dimension=0, tiled=True),
        lax.psum_scatter(grad_value, (EXP, CTX, DP), scatter_dimension=0, tiled=True),
        lax.psum_scatter(grad_out_w, (EXP, CTX, DP), scatter_dimension=0, tiled=True),
        lax.psum_scatter(
            grad_gain_two, (EXP, CTX, DP), scatter_dimension=0, tiled=True
        ),
        lax.psum_scatter(
            grad_router, (EXP, CTX, DP), scatter_dimension=0, tiled=True
        ),
        lax.psum_scatter(
            grad_gate_vec, (EXP, CTX, DP), scatter_dimension=0, tiled=True
        ),
    )
    return (
        output[None],
        input_grad[None],
        dense[0],
        dense[1],
        dense[2],
        dense[3],
        dense[4],
        dense[5],
        dense[6],
        dense[7],
        sums_gate,
        sums_up,
        sums_down,
        expert_sums[0],
        expert_sums[1],
        expert_sums[2],
    )

def attention_probs(q_blk, k_part, q_code, k_code, first_row, scale_factor):
    scores = lax.dot_general(
        q_blk, k_part, (((1,), (1,)), ((), ())), preferred_element_type=jnp.float32
    )
    row = first_row + lax.broadcasted_iota(jnp.int32, scores.shape, 0)
    col = lax.broadcasted_iota(jnp.int32, scores.shape, 1)
    allowed = ((col < row) & (k_code == q_code)) | (col == row)
    logits = jnp.where(allowed, scores * scale_factor, NEG)
    exp_scores = jnp.exp(logits - jnp.max(logits, axis=1, keepdims=True))
    return exp_scores * (1.0 / jnp.sum(exp_scores, axis=1, keepdims=True))


def attend_kernel(heads, step, qkv_ref, q_code_ref, k_code_ref, out_ref):
    seq_len = qkv_ref.shape[0]
    width = heads * HEAD_DIM
    for head in range(heads):
        at = head * HEAD_DIM
        for first in range(0, seq_len, step):
            upto = first + step
            probs = attention_probs(
                qkv_ref[first:upto, at : at + HEAD_DIM],
                qkv_ref[0:upto, width + at : width + at + HEAD_DIM],
                q_code_ref[first:upto, :],
                k_code_ref[0, :, 0:upto],
                first,
                HEAD_DIM**-0.5,
            )
            out_ref[first:upto, at : at + HEAD_DIM] = jnp.dot(
                probs.astype(jnp.bfloat16),
                qkv_ref[0:upto, 2 * width + at : 2 * width + at + HEAD_DIM],
                preferred_element_type=jnp.float32,
            ).astype(jnp.bfloat16)


def attend_back_kernel(
    heads, step, qkv_ref, grad_ref, q_code_ref, k_code_ref, out_ref, key_acc, value_acc
):
    seq_len = qkv_ref.shape[0]
    width = heads * HEAD_DIM
    for head in range(heads):
        at = head * HEAD_DIM
        key_at, value_at = width + at, 2 * width + at
        key_acc[...] = jnp.zeros_like(key_acc)
        value_acc[...] = jnp.zeros_like(value_acc)
        for first in range(0, seq_len, step):
            upto = first + step
            q_blk = qkv_ref[first:upto, at : at + HEAD_DIM]
            k_part = qkv_ref[0:upto, key_at : key_at + HEAD_DIM]
            v_part = qkv_ref[0:upto, value_at : value_at + HEAD_DIM]
            g_blk = grad_ref[first:upto, at : at + HEAD_DIM]
            probs = attention_probs(
                q_blk,
                k_part,
                q_code_ref[first:upto, :],
                k_code_ref[0, :, 0:upto],
                first,
                HEAD_DIM**-0.5,
            )
            prob_grad = lax.dot_general(
                g_blk, v_part, (((1,), (1,)), ((), ())), preferred_element_type=jnp.float32
            )
            inner = jnp.sum(probs * prob_grad, axis=1, keepdims=True)
            score_grad = (probs * (prob_grad - inner) * HEAD_DIM**-0.5).astype(jnp.bfloat16)
            out_ref[first:upto, at : at + HEAD_DIM] = jnp.dot(
                score_grad, k_part, preferred_element_type=jnp.float32
            ).astype(jnp.bfloat16)
            key_acc[0:upto, :] += lax.dot_general(
                score_grad, q_blk, (((0,), (0,)), ((), ())), preferred_element_type=jnp.float32
            )
            value_acc[0:upto, :] += lax.dot_general(
                probs.astype(jnp.bfloat16),
                g_blk,
                (((0,), (0,)), ((), ())),
                preferred_element_type=jnp.float32,
            )
        out_ref[:, key_at : key_at + HEAD_DIM] = key_acc[...].astype(jnp.bfloat16)
        out_ref[:, value_at : value_at + HEAD_DIM] = value_acc[...].astype(jnp.bfloat16)


def attention_call(qkv, grads, q_codes, k_codes, seq_len):
    rows, triple = qkv.shape
    width = triple // 3
    heads = width // HEAD_DIM
    step = min(256, seq_len)
    specs = [pl.BlockSpec((seq_len, triple), lambda s: (s, 0))]
    operands = [qkv]
    if grads is not None:
        specs.append(pl.BlockSpec((seq_len, width), lambda s: (s, 0)))
        operands.append(grads)
    specs += [
        pl.BlockSpec((seq_len, 1), lambda s: (s, 0)),
        pl.BlockSpec((1, 1, seq_len), lambda s: (s, 0, 0)),
    ]
    operands += [q_codes, k_codes]
    out_width = width if grads is None else triple
    body = attend_kernel if grads is None else attend_back_kernel
    passes = 2 if grads is None else 5
    area = rows * seq_len * heads
    return pl.pallas_call(
        partial(body, heads, step),
        grid=(rows // seq_len,),
        in_specs=specs,
        out_specs=pl.BlockSpec((seq_len, out_width), lambda s: (s, 0)),
        out_shape=jax.ShapeDtypeStruct((rows, out_width), jnp.bfloat16),
        scratch_shapes=[]
        if grads is None
        else [pltpu.VMEM((seq_len, HEAD_DIM), jnp.float32)] * 2,
        compiler_params=pltpu.CompilerParams(vmem_limit_bytes=48 * 2**20),
        cost_estimate=pl.CostEstimate(
            flops=2 * passes * area * HEAD_DIM,
            bytes_accessed=2 * rows * (triple + out_width),
            transcendentals=area,
        ),
    )(*operands)


MESH_ID = pl.DeviceIdType.MESH


def other_in_pair(index, bit):
    return index + bit - 2 * bit * (lax.div(index, bit) % 2)


def plane_places():
    at = lax.axis_index(EXP)
    core = lax.axis_index(CTX)
    across, along = other_in_pair(at, 1), other_in_pair(at, 2)
    return at, core, across, along, other_in_pair(along, 1)


def greet(across, along, core):
    barrier = pltpu.get_barrier_semaphore()
    for target in ({EXP: across}, {EXP: along}, {CTX: 1 - core}):
        pl.semaphore_signal(barrier, inc=1, device_id=target, device_id_type=MESH_ID)
    pl.semaphore_wait(barrier, 3)


def plane_gather_kernel(with_info, relative, *refs):
    if with_info:
        own_ref, info_ref, all_ref, info_all_ref, send_sem, recv_sem, local_sem = refs
    else:
        own_ref, all_ref, send_sem, recv_sem, local_sem = refs
    at, core, across, along, far = plane_places()
    rows = own_ref.shape[0]
    half = rows // 2
    top, bottom, whole = pl.ds(0, half), pl.ds(half, half), pl.ds(0, rows)
    greet(across, along, core)
    started = []
    twin_id = {CTX: 1 - core}

    def slot_of(place, shift, for_twin):
        if relative:
            return shift + 4 * for_twin
        return place * 2 + core

    def send(number, src, dst, target):
        copy = pltpu.make_async_remote_copy(
            src_ref=src,
            dst_ref=dst,
            send_sem=send_sem.at[number],
            recv_sem=recv_sem.at[number],
            device_id=target,
            device_id_type=MESH_ID,
        )
        copy.start()
        started.append(copy)
        return copy

    def piece(place, shift, part, for_twin=0):
        return all_ref.at[slot_of(place, shift, for_twin), part]

    x_top = send(0, own_ref.at[top], piece(at, 1, top), {EXP: across})
    y_bottom = send(1, own_ref.at[bottom], piece(at, 2, bottom), {EXP: along})
    x_bottom = send(2, own_ref.at[bottom], piece(at, 1, bottom), {EXP: across})
    y_top = send(3, own_ref.at[top], piece(at, 2, top), {EXP: along})
    twins = [send(4, own_ref, piece(at, 0, whole, 1), twin_id)]
    heres = [pltpu.make_async_copy(own_ref, piece(at, 0, whole), local_sem.at[0])]
    heres[0].start()
    if with_info:
        info_at = lambda place: info_all_ref.at[place * 2 + core]
        heres.append(pltpu.make_async_copy(info_ref, info_at(at), local_sem.at[1]))
        heres[1].start()
        info_x = send(13, info_ref, info_at(at), {EXP: across})
        info_y = send(14, info_ref, info_at(at), {EXP: along})
        twins.append(send(15, info_ref, info_at(at), twin_id))
        info_x.wait_recv()
        info_far = send(16, info_at(across), info_at(across), {EXP: along})
        twins.append(send(17, info_at(across), info_at(across), twin_id))
        info_y.wait_recv()
        twins.append(send(18, info_at(along), info_at(along), twin_id))
        info_far.wait_recv()
        twins.append(send(19, info_at(far), info_at(far), twin_id))

    def hand_on(number, place, shift, part):
        src = piece(place, shift, part)
        twins.append(send(number, src, piece(place, shift, part, 1), twin_id))

    x_top.wait_recv()
    far_top = send(5, piece(across, 1, top), piece(across, 3, top), {EXP: along})
    hand_on(6, across, 1, top)
    y_bottom.wait_recv()
    far_bottom = send(7, piece(along, 2, bottom), piece(along, 3, bottom), {EXP: across})
    hand_on(8, along, 2, bottom)
    x_bottom.wait_recv()
    hand_on(9, across, 1, bottom)
    y_top.wait_recv()
    hand_on(10, along, 2, top)
    far_top.wait_recv()
    hand_on(11, far, 3, top)
    far_bottom.wait_recv()
    hand_on(12, far, 3, bottom)
    for copy in twins:
        copy.wait_recv()
    for copy in started:
        copy.wait_send()
    for copy in heres:
        copy.wait()


def plane_gather(own, info, relative, number):
    plane = lax.axis_size(PLANE)
    operands = [own] if info is None else [own, info]
    outs = [jax.ShapeDtypeStruct((plane, *v.shape), v.dtype) for v in operands]
    anywhere = pl.BlockSpec(memory_space=pl.ANY)
    return pl.pallas_call(
        partial(plane_gather_kernel, info is not None, relative),
        out_shape=outs,
        in_specs=[anywhere] * len(operands),
        out_specs=[anywhere] * len(operands),
        scratch_shapes=[
            pltpu.SemaphoreType.DMA((20,)),
            pltpu.SemaphoreType.DMA((20,)),
            pltpu.SemaphoreType.DMA((2,)),
        ],
        compiler_params=pltpu.CompilerParams(collective_id=number, has_side_effects=True),
        cost_estimate=pl.CostEstimate(
            flops=0, bytes_accessed=own.size, transcendentals=0
        ),
    )(*operands)


def norm_qkv_kernel(hidden_ref, gain_ref, w_ref, norm_ref, qkv_ref):
    values = hidden_ref[...].astype(jnp.float32)
    inv = lax.rsqrt(jnp.mean(values * values, axis=1, keepdims=True) + EPS)
    norm_ref[...] = low(values * inv * gain_ref[...])
    qkv_ref[...] = low(mm(norm_ref[...], w_ref[...]))


def norm_qkv(hidden, gain, w, block):
    rows, width = hidden.shape
    cols = w.shape[1]
    return pl.pallas_call(
        norm_qkv_kernel,
        grid=(rows // block,),
        in_specs=[
            pl.BlockSpec((block, width), lambda i: (i, 0)),
            pl.BlockSpec((1, width), lambda i: (0, 0)),
            pl.BlockSpec((width, cols), lambda i: (0, 0)),
        ],
        out_specs=[
            pl.BlockSpec((block, width), lambda i: (i, 0)),
            pl.BlockSpec((block, cols), lambda i: (i, 0)),
        ],
        out_shape=[
            jax.ShapeDtypeStruct((rows, width), jnp.bfloat16),
            jax.ShapeDtypeStruct((rows, cols), jnp.bfloat16),
        ],
        compiler_params=pltpu.CompilerParams(vmem_limit_bytes=48 * 2**20),
        cost_estimate=pl.CostEstimate(
            flops=2 * rows * width * cols,
            bytes_accessed=4 * rows * width,
            transcendentals=0,
        ),
    )(hidden, gain, w)


def chosen_rows(slots, capacity):
    lanes = lax.broadcasted_iota(jnp.int32, (slots.shape[0], capacity), 1)
    return (slots == lanes).astype(jnp.bfloat16)


def hand_out(step_at, half, blocks, out_refs, sems):
    copies = [
        pltpu.make_async_copy(blocks.at[k], out_refs[k], sems.at[k]) for k in range(half)
    ]
    for k in range(half):

        @pl.when(step_at == half + k)
        def _():
            copies[k].start()

    @pl.when(step_at == 2 * half - 1)
    def _():
        for copy in copies:
            copy.wait()


def output_kernel(
    half,
    hidden_ref,
    down_ref,
    rows_ref,
    slot_ref,
    sg_ref,
    gate_ref,
    cot_ref,
    *refs,
):
    near_refs, dots_ref, refs = refs[:half], refs[half], refs[half + 1 :]
    given, got, send_sem, recv_sem, out_sem = refs
    step_at = pl.program_id(0)
    is_far = step_at < half
    slot = lax.rem(step_at, half)
    twin_id = {CTX: 1 - lax.axis_index(CTX)}

    @pl.when(step_at == 0)
    def _():
        barrier = pltpu.get_barrier_semaphore()
        pl.semaphore_signal(barrier, inc=1, device_id=twin_id, device_id_type=MESH_ID)
        pl.semaphore_wait(barrier, 1)

    def block_copy(k):
        return pltpu.make_async_remote_copy(
            src_ref=given.at[k],
            dst_ref=got.at[k],
            send_sem=send_sem.at[k],
            recv_sem=recv_sem.at[k],
            device_id=twin_id,
            device_id_type=MESH_ID,
        )

    def make(store):
        chosen = chosen_rows(slot_ref[...], rows_ref.shape[1])
        hidden = hidden_ref[...].T
        tokens, width = cot_ref.shape
        step, lanes = 512, 128
        gate_dot = jnp.zeros((tokens, lanes), jnp.float32)
        shared_dot = jnp.zeros((tokens, lanes), jnp.float32)
        for first in range(0, width, step):
            cols = pl.ds(first, step)
            shared = mm(hidden, down_ref[:, cols])
            picked = mm(chosen, rows_ref[0, :, cols])
            cot = cot_ref[:, cols].astype(jnp.float32)
            gate_part, shared_part = picked * cot, shared * cot
            for at in range(0, step, lanes):
                gate_dot += gate_part[:, at : at + lanes]
                shared_dot += shared_part[:, at : at + lanes]
            store(cols, sg_ref[...] * shared + gate_ref[...] * picked)
        lane = lax.broadcasted_iota(jnp.int32, dots_ref.shape, 1)
        gate_dot = jnp.sum(gate_dot, axis=1, keepdims=True)
        shared_dot = jnp.sum(shared_dot, axis=1, keepdims=True)
        dots_ref[...] = jnp.where(lane == 0, gate_dot, jnp.where(lane == 1, shared_dot, 0.0))

    @pl.when(is_far)
    def _():
        def store(cols, total):
            given[slot, :, cols] = low(total)

        make(store)
        block_copy(slot).start()

    @pl.when(jnp.logical_not(is_far))
    def _():
        block_copy(slot).wait_recv()

        def store(cols, total):
            got[slot, :, cols] = low(total + got[slot, :, cols].astype(jnp.float32))

        make(store)

    hand_out(step_at, half, got, near_refs, out_sem)

    @pl.when(step_at == 2 * half - 1)
    def _():
        for k in range(half):
            block_copy(k).wait_send()


def output_parts(hidden, down, rows, slots, sg, gates, cot):
    blocks, capacity, width = rows.shape
    units, count = hidden.shape
    tokens, half = count // blocks, blocks // 2
    at = lambda i: lax.rem(i + half, blocks)
    column = pl.BlockSpec((tokens, 1), lambda i: (at(i), 0))
    return pl.pallas_call(
        partial(output_kernel, half),
        grid=(blocks,),
        in_specs=[
            pl.BlockSpec((units, tokens), lambda i: (0, at(i))),
            pl.BlockSpec((units, width), lambda i: (0, 0)),
            pl.BlockSpec((1, capacity, width), lambda i: (at(i), 0, 0)),
            column,
            column,
            column,
            pl.BlockSpec((tokens, width), lambda i: (at(i), 0)),
        ],
        out_specs=[
            *[pl.BlockSpec(memory_space=pl.ANY)] * half,
            pl.BlockSpec((tokens, 128), lambda i: (at(i), 0)),
        ],
        out_shape=[
            *[jax.ShapeDtypeStruct((tokens, width), jnp.bfloat16)] * half,
            jax.ShapeDtypeStruct((count, 128), jnp.float32),
        ],
        scratch_shapes=[
            pltpu.VMEM((half, tokens, width), jnp.bfloat16),
            pltpu.VMEM((half, tokens, width), jnp.bfloat16),
            pltpu.SemaphoreType.DMA((half,)),
            pltpu.SemaphoreType.DMA((half,)),
            pltpu.SemaphoreType.DMA((half,)),
        ],
        compiler_params=pltpu.CompilerParams(
            collective_id=4, has_side_effects=True, vmem_limit_bytes=56 * 2**20
        ),
        cost_estimate=pl.CostEstimate(
            flops=2 * count * width * (units + capacity),
            bytes_accessed=6 * count * width,
            transcendentals=0,
        ),
    )(hidden, down, rows, slots, sg, gates, cot)


def scatter_step(compute, out_ref, scratch):
    given, total, x_got, y_got, x_last, y_last, send_sem, recv_sem = scratch
    at, core, across, along, far = plane_places()
    step_at = pl.program_id(0)
    row = step_at // 2
    is_twin = step_at % 2 == 0
    rows = total.shape[1]
    half = rows // 2
    top, bottom = pl.ds(0, half), pl.ds(half, half)

    def copy_of(number, src, dst, target):
        return pltpu.make_async_remote_copy(
            src_ref=src,
            dst_ref=dst,
            send_sem=send_sem.at[number],
            recv_sem=recv_sem.at[number],
            device_id=target,
            device_id_type=MESH_ID,
        )

    def twin_copy(k):
        return copy_of(k, given.at[k % 2], total.at[k], {CTX: 1 - core})

    far_x = copy_of(4, total.at[0, top], x_got.at[0], {EXP: across})
    far_y = copy_of(5, total.at[0, bottom], y_got.at[0], {EXP: along})
    own_x = copy_of(6, total.at[1, top], x_got.at[1], {EXP: across})
    own_y = copy_of(7, total.at[2, bottom], y_got.at[1], {EXP: along})
    last_y = copy_of(8, total.at[2, top], y_last, {EXP: along})
    last_x = copy_of(9, total.at[1, bottom], x_last, {EXP: across})

    @pl.when(step_at == 0)
    def _():
        greet(across, along, core)

    @pl.when(is_twin)
    def _():
        @pl.when(row >= 2)
        def _():
            twin_copy(row - 2).wait_send()

        def store(cols, values):
            given[row % 2, :, cols] = low(values)

        compute(store)
        twin_copy(row).start()

    @pl.when(jnp.logical_not(is_twin))
    def _():
        twin_copy(row).wait_recv()

        def store(cols, values):
            total[row, :, cols] = low(values + total[row, :, cols].astype(jnp.float32))

        compute(store)

    @pl.when(step_at == 1)
    def _():
        far_x.start()
        far_y.start()

    @pl.when(step_at == 3)
    def _():
        own_x.start()

    @pl.when(step_at == 5)
    def _():
        own_y.start()

    @pl.when(step_at == 7)
    def _():
        def add_half(k, first, got):
            @pl.loop(0, half // 64)
            def _(i):
                take = pl.ds(pl.multiple_of(i * 64, 64), 64)
                into = pl.ds(pl.multiple_of(first + i * 64, 64), 64)
                total[k, into] = low(
                    total[k, into].astype(jnp.float32) + got[0, take].astype(jnp.float32)
                )

        def finish(first, near, later):
            @pl.loop(0, half // 64)
            def _(i):
                take = pl.ds(pl.multiple_of(i * 64, 64), 64)
                into = pl.ds(pl.multiple_of(first + i * 64, 64), 64)
                out_ref[into] = (
                    total[3, into].astype(jnp.float32)
                    + near[1, take].astype(jnp.float32)
                    + later[take].astype(jnp.float32)
                )

        far_x.wait_recv()
        add_half(2, 0, x_got)
        last_y.start()
        far_y.wait_recv()
        add_half(1, half, y_got)
        last_x.start()
        own_x.wait_recv()
        last_y.wait_recv()
        finish(0, x_got, y_last)
        own_y.wait_recv()
        last_x.wait_recv()
        finish(half, y_got, x_last)
        for copy in (twin_copy(2), twin_copy(3), far_x, far_y, own_x, own_y, last_y, last_x):
            copy.wait_send()


def step_slot(i):
    row = i // 2
    shift = jnp.where(row == 0, 3, jnp.where(row == 3, 0, row))
    return shift + 4 * (1 - i % 2)


def scatter_scratch(tokens, width):
    vmem = lambda *shape: pltpu.VMEM(shape, jnp.bfloat16)
    return [
        vmem(2, tokens, width),
        vmem(4, tokens, width),
        vmem(2, tokens // 2, width),
        vmem(2, tokens // 2, width),
        vmem(tokens // 2, width),
        vmem(tokens // 2, width),
        pltpu.SemaphoreType.DMA((10,)),
        pltpu.SemaphoreType.DMA((10,)),
    ]


def n2_grad_kernel(dgate_ref, dup_ref, gate_ref, up_ref, rows_ref, slot_ref, out_ref, *scratch):
    def compute(store):
        chosen = chosen_rows(slot_ref[...], rows_ref.shape[1])
        dgate, dup = dgate_ref[...].T, dup_ref[...].T
        step = 512
        for first in range(0, gate_ref.shape[1], step):
            cols = pl.ds(first, step)
            total = mm(dgate, gate_ref[:, cols]) + mm(dup, up_ref[:, cols])
            store(cols, total + mm(chosen, rows_ref[0, :, cols]))

    scatter_step(compute, out_ref, scratch)


def n2_grad_sum(dgate, dup, gate_w, up_w, rows, slots):
    blocks, capacity, width = rows.shape
    units, count = dgate.shape
    tokens = count // blocks
    by_units = pl.BlockSpec((units, tokens), lambda i: (0, step_slot(i)))
    whole = pl.BlockSpec((units, width), lambda i: (0, 0), pipeline_mode=pl.Buffered(1))
    return pl.pallas_call(
        n2_grad_kernel,
        grid=(blocks,),
        in_specs=[
            by_units,
            by_units,
            whole,
            whole,
            pl.BlockSpec((1, capacity, width), lambda i: (step_slot(i), 0, 0)),
            pl.BlockSpec((tokens, 1), lambda i: (step_slot(i), 0)),
        ],
        out_specs=pl.BlockSpec((tokens, width), lambda i: (0, 0)),
        out_shape=jax.ShapeDtypeStruct((tokens, width), jnp.float32),
        scratch_shapes=scatter_scratch(tokens, width),
        compiler_params=pltpu.CompilerParams(
            collective_id=3, has_side_effects=True, vmem_limit_bytes=56 * 2**20
        ),
        cost_estimate=pl.CostEstimate(
            flops=2 * count * width * (2 * units + capacity),
            bytes_accessed=4 * count * width,
            transcendentals=0,
        ),
    )(dgate, dup, gate_w, up_w, rows, slots)


def unit_grad_kernel(hid_ref, dgate_ref, dup_ref, cot_ref, n2_ref, out_ref):
    units = hid_ref.shape[0]
    out_ref[0, :units] = low(mm(hid_ref[...], cot_ref[...]))
    out_ref[0, units : 2 * units] = low(mm(dgate_ref[...], n2_ref[...]))
    out_ref[0, 2 * units :] = low(mm(dup_ref[...], n2_ref[...]))


def unit_grads(hidden, dgate, dup, cots, n2, depth, halves):
    units, count = hidden.shape
    width = n2.shape[1]
    cols = width // (depth * halves)
    whole = pl.BlockSpec((units, count), lambda i: (0, 0), pipeline_mode=pl.Buffered(1))
    strip = pl.BlockSpec((count, cols), lambda i: (0, i))
    return pl.pallas_call(
        unit_grad_kernel,
        grid=(depth * halves,),
        in_specs=[whole, whole, whole, strip, strip],
        out_specs=pl.BlockSpec(
            (1, 3 * units, cols), lambda i: (lax.rem(i, depth), 0, i // depth)
        ),
        out_shape=jax.ShapeDtypeStruct((depth, 3 * units, halves * cols), jnp.bfloat16),
        compiler_params=pltpu.CompilerParams(vmem_limit_bytes=48 * 2**20),
        cost_estimate=pl.CostEstimate(
            flops=6 * units * count * width,
            bytes_accessed=2 * (3 * units * count + 2 * count * width + 3 * units * width),
            transcendentals=0,
        ),
    )(hidden, dgate, dup, cots, n2)


def n1_grad_kernel(half, grads_ref, w_ref, *refs):
    near_refs, refs = refs[:half], refs[half:]
    rows_in, given, got, load_sem, send_sem, recv_sem, out_sem = refs
    place, core = lax.axis_index(EXP), lax.axis_index(CTX)
    step_at = pl.program_id(0)
    is_far = step_at < half
    slot = lax.rem(step_at, half)
    tokens = rows_in.shape[1]
    twin_id = {CTX: 1 - core}

    def load(step, k):
        column, level = place % 2, place // 2
        there = (column + k % 2) % 2 + 2 * ((level + k // 2) % 2)
        owner = 1 - core if step < half else core
        first = pl.multiple_of((there * 2 + owner) * tokens, tokens)
        return pltpu.make_async_copy(
            grads_ref.at[pl.ds(first, tokens)], rows_in.at[step], load_sem.at[step]
        )

    loads = [load(step, step % half) for step in range(2 * half)]

    @pl.when(step_at == 0)
    def _():
        for copy in loads:
            copy.start()
        barrier = pltpu.get_barrier_semaphore()
        pl.semaphore_signal(barrier, inc=1, device_id=twin_id, device_id_type=MESH_ID)
        pl.semaphore_wait(barrier, 1)

    for step in range(2 * half):

        @pl.when(step_at == step)
        def _():
            loads[step].wait()

    def block_copy(k):
        return pltpu.make_async_remote_copy(
            src_ref=given.at[k],
            dst_ref=got.at[k],
            send_sem=send_sem.at[k],
            recv_sem=recv_sem.at[k],
            device_id=twin_id,
            device_id_type=MESH_ID,
        )

    def make(store):
        step = 512
        for first in range(0, w_ref.shape[0], step):
            cols = pl.ds(first, step)
            store(cols, mm(rows_in[step_at], w_ref[cols, :], ((1,), (1,))))

    @pl.when(is_far)
    def _():
        def store(cols, total):
            given[slot, :, cols] = low(total)

        make(store)
        block_copy(slot).start()

    @pl.when(jnp.logical_not(is_far))
    def _():
        block_copy(slot).wait_recv()

        def store(cols, total):
            got[slot, :, cols] = low(total + got[slot, :, cols].astype(jnp.float32))

        make(store)

    hand_out(step_at, half, got, near_refs, out_sem)

    @pl.when(step_at == 2 * half - 1)
    def _():
        for k in range(half):
            block_copy(k).wait_send()


def n1_grad_parts(grads, w, blocks):
    rows, cols = grads.shape
    width = w.shape[0]
    tokens, half = rows // blocks, blocks // 2
    return pl.pallas_call(
        partial(n1_grad_kernel, half),
        grid=(blocks,),
        in_specs=[
            pl.BlockSpec(memory_space=pl.ANY),
            pl.BlockSpec((width, cols), lambda i: (0, 0)),
        ],
        out_specs=[pl.BlockSpec(memory_space=pl.ANY)] * half,
        out_shape=[jax.ShapeDtypeStruct((tokens, width), jnp.bfloat16)] * half,
        scratch_shapes=[
            pltpu.VMEM((blocks, tokens, cols), jnp.bfloat16),
            pltpu.VMEM((half, tokens, width), jnp.bfloat16),
            pltpu.VMEM((half, tokens, width), jnp.bfloat16),
            pltpu.SemaphoreType.DMA((blocks,)),
            pltpu.SemaphoreType.DMA((half,)),
            pltpu.SemaphoreType.DMA((half,)),
            pltpu.SemaphoreType.DMA((half,)),
        ],
        compiler_params=pltpu.CompilerParams(
            collective_id=1, has_side_effects=True, vmem_limit_bytes=48 * 2**20
        ),
        cost_estimate=pl.CostEstimate(
            flops=2 * rows * width * cols,
            bytes_accessed=4 * rows * width,
            transcendentals=0,
        ),
    )(grads, w)


def after(values, others):
    return lax.optimization_barrier((values, others))[0]


def swap(values, bits):
    return lax.ppermute(values, EXP, [(i, i ^ bits) for i in range(4)])


def twin(values):
    return lax.ppermute(values, CTX, [(0, 1), (1, 0)])


def twin_sums(ours, theirs):
    got = twin(theirs)
    return [low(ours[k].astype(jnp.float32) + got[k].astype(jnp.float32)) for k in range(4)]


def hops(sums):
    return [sums[0]] + [swap(sums[k], k) for k in (1, 2, 3)]


def sum_up(parts):
    return sum(v.astype(jnp.float32) for v in parts)


def mm(left, right, dims=((1,), (0,))):
    return lax.dot_general(left, right, (dims, ((), ())), preferred_element_type=jnp.float32)


def low(values):
    return values.astype(jnp.bfloat16)


def local_plane(
    hidden,
    cotangent,
    segments,
    padding,
    routes,
    order,
    norm1_gain,
    w_query,
    w_key,
    w_value,
    w_out,
    norm2_gain,
    router,
    shared_gate_vec,
    shared_w_gate,
    shared_w_up,
    shared_w_down,
    expert_w_gate,
    expert_w_up,
    expert_w_down,
):
    plane = lax.axis_size(PLANE)
    groups = lax.axis_size(EXP)
    halves = lax.axis_size(CTX)
    depth = lax.axis_size(DP)
    me = lax.axis_index(PLANE)
    core = lax.axis_index(CTX)
    tokens, width = hidden.shape[1], hidden.shape[2]
    all_tokens = plane * tokens
    seq_len = halves * tokens
    experts_all = router.shape[1]
    head_cols = width // plane
    shard = width // depth

    token_info = jnp.concatenate(
        [segments + 1, jnp.where(padding > 0, segments + 1, 0), order[0], routes[0].T]
    )
    info_rows = token_info.shape[0]
    token_info = jnp.concatenate([token_info, jnp.zeros((8 - info_rows, tokens), jnp.int32)])

    hidden_all, info_all = plane_gather(hidden[0], token_info, False, 0)
    hidden_all = hidden_all.reshape(all_tokens, width)
    place = lax.axis_index(EXP)
    away = [(place ^ k) * 2 + (core ^ j) for j in (0, 1) for k in range(4)]
    away = jnp.stack(away)
    out_rows = shard // plane
    w_out_part = lax.dynamic_slice(w_out, (me * out_rows, 0), (out_rows, width))
    w_qkv_part = jnp.concatenate(
        [
            lax.dynamic_slice(w, (0, me * head_cols), (shard, head_cols))
            for w in (w_query, w_key, w_value)
        ]
        + [router, norm1_gain[:, None], norm2_gain[:, None], shared_gate_vec[:, None]]
        + [jnp.zeros((shard, 128 - experts_all - 3), jnp.bfloat16)]
        + [w_out_part.reshape(shard, -1)],
        axis=1,
    )
    w_qkv = lax.all_gather(w_qkv_part, DP, axis=0, tiled=True)
    w_out_part = w_qkv[:, 3 * head_cols + 128 :].reshape(depth, out_rows, width)
    small = w_qkv[:, 3 * head_cols : 3 * head_cols + 128].T
    w_qkv = w_qkv[:, : 3 * head_cols]
    router_t = small[:experts_all]
    g_one = small[experts_all].astype(jnp.float32)
    g_two = small[experts_all + 1].astype(jnp.float32)
    gate_vec = small[experts_all + 2]
    w_out_part = after(w_out_part, info_all)
    w_out_got = [swap(w_out_part, k) for k in (1, 2, 3)]

    def normed(values, gain):
        values = values.astype(jnp.float32)
        inv = lax.rsqrt(jnp.mean(values * values, axis=1, keepdims=True) + EPS)
        return values, inv, low(values * inv * gain)

    n1_all, qkv = norm_qkv(hidden_all, g_one[None], w_qkv, tokens)
    q_codes = info_all[:, 0].reshape(all_tokens, 1)
    k_codes = info_all[:, 1].reshape(all_tokens // seq_len, 1, seq_len)
    attended_cols = attention_call(qkv, None, q_codes, k_codes, seq_len)
    pieces = [w_out_part] + [after(v, attended_cols) for v in w_out_got]
    w_out_near = jnp.zeros((depth, groups, 1, out_rows, width), jnp.bfloat16)
    for k in range(4):
        w_out_near = lax.dynamic_update_slice(
            w_out_near, pieces[k][:, None, None], (0, place ^ k, 0, 0, 0)
        )
    w_out_far = twin(w_out_near)
    w_out_full = jnp.where(
        core == 0,
        jnp.concatenate([w_out_near, w_out_far], axis=2),
        jnp.concatenate([w_out_far, w_out_near], axis=2),
    ).reshape(width, width)

    x_rows, inv_one, _ = normed(hidden[0], g_one)
    cot_rows = cotangent[0].astype(jnp.float32)

    def to_tokens(cols):
        got = lax.all_to_all(
            cols.reshape(plane, tokens, head_cols), PLANE, split_axis=0, concat_axis=0, tiled=True
        )
        return got.transpose(1, 0, 2).reshape(tokens, width)

    def to_columns(rows_in):
        send = rows_in.reshape(tokens, plane, head_cols).transpose(1, 0, 2)
        got = lax.all_to_all(send, PLANE, split_axis=0, concat_axis=0, tiled=True)
        return got.reshape(all_tokens, head_cols)

    attended = to_tokens(attended_cols)
    residual = x_rows + mm(attended, w_out_full)
    residual, inv_two, n2 = normed(residual, g_two)

    units = shared_w_gate.shape[1]
    part = units // (depth * halves)
    pick = lambda w: lax.dynamic_index_in_dim(
        w.reshape(w.shape[0], depth, halves, part), core, axis=2, keepdims=False
    ).reshape(w.shape[0], depth * part)
    sh_gate_up = jnp.concatenate([pick(shared_w_gate), pick(shared_w_up)], axis=1)
    sh_gate_up = lax.all_gather(sh_gate_up, DP, axis=0, tiled=True)
    sh_gate_t, sh_up_t = sh_gate_up[:, : depth * part].T, sh_gate_up[:, depth * part :].T
    sh_down = lax.all_gather(
        lax.dynamic_slice(shared_w_down, (core * part, 0), (part, width)), DP, axis=0, tiled=True
    )
    n2 = after(n2, sh_gate_up)
    n2_all = plane_gather(n2, None, True, 2)[0].reshape(all_tokens, width)
    cot_own = after(cotangent[0], n2_all)
    cot_got = [swap(cot_own, k) for k in (1, 2, 3)]
    ex_gate = lax.all_gather(after(expert_w_gate[0], info_all), DP, axis=0, tiled=True)
    ex_up = lax.all_gather(after(expert_w_up[0], info_all), DP, axis=0, tiled=True)
    ex_down = lax.all_gather(after(expert_w_down[0], info_all), DP, axis=1, tiled=True)

    small_w = jnp.concatenate([router_t, gate_vec[None]])

    def gates_of(rows_in):
        both = mm(rows_in, small_w, ((1,), (1,)))
        z = both[:, :experts_all]
        e = jnp.exp(z - jnp.max(z, axis=1, keepdims=True))
        return e / jnp.sum(e, axis=1, keepdims=True), jax.nn.sigmoid(both[:, experts_all:])

    probs_all, sg_all = gates_of(n2_all)
    expert_gate = lax.dynamic_slice(probs_all, (0, me), (all_tokens, 1))

    capacity = (9 * tokens * TOP + 8 * experts_all - 1) // (8 * experts_all)
    info_away = info_all[away]
    order_all = info_away[:, 2]
    routed_here = jnp.any(info_away[:, 3 : 3 + TOP] == me, axis=1)
    earlier = (order_all[:, None, :] < order_all[:, :, None]) & routed_here[:, None, :]
    slots = jnp.sum(earlier.astype(jnp.int32), axis=2)
    slots = jnp.where(routed_here, slots, capacity)
    chosen = slots[:, None, :] == jnp.arange(capacity, dtype=jnp.int32)[None, :, None]
    onehot = chosen.astype(jnp.bfloat16)

    def rows_of(values):
        got = lax.dot_general(
            onehot,
            values.reshape(plane, tokens, width),
            (((2,), (1,)), ((0,), (0,))),
            preferred_element_type=jnp.float32,
        )
        return got.reshape(plane * capacity, width)

    slot_gates = jnp.sum(
        jnp.where(chosen, expert_gate.reshape(plane, 1, tokens), 0.0), axis=2
    ).reshape(plane * capacity, 1)
    expert_rows = low(rows_of(n2_all))
    gate_pre = mm(sh_gate_t, n2_all, ((1,), (1,)))
    up_pre = mm(sh_up_t, n2_all, ((1,), (1,)))
    gate_act = gate_pre * jax.nn.sigmoid(gate_pre)
    shared_hidden = low(gate_act * up_pre)
    expert_rows = after(expert_rows, (shared_hidden, sh_down))
    gate_e = mm(expert_rows, ex_gate)
    up_e = mm(expert_rows, ex_up)
    act_e = gate_e * jax.nn.sigmoid(gate_e)
    hidden_e = low(act_e * up_e)
    cot_near = jnp.concatenate([cot_own] + [after(v, gate_e) for v in cot_got])
    cot_all = jnp.concatenate([cot_near, twin(cot_near)])
    row_cots = low(rows_of(cot_all))
    row_grads = low(row_cots.astype(jnp.float32) * slot_gates)

    shared_grads = low(sg_all * cot_all.astype(jnp.float32))
    shared_hgrad = mm(sh_down, shared_grads, ((1,), (1,)))
    gate_grad_s = low(shared_hgrad * up_pre * silu_grad(gate_pre))
    up_grad_s = low(shared_hgrad * gate_act)
    rows_out = width // (halves * depth)

    def shared_scatter(total):
        first, second = total[:, :, :rows_out], total[:, :, rows_out:]
        keep = jnp.where(core == 0, first, second)
        got = twin(jnp.where(core == 0, second, first))
        both = [v.reshape(3, depth, part, rows_out) for v in (keep, got)]
        both = jnp.where(core == 0, jnp.stack(both, axis=2), jnp.stack(both[::-1], axis=2))
        return both.reshape(3, units, rows_out).astype(jnp.float32)

    scatter = lambda v, dim: lax.psum_scatter(v, DP, scatter_dimension=dim, tiled=True)
    shared_sums = unit_grads(
        shared_hidden, gate_grad_s, up_grad_s, shared_grads, n2_all, depth, halves
    )
    shared_sums = scatter(shared_sums.reshape(3 * depth * depth * part, -1), 0)
    result_e = low(mm(hidden_e, ex_down))
    hgrad_e = mm(row_grads, ex_down, ((1,), (1,)))
    gate_grad_e = low(hgrad_e * up_e * silu_grad(gate_e))
    up_grad_e = low(hgrad_e * act_e)

    grad_ex_down = low(mm(hidden_e, row_grads, ((0,), (0,))))
    grad_ex_gate = low(mm(expert_rows, gate_grad_e, ((0,), (0,))))
    grad_ex_up = low(mm(expert_rows, up_grad_e, ((0,), (0,))))
    grads_made = (grad_ex_down, grad_ex_gate, grad_ex_up)
    grads = [scatter(v, dim) for v, dim in zip(grads_made, (1, 0, 0))]
    slots = slots.reshape(all_tokens, 1)
    *out_near, dots = output_parts(
        shared_hidden,
        sh_down,
        result_e.reshape(plane, capacity, width),
        after(slots, grads_made),
        sg_all,
        expert_gate,
        cot_all,
    )
    rows_grad = low(
        mm(gate_grad_e, ex_gate, ((1,), (1,))) + mm(up_grad_e, ex_up, ((1,), (1,)))
    )

    out_got = [swap(out_near[k], k) for k in (1, 2)]
    slots, out_got, _ = lax.optimization_barrier((slots, out_got, shared_sums))
    n2_grad = n2_grad_sum(
        gate_grad_s,
        up_grad_s,
        sh_gate_t,
        sh_up_t,
        rows_grad.reshape(plane, capacity, width),
        slots,
    )
    out_far = swap(after(out_near[3], n2_grad), 3)

    dots = dots.reshape(plane, tokens, 128)[:, :, :2].transpose(0, 2, 1)
    back = jnp.arange(plane, dtype=jnp.int32) ^ me
    dots = dots[(back // 2) + 4 * (back % 2)]
    dots = lax.all_to_all(dots, PLANE, split_axis=0, concat_axis=0, tiled=True)
    probs_grad = dots[:, 0].T
    probs, sg = gates_of(n2)
    logit_grad = low(probs * (probs_grad - jnp.sum(probs * probs_grad, axis=1, keepdims=True)))
    sg_logit_grad = low(jnp.sum(dots[:, 1], axis=0)[:, None] * sg * (1.0 - sg))
    n2_grad = (
        n2_grad
        + mm(logit_grad, router_t)
        + sg_logit_grad.astype(jnp.float32) * gate_vec.astype(jnp.float32)[None]
    )
    residual_grad, grad_gain_two = norm_back(residual, inv_two, g_two, n2_grad)
    residual_grad = residual_grad + cot_rows
    low_residual = low(residual_grad)

    attended_grad = low(mm(low_residual, w_out_full, ((1,), (1,))))
    low_residual = after(low_residual, attended_grad)
    out_got = after(out_got, attended_grad)
    output = residual + out_near[0].astype(jnp.float32) + sum_up(out_got)
    attended_grad = to_columns(attended_grad)
    grad_out = low(mm(attended, low_residual, ((0,), (0,))))
    grad_out = grad_out.reshape(groups, halves, width // plane, width)
    block_of = lambda k, c: lax.dynamic_slice(
        grad_out, (place ^ k, c, 0, 0), (1, 1, width // plane, width)
    )[0, 0]
    out_grad_sums = twin_sums(
        [block_of(k, core) for k in range(4)],
        jnp.stack([block_of(k, 1 - core) for k in range(4)]),
    )
    attended_grad = after(attended_grad, (out_grad_sums, output, grads[0]))
    qkv_grad = attention_call(qkv, attended_grad, q_codes, k_codes, seq_len)
    grad_qkv = low(mm(n1_all, qkv_grad, ((0,), (0,))))
    fine = shard // plane
    grad_qkv = (
        grad_qkv.reshape(plane, depth, fine, 3 * head_cols)
        .transpose(1, 0, 2, 3)
        .reshape(width, 3 * head_cols)
    )
    out_grad_got = hops(out_grad_sums)
    qkv_grad = after(qkv_grad, (grad_qkv, grads[1]))
    n1_near = n1_grad_parts(qkv_grad, w_qkv, plane)
    n1_near, out_far, out_grad_got = lax.optimization_barrier((n1_near, out_far, out_grad_got))
    output = low(output + out_far.astype(jnp.float32))
    grad_out = low(sum_up(out_grad_got))
    n1_got = hops(n1_near)
    grad_qkv = lax.psum_scatter(grad_qkv, DP, scatter_dimension=0, tiled=True)
    qkv_sum = grad_qkv
    w_rows = (
        w_qkv.reshape(plane, depth, fine, 3 * head_cols)
        .transpose(1, 0, 2, 3)
        .reshape(depth, plane * fine, 3 * head_cols)
    )
    w_rows = lax.dynamic_index_in_dim(w_rows, lax.axis_index(DP), axis=0, keepdims=False)
    gain_dots = jnp.sum(grad_qkv.astype(jnp.float32) * w_rows.astype(jnp.float32), axis=1)
    gain_dots = lax.all_to_all(
        gain_dots.reshape(plane, 1, fine), PLANE, split_axis=0, concat_axis=0, tiled=True
    )
    my_gain = lax.dynamic_slice(
        g_one, ((me * depth + lax.axis_index(DP)) * fine,), (fine,)
    )
    grad_gain_one = jnp.sum(gain_dots[:, 0], axis=0) / my_gain
    grad_qkv = lax.all_to_all(
        grad_qkv.reshape(plane, fine, 3 * head_cols),
        PLANE,
        split_axis=0,
        concat_axis=0,
        tiled=True,
    )
    grad_qkv = (
        grad_qkv.reshape(plane, fine, 3, head_cols)
        .transpose(2, 1, 0, 3)
        .reshape(3, fine, width)
        .astype(jnp.float32)
    )
    grad_ex_down, grad_ex_gate, grad_ex_up = [
        v.astype(jnp.float32)[None] for v in after(grads, n1_near)
    ]
    grad_out = scatter(after(grad_out, qkv_sum), 0).astype(jnp.float32)
    shared_sums = after(shared_sums, n1_near)
    shared_sums = shared_scatter(shared_sums.reshape(3, units // halves, -1))
    grad_sh_down, grad_sh_gate, grad_sh_up = [shared_sums[k] for k in range(3)]
    grad_sh_gate, grad_sh_up = grad_sh_gate.T, grad_sh_up.T
    dz_all = jnp.concatenate([logit_grad, sg_logit_grad], axis=1)
    dz_all = after(dz_all, n1_near)
    small_grads = mm(n2, dz_all, ((0,), (0,)))
    small_grads = jnp.concatenate([small_grads, grad_gain_two[:, None]], axis=1).T
    small_grads = jnp.pad(small_grads, ((0, 14 - experts_all), (0, 0)))
    small_grads = small_grads.reshape(16, plane, width // plane).transpose(1, 0, 2)
    small_grads = jnp.sum(
        lax.all_to_all(small_grads, PLANE, split_axis=0, concat_axis=0, tiled=True), axis=0
    )
    small_grads = small_grads.reshape(16, depth, shard // plane).transpose(1, 0, 2)
    small_grads = jnp.sum(
        lax.all_to_all(small_grads, DP, split_axis=0, concat_axis=0, tiled=True), axis=0
    )
    n1_grad = sum_up(after(n1_got, qkv_sum))
    input_part, _ = norm_back(x_rows, inv_one, g_one, n1_grad)
    input_grad = low(residual_grad + input_part)
    return (
        output[None],
        input_grad[None],
        grad_gain_one,
        grad_qkv[0],
        grad_qkv[1],
        grad_qkv[2],
        grad_out,
        small_grads[experts_all + 1],
        small_grads[:experts_all].T,
        small_grads[experts_all],
        grad_sh_gate,
        grad_sh_up,
        grad_sh_down,
        grad_ex_gate,
        grad_ex_up,
        grad_ex_down,
    )


def solution(mesh):
    in_specs = (
        P((EXP, DP), CTX, None),
        P((EXP, DP), CTX, None),
        P((EXP, DP), CTX),
        P((EXP, DP), CTX),
        P((EXP, DP), CTX, None),
        P((EXP, DP), CTX, None),
        P(DP),
        P(DP, None),
        P(DP, None),
        P(DP, None),
        P(DP, None),
        P(DP),
        P(DP, None),
        P(DP),
        P(DP, EXP),
        P(DP, EXP),
        P((EXP, DP), None),
        P((EXP, CTX), DP, None),
        P((EXP, CTX), DP, None),
        P((EXP, CTX), None, DP),
    )
    out_specs = (
        P((EXP, DP), CTX, None),
        P((EXP, DP), CTX, None),
        P((EXP, CTX, DP)),
        P((EXP, CTX, DP), None),
        P((EXP, CTX, DP), None),
        P((EXP, CTX, DP), None),
        P((EXP, CTX, DP), None),
        P((EXP, CTX, DP)),
        P((EXP, CTX, DP), None),
        P((EXP, CTX, DP)),
        P((CTX, DP), EXP),
        P((CTX, DP), EXP),
        P(EXP, (CTX, DP)),
        P((EXP, CTX), DP, None),
        P((EXP, CTX), DP, None),
        P((EXP, CTX), None, DP),
    )
    plane = mesh.shape[EXP] * mesh.shape[CTX]

    def run(*args):
        square = mesh.shape[EXP] == 4 and mesh.shape[CTX] == 2 and mesh.shape[DP] == 4
        one_each = square and args[12].shape[1] == plane
        local = local_plane if one_each else local_general
        return jax.shard_map(
            local, mesh=mesh, in_specs=in_specs, out_specs=out_specs, check_vma=False
        )(*args)

    return run
```

```python
from functools import partial

import jax
import jax.numpy as jnp
from jax import lax
from jax.experimental import pallas as pl
from jax.experimental.pallas import tpu as pltpu
from jax.sharding import PartitionSpec as P

EXP, CTX, DP = "experts", "context", "dp"
PLANE = (EXP, CTX)
HEADS = 16
HEAD_DIM = 128
TOP = 4


EPS = 1e-06
NEG = -1e30


def silu_grad(pre_act):
    logistic = jax.nn.sigmoid(pre_act)
    return logistic * (1.0 + pre_act * (1.0 - logistic))


def block_slots(route_row, priority, expert_count):
    matches = (route_row[:, None] == jnp.arange(expert_count, dtype=jnp.int32)[None, :]).astype(
        jnp.int32
    )
    ordered = jnp.zeros_like(matches).at[priority].set(matches)
    before = jnp.cumsum(ordered, axis=0) - ordered
    return jnp.sum(before[priority] * matches, axis=1)


def norm_back(values_in, inv_rms, gain_vec, gradient):
    weighted = gradient * gain_vec
    inner_sum = jnp.mean(weighted * values_in, axis=1, keepdims=True)
    d_value = inv_rms * weighted - values_in * inv_rms**3 * inner_sum
    d_gain = jnp.sum(gradient * values_in * inv_rms, axis=0)
    return (d_value, d_gain)


def attend_head(packed, allowed, scale_factor):
    query_h, key_h, value_h = packed
    raw_scores = jnp.einsum("th,lh->tl", query_h, key_h, preferred_element_type=jnp.float32)
    logits = jnp.where(allowed, raw_scores * scale_factor, NEG)
    row_max = jnp.max(logits, axis=1, keepdims=True)
    exp_scores = jnp.exp(logits - row_max)
    row_total = jnp.sum(exp_scores, axis=1, keepdims=True)
    attn_probs = (exp_scores / row_total).astype(jnp.bfloat16)
    head_out = jnp.dot(attn_probs, value_h, preferred_element_type=jnp.float32).astype(jnp.bfloat16)
    return (head_out, row_max + jnp.log(row_total))


def attend_back(packed, allowed, scale_factor):
    query_h, key_h, value_h, out_grad, log_total = packed
    raw_scores = jnp.einsum("th,lh->tl", query_h, key_h, preferred_element_type=jnp.float32)
    logits = jnp.where(allowed, raw_scores * scale_factor, NEG)
    attn_probs = jnp.exp(logits - log_total)
    prob_grad = jnp.einsum("th,lh->tl", out_grad, value_h, preferred_element_type=jnp.float32)
    inner_sum = jnp.sum(attn_probs * prob_grad, axis=1, keepdims=True)
    score_grad = (attn_probs * (prob_grad - inner_sum) * scale_factor).astype(jnp.bfloat16)
    query_grad = jnp.dot(score_grad, key_h, preferred_element_type=jnp.float32)
    key_grad = jnp.einsum("tl,th->lh", score_grad, query_h, preferred_element_type=jnp.float32)
    value_grad = jnp.einsum(
        "tl,th->lh", attn_probs.astype(jnp.bfloat16), out_grad, preferred_element_type=jnp.float32
    )
    return (query_grad, key_grad, value_grad)


def local_general(
    hidden,
    cotangent,
    segments,
    padding,
    routes,
    order,
    norm1_gain,
    w_query,
    w_key,
    w_value,
    w_out,
    norm2_gain,
    router,
    shared_gate_vec,
    shared_w_gate,
    shared_w_up,
    shared_w_down,
    expert_w_gate,
    expert_w_up,
    expert_w_down,
):
    fetched = (
        lax.all_gather(norm1_gain, DP, axis=0, tiled=True),
        lax.all_gather(w_query, DP, axis=0, tiled=True),
        lax.all_gather(w_key, DP, axis=0, tiled=True),
        lax.all_gather(w_value, DP, axis=0, tiled=True),
        lax.all_gather(w_out, DP, axis=0, tiled=True),
        lax.all_gather(norm2_gain, DP, axis=0, tiled=True),
        lax.all_gather(router, DP, axis=0, tiled=True),
        lax.all_gather(shared_gate_vec, DP, axis=0, tiled=True),
        lax.all_gather(shared_w_gate, DP, axis=0, tiled=True),
        lax.all_gather(shared_w_up, DP, axis=0, tiled=True),
        lax.all_gather(shared_w_down, DP, axis=0, tiled=True),
        lax.all_gather(expert_w_gate, DP, axis=1, tiled=True),
        lax.all_gather(expert_w_up, DP, axis=1, tiled=True),
        lax.all_gather(expert_w_down, DP, axis=2, tiled=True),
    )
    (
        gain_one,
        query_w,
        key_w,
        value_w,
        out_w,
        gain_two,
        router_full,
        gate_vec,
        sh_gate,
        sh_up,
        sh_down,
        ex_gate,
        ex_up,
        ex_down,
    ) = fetched
    sh_gate, sh_up, sh_down = (
        lax.all_gather(sh_gate, EXP, axis=1, tiled=True),
        lax.all_gather(sh_up, EXP, axis=1, tiled=True),
        lax.all_gather(sh_down, EXP, axis=0, tiled=True),
    )
    tokens_here = hidden.shape[1]
    model_width = hidden.shape[2]
    x_rows = hidden[0].astype(jnp.float32)
    cot_rows = cotangent[0].astype(jnp.float32)
    inv_one = lax.rsqrt(jnp.mean(x_rows * x_rows, axis=1, keepdims=True) + EPS)
    g_one = gain_one.astype(jnp.float32)
    normed_one = (x_rows * inv_one * g_one).astype(jnp.bfloat16)
    queries = jnp.dot(normed_one, query_w, preferred_element_type=jnp.float32).astype(jnp.bfloat16)
    keys_own = jnp.dot(normed_one, key_w, preferred_element_type=jnp.float32).astype(jnp.bfloat16)
    values_own = jnp.dot(normed_one, value_w, preferred_element_type=jnp.float32).astype(
        jnp.bfloat16
    )
    own_codes = jnp.where(padding[0] > 0, segments[0] + 1, 0)
    code_parts = jnp.stack([own_codes // 64, own_codes % 64]).astype(jnp.bfloat16)
    keys_all, values_all, parts_all = (
        lax.all_gather(keys_own, CTX, axis=0, tiled=True),
        lax.all_gather(values_own, CTX, axis=0, tiled=True),
        lax.all_gather(code_parts, CTX, axis=1, tiled=True),
    )
    key_codes = parts_all[0].astype(jnp.int32) * 64 + parts_all[1].astype(jnp.int32)
    seq_total = keys_all.shape[0]
    query_pos = lax.axis_index(CTX) * tokens_here + jnp.arange(tokens_here, dtype=jnp.int32)
    key_pos = jnp.arange(seq_total, dtype=jnp.int32)
    same_doc = key_codes[None, :] == (segments[0] + 1)[:, None]
    allowed = (key_pos[None, :] <= query_pos[:, None]) & (
        same_doc | (key_pos[None, :] == query_pos[:, None])
    )
    scale_factor = HEAD_DIM ** (-0.5)

    def to_heads(rows_in):
        return rows_in.reshape(rows_in.shape[0], HEADS, HEAD_DIM).transpose(1, 0, 2)

    def from_heads(heads_in):
        return heads_in.transpose(1, 0, 2).reshape(heads_in.shape[1], model_width)

    head_q = to_heads(queries)
    head_k = to_heads(keys_all)
    head_v = to_heads(values_all)
    head_out, log_total = lax.map(
        partial(attend_head, allowed=allowed, scale_factor=scale_factor), (head_q, head_k, head_v)
    )
    attended = from_heads(head_out)
    residual = x_rows + jnp.dot(attended, out_w, preferred_element_type=jnp.float32)
    inv_two = lax.rsqrt(jnp.mean(residual * residual, axis=1, keepdims=True) + EPS)
    g_two = gain_two.astype(jnp.float32)
    normed_two = (residual * inv_two * g_two).astype(jnp.bfloat16)
    router_logits = jnp.dot(normed_two, router_full, preferred_element_type=jnp.float32)
    router_exp = jnp.exp(router_logits - jnp.max(router_logits, axis=1, keepdims=True))
    router_probs = router_exp / jnp.sum(router_exp, axis=1, keepdims=True)
    route_gates = jnp.take_along_axis(router_probs, routes[0], axis=1)
    shared_gate = jax.nn.sigmoid(jnp.dot(normed_two, gate_vec, preferred_element_type=jnp.float32))
    shared_scaled = (shared_gate[:, None] * cot_rows).astype(jnp.bfloat16)
    rows_group, grads_group = (normed_two, shared_scaled)
    gate_pre = jnp.dot(rows_group, sh_gate, preferred_element_type=jnp.float32)
    up_pre = jnp.dot(rows_group, sh_up, preferred_element_type=jnp.float32)
    gate_act = gate_pre * jax.nn.sigmoid(gate_pre)
    shared_hidden = (gate_act * up_pre).astype(jnp.bfloat16)
    shared_part = jnp.dot(shared_hidden, sh_down, preferred_element_type=jnp.float32)
    experts_all = router_full.shape[1]
    capacity = (9 * tokens_here * TOP + 8 * experts_all - 1) // (8 * experts_all)
    priority = (order[0, 0][:, None] * TOP + jnp.arange(TOP, dtype=jnp.int32)[None, :]).reshape(-1)
    flat_routes = routes[0].reshape(-1)
    slot_index = block_slots(flat_routes, priority, experts_all)
    kept_rows = slot_index < capacity
    target = flat_routes * capacity + jnp.minimum(slot_index, capacity - 1)
    row_gates = route_gates.reshape(-1)
    cot_repeated = jnp.repeat(cot_rows, TOP, axis=0)
    source_rows = jnp.repeat(normed_two, TOP, axis=0)
    source_grads = (cot_repeated * row_gates[:, None]).astype(jnp.bfloat16)
    empty_slots = jnp.zeros((experts_all * capacity, model_width), jnp.bfloat16)
    send_rows = empty_slots.at[target].add(
        jnp.where(kept_rows[:, None], source_rows, jnp.zeros_like(source_rows))
    )
    send_grads = empty_slots.at[target].add(
        jnp.where(kept_rows[:, None], source_grads, jnp.zeros_like(source_grads))
    )
    recv_rows, recv_grads = (
        lax.all_to_all(
            send_rows.reshape(experts_all, capacity, model_width),
            (EXP, CTX),
            split_axis=0,
            concat_axis=0,
            tiled=True,
        ),
        lax.all_to_all(
            send_grads.reshape(experts_all, capacity, model_width),
            (EXP, CTX),
            split_axis=0,
            concat_axis=0,
            tiled=True,
        ),
    )
    local_count = ex_gate.shape[0]
    sources = experts_all // local_count

    def to_local(buffer_in):
        return (
            buffer_in.reshape(sources, local_count, capacity, model_width)
            .transpose(1, 0, 2, 3)
            .reshape(local_count, sources * capacity, model_width)
        )

    def to_owner(buffer_in):
        return (
            buffer_in.reshape(local_count, sources, capacity, model_width)
            .transpose(1, 0, 2, 3)
            .reshape(experts_all, capacity, model_width)
        )

    expert_rows = to_local(recv_rows)
    expert_grads_in = to_local(recv_grads)
    gate_e = jnp.einsum("erd,edf->erf", expert_rows, ex_gate, preferred_element_type=jnp.float32)
    up_e = jnp.einsum("erd,edf->erf", expert_rows, ex_up, preferred_element_type=jnp.float32)
    act_e = gate_e * jax.nn.sigmoid(gate_e)
    hidden_e = (act_e * up_e).astype(jnp.bfloat16)
    result_e = jnp.einsum(
        "erf,efd->erd", hidden_e, ex_down, preferred_element_type=jnp.float32
    ).astype(jnp.bfloat16)
    returned = lax.all_to_all(
        to_owner(result_e), (EXP, CTX), split_axis=0, concat_axis=0, tiled=True
    )
    picked = returned.reshape(experts_all * capacity, model_width)[target]
    picked = jnp.where(kept_rows[:, None], picked, jnp.zeros_like(picked)).astype(jnp.float32)
    routed = jnp.sum((picked * row_gates[:, None]).reshape(tokens_here, TOP, model_width), axis=1)
    output = (residual + shared_gate[:, None] * shared_part + routed).astype(jnp.bfloat16)
    gate_grads = jnp.sum(picked * cot_repeated, axis=1).reshape(tokens_here, TOP)
    hidden_grad_e = jnp.einsum(
        "erd,efd->erf", expert_grads_in, ex_down, preferred_element_type=jnp.float32
    )
    gate_grad_e = (hidden_grad_e * up_e * silu_grad(gate_e)).astype(jnp.bfloat16)
    up_grad_e = (hidden_grad_e * act_e).astype(jnp.bfloat16)
    grad_ex_down = jnp.einsum(
        "erf,erd->efd", hidden_e, expert_grads_in, preferred_element_type=jnp.float32
    )
    grad_ex_gate = jnp.einsum(
        "erd,erf->edf", expert_rows, gate_grad_e, preferred_element_type=jnp.float32
    )
    grad_ex_up = jnp.einsum(
        "erd,erf->edf", expert_rows, up_grad_e, preferred_element_type=jnp.float32
    )
    expert_sums = (
        lax.psum_scatter(grad_ex_gate, DP, scatter_dimension=1, tiled=True),
        lax.psum_scatter(grad_ex_up, DP, scatter_dimension=1, tiled=True),
        lax.psum_scatter(grad_ex_down, DP, scatter_dimension=2, tiled=True),
    )
    rows_grad_e = jnp.einsum(
        "erf,edf->erd", gate_grad_e, ex_gate, preferred_element_type=jnp.float32
    )
    rows_grad_e = (
        rows_grad_e
        + jnp.einsum("erf,edf->erd", up_grad_e, ex_up, preferred_element_type=jnp.float32)
    ).astype(jnp.bfloat16)
    returned_grads = lax.all_to_all(
        to_owner(rows_grad_e), (EXP, CTX), split_axis=0, concat_axis=0, tiled=True
    )
    routed_grad = returned_grads.reshape(experts_all * capacity, model_width)[target]
    routed_grad = jnp.where(kept_rows[:, None], routed_grad, jnp.zeros_like(routed_grad)).astype(
        jnp.float32
    )
    norm_grad = jnp.sum(routed_grad.reshape(tokens_here, TOP, model_width), axis=1)
    choose = (
        routes[0][:, :, None] == jnp.arange(experts_all, dtype=jnp.int32)[None, None, :]
    ).astype(jnp.float32)
    probs_grad = jnp.einsum("tk,tke->te", gate_grads, choose)
    logit_grad = (
        router_probs * (probs_grad - jnp.sum(router_probs * probs_grad, axis=1, keepdims=True))
    ).astype(jnp.bfloat16)
    grad_router = jnp.dot(normed_two.T, logit_grad, preferred_element_type=jnp.float32)
    gate_logit_grad = (
        jnp.sum(cot_rows * shared_part, axis=1) * shared_gate * (1.0 - shared_gate)
    ).astype(jnp.bfloat16)
    grad_gate_vec = jnp.dot(gate_logit_grad, normed_two, preferred_element_type=jnp.float32)
    norm_grad = norm_grad + jnp.dot(logit_grad, router_full.T, preferred_element_type=jnp.float32)
    norm_grad = (
        norm_grad
        + gate_logit_grad.astype(jnp.float32)[:, None] * gate_vec.astype(jnp.float32)[None, :]
    )
    shared_hgrad = jnp.dot(grads_group, sh_down.T, preferred_element_type=jnp.float32)
    gate_grad_s = (shared_hgrad * up_pre * silu_grad(gate_pre)).astype(jnp.bfloat16)
    up_grad_s = (shared_hgrad * gate_act).astype(jnp.bfloat16)
    shared_rows_grad = jnp.dot(gate_grad_s, sh_gate.T, preferred_element_type=jnp.float32)
    shared_rows_grad = shared_rows_grad + jnp.dot(
        up_grad_s, sh_up.T, preferred_element_type=jnp.float32
    )
    groups = lax.axis_size(EXP)
    parts_cd = lax.axis_size((CTX, DP))
    rows_count = rows_group.shape[0]
    arr_gate = jnp.einsum(
        "td,tes->eds",
        rows_group,
        gate_grad_s.reshape(rows_count, groups, -1),
        preferred_element_type=jnp.float32,
    ).reshape(groups * model_width, -1)
    arr_up = jnp.einsum(
        "td,tes->eds",
        rows_group,
        up_grad_s.reshape(rows_count, groups, -1),
        preferred_element_type=jnp.float32,
    ).reshape(groups * model_width, -1)
    arr_down = jnp.einsum(
        "tes,tcd->ecsd",
        shared_hidden.reshape(rows_count, groups, -1),
        grads_group.reshape(rows_count, parts_cd, -1),
        preferred_element_type=jnp.float32,
    ).reshape(-1, model_width // parts_cd)
    sums_gate, sums_up, sums_down = (
        lax.psum_scatter(arr_gate, (EXP, CTX, DP), scatter_dimension=0, tiled=True),
        lax.psum_scatter(arr_up, (EXP, CTX, DP), scatter_dimension=0, tiled=True),
        lax.psum_scatter(arr_down, (EXP, CTX, DP), scatter_dimension=0, tiled=True),
    )
    norm_grad = norm_grad + shared_rows_grad
    residual_grad, grad_gain_two = norm_back(residual, inv_two, g_two, norm_grad)
    residual_grad = residual_grad + cot_rows
    low_residual = residual_grad.astype(jnp.bfloat16)
    grad_out_w = jnp.dot(attended.T, low_residual, preferred_element_type=jnp.float32)
    attended_grad = jnp.dot(low_residual, out_w.T, preferred_element_type=jnp.float32).astype(
        jnp.bfloat16
    )
    head_q_grad, head_k_grad, head_v_grad = lax.map(
        partial(attend_back, allowed=allowed, scale_factor=scale_factor),
        (head_q, head_k, head_v, to_heads(attended_grad), log_total),
    )
    key_sum, value_sum = (
        lax.psum_scatter(from_heads(head_k_grad), CTX, scatter_dimension=0, tiled=True),
        lax.psum_scatter(from_heads(head_v_grad), CTX, scatter_dimension=0, tiled=True),
    )
    query_low = from_heads(head_q_grad).astype(jnp.bfloat16)
    key_low = key_sum.astype(jnp.bfloat16)
    value_low = value_sum.astype(jnp.bfloat16)
    grad_query = jnp.dot(normed_one.T, query_low, preferred_element_type=jnp.float32)
    grad_key = jnp.dot(normed_one.T, key_low, preferred_element_type=jnp.float32)
    grad_value = jnp.dot(normed_one.T, value_low, preferred_element_type=jnp.float32)
    normed_grad = jnp.dot(query_low, query_w.T, preferred_element_type=jnp.float32)
    normed_grad = normed_grad + jnp.dot(key_low, key_w.T, preferred_element_type=jnp.float32)
    normed_grad = normed_grad + jnp.dot(value_low, value_w.T, preferred_element_type=jnp.float32)
    input_part, grad_gain_one = norm_back(x_rows, inv_one, g_one, normed_grad)
    input_grad = (residual_grad + input_part).astype(jnp.bfloat16)
    dense = (
        lax.psum_scatter(
            grad_gain_one, (EXP, CTX, DP), scatter_dimension=0, tiled=True
        ),
        lax.psum_scatter(grad_query, (EXP, CTX, DP), scatter_dimension=0, tiled=True),
        lax.psum_scatter(grad_key, (EXP, CTX, DP), scatter_dimension=0, tiled=True),
        lax.psum_scatter(grad_value, (EXP, CTX, DP), scatter_dimension=0, tiled=True),
        lax.psum_scatter(grad_out_w, (EXP, CTX, DP), scatter_dimension=0, tiled=True),
        lax.psum_scatter(
            grad_gain_two, (EXP, CTX, DP), scatter_dimension=0, tiled=True
        ),
        lax.psum_scatter(
            grad_router, (EXP, CTX, DP), scatter_dimension=0, tiled=True
        ),
        lax.psum_scatter(
            grad_gate_vec, (EXP, CTX, DP), scatter_dimension=0, tiled=True
        ),
    )
    return (
        output[None],
        input_grad[None],
        dense[0],
        dense[1],
        dense[2],
        dense[3],
        dense[4],
        dense[5],
        dense[6],
        dense[7],
        sums_gate,
        sums_up,
        sums_down,
        expert_sums[0],
        expert_sums[1],
        expert_sums[2],
    )

def attention_probs(q_blk, k_part, q_code, k_code, first_row, scale_factor):
    scores = lax.dot_general(
        q_blk, k_part, (((1,), (1,)), ((), ())), preferred_element_type=jnp.float32
    )
    row = first_row + lax.broadcasted_iota(jnp.int32, scores.shape, 0)
    col = lax.broadcasted_iota(jnp.int32, scores.shape, 1)
    allowed = ((col < row) & (k_code == q_code)) | (col == row)
    logits = jnp.where(allowed, scores * scale_factor, NEG)
    exp_scores = jnp.exp(logits - jnp.max(logits, axis=1, keepdims=True))
    return exp_scores * (1.0 / jnp.sum(exp_scores, axis=1, keepdims=True))


def attend_kernel(heads, step, qkv_ref, q_code_ref, k_code_ref, out_ref):
    seq_len = qkv_ref.shape[0]
    width = heads * HEAD_DIM
    for head in range(heads):
        at = head * HEAD_DIM
        for first in range(0, seq_len, step):
            upto = first + step
            probs = attention_probs(
                qkv_ref[first:upto, at : at + HEAD_DIM],
                qkv_ref[0:upto, width + at : width + at + HEAD_DIM],
                q_code_ref[first:upto, :],
                k_code_ref[0, :, 0:upto],
                first,
                HEAD_DIM**-0.5,
            )
            out_ref[first:upto, at : at + HEAD_DIM] = jnp.dot(
                probs.astype(jnp.bfloat16),
                qkv_ref[0:upto, 2 * width + at : 2 * width + at + HEAD_DIM],
                preferred_element_type=jnp.float32,
            ).astype(jnp.bfloat16)


def attend_back_kernel(
    heads, step, qkv_ref, grad_ref, q_code_ref, k_code_ref, out_ref, key_acc, value_acc
):
    seq_len = qkv_ref.shape[0]
    width = heads * HEAD_DIM
    for head in range(heads):
        at = head * HEAD_DIM
        key_at, value_at = width + at, 2 * width + at
        key_acc[...] = jnp.zeros_like(key_acc)
        value_acc[...] = jnp.zeros_like(value_acc)
        for first in range(0, seq_len, step):
            upto = first + step
            q_blk = qkv_ref[first:upto, at : at + HEAD_DIM]
            k_part = qkv_ref[0:upto, key_at : key_at + HEAD_DIM]
            v_part = qkv_ref[0:upto, value_at : value_at + HEAD_DIM]
            g_blk = grad_ref[first:upto, at : at + HEAD_DIM]
            probs = attention_probs(
                q_blk,
                k_part,
                q_code_ref[first:upto, :],
                k_code_ref[0, :, 0:upto],
                first,
                HEAD_DIM**-0.5,
            )
            prob_grad = lax.dot_general(
                g_blk, v_part, (((1,), (1,)), ((), ())), preferred_element_type=jnp.float32
            )
            inner = jnp.sum(probs * prob_grad, axis=1, keepdims=True)
            score_grad = (probs * (prob_grad - inner) * HEAD_DIM**-0.5).astype(jnp.bfloat16)
            out_ref[first:upto, at : at + HEAD_DIM] = jnp.dot(
                score_grad, k_part, preferred_element_type=jnp.float32
            ).astype(jnp.bfloat16)
            key_acc[0:upto, :] += lax.dot_general(
                score_grad, q_blk, (((0,), (0,)), ((), ())), preferred_element_type=jnp.float32
            )
            value_acc[0:upto, :] += lax.dot_general(
                probs.astype(jnp.bfloat16),
                g_blk,
                (((0,), (0,)), ((), ())),
                preferred_element_type=jnp.float32,
            )
        out_ref[:, key_at : key_at + HEAD_DIM] = key_acc[...].astype(jnp.bfloat16)
        out_ref[:, value_at : value_at + HEAD_DIM] = value_acc[...].astype(jnp.bfloat16)


def attention_call(qkv, grads, q_codes, k_codes, seq_len):
    rows, triple = qkv.shape
    width = triple // 3
    heads = width // HEAD_DIM
    step = min(256, seq_len)
    specs = [pl.BlockSpec((seq_len, triple), lambda s: (s, 0))]
    operands = [qkv]
    if grads is not None:
        specs.append(pl.BlockSpec((seq_len, width), lambda s: (s, 0)))
        operands.append(grads)
    specs += [
        pl.BlockSpec((seq_len, 1), lambda s: (s, 0)),
        pl.BlockSpec((1, 1, seq_len), lambda s: (s, 0, 0)),
    ]
    operands += [q_codes, k_codes]
    out_width = width if grads is None else triple
    body = attend_kernel if grads is None else attend_back_kernel
    passes = 2 if grads is None else 5
    area = rows * seq_len * heads
    return pl.pallas_call(
        partial(body, heads, step),
        grid=(rows // seq_len,),
        in_specs=specs,
        out_specs=pl.BlockSpec((seq_len, out_width), lambda s: (s, 0)),
        out_shape=jax.ShapeDtypeStruct((rows, out_width), jnp.bfloat16),
        scratch_shapes=[]
        if grads is None
        else [pltpu.VMEM((seq_len, HEAD_DIM), jnp.float32)] * 2,
        compiler_params=pltpu.CompilerParams(vmem_limit_bytes=48 * 2**20),
        cost_estimate=pl.CostEstimate(
            flops=2 * passes * area * HEAD_DIM,
            bytes_accessed=2 * rows * (triple + out_width),
            transcendentals=area,
        ),
    )(*operands)


MESH_ID = pl.DeviceIdType.MESH


def other_in_pair(index, bit):
    return index + bit - 2 * bit * (lax.div(index, bit) % 2)


def plane_places():
    at = lax.axis_index(EXP)
    core = lax.axis_index(CTX)
    across, along = other_in_pair(at, 1), other_in_pair(at, 2)
    return at, core, across, along, other_in_pair(along, 1)


def greet(across, along, core):
    barrier = pltpu.get_barrier_semaphore()
    for target in ({EXP: across}, {EXP: along}, {CTX: 1 - core}):
        pl.semaphore_signal(barrier, inc=1, device_id=target, device_id_type=MESH_ID)
    pl.semaphore_wait(barrier, 3)


def plane_gather_kernel(with_info, relative, *refs):
    if with_info:
        own_ref, info_ref, all_ref, info_all_ref, send_sem, recv_sem, local_sem = refs
    else:
        own_ref, all_ref, send_sem, recv_sem, local_sem = refs
    at, core, across, along, far = plane_places()
    rows = own_ref.shape[0]
    half = rows // 2
    top, bottom, whole = pl.ds(0, half), pl.ds(half, half), pl.ds(0, rows)
    greet(across, along, core)
    started = []
    twin_id = {CTX: 1 - core}

    def slot_of(place, shift, for_twin):
        if relative:
            return shift + 4 * for_twin
        return place * 2 + core

    def send(number, src, dst, target):
        copy = pltpu.make_async_remote_copy(
            src_ref=src,
            dst_ref=dst,
            send_sem=send_sem.at[number],
            recv_sem=recv_sem.at[number],
            device_id=target,
            device_id_type=MESH_ID,
        )
        copy.start()
        started.append(copy)
        return copy

    def piece(place, shift, part, for_twin=0):
        return all_ref.at[slot_of(place, shift, for_twin), part]

    x_top = send(0, own_ref.at[top], piece(at, 1, top), {EXP: across})
    y_bottom = send(1, own_ref.at[bottom], piece(at, 2, bottom), {EXP: along})
    x_bottom = send(2, own_ref.at[bottom], piece(at, 1, bottom), {EXP: across})
    y_top = send(3, own_ref.at[top], piece(at, 2, top), {EXP: along})
    twins = [send(4, own_ref, piece(at, 0, whole, 1), twin_id)]
    heres = [pltpu.make_async_copy(own_ref, piece(at, 0, whole), local_sem.at[0])]
    heres[0].start()
    if with_info:
        info_at = lambda place: info_all_ref.at[place * 2 + core]
        heres.append(pltpu.make_async_copy(info_ref, info_at(at), local_sem.at[1]))
        heres[1].start()
        info_x = send(13, info_ref, info_at(at), {EXP: across})
        info_y = send(14, info_ref, info_at(at), {EXP: along})
        twins.append(send(15, info_ref, info_at(at), twin_id))
        info_x.wait_recv()
        info_far = send(16, info_at(across), info_at(across), {EXP: along})
        twins.append(send(17, info_at(across), info_at(across), twin_id))
        info_y.wait_recv()
        twins.append(send(18, info_at(along), info_at(along), twin_id))
        info_far.wait_recv()
        twins.append(send(19, info_at(far), info_at(far), twin_id))

    def hand_on(number, place, shift, part):
        src = piece(place, shift, part)
        twins.append(send(number, src, piece(place, shift, part, 1), twin_id))

    x_top.wait_recv()
    far_top = send(5, piece(across, 1, top), piece(across, 3, top), {EXP: along})
    hand_on(6, across, 1, top)
    y_bottom.wait_recv()
    far_bottom = send(7, piece(along, 2, bottom), piece(along, 3, bottom), {EXP: across})
    hand_on(8, along, 2, bottom)
    x_bottom.wait_recv()
    hand_on(9, across, 1, bottom)
    y_top.wait_recv()
    hand_on(10, along, 2, top)
    far_top.wait_recv()
    hand_on(11, far, 3, top)
    far_bottom.wait_recv()
    hand_on(12, far, 3, bottom)
    for copy in twins:
        copy.wait_recv()
    for copy in started:
        copy.wait_send()
    for copy in heres:
        copy.wait()


def plane_gather(own, info, relative, number):
    plane = lax.axis_size(PLANE)
    operands = [own] if info is None else [own, info]
    outs = [jax.ShapeDtypeStruct((plane, *v.shape), v.dtype) for v in operands]
    anywhere = pl.BlockSpec(memory_space=pl.ANY)
    return pl.pallas_call(
        partial(plane_gather_kernel, info is not None, relative),
        out_shape=outs,
        in_specs=[anywhere] * len(operands),
        out_specs=[anywhere] * len(operands),
        scratch_shapes=[
            pltpu.SemaphoreType.DMA((20,)),
            pltpu.SemaphoreType.DMA((20,)),
            pltpu.SemaphoreType.DMA((2,)),
        ],
        compiler_params=pltpu.CompilerParams(collective_id=number, has_side_effects=True),
        cost_estimate=pl.CostEstimate(
            flops=0, bytes_accessed=own.size, transcendentals=0
        ),
    )(*operands)


def norm_qkv_kernel(hidden_ref, gain_ref, w_ref, norm_ref, qkv_ref):
    values = hidden_ref[...].astype(jnp.float32)
    inv = lax.rsqrt(jnp.mean(values * values, axis=1, keepdims=True) + EPS)
    norm_ref[...] = low(values * inv * gain_ref[...])
    qkv_ref[...] = low(mm(norm_ref[...], w_ref[...]))


def norm_qkv(hidden, gain, w, block):
    rows, width = hidden.shape
    cols = w.shape[1]
    return pl.pallas_call(
        norm_qkv_kernel,
        grid=(rows // block,),
        in_specs=[
            pl.BlockSpec((block, width), lambda i: (i, 0)),
            pl.BlockSpec((1, width), lambda i: (0, 0)),
            pl.BlockSpec((width, cols), lambda i: (0, 0)),
        ],
        out_specs=[
            pl.BlockSpec((block, width), lambda i: (i, 0)),
            pl.BlockSpec((block, cols), lambda i: (i, 0)),
        ],
        out_shape=[
            jax.ShapeDtypeStruct((rows, width), jnp.bfloat16),
            jax.ShapeDtypeStruct((rows, cols), jnp.bfloat16),
        ],
        compiler_params=pltpu.CompilerParams(vmem_limit_bytes=48 * 2**20),
        cost_estimate=pl.CostEstimate(
            flops=2 * rows * width * cols,
            bytes_accessed=4 * rows * width,
            transcendentals=0,
        ),
    )(hidden, gain, w)


def chosen_rows(slots, capacity):
    lanes = lax.broadcasted_iota(jnp.int32, (slots.shape[0], capacity), 1)
    return (slots == lanes).astype(jnp.bfloat16)


def hand_out(step_at, half, blocks, out_refs, sems):
    copies = [
        pltpu.make_async_copy(blocks.at[k], out_refs[k], sems.at[k]) for k in range(half)
    ]
    for k in range(half):

        @pl.when(step_at == half + k)
        def _():
            copies[k].start()

    @pl.when(step_at == 2 * half - 1)
    def _():
        for copy in copies:
            copy.wait()


def output_kernel(
    half,
    hidden_ref,
    down_ref,
    rows_ref,
    slot_ref,
    sg_ref,
    gate_ref,
    cot_ref,
    *refs,
):
    near_refs, dots_ref, refs = refs[:half], refs[half], refs[half + 1 :]
    given, got, send_sem, recv_sem, out_sem = refs
    step_at = pl.program_id(0)
    is_far = step_at < half
    slot = lax.rem(step_at, half)
    twin_id = {CTX: 1 - lax.axis_index(CTX)}

    @pl.when(step_at == 0)
    def _():
        barrier = pltpu.get_barrier_semaphore()
        pl.semaphore_signal(barrier, inc=1, device_id=twin_id, device_id_type=MESH_ID)
        pl.semaphore_wait(barrier, 1)

    def block_copy(k):
        return pltpu.make_async_remote_copy(
            src_ref=given.at[k],
            dst_ref=got.at[k],
            send_sem=send_sem.at[k],
            recv_sem=recv_sem.at[k],
            device_id=twin_id,
            device_id_type=MESH_ID,
        )

    def make(store):
        chosen = chosen_rows(slot_ref[...], rows_ref.shape[1])
        hidden = hidden_ref[...].T
        tokens, width = cot_ref.shape
        step, lanes = 512, 128
        gate_dot = jnp.zeros((tokens, lanes), jnp.float32)
        shared_dot = jnp.zeros((tokens, lanes), jnp.float32)
        for first in range(0, width, step):
            cols = pl.ds(first, step)
            shared = mm(hidden, down_ref[:, cols])
            picked = mm(chosen, rows_ref[0, :, cols])
            cot = cot_ref[:, cols].astype(jnp.float32)
            gate_part, shared_part = picked * cot, shared * cot
            for at in range(0, step, lanes):
                gate_dot += gate_part[:, at : at + lanes]
                shared_dot += shared_part[:, at : at + lanes]
            store(cols, sg_ref[...] * shared + gate_ref[...] * picked)
        lane = lax.broadcasted_iota(jnp.int32, dots_ref.shape, 1)
        gate_dot = jnp.sum(gate_dot, axis=1, keepdims=True)
        shared_dot = jnp.sum(shared_dot, axis=1, keepdims=True)
        dots_ref[...] = jnp.where(lane == 0, gate_dot, jnp.where(lane == 1, shared_dot, 0.0))

    @pl.when(is_far)
    def _():
        def store(cols, total):
            given[slot, :, cols] = low(total)

        make(store)
        block_copy(slot).start()

    @pl.when(jnp.logical_not(is_far))
    def _():
        block_copy(slot).wait_recv()

        def store(cols, total):
            got[slot, :, cols] = low(total + got[slot, :, cols].astype(jnp.float32))

        make(store)

    hand_out(step_at, half, got, near_refs, out_sem)

    @pl.when(step_at == 2 * half - 1)
    def _():
        for k in range(half):
            block_copy(k).wait_send()


def output_parts(hidden, down, rows, slots, sg, gates, cot):
    blocks, capacity, width = rows.shape
    units, count = hidden.shape
    tokens, half = count // blocks, blocks // 2
    at = lambda i: lax.rem(i + half, blocks)
    column = pl.BlockSpec((tokens, 1), lambda i: (at(i), 0))
    return pl.pallas_call(
        partial(output_kernel, half),
        grid=(blocks,),
        in_specs=[
            pl.BlockSpec((units, tokens), lambda i: (0, at(i))),
            pl.BlockSpec((units, width), lambda i: (0, 0)),
            pl.BlockSpec((1, capacity, width), lambda i: (at(i), 0, 0)),
            column,
            column,
            column,
            pl.BlockSpec((tokens, width), lambda i: (at(i), 0)),
        ],
        out_specs=[
            *[pl.BlockSpec(memory_space=pl.ANY)] * half,
            pl.BlockSpec((tokens, 128), lambda i: (at(i), 0)),
        ],
        out_shape=[
            *[jax.ShapeDtypeStruct((tokens, width), jnp.bfloat16)] * half,
            jax.ShapeDtypeStruct((count, 128), jnp.float32),
        ],
        scratch_shapes=[
            pltpu.VMEM((half, tokens, width), jnp.bfloat16),
            pltpu.VMEM((half, tokens, width), jnp.bfloat16),
            pltpu.SemaphoreType.DMA((half,)),
            pltpu.SemaphoreType.DMA((half,)),
            pltpu.SemaphoreType.DMA((half,)),
        ],
        compiler_params=pltpu.CompilerParams(
            collective_id=4, has_side_effects=True, vmem_limit_bytes=56 * 2**20
        ),
        cost_estimate=pl.CostEstimate(
            flops=2 * count * width * (units + capacity),
            bytes_accessed=6 * count * width,
            transcendentals=0,
        ),
    )(hidden, down, rows, slots, sg, gates, cot)


def scatter_step(compute, out_ref, scratch):
    given, total, x_got, y_got, x_last, y_last, send_sem, recv_sem = scratch
    at, core, across, along, far = plane_places()
    step_at = pl.program_id(0)
    row = step_at // 2
    is_twin = step_at % 2 == 0
    rows = total.shape[1]
    half = rows // 2
    top, bottom = pl.ds(0, half), pl.ds(half, half)

    def copy_of(number, src, dst, target):
        return pltpu.make_async_remote_copy(
            src_ref=src,
            dst_ref=dst,
            send_sem=send_sem.at[number],
            recv_sem=recv_sem.at[number],
            device_id=target,
            device_id_type=MESH_ID,
        )

    def twin_copy(k):
        return copy_of(k, given.at[k % 2], total.at[k], {CTX: 1 - core})

    far_x = copy_of(4, total.at[0, top], x_got.at[0], {EXP: across})
    far_y = copy_of(5, total.at[0, bottom], y_got.at[0], {EXP: along})
    own_x = copy_of(6, total.at[1, top], x_got.at[1], {EXP: across})
    own_y = copy_of(7, total.at[2, bottom], y_got.at[1], {EXP: along})
    last_y = copy_of(8, total.at[2, top], y_last, {EXP: along})
    last_x = copy_of(9, total.at[1, bottom], x_last, {EXP: across})

    @pl.when(step_at == 0)
    def _():
        greet(across, along, core)

    @pl.when(is_twin)
    def _():
        @pl.when(row >= 2)
        def _():
            twin_copy(row - 2).wait_send()

        def store(cols, values):
            given[row % 2, :, cols] = low(values)

        compute(store)
        twin_copy(row).start()

    @pl.when(jnp.logical_not(is_twin))
    def _():
        twin_copy(row).wait_recv()

        def store(cols, values):
            total[row, :, cols] = low(values + total[row, :, cols].astype(jnp.float32))

        compute(store)

    @pl.when(step_at == 1)
    def _():
        far_x.start()
        far_y.start()

    @pl.when(step_at == 3)
    def _():
        own_x.start()

    @pl.when(step_at == 5)
    def _():
        own_y.start()

    @pl.when(step_at == 7)
    def _():
        def add_half(k, first, got):
            @pl.loop(0, half // 64)
            def _(i):
                take = pl.ds(pl.multiple_of(i * 64, 64), 64)
                into = pl.ds(pl.multiple_of(first + i * 64, 64), 64)
                total[k, into] = low(
                    total[k, into].astype(jnp.float32) + got[0, take].astype(jnp.float32)
                )

        def finish(first, near, later):
            @pl.loop(0, half // 64)
            def _(i):
                take = pl.ds(pl.multiple_of(i * 64, 64), 64)
                into = pl.ds(pl.multiple_of(first + i * 64, 64), 64)
                out_ref[into] = (
                    total[3, into].astype(jnp.float32)
                    + near[1, take].astype(jnp.float32)
                    + later[take].astype(jnp.float32)
                )

        far_x.wait_recv()
        add_half(2, 0, x_got)
        last_y.start()
        far_y.wait_recv()
        add_half(1, half, y_got)
        last_x.start()
        own_x.wait_recv()
        last_y.wait_recv()
        finish(0, x_got, y_last)
        own_y.wait_recv()
        last_x.wait_recv()
        finish(half, y_got, x_last)
        for copy in (twin_copy(2), twin_copy(3), far_x, far_y, own_x, own_y, last_y, last_x):
            copy.wait_send()


def step_slot(i):
    row = i // 2
    shift = jnp.where(row == 0, 3, jnp.where(row == 3, 0, row))
    return shift + 4 * (1 - i % 2)


def scatter_scratch(tokens, width):
    vmem = lambda *shape: pltpu.VMEM(shape, jnp.bfloat16)
    return [
        vmem(2, tokens, width),
        vmem(4, tokens, width),
        vmem(2, tokens // 2, width),
        vmem(2, tokens // 2, width),
        vmem(tokens // 2, width),
        vmem(tokens // 2, width),
        pltpu.SemaphoreType.DMA((10,)),
        pltpu.SemaphoreType.DMA((10,)),
    ]


def n2_grad_kernel(dgate_ref, dup_ref, gate_ref, up_ref, rows_ref, slot_ref, out_ref, *scratch):
    def compute(store):
        chosen = chosen_rows(slot_ref[...], rows_ref.shape[1])
        dgate, dup = dgate_ref[...].T, dup_ref[...].T
        step = 512
        for first in range(0, gate_ref.shape[1], step):
            cols = pl.ds(first, step)
            total = mm(dgate, gate_ref[:, cols]) + mm(dup, up_ref[:, cols])
            store(cols, total + mm(chosen, rows_ref[0, :, cols]))

    scatter_step(compute, out_ref, scratch)


def n2_grad_sum(dgate, dup, gate_w, up_w, rows, slots):
    blocks, capacity, width = rows.shape
    units, count = dgate.shape
    tokens = count // blocks
    by_units = pl.BlockSpec((units, tokens), lambda i: (0, step_slot(i)))
    whole = pl.BlockSpec((units, width), lambda i: (0, 0), pipeline_mode=pl.Buffered(1))
    return pl.pallas_call(
        n2_grad_kernel,
        grid=(blocks,),
        in_specs=[
            by_units,
            by_units,
            whole,
            whole,
            pl.BlockSpec((1, capacity, width), lambda i: (step_slot(i), 0, 0)),
            pl.BlockSpec((tokens, 1), lambda i: (step_slot(i), 0)),
        ],
        out_specs=pl.BlockSpec((tokens, width), lambda i: (0, 0)),
        out_shape=jax.ShapeDtypeStruct((tokens, width), jnp.float32),
        scratch_shapes=scatter_scratch(tokens, width),
        compiler_params=pltpu.CompilerParams(
            collective_id=3, has_side_effects=True, vmem_limit_bytes=56 * 2**20
        ),
        cost_estimate=pl.CostEstimate(
            flops=2 * count * width * (2 * units + capacity),
            bytes_accessed=4 * count * width,
            transcendentals=0,
        ),
    )(dgate, dup, gate_w, up_w, rows, slots)


def unit_grad_kernel(hid_ref, dgate_ref, dup_ref, cot_ref, n2_ref, out_ref):
    units = hid_ref.shape[0]
    out_ref[0, :units] = low(mm(hid_ref[...], cot_ref[...]))
    out_ref[0, units : 2 * units] = low(mm(dgate_ref[...], n2_ref[...]))
    out_ref[0, 2 * units :] = low(mm(dup_ref[...], n2_ref[...]))


def unit_grads(hidden, dgate, dup, cots, n2, depth, halves):
    units, count = hidden.shape
    width = n2.shape[1]
    cols = width // (depth * halves)
    whole = pl.BlockSpec((units, count), lambda i: (0, 0), pipeline_mode=pl.Buffered(1))
    strip = pl.BlockSpec((count, cols), lambda i: (0, i))
    return pl.pallas_call(
        unit_grad_kernel,
        grid=(depth * halves,),
        in_specs=[whole, whole, whole, strip, strip],
        out_specs=pl.BlockSpec(
            (1, 3 * units, cols), lambda i: (lax.rem(i, depth), 0, i // depth)
        ),
        out_shape=jax.ShapeDtypeStruct((depth, 3 * units, halves * cols), jnp.bfloat16),
        compiler_params=pltpu.CompilerParams(vmem_limit_bytes=48 * 2**20),
        cost_estimate=pl.CostEstimate(
            flops=6 * units * count * width,
            bytes_accessed=2 * (3 * units * count + 2 * count * width + 3 * units * width),
            transcendentals=0,
        ),
    )(hidden, dgate, dup, cots, n2)


def n1_grad_kernel(half, grads_ref, w_ref, *refs):
    near_refs, refs = refs[:half], refs[half:]
    rows_in, given, got, load_sem, send_sem, recv_sem, out_sem = refs
    place, core = lax.axis_index(EXP), lax.axis_index(CTX)
    step_at = pl.program_id(0)
    is_far = step_at < half
    slot = lax.rem(step_at, half)
    tokens = rows_in.shape[1]
    twin_id = {CTX: 1 - core}

    def load(step, k):
        column, level = place % 2, place // 2
        there = (column + k % 2) % 2 + 2 * ((level + k // 2) % 2)
        owner = 1 - core if step < half else core
        first = pl.multiple_of((there * 2 + owner) * tokens, tokens)
        return pltpu.make_async_copy(
            grads_ref.at[pl.ds(first, tokens)], rows_in.at[step], load_sem.at[step]
        )

    loads = [load(step, step % half) for step in range(2 * half)]

    @pl.when(step_at == 0)
    def _():
        for copy in loads:
            copy.start()
        barrier = pltpu.get_barrier_semaphore()
        pl.semaphore_signal(barrier, inc=1, device_id=twin_id, device_id_type=MESH_ID)
        pl.semaphore_wait(barrier, 1)

    for step in range(2 * half):

        @pl.when(step_at == step)
        def _():
            loads[step].wait()

    def block_copy(k):
        return pltpu.make_async_remote_copy(
            src_ref=given.at[k],
            dst_ref=got.at[k],
            send_sem=send_sem.at[k],
            recv_sem=recv_sem.at[k],
            device_id=twin_id,
            device_id_type=MESH_ID,
        )

    def make(store):
        step = 512
        for first in range(0, w_ref.shape[0], step):
            cols = pl.ds(first, step)
            store(cols, mm(rows_in[step_at], w_ref[cols, :], ((1,), (1,))))

    @pl.when(is_far)
    def _():
        def store(cols, total):
            given[slot, :, cols] = low(total)

        make(store)
        block_copy(slot).start()

    @pl.when(jnp.logical_not(is_far))
    def _():
        block_copy(slot).wait_recv()

        def store(cols, total):
            got[slot, :, cols] = low(total + got[slot, :, cols].astype(jnp.float32))

        make(store)

    hand_out(step_at, half, got, near_refs, out_sem)

    @pl.when(step_at == 2 * half - 1)
    def _():
        for k in range(half):
            block_copy(k).wait_send()


def n1_grad_parts(grads, w, blocks):
    rows, cols = grads.shape
    width = w.shape[0]
    tokens, half = rows // blocks, blocks // 2
    return pl.pallas_call(
        partial(n1_grad_kernel, half),
        grid=(blocks,),
        in_specs=[
            pl.BlockSpec(memory_space=pl.ANY),
            pl.BlockSpec((width, cols), lambda i: (0, 0)),
        ],
        out_specs=[pl.BlockSpec(memory_space=pl.ANY)] * half,
        out_shape=[jax.ShapeDtypeStruct((tokens, width), jnp.bfloat16)] * half,
        scratch_shapes=[
            pltpu.VMEM((blocks, tokens, cols), jnp.bfloat16),
            pltpu.VMEM((half, tokens, width), jnp.bfloat16),
            pltpu.VMEM((half, tokens, width), jnp.bfloat16),
            pltpu.SemaphoreType.DMA((blocks,)),
            pltpu.SemaphoreType.DMA((half,)),
            pltpu.SemaphoreType.DMA((half,)),
            pltpu.SemaphoreType.DMA((half,)),
        ],
        compiler_params=pltpu.CompilerParams(
            collective_id=1, has_side_effects=True, vmem_limit_bytes=48 * 2**20
        ),
        cost_estimate=pl.CostEstimate(
            flops=2 * rows * width * cols,
            bytes_accessed=4 * rows * width,
            transcendentals=0,
        ),
    )(grads, w)


def after(values, others):
    return lax.optimization_barrier((values, others))[0]


def swap(values, bits):
    return lax.ppermute(values, EXP, [(i, i ^ bits) for i in range(4)])


def twin(values):
    return lax.ppermute(values, CTX, [(0, 1), (1, 0)])


def twin_sums(ours, theirs):
    got = twin(theirs)
    return [low(ours[k].astype(jnp.float32) + got[k].astype(jnp.float32)) for k in range(4)]


def hops(sums):
    return [sums[0]] + [swap(sums[k], k) for k in (1, 2, 3)]


def sum_up(parts):
    return sum(v.astype(jnp.float32) for v in parts)


def mm(left, right, dims=((1,), (0,))):
    return lax.dot_general(left, right, (dims, ((), ())), preferred_element_type=jnp.float32)


def low(values):
    return values.astype(jnp.bfloat16)


def local_plane(
    hidden,
    cotangent,
    segments,
    padding,
    routes,
    order,
    norm1_gain,
    w_query,
    w_key,
    w_value,
    w_out,
    norm2_gain,
    router,
    shared_gate_vec,
    shared_w_gate,
    shared_w_up,
    shared_w_down,
    expert_w_gate,
    expert_w_up,
    expert_w_down,
):
    plane = lax.axis_size(PLANE)
    groups = lax.axis_size(EXP)
    halves = lax.axis_size(CTX)
    depth = lax.axis_size(DP)
    me = lax.axis_index(PLANE)
    core = lax.axis_index(CTX)
    tokens, width = hidden.shape[1], hidden.shape[2]
    all_tokens = plane * tokens
    seq_len = halves * tokens
    experts_all = router.shape[1]
    head_cols = width // plane
    shard = width // depth

    token_info = jnp.concatenate(
        [segments + 1, jnp.where(padding > 0, segments + 1, 0), order[0], routes[0].T]
    )
    info_rows = token_info.shape[0]
    token_info = jnp.concatenate([token_info, jnp.zeros((8 - info_rows, tokens), jnp.int32)])

    hidden_all, info_all = plane_gather(hidden[0], token_info, False, 0)
    hidden_all = hidden_all.reshape(all_tokens, width)
    place = lax.axis_index(EXP)
    away = [(place ^ k) * 2 + (core ^ j) for j in (0, 1) for k in range(4)]
    away = jnp.stack(away)
    out_rows = shard // plane
    w_out_part = lax.dynamic_slice(w_out, (me * out_rows, 0), (out_rows, width))
    w_qkv_part = jnp.concatenate(
        [
            lax.dynamic_slice(w, (0, me * head_cols), (shard, head_cols))
            for w in (w_query, w_key, w_value)
        ]
        + [router, norm1_gain[:, None], norm2_gain[:, None], shared_gate_vec[:, None]]
        + [jnp.zeros((shard, 128 - experts_all - 3), jnp.bfloat16)]
        + [w_out_part.reshape(shard, -1)],
        axis=1,
    )
    w_qkv = lax.all_gather(w_qkv_part, DP, axis=0, tiled=True)
    w_out_part = w_qkv[:, 3 * head_cols + 128 :].reshape(depth, out_rows, width)
    small = w_qkv[:, 3 * head_cols : 3 * head_cols + 128].T
    w_qkv = w_qkv[:, : 3 * head_cols]
    router_t = small[:experts_all]
    g_one = small[experts_all].astype(jnp.float32)
    g_two = small[experts_all + 1].astype(jnp.float32)
    gate_vec = small[experts_all + 2]
    w_out_part = after(w_out_part, info_all)
    w_out_got = [swap(w_out_part, k) for k in (1, 2, 3)]

    def normed(values, gain):
        values = values.astype(jnp.float32)
        inv = lax.rsqrt(jnp.mean(values * values, axis=1, keepdims=True) + EPS)
        return values, inv, low(values * inv * gain)

    n1_all, qkv = norm_qkv(hidden_all, g_one[None], w_qkv, tokens)
    q_codes = info_all[:, 0].reshape(all_tokens, 1)
    k_codes = info_all[:, 1].reshape(all_tokens // seq_len, 1, seq_len)
    attended_cols = attention_call(qkv, None, q_codes, k_codes, seq_len)
    pieces = [w_out_part] + [after(v, attended_cols) for v in w_out_got]
    w_out_near = jnp.zeros((depth, groups, 1, out_rows, width), jnp.bfloat16)
    for k in range(4):
        w_out_near = lax.dynamic_update_slice(
            w_out_near, pieces[k][:, None, None], (0, place ^ k, 0, 0, 0)
        )
    w_out_far = twin(w_out_near)
    w_out_full = jnp.where(
        core == 0,
        jnp.concatenate([w_out_near, w_out_far], axis=2),
        jnp.concatenate([w_out_far, w_out_near], axis=2),
    ).reshape(width, width)

    x_rows, inv_one, _ = normed(hidden[0], g_one)
    cot_rows = cotangent[0].astype(jnp.float32)

    def to_tokens(cols):
        got = lax.all_to_all(
            cols.reshape(plane, tokens, head_cols), PLANE, split_axis=0, concat_axis=0, tiled=True
        )
        return got.transpose(1, 0, 2).reshape(tokens, width)

    def to_columns(rows_in):
        send = rows_in.reshape(tokens, plane, head_cols).transpose(1, 0, 2)
        got = lax.all_to_all(send, PLANE, split_axis=0, concat_axis=0, tiled=True)
        return got.reshape(all_tokens, head_cols)

    attended = to_tokens(attended_cols)
    residual = x_rows + mm(attended, w_out_full)
    residual, inv_two, n2 = normed(residual, g_two)

    units = shared_w_gate.shape[1]
    part = units // (depth * halves)
    pick = lambda w: lax.dynamic_index_in_dim(
        w.reshape(w.shape[0], depth, halves, part), core, axis=2, keepdims=False
    ).reshape(w.shape[0], depth * part)
    sh_gate_up = jnp.concatenate([pick(shared_w_gate), pick(shared_w_up)], axis=1)
    sh_gate_up = lax.all_gather(sh_gate_up, DP, axis=0, tiled=True)
    sh_gate_t, sh_up_t = sh_gate_up[:, : depth * part].T, sh_gate_up[:, depth * part :].T
    sh_down = lax.all_gather(
        lax.dynamic_slice(shared_w_down, (core * part, 0), (part, width)), DP, axis=0, tiled=True
    )
    n2 = after(n2, sh_gate_up)
    n2_all = plane_gather(n2, None, True, 2)[0].reshape(all_tokens, width)
    cot_own = after(cotangent[0], n2_all)
    cot_got = [swap(cot_own, k) for k in (1, 2, 3)]
    ex_gate = lax.all_gather(after(expert_w_gate[0], info_all), DP, axis=0, tiled=True)
    ex_up = lax.all_gather(after(expert_w_up[0], info_all), DP, axis=0, tiled=True)
    ex_down = lax.all_gather(after(expert_w_down[0], info_all), DP, axis=1, tiled=True)

    small_w = jnp.concatenate([router_t, gate_vec[None]])

    def gates_of(rows_in):
        both = mm(rows_in, small_w, ((1,), (1,)))
        z = both[:, :experts_all]
        e = jnp.exp(z - jnp.max(z, axis=1, keepdims=True))
        return e / jnp.sum(e, axis=1, keepdims=True), jax.nn.sigmoid(both[:, experts_all:])

    probs_all, sg_all = gates_of(n2_all)
    expert_gate = lax.dynamic_slice(probs_all, (0, me), (all_tokens, 1))

    capacity = (9 * tokens * TOP + 8 * experts_all - 1) // (8 * experts_all)
    info_away = info_all[away]
    order_all = info_away[:, 2]
    routed_here = jnp.any(info_away[:, 3 : 3 + TOP] == me, axis=1)
    earlier = (order_all[:, None, :] < order_all[:, :, None]) & routed_here[:, None, :]
    slots = jnp.sum(earlier.astype(jnp.int32), axis=2)
    slots = jnp.where(routed_here, slots, capacity)
    chosen = slots[:, None, :] == jnp.arange(capacity, dtype=jnp.int32)[None, :, None]
    onehot = chosen.astype(jnp.bfloat16)

    def rows_of(values):
        got = lax.dot_general(
            onehot,
            values.reshape(plane, tokens, width),
            (((2,), (1,)), ((0,), (0,))),
            preferred_element_type=jnp.float32,
        )
        return got.reshape(plane * capacity, width)

    slot_gates = jnp.sum(
        jnp.where(chosen, expert_gate.reshape(plane, 1, tokens), 0.0), axis=2
    ).reshape(plane * capacity, 1)
    expert_rows = low(rows_of(n2_all))
    gate_pre = mm(sh_gate_t, n2_all, ((1,), (1,)))
    up_pre = mm(sh_up_t, n2_all, ((1,), (1,)))
    gate_act = gate_pre * jax.nn.sigmoid(gate_pre)
    shared_hidden = low(gate_act * up_pre)
    expert_rows = after(expert_rows, (shared_hidden, sh_down))
    gate_e = mm(expert_rows, ex_gate)
    up_e = mm(expert_rows, ex_up)
    act_e = gate_e * jax.nn.sigmoid(gate_e)
    hidden_e = low(act_e * up_e)
    cot_near = jnp.concatenate([cot_own] + [after(v, gate_e) for v in cot_got])
    cot_all = jnp.concatenate([cot_near, twin(cot_near)])
    row_cots = low(rows_of(cot_all))
    row_grads = low(row_cots.astype(jnp.float32) * slot_gates)

    shared_grads = low(sg_all * cot_all.astype(jnp.float32))
    shared_hgrad = mm(sh_down, shared_grads, ((1,), (1,)))
    gate_grad_s = low(shared_hgrad * up_pre * silu_grad(gate_pre))
    up_grad_s = low(shared_hgrad * gate_act)
    rows_out = width // (halves * depth)

    def shared_scatter(total):
        first, second = total[:, :, :rows_out], total[:, :, rows_out:]
        keep = jnp.where(core == 0, first, second)
        got = twin(jnp.where(core == 0, second, first))
        both = [v.reshape(3, depth, part, rows_out) for v in (keep, got)]
        both = jnp.where(core == 0, jnp.stack(both, axis=2), jnp.stack(both[::-1], axis=2))
        return both.reshape(3, units, rows_out).astype(jnp.float32)

    scatter = lambda v, dim: lax.psum_scatter(v, DP, scatter_dimension=dim, tiled=True)
    shared_sums = unit_grads(
        shared_hidden, gate_grad_s, up_grad_s, shared_grads, n2_all, depth, halves
    )
    shared_sums = scatter(shared_sums.reshape(3 * depth * depth * part, -1), 0)
    result_e = low(mm(hidden_e, ex_down))
    hgrad_e = mm(row_grads, ex_down, ((1,), (1,)))
    gate_grad_e = low(hgrad_e * up_e * silu_grad(gate_e))
    up_grad_e = low(hgrad_e * act_e)

    grad_ex_down = low(mm(hidden_e, row_grads, ((0,), (0,))))
    grad_ex_gate = low(mm(expert_rows, gate_grad_e, ((0,), (0,))))
    grad_ex_up = low(mm(expert_rows, up_grad_e, ((0,), (0,))))
    grads_made = (grad_ex_down, grad_ex_gate, grad_ex_up)
    grads = [scatter(v, dim) for v, dim in zip(grads_made, (1, 0, 0))]
    slots = slots.reshape(all_tokens, 1)
    *out_near, dots = output_parts(
        shared_hidden,
        sh_down,
        result_e.reshape(plane, capacity, width),
        slots,
        sg_all,
        expert_gate,
        cot_all,
    )
    rows_grad = low(
        mm(gate_grad_e, ex_gate, ((1,), (1,))) + mm(up_grad_e, ex_up, ((1,), (1,)))
    )

    out_got = hops(out_near)
    slots, out_got, _ = lax.optimization_barrier((slots, out_got, (shared_sums, grads_made)))
    n2_grad = n2_grad_sum(
        gate_grad_s,
        up_grad_s,
        sh_gate_t,
        sh_up_t,
        rows_grad.reshape(plane, capacity, width),
        slots,
    )

    dots = dots.reshape(plane, tokens, 128)[:, :, :2].transpose(0, 2, 1)
    back = jnp.arange(plane, dtype=jnp.int32) ^ me
    dots = dots[(back // 2) + 4 * (back % 2)]
    dots = lax.all_to_all(dots, PLANE, split_axis=0, concat_axis=0, tiled=True)
    probs_grad = dots[:, 0].T
    probs, sg = gates_of(n2)
    logit_grad = low(probs * (probs_grad - jnp.sum(probs * probs_grad, axis=1, keepdims=True)))
    sg_logit_grad = low(jnp.sum(dots[:, 1], axis=0)[:, None] * sg * (1.0 - sg))
    n2_grad = (
        n2_grad
        + mm(logit_grad, router_t)
        + sg_logit_grad.astype(jnp.float32) * gate_vec.astype(jnp.float32)[None]
    )
    residual_grad, grad_gain_two = norm_back(residual, inv_two, g_two, n2_grad)
    residual_grad = residual_grad + cot_rows
    low_residual = low(residual_grad)

    attended_grad = low(mm(low_residual, w_out_full, ((1,), (1,))))
    low_residual = after(low_residual, attended_grad)
    output = low(residual + sum_up(after(out_got, attended_grad)))
    attended_grad = to_columns(attended_grad)
    grad_out = low(mm(attended, low_residual, ((0,), (0,))))
    grad_out = grad_out.reshape(groups, halves, width // plane, width)
    block_of = lambda k, c: lax.dynamic_slice(
        grad_out, (place ^ k, c, 0, 0), (1, 1, width // plane, width)
    )[0, 0]
    out_grad_sums = twin_sums(
        [block_of(k, core) for k in range(4)],
        jnp.stack([block_of(k, 1 - core) for k in range(4)]),
    )
    dz_all = jnp.concatenate([logit_grad, sg_logit_grad], axis=1)
    dz_all = after(dz_all, out_grad_sums)
    small_grads = mm(n2, dz_all, ((0,), (0,)))
    small_grads = jnp.concatenate([small_grads, grad_gain_two[:, None]], axis=1).T
    small_grads = jnp.pad(small_grads, ((0, 14 - experts_all), (0, 0)))
    small_grads = small_grads.reshape(16, plane, width // plane).transpose(1, 0, 2)
    attended_grad, small_grads = lax.optimization_barrier((attended_grad, small_grads))
    small_grads = jnp.sum(
        lax.all_to_all(small_grads, PLANE, split_axis=0, concat_axis=0, tiled=True), axis=0
    )
    attended_grad = after(attended_grad, (out_grad_sums, output, grads[0]))
    qkv_grad = attention_call(qkv, attended_grad, q_codes, k_codes, seq_len)
    grad_qkv = low(mm(n1_all, qkv_grad, ((0,), (0,))))
    fine = shard // plane
    grad_qkv = (
        grad_qkv.reshape(plane, depth, fine, 3 * head_cols)
        .transpose(1, 0, 2, 3)
        .reshape(width, 3 * head_cols)
    )
    out_grad_got = hops(out_grad_sums)
    qkv_grad, out_grad_got, small_grads, _ = lax.optimization_barrier(
        (qkv_grad, out_grad_got, small_grads, (grad_qkv, grads[1]))
    )
    n1_near = n1_grad_parts(qkv_grad, w_qkv, plane)
    grad_out = low(sum_up(out_grad_got))
    n1_got = hops(n1_near)
    grad_qkv = lax.psum_scatter(grad_qkv, DP, scatter_dimension=0, tiled=True)
    qkv_sum = grad_qkv
    w_rows = (
        w_qkv.reshape(plane, depth, fine, 3 * head_cols)
        .transpose(1, 0, 2, 3)
        .reshape(depth, plane * fine, 3 * head_cols)
    )
    w_rows = lax.dynamic_index_in_dim(w_rows, lax.axis_index(DP), axis=0, keepdims=False)
    gain_dots = jnp.sum(grad_qkv.astype(jnp.float32) * w_rows.astype(jnp.float32), axis=1)
    gain_dots = lax.all_to_all(
        gain_dots.reshape(plane, 1, fine), PLANE, split_axis=0, concat_axis=0, tiled=True
    )
    my_gain = lax.dynamic_slice(
        g_one, ((me * depth + lax.axis_index(DP)) * fine,), (fine,)
    )
    grad_gain_one = jnp.sum(gain_dots[:, 0], axis=0) / my_gain
    grad_qkv = lax.all_to_all(
        grad_qkv.reshape(plane, fine, 3 * head_cols),
        PLANE,
        split_axis=0,
        concat_axis=0,
        tiled=True,
    )
    grad_qkv = (
        grad_qkv.reshape(plane, fine, 3, head_cols)
        .transpose(2, 1, 0, 3)
        .reshape(3, fine, width)
        .astype(jnp.float32)
    )
    grad_ex_down, grad_ex_gate, grad_ex_up = [
        v.astype(jnp.float32)[None] for v in after(grads, n1_near)
    ]
    grad_out = scatter(after(grad_out, qkv_sum), 0).astype(jnp.float32)
    shared_sums = after(shared_sums, n1_near)
    shared_sums = shared_scatter(shared_sums.reshape(3, units // halves, -1))
    grad_sh_down, grad_sh_gate, grad_sh_up = [shared_sums[k] for k in range(3)]
    grad_sh_gate, grad_sh_up = grad_sh_gate.T, grad_sh_up.T
    small_grads = after(small_grads, n1_near)
    small_grads = small_grads.reshape(16, depth, shard // plane).transpose(1, 0, 2)
    small_grads = jnp.sum(
        lax.all_to_all(small_grads, DP, split_axis=0, concat_axis=0, tiled=True), axis=0
    )
    n1_grad = sum_up(after(n1_got, qkv_sum))
    input_part, _ = norm_back(x_rows, inv_one, g_one, n1_grad)
    input_grad = low(residual_grad + input_part)
    return (
        output[None],
        input_grad[None],
        grad_gain_one,
        grad_qkv[0],
        grad_qkv[1],
        grad_qkv[2],
        grad_out,
        small_grads[experts_all + 1],
        small_grads[:experts_all].T,
        small_grads[experts_all],
        grad_sh_gate,
        grad_sh_up,
        grad_sh_down,
        grad_ex_gate,
        grad_ex_up,
        grad_ex_down,
    )


def solution(mesh):
    in_specs = (
        P((EXP, DP), CTX, None),
        P((EXP, DP), CTX, None),
        P((EXP, DP), CTX),
        P((EXP, DP), CTX),
        P((EXP, DP), CTX, None),
        P((EXP, DP), CTX, None),
        P(DP),
        P(DP, None),
        P(DP, None),
        P(DP, None),
        P(DP, None),
        P(DP),
        P(DP, None),
        P(DP),
        P(DP, EXP),
        P(DP, EXP),
        P((EXP, DP), None),
        P((EXP, CTX), DP, None),
        P((EXP, CTX), DP, None),
        P((EXP, CTX), None, DP),
    )
    out_specs = (
        P((EXP, DP), CTX, None),
        P((EXP, DP), CTX, None),
        P((EXP, CTX, DP)),
        P((EXP, CTX, DP), None),
        P((EXP, CTX, DP), None),
        P((EXP, CTX, DP), None),
        P((EXP, CTX, DP), None),
        P((EXP, CTX, DP)),
        P((EXP, CTX, DP), None),
        P((EXP, CTX, DP)),
        P((CTX, DP), EXP),
        P((CTX, DP), EXP),
        P(EXP, (CTX, DP)),
        P((EXP, CTX), DP, None),
        P((EXP, CTX), DP, None),
        P((EXP, CTX), None, DP),
    )
    plane = mesh.shape[EXP] * mesh.shape[CTX]

    def run(*args):
        square = mesh.shape[EXP] == 4 and mesh.shape[CTX] == 2 and mesh.shape[DP] == 4
        one_each = square and args[12].shape[1] == plane
        local = local_plane if one_each else local_general
        return jax.shard_map(
            local, mesh=mesh, in_specs=in_specs, out_specs=out_specs, check_vma=False
        )(*args)

    return run
```

```python
from functools import partial

import jax
import jax.numpy as jnp
from jax import lax
from jax.experimental import pallas as pl
from jax.experimental.pallas import tpu as pltpu
from jax.sharding import PartitionSpec as P

EXP, CTX, DP = "experts", "context", "dp"
PLANE = (EXP, CTX)
HEADS = 16
HEAD_DIM = 128
TOP = 4


EPS = 1e-06
NEG = -1e30


def silu_grad(pre_act):
    logistic = jax.nn.sigmoid(pre_act)
    return logistic * (1.0 + pre_act * (1.0 - logistic))


def block_slots(route_row, priority, expert_count):
    matches = (route_row[:, None] == jnp.arange(expert_count, dtype=jnp.int32)[None, :]).astype(
        jnp.int32
    )
    ordered = jnp.zeros_like(matches).at[priority].set(matches)
    before = jnp.cumsum(ordered, axis=0) - ordered
    return jnp.sum(before[priority] * matches, axis=1)


def norm_back(values_in, inv_rms, gain_vec, gradient):
    weighted = gradient * gain_vec
    inner_sum = jnp.mean(weighted * values_in, axis=1, keepdims=True)
    d_value = inv_rms * weighted - values_in * inv_rms**3 * inner_sum
    d_gain = jnp.sum(gradient * values_in * inv_rms, axis=0)
    return (d_value, d_gain)


def attend_head(packed, allowed, scale_factor):
    query_h, key_h, value_h = packed
    raw_scores = jnp.einsum("th,lh->tl", query_h, key_h, preferred_element_type=jnp.float32)
    logits = jnp.where(allowed, raw_scores * scale_factor, NEG)
    row_max = jnp.max(logits, axis=1, keepdims=True)
    exp_scores = jnp.exp(logits - row_max)
    row_total = jnp.sum(exp_scores, axis=1, keepdims=True)
    attn_probs = (exp_scores / row_total).astype(jnp.bfloat16)
    head_out = jnp.dot(attn_probs, value_h, preferred_element_type=jnp.float32).astype(jnp.bfloat16)
    return (head_out, row_max + jnp.log(row_total))


def attend_back(packed, allowed, scale_factor):
    query_h, key_h, value_h, out_grad, log_total = packed
    raw_scores = jnp.einsum("th,lh->tl", query_h, key_h, preferred_element_type=jnp.float32)
    logits = jnp.where(allowed, raw_scores * scale_factor, NEG)
    attn_probs = jnp.exp(logits - log_total)
    prob_grad = jnp.einsum("th,lh->tl", out_grad, value_h, preferred_element_type=jnp.float32)
    inner_sum = jnp.sum(attn_probs * prob_grad, axis=1, keepdims=True)
    score_grad = (attn_probs * (prob_grad - inner_sum) * scale_factor).astype(jnp.bfloat16)
    query_grad = jnp.dot(score_grad, key_h, preferred_element_type=jnp.float32)
    key_grad = jnp.einsum("tl,th->lh", score_grad, query_h, preferred_element_type=jnp.float32)
    value_grad = jnp.einsum(
        "tl,th->lh", attn_probs.astype(jnp.bfloat16), out_grad, preferred_element_type=jnp.float32
    )
    return (query_grad, key_grad, value_grad)


def local_general(
    hidden,
    cotangent,
    segments,
    padding,
    routes,
    order,
    norm1_gain,
    w_query,
    w_key,
    w_value,
    w_out,
    norm2_gain,
    router,
    shared_gate_vec,
    shared_w_gate,
    shared_w_up,
    shared_w_down,
    expert_w_gate,
    expert_w_up,
    expert_w_down,
):
    fetched = (
        lax.all_gather(norm1_gain, DP, axis=0, tiled=True),
        lax.all_gather(w_query, DP, axis=0, tiled=True),
        lax.all_gather(w_key, DP, axis=0, tiled=True),
        lax.all_gather(w_value, DP, axis=0, tiled=True),
        lax.all_gather(w_out, DP, axis=0, tiled=True),
        lax.all_gather(norm2_gain, DP, axis=0, tiled=True),
        lax.all_gather(router, DP, axis=0, tiled=True),
        lax.all_gather(shared_gate_vec, DP, axis=0, tiled=True),
        lax.all_gather(shared_w_gate, DP, axis=0, tiled=True),
        lax.all_gather(shared_w_up, DP, axis=0, tiled=True),
        lax.all_gather(shared_w_down, DP, axis=0, tiled=True),
        lax.all_gather(expert_w_gate, DP, axis=1, tiled=True),
        lax.all_gather(expert_w_up, DP, axis=1, tiled=True),
        lax.all_gather(expert_w_down, DP, axis=2, tiled=True),
    )
    (
        gain_one,
        query_w,
        key_w,
        value_w,
        out_w,
        gain_two,
        router_full,
        gate_vec,
        sh_gate,
        sh_up,
        sh_down,
        ex_gate,
        ex_up,
        ex_down,
    ) = fetched
    sh_gate, sh_up, sh_down = (
        lax.all_gather(sh_gate, EXP, axis=1, tiled=True),
        lax.all_gather(sh_up, EXP, axis=1, tiled=True),
        lax.all_gather(sh_down, EXP, axis=0, tiled=True),
    )
    tokens_here = hidden.shape[1]
    model_width = hidden.shape[2]
    x_rows = hidden[0].astype(jnp.float32)
    cot_rows = cotangent[0].astype(jnp.float32)
    inv_one = lax.rsqrt(jnp.mean(x_rows * x_rows, axis=1, keepdims=True) + EPS)
    g_one = gain_one.astype(jnp.float32)
    normed_one = (x_rows * inv_one * g_one).astype(jnp.bfloat16)
    queries = jnp.dot(normed_one, query_w, preferred_element_type=jnp.float32).astype(jnp.bfloat16)
    keys_own = jnp.dot(normed_one, key_w, preferred_element_type=jnp.float32).astype(jnp.bfloat16)
    values_own = jnp.dot(normed_one, value_w, preferred_element_type=jnp.float32).astype(
        jnp.bfloat16
    )
    own_codes = jnp.where(padding[0] > 0, segments[0] + 1, 0)
    code_parts = jnp.stack([own_codes // 64, own_codes % 64]).astype(jnp.bfloat16)
    keys_all, values_all, parts_all = (
        lax.all_gather(keys_own, CTX, axis=0, tiled=True),
        lax.all_gather(values_own, CTX, axis=0, tiled=True),
        lax.all_gather(code_parts, CTX, axis=1, tiled=True),
    )
    key_codes = parts_all[0].astype(jnp.int32) * 64 + parts_all[1].astype(jnp.int32)
    seq_total = keys_all.shape[0]
    query_pos = lax.axis_index(CTX) * tokens_here + jnp.arange(tokens_here, dtype=jnp.int32)
    key_pos = jnp.arange(seq_total, dtype=jnp.int32)
    same_doc = key_codes[None, :] == (segments[0] + 1)[:, None]
    allowed = (key_pos[None, :] <= query_pos[:, None]) & (
        same_doc | (key_pos[None, :] == query_pos[:, None])
    )
    scale_factor = HEAD_DIM ** (-0.5)

    def to_heads(rows_in):
        return rows_in.reshape(rows_in.shape[0], HEADS, HEAD_DIM).transpose(1, 0, 2)

    def from_heads(heads_in):
        return heads_in.transpose(1, 0, 2).reshape(heads_in.shape[1], model_width)

    head_q = to_heads(queries)
    head_k = to_heads(keys_all)
    head_v = to_heads(values_all)
    head_out, log_total = lax.map(
        partial(attend_head, allowed=allowed, scale_factor=scale_factor), (head_q, head_k, head_v)
    )
    attended = from_heads(head_out)
    residual = x_rows + jnp.dot(attended, out_w, preferred_element_type=jnp.float32)
    inv_two = lax.rsqrt(jnp.mean(residual * residual, axis=1, keepdims=True) + EPS)
    g_two = gain_two.astype(jnp.float32)
    normed_two = (residual * inv_two * g_two).astype(jnp.bfloat16)
    router_logits = jnp.dot(normed_two, router_full, preferred_element_type=jnp.float32)
    router_exp = jnp.exp(router_logits - jnp.max(router_logits, axis=1, keepdims=True))
    router_probs = router_exp / jnp.sum(router_exp, axis=1, keepdims=True)
    route_gates = jnp.take_along_axis(router_probs, routes[0], axis=1)
    shared_gate = jax.nn.sigmoid(jnp.dot(normed_two, gate_vec, preferred_element_type=jnp.float32))
    shared_scaled = (shared_gate[:, None] * cot_rows).astype(jnp.bfloat16)
    rows_group, grads_group = (normed_two, shared_scaled)
    gate_pre = jnp.dot(rows_group, sh_gate, preferred_element_type=jnp.float32)
    up_pre = jnp.dot(rows_group, sh_up, preferred_element_type=jnp.float32)
    gate_act = gate_pre * jax.nn.sigmoid(gate_pre)
    shared_hidden = (gate_act * up_pre).astype(jnp.bfloat16)
    shared_part = jnp.dot(shared_hidden, sh_down, preferred_element_type=jnp.float32)
    experts_all = router_full.shape[1]
    capacity = (9 * tokens_here * TOP + 8 * experts_all - 1) // (8 * experts_all)
    priority = (order[0, 0][:, None] * TOP + jnp.arange(TOP, dtype=jnp.int32)[None, :]).reshape(-1)
    flat_routes = routes[0].reshape(-1)
    slot_index = block_slots(flat_routes, priority, experts_all)
    kept_rows = slot_index < capacity
    target = flat_routes * capacity + jnp.minimum(slot_index, capacity - 1)
    row_gates = route_gates.reshape(-1)
    cot_repeated = jnp.repeat(cot_rows, TOP, axis=0)
    source_rows = jnp.repeat(normed_two, TOP, axis=0)
    source_grads = (cot_repeated * row_gates[:, None]).astype(jnp.bfloat16)
    empty_slots = jnp.zeros((experts_all * capacity, model_width), jnp.bfloat16)
    send_rows = empty_slots.at[target].add(
        jnp.where(kept_rows[:, None], source_rows, jnp.zeros_like(source_rows))
    )
    send_grads = empty_slots.at[target].add(
        jnp.where(kept_rows[:, None], source_grads, jnp.zeros_like(source_grads))
    )
    recv_rows, recv_grads = (
        lax.all_to_all(
            send_rows.reshape(experts_all, capacity, model_width),
            (EXP, CTX),
            split_axis=0,
            concat_axis=0,
            tiled=True,
        ),
        lax.all_to_all(
            send_grads.reshape(experts_all, capacity, model_width),
            (EXP, CTX),
            split_axis=0,
            concat_axis=0,
            tiled=True,
        ),
    )
    local_count = ex_gate.shape[0]
    sources = experts_all // local_count

    def to_local(buffer_in):
        return (
            buffer_in.reshape(sources, local_count, capacity, model_width)
            .transpose(1, 0, 2, 3)
            .reshape(local_count, sources * capacity, model_width)
        )

    def to_owner(buffer_in):
        return (
            buffer_in.reshape(local_count, sources, capacity, model_width)
            .transpose(1, 0, 2, 3)
            .reshape(experts_all, capacity, model_width)
        )

    expert_rows = to_local(recv_rows)
    expert_grads_in = to_local(recv_grads)
    gate_e = jnp.einsum("erd,edf->erf", expert_rows, ex_gate, preferred_element_type=jnp.float32)
    up_e = jnp.einsum("erd,edf->erf", expert_rows, ex_up, preferred_element_type=jnp.float32)
    act_e = gate_e * jax.nn.sigmoid(gate_e)
    hidden_e = (act_e * up_e).astype(jnp.bfloat16)
    result_e = jnp.einsum(
        "erf,efd->erd", hidden_e, ex_down, preferred_element_type=jnp.float32
    ).astype(jnp.bfloat16)
    returned = lax.all_to_all(
        to_owner(result_e), (EXP, CTX), split_axis=0, concat_axis=0, tiled=True
    )
    picked = returned.reshape(experts_all * capacity, model_width)[target]
    picked = jnp.where(kept_rows[:, None], picked, jnp.zeros_like(picked)).astype(jnp.float32)
    routed = jnp.sum((picked * row_gates[:, None]).reshape(tokens_here, TOP, model_width), axis=1)
    output = (residual + shared_gate[:, None] * shared_part + routed).astype(jnp.bfloat16)
    gate_grads = jnp.sum(picked * cot_repeated, axis=1).reshape(tokens_here, TOP)
    hidden_grad_e = jnp.einsum(
        "erd,efd->erf", expert_grads_in, ex_down, preferred_element_type=jnp.float32
    )
    gate_grad_e = (hidden_grad_e * up_e * silu_grad(gate_e)).astype(jnp.bfloat16)
    up_grad_e = (hidden_grad_e * act_e).astype(jnp.bfloat16)
    grad_ex_down = jnp.einsum(
        "erf,erd->efd", hidden_e, expert_grads_in, preferred_element_type=jnp.float32
    )
    grad_ex_gate = jnp.einsum(
        "erd,erf->edf", expert_rows, gate_grad_e, preferred_element_type=jnp.float32
    )
    grad_ex_up = jnp.einsum(
        "erd,erf->edf", expert_rows, up_grad_e, preferred_element_type=jnp.float32
    )
    expert_sums = (
        lax.psum_scatter(grad_ex_gate, DP, scatter_dimension=1, tiled=True),
        lax.psum_scatter(grad_ex_up, DP, scatter_dimension=1, tiled=True),
        lax.psum_scatter(grad_ex_down, DP, scatter_dimension=2, tiled=True),
    )
    rows_grad_e = jnp.einsum(
        "erf,edf->erd", gate_grad_e, ex_gate, preferred_element_type=jnp.float32
    )
    rows_grad_e = (
        rows_grad_e
        + jnp.einsum("erf,edf->erd", up_grad_e, ex_up, preferred_element_type=jnp.float32)
    ).astype(jnp.bfloat16)
    returned_grads = lax.all_to_all(
        to_owner(rows_grad_e), (EXP, CTX), split_axis=0, concat_axis=0, tiled=True
    )
    routed_grad = returned_grads.reshape(experts_all * capacity, model_width)[target]
    routed_grad = jnp.where(kept_rows[:, None], routed_grad, jnp.zeros_like(routed_grad)).astype(
        jnp.float32
    )
    norm_grad = jnp.sum(routed_grad.reshape(tokens_here, TOP, model_width), axis=1)
    choose = (
        routes[0][:, :, None] == jnp.arange(experts_all, dtype=jnp.int32)[None, None, :]
    ).astype(jnp.float32)
    probs_grad = jnp.einsum("tk,tke->te", gate_grads, choose)
    logit_grad = (
        router_probs * (probs_grad - jnp.sum(router_probs * probs_grad, axis=1, keepdims=True))
    ).astype(jnp.bfloat16)
    grad_router = jnp.dot(normed_two.T, logit_grad, preferred_element_type=jnp.float32)
    gate_logit_grad = (
        jnp.sum(cot_rows * shared_part, axis=1) * shared_gate * (1.0 - shared_gate)
    ).astype(jnp.bfloat16)
    grad_gate_vec = jnp.dot(gate_logit_grad, normed_two, preferred_element_type=jnp.float32)
    norm_grad = norm_grad + jnp.dot(logit_grad, router_full.T, preferred_element_type=jnp.float32)
    norm_grad = (
        norm_grad
        + gate_logit_grad.astype(jnp.float32)[:, None] * gate_vec.astype(jnp.float32)[None, :]
    )
    shared_hgrad = jnp.dot(grads_group, sh_down.T, preferred_element_type=jnp.float32)
    gate_grad_s = (shared_hgrad * up_pre * silu_grad(gate_pre)).astype(jnp.bfloat16)
    up_grad_s = (shared_hgrad * gate_act).astype(jnp.bfloat16)
    shared_rows_grad = jnp.dot(gate_grad_s, sh_gate.T, preferred_element_type=jnp.float32)
    shared_rows_grad = shared_rows_grad + jnp.dot(
        up_grad_s, sh_up.T, preferred_element_type=jnp.float32
    )
    groups = lax.axis_size(EXP)
    parts_cd = lax.axis_size((CTX, DP))
    rows_count = rows_group.shape[0]
    arr_gate = jnp.einsum(
        "td,tes->eds",
        rows_group,
        gate_grad_s.reshape(rows_count, groups, -1),
        preferred_element_type=jnp.float32,
    ).reshape(groups * model_width, -1)
    arr_up = jnp.einsum(
        "td,tes->eds",
        rows_group,
        up_grad_s.reshape(rows_count, groups, -1),
        preferred_element_type=jnp.float32,
    ).reshape(groups * model_width, -1)
    arr_down = jnp.einsum(
        "tes,tcd->ecsd",
        shared_hidden.reshape(rows_count, groups, -1),
        grads_group.reshape(rows_count, parts_cd, -1),
        preferred_element_type=jnp.float32,
    ).reshape(-1, model_width // parts_cd)
    sums_gate, sums_up, sums_down = (
        lax.psum_scatter(arr_gate, (EXP, CTX, DP), scatter_dimension=0, tiled=True),
        lax.psum_scatter(arr_up, (EXP, CTX, DP), scatter_dimension=0, tiled=True),
        lax.psum_scatter(arr_down, (EXP, CTX, DP), scatter_dimension=0, tiled=True),
    )
    norm_grad = norm_grad + shared_rows_grad
    residual_grad, grad_gain_two = norm_back(residual, inv_two, g_two, norm_grad)
    residual_grad = residual_grad + cot_rows
    low_residual = residual_grad.astype(jnp.bfloat16)
    grad_out_w = jnp.dot(attended.T, low_residual, preferred_element_type=jnp.float32)
    attended_grad = jnp.dot(low_residual, out_w.T, preferred_element_type=jnp.float32).astype(
        jnp.bfloat16
    )
    head_q_grad, head_k_grad, head_v_grad = lax.map(
        partial(attend_back, allowed=allowed, scale_factor=scale_factor),
        (head_q, head_k, head_v, to_heads(attended_grad), log_total),
    )
    key_sum, value_sum = (
        lax.psum_scatter(from_heads(head_k_grad), CTX, scatter_dimension=0, tiled=True),
        lax.psum_scatter(from_heads(head_v_grad), CTX, scatter_dimension=0, tiled=True),
    )
    query_low = from_heads(head_q_grad).astype(jnp.bfloat16)
    key_low = key_sum.astype(jnp.bfloat16)
    value_low = value_sum.astype(jnp.bfloat16)
    grad_query = jnp.dot(normed_one.T, query_low, preferred_element_type=jnp.float32)
    grad_key = jnp.dot(normed_one.T, key_low, preferred_element_type=jnp.float32)
    grad_value = jnp.dot(normed_one.T, value_low, preferred_element_type=jnp.float32)
    normed_grad = jnp.dot(query_low, query_w.T, preferred_element_type=jnp.float32)
    normed_grad = normed_grad + jnp.dot(key_low, key_w.T, preferred_element_type=jnp.float32)
    normed_grad = normed_grad + jnp.dot(value_low, value_w.T, preferred_element_type=jnp.float32)
    input_part, grad_gain_one = norm_back(x_rows, inv_one, g_one, normed_grad)
    input_grad = (residual_grad + input_part).astype(jnp.bfloat16)
    dense = (
        lax.psum_scatter(
            grad_gain_one, (EXP, CTX, DP), scatter_dimension=0, tiled=True
        ),
        lax.psum_scatter(grad_query, (EXP, CTX, DP), scatter_dimension=0, tiled=True),
        lax.psum_scatter(grad_key, (EXP, CTX, DP), scatter_dimension=0, tiled=True),
        lax.psum_scatter(grad_value, (EXP, CTX, DP), scatter_dimension=0, tiled=True),
        lax.psum_scatter(grad_out_w, (EXP, CTX, DP), scatter_dimension=0, tiled=True),
        lax.psum_scatter(
            grad_gain_two, (EXP, CTX, DP), scatter_dimension=0, tiled=True
        ),
        lax.psum_scatter(
            grad_router, (EXP, CTX, DP), scatter_dimension=0, tiled=True
        ),
        lax.psum_scatter(
            grad_gate_vec, (EXP, CTX, DP), scatter_dimension=0, tiled=True
        ),
    )
    return (
        output[None],
        input_grad[None],
        dense[0],
        dense[1],
        dense[2],
        dense[3],
        dense[4],
        dense[5],
        dense[6],
        dense[7],
        sums_gate,
        sums_up,
        sums_down,
        expert_sums[0],
        expert_sums[1],
        expert_sums[2],
    )

def attention_probs(q_blk, k_part, q_code, k_code, first_row, scale_factor):
    scores = lax.dot_general(
        q_blk, k_part, (((1,), (1,)), ((), ())), preferred_element_type=jnp.float32
    )
    row = first_row + lax.broadcasted_iota(jnp.int32, scores.shape, 0)
    col = lax.broadcasted_iota(jnp.int32, scores.shape, 1)
    allowed = ((col < row) & (k_code == q_code)) | (col == row)
    logits = jnp.where(allowed, scores * scale_factor, NEG)
    exp_scores = jnp.exp(logits - jnp.max(logits, axis=1, keepdims=True))
    return exp_scores * (1.0 / jnp.sum(exp_scores, axis=1, keepdims=True))


def attend_kernel(heads, step, qkv_ref, q_code_ref, k_code_ref, out_ref):
    seq_len = qkv_ref.shape[0]
    width = heads * HEAD_DIM
    for head in range(heads):
        at = head * HEAD_DIM
        for first in range(0, seq_len, step):
            upto = first + step
            probs = attention_probs(
                qkv_ref[first:upto, at : at + HEAD_DIM],
                qkv_ref[0:upto, width + at : width + at + HEAD_DIM],
                q_code_ref[first:upto, :],
                k_code_ref[0, :, 0:upto],
                first,
                HEAD_DIM**-0.5,
            )
            out_ref[first:upto, at : at + HEAD_DIM] = jnp.dot(
                probs.astype(jnp.bfloat16),
                qkv_ref[0:upto, 2 * width + at : 2 * width + at + HEAD_DIM],
                preferred_element_type=jnp.float32,
            ).astype(jnp.bfloat16)


def attend_back_kernel(
    heads, step, qkv_ref, grad_ref, q_code_ref, k_code_ref, out_ref, key_acc, value_acc
):
    seq_len = qkv_ref.shape[0]
    width = heads * HEAD_DIM
    for head in range(heads):
        at = head * HEAD_DIM
        key_at, value_at = width + at, 2 * width + at
        key_acc[...] = jnp.zeros_like(key_acc)
        value_acc[...] = jnp.zeros_like(value_acc)
        for first in range(0, seq_len, step):
            upto = first + step
            q_blk = qkv_ref[first:upto, at : at + HEAD_DIM]
            k_part = qkv_ref[0:upto, key_at : key_at + HEAD_DIM]
            v_part = qkv_ref[0:upto, value_at : value_at + HEAD_DIM]
            g_blk = grad_ref[first:upto, at : at + HEAD_DIM]
            probs = attention_probs(
                q_blk,
                k_part,
                q_code_ref[first:upto, :],
                k_code_ref[0, :, 0:upto],
                first,
                HEAD_DIM**-0.5,
            )
            prob_grad = lax.dot_general(
                g_blk, v_part, (((1,), (1,)), ((), ())), preferred_element_type=jnp.float32
            )
            inner = jnp.sum(probs * prob_grad, axis=1, keepdims=True)
            score_grad = (probs * (prob_grad - inner) * HEAD_DIM**-0.5).astype(jnp.bfloat16)
            out_ref[first:upto, at : at + HEAD_DIM] = jnp.dot(
                score_grad, k_part, preferred_element_type=jnp.float32
            ).astype(jnp.bfloat16)
            key_acc[0:upto, :] += lax.dot_general(
                score_grad, q_blk, (((0,), (0,)), ((), ())), preferred_element_type=jnp.float32
            )
            value_acc[0:upto, :] += lax.dot_general(
                probs.astype(jnp.bfloat16),
                g_blk,
                (((0,), (0,)), ((), ())),
                preferred_element_type=jnp.float32,
            )
        out_ref[:, key_at : key_at + HEAD_DIM] = key_acc[...].astype(jnp.bfloat16)
        out_ref[:, value_at : value_at + HEAD_DIM] = value_acc[...].astype(jnp.bfloat16)


def attention_call(qkv, grads, q_codes, k_codes, seq_len):
    rows, triple = qkv.shape
    width = triple // 3
    heads = width // HEAD_DIM
    step = min(256, seq_len)
    specs = [pl.BlockSpec((seq_len, triple), lambda s: (s, 0))]
    operands = [qkv]
    if grads is not None:
        specs.append(pl.BlockSpec((seq_len, width), lambda s: (s, 0)))
        operands.append(grads)
    specs += [
        pl.BlockSpec((seq_len, 1), lambda s: (s, 0)),
        pl.BlockSpec((1, 1, seq_len), lambda s: (s, 0, 0)),
    ]
    operands += [q_codes, k_codes]
    out_width = width if grads is None else triple
    body = attend_kernel if grads is None else attend_back_kernel
    passes = 2 if grads is None else 5
    area = rows * seq_len * heads
    return pl.pallas_call(
        partial(body, heads, step),
        grid=(rows // seq_len,),
        in_specs=specs,
        out_specs=pl.BlockSpec((seq_len, out_width), lambda s: (s, 0)),
        out_shape=jax.ShapeDtypeStruct((rows, out_width), jnp.bfloat16),
        scratch_shapes=[]
        if grads is None
        else [pltpu.VMEM((seq_len, HEAD_DIM), jnp.float32)] * 2,
        compiler_params=pltpu.CompilerParams(vmem_limit_bytes=48 * 2**20),
        cost_estimate=pl.CostEstimate(
            flops=2 * passes * area * HEAD_DIM,
            bytes_accessed=2 * rows * (triple + out_width),
            transcendentals=area,
        ),
    )(*operands)


MESH_ID = pl.DeviceIdType.MESH


def other_in_pair(index, bit):
    return index + bit - 2 * bit * (lax.div(index, bit) % 2)


def plane_places():
    at = lax.axis_index(EXP)
    core = lax.axis_index(CTX)
    across, along = other_in_pair(at, 1), other_in_pair(at, 2)
    return at, core, across, along, other_in_pair(along, 1)


def greet(across, along, core):
    barrier = pltpu.get_barrier_semaphore()
    for target in ({EXP: across}, {EXP: along}, {CTX: 1 - core}):
        pl.semaphore_signal(barrier, inc=1, device_id=target, device_id_type=MESH_ID)
    pl.semaphore_wait(barrier, 3)


def plane_gather_kernel(with_info, relative, *refs):
    if with_info:
        own_ref, info_ref, all_ref, info_all_ref, send_sem, recv_sem, local_sem = refs
    else:
        own_ref, all_ref, send_sem, recv_sem, local_sem = refs
    at, core, across, along, far = plane_places()
    rows = own_ref.shape[0]
    half = rows // 2
    top, bottom, whole = pl.ds(0, half), pl.ds(half, half), pl.ds(0, rows)
    greet(across, along, core)
    started = []
    twin_id = {CTX: 1 - core}

    def slot_of(place, shift, for_twin):
        if relative:
            return shift + 4 * for_twin
        return place * 2 + core

    def send(number, src, dst, target):
        copy = pltpu.make_async_remote_copy(
            src_ref=src,
            dst_ref=dst,
            send_sem=send_sem.at[number],
            recv_sem=recv_sem.at[number],
            device_id=target,
            device_id_type=MESH_ID,
        )
        copy.start()
        started.append(copy)
        return copy

    def piece(place, shift, part, for_twin=0):
        return all_ref.at[slot_of(place, shift, for_twin), part]

    x_top = send(0, own_ref.at[top], piece(at, 1, top), {EXP: across})
    y_bottom = send(1, own_ref.at[bottom], piece(at, 2, bottom), {EXP: along})
    x_bottom = send(2, own_ref.at[bottom], piece(at, 1, bottom), {EXP: across})
    y_top = send(3, own_ref.at[top], piece(at, 2, top), {EXP: along})
    twins = [send(4, own_ref, piece(at, 0, whole, 1), twin_id)]
    heres = [pltpu.make_async_copy(own_ref, piece(at, 0, whole), local_sem.at[0])]
    heres[0].start()
    if with_info:
        info_at = lambda place: info_all_ref.at[place * 2 + core]
        heres.append(pltpu.make_async_copy(info_ref, info_at(at), local_sem.at[1]))
        heres[1].start()
        info_x = send(13, info_ref, info_at(at), {EXP: across})
        info_y = send(14, info_ref, info_at(at), {EXP: along})
        twins.append(send(15, info_ref, info_at(at), twin_id))
        info_x.wait_recv()
        info_far = send(16, info_at(across), info_at(across), {EXP: along})
        twins.append(send(17, info_at(across), info_at(across), twin_id))
        info_y.wait_recv()
        twins.append(send(18, info_at(along), info_at(along), twin_id))
        info_far.wait_recv()
        twins.append(send(19, info_at(far), info_at(far), twin_id))

    def hand_on(number, place, shift, part):
        src = piece(place, shift, part)
        twins.append(send(number, src, piece(place, shift, part, 1), twin_id))

    x_top.wait_recv()
    far_top = send(5, piece(across, 1, top), piece(across, 3, top), {EXP: along})
    hand_on(6, across, 1, top)
    y_bottom.wait_recv()
    far_bottom = send(7, piece(along, 2, bottom), piece(along, 3, bottom), {EXP: across})
    hand_on(8, along, 2, bottom)
    x_bottom.wait_recv()
    hand_on(9, across, 1, bottom)
    y_top.wait_recv()
    hand_on(10, along, 2, top)
    far_top.wait_recv()
    hand_on(11, far, 3, top)
    far_bottom.wait_recv()
    hand_on(12, far, 3, bottom)
    for copy in twins:
        copy.wait_recv()
    for copy in started:
        copy.wait_send()
    for copy in heres:
        copy.wait()


def plane_gather(own, info, relative, number):
    plane = lax.axis_size(PLANE)
    operands = [own] if info is None else [own, info]
    outs = [jax.ShapeDtypeStruct((plane, *v.shape), v.dtype) for v in operands]
    anywhere = pl.BlockSpec(memory_space=pl.ANY)
    return pl.pallas_call(
        partial(plane_gather_kernel, info is not None, relative),
        out_shape=outs,
        in_specs=[anywhere] * len(operands),
        out_specs=[anywhere] * len(operands),
        scratch_shapes=[
            pltpu.SemaphoreType.DMA((20,)),
            pltpu.SemaphoreType.DMA((20,)),
            pltpu.SemaphoreType.DMA((2,)),
        ],
        compiler_params=pltpu.CompilerParams(collective_id=number, has_side_effects=True),
        cost_estimate=pl.CostEstimate(
            flops=0, bytes_accessed=own.size, transcendentals=0
        ),
    )(*operands)


def norm_qkv_kernel(hidden_ref, gain_ref, w_ref, norm_ref, qkv_ref):
    values = hidden_ref[...].astype(jnp.float32)
    inv = lax.rsqrt(jnp.mean(values * values, axis=1, keepdims=True) + EPS)
    norm_ref[...] = low(values * inv * gain_ref[...])
    qkv_ref[...] = low(mm(norm_ref[...], w_ref[...]))


def norm_qkv(hidden, gain, w, block):
    rows, width = hidden.shape
    cols = w.shape[1]
    return pl.pallas_call(
        norm_qkv_kernel,
        grid=(rows // block,),
        in_specs=[
            pl.BlockSpec((block, width), lambda i: (i, 0)),
            pl.BlockSpec((1, width), lambda i: (0, 0)),
            pl.BlockSpec((width, cols), lambda i: (0, 0)),
        ],
        out_specs=[
            pl.BlockSpec((block, width), lambda i: (i, 0)),
            pl.BlockSpec((block, cols), lambda i: (i, 0)),
        ],
        out_shape=[
            jax.ShapeDtypeStruct((rows, width), jnp.bfloat16),
            jax.ShapeDtypeStruct((rows, cols), jnp.bfloat16),
        ],
        compiler_params=pltpu.CompilerParams(vmem_limit_bytes=48 * 2**20),
        cost_estimate=pl.CostEstimate(
            flops=2 * rows * width * cols,
            bytes_accessed=4 * rows * width,
            transcendentals=0,
        ),
    )(hidden, gain, w)


def chosen_rows(slots, capacity):
    lanes = lax.broadcasted_iota(jnp.int32, (slots.shape[0], capacity), 1)
    return (slots == lanes).astype(jnp.bfloat16)


def hand_out(step_at, half, blocks, pieces, sems):
    copies = [
        pltpu.make_async_copy(blocks.at[k, part], goal, sems.at[number])
        for number, (k, part, goal) in enumerate(pieces)
    ]
    for k in range(half):

        @pl.when(step_at == half + k)
        def _():
            for copy, piece in zip(copies, pieces):
                if piece[0] == k:
                    copy.start()

    @pl.when(step_at == 2 * half - 1)
    def _():
        for copy in copies:
            copy.wait()


def output_kernel(
    half,
    hidden_ref,
    down_ref,
    rows_ref,
    slot_ref,
    sg_ref,
    gate_ref,
    cot_ref,
    *refs,
):
    near_refs, dots_ref, refs = refs[:half], refs[half], refs[half + 1 :]
    given, got, send_sem, recv_sem, out_sem = refs
    step_at = pl.program_id(0)
    is_far = step_at < half
    slot = lax.rem(step_at, half)
    twin_id = {CTX: 1 - lax.axis_index(CTX)}

    @pl.when(step_at == 0)
    def _():
        barrier = pltpu.get_barrier_semaphore()
        pl.semaphore_signal(barrier, inc=1, device_id=twin_id, device_id_type=MESH_ID)
        pl.semaphore_wait(barrier, 1)

    def block_copy(k):
        return pltpu.make_async_remote_copy(
            src_ref=given.at[k],
            dst_ref=got.at[k],
            send_sem=send_sem.at[k],
            recv_sem=recv_sem.at[k],
            device_id=twin_id,
            device_id_type=MESH_ID,
        )

    def make(store):
        chosen = chosen_rows(slot_ref[...], rows_ref.shape[1])
        hidden = hidden_ref[...].T
        tokens, width = cot_ref.shape
        step, lanes = 512, 128
        gate_dot = jnp.zeros((tokens, lanes), jnp.float32)
        shared_dot = jnp.zeros((tokens, lanes), jnp.float32)
        for first in range(0, width, step):
            cols = pl.ds(first, step)
            shared = mm(hidden, down_ref[:, cols])
            picked = mm(chosen, rows_ref[0, :, cols])
            cot = cot_ref[:, cols].astype(jnp.float32)
            gate_part, shared_part = picked * cot, shared * cot
            for at in range(0, step, lanes):
                gate_dot += gate_part[:, at : at + lanes]
                shared_dot += shared_part[:, at : at + lanes]
            store(cols, sg_ref[...] * shared + gate_ref[...] * picked)
        lane = lax.broadcasted_iota(jnp.int32, dots_ref.shape, 1)
        gate_dot = jnp.sum(gate_dot, axis=1, keepdims=True)
        shared_dot = jnp.sum(shared_dot, axis=1, keepdims=True)
        dots_ref[...] = jnp.where(lane == 0, gate_dot, jnp.where(lane == 1, shared_dot, 0.0))

    @pl.when(is_far)
    def _():
        def store(cols, total):
            given[slot, :, cols] = low(total)

        make(store)
        block_copy(slot).start()

    @pl.when(jnp.logical_not(is_far))
    def _():
        block_copy(slot).wait_recv()

        def store(cols, total):
            got[slot, :, cols] = low(total + got[slot, :, cols].astype(jnp.float32))

        make(store)

    everything = pl.ds(0, got.shape[1])
    pieces = [(k, everything, near_refs[k]) for k in range(half)]
    hand_out(step_at, half, got, pieces, out_sem)

    @pl.when(step_at == 2 * half - 1)
    def _():
        for k in range(half):
            block_copy(k).wait_send()


def output_parts(hidden, down, rows, slots, sg, gates, cot):
    blocks, capacity, width = rows.shape
    units, count = hidden.shape
    tokens, half = count // blocks, blocks // 2
    at = lambda i: lax.rem(i + half, blocks)
    column = pl.BlockSpec((tokens, 1), lambda i: (at(i), 0))
    return pl.pallas_call(
        partial(output_kernel, half),
        grid=(blocks,),
        in_specs=[
            pl.BlockSpec((units, tokens), lambda i: (0, at(i))),
            pl.BlockSpec((units, width), lambda i: (0, 0)),
            pl.BlockSpec((1, capacity, width), lambda i: (at(i), 0, 0)),
            column,
            column,
            column,
            pl.BlockSpec((tokens, width), lambda i: (at(i), 0)),
        ],
        out_specs=[
            *[pl.BlockSpec(memory_space=pl.ANY)] * half,
            pl.BlockSpec((tokens, 128), lambda i: (at(i), 0)),
        ],
        out_shape=[
            *[jax.ShapeDtypeStruct((tokens, width), jnp.bfloat16)] * half,
            jax.ShapeDtypeStruct((count, 128), jnp.float32),
        ],
        scratch_shapes=[
            pltpu.VMEM((half, tokens, width), jnp.bfloat16),
            pltpu.VMEM((half, tokens, width), jnp.bfloat16),
            pltpu.SemaphoreType.DMA((half,)),
            pltpu.SemaphoreType.DMA((half,)),
            pltpu.SemaphoreType.DMA((half,)),
        ],
        compiler_params=pltpu.CompilerParams(
            collective_id=4, has_side_effects=True, vmem_limit_bytes=56 * 2**20
        ),
        cost_estimate=pl.CostEstimate(
            flops=2 * count * width * (units + capacity),
            bytes_accessed=6 * count * width,
            transcendentals=0,
        ),
    )(hidden, down, rows, slots, sg, gates, cot)


def scatter_step(compute, out_ref, scratch):
    given, total, x_got, y_got, x_last, y_last, send_sem, recv_sem = scratch
    at, core, across, along, far = plane_places()
    step_at = pl.program_id(0)
    row = step_at // 2
    is_twin = step_at % 2 == 0
    rows = total.shape[1]
    half = rows // 2
    top, bottom = pl.ds(0, half), pl.ds(half, half)

    def copy_of(number, src, dst, target):
        return pltpu.make_async_remote_copy(
            src_ref=src,
            dst_ref=dst,
            send_sem=send_sem.at[number],
            recv_sem=recv_sem.at[number],
            device_id=target,
            device_id_type=MESH_ID,
        )

    def twin_copy(k):
        return copy_of(k, given.at[k % 2], total.at[k], {CTX: 1 - core})

    far_x = copy_of(4, total.at[0, top], x_got.at[0], {EXP: across})
    far_y = copy_of(5, total.at[0, bottom], y_got.at[0], {EXP: along})
    own_x = copy_of(6, total.at[1, top], x_got.at[1], {EXP: across})
    own_y = copy_of(7, total.at[2, bottom], y_got.at[1], {EXP: along})
    last_y = copy_of(8, total.at[2, top], y_last, {EXP: along})
    last_x = copy_of(9, total.at[1, bottom], x_last, {EXP: across})

    @pl.when(step_at == 0)
    def _():
        greet(across, along, core)

    @pl.when(is_twin)
    def _():
        @pl.when(row >= 2)
        def _():
            twin_copy(row - 2).wait_send()

        def store(cols, values):
            given[row % 2, :, cols] = low(values)

        compute(store)
        twin_copy(row).start()

    @pl.when(jnp.logical_not(is_twin))
    def _():
        twin_copy(row).wait_recv()

        def store(cols, values):
            total[row, :, cols] = low(values + total[row, :, cols].astype(jnp.float32))

        compute(store)

    @pl.when(step_at == 1)
    def _():
        far_x.start()
        far_y.start()

    @pl.when(step_at == 3)
    def _():
        own_x.start()

    @pl.when(step_at == 5)
    def _():
        own_y.start()

    @pl.when(step_at == 7)
    def _():
        def add_half(k, first, got):
            @pl.loop(0, half // 64)
            def _(i):
                take = pl.ds(pl.multiple_of(i * 64, 64), 64)
                into = pl.ds(pl.multiple_of(first + i * 64, 64), 64)
                total[k, into] = low(
                    total[k, into].astype(jnp.float32) + got[0, take].astype(jnp.float32)
                )

        def finish(first, near, later):
            @pl.loop(0, half // 64)
            def _(i):
                take = pl.ds(pl.multiple_of(i * 64, 64), 64)
                into = pl.ds(pl.multiple_of(first + i * 64, 64), 64)
                out_ref[into] = (
                    total[3, into].astype(jnp.float32)
                    + near[1, take].astype(jnp.float32)
                    + later[take].astype(jnp.float32)
                )

        far_x.wait_recv()
        add_half(2, 0, x_got)
        last_y.start()
        far_y.wait_recv()
        add_half(1, half, y_got)
        last_x.start()
        own_x.wait_recv()
        last_y.wait_recv()
        finish(0, x_got, y_last)
        own_y.wait_recv()
        last_x.wait_recv()
        finish(half, y_got, x_last)
        for copy in (twin_copy(2), twin_copy(3), far_x, far_y, own_x, own_y, last_y, last_x):
            copy.wait_send()


def step_slot(i):
    row = i // 2
    shift = jnp.where(row == 0, 3, jnp.where(row == 3, 0, row))
    return shift + 4 * (1 - i % 2)


def scatter_scratch(tokens, width):
    vmem = lambda *shape: pltpu.VMEM(shape, jnp.bfloat16)
    return [
        vmem(2, tokens, width),
        vmem(4, tokens, width),
        vmem(2, tokens // 2, width),
        vmem(2, tokens // 2, width),
        vmem(tokens // 2, width),
        vmem(tokens // 2, width),
        pltpu.SemaphoreType.DMA((10,)),
        pltpu.SemaphoreType.DMA((10,)),
    ]


def n2_grad_kernel(dgate_ref, dup_ref, gate_ref, up_ref, rows_ref, slot_ref, out_ref, *scratch):
    def compute(store):
        chosen = chosen_rows(slot_ref[...], rows_ref.shape[1])
        dgate, dup = dgate_ref[...].T, dup_ref[...].T
        step = 512
        for first in range(0, gate_ref.shape[1], step):
            cols = pl.ds(first, step)
            total = mm(dgate, gate_ref[:, cols]) + mm(dup, up_ref[:, cols])
            store(cols, total + mm(chosen, rows_ref[0, :, cols]))

    scatter_step(compute, out_ref, scratch)


def n2_grad_sum(dgate, dup, gate_w, up_w, rows, slots):
    blocks, capacity, width = rows.shape
    units, count = dgate.shape
    tokens = count // blocks
    by_units = pl.BlockSpec((units, tokens), lambda i: (0, step_slot(i)))
    whole = pl.BlockSpec((units, width), lambda i: (0, 0), pipeline_mode=pl.Buffered(1))
    return pl.pallas_call(
        n2_grad_kernel,
        grid=(blocks,),
        in_specs=[
            by_units,
            by_units,
            whole,
            whole,
            pl.BlockSpec((1, capacity, width), lambda i: (step_slot(i), 0, 0)),
            pl.BlockSpec((tokens, 1), lambda i: (step_slot(i), 0)),
        ],
        out_specs=pl.BlockSpec((tokens, width), lambda i: (0, 0)),
        out_shape=jax.ShapeDtypeStruct((tokens, width), jnp.float32),
        scratch_shapes=scatter_scratch(tokens, width),
        compiler_params=pltpu.CompilerParams(
            collective_id=3, has_side_effects=True, vmem_limit_bytes=56 * 2**20
        ),
        cost_estimate=pl.CostEstimate(
            flops=2 * count * width * (2 * units + capacity),
            bytes_accessed=4 * count * width,
            transcendentals=0,
        ),
    )(dgate, dup, gate_w, up_w, rows, slots)


def unit_grad_kernel(hid_ref, dgate_ref, dup_ref, cot_ref, n2_ref, out_ref):
    units = hid_ref.shape[0]
    out_ref[0, :units] = low(mm(hid_ref[...], cot_ref[...]))
    out_ref[0, units : 2 * units] = low(mm(dgate_ref[...], n2_ref[...]))
    out_ref[0, 2 * units :] = low(mm(dup_ref[...], n2_ref[...]))


def unit_grads(hidden, dgate, dup, cots, n2, depth, halves):
    units, count = hidden.shape
    width = n2.shape[1]
    cols = width // (depth * halves)
    whole = pl.BlockSpec((units, count), lambda i: (0, 0), pipeline_mode=pl.Buffered(1))
    strip = pl.BlockSpec((count, cols), lambda i: (0, i))
    return pl.pallas_call(
        unit_grad_kernel,
        grid=(depth * halves,),
        in_specs=[whole, whole, whole, strip, strip],
        out_specs=pl.BlockSpec(
            (1, 3 * units, cols), lambda i: (lax.rem(i, depth), 0, i // depth)
        ),
        out_shape=jax.ShapeDtypeStruct((depth, 3 * units, halves * cols), jnp.bfloat16),
        compiler_params=pltpu.CompilerParams(vmem_limit_bytes=48 * 2**20),
        cost_estimate=pl.CostEstimate(
            flops=6 * units * count * width,
            bytes_accessed=2 * (3 * units * count + 2 * count * width + 3 * units * width),
            transcendentals=0,
        ),
    )(hidden, dgate, dup, cots, n2)


def n1_grad_kernel(half, grads_ref, w_ref, *refs):
    near_refs, refs = refs[:half], refs[half:]
    rows_in, given, got, load_sem, send_sem, recv_sem, out_sem = refs
    place, core = lax.axis_index(EXP), lax.axis_index(CTX)
    step_at = pl.program_id(0)
    is_far = step_at < half
    slot = lax.rem(step_at, half)
    tokens = rows_in.shape[1]
    twin_id = {CTX: 1 - core}

    def load(step, k):
        column, level = place % 2, place // 2
        there = (column + k % 2) % 2 + 2 * ((level + k // 2) % 2)
        owner = 1 - core if step < half else core
        first = pl.multiple_of((there * 2 + owner) * tokens, tokens)
        return pltpu.make_async_copy(
            grads_ref.at[pl.ds(first, tokens)], rows_in.at[step], load_sem.at[step]
        )

    loads = [load(step, step % half) for step in range(2 * half)]

    @pl.when(step_at == 0)
    def _():
        for copy in loads:
            copy.start()
        barrier = pltpu.get_barrier_semaphore()
        pl.semaphore_signal(barrier, inc=1, device_id=twin_id, device_id_type=MESH_ID)
        pl.semaphore_wait(barrier, 1)

    for step in range(2 * half):

        @pl.when(step_at == step)
        def _():
            loads[step].wait()

    def block_copy(k):
        return pltpu.make_async_remote_copy(
            src_ref=given.at[k],
            dst_ref=got.at[k],
            send_sem=send_sem.at[k],
            recv_sem=recv_sem.at[k],
            device_id=twin_id,
            device_id_type=MESH_ID,
        )

    def make(store):
        step = 512
        for first in range(0, w_ref.shape[0], step):
            cols = pl.ds(first, step)
            store(cols, mm(rows_in[step_at], w_ref[cols, :], ((1,), (1,))))

    @pl.when(is_far)
    def _():
        def store(cols, total):
            given[slot, :, cols] = low(total)

        make(store)
        block_copy(slot).start()

    @pl.when(jnp.logical_not(is_far))
    def _():
        block_copy(slot).wait_recv()

        def store(cols, total):
            got[slot, :, cols] = low(total + got[slot, :, cols].astype(jnp.float32))

        make(store)

    own, x_send, y_send, rest = near_refs
    top, bottom = pl.ds(0, tokens // 2), pl.ds(tokens // 2, tokens // 2)
    pieces = [
        (0, pl.ds(0, tokens), own),
        (1, top, x_send.at[bottom]),
        (1, bottom, rest.at[bottom]),
        (2, top, rest.at[top]),
        (2, bottom, y_send.at[bottom]),
        (3, top, x_send.at[top]),
        (3, bottom, y_send.at[top]),
    ]
    hand_out(step_at, half, got, pieces, out_sem)

    @pl.when(step_at == 2 * half - 1)
    def _():
        for k in range(half):
            block_copy(k).wait_send()


def n1_grad_parts(grads, w, blocks):
    rows, cols = grads.shape
    width = w.shape[0]
    tokens, half = rows // blocks, blocks // 2
    return pl.pallas_call(
        partial(n1_grad_kernel, half),
        grid=(blocks,),
        in_specs=[
            pl.BlockSpec(memory_space=pl.ANY),
            pl.BlockSpec((width, cols), lambda i: (0, 0)),
        ],
        out_specs=[pl.BlockSpec(memory_space=pl.ANY)] * half,
        out_shape=[jax.ShapeDtypeStruct((tokens, width), jnp.bfloat16)] * half,
        scratch_shapes=[
            pltpu.VMEM((blocks, tokens, cols), jnp.bfloat16),
            pltpu.VMEM((half, tokens, width), jnp.bfloat16),
            pltpu.VMEM((half, tokens, width), jnp.bfloat16),
            pltpu.SemaphoreType.DMA((blocks,)),
            pltpu.SemaphoreType.DMA((half,)),
            pltpu.SemaphoreType.DMA((half,)),
            pltpu.SemaphoreType.DMA((7,)),
        ],
        compiler_params=pltpu.CompilerParams(
            collective_id=1, has_side_effects=True, vmem_limit_bytes=48 * 2**20
        ),
        cost_estimate=pl.CostEstimate(
            flops=2 * rows * width * cols,
            bytes_accessed=4 * rows * width,
            transcendentals=0,
        ),
    )(grads, w)


def after(values, others):
    return lax.optimization_barrier((values, others))[0]


def swap(values, bits):
    return lax.ppermute(values, EXP, [(i, i ^ bits) for i in range(4)])


def twin(values):
    return lax.ppermute(values, CTX, [(0, 1), (1, 0)])


def twin_sums(ours, theirs):
    got = twin(theirs)
    return [low(ours[k].astype(jnp.float32) + got[k].astype(jnp.float32)) for k in range(4)]


def hops(sums):
    return [sums[0]] + [swap(sums[k], k) for k in (1, 2, 3)]


def two_stage_sum(own, x_send, y_send, rest, later):
    half = own.shape[0] // 2
    wide = lambda v: v.astype(jnp.float32)
    x_got, y_got = swap(x_send, 1), swap(y_send, 2)
    y_last = swap(low(wide(rest[:half]) + wide(x_got[:half])), 2)
    x_last = swap(low(wide(rest[half:]) + wide(y_got[:half])), 1)
    x_last, y_last = after((x_last, y_last), later)
    return jnp.concatenate(
        [
            wide(own[:half]) + wide(x_got[half:]) + wide(y_last),
            wide(own[half:]) + wide(y_got[half:]) + wide(x_last),
        ]
    )


def sum_up(parts):
    return sum(v.astype(jnp.float32) for v in parts)


def mm(left, right, dims=((1,), (0,))):
    return lax.dot_general(left, right, (dims, ((), ())), preferred_element_type=jnp.float32)


def low(values):
    return values.astype(jnp.bfloat16)


def local_plane(
    hidden,
    cotangent,
    segments,
    padding,
    routes,
    order,
    norm1_gain,
    w_query,
    w_key,
    w_value,
    w_out,
    norm2_gain,
    router,
    shared_gate_vec,
    shared_w_gate,
    shared_w_up,
    shared_w_down,
    expert_w_gate,
    expert_w_up,
    expert_w_down,
):
    plane = lax.axis_size(PLANE)
    groups = lax.axis_size(EXP)
    halves = lax.axis_size(CTX)
    depth = lax.axis_size(DP)
    me = lax.axis_index(PLANE)
    core = lax.axis_index(CTX)
    tokens, width = hidden.shape[1], hidden.shape[2]
    all_tokens = plane * tokens
    seq_len = halves * tokens
    experts_all = router.shape[1]
    head_cols = width // plane
    shard = width // depth

    token_info = jnp.concatenate(
        [segments + 1, jnp.where(padding > 0, segments + 1, 0), order[0], routes[0].T]
    )
    info_rows = token_info.shape[0]
    token_info = jnp.concatenate([token_info, jnp.zeros((8 - info_rows, tokens), jnp.int32)])

    hidden_all, info_all = plane_gather(hidden[0], token_info, False, 0)
    hidden_all = hidden_all.reshape(all_tokens, width)
    place = lax.axis_index(EXP)
    away = [(place ^ k) * 2 + (core ^ j) for j in (0, 1) for k in range(4)]
    away = jnp.stack(away)
    out_rows = shard // plane
    w_out_part = lax.dynamic_slice(w_out, (me * out_rows, 0), (out_rows, width))
    w_qkv_part = jnp.concatenate(
        [
            lax.dynamic_slice(w, (0, me * head_cols), (shard, head_cols))
            for w in (w_query, w_key, w_value)
        ]
        + [router, norm1_gain[:, None], norm2_gain[:, None], shared_gate_vec[:, None]]
        + [jnp.zeros((shard, 128 - experts_all - 3), jnp.bfloat16)]
        + [w_out_part.reshape(shard, -1)],
        axis=1,
    )
    w_qkv = lax.all_gather(w_qkv_part, DP, axis=0, tiled=True)
    w_out_part = w_qkv[:, 3 * head_cols + 128 :].reshape(depth, out_rows, width)
    small = w_qkv[:, 3 * head_cols : 3 * head_cols + 128].T
    w_qkv = w_qkv[:, : 3 * head_cols]
    router_t = small[:experts_all]
    g_one = small[experts_all].astype(jnp.float32)
    g_two = small[experts_all + 1].astype(jnp.float32)
    gate_vec = small[experts_all + 2]
    w_out_part = after(w_out_part, info_all)
    w_out_got = [swap(w_out_part, k) for k in (1, 2, 3)]

    def normed(values, gain):
        values = values.astype(jnp.float32)
        inv = lax.rsqrt(jnp.mean(values * values, axis=1, keepdims=True) + EPS)
        return values, inv, low(values * inv * gain)

    n1_all, qkv = norm_qkv(hidden_all, g_one[None], w_qkv, tokens)
    q_codes = info_all[:, 0].reshape(all_tokens, 1)
    k_codes = info_all[:, 1].reshape(all_tokens // seq_len, 1, seq_len)
    attended_cols = attention_call(qkv, None, q_codes, k_codes, seq_len)
    pieces = [w_out_part] + [after(v, attended_cols) for v in w_out_got]
    w_out_near = jnp.zeros((depth, groups, 1, out_rows, width), jnp.bfloat16)
    for k in range(4):
        w_out_near = lax.dynamic_update_slice(
            w_out_near, pieces[k][:, None, None], (0, place ^ k, 0, 0, 0)
        )
    w_out_far = twin(w_out_near)
    w_out_full = jnp.where(
        core == 0,
        jnp.concatenate([w_out_near, w_out_far], axis=2),
        jnp.concatenate([w_out_far, w_out_near], axis=2),
    ).reshape(width, width)

    x_rows, inv_one, _ = normed(hidden[0], g_one)
    cot_rows = cotangent[0].astype(jnp.float32)

    def to_tokens(cols):
        got = lax.all_to_all(
            cols.reshape(plane, tokens, head_cols), PLANE, split_axis=0, concat_axis=0, tiled=True
        )
        return got.transpose(1, 0, 2).reshape(tokens, width)

    def to_columns(rows_in):
        send = rows_in.reshape(tokens, plane, head_cols).transpose(1, 0, 2)
        got = lax.all_to_all(send, PLANE, split_axis=0, concat_axis=0, tiled=True)
        return got.reshape(all_tokens, head_cols)

    attended = to_tokens(attended_cols)
    residual = x_rows + mm(attended, w_out_full)
    residual, inv_two, n2 = normed(residual, g_two)

    units = shared_w_gate.shape[1]
    part = units // (depth * halves)
    pick = lambda w: lax.dynamic_index_in_dim(
        w.reshape(w.shape[0], depth, halves, part), core, axis=2, keepdims=False
    ).reshape(w.shape[0], depth * part)
    sh_gate_up = jnp.concatenate([pick(shared_w_gate), pick(shared_w_up)], axis=1)
    sh_gate_up = lax.all_gather(sh_gate_up, DP, axis=0, tiled=True)
    sh_gate_t, sh_up_t = sh_gate_up[:, : depth * part].T, sh_gate_up[:, depth * part :].T
    sh_down = lax.all_gather(
        lax.dynamic_slice(shared_w_down, (core * part, 0), (part, width)), DP, axis=0, tiled=True
    )
    n2 = after(n2, sh_gate_up)
    n2_all = plane_gather(n2, None, True, 2)[0].reshape(all_tokens, width)
    cot_own = after(cotangent[0], n2_all)
    cot_got = [swap(cot_own, k) for k in (1, 2, 3)]
    ex_gate = lax.all_gather(after(expert_w_gate[0], info_all), DP, axis=0, tiled=True)
    ex_up = lax.all_gather(after(expert_w_up[0], info_all), DP, axis=0, tiled=True)
    ex_down = lax.all_gather(after(expert_w_down[0], info_all), DP, axis=1, tiled=True)

    small_w = jnp.concatenate([router_t, gate_vec[None]])

    def gates_of(rows_in):
        both = mm(rows_in, small_w, ((1,), (1,)))
        z = both[:, :experts_all]
        e = jnp.exp(z - jnp.max(z, axis=1, keepdims=True))
        return e / jnp.sum(e, axis=1, keepdims=True), jax.nn.sigmoid(both[:, experts_all:])

    probs_all, sg_all = gates_of(n2_all)
    expert_gate = lax.dynamic_slice(probs_all, (0, me), (all_tokens, 1))

    capacity = (9 * tokens * TOP + 8 * experts_all - 1) // (8 * experts_all)
    info_away = info_all[away]
    order_all = info_away[:, 2]
    routed_here = jnp.any(info_away[:, 3 : 3 + TOP] == me, axis=1)
    earlier = (order_all[:, None, :] < order_all[:, :, None]) & routed_here[:, None, :]
    slots = jnp.sum(earlier.astype(jnp.int32), axis=2)
    slots = jnp.where(routed_here, slots, capacity)
    chosen = slots[:, None, :] == jnp.arange(capacity, dtype=jnp.int32)[None, :, None]
    onehot = chosen.astype(jnp.bfloat16)

    def rows_of(values):
        got = lax.dot_general(
            onehot,
            values.reshape(plane, tokens, width),
            (((2,), (1,)), ((0,), (0,))),
            preferred_element_type=jnp.float32,
        )
        return got.reshape(plane * capacity, width)

    slot_gates = jnp.sum(
        jnp.where(chosen, expert_gate.reshape(plane, 1, tokens), 0.0), axis=2
    ).reshape(plane * capacity, 1)
    expert_rows = low(rows_of(n2_all))
    gate_pre = mm(sh_gate_t, n2_all, ((1,), (1,)))
    up_pre = mm(sh_up_t, n2_all, ((1,), (1,)))
    gate_act = gate_pre * jax.nn.sigmoid(gate_pre)
    shared_hidden = low(gate_act * up_pre)
    expert_rows = after(expert_rows, (shared_hidden, sh_down))
    gate_e = mm(expert_rows, ex_gate)
    up_e = mm(expert_rows, ex_up)
    act_e = gate_e * jax.nn.sigmoid(gate_e)
    hidden_e = low(act_e * up_e)
    cot_near = jnp.concatenate([cot_own] + [after(v, gate_e) for v in cot_got])
    cot_all = jnp.concatenate([cot_near, twin(cot_near)])
    row_cots = low(rows_of(cot_all))
    row_grads = low(row_cots.astype(jnp.float32) * slot_gates)

    shared_grads = low(sg_all * cot_all.astype(jnp.float32))
    shared_hgrad = mm(sh_down, shared_grads, ((1,), (1,)))
    gate_grad_s = low(shared_hgrad * up_pre * silu_grad(gate_pre))
    up_grad_s = low(shared_hgrad * gate_act)
    rows_out = width // (halves * depth)

    def shared_scatter(total):
        first, second = total[:, :, :rows_out], total[:, :, rows_out:]
        keep = jnp.where(core == 0, first, second)
        got = twin(jnp.where(core == 0, second, first))
        both = [v.reshape(3, depth, part, rows_out) for v in (keep, got)]
        both = jnp.where(core == 0, jnp.stack(both, axis=2), jnp.stack(both[::-1], axis=2))
        return both.reshape(3, units, rows_out).astype(jnp.float32)

    scatter = lambda v, dim: lax.psum_scatter(v, DP, scatter_dimension=dim, tiled=True)
    shared_sums = unit_grads(
        shared_hidden, gate_grad_s, up_grad_s, shared_grads, n2_all, depth, halves
    )
    shared_sums = scatter(shared_sums.reshape(3 * depth * depth * part, -1), 0)
    result_e = low(mm(hidden_e, ex_down))
    hgrad_e = mm(row_grads, ex_down, ((1,), (1,)))
    gate_grad_e = low(hgrad_e * up_e * silu_grad(gate_e))
    up_grad_e = low(hgrad_e * act_e)

    grad_ex_down = low(mm(hidden_e, row_grads, ((0,), (0,))))
    slots = slots.reshape(all_tokens, 1)
    *out_near, dots = output_parts(
        shared_hidden,
        sh_down,
        result_e.reshape(plane, capacity, width),
        slots,
        sg_all,
        expert_gate,
        cot_all,
    )
    expert_rows = after(expert_rows, out_near)
    grad_ex_gate = low(mm(expert_rows, gate_grad_e, ((0,), (0,))))
    grad_ex_up = low(mm(expert_rows, up_grad_e, ((0,), (0,))))
    grads_made = (grad_ex_down, grad_ex_gate, grad_ex_up)
    grads = [scatter(v, dim) for v, dim in zip(grads_made, (1, 0, 0))]
    rows_grad = low(
        mm(gate_grad_e, ex_gate, ((1,), (1,))) + mm(up_grad_e, ex_up, ((1,), (1,)))
    )

    out_got = hops(out_near)
    slots, out_got, _ = lax.optimization_barrier((slots, out_got, (shared_sums, grads_made)))
    n2_grad = n2_grad_sum(
        gate_grad_s,
        up_grad_s,
        sh_gate_t,
        sh_up_t,
        rows_grad.reshape(plane, capacity, width),
        slots,
    )

    dots = dots.reshape(plane, tokens, 128)[:, :, :2].transpose(0, 2, 1)
    back = jnp.arange(plane, dtype=jnp.int32) ^ me
    dots = dots[(back // 2) + 4 * (back % 2)]
    dots = lax.all_to_all(dots, PLANE, split_axis=0, concat_axis=0, tiled=True)
    probs_grad = dots[:, 0].T
    probs, sg = gates_of(n2)
    logit_grad = low(probs * (probs_grad - jnp.sum(probs * probs_grad, axis=1, keepdims=True)))
    sg_logit_grad = low(jnp.sum(dots[:, 1], axis=0)[:, None] * sg * (1.0 - sg))
    n2_grad = (
        n2_grad
        + mm(logit_grad, router_t)
        + sg_logit_grad.astype(jnp.float32) * gate_vec.astype(jnp.float32)[None]
    )
    residual_grad, grad_gain_two = norm_back(residual, inv_two, g_two, n2_grad)
    residual_grad = residual_grad + cot_rows
    low_residual = low(residual_grad)

    attended_grad = low(mm(low_residual, w_out_full, ((1,), (1,))))
    low_residual = after(low_residual, attended_grad)
    output = low(residual + sum_up(after(out_got, attended_grad)))
    attended_grad = to_columns(attended_grad)
    grad_out = low(mm(attended, low_residual, ((0,), (0,))))
    grad_out = grad_out.reshape(groups, halves, width // plane, width)
    block_of = lambda k, c: lax.dynamic_slice(
        grad_out, (place ^ k, c, 0, 0), (1, 1, width // plane, width)
    )[0, 0]
    out_grad_sums = twin_sums(
        [block_of(k, core) for k in range(4)],
        jnp.stack([block_of(k, 1 - core) for k in range(4)]),
    )
    dz_all = jnp.concatenate([logit_grad, sg_logit_grad], axis=1)
    dz_all = after(dz_all, out_grad_sums)
    small_grads = mm(n2, dz_all, ((0,), (0,)))
    small_grads = jnp.concatenate([small_grads, grad_gain_two[:, None]], axis=1).T
    small_grads = jnp.pad(small_grads, ((0, 14 - experts_all), (0, 0)))
    small_grads = small_grads.reshape(16, plane, width // plane).transpose(1, 0, 2)
    attended_grad, small_grads = lax.optimization_barrier((attended_grad, small_grads))
    attended_grad = after(attended_grad, (out_grad_sums, output, grads[0]))
    qkv_grad = attention_call(qkv, attended_grad, q_codes, k_codes, seq_len)
    out_grad_got = hops(out_grad_sums)
    qkv_grad, out_grad_got = lax.optimization_barrier((qkv_grad, out_grad_got))
    small_grads = after(small_grads, qkv_grad)
    small_grads = jnp.sum(
        lax.all_to_all(small_grads, PLANE, split_axis=0, concat_axis=0, tiled=True), axis=0
    )
    grad_qkv = low(mm(n1_all, qkv_grad, ((0,), (0,))))
    fine = shard // plane
    grad_qkv = (
        grad_qkv.reshape(plane, depth, fine, 3 * head_cols)
        .transpose(1, 0, 2, 3)
        .reshape(width, 3 * head_cols)
    )
    qkv_grad, small_grads, _ = lax.optimization_barrier(
        (qkv_grad, small_grads, (grad_qkv, grads[1]))
    )
    n1_near = n1_grad_parts(qkv_grad, w_qkv, plane)
    grad_out = low(sum_up(out_grad_got))
    grad_qkv = lax.psum_scatter(grad_qkv, DP, scatter_dimension=0, tiled=True)
    qkv_sum = grad_qkv
    w_rows = (
        w_qkv.reshape(plane, depth, fine, 3 * head_cols)
        .transpose(1, 0, 2, 3)
        .reshape(depth, plane * fine, 3 * head_cols)
    )
    w_rows = lax.dynamic_index_in_dim(w_rows, lax.axis_index(DP), axis=0, keepdims=False)
    gain_dots = jnp.sum(grad_qkv.astype(jnp.float32) * w_rows.astype(jnp.float32), axis=1)
    gain_dots = lax.all_to_all(
        gain_dots.reshape(plane, 1, fine), PLANE, split_axis=0, concat_axis=0, tiled=True
    )
    my_gain = lax.dynamic_slice(
        g_one, ((me * depth + lax.axis_index(DP)) * fine,), (fine,)
    )
    grad_gain_one = jnp.sum(gain_dots[:, 0], axis=0) / my_gain
    grad_qkv = lax.all_to_all(
        grad_qkv.reshape(plane, fine, 3 * head_cols),
        PLANE,
        split_axis=0,
        concat_axis=0,
        tiled=True,
    )
    grad_qkv = (
        grad_qkv.reshape(plane, fine, 3, head_cols)
        .transpose(2, 1, 0, 3)
        .reshape(3, fine, width)
        .astype(jnp.float32)
    )
    grad_ex_down, grad_ex_gate, grad_ex_up = [
        v.astype(jnp.float32)[None] for v in after(grads, n1_near)
    ]
    grad_out = scatter(after(grad_out, qkv_sum), 0).astype(jnp.float32)
    shared_sums = after(shared_sums, n1_near)
    shared_sums = shared_scatter(shared_sums.reshape(3, units // halves, -1))
    grad_sh_down, grad_sh_gate, grad_sh_up = [shared_sums[k] for k in range(3)]
    grad_sh_gate, grad_sh_up = grad_sh_gate.T, grad_sh_up.T
    small_grads = after(small_grads, n1_near)
    small_grads = small_grads.reshape(16, depth, shard // plane).transpose(1, 0, 2)
    small_grads = jnp.sum(
        lax.all_to_all(small_grads, DP, split_axis=0, concat_axis=0, tiled=True), axis=0
    )
    n1_grad = two_stage_sum(*n1_near, grad_qkv)
    input_part, _ = norm_back(x_rows, inv_one, g_one, n1_grad)
    input_grad = low(residual_grad + input_part)
    return (
        output[None],
        input_grad[None],
        grad_gain_one,
        grad_qkv[0],
        grad_qkv[1],
        grad_qkv[2],
        grad_out,
        small_grads[experts_all + 1],
        small_grads[:experts_all].T,
        small_grads[experts_all],
        grad_sh_gate,
        grad_sh_up,
        grad_sh_down,
        grad_ex_gate,
        grad_ex_up,
        grad_ex_down,
    )


def solution(mesh):
    in_specs = (
        P((EXP, DP), CTX, None),
        P((EXP, DP), CTX, None),
        P((EXP, DP), CTX),
        P((EXP, DP), CTX),
        P((EXP, DP), CTX, None),
        P((EXP, DP), CTX, None),
        P(DP),
        P(DP, None),
        P(DP, None),
        P(DP, None),
        P(DP, None),
        P(DP),
        P(DP, None),
        P(DP),
        P(DP, EXP),
        P(DP, EXP),
        P((EXP, DP), None),
        P((EXP, CTX), DP, None),
        P((EXP, CTX), DP, None),
        P((EXP, CTX), None, DP),
    )
    out_specs = (
        P((EXP, DP), CTX, None),
        P((EXP, DP), CTX, None),
        P((EXP, CTX, DP)),
        P((EXP, CTX, DP), None),
        P((EXP, CTX, DP), None),
        P((EXP, CTX, DP), None),
        P((EXP, CTX, DP), None),
        P((EXP, CTX, DP)),
        P((EXP, CTX, DP), None),
        P((EXP, CTX, DP)),
        P((CTX, DP), EXP),
        P((CTX, DP), EXP),
        P(EXP, (CTX, DP)),
        P((EXP, CTX), DP, None),
        P((EXP, CTX), DP, None),
        P((EXP, CTX), None, DP),
    )
    plane = mesh.shape[EXP] * mesh.shape[CTX]

    def run(*args):
        square = mesh.shape[EXP] == 4 and mesh.shape[CTX] == 2 and mesh.shape[DP] == 4
        one_each = square and args[12].shape[1] == plane
        local = local_plane if one_each else local_general
        return jax.shard_map(
            local, mesh=mesh, in_specs=in_specs, out_specs=out_specs, check_vma=False
        )(*args)

    return run
```

```python
from functools import partial

import jax
import jax.numpy as jnp
from jax import lax
from jax.experimental import pallas as pl
from jax.experimental.pallas import tpu as pltpu
from jax.sharding import PartitionSpec as P

EXP, CTX, DP = "experts", "context", "dp"
PLANE = (EXP, CTX)
HEADS = 16
HEAD_DIM = 128
TOP = 4


EPS = 1e-06
NEG = -1e30


def silu_grad(pre_act):
    logistic = jax.nn.sigmoid(pre_act)
    return logistic * (1.0 + pre_act * (1.0 - logistic))


def block_slots(route_row, priority, expert_count):
    matches = (route_row[:, None] == jnp.arange(expert_count, dtype=jnp.int32)[None, :]).astype(
        jnp.int32
    )
    ordered = jnp.zeros_like(matches).at[priority].set(matches)
    before = jnp.cumsum(ordered, axis=0) - ordered
    return jnp.sum(before[priority] * matches, axis=1)


def norm_back(values_in, inv_rms, gain_vec, gradient):
    weighted = gradient * gain_vec
    inner_sum = jnp.mean(weighted * values_in, axis=1, keepdims=True)
    d_value = inv_rms * weighted - values_in * inv_rms**3 * inner_sum
    d_gain = jnp.sum(gradient * values_in * inv_rms, axis=0)
    return (d_value, d_gain)


def attend_head(packed, allowed, scale_factor):
    query_h, key_h, value_h = packed
    raw_scores = jnp.einsum("th,lh->tl", query_h, key_h, preferred_element_type=jnp.float32)
    logits = jnp.where(allowed, raw_scores * scale_factor, NEG)
    row_max = jnp.max(logits, axis=1, keepdims=True)
    exp_scores = jnp.exp(logits - row_max)
    row_total = jnp.sum(exp_scores, axis=1, keepdims=True)
    attn_probs = (exp_scores / row_total).astype(jnp.bfloat16)
    head_out = jnp.dot(attn_probs, value_h, preferred_element_type=jnp.float32).astype(jnp.bfloat16)
    return (head_out, row_max + jnp.log(row_total))


def attend_back(packed, allowed, scale_factor):
    query_h, key_h, value_h, out_grad, log_total = packed
    raw_scores = jnp.einsum("th,lh->tl", query_h, key_h, preferred_element_type=jnp.float32)
    logits = jnp.where(allowed, raw_scores * scale_factor, NEG)
    attn_probs = jnp.exp(logits - log_total)
    prob_grad = jnp.einsum("th,lh->tl", out_grad, value_h, preferred_element_type=jnp.float32)
    inner_sum = jnp.sum(attn_probs * prob_grad, axis=1, keepdims=True)
    score_grad = (attn_probs * (prob_grad - inner_sum) * scale_factor).astype(jnp.bfloat16)
    query_grad = jnp.dot(score_grad, key_h, preferred_element_type=jnp.float32)
    key_grad = jnp.einsum("tl,th->lh", score_grad, query_h, preferred_element_type=jnp.float32)
    value_grad = jnp.einsum(
        "tl,th->lh", attn_probs.astype(jnp.bfloat16), out_grad, preferred_element_type=jnp.float32
    )
    return (query_grad, key_grad, value_grad)


def local_general(
    hidden,
    cotangent,
    segments,
    padding,
    routes,
    order,
    norm1_gain,
    w_query,
    w_key,
    w_value,
    w_out,
    norm2_gain,
    router,
    shared_gate_vec,
    shared_w_gate,
    shared_w_up,
    shared_w_down,
    expert_w_gate,
    expert_w_up,
    expert_w_down,
):
    fetched = (
        lax.all_gather(norm1_gain, DP, axis=0, tiled=True),
        lax.all_gather(w_query, DP, axis=0, tiled=True),
        lax.all_gather(w_key, DP, axis=0, tiled=True),
        lax.all_gather(w_value, DP, axis=0, tiled=True),
        lax.all_gather(w_out, DP, axis=0, tiled=True),
        lax.all_gather(norm2_gain, DP, axis=0, tiled=True),
        lax.all_gather(router, DP, axis=0, tiled=True),
        lax.all_gather(shared_gate_vec, DP, axis=0, tiled=True),
        lax.all_gather(shared_w_gate, DP, axis=0, tiled=True),
        lax.all_gather(shared_w_up, DP, axis=0, tiled=True),
        lax.all_gather(shared_w_down, DP, axis=0, tiled=True),
        lax.all_gather(expert_w_gate, DP, axis=1, tiled=True),
        lax.all_gather(expert_w_up, DP, axis=1, tiled=True),
        lax.all_gather(expert_w_down, DP, axis=2, tiled=True),
    )
    (
        gain_one,
        query_w,
        key_w,
        value_w,
        out_w,
        gain_two,
        router_full,
        gate_vec,
        sh_gate,
        sh_up,
        sh_down,
        ex_gate,
        ex_up,
        ex_down,
    ) = fetched
    sh_gate, sh_up, sh_down = (
        lax.all_gather(sh_gate, EXP, axis=1, tiled=True),
        lax.all_gather(sh_up, EXP, axis=1, tiled=True),
        lax.all_gather(sh_down, EXP, axis=0, tiled=True),
    )
    tokens_here = hidden.shape[1]
    model_width = hidden.shape[2]
    x_rows = hidden[0].astype(jnp.float32)
    cot_rows = cotangent[0].astype(jnp.float32)
    inv_one = lax.rsqrt(jnp.mean(x_rows * x_rows, axis=1, keepdims=True) + EPS)
    g_one = gain_one.astype(jnp.float32)
    normed_one = (x_rows * inv_one * g_one).astype(jnp.bfloat16)
    queries = jnp.dot(normed_one, query_w, preferred_element_type=jnp.float32).astype(jnp.bfloat16)
    keys_own = jnp.dot(normed_one, key_w, preferred_element_type=jnp.float32).astype(jnp.bfloat16)
    values_own = jnp.dot(normed_one, value_w, preferred_element_type=jnp.float32).astype(
        jnp.bfloat16
    )
    own_codes = jnp.where(padding[0] > 0, segments[0] + 1, 0)
    code_parts = jnp.stack([own_codes // 64, own_codes % 64]).astype(jnp.bfloat16)
    keys_all, values_all, parts_all = (
        lax.all_gather(keys_own, CTX, axis=0, tiled=True),
        lax.all_gather(values_own, CTX, axis=0, tiled=True),
        lax.all_gather(code_parts, CTX, axis=1, tiled=True),
    )
    key_codes = parts_all[0].astype(jnp.int32) * 64 + parts_all[1].astype(jnp.int32)
    seq_total = keys_all.shape[0]
    query_pos = lax.axis_index(CTX) * tokens_here + jnp.arange(tokens_here, dtype=jnp.int32)
    key_pos = jnp.arange(seq_total, dtype=jnp.int32)
    same_doc = key_codes[None, :] == (segments[0] + 1)[:, None]
    allowed = (key_pos[None, :] <= query_pos[:, None]) & (
        same_doc | (key_pos[None, :] == query_pos[:, None])
    )
    scale_factor = HEAD_DIM ** (-0.5)

    def to_heads(rows_in):
        return rows_in.reshape(rows_in.shape[0], HEADS, HEAD_DIM).transpose(1, 0, 2)

    def from_heads(heads_in):
        return heads_in.transpose(1, 0, 2).reshape(heads_in.shape[1], model_width)

    head_q = to_heads(queries)
    head_k = to_heads(keys_all)
    head_v = to_heads(values_all)
    head_out, log_total = lax.map(
        partial(attend_head, allowed=allowed, scale_factor=scale_factor), (head_q, head_k, head_v)
    )
    attended = from_heads(head_out)
    residual = x_rows + jnp.dot(attended, out_w, preferred_element_type=jnp.float32)
    inv_two = lax.rsqrt(jnp.mean(residual * residual, axis=1, keepdims=True) + EPS)
    g_two = gain_two.astype(jnp.float32)
    normed_two = (residual * inv_two * g_two).astype(jnp.bfloat16)
    router_logits = jnp.dot(normed_two, router_full, preferred_element_type=jnp.float32)
    router_exp = jnp.exp(router_logits - jnp.max(router_logits, axis=1, keepdims=True))
    router_probs = router_exp / jnp.sum(router_exp, axis=1, keepdims=True)
    route_gates = jnp.take_along_axis(router_probs, routes[0], axis=1)
    shared_gate = jax.nn.sigmoid(jnp.dot(normed_two, gate_vec, preferred_element_type=jnp.float32))
    shared_scaled = (shared_gate[:, None] * cot_rows).astype(jnp.bfloat16)
    rows_group, grads_group = (normed_two, shared_scaled)
    gate_pre = jnp.dot(rows_group, sh_gate, preferred_element_type=jnp.float32)
    up_pre = jnp.dot(rows_group, sh_up, preferred_element_type=jnp.float32)
    gate_act = gate_pre * jax.nn.sigmoid(gate_pre)
    shared_hidden = (gate_act * up_pre).astype(jnp.bfloat16)
    shared_part = jnp.dot(shared_hidden, sh_down, preferred_element_type=jnp.float32)
    experts_all = router_full.shape[1]
    capacity = (9 * tokens_here * TOP + 8 * experts_all - 1) // (8 * experts_all)
    priority = (order[0, 0][:, None] * TOP + jnp.arange(TOP, dtype=jnp.int32)[None, :]).reshape(-1)
    flat_routes = routes[0].reshape(-1)
    slot_index = block_slots(flat_routes, priority, experts_all)
    kept_rows = slot_index < capacity
    target = flat_routes * capacity + jnp.minimum(slot_index, capacity - 1)
    row_gates = route_gates.reshape(-1)
    cot_repeated = jnp.repeat(cot_rows, TOP, axis=0)
    source_rows = jnp.repeat(normed_two, TOP, axis=0)
    source_grads = (cot_repeated * row_gates[:, None]).astype(jnp.bfloat16)
    empty_slots = jnp.zeros((experts_all * capacity, model_width), jnp.bfloat16)
    send_rows = empty_slots.at[target].add(
        jnp.where(kept_rows[:, None], source_rows, jnp.zeros_like(source_rows))
    )
    send_grads = empty_slots.at[target].add(
        jnp.where(kept_rows[:, None], source_grads, jnp.zeros_like(source_grads))
    )
    recv_rows, recv_grads = (
        lax.all_to_all(
            send_rows.reshape(experts_all, capacity, model_width),
            (EXP, CTX),
            split_axis=0,
            concat_axis=0,
            tiled=True,
        ),
        lax.all_to_all(
            send_grads.reshape(experts_all, capacity, model_width),
            (EXP, CTX),
            split_axis=0,
            concat_axis=0,
            tiled=True,
        ),
    )
    local_count = ex_gate.shape[0]
    sources = experts_all // local_count

    def to_local(buffer_in):
        return (
            buffer_in.reshape(sources, local_count, capacity, model_width)
            .transpose(1, 0, 2, 3)
            .reshape(local_count, sources * capacity, model_width)
        )

    def to_owner(buffer_in):
        return (
            buffer_in.reshape(local_count, sources, capacity, model_width)
            .transpose(1, 0, 2, 3)
            .reshape(experts_all, capacity, model_width)
        )

    expert_rows = to_local(recv_rows)
    expert_grads_in = to_local(recv_grads)
    gate_e = jnp.einsum("erd,edf->erf", expert_rows, ex_gate, preferred_element_type=jnp.float32)
    up_e = jnp.einsum("erd,edf->erf", expert_rows, ex_up, preferred_element_type=jnp.float32)
    act_e = gate_e * jax.nn.sigmoid(gate_e)
    hidden_e = (act_e * up_e).astype(jnp.bfloat16)
    result_e = jnp.einsum(
        "erf,efd->erd", hidden_e, ex_down, preferred_element_type=jnp.float32
    ).astype(jnp.bfloat16)
    returned = lax.all_to_all(
        to_owner(result_e), (EXP, CTX), split_axis=0, concat_axis=0, tiled=True
    )
    picked = returned.reshape(experts_all * capacity, model_width)[target]
    picked = jnp.where(kept_rows[:, None], picked, jnp.zeros_like(picked)).astype(jnp.float32)
    routed = jnp.sum((picked * row_gates[:, None]).reshape(tokens_here, TOP, model_width), axis=1)
    output = (residual + shared_gate[:, None] * shared_part + routed).astype(jnp.bfloat16)
    gate_grads = jnp.sum(picked * cot_repeated, axis=1).reshape(tokens_here, TOP)
    hidden_grad_e = jnp.einsum(
        "erd,efd->erf", expert_grads_in, ex_down, preferred_element_type=jnp.float32
    )
    gate_grad_e = (hidden_grad_e * up_e * silu_grad(gate_e)).astype(jnp.bfloat16)
    up_grad_e = (hidden_grad_e * act_e).astype(jnp.bfloat16)
    grad_ex_down = jnp.einsum(
        "erf,erd->efd", hidden_e, expert_grads_in, preferred_element_type=jnp.float32
    )
    grad_ex_gate = jnp.einsum(
        "erd,erf->edf", expert_rows, gate_grad_e, preferred_element_type=jnp.float32
    )
    grad_ex_up = jnp.einsum(
        "erd,erf->edf", expert_rows, up_grad_e, preferred_element_type=jnp.float32
    )
    expert_sums = (
        lax.psum_scatter(grad_ex_gate, DP, scatter_dimension=1, tiled=True),
        lax.psum_scatter(grad_ex_up, DP, scatter_dimension=1, tiled=True),
        lax.psum_scatter(grad_ex_down, DP, scatter_dimension=2, tiled=True),
    )
    rows_grad_e = jnp.einsum(
        "erf,edf->erd", gate_grad_e, ex_gate, preferred_element_type=jnp.float32
    )
    rows_grad_e = (
        rows_grad_e
        + jnp.einsum("erf,edf->erd", up_grad_e, ex_up, preferred_element_type=jnp.float32)
    ).astype(jnp.bfloat16)
    returned_grads = lax.all_to_all(
        to_owner(rows_grad_e), (EXP, CTX), split_axis=0, concat_axis=0, tiled=True
    )
    routed_grad = returned_grads.reshape(experts_all * capacity, model_width)[target]
    routed_grad = jnp.where(kept_rows[:, None], routed_grad, jnp.zeros_like(routed_grad)).astype(
        jnp.float32
    )
    norm_grad = jnp.sum(routed_grad.reshape(tokens_here, TOP, model_width), axis=1)
    choose = (
        routes[0][:, :, None] == jnp.arange(experts_all, dtype=jnp.int32)[None, None, :]
    ).astype(jnp.float32)
    probs_grad = jnp.einsum("tk,tke->te", gate_grads, choose)
    logit_grad = (
        router_probs * (probs_grad - jnp.sum(router_probs * probs_grad, axis=1, keepdims=True))
    ).astype(jnp.bfloat16)
    grad_router = jnp.dot(normed_two.T, logit_grad, preferred_element_type=jnp.float32)
    gate_logit_grad = (
        jnp.sum(cot_rows * shared_part, axis=1) * shared_gate * (1.0 - shared_gate)
    ).astype(jnp.bfloat16)
    grad_gate_vec = jnp.dot(gate_logit_grad, normed_two, preferred_element_type=jnp.float32)
    norm_grad = norm_grad + jnp.dot(logit_grad, router_full.T, preferred_element_type=jnp.float32)
    norm_grad = (
        norm_grad
        + gate_logit_grad.astype(jnp.float32)[:, None] * gate_vec.astype(jnp.float32)[None, :]
    )
    shared_hgrad = jnp.dot(grads_group, sh_down.T, preferred_element_type=jnp.float32)
    gate_grad_s = (shared_hgrad * up_pre * silu_grad(gate_pre)).astype(jnp.bfloat16)
    up_grad_s = (shared_hgrad * gate_act).astype(jnp.bfloat16)
    shared_rows_grad = jnp.dot(gate_grad_s, sh_gate.T, preferred_element_type=jnp.float32)
    shared_rows_grad = shared_rows_grad + jnp.dot(
        up_grad_s, sh_up.T, preferred_element_type=jnp.float32
    )
    groups = lax.axis_size(EXP)
    parts_cd = lax.axis_size((CTX, DP))
    rows_count = rows_group.shape[0]
    arr_gate = jnp.einsum(
        "td,tes->eds",
        rows_group,
        gate_grad_s.reshape(rows_count, groups, -1),
        preferred_element_type=jnp.float32,
    ).reshape(groups * model_width, -1)
    arr_up = jnp.einsum(
        "td,tes->eds",
        rows_group,
        up_grad_s.reshape(rows_count, groups, -1),
        preferred_element_type=jnp.float32,
    ).reshape(groups * model_width, -1)
    arr_down = jnp.einsum(
        "tes,tcd->ecsd",
        shared_hidden.reshape(rows_count, groups, -1),
        grads_group.reshape(rows_count, parts_cd, -1),
        preferred_element_type=jnp.float32,
    ).reshape(-1, model_width // parts_cd)
    sums_gate, sums_up, sums_down = (
        lax.psum_scatter(arr_gate, (EXP, CTX, DP), scatter_dimension=0, tiled=True),
        lax.psum_scatter(arr_up, (EXP, CTX, DP), scatter_dimension=0, tiled=True),
        lax.psum_scatter(arr_down, (EXP, CTX, DP), scatter_dimension=0, tiled=True),
    )
    norm_grad = norm_grad + shared_rows_grad
    residual_grad, grad_gain_two = norm_back(residual, inv_two, g_two, norm_grad)
    residual_grad = residual_grad + cot_rows
    low_residual = residual_grad.astype(jnp.bfloat16)
    grad_out_w = jnp.dot(attended.T, low_residual, preferred_element_type=jnp.float32)
    attended_grad = jnp.dot(low_residual, out_w.T, preferred_element_type=jnp.float32).astype(
        jnp.bfloat16
    )
    head_q_grad, head_k_grad, head_v_grad = lax.map(
        partial(attend_back, allowed=allowed, scale_factor=scale_factor),
        (head_q, head_k, head_v, to_heads(attended_grad), log_total),
    )
    key_sum, value_sum = (
        lax.psum_scatter(from_heads(head_k_grad), CTX, scatter_dimension=0, tiled=True),
        lax.psum_scatter(from_heads(head_v_grad), CTX, scatter_dimension=0, tiled=True),
    )
    query_low = from_heads(head_q_grad).astype(jnp.bfloat16)
    key_low = key_sum.astype(jnp.bfloat16)
    value_low = value_sum.astype(jnp.bfloat16)
    grad_query = jnp.dot(normed_one.T, query_low, preferred_element_type=jnp.float32)
    grad_key = jnp.dot(normed_one.T, key_low, preferred_element_type=jnp.float32)
    grad_value = jnp.dot(normed_one.T, value_low, preferred_element_type=jnp.float32)
    normed_grad = jnp.dot(query_low, query_w.T, preferred_element_type=jnp.float32)
    normed_grad = normed_grad + jnp.dot(key_low, key_w.T, preferred_element_type=jnp.float32)
    normed_grad = normed_grad + jnp.dot(value_low, value_w.T, preferred_element_type=jnp.float32)
    input_part, grad_gain_one = norm_back(x_rows, inv_one, g_one, normed_grad)
    input_grad = (residual_grad + input_part).astype(jnp.bfloat16)
    dense = (
        lax.psum_scatter(
            grad_gain_one, (EXP, CTX, DP), scatter_dimension=0, tiled=True
        ),
        lax.psum_scatter(grad_query, (EXP, CTX, DP), scatter_dimension=0, tiled=True),
        lax.psum_scatter(grad_key, (EXP, CTX, DP), scatter_dimension=0, tiled=True),
        lax.psum_scatter(grad_value, (EXP, CTX, DP), scatter_dimension=0, tiled=True),
        lax.psum_scatter(grad_out_w, (EXP, CTX, DP), scatter_dimension=0, tiled=True),
        lax.psum_scatter(
            grad_gain_two, (EXP, CTX, DP), scatter_dimension=0, tiled=True
        ),
        lax.psum_scatter(
            grad_router, (EXP, CTX, DP), scatter_dimension=0, tiled=True
        ),
        lax.psum_scatter(
            grad_gate_vec, (EXP, CTX, DP), scatter_dimension=0, tiled=True
        ),
    )
    return (
        output[None],
        input_grad[None],
        dense[0],
        dense[1],
        dense[2],
        dense[3],
        dense[4],
        dense[5],
        dense[6],
        dense[7],
        sums_gate,
        sums_up,
        sums_down,
        expert_sums[0],
        expert_sums[1],
        expert_sums[2],
    )

def attention_probs(q_blk, k_part, q_code, k_code, first_row, scale_factor):
    scores = lax.dot_general(
        q_blk, k_part, (((1,), (1,)), ((), ())), preferred_element_type=jnp.float32
    )
    row = first_row + lax.broadcasted_iota(jnp.int32, scores.shape, 0)
    col = lax.broadcasted_iota(jnp.int32, scores.shape, 1)
    allowed = ((col < row) & (k_code == q_code)) | (col == row)
    logits = jnp.where(allowed, scores * scale_factor, NEG)
    exp_scores = jnp.exp(logits - jnp.max(logits, axis=1, keepdims=True))
    return exp_scores * (1.0 / jnp.sum(exp_scores, axis=1, keepdims=True))


def attend_kernel(heads, step, qkv_ref, q_code_ref, k_code_ref, out_ref):
    seq_len = qkv_ref.shape[0]
    width = heads * HEAD_DIM
    for head in range(heads):
        at = head * HEAD_DIM
        for first in range(0, seq_len, step):
            upto = first + step
            probs = attention_probs(
                qkv_ref[first:upto, at : at + HEAD_DIM],
                qkv_ref[0:upto, width + at : width + at + HEAD_DIM],
                q_code_ref[first:upto, :],
                k_code_ref[0, :, 0:upto],
                first,
                HEAD_DIM**-0.5,
            )
            out_ref[first:upto, at : at + HEAD_DIM] = jnp.dot(
                probs.astype(jnp.bfloat16),
                qkv_ref[0:upto, 2 * width + at : 2 * width + at + HEAD_DIM],
                preferred_element_type=jnp.float32,
            ).astype(jnp.bfloat16)


def attend_back_kernel(
    heads, step, qkv_ref, grad_ref, q_code_ref, k_code_ref, out_ref, key_acc, value_acc
):
    seq_len = qkv_ref.shape[0]
    width = heads * HEAD_DIM
    for head in range(heads):
        at = head * HEAD_DIM
        key_at, value_at = width + at, 2 * width + at
        key_acc[...] = jnp.zeros_like(key_acc)
        value_acc[...] = jnp.zeros_like(value_acc)
        for first in range(0, seq_len, step):
            upto = first + step
            q_blk = qkv_ref[first:upto, at : at + HEAD_DIM]
            k_part = qkv_ref[0:upto, key_at : key_at + HEAD_DIM]
            v_part = qkv_ref[0:upto, value_at : value_at + HEAD_DIM]
            g_blk = grad_ref[first:upto, at : at + HEAD_DIM]
            probs = attention_probs(
                q_blk,
                k_part,
                q_code_ref[first:upto, :],
                k_code_ref[0, :, 0:upto],
                first,
                HEAD_DIM**-0.5,
            )
            prob_grad = lax.dot_general(
                g_blk, v_part, (((1,), (1,)), ((), ())), preferred_element_type=jnp.float32
            )
            inner = jnp.sum(probs * prob_grad, axis=1, keepdims=True)
            score_grad = (probs * (prob_grad - inner) * HEAD_DIM**-0.5).astype(jnp.bfloat16)
            out_ref[first:upto, at : at + HEAD_DIM] = jnp.dot(
                score_grad, k_part, preferred_element_type=jnp.float32
            ).astype(jnp.bfloat16)
            key_acc[0:upto, :] += lax.dot_general(
                score_grad, q_blk, (((0,), (0,)), ((), ())), preferred_element_type=jnp.float32
            )
            value_acc[0:upto, :] += lax.dot_general(
                probs.astype(jnp.bfloat16),
                g_blk,
                (((0,), (0,)), ((), ())),
                preferred_element_type=jnp.float32,
            )
        out_ref[:, key_at : key_at + HEAD_DIM] = key_acc[...].astype(jnp.bfloat16)
        out_ref[:, value_at : value_at + HEAD_DIM] = value_acc[...].astype(jnp.bfloat16)


def attention_call(qkv, grads, q_codes, k_codes, seq_len):
    rows, triple = qkv.shape
    width = triple // 3
    heads = width // HEAD_DIM
    step = min(256, seq_len)
    specs = [pl.BlockSpec((seq_len, triple), lambda s: (s, 0))]
    operands = [qkv]
    if grads is not None:
        specs.append(pl.BlockSpec((seq_len, width), lambda s: (s, 0)))
        operands.append(grads)
    specs += [
        pl.BlockSpec((seq_len, 1), lambda s: (s, 0)),
        pl.BlockSpec((1, 1, seq_len), lambda s: (s, 0, 0)),
    ]
    operands += [q_codes, k_codes]
    out_width = width if grads is None else triple
    body = attend_kernel if grads is None else attend_back_kernel
    passes = 2 if grads is None else 5
    area = rows * seq_len * heads
    return pl.pallas_call(
        partial(body, heads, step),
        grid=(rows // seq_len,),
        in_specs=specs,
        out_specs=pl.BlockSpec((seq_len, out_width), lambda s: (s, 0)),
        out_shape=jax.ShapeDtypeStruct((rows, out_width), jnp.bfloat16),
        scratch_shapes=[]
        if grads is None
        else [pltpu.VMEM((seq_len, HEAD_DIM), jnp.float32)] * 2,
        compiler_params=pltpu.CompilerParams(vmem_limit_bytes=48 * 2**20),
        cost_estimate=pl.CostEstimate(
            flops=2 * passes * area * HEAD_DIM,
            bytes_accessed=2 * rows * (triple + out_width),
            transcendentals=area,
        ),
    )(*operands)


MESH_ID = pl.DeviceIdType.MESH


def other_in_pair(index, bit):
    return index + bit - 2 * bit * (lax.div(index, bit) % 2)


def plane_places():
    at = lax.axis_index(EXP)
    core = lax.axis_index(CTX)
    across, along = other_in_pair(at, 1), other_in_pair(at, 2)
    return at, core, across, along, other_in_pair(along, 1)


def greet(across, along, core):
    barrier = pltpu.get_barrier_semaphore()
    for target in ({EXP: across}, {EXP: along}, {CTX: 1 - core}):
        pl.semaphore_signal(barrier, inc=1, device_id=target, device_id_type=MESH_ID)
    pl.semaphore_wait(barrier, 3)


def plane_gather_kernel(with_info, relative, *refs):
    if with_info:
        own_ref, info_ref, all_ref, info_all_ref, send_sem, recv_sem, local_sem = refs
    else:
        own_ref, all_ref, send_sem, recv_sem, local_sem = refs
    at, core, across, along, far = plane_places()
    rows = own_ref.shape[0]
    half = rows // 2
    top, bottom, whole = pl.ds(0, half), pl.ds(half, half), pl.ds(0, rows)
    greet(across, along, core)
    started = []
    twin_id = {CTX: 1 - core}

    def slot_of(place, shift, for_twin):
        if relative:
            return shift + 4 * for_twin
        return place * 2 + core

    def send(number, src, dst, target):
        copy = pltpu.make_async_remote_copy(
            src_ref=src,
            dst_ref=dst,
            send_sem=send_sem.at[number],
            recv_sem=recv_sem.at[number],
            device_id=target,
            device_id_type=MESH_ID,
        )
        copy.start()
        started.append(copy)
        return copy

    def piece(place, shift, part, for_twin=0):
        return all_ref.at[slot_of(place, shift, for_twin), part]

    x_top = send(0, own_ref.at[top], piece(at, 1, top), {EXP: across})
    y_bottom = send(1, own_ref.at[bottom], piece(at, 2, bottom), {EXP: along})
    x_bottom = send(2, own_ref.at[bottom], piece(at, 1, bottom), {EXP: across})
    y_top = send(3, own_ref.at[top], piece(at, 2, top), {EXP: along})
    twins = [send(4, own_ref, piece(at, 0, whole, 1), twin_id)]
    heres = [pltpu.make_async_copy(own_ref, piece(at, 0, whole), local_sem.at[0])]
    heres[0].start()
    if with_info:
        info_at = lambda place: info_all_ref.at[place * 2 + core]
        heres.append(pltpu.make_async_copy(info_ref, info_at(at), local_sem.at[1]))
        heres[1].start()
        info_x = send(13, info_ref, info_at(at), {EXP: across})
        info_y = send(14, info_ref, info_at(at), {EXP: along})
        twins.append(send(15, info_ref, info_at(at), twin_id))
        info_x.wait_recv()
        info_far = send(16, info_at(across), info_at(across), {EXP: along})
        twins.append(send(17, info_at(across), info_at(across), twin_id))
        info_y.wait_recv()
        twins.append(send(18, info_at(along), info_at(along), twin_id))
        info_far.wait_recv()
        twins.append(send(19, info_at(far), info_at(far), twin_id))

    def hand_on(number, place, shift, part):
        src = piece(place, shift, part)
        twins.append(send(number, src, piece(place, shift, part, 1), twin_id))

    x_top.wait_recv()
    far_top = send(5, piece(across, 1, top), piece(across, 3, top), {EXP: along})
    hand_on(6, across, 1, top)
    y_bottom.wait_recv()
    far_bottom = send(7, piece(along, 2, bottom), piece(along, 3, bottom), {EXP: across})
    hand_on(8, along, 2, bottom)
    x_bottom.wait_recv()
    hand_on(9, across, 1, bottom)
    y_top.wait_recv()
    hand_on(10, along, 2, top)
    far_top.wait_recv()
    hand_on(11, far, 3, top)
    far_bottom.wait_recv()
    hand_on(12, far, 3, bottom)
    for copy in twins:
        copy.wait_recv()
    for copy in started:
        copy.wait_send()
    for copy in heres:
        copy.wait()


def plane_gather(own, info, relative, number):
    plane = lax.axis_size(PLANE)
    operands = [own] if info is None else [own, info]
    outs = [jax.ShapeDtypeStruct((plane, *v.shape), v.dtype) for v in operands]
    anywhere = pl.BlockSpec(memory_space=pl.ANY)
    return pl.pallas_call(
        partial(plane_gather_kernel, info is not None, relative),
        out_shape=outs,
        in_specs=[anywhere] * len(operands),
        out_specs=[anywhere] * len(operands),
        scratch_shapes=[
            pltpu.SemaphoreType.DMA((20,)),
            pltpu.SemaphoreType.DMA((20,)),
            pltpu.SemaphoreType.DMA((2,)),
        ],
        compiler_params=pltpu.CompilerParams(collective_id=number, has_side_effects=True),
        cost_estimate=pl.CostEstimate(
            flops=0, bytes_accessed=own.size, transcendentals=0
        ),
    )(*operands)


def norm_qkv_kernel(hidden_ref, gain_ref, w_ref, norm_ref, qkv_ref):
    values = hidden_ref[...].astype(jnp.float32)
    inv = lax.rsqrt(jnp.mean(values * values, axis=1, keepdims=True) + EPS)
    norm_ref[...] = low(values * inv * gain_ref[...])
    qkv_ref[...] = low(mm(norm_ref[...], w_ref[...]))


def norm_qkv(hidden, gain, w, block):
    rows, width = hidden.shape
    cols = w.shape[1]
    return pl.pallas_call(
        norm_qkv_kernel,
        grid=(rows // block,),
        in_specs=[
            pl.BlockSpec((block, width), lambda i: (i, 0)),
            pl.BlockSpec((1, width), lambda i: (0, 0)),
            pl.BlockSpec((width, cols), lambda i: (0, 0)),
        ],
        out_specs=[
            pl.BlockSpec((block, width), lambda i: (i, 0)),
            pl.BlockSpec((block, cols), lambda i: (i, 0)),
        ],
        out_shape=[
            jax.ShapeDtypeStruct((rows, width), jnp.bfloat16),
            jax.ShapeDtypeStruct((rows, cols), jnp.bfloat16),
        ],
        compiler_params=pltpu.CompilerParams(vmem_limit_bytes=48 * 2**20),
        cost_estimate=pl.CostEstimate(
            flops=2 * rows * width * cols,
            bytes_accessed=4 * rows * width,
            transcendentals=0,
        ),
    )(hidden, gain, w)


def chosen_rows(slots, capacity):
    lanes = lax.broadcasted_iota(jnp.int32, (slots.shape[0], capacity), 1)
    return (slots == lanes).astype(jnp.bfloat16)


def hand_out(step_at, half, blocks, pieces, sems):
    copies = [
        pltpu.make_async_copy(blocks.at[k, part], goal, sems.at[number])
        for number, (k, part, goal) in enumerate(pieces)
    ]
    for k in range(half):

        @pl.when(step_at == half + k)
        def _():
            for copy, piece in zip(copies, pieces):
                if piece[0] == k:
                    copy.start()

    @pl.when(step_at == 2 * half - 1)
    def _():
        for copy in copies:
            copy.wait()


def output_kernel(
    half,
    hidden_ref,
    down_ref,
    rows_ref,
    slot_ref,
    sg_ref,
    gate_ref,
    cot_ref,
    *refs,
):
    near_refs, dots_ref, refs = refs[:half], refs[half], refs[half + 1 :]
    given, got, send_sem, recv_sem, out_sem = refs
    step_at = pl.program_id(0)
    is_far = step_at < half
    slot = lax.rem(step_at, half)
    twin_id = {CTX: 1 - lax.axis_index(CTX)}

    @pl.when(step_at == 0)
    def _():
        barrier = pltpu.get_barrier_semaphore()
        pl.semaphore_signal(barrier, inc=1, device_id=twin_id, device_id_type=MESH_ID)
        pl.semaphore_wait(barrier, 1)

    def block_copy(k):
        return pltpu.make_async_remote_copy(
            src_ref=given.at[k],
            dst_ref=got.at[k],
            send_sem=send_sem.at[k],
            recv_sem=recv_sem.at[k],
            device_id=twin_id,
            device_id_type=MESH_ID,
        )

    def make(store):
        chosen = chosen_rows(slot_ref[...], rows_ref.shape[1])
        hidden = hidden_ref[...].T
        tokens, width = cot_ref.shape
        step, lanes = 512, 128
        gate_dot = jnp.zeros((tokens, lanes), jnp.float32)
        shared_dot = jnp.zeros((tokens, lanes), jnp.float32)
        for first in range(0, width, step):
            cols = pl.ds(first, step)
            shared = mm(hidden, down_ref[:, cols])
            picked = mm(chosen, rows_ref[0, :, cols])
            cot = cot_ref[:, cols].astype(jnp.float32)
            gate_part, shared_part = picked * cot, shared * cot
            for at in range(0, step, lanes):
                gate_dot += gate_part[:, at : at + lanes]
                shared_dot += shared_part[:, at : at + lanes]
            store(cols, sg_ref[...] * shared + gate_ref[...] * picked)
        lane = lax.broadcasted_iota(jnp.int32, dots_ref.shape, 1)
        gate_dot = jnp.sum(gate_dot, axis=1, keepdims=True)
        shared_dot = jnp.sum(shared_dot, axis=1, keepdims=True)
        dots_ref[...] = jnp.where(lane == 0, gate_dot, jnp.where(lane == 1, shared_dot, 0.0))

    @pl.when(is_far)
    def _():
        def store(cols, total):
            given[slot, :, cols] = low(total)

        make(store)
        block_copy(slot).start()

    @pl.when(jnp.logical_not(is_far))
    def _():
        block_copy(slot).wait_recv()

        def store(cols, total):
            got[slot, :, cols] = low(total + got[slot, :, cols].astype(jnp.float32))

        make(store)

    everything = pl.ds(0, got.shape[1])
    pieces = [(k, everything, near_refs[k]) for k in range(half)]
    hand_out(step_at, half, got, pieces, out_sem)

    @pl.when(step_at == 2 * half - 1)
    def _():
        for k in range(half):
            block_copy(k).wait_send()


def output_parts(hidden, down, rows, slots, sg, gates, cot):
    blocks, capacity, width = rows.shape
    units, count = hidden.shape
    tokens, half = count // blocks, blocks // 2
    at = lambda i: lax.rem(i + half, blocks)
    column = pl.BlockSpec((tokens, 1), lambda i: (at(i), 0))
    return pl.pallas_call(
        partial(output_kernel, half),
        grid=(blocks,),
        in_specs=[
            pl.BlockSpec((units, tokens), lambda i: (0, at(i))),
            pl.BlockSpec((units, width), lambda i: (0, 0)),
            pl.BlockSpec((1, capacity, width), lambda i: (at(i), 0, 0)),
            column,
            column,
            column,
            pl.BlockSpec((tokens, width), lambda i: (at(i), 0)),
        ],
        out_specs=[
            *[pl.BlockSpec(memory_space=pl.ANY)] * half,
            pl.BlockSpec((tokens, 128), lambda i: (at(i), 0)),
        ],
        out_shape=[
            *[jax.ShapeDtypeStruct((tokens, width), jnp.bfloat16)] * half,
            jax.ShapeDtypeStruct((count, 128), jnp.float32),
        ],
        scratch_shapes=[
            pltpu.VMEM((half, tokens, width), jnp.bfloat16),
            pltpu.VMEM((half, tokens, width), jnp.bfloat16),
            pltpu.SemaphoreType.DMA((half,)),
            pltpu.SemaphoreType.DMA((half,)),
            pltpu.SemaphoreType.DMA((half,)),
        ],
        compiler_params=pltpu.CompilerParams(
            collective_id=4, has_side_effects=True, vmem_limit_bytes=56 * 2**20
        ),
        cost_estimate=pl.CostEstimate(
            flops=2 * count * width * (units + capacity),
            bytes_accessed=6 * count * width,
            transcendentals=0,
        ),
    )(hidden, down, rows, slots, sg, gates, cot)


def scatter_step(compute, out_ref, scratch):
    given, total, x_got, y_got, x_last, y_last, send_sem, recv_sem = scratch
    at, core, across, along, far = plane_places()
    step_at = pl.program_id(0)
    row = step_at // 2
    is_twin = step_at % 2 == 0
    rows = total.shape[1]
    half = rows // 2
    top, bottom = pl.ds(0, half), pl.ds(half, half)

    def copy_of(number, src, dst, target):
        return pltpu.make_async_remote_copy(
            src_ref=src,
            dst_ref=dst,
            send_sem=send_sem.at[number],
            recv_sem=recv_sem.at[number],
            device_id=target,
            device_id_type=MESH_ID,
        )

    def twin_copy(k):
        return copy_of(k, given.at[k % 2], total.at[k], {CTX: 1 - core})

    far_x = copy_of(4, total.at[0, top], x_got.at[0], {EXP: across})
    far_y = copy_of(5, total.at[0, bottom], y_got.at[0], {EXP: along})
    own_x = copy_of(6, total.at[1, top], x_got.at[1], {EXP: across})
    own_y = copy_of(7, total.at[2, bottom], y_got.at[1], {EXP: along})
    last_y = copy_of(8, total.at[2, top], y_last, {EXP: along})
    last_x = copy_of(9, total.at[1, bottom], x_last, {EXP: across})

    @pl.when(step_at == 0)
    def _():
        greet(across, along, core)

    @pl.when(is_twin)
    def _():
        @pl.when(row >= 2)
        def _():
            twin_copy(row - 2).wait_send()

        def store(cols, values):
            given[row % 2, :, cols] = low(values)

        compute(store)
        twin_copy(row).start()

    @pl.when(jnp.logical_not(is_twin))
    def _():
        twin_copy(row).wait_recv()

        def store(cols, values):
            total[row, :, cols] = low(values + total[row, :, cols].astype(jnp.float32))

        compute(store)

    @pl.when(step_at == 1)
    def _():
        far_x.start()
        far_y.start()

    @pl.when(step_at == 3)
    def _():
        own_x.start()

    @pl.when(step_at == 5)
    def _():
        own_y.start()

    @pl.when(step_at == 7)
    def _():
        def add_half(k, first, got):
            @pl.loop(0, half // 64)
            def _(i):
                take = pl.ds(pl.multiple_of(i * 64, 64), 64)
                into = pl.ds(pl.multiple_of(first + i * 64, 64), 64)
                total[k, into] = low(
                    total[k, into].astype(jnp.float32) + got[0, take].astype(jnp.float32)
                )

        def finish(first, near, later):
            @pl.loop(0, half // 64)
            def _(i):
                take = pl.ds(pl.multiple_of(i * 64, 64), 64)
                into = pl.ds(pl.multiple_of(first + i * 64, 64), 64)
                out_ref[into] = (
                    total[3, into].astype(jnp.float32)
                    + near[1, take].astype(jnp.float32)
                    + later[take].astype(jnp.float32)
                )

        far_x.wait_recv()
        add_half(2, 0, x_got)
        last_y.start()
        far_y.wait_recv()
        add_half(1, half, y_got)
        last_x.start()
        own_x.wait_recv()
        last_y.wait_recv()
        finish(0, x_got, y_last)
        own_y.wait_recv()
        last_x.wait_recv()
        finish(half, y_got, x_last)
        for copy in (twin_copy(2), twin_copy(3), far_x, far_y, own_x, own_y, last_y, last_x):
            copy.wait_send()


def step_slot(i):
    row = i // 2
    shift = jnp.where(row == 0, 3, jnp.where(row == 3, 0, row))
    return shift + 4 * (1 - i % 2)


def scatter_scratch(tokens, width):
    vmem = lambda *shape: pltpu.VMEM(shape, jnp.bfloat16)
    return [
        vmem(2, tokens, width),
        vmem(4, tokens, width),
        vmem(2, tokens // 2, width),
        vmem(2, tokens // 2, width),
        vmem(tokens // 2, width),
        vmem(tokens // 2, width),
        pltpu.SemaphoreType.DMA((10,)),
        pltpu.SemaphoreType.DMA((10,)),
    ]


def n2_grad_kernel(dgate_ref, dup_ref, gate_ref, up_ref, rows_ref, slot_ref, out_ref, *scratch):
    def compute(store):
        chosen = chosen_rows(slot_ref[...], rows_ref.shape[1])
        dgate, dup = dgate_ref[...].T, dup_ref[...].T
        step = 512
        for first in range(0, gate_ref.shape[1], step):
            cols = pl.ds(first, step)
            total = mm(dgate, gate_ref[:, cols]) + mm(dup, up_ref[:, cols])
            store(cols, total + mm(chosen, rows_ref[0, :, cols]))

    scatter_step(compute, out_ref, scratch)


def n2_grad_sum(dgate, dup, gate_w, up_w, rows, slots):
    blocks, capacity, width = rows.shape
    units, count = dgate.shape
    tokens = count // blocks
    by_units = pl.BlockSpec((units, tokens), lambda i: (0, step_slot(i)))
    whole = pl.BlockSpec((units, width), lambda i: (0, 0), pipeline_mode=pl.Buffered(1))
    return pl.pallas_call(
        n2_grad_kernel,
        grid=(blocks,),
        in_specs=[
            by_units,
            by_units,
            whole,
            whole,
            pl.BlockSpec((1, capacity, width), lambda i: (step_slot(i), 0, 0)),
            pl.BlockSpec((tokens, 1), lambda i: (step_slot(i), 0)),
        ],
        out_specs=pl.BlockSpec((tokens, width), lambda i: (0, 0)),
        out_shape=jax.ShapeDtypeStruct((tokens, width), jnp.float32),
        scratch_shapes=scatter_scratch(tokens, width),
        compiler_params=pltpu.CompilerParams(
            collective_id=3, has_side_effects=True, vmem_limit_bytes=56 * 2**20
        ),
        cost_estimate=pl.CostEstimate(
            flops=2 * count * width * (2 * units + capacity),
            bytes_accessed=4 * count * width,
            transcendentals=0,
        ),
    )(dgate, dup, gate_w, up_w, rows, slots)


def unit_grad_kernel(hid_ref, dgate_ref, dup_ref, cot_ref, n2_ref, out_ref):
    units = hid_ref.shape[0]
    out_ref[0, :units] = low(mm(hid_ref[...], cot_ref[...]))
    out_ref[0, units : 2 * units] = low(mm(dgate_ref[...], n2_ref[...]))
    out_ref[0, 2 * units :] = low(mm(dup_ref[...], n2_ref[...]))


def unit_grads(hidden, dgate, dup, cots, n2, depth, halves):
    units, count = hidden.shape
    width = n2.shape[1]
    cols = width // (depth * halves)
    whole = pl.BlockSpec((units, count), lambda i: (0, 0), pipeline_mode=pl.Buffered(1))
    strip = pl.BlockSpec((count, cols), lambda i: (0, i))
    return pl.pallas_call(
        unit_grad_kernel,
        grid=(depth * halves,),
        in_specs=[whole, whole, whole, strip, strip],
        out_specs=pl.BlockSpec(
            (1, 3 * units, cols), lambda i: (lax.rem(i, depth), 0, i // depth)
        ),
        out_shape=jax.ShapeDtypeStruct((depth, 3 * units, halves * cols), jnp.bfloat16),
        compiler_params=pltpu.CompilerParams(vmem_limit_bytes=48 * 2**20),
        cost_estimate=pl.CostEstimate(
            flops=6 * units * count * width,
            bytes_accessed=2 * (3 * units * count + 2 * count * width + 3 * units * width),
            transcendentals=0,
        ),
    )(hidden, dgate, dup, cots, n2)


def n1_grad_kernel(half, grads_ref, w_ref, *refs):
    near_refs, refs = refs[:half], refs[half:]
    rows_in, given, got, load_sem, send_sem, recv_sem, out_sem = refs
    place, core = lax.axis_index(EXP), lax.axis_index(CTX)
    step_at = pl.program_id(0)
    is_far = step_at < half
    slot = lax.rem(step_at, half)
    tokens = rows_in.shape[1]
    twin_id = {CTX: 1 - core}

    def load(step, k):
        column, level = place % 2, place // 2
        there = (column + k % 2) % 2 + 2 * ((level + k // 2) % 2)
        owner = 1 - core if step < half else core
        first = pl.multiple_of((there * 2 + owner) * tokens, tokens)
        return pltpu.make_async_copy(
            grads_ref.at[pl.ds(first, tokens)], rows_in.at[step], load_sem.at[step]
        )

    loads = [load(step, step % half) for step in range(2 * half)]

    @pl.when(step_at == 0)
    def _():
        for copy in loads:
            copy.start()
        barrier = pltpu.get_barrier_semaphore()
        pl.semaphore_signal(barrier, inc=1, device_id=twin_id, device_id_type=MESH_ID)
        pl.semaphore_wait(barrier, 1)

    for step in range(2 * half):

        @pl.when(step_at == step)
        def _():
            loads[step].wait()

    def block_copy(k):
        return pltpu.make_async_remote_copy(
            src_ref=given.at[k],
            dst_ref=got.at[k],
            send_sem=send_sem.at[k],
            recv_sem=recv_sem.at[k],
            device_id=twin_id,
            device_id_type=MESH_ID,
        )

    def make(store):
        step = 512
        for first in range(0, w_ref.shape[0], step):
            cols = pl.ds(first, step)
            store(cols, mm(rows_in[step_at], w_ref[cols, :], ((1,), (1,))))

    @pl.when(is_far)
    def _():
        def store(cols, total):
            given[slot, :, cols] = low(total)

        make(store)
        block_copy(slot).start()

    @pl.when(jnp.logical_not(is_far))
    def _():
        block_copy(slot).wait_recv()

        def store(cols, total):
            got[slot, :, cols] = low(total + got[slot, :, cols].astype(jnp.float32))

        make(store)

    own, x_send, y_send, rest = near_refs
    top, bottom = pl.ds(0, tokens // 2), pl.ds(tokens // 2, tokens // 2)
    pieces = [
        (0, pl.ds(0, tokens), own),
        (1, top, x_send.at[bottom]),
        (1, bottom, rest.at[bottom]),
        (2, top, rest.at[top]),
        (2, bottom, y_send.at[bottom]),
        (3, top, x_send.at[top]),
        (3, bottom, y_send.at[top]),
    ]
    hand_out(step_at, half, got, pieces, out_sem)

    @pl.when(step_at == 2 * half - 1)
    def _():
        for k in range(half):
            block_copy(k).wait_send()


def n1_grad_parts(grads, w, blocks):
    rows, cols = grads.shape
    width = w.shape[0]
    tokens, half = rows // blocks, blocks // 2
    return pl.pallas_call(
        partial(n1_grad_kernel, half),
        grid=(blocks,),
        in_specs=[
            pl.BlockSpec(memory_space=pl.ANY),
            pl.BlockSpec((width, cols), lambda i: (0, 0)),
        ],
        out_specs=[pl.BlockSpec(memory_space=pl.ANY)] * half,
        out_shape=[jax.ShapeDtypeStruct((tokens, width), jnp.bfloat16)] * half,
        scratch_shapes=[
            pltpu.VMEM((blocks, tokens, cols), jnp.bfloat16),
            pltpu.VMEM((half, tokens, width), jnp.bfloat16),
            pltpu.VMEM((half, tokens, width), jnp.bfloat16),
            pltpu.SemaphoreType.DMA((blocks,)),
            pltpu.SemaphoreType.DMA((half,)),
            pltpu.SemaphoreType.DMA((half,)),
            pltpu.SemaphoreType.DMA((7,)),
        ],
        compiler_params=pltpu.CompilerParams(
            collective_id=1, has_side_effects=True, vmem_limit_bytes=48 * 2**20
        ),
        cost_estimate=pl.CostEstimate(
            flops=2 * rows * width * cols,
            bytes_accessed=4 * rows * width,
            transcendentals=0,
        ),
    )(grads, w)


def after(values, others):
    return lax.optimization_barrier((values, others))[0]


def swap(values, bits):
    return lax.ppermute(values, EXP, [(i, i ^ bits) for i in range(4)])


def twin(values):
    return lax.ppermute(values, CTX, [(0, 1), (1, 0)])


def twin_sums(ours, theirs):
    got = twin(theirs)
    return [low(ours[k].astype(jnp.float32) + got[k].astype(jnp.float32)) for k in range(4)]


def hops(sums):
    return [sums[0]] + [swap(sums[k], k) for k in (1, 2, 3)]


def two_stage_sum(own, x_send, y_send, rest, between, later):
    half = own.shape[0] // 2
    wide = lambda v: v.astype(jnp.float32)
    x_got, y_got = after((swap(x_send, 1), swap(y_send, 2)), between)
    y_last = swap(low(wide(rest[:half]) + wide(x_got[:half])), 2)
    x_last = swap(low(wide(rest[half:]) + wide(y_got[:half])), 1)
    x_last, y_last = after((x_last, y_last), later)
    return jnp.concatenate(
        [
            wide(own[:half]) + wide(x_got[half:]) + wide(y_last),
            wide(own[half:]) + wide(y_got[half:]) + wide(x_last),
        ]
    )


def sum_up(parts):
    return sum(v.astype(jnp.float32) for v in parts)


def mm(left, right, dims=((1,), (0,))):
    return lax.dot_general(left, right, (dims, ((), ())), preferred_element_type=jnp.float32)


def low(values):
    return values.astype(jnp.bfloat16)


def local_plane(
    hidden,
    cotangent,
    segments,
    padding,
    routes,
    order,
    norm1_gain,
    w_query,
    w_key,
    w_value,
    w_out,
    norm2_gain,
    router,
    shared_gate_vec,
    shared_w_gate,
    shared_w_up,
    shared_w_down,
    expert_w_gate,
    expert_w_up,
    expert_w_down,
):
    plane = lax.axis_size(PLANE)
    groups = lax.axis_size(EXP)
    halves = lax.axis_size(CTX)
    depth = lax.axis_size(DP)
    me = lax.axis_index(PLANE)
    core = lax.axis_index(CTX)
    tokens, width = hidden.shape[1], hidden.shape[2]
    all_tokens = plane * tokens
    seq_len = halves * tokens
    experts_all = router.shape[1]
    head_cols = width // plane
    shard = width // depth

    token_info = jnp.concatenate(
        [segments + 1, jnp.where(padding > 0, segments + 1, 0), order[0], routes[0].T]
    )
    info_rows = token_info.shape[0]
    token_info = jnp.concatenate([token_info, jnp.zeros((8 - info_rows, tokens), jnp.int32)])

    hidden_all, info_all = plane_gather(hidden[0], token_info, False, 0)
    hidden_all = hidden_all.reshape(all_tokens, width)
    place = lax.axis_index(EXP)
    away = [(place ^ k) * 2 + (core ^ j) for j in (0, 1) for k in range(4)]
    away = jnp.stack(away)
    out_rows = shard // plane
    w_out_part = lax.dynamic_slice(w_out, (me * out_rows, 0), (out_rows, width))
    w_qkv_part = jnp.concatenate(
        [
            lax.dynamic_slice(w, (0, me * head_cols), (shard, head_cols))
            for w in (w_query, w_key, w_value)
        ]
        + [router, norm1_gain[:, None], norm2_gain[:, None], shared_gate_vec[:, None]]
        + [jnp.zeros((shard, 128 - experts_all - 3), jnp.bfloat16)]
        + [w_out_part.reshape(shard, -1)],
        axis=1,
    )
    w_qkv = lax.all_gather(w_qkv_part, DP, axis=0, tiled=True)
    w_out_part = w_qkv[:, 3 * head_cols + 128 :].reshape(depth, out_rows, width)
    small = w_qkv[:, 3 * head_cols : 3 * head_cols + 128].T
    w_qkv = w_qkv[:, : 3 * head_cols]
    router_t = small[:experts_all]
    g_one = small[experts_all].astype(jnp.float32)
    g_two = small[experts_all + 1].astype(jnp.float32)
    gate_vec = small[experts_all + 2]
    w_out_part = after(w_out_part, info_all)
    w_out_got = [swap(w_out_part, k) for k in (1, 2, 3)]

    def normed(values, gain):
        values = values.astype(jnp.float32)
        inv = lax.rsqrt(jnp.mean(values * values, axis=1, keepdims=True) + EPS)
        return values, inv, low(values * inv * gain)

    n1_all, qkv = norm_qkv(hidden_all, g_one[None], w_qkv, tokens)
    q_codes = info_all[:, 0].reshape(all_tokens, 1)
    k_codes = info_all[:, 1].reshape(all_tokens // seq_len, 1, seq_len)
    attended_cols = attention_call(qkv, None, q_codes, k_codes, seq_len)
    pieces = [w_out_part] + [after(v, attended_cols) for v in w_out_got]
    w_out_near = jnp.zeros((depth, groups, 1, out_rows, width), jnp.bfloat16)
    for k in range(4):
        w_out_near = lax.dynamic_update_slice(
            w_out_near, pieces[k][:, None, None], (0, place ^ k, 0, 0, 0)
        )
    w_out_far = twin(w_out_near)
    w_out_full = jnp.where(
        core == 0,
        jnp.concatenate([w_out_near, w_out_far], axis=2),
        jnp.concatenate([w_out_far, w_out_near], axis=2),
    ).reshape(width, width)

    x_rows, inv_one, _ = normed(hidden[0], g_one)
    cot_rows = cotangent[0].astype(jnp.float32)

    def to_tokens(cols):
        got = lax.all_to_all(
            cols.reshape(plane, tokens, head_cols), PLANE, split_axis=0, concat_axis=0, tiled=True
        )
        return got.transpose(1, 0, 2).reshape(tokens, width)

    def to_columns(rows_in):
        send = rows_in.reshape(tokens, plane, head_cols).transpose(1, 0, 2)
        got = lax.all_to_all(send, PLANE, split_axis=0, concat_axis=0, tiled=True)
        return got.reshape(all_tokens, head_cols)

    attended = to_tokens(attended_cols)
    residual = x_rows + mm(attended, w_out_full)
    residual, inv_two, n2 = normed(residual, g_two)

    units = shared_w_gate.shape[1]
    part = units // (depth * halves)
    pick = lambda w: lax.dynamic_index_in_dim(
        w.reshape(w.shape[0], depth, halves, part), core, axis=2, keepdims=False
    ).reshape(w.shape[0], depth * part)
    sh_gate_up = jnp.concatenate([pick(shared_w_gate), pick(shared_w_up)], axis=1)
    sh_gate_up = lax.all_gather(sh_gate_up, DP, axis=0, tiled=True)
    sh_gate_t, sh_up_t = sh_gate_up[:, : depth * part].T, sh_gate_up[:, depth * part :].T
    sh_down = lax.all_gather(
        lax.dynamic_slice(shared_w_down, (core * part, 0), (part, width)), DP, axis=0, tiled=True
    )
    n2 = after(n2, sh_gate_up)
    n2_all = plane_gather(n2, None, True, 2)[0].reshape(all_tokens, width)
    cot_own = after(cotangent[0], n2_all)
    cot_got = [swap(cot_own, k) for k in (1, 2, 3)]
    ex_gate = lax.all_gather(after(expert_w_gate[0], info_all), DP, axis=0, tiled=True)
    ex_up = lax.all_gather(after(expert_w_up[0], info_all), DP, axis=0, tiled=True)
    ex_down = lax.all_gather(after(expert_w_down[0], info_all), DP, axis=1, tiled=True)

    small_w = jnp.concatenate([router_t, gate_vec[None]])

    def gates_of(rows_in):
        both = mm(rows_in, small_w, ((1,), (1,)))
        z = both[:, :experts_all]
        e = jnp.exp(z - jnp.max(z, axis=1, keepdims=True))
        return e / jnp.sum(e, axis=1, keepdims=True), jax.nn.sigmoid(both[:, experts_all:])

    probs_all, sg_all = gates_of(n2_all)
    expert_gate = lax.dynamic_slice(probs_all, (0, me), (all_tokens, 1))

    capacity = (9 * tokens * TOP + 8 * experts_all - 1) // (8 * experts_all)
    info_away = info_all[away]
    order_all = info_away[:, 2]
    routed_here = jnp.any(info_away[:, 3 : 3 + TOP] == me, axis=1)
    earlier = (order_all[:, None, :] < order_all[:, :, None]) & routed_here[:, None, :]
    slots = jnp.sum(earlier.astype(jnp.int32), axis=2)
    slots = jnp.where(routed_here, slots, capacity)
    chosen = slots[:, None, :] == jnp.arange(capacity, dtype=jnp.int32)[None, :, None]
    onehot = chosen.astype(jnp.bfloat16)

    def rows_of(values):
        got = lax.dot_general(
            onehot,
            values.reshape(plane, tokens, width),
            (((2,), (1,)), ((0,), (0,))),
            preferred_element_type=jnp.float32,
        )
        return got.reshape(plane * capacity, width)

    slot_gates = jnp.sum(
        jnp.where(chosen, expert_gate.reshape(plane, 1, tokens), 0.0), axis=2
    ).reshape(plane * capacity, 1)
    expert_rows = low(rows_of(n2_all))
    gate_pre = mm(sh_gate_t, n2_all, ((1,), (1,)))
    up_pre = mm(sh_up_t, n2_all, ((1,), (1,)))
    gate_act = gate_pre * jax.nn.sigmoid(gate_pre)
    shared_hidden = low(gate_act * up_pre)
    expert_rows = after(expert_rows, (shared_hidden, sh_down))
    gate_e = mm(expert_rows, ex_gate)
    up_e = mm(expert_rows, ex_up)
    act_e = gate_e * jax.nn.sigmoid(gate_e)
    hidden_e = low(act_e * up_e)
    cot_near = jnp.concatenate([cot_own] + [after(v, gate_e) for v in cot_got])
    cot_all = jnp.concatenate([cot_near, twin(cot_near)])
    row_cots = low(rows_of(cot_all))
    row_grads = low(row_cots.astype(jnp.float32) * slot_gates)

    shared_grads = low(sg_all * cot_all.astype(jnp.float32))
    shared_hgrad = mm(sh_down, shared_grads, ((1,), (1,)))
    gate_grad_s = low(shared_hgrad * up_pre * silu_grad(gate_pre))
    up_grad_s = low(shared_hgrad * gate_act)
    rows_out = width // (halves * depth)

    def shared_scatter(total):
        first, second = total[:, :, :rows_out], total[:, :, rows_out:]
        keep = jnp.where(core == 0, first, second)
        got = twin(jnp.where(core == 0, second, first))
        both = [v.reshape(3, depth, part, rows_out) for v in (keep, got)]
        both = jnp.where(core == 0, jnp.stack(both, axis=2), jnp.stack(both[::-1], axis=2))
        return both.reshape(3, units, rows_out).astype(jnp.float32)

    scatter = lambda v, dim: lax.psum_scatter(v, DP, scatter_dimension=dim, tiled=True)
    shared_sums = unit_grads(
        shared_hidden, gate_grad_s, up_grad_s, shared_grads, n2_all, depth, halves
    )
    shared_sums = scatter(shared_sums.reshape(3 * depth * depth * part, -1), 0)
    result_e = low(mm(hidden_e, ex_down))
    hgrad_e = mm(row_grads, ex_down, ((1,), (1,)))
    gate_grad_e = low(hgrad_e * up_e * silu_grad(gate_e))
    up_grad_e = low(hgrad_e * act_e)

    grad_ex_down = low(mm(hidden_e, row_grads, ((0,), (0,))))
    slots = slots.reshape(all_tokens, 1)
    *out_near, dots = output_parts(
        shared_hidden,
        sh_down,
        result_e.reshape(plane, capacity, width),
        slots,
        sg_all,
        expert_gate,
        cot_all,
    )
    expert_rows = after(expert_rows, out_near)
    grad_ex_gate = low(mm(expert_rows, gate_grad_e, ((0,), (0,))))
    grad_ex_up = low(mm(expert_rows, up_grad_e, ((0,), (0,))))
    grads_made = (grad_ex_down, grad_ex_gate, grad_ex_up)
    grads = [scatter(v, dim) for v, dim in zip(grads_made, (1, 0, 0))]
    rows_grad = low(
        mm(gate_grad_e, ex_gate, ((1,), (1,))) + mm(up_grad_e, ex_up, ((1,), (1,)))
    )

    out_got = [out_near[0]] + [swap(out_near[k], k) for k in (1, 2)]
    slots, out_got, _ = lax.optimization_barrier((slots, out_got, (shared_sums, grads_made)))
    n2_grad = n2_grad_sum(
        gate_grad_s,
        up_grad_s,
        sh_gate_t,
        sh_up_t,
        rows_grad.reshape(plane, capacity, width),
        slots,
    )
    out_far = swap(after(out_near[3], n2_grad), 3)

    dots = dots.reshape(plane, tokens, 128)[:, :, :2].transpose(0, 2, 1)
    back = jnp.arange(plane, dtype=jnp.int32) ^ me
    dots = dots[(back // 2) + 4 * (back % 2)]
    dots = lax.all_to_all(dots, PLANE, split_axis=0, concat_axis=0, tiled=True)
    probs_grad = dots[:, 0].T
    probs, sg = gates_of(n2)
    logit_grad = low(probs * (probs_grad - jnp.sum(probs * probs_grad, axis=1, keepdims=True)))
    sg_logit_grad = low(jnp.sum(dots[:, 1], axis=0)[:, None] * sg * (1.0 - sg))
    n2_grad = (
        n2_grad
        + mm(logit_grad, router_t)
        + sg_logit_grad.astype(jnp.float32) * gate_vec.astype(jnp.float32)[None]
    )
    residual_grad, grad_gain_two = norm_back(residual, inv_two, g_two, n2_grad)
    residual_grad = residual_grad + cot_rows
    low_residual = low(residual_grad)

    attended_grad = low(mm(low_residual, w_out_full, ((1,), (1,))))
    low_residual = after(low_residual, attended_grad)
    output = residual + sum_up(after(out_got, attended_grad))
    attended_grad = to_columns(attended_grad)
    grad_out = low(mm(attended, low_residual, ((0,), (0,))))
    grad_out = grad_out.reshape(groups, halves, width // plane, width)
    block_of = lambda k, c: lax.dynamic_slice(
        grad_out, (place ^ k, c, 0, 0), (1, 1, width // plane, width)
    )[0, 0]
    out_grad_sums = twin_sums(
        [block_of(k, core) for k in range(4)],
        jnp.stack([block_of(k, 1 - core) for k in range(4)]),
    )
    dz_all = jnp.concatenate([logit_grad, sg_logit_grad], axis=1)
    dz_all = after(dz_all, out_grad_sums)
    small_grads = mm(n2, dz_all, ((0,), (0,)))
    small_grads = jnp.concatenate([small_grads, grad_gain_two[:, None]], axis=1).T
    small_grads = jnp.pad(small_grads, ((0, 14 - experts_all), (0, 0)))
    small_grads = small_grads.reshape(16, plane, width // plane).transpose(1, 0, 2)
    attended_grad, small_grads = lax.optimization_barrier((attended_grad, small_grads))
    attended_grad = after(attended_grad, (out_grad_sums, output, grads[0]))
    qkv_grad = attention_call(qkv, attended_grad, q_codes, k_codes, seq_len)
    out_grad_got = hops(out_grad_sums)
    qkv_grad, out_grad_got = lax.optimization_barrier((qkv_grad, out_grad_got))
    small_grads = after(small_grads, qkv_grad)
    small_grads = jnp.sum(
        lax.all_to_all(small_grads, PLANE, split_axis=0, concat_axis=0, tiled=True), axis=0
    )
    grad_qkv = low(mm(n1_all, qkv_grad, ((0,), (0,))))
    fine = shard // plane
    grad_qkv = (
        grad_qkv.reshape(plane, depth, fine, 3 * head_cols)
        .transpose(1, 0, 2, 3)
        .reshape(width, 3 * head_cols)
    )
    qkv_grad, small_grads, out_far, _ = lax.optimization_barrier(
        (qkv_grad, small_grads, out_far, (grad_qkv, grads[1]))
    )
    output = low(output + out_far.astype(jnp.float32))
    n1_near = n1_grad_parts(qkv_grad, w_qkv, plane)
    grad_out = low(sum_up(out_grad_got))
    grad_qkv = lax.psum_scatter(grad_qkv, DP, scatter_dimension=0, tiled=True)
    qkv_sum = grad_qkv
    w_rows = (
        w_qkv.reshape(plane, depth, fine, 3 * head_cols)
        .transpose(1, 0, 2, 3)
        .reshape(depth, plane * fine, 3 * head_cols)
    )
    w_rows = lax.dynamic_index_in_dim(w_rows, lax.axis_index(DP), axis=0, keepdims=False)
    gain_dots = jnp.sum(grad_qkv.astype(jnp.float32) * w_rows.astype(jnp.float32), axis=1)
    my_gain = lax.dynamic_slice(
        g_one, ((me * depth + lax.axis_index(DP)) * fine,), (fine,)
    )
    gain_dots = jnp.broadcast_to(low(gain_dots).reshape(plane, fine, 1), (plane, fine, 128))
    grad_qkv = lax.all_to_all(
        jnp.concatenate([grad_qkv.reshape(plane, fine, 3 * head_cols), gain_dots], axis=2),
        PLANE,
        split_axis=0,
        concat_axis=0,
        tiled=True,
    )
    gain_dots = grad_qkv[:, :, 3 * head_cols].astype(jnp.float32)
    grad_gain_one = jnp.sum(gain_dots, axis=0) / my_gain
    grad_qkv = (
        grad_qkv[:, :, : 3 * head_cols]
        .reshape(plane, fine, 3, head_cols)
        .transpose(2, 1, 0, 3)
        .reshape(3, fine, width)
        .astype(jnp.float32)
    )
    grad_ex_down, grad_ex_gate, grad_ex_up = [
        v.astype(jnp.float32)[None] for v in after(grads, n1_near)
    ]
    grad_out = scatter(after(grad_out, qkv_sum), 0).astype(jnp.float32)
    shared_sums = after(shared_sums, n1_near)
    shared_sums = shared_scatter(shared_sums.reshape(3, units // halves, -1))
    grad_sh_down, grad_sh_gate, grad_sh_up = [shared_sums[k] for k in range(3)]
    grad_sh_gate, grad_sh_up = grad_sh_gate.T, grad_sh_up.T
    small_grads = after(small_grads, n1_near)
    small_grads = small_grads.reshape(16, depth, shard // plane).transpose(1, 0, 2)
    small_grads = jnp.sum(
        lax.all_to_all(small_grads, DP, split_axis=0, concat_axis=0, tiled=True), axis=0
    )
    n1_grad = two_stage_sum(*n1_near, qkv_sum, grad_qkv)
    input_part, _ = norm_back(x_rows, inv_one, g_one, n1_grad)
    input_grad = low(residual_grad + input_part)
    return (
        output[None],
        input_grad[None],
        grad_gain_one,
        grad_qkv[0],
        grad_qkv[1],
        grad_qkv[2],
        grad_out,
        small_grads[experts_all + 1],
        small_grads[:experts_all].T,
        small_grads[experts_all],
        grad_sh_gate,
        grad_sh_up,
        grad_sh_down,
        grad_ex_gate,
        grad_ex_up,
        grad_ex_down,
    )


def solution(mesh):
    in_specs = (
        P((EXP, DP), CTX, None),
        P((EXP, DP), CTX, None),
        P((EXP, DP), CTX),
        P((EXP, DP), CTX),
        P((EXP, DP), CTX, None),
        P((EXP, DP), CTX, None),
        P(DP),
        P(DP, None),
        P(DP, None),
        P(DP, None),
        P(DP, None),
        P(DP),
        P(DP, None),
        P(DP),
        P(DP, EXP),
        P(DP, EXP),
        P((EXP, DP), None),
        P((EXP, CTX), DP, None),
        P((EXP, CTX), DP, None),
        P((EXP, CTX), None, DP),
    )
    out_specs = (
        P((EXP, DP), CTX, None),
        P((EXP, DP), CTX, None),
        P((EXP, CTX, DP)),
        P((EXP, CTX, DP), None),
        P((EXP, CTX, DP), None),
        P((EXP, CTX, DP), None),
        P((EXP, CTX, DP), None),
        P((EXP, CTX, DP)),
        P((EXP, CTX, DP), None),
        P((EXP, CTX, DP)),
        P((CTX, DP), EXP),
        P((CTX, DP), EXP),
        P(EXP, (CTX, DP)),
        P((EXP, CTX), DP, None),
        P((EXP, CTX), DP, None),
        P((EXP, CTX), None, DP),
    )
    plane = mesh.shape[EXP] * mesh.shape[CTX]

    def run(*args):
        square = mesh.shape[EXP] == 4 and mesh.shape[CTX] == 2 and mesh.shape[DP] == 4
        one_each = square and args[12].shape[1] == plane
        local = local_plane if one_each else local_general
        return jax.shard_map(
            local, mesh=mesh, in_specs=in_specs, out_specs=out_specs, check_vma=False
        )(*args)

    return run
```

```python
from functools import partial

import jax
import jax.numpy as jnp
from jax import lax
from jax.experimental import pallas as pl
from jax.experimental.pallas import tpu as pltpu
from jax.sharding import PartitionSpec as P

EXP, CTX, DP = "experts", "context", "dp"
PLANE = (EXP, CTX)
HEADS = 16
HEAD_DIM = 128
TOP = 4


EPS = 1e-06
NEG = -1e30


def silu_grad(pre_act):
    logistic = jax.nn.sigmoid(pre_act)
    return logistic * (1.0 + pre_act * (1.0 - logistic))


def block_slots(route_row, priority, expert_count):
    matches = (route_row[:, None] == jnp.arange(expert_count, dtype=jnp.int32)[None, :]).astype(
        jnp.int32
    )
    ordered = jnp.zeros_like(matches).at[priority].set(matches)
    before = jnp.cumsum(ordered, axis=0) - ordered
    return jnp.sum(before[priority] * matches, axis=1)


def norm_back(values_in, inv_rms, gain_vec, gradient):
    weighted = gradient * gain_vec
    inner_sum = jnp.mean(weighted * values_in, axis=1, keepdims=True)
    d_value = inv_rms * weighted - values_in * inv_rms**3 * inner_sum
    d_gain = jnp.sum(gradient * values_in * inv_rms, axis=0)
    return (d_value, d_gain)


def attend_head(packed, allowed, scale_factor):
    query_h, key_h, value_h = packed
    raw_scores = jnp.einsum("th,lh->tl", query_h, key_h, preferred_element_type=jnp.float32)
    logits = jnp.where(allowed, raw_scores * scale_factor, NEG)
    row_max = jnp.max(logits, axis=1, keepdims=True)
    exp_scores = jnp.exp(logits - row_max)
    row_total = jnp.sum(exp_scores, axis=1, keepdims=True)
    attn_probs = (exp_scores / row_total).astype(jnp.bfloat16)
    head_out = jnp.dot(attn_probs, value_h, preferred_element_type=jnp.float32).astype(jnp.bfloat16)
    return (head_out, row_max + jnp.log(row_total))


def attend_back(packed, allowed, scale_factor):
    query_h, key_h, value_h, out_grad, log_total = packed
    raw_scores = jnp.einsum("th,lh->tl", query_h, key_h, preferred_element_type=jnp.float32)
    logits = jnp.where(allowed, raw_scores * scale_factor, NEG)
    attn_probs = jnp.exp(logits - log_total)
    prob_grad = jnp.einsum("th,lh->tl", out_grad, value_h, preferred_element_type=jnp.float32)
    inner_sum = jnp.sum(attn_probs * prob_grad, axis=1, keepdims=True)
    score_grad = (attn_probs * (prob_grad - inner_sum) * scale_factor).astype(jnp.bfloat16)
    query_grad = jnp.dot(score_grad, key_h, preferred_element_type=jnp.float32)
    key_grad = jnp.einsum("tl,th->lh", score_grad, query_h, preferred_element_type=jnp.float32)
    value_grad = jnp.einsum(
        "tl,th->lh", attn_probs.astype(jnp.bfloat16), out_grad, preferred_element_type=jnp.float32
    )
    return (query_grad, key_grad, value_grad)


def local_general(
    hidden,
    cotangent,
    segments,
    padding,
    routes,
    order,
    norm1_gain,
    w_query,
    w_key,
    w_value,
    w_out,
    norm2_gain,
    router,
    shared_gate_vec,
    shared_w_gate,
    shared_w_up,
    shared_w_down,
    expert_w_gate,
    expert_w_up,
    expert_w_down,
):
    fetched = (
        lax.all_gather(norm1_gain, DP, axis=0, tiled=True),
        lax.all_gather(w_query, DP, axis=0, tiled=True),
        lax.all_gather(w_key, DP, axis=0, tiled=True),
        lax.all_gather(w_value, DP, axis=0, tiled=True),
        lax.all_gather(w_out, DP, axis=0, tiled=True),
        lax.all_gather(norm2_gain, DP, axis=0, tiled=True),
        lax.all_gather(router, DP, axis=0, tiled=True),
        lax.all_gather(shared_gate_vec, DP, axis=0, tiled=True),
        lax.all_gather(shared_w_gate, DP, axis=0, tiled=True),
        lax.all_gather(shared_w_up, DP, axis=0, tiled=True),
        lax.all_gather(shared_w_down, DP, axis=0, tiled=True),
        lax.all_gather(expert_w_gate, DP, axis=1, tiled=True),
        lax.all_gather(expert_w_up, DP, axis=1, tiled=True),
        lax.all_gather(expert_w_down, DP, axis=2, tiled=True),
    )
    (
        gain_one,
        query_w,
        key_w,
        value_w,
        out_w,
        gain_two,
        router_full,
        gate_vec,
        sh_gate,
        sh_up,
        sh_down,
        ex_gate,
        ex_up,
        ex_down,
    ) = fetched
    sh_gate, sh_up, sh_down = (
        lax.all_gather(sh_gate, EXP, axis=1, tiled=True),
        lax.all_gather(sh_up, EXP, axis=1, tiled=True),
        lax.all_gather(sh_down, EXP, axis=0, tiled=True),
    )
    tokens_here = hidden.shape[1]
    model_width = hidden.shape[2]
    x_rows = hidden[0].astype(jnp.float32)
    cot_rows = cotangent[0].astype(jnp.float32)
    inv_one = lax.rsqrt(jnp.mean(x_rows * x_rows, axis=1, keepdims=True) + EPS)
    g_one = gain_one.astype(jnp.float32)
    normed_one = (x_rows * inv_one * g_one).astype(jnp.bfloat16)
    queries = jnp.dot(normed_one, query_w, preferred_element_type=jnp.float32).astype(jnp.bfloat16)
    keys_own = jnp.dot(normed_one, key_w, preferred_element_type=jnp.float32).astype(jnp.bfloat16)
    values_own = jnp.dot(normed_one, value_w, preferred_element_type=jnp.float32).astype(
        jnp.bfloat16
    )
    own_codes = jnp.where(padding[0] > 0, segments[0] + 1, 0)
    code_parts = jnp.stack([own_codes // 64, own_codes % 64]).astype(jnp.bfloat16)
    keys_all, values_all, parts_all = (
        lax.all_gather(keys_own, CTX, axis=0, tiled=True),
        lax.all_gather(values_own, CTX, axis=0, tiled=True),
        lax.all_gather(code_parts, CTX, axis=1, tiled=True),
    )
    key_codes = parts_all[0].astype(jnp.int32) * 64 + parts_all[1].astype(jnp.int32)
    seq_total = keys_all.shape[0]
    query_pos = lax.axis_index(CTX) * tokens_here + jnp.arange(tokens_here, dtype=jnp.int32)
    key_pos = jnp.arange(seq_total, dtype=jnp.int32)
    same_doc = key_codes[None, :] == (segments[0] + 1)[:, None]
    allowed = (key_pos[None, :] <= query_pos[:, None]) & (
        same_doc | (key_pos[None, :] == query_pos[:, None])
    )
    scale_factor = HEAD_DIM ** (-0.5)

    def to_heads(rows_in):
        return rows_in.reshape(rows_in.shape[0], HEADS, HEAD_DIM).transpose(1, 0, 2)

    def from_heads(heads_in):
        return heads_in.transpose(1, 0, 2).reshape(heads_in.shape[1], model_width)

    head_q = to_heads(queries)
    head_k = to_heads(keys_all)
    head_v = to_heads(values_all)
    head_out, log_total = lax.map(
        partial(attend_head, allowed=allowed, scale_factor=scale_factor), (head_q, head_k, head_v)
    )
    attended = from_heads(head_out)
    residual = x_rows + jnp.dot(attended, out_w, preferred_element_type=jnp.float32)
    inv_two = lax.rsqrt(jnp.mean(residual * residual, axis=1, keepdims=True) + EPS)
    g_two = gain_two.astype(jnp.float32)
    normed_two = (residual * inv_two * g_two).astype(jnp.bfloat16)
    router_logits = jnp.dot(normed_two, router_full, preferred_element_type=jnp.float32)
    router_exp = jnp.exp(router_logits - jnp.max(router_logits, axis=1, keepdims=True))
    router_probs = router_exp / jnp.sum(router_exp, axis=1, keepdims=True)
    route_gates = jnp.take_along_axis(router_probs, routes[0], axis=1)
    shared_gate = jax.nn.sigmoid(jnp.dot(normed_two, gate_vec, preferred_element_type=jnp.float32))
    shared_scaled = (shared_gate[:, None] * cot_rows).astype(jnp.bfloat16)
    rows_group, grads_group = (normed_two, shared_scaled)
    gate_pre = jnp.dot(rows_group, sh_gate, preferred_element_type=jnp.float32)
    up_pre = jnp.dot(rows_group, sh_up, preferred_element_type=jnp.float32)
    gate_act = gate_pre * jax.nn.sigmoid(gate_pre)
    shared_hidden = (gate_act * up_pre).astype(jnp.bfloat16)
    shared_part = jnp.dot(shared_hidden, sh_down, preferred_element_type=jnp.float32)
    experts_all = router_full.shape[1]
    capacity = (9 * tokens_here * TOP + 8 * experts_all - 1) // (8 * experts_all)
    priority = (order[0, 0][:, None] * TOP + jnp.arange(TOP, dtype=jnp.int32)[None, :]).reshape(-1)
    flat_routes = routes[0].reshape(-1)
    slot_index = block_slots(flat_routes, priority, experts_all)
    kept_rows = slot_index < capacity
    target = flat_routes * capacity + jnp.minimum(slot_index, capacity - 1)
    row_gates = route_gates.reshape(-1)
    cot_repeated = jnp.repeat(cot_rows, TOP, axis=0)
    source_rows = jnp.repeat(normed_two, TOP, axis=0)
    source_grads = (cot_repeated * row_gates[:, None]).astype(jnp.bfloat16)
    empty_slots = jnp.zeros((experts_all * capacity, model_width), jnp.bfloat16)
    send_rows = empty_slots.at[target].add(
        jnp.where(kept_rows[:, None], source_rows, jnp.zeros_like(source_rows))
    )
    send_grads = empty_slots.at[target].add(
        jnp.where(kept_rows[:, None], source_grads, jnp.zeros_like(source_grads))
    )
    recv_rows, recv_grads = (
        lax.all_to_all(
            send_rows.reshape(experts_all, capacity, model_width),
            (EXP, CTX),
            split_axis=0,
            concat_axis=0,
            tiled=True,
        ),
        lax.all_to_all(
            send_grads.reshape(experts_all, capacity, model_width),
            (EXP, CTX),
            split_axis=0,
            concat_axis=0,
            tiled=True,
        ),
    )
    local_count = ex_gate.shape[0]
    sources = experts_all // local_count

    def to_local(buffer_in):
        return (
            buffer_in.reshape(sources, local_count, capacity, model_width)
            .transpose(1, 0, 2, 3)
            .reshape(local_count, sources * capacity, model_width)
        )

    def to_owner(buffer_in):
        return (
            buffer_in.reshape(local_count, sources, capacity, model_width)
            .transpose(1, 0, 2, 3)
            .reshape(experts_all, capacity, model_width)
        )

    expert_rows = to_local(recv_rows)
    expert_grads_in = to_local(recv_grads)
    gate_e = jnp.einsum("erd,edf->erf", expert_rows, ex_gate, preferred_element_type=jnp.float32)
    up_e = jnp.einsum("erd,edf->erf", expert_rows, ex_up, preferred_element_type=jnp.float32)
    act_e = gate_e * jax.nn.sigmoid(gate_e)
    hidden_e = (act_e * up_e).astype(jnp.bfloat16)
    result_e = jnp.einsum(
        "erf,efd->erd", hidden_e, ex_down, preferred_element_type=jnp.float32
    ).astype(jnp.bfloat16)
    returned = lax.all_to_all(
        to_owner(result_e), (EXP, CTX), split_axis=0, concat_axis=0, tiled=True
    )
    picked = returned.reshape(experts_all * capacity, model_width)[target]
    picked = jnp.where(kept_rows[:, None], picked, jnp.zeros_like(picked)).astype(jnp.float32)
    routed = jnp.sum((picked * row_gates[:, None]).reshape(tokens_here, TOP, model_width), axis=1)
    output = (residual + shared_gate[:, None] * shared_part + routed).astype(jnp.bfloat16)
    gate_grads = jnp.sum(picked * cot_repeated, axis=1).reshape(tokens_here, TOP)
    hidden_grad_e = jnp.einsum(
        "erd,efd->erf", expert_grads_in, ex_down, preferred_element_type=jnp.float32
    )
    gate_grad_e = (hidden_grad_e * up_e * silu_grad(gate_e)).astype(jnp.bfloat16)
    up_grad_e = (hidden_grad_e * act_e).astype(jnp.bfloat16)
    grad_ex_down = jnp.einsum(
        "erf,erd->efd", hidden_e, expert_grads_in, preferred_element_type=jnp.float32
    )
    grad_ex_gate = jnp.einsum(
        "erd,erf->edf", expert_rows, gate_grad_e, preferred_element_type=jnp.float32
    )
    grad_ex_up = jnp.einsum(
        "erd,erf->edf", expert_rows, up_grad_e, preferred_element_type=jnp.float32
    )
    expert_sums = (
        lax.psum_scatter(grad_ex_gate, DP, scatter_dimension=1, tiled=True),
        lax.psum_scatter(grad_ex_up, DP, scatter_dimension=1, tiled=True),
        lax.psum_scatter(grad_ex_down, DP, scatter_dimension=2, tiled=True),
    )
    rows_grad_e = jnp.einsum(
        "erf,edf->erd", gate_grad_e, ex_gate, preferred_element_type=jnp.float32
    )
    rows_grad_e = (
        rows_grad_e
        + jnp.einsum("erf,edf->erd", up_grad_e, ex_up, preferred_element_type=jnp.float32)
    ).astype(jnp.bfloat16)
    returned_grads = lax.all_to_all(
        to_owner(rows_grad_e), (EXP, CTX), split_axis=0, concat_axis=0, tiled=True
    )
    routed_grad = returned_grads.reshape(experts_all * capacity, model_width)[target]
    routed_grad = jnp.where(kept_rows[:, None], routed_grad, jnp.zeros_like(routed_grad)).astype(
        jnp.float32
    )
    norm_grad = jnp.sum(routed_grad.reshape(tokens_here, TOP, model_width), axis=1)
    choose = (
        routes[0][:, :, None] == jnp.arange(experts_all, dtype=jnp.int32)[None, None, :]
    ).astype(jnp.float32)
    probs_grad = jnp.einsum("tk,tke->te", gate_grads, choose)
    logit_grad = (
        router_probs * (probs_grad - jnp.sum(router_probs * probs_grad, axis=1, keepdims=True))
    ).astype(jnp.bfloat16)
    grad_router = jnp.dot(normed_two.T, logit_grad, preferred_element_type=jnp.float32)
    gate_logit_grad = (
        jnp.sum(cot_rows * shared_part, axis=1) * shared_gate * (1.0 - shared_gate)
    ).astype(jnp.bfloat16)
    grad_gate_vec = jnp.dot(gate_logit_grad, normed_two, preferred_element_type=jnp.float32)
    norm_grad = norm_grad + jnp.dot(logit_grad, router_full.T, preferred_element_type=jnp.float32)
    norm_grad = (
        norm_grad
        + gate_logit_grad.astype(jnp.float32)[:, None] * gate_vec.astype(jnp.float32)[None, :]
    )
    shared_hgrad = jnp.dot(grads_group, sh_down.T, preferred_element_type=jnp.float32)
    gate_grad_s = (shared_hgrad * up_pre * silu_grad(gate_pre)).astype(jnp.bfloat16)
    up_grad_s = (shared_hgrad * gate_act).astype(jnp.bfloat16)
    shared_rows_grad = jnp.dot(gate_grad_s, sh_gate.T, preferred_element_type=jnp.float32)
    shared_rows_grad = shared_rows_grad + jnp.dot(
        up_grad_s, sh_up.T, preferred_element_type=jnp.float32
    )
    groups = lax.axis_size(EXP)
    parts_cd = lax.axis_size((CTX, DP))
    rows_count = rows_group.shape[0]
    arr_gate = jnp.einsum(
        "td,tes->eds",
        rows_group,
        gate_grad_s.reshape(rows_count, groups, -1),
        preferred_element_type=jnp.float32,
    ).reshape(groups * model_width, -1)
    arr_up = jnp.einsum(
        "td,tes->eds",
        rows_group,
        up_grad_s.reshape(rows_count, groups, -1),
        preferred_element_type=jnp.float32,
    ).reshape(groups * model_width, -1)
    arr_down = jnp.einsum(
        "tes,tcd->ecsd",
        shared_hidden.reshape(rows_count, groups, -1),
        grads_group.reshape(rows_count, parts_cd, -1),
        preferred_element_type=jnp.float32,
    ).reshape(-1, model_width // parts_cd)
    sums_gate, sums_up, sums_down = (
        lax.psum_scatter(arr_gate, (EXP, CTX, DP), scatter_dimension=0, tiled=True),
        lax.psum_scatter(arr_up, (EXP, CTX, DP), scatter_dimension=0, tiled=True),
        lax.psum_scatter(arr_down, (EXP, CTX, DP), scatter_dimension=0, tiled=True),
    )
    norm_grad = norm_grad + shared_rows_grad
    residual_grad, grad_gain_two = norm_back(residual, inv_two, g_two, norm_grad)
    residual_grad = residual_grad + cot_rows
    low_residual = residual_grad.astype(jnp.bfloat16)
    grad_out_w = jnp.dot(attended.T, low_residual, preferred_element_type=jnp.float32)
    attended_grad = jnp.dot(low_residual, out_w.T, preferred_element_type=jnp.float32).astype(
        jnp.bfloat16
    )
    head_q_grad, head_k_grad, head_v_grad = lax.map(
        partial(attend_back, allowed=allowed, scale_factor=scale_factor),
        (head_q, head_k, head_v, to_heads(attended_grad), log_total),
    )
    key_sum, value_sum = (
        lax.psum_scatter(from_heads(head_k_grad), CTX, scatter_dimension=0, tiled=True),
        lax.psum_scatter(from_heads(head_v_grad), CTX, scatter_dimension=0, tiled=True),
    )
    query_low = from_heads(head_q_grad).astype(jnp.bfloat16)
    key_low = key_sum.astype(jnp.bfloat16)
    value_low = value_sum.astype(jnp.bfloat16)
    grad_query = jnp.dot(normed_one.T, query_low, preferred_element_type=jnp.float32)
    grad_key = jnp.dot(normed_one.T, key_low, preferred_element_type=jnp.float32)
    grad_value = jnp.dot(normed_one.T, value_low, preferred_element_type=jnp.float32)
    normed_grad = jnp.dot(query_low, query_w.T, preferred_element_type=jnp.float32)
    normed_grad = normed_grad + jnp.dot(key_low, key_w.T, preferred_element_type=jnp.float32)
    normed_grad = normed_grad + jnp.dot(value_low, value_w.T, preferred_element_type=jnp.float32)
    input_part, grad_gain_one = norm_back(x_rows, inv_one, g_one, normed_grad)
    input_grad = (residual_grad + input_part).astype(jnp.bfloat16)
    dense = (
        lax.psum_scatter(
            grad_gain_one, (EXP, CTX, DP), scatter_dimension=0, tiled=True
        ),
        lax.psum_scatter(grad_query, (EXP, CTX, DP), scatter_dimension=0, tiled=True),
        lax.psum_scatter(grad_key, (EXP, CTX, DP), scatter_dimension=0, tiled=True),
        lax.psum_scatter(grad_value, (EXP, CTX, DP), scatter_dimension=0, tiled=True),
        lax.psum_scatter(grad_out_w, (EXP, CTX, DP), scatter_dimension=0, tiled=True),
        lax.psum_scatter(
            grad_gain_two, (EXP, CTX, DP), scatter_dimension=0, tiled=True
        ),
        lax.psum_scatter(
            grad_router, (EXP, CTX, DP), scatter_dimension=0, tiled=True
        ),
        lax.psum_scatter(
            grad_gate_vec, (EXP, CTX, DP), scatter_dimension=0, tiled=True
        ),
    )
    return (
        output[None],
        input_grad[None],
        dense[0],
        dense[1],
        dense[2],
        dense[3],
        dense[4],
        dense[5],
        dense[6],
        dense[7],
        sums_gate,
        sums_up,
        sums_down,
        expert_sums[0],
        expert_sums[1],
        expert_sums[2],
    )

def attention_probs(q_blk, k_part, q_code, k_code, first_row, scale_factor):
    scores = lax.dot_general(
        q_blk, k_part, (((1,), (1,)), ((), ())), preferred_element_type=jnp.float32
    )
    row = first_row + lax.broadcasted_iota(jnp.int32, scores.shape, 0)
    col = lax.broadcasted_iota(jnp.int32, scores.shape, 1)
    allowed = ((col < row) & (k_code == q_code)) | (col == row)
    logits = jnp.where(allowed, scores * scale_factor, NEG)
    exp_scores = jnp.exp(logits - jnp.max(logits, axis=1, keepdims=True))
    return exp_scores * (1.0 / jnp.sum(exp_scores, axis=1, keepdims=True))


def attend_kernel(heads, step, qkv_ref, q_code_ref, k_code_ref, out_ref):
    seq_len = qkv_ref.shape[0]
    width = heads * HEAD_DIM
    for head in range(heads):
        at = head * HEAD_DIM
        for first in range(0, seq_len, step):
            upto = first + step
            probs = attention_probs(
                qkv_ref[first:upto, at : at + HEAD_DIM],
                qkv_ref[0:upto, width + at : width + at + HEAD_DIM],
                q_code_ref[first:upto, :],
                k_code_ref[0, :, 0:upto],
                first,
                HEAD_DIM**-0.5,
            )
            out_ref[first:upto, at : at + HEAD_DIM] = jnp.dot(
                probs.astype(jnp.bfloat16),
                qkv_ref[0:upto, 2 * width + at : 2 * width + at + HEAD_DIM],
                preferred_element_type=jnp.float32,
            ).astype(jnp.bfloat16)


def attend_back_kernel(
    heads, step, qkv_ref, grad_ref, q_code_ref, k_code_ref, out_ref, key_acc, value_acc
):
    seq_len = qkv_ref.shape[0]
    width = heads * HEAD_DIM
    for head in range(heads):
        at = head * HEAD_DIM
        key_at, value_at = width + at, 2 * width + at
        key_acc[...] = jnp.zeros_like(key_acc)
        value_acc[...] = jnp.zeros_like(value_acc)
        for first in range(0, seq_len, step):
            upto = first + step
            q_blk = qkv_ref[first:upto, at : at + HEAD_DIM]
            k_part = qkv_ref[0:upto, key_at : key_at + HEAD_DIM]
            v_part = qkv_ref[0:upto, value_at : value_at + HEAD_DIM]
            g_blk = grad_ref[first:upto, at : at + HEAD_DIM]
            probs = attention_probs(
                q_blk,
                k_part,
                q_code_ref[first:upto, :],
                k_code_ref[0, :, 0:upto],
                first,
                HEAD_DIM**-0.5,
            )
            prob_grad = lax.dot_general(
                g_blk, v_part, (((1,), (1,)), ((), ())), preferred_element_type=jnp.float32
            )
            inner = jnp.sum(probs * prob_grad, axis=1, keepdims=True)
            score_grad = (probs * (prob_grad - inner) * HEAD_DIM**-0.5).astype(jnp.bfloat16)
            out_ref[first:upto, at : at + HEAD_DIM] = jnp.dot(
                score_grad, k_part, preferred_element_type=jnp.float32
            ).astype(jnp.bfloat16)
            key_acc[0:upto, :] += lax.dot_general(
                score_grad, q_blk, (((0,), (0,)), ((), ())), preferred_element_type=jnp.float32
            )
            value_acc[0:upto, :] += lax.dot_general(
                probs.astype(jnp.bfloat16),
                g_blk,
                (((0,), (0,)), ((), ())),
                preferred_element_type=jnp.float32,
            )
        out_ref[:, key_at : key_at + HEAD_DIM] = key_acc[...].astype(jnp.bfloat16)
        out_ref[:, value_at : value_at + HEAD_DIM] = value_acc[...].astype(jnp.bfloat16)


def attention_call(qkv, grads, q_codes, k_codes, seq_len):
    rows, triple = qkv.shape
    width = triple // 3
    heads = width // HEAD_DIM
    step = min(256, seq_len)
    specs = [pl.BlockSpec((seq_len, triple), lambda s: (s, 0))]
    operands = [qkv]
    if grads is not None:
        specs.append(pl.BlockSpec((seq_len, width), lambda s: (s, 0)))
        operands.append(grads)
    specs += [
        pl.BlockSpec((seq_len, 1), lambda s: (s, 0)),
        pl.BlockSpec((1, 1, seq_len), lambda s: (s, 0, 0)),
    ]
    operands += [q_codes, k_codes]
    out_width = width if grads is None else triple
    body = attend_kernel if grads is None else attend_back_kernel
    passes = 2 if grads is None else 5
    area = rows * seq_len * heads
    return pl.pallas_call(
        partial(body, heads, step),
        grid=(rows // seq_len,),
        in_specs=specs,
        out_specs=pl.BlockSpec((seq_len, out_width), lambda s: (s, 0)),
        out_shape=jax.ShapeDtypeStruct((rows, out_width), jnp.bfloat16),
        scratch_shapes=[]
        if grads is None
        else [pltpu.VMEM((seq_len, HEAD_DIM), jnp.float32)] * 2,
        compiler_params=pltpu.CompilerParams(vmem_limit_bytes=48 * 2**20),
        cost_estimate=pl.CostEstimate(
            flops=2 * passes * area * HEAD_DIM,
            bytes_accessed=2 * rows * (triple + out_width),
            transcendentals=area,
        ),
    )(*operands)


MESH_ID = pl.DeviceIdType.MESH


def other_in_pair(index, bit):
    return index + bit - 2 * bit * (lax.div(index, bit) % 2)


def plane_places():
    at = lax.axis_index(EXP)
    core = lax.axis_index(CTX)
    across, along = other_in_pair(at, 1), other_in_pair(at, 2)
    return at, core, across, along, other_in_pair(along, 1)


def greet(across, along, core):
    barrier = pltpu.get_barrier_semaphore()
    for target in ({EXP: across}, {EXP: along}, {CTX: 1 - core}):
        pl.semaphore_signal(barrier, inc=1, device_id=target, device_id_type=MESH_ID)
    pl.semaphore_wait(barrier, 3)


def plane_gather_kernel(with_info, relative, *refs):
    if with_info:
        own_ref, info_ref, all_ref, info_all_ref, send_sem, recv_sem, local_sem = refs
    else:
        own_ref, all_ref, send_sem, recv_sem, local_sem = refs
    at, core, across, along, far = plane_places()
    rows = own_ref.shape[0]
    half = rows // 2
    top, bottom, whole = pl.ds(0, half), pl.ds(half, half), pl.ds(0, rows)
    greet(across, along, core)
    started = []
    twin_id = {CTX: 1 - core}

    def slot_of(place, shift, for_twin):
        if relative:
            return shift + 4 * for_twin
        return place * 2 + core

    def send(number, src, dst, target):
        copy = pltpu.make_async_remote_copy(
            src_ref=src,
            dst_ref=dst,
            send_sem=send_sem.at[number],
            recv_sem=recv_sem.at[number],
            device_id=target,
            device_id_type=MESH_ID,
        )
        copy.start()
        started.append(copy)
        return copy

    def piece(place, shift, part, for_twin=0):
        return all_ref.at[slot_of(place, shift, for_twin), part]

    x_top = send(0, own_ref.at[top], piece(at, 1, top), {EXP: across})
    y_bottom = send(1, own_ref.at[bottom], piece(at, 2, bottom), {EXP: along})
    x_bottom = send(2, own_ref.at[bottom], piece(at, 1, bottom), {EXP: across})
    y_top = send(3, own_ref.at[top], piece(at, 2, top), {EXP: along})
    twins = [send(4, own_ref, piece(at, 0, whole, 1), twin_id)]
    heres = [pltpu.make_async_copy(own_ref, piece(at, 0, whole), local_sem.at[0])]
    heres[0].start()
    if with_info:
        info_at = lambda place: info_all_ref.at[place * 2 + core]
        heres.append(pltpu.make_async_copy(info_ref, info_at(at), local_sem.at[1]))
        heres[1].start()
        info_x = send(13, info_ref, info_at(at), {EXP: across})
        info_y = send(14, info_ref, info_at(at), {EXP: along})
        twins.append(send(15, info_ref, info_at(at), twin_id))
        info_x.wait_recv()
        info_far = send(16, info_at(across), info_at(across), {EXP: along})
        twins.append(send(17, info_at(across), info_at(across), twin_id))
        info_y.wait_recv()
        twins.append(send(18, info_at(along), info_at(along), twin_id))
        info_far.wait_recv()
        twins.append(send(19, info_at(far), info_at(far), twin_id))

    def hand_on(number, place, shift, part):
        src = piece(place, shift, part)
        twins.append(send(number, src, piece(place, shift, part, 1), twin_id))

    x_top.wait_recv()
    far_top = send(5, piece(across, 1, top), piece(across, 3, top), {EXP: along})
    hand_on(6, across, 1, top)
    y_bottom.wait_recv()
    far_bottom = send(7, piece(along, 2, bottom), piece(along, 3, bottom), {EXP: across})
    hand_on(8, along, 2, bottom)
    x_bottom.wait_recv()
    hand_on(9, across, 1, bottom)
    y_top.wait_recv()
    hand_on(10, along, 2, top)
    far_top.wait_recv()
    hand_on(11, far, 3, top)
    far_bottom.wait_recv()
    hand_on(12, far, 3, bottom)
    for copy in twins:
        copy.wait_recv()
    for copy in started:
        copy.wait_send()
    for copy in heres:
        copy.wait()


def plane_gather(own, info, relative, number):
    plane = lax.axis_size(PLANE)
    operands = [own] if info is None else [own, info]
    outs = [jax.ShapeDtypeStruct((plane, *v.shape), v.dtype) for v in operands]
    anywhere = pl.BlockSpec(memory_space=pl.ANY)
    return pl.pallas_call(
        partial(plane_gather_kernel, info is not None, relative),
        out_shape=outs,
        in_specs=[anywhere] * len(operands),
        out_specs=[anywhere] * len(operands),
        scratch_shapes=[
            pltpu.SemaphoreType.DMA((20,)),
            pltpu.SemaphoreType.DMA((20,)),
            pltpu.SemaphoreType.DMA((2,)),
        ],
        compiler_params=pltpu.CompilerParams(collective_id=number, has_side_effects=True),
        cost_estimate=pl.CostEstimate(
            flops=0, bytes_accessed=own.size, transcendentals=0
        ),
    )(*operands)


def norm_qkv_kernel(hidden_ref, gain_ref, w_ref, norm_ref, qkv_ref):
    values = hidden_ref[...].astype(jnp.float32)
    inv = lax.rsqrt(jnp.mean(values * values, axis=1, keepdims=True) + EPS)
    norm_ref[...] = low(values * inv * gain_ref[...])
    qkv_ref[...] = low(mm(norm_ref[...], w_ref[...]))


def norm_qkv(hidden, gain, w, block):
    rows, width = hidden.shape
    cols = w.shape[1]
    return pl.pallas_call(
        norm_qkv_kernel,
        grid=(rows // block,),
        in_specs=[
            pl.BlockSpec((block, width), lambda i: (i, 0)),
            pl.BlockSpec((1, width), lambda i: (0, 0)),
            pl.BlockSpec((width, cols), lambda i: (0, 0)),
        ],
        out_specs=[
            pl.BlockSpec((block, width), lambda i: (i, 0)),
            pl.BlockSpec((block, cols), lambda i: (i, 0)),
        ],
        out_shape=[
            jax.ShapeDtypeStruct((rows, width), jnp.bfloat16),
            jax.ShapeDtypeStruct((rows, cols), jnp.bfloat16),
        ],
        compiler_params=pltpu.CompilerParams(vmem_limit_bytes=48 * 2**20),
        cost_estimate=pl.CostEstimate(
            flops=2 * rows * width * cols,
            bytes_accessed=4 * rows * width,
            transcendentals=0,
        ),
    )(hidden, gain, w)


def chosen_rows(slots, capacity):
    lanes = lax.broadcasted_iota(jnp.int32, (slots.shape[0], capacity), 1)
    return (slots == lanes).astype(jnp.bfloat16)


def hand_out(step_at, half, blocks, pieces, sems):
    copies = [
        pltpu.make_async_copy(blocks.at[k, part], goal, sems.at[number])
        for number, (k, part, goal) in enumerate(pieces)
    ]
    for k in range(half):

        @pl.when(step_at == half + k)
        def _():
            for copy, piece in zip(copies, pieces):
                if piece[0] == k:
                    copy.start()

    @pl.when(step_at == 2 * half - 1)
    def _():
        for copy in copies:
            copy.wait()


def output_kernel(
    half,
    hidden_ref,
    down_ref,
    rows_ref,
    slot_ref,
    sg_ref,
    gate_ref,
    cot_ref,
    *refs,
):
    near_refs, dots_ref, refs = refs[:half], refs[half], refs[half + 1 :]
    given, got, send_sem, recv_sem, out_sem = refs
    step_at = pl.program_id(0)
    is_far = step_at < half
    slot = lax.rem(step_at, half)
    twin_id = {CTX: 1 - lax.axis_index(CTX)}

    @pl.when(step_at == 0)
    def _():
        barrier = pltpu.get_barrier_semaphore()
        pl.semaphore_signal(barrier, inc=1, device_id=twin_id, device_id_type=MESH_ID)
        pl.semaphore_wait(barrier, 1)

    def block_copy(k):
        return pltpu.make_async_remote_copy(
            src_ref=given.at[k],
            dst_ref=got.at[k],
            send_sem=send_sem.at[k],
            recv_sem=recv_sem.at[k],
            device_id=twin_id,
            device_id_type=MESH_ID,
        )

    def make(store):
        chosen = chosen_rows(slot_ref[...], rows_ref.shape[1])
        hidden = hidden_ref[...].T
        tokens, width = cot_ref.shape
        step, lanes = 512, 128
        gate_dot = jnp.zeros((tokens, lanes), jnp.float32)
        shared_dot = jnp.zeros((tokens, lanes), jnp.float32)
        for first in range(0, width, step):
            cols = pl.ds(first, step)
            shared = mm(hidden, down_ref[:, cols])
            picked = mm(chosen, rows_ref[0, :, cols])
            cot = cot_ref[:, cols].astype(jnp.float32)
            gate_part, shared_part = picked * cot, shared * cot
            for at in range(0, step, lanes):
                gate_dot += gate_part[:, at : at + lanes]
                shared_dot += shared_part[:, at : at + lanes]
            store(cols, sg_ref[...] * shared + gate_ref[...] * picked)
        lane = lax.broadcasted_iota(jnp.int32, dots_ref.shape, 1)
        gate_dot = jnp.sum(gate_dot, axis=1, keepdims=True)
        shared_dot = jnp.sum(shared_dot, axis=1, keepdims=True)
        dots_ref[...] = jnp.where(lane == 0, gate_dot, jnp.where(lane == 1, shared_dot, 0.0))

    @pl.when(is_far)
    def _():
        def store(cols, total):
            given[slot, :, cols] = low(total)

        make(store)
        block_copy(slot).start()

    @pl.when(jnp.logical_not(is_far))
    def _():
        block_copy(slot).wait_recv()

        def store(cols, total):
            got[slot, :, cols] = low(total + got[slot, :, cols].astype(jnp.float32))

        make(store)

    everything = pl.ds(0, got.shape[1])
    pieces = [(k, everything, near_refs[k]) for k in range(half)]
    hand_out(step_at, half, got, pieces, out_sem)

    @pl.when(step_at == 2 * half - 1)
    def _():
        for k in range(half):
            block_copy(k).wait_send()


def output_parts(hidden, down, rows, slots, sg, gates, cot):
    blocks, capacity, width = rows.shape
    units, count = hidden.shape
    tokens, half = count // blocks, blocks // 2
    at = lambda i: lax.rem(i + half, blocks)
    column = pl.BlockSpec((tokens, 1), lambda i: (at(i), 0))
    return pl.pallas_call(
        partial(output_kernel, half),
        grid=(blocks,),
        in_specs=[
            pl.BlockSpec((units, tokens), lambda i: (0, at(i))),
            pl.BlockSpec((units, width), lambda i: (0, 0)),
            pl.BlockSpec((1, capacity, width), lambda i: (at(i), 0, 0)),
            column,
            column,
            column,
            pl.BlockSpec((tokens, width), lambda i: (at(i), 0)),
        ],
        out_specs=[
            *[pl.BlockSpec(memory_space=pl.ANY)] * half,
            pl.BlockSpec((tokens, 128), lambda i: (at(i), 0)),
        ],
        out_shape=[
            *[jax.ShapeDtypeStruct((tokens, width), jnp.bfloat16)] * half,
            jax.ShapeDtypeStruct((count, 128), jnp.float32),
        ],
        scratch_shapes=[
            pltpu.VMEM((half, tokens, width), jnp.bfloat16),
            pltpu.VMEM((half, tokens, width), jnp.bfloat16),
            pltpu.SemaphoreType.DMA((half,)),
            pltpu.SemaphoreType.DMA((half,)),
            pltpu.SemaphoreType.DMA((half,)),
        ],
        compiler_params=pltpu.CompilerParams(
            collective_id=4, has_side_effects=True, vmem_limit_bytes=56 * 2**20
        ),
        cost_estimate=pl.CostEstimate(
            flops=2 * count * width * (units + capacity),
            bytes_accessed=6 * count * width,
            transcendentals=0,
        ),
    )(hidden, down, rows, slots, sg, gates, cot)


def scatter_step(compute, out_ref, scratch):
    given, total, x_got, y_got, x_last, y_last, send_sem, recv_sem = scratch
    at, core, across, along, far = plane_places()
    step_at = pl.program_id(0)
    row = step_at // 2
    is_twin = step_at % 2 == 0
    rows = total.shape[1]
    half = rows // 2
    top, bottom = pl.ds(0, half), pl.ds(half, half)

    def copy_of(number, src, dst, target):
        return pltpu.make_async_remote_copy(
            src_ref=src,
            dst_ref=dst,
            send_sem=send_sem.at[number],
            recv_sem=recv_sem.at[number],
            device_id=target,
            device_id_type=MESH_ID,
        )

    def twin_copy(k):
        return copy_of(k, given.at[k % 2], total.at[k], {CTX: 1 - core})

    far_x = copy_of(4, total.at[0, top], x_got.at[0], {EXP: across})
    far_y = copy_of(5, total.at[0, bottom], y_got.at[0], {EXP: along})
    own_x = copy_of(6, total.at[1, top], x_got.at[1], {EXP: across})
    own_y = copy_of(7, total.at[2, bottom], y_got.at[1], {EXP: along})
    last_y = copy_of(8, total.at[2, top], y_last, {EXP: along})
    last_x = copy_of(9, total.at[1, bottom], x_last, {EXP: across})

    @pl.when(step_at == 0)
    def _():
        greet(across, along, core)

    @pl.when(is_twin)
    def _():
        @pl.when(row >= 2)
        def _():
            twin_copy(row - 2).wait_send()

        def store(cols, values):
            given[row % 2, :, cols] = low(values)

        compute(store)
        twin_copy(row).start()

    @pl.when(jnp.logical_not(is_twin))
    def _():
        twin_copy(row).wait_recv()

        def store(cols, values):
            total[row, :, cols] = low(values + total[row, :, cols].astype(jnp.float32))

        compute(store)

    @pl.when(step_at == 1)
    def _():
        far_x.start()
        far_y.start()

    @pl.when(step_at == 3)
    def _():
        own_x.start()

    @pl.when(step_at == 5)
    def _():
        own_y.start()

    @pl.when(step_at == 7)
    def _():
        def add_half(k, first, got):
            @pl.loop(0, half // 64)
            def _(i):
                take = pl.ds(pl.multiple_of(i * 64, 64), 64)
                into = pl.ds(pl.multiple_of(first + i * 64, 64), 64)
                total[k, into] = low(
                    total[k, into].astype(jnp.float32) + got[0, take].astype(jnp.float32)
                )

        def finish(first, near, later):
            @pl.loop(0, half // 64)
            def _(i):
                take = pl.ds(pl.multiple_of(i * 64, 64), 64)
                into = pl.ds(pl.multiple_of(first + i * 64, 64), 64)
                out_ref[into] = (
                    total[3, into].astype(jnp.float32)
                    + near[1, take].astype(jnp.float32)
                    + later[take].astype(jnp.float32)
                )

        far_x.wait_recv()
        add_half(2, 0, x_got)
        last_y.start()
        far_y.wait_recv()
        add_half(1, half, y_got)
        last_x.start()
        own_x.wait_recv()
        last_y.wait_recv()
        finish(0, x_got, y_last)
        own_y.wait_recv()
        last_x.wait_recv()
        finish(half, y_got, x_last)
        for copy in (twin_copy(2), twin_copy(3), far_x, far_y, own_x, own_y, last_y, last_x):
            copy.wait_send()


def step_slot(i):
    row = i // 2
    shift = jnp.where(row == 0, 3, jnp.where(row == 3, 0, row))
    return shift + 4 * (1 - i % 2)


def scatter_scratch(tokens, width):
    vmem = lambda *shape: pltpu.VMEM(shape, jnp.bfloat16)
    return [
        vmem(2, tokens, width),
        vmem(4, tokens, width),
        vmem(2, tokens // 2, width),
        vmem(2, tokens // 2, width),
        vmem(tokens // 2, width),
        vmem(tokens // 2, width),
        pltpu.SemaphoreType.DMA((10,)),
        pltpu.SemaphoreType.DMA((10,)),
    ]


def n2_grad_kernel(dgate_ref, dup_ref, gate_ref, up_ref, rows_ref, slot_ref, out_ref, *scratch):
    def compute(store):
        chosen = chosen_rows(slot_ref[...], rows_ref.shape[1])
        dgate, dup = dgate_ref[...].T, dup_ref[...].T
        step = 512
        for first in range(0, gate_ref.shape[1], step):
            cols = pl.ds(first, step)
            total = mm(dgate, gate_ref[:, cols]) + mm(dup, up_ref[:, cols])
            store(cols, total + mm(chosen, rows_ref[0, :, cols]))

    scatter_step(compute, out_ref, scratch)


def n2_grad_sum(dgate, dup, gate_w, up_w, rows, slots):
    blocks, capacity, width = rows.shape
    units, count = dgate.shape
    tokens = count // blocks
    by_units = pl.BlockSpec((units, tokens), lambda i: (0, step_slot(i)))
    whole = pl.BlockSpec((units, width), lambda i: (0, 0), pipeline_mode=pl.Buffered(1))
    return pl.pallas_call(
        n2_grad_kernel,
        grid=(blocks,),
        in_specs=[
            by_units,
            by_units,
            whole,
            whole,
            pl.BlockSpec((1, capacity, width), lambda i: (step_slot(i), 0, 0)),
            pl.BlockSpec((tokens, 1), lambda i: (step_slot(i), 0)),
        ],
        out_specs=pl.BlockSpec((tokens, width), lambda i: (0, 0)),
        out_shape=jax.ShapeDtypeStruct((tokens, width), jnp.float32),
        scratch_shapes=scatter_scratch(tokens, width),
        compiler_params=pltpu.CompilerParams(
            collective_id=3, has_side_effects=True, vmem_limit_bytes=56 * 2**20
        ),
        cost_estimate=pl.CostEstimate(
            flops=2 * count * width * (2 * units + capacity),
            bytes_accessed=4 * count * width,
            transcendentals=0,
        ),
    )(dgate, dup, gate_w, up_w, rows, slots)


def unit_grad_kernel(hid_ref, dgate_ref, dup_ref, cot_ref, n2_ref, out_ref):
    units = hid_ref.shape[0]
    out_ref[0, :units] = low(mm(hid_ref[...], cot_ref[...]))
    out_ref[0, units : 2 * units] = low(mm(dgate_ref[...], n2_ref[...]))
    out_ref[0, 2 * units :] = low(mm(dup_ref[...], n2_ref[...]))


def unit_grads(hidden, dgate, dup, cots, n2, depth, halves):
    units, count = hidden.shape
    width = n2.shape[1]
    cols = width // (depth * halves)
    whole = pl.BlockSpec((units, count), lambda i: (0, 0), pipeline_mode=pl.Buffered(1))
    strip = pl.BlockSpec((count, cols), lambda i: (0, i))
    return pl.pallas_call(
        unit_grad_kernel,
        grid=(depth * halves,),
        in_specs=[whole, whole, whole, strip, strip],
        out_specs=pl.BlockSpec(
            (1, 3 * units, cols), lambda i: (lax.rem(i, depth), 0, i // depth)
        ),
        out_shape=jax.ShapeDtypeStruct((depth, 3 * units, halves * cols), jnp.bfloat16),
        compiler_params=pltpu.CompilerParams(vmem_limit_bytes=48 * 2**20),
        cost_estimate=pl.CostEstimate(
            flops=6 * units * count * width,
            bytes_accessed=2 * (3 * units * count + 2 * count * width + 3 * units * width),
            transcendentals=0,
        ),
    )(hidden, dgate, dup, cots, n2)


def n1_grad_kernel(half, grads_ref, w_ref, *refs):
    near_refs, refs = refs[:half], refs[half:]
    rows_in, given, got, load_sem, send_sem, recv_sem, out_sem = refs
    place, core = lax.axis_index(EXP), lax.axis_index(CTX)
    step_at = pl.program_id(0)
    is_far = step_at < half
    slot = lax.rem(step_at, half)
    tokens = rows_in.shape[1]
    twin_id = {CTX: 1 - core}

    def load(step, k):
        column, level = place % 2, place // 2
        there = (column + k % 2) % 2 + 2 * ((level + k // 2) % 2)
        owner = 1 - core if step < half else core
        first = pl.multiple_of((there * 2 + owner) * tokens, tokens)
        return pltpu.make_async_copy(
            grads_ref.at[pl.ds(first, tokens)], rows_in.at[step], load_sem.at[step]
        )

    loads = [load(step, step % half) for step in range(2 * half)]

    @pl.when(step_at == 0)
    def _():
        for copy in loads:
            copy.start()
        barrier = pltpu.get_barrier_semaphore()
        pl.semaphore_signal(barrier, inc=1, device_id=twin_id, device_id_type=MESH_ID)
        pl.semaphore_wait(barrier, 1)

    for step in range(2 * half):

        @pl.when(step_at == step)
        def _():
            loads[step].wait()

    def block_copy(k):
        return pltpu.make_async_remote_copy(
            src_ref=given.at[k],
            dst_ref=got.at[k],
            send_sem=send_sem.at[k],
            recv_sem=recv_sem.at[k],
            device_id=twin_id,
            device_id_type=MESH_ID,
        )

    def make(store):
        step = 512
        for first in range(0, w_ref.shape[0], step):
            cols = pl.ds(first, step)
            store(cols, mm(rows_in[step_at], w_ref[cols, :], ((1,), (1,))))

    @pl.when(is_far)
    def _():
        def store(cols, total):
            given[slot, :, cols] = low(total)

        make(store)
        block_copy(slot).start()

    @pl.when(jnp.logical_not(is_far))
    def _():
        block_copy(slot).wait_recv()

        def store(cols, total):
            got[slot, :, cols] = low(total + got[slot, :, cols].astype(jnp.float32))

        make(store)

    own, x_send, y_send, rest = near_refs
    top, bottom = pl.ds(0, tokens // 2), pl.ds(tokens // 2, tokens // 2)
    pieces = [
        (0, pl.ds(0, tokens), own),
        (1, top, x_send.at[bottom]),
        (1, bottom, rest.at[bottom]),
        (2, top, rest.at[top]),
        (2, bottom, y_send.at[bottom]),
        (3, top, x_send.at[top]),
        (3, bottom, y_send.at[top]),
    ]
    hand_out(step_at, half, got, pieces, out_sem)

    @pl.when(step_at == 2 * half - 1)
    def _():
        for k in range(half):
            block_copy(k).wait_send()


def n1_grad_parts(grads, w, blocks):
    rows, cols = grads.shape
    width = w.shape[0]
    tokens, half = rows // blocks, blocks // 2
    return pl.pallas_call(
        partial(n1_grad_kernel, half),
        grid=(blocks,),
        in_specs=[
            pl.BlockSpec(memory_space=pl.ANY),
            pl.BlockSpec((width, cols), lambda i: (0, 0)),
        ],
        out_specs=[pl.BlockSpec(memory_space=pl.ANY)] * half,
        out_shape=[jax.ShapeDtypeStruct((tokens, width), jnp.bfloat16)] * half,
        scratch_shapes=[
            pltpu.VMEM((blocks, tokens, cols), jnp.bfloat16),
            pltpu.VMEM((half, tokens, width), jnp.bfloat16),
            pltpu.VMEM((half, tokens, width), jnp.bfloat16),
            pltpu.SemaphoreType.DMA((blocks,)),
            pltpu.SemaphoreType.DMA((half,)),
            pltpu.SemaphoreType.DMA((half,)),
            pltpu.SemaphoreType.DMA((7,)),
        ],
        compiler_params=pltpu.CompilerParams(
            collective_id=1, has_side_effects=True, vmem_limit_bytes=48 * 2**20
        ),
        cost_estimate=pl.CostEstimate(
            flops=2 * rows * width * cols,
            bytes_accessed=4 * rows * width,
            transcendentals=0,
        ),
    )(grads, w)


def after(values, others):
    return lax.optimization_barrier((values, others))[0]


def swap(values, bits):
    return lax.ppermute(values, EXP, [(i, i ^ bits) for i in range(4)])


def twin(values):
    return lax.ppermute(values, CTX, [(0, 1), (1, 0)])


def twin_sums(ours, theirs):
    got = twin(theirs)
    return [low(ours[k].astype(jnp.float32) + got[k].astype(jnp.float32)) for k in range(4)]


def hops(sums):
    return [sums[0]] + [swap(sums[k], k) for k in (1, 2, 3)]


def two_stage_sum(own, x_send, y_send, rest, between, later):
    half = own.shape[0] // 2
    wide = lambda v: v.astype(jnp.float32)
    x_got, y_got = after((swap(x_send, 1), swap(y_send, 2)), between)
    y_last = swap(low(wide(rest[:half]) + wide(x_got[:half])), 2)
    x_last = swap(low(wide(rest[half:]) + wide(y_got[:half])), 1)
    x_last, y_last = after((x_last, y_last), later)
    return jnp.concatenate(
        [
            wide(own[:half]) + wide(x_got[half:]) + wide(y_last),
            wide(own[half:]) + wide(y_got[half:]) + wide(x_last),
        ]
    )


def sum_up(parts):
    return sum(v.astype(jnp.float32) for v in parts)


def mm(left, right, dims=((1,), (0,))):
    return lax.dot_general(left, right, (dims, ((), ())), preferred_element_type=jnp.float32)


def low(values):
    return values.astype(jnp.bfloat16)


def local_plane(
    hidden,
    cotangent,
    segments,
    padding,
    routes,
    order,
    norm1_gain,
    w_query,
    w_key,
    w_value,
    w_out,
    norm2_gain,
    router,
    shared_gate_vec,
    shared_w_gate,
    shared_w_up,
    shared_w_down,
    expert_w_gate,
    expert_w_up,
    expert_w_down,
):
    plane = lax.axis_size(PLANE)
    groups = lax.axis_size(EXP)
    halves = lax.axis_size(CTX)
    depth = lax.axis_size(DP)
    me = lax.axis_index(PLANE)
    core = lax.axis_index(CTX)
    tokens, width = hidden.shape[1], hidden.shape[2]
    all_tokens = plane * tokens
    seq_len = halves * tokens
    experts_all = router.shape[1]
    head_cols = width // plane
    shard = width // depth

    token_info = jnp.concatenate(
        [segments + 1, jnp.where(padding > 0, segments + 1, 0), order[0], routes[0].T]
    )
    info_rows = token_info.shape[0]
    token_info = jnp.concatenate([token_info, jnp.zeros((8 - info_rows, tokens), jnp.int32)])

    hidden_all, info_all = plane_gather(hidden[0], token_info, False, 0)
    hidden_all = hidden_all.reshape(all_tokens, width)
    place = lax.axis_index(EXP)
    away = [(place ^ k) * 2 + (core ^ j) for j in (0, 1) for k in range(4)]
    away = jnp.stack(away)
    out_rows = shard // plane
    w_out_part = lax.dynamic_slice(w_out, (me * out_rows, 0), (out_rows, width))
    w_qkv_part = jnp.concatenate(
        [
            lax.dynamic_slice(w, (0, me * head_cols), (shard, head_cols))
            for w in (w_query, w_key, w_value)
        ]
        + [router, norm1_gain[:, None], norm2_gain[:, None], shared_gate_vec[:, None]]
        + [jnp.zeros((shard, 128 - experts_all - 3), jnp.bfloat16)]
        + [w_out_part.reshape(shard, -1)],
        axis=1,
    )
    w_qkv = lax.all_gather(w_qkv_part, DP, axis=0, tiled=True)
    w_out_part = w_qkv[:, 3 * head_cols + 128 :].reshape(depth, out_rows, width)
    small = w_qkv[:, 3 * head_cols : 3 * head_cols + 128].T
    w_qkv = w_qkv[:, : 3 * head_cols]
    router_t = small[:experts_all]
    g_one = small[experts_all].astype(jnp.float32)
    g_two = small[experts_all + 1].astype(jnp.float32)
    gate_vec = small[experts_all + 2]
    w_out_part = after(w_out_part, info_all)
    w_out_got = [swap(w_out_part, k) for k in (1, 2, 3)]

    def normed(values, gain):
        values = values.astype(jnp.float32)
        inv = lax.rsqrt(jnp.mean(values * values, axis=1, keepdims=True) + EPS)
        return values, inv, low(values * inv * gain)

    n1_all, qkv = norm_qkv(hidden_all, g_one[None], w_qkv, tokens)
    q_codes = info_all[:, 0].reshape(all_tokens, 1)
    k_codes = info_all[:, 1].reshape(all_tokens // seq_len, 1, seq_len)
    attended_cols = attention_call(qkv, None, q_codes, k_codes, seq_len)
    pieces = [w_out_part] + [after(v, attended_cols) for v in w_out_got]
    w_out_near = jnp.zeros((depth, groups, 1, out_rows, width), jnp.bfloat16)
    for k in range(4):
        w_out_near = lax.dynamic_update_slice(
            w_out_near, pieces[k][:, None, None], (0, place ^ k, 0, 0, 0)
        )
    w_out_far = twin(w_out_near)
    w_out_full = jnp.where(
        core == 0,
        jnp.concatenate([w_out_near, w_out_far], axis=2),
        jnp.concatenate([w_out_far, w_out_near], axis=2),
    ).reshape(width, width)

    x_rows, inv_one, _ = normed(hidden[0], g_one)
    cot_rows = cotangent[0].astype(jnp.float32)

    def to_tokens(cols):
        got = lax.all_to_all(
            cols.reshape(plane, tokens, head_cols), PLANE, split_axis=0, concat_axis=0, tiled=True
        )
        return got.transpose(1, 0, 2).reshape(tokens, width)

    def to_columns(rows_in):
        send = rows_in.reshape(tokens, plane, head_cols).transpose(1, 0, 2)
        got = lax.all_to_all(send, PLANE, split_axis=0, concat_axis=0, tiled=True)
        return got.reshape(all_tokens, head_cols)

    attended = to_tokens(attended_cols)
    residual = x_rows + mm(attended, w_out_full)
    residual, inv_two, n2 = normed(residual, g_two)

    units = shared_w_gate.shape[1]
    part = units // (depth * halves)
    pick = lambda w: lax.dynamic_index_in_dim(
        w.reshape(w.shape[0], depth, halves, part), core, axis=2, keepdims=False
    ).reshape(w.shape[0], depth * part)
    sh_gate_up = jnp.concatenate([pick(shared_w_gate), pick(shared_w_up)], axis=1)
    sh_gate_up = lax.all_gather(sh_gate_up, DP, axis=0, tiled=True)
    sh_gate_t, sh_up_t = sh_gate_up[:, : depth * part].T, sh_gate_up[:, depth * part :].T
    sh_down = lax.all_gather(
        lax.dynamic_slice(shared_w_down, (core * part, 0), (part, width)), DP, axis=0, tiled=True
    )
    n2 = after(n2, sh_gate_up)
    n2_all = plane_gather(n2, None, True, 2)[0].reshape(all_tokens, width)
    cot_own = after(cotangent[0], n2_all)
    cot_got = [swap(cot_own, k) for k in (1, 2, 3)]
    ex_gate = lax.all_gather(after(expert_w_gate[0], info_all), DP, axis=0, tiled=True)
    ex_up = lax.all_gather(after(expert_w_up[0], info_all), DP, axis=0, tiled=True)
    ex_down = lax.all_gather(after(expert_w_down[0], info_all), DP, axis=1, tiled=True)

    small_w = jnp.concatenate([router_t, gate_vec[None]])

    def gates_of(rows_in):
        both = mm(rows_in, small_w, ((1,), (1,)))
        z = both[:, :experts_all]
        e = jnp.exp(z - jnp.max(z, axis=1, keepdims=True))
        return e / jnp.sum(e, axis=1, keepdims=True), jax.nn.sigmoid(both[:, experts_all:])

    probs_all, sg_all = gates_of(n2_all)
    expert_gate = lax.dynamic_slice(probs_all, (0, me), (all_tokens, 1))

    capacity = (9 * tokens * TOP + 8 * experts_all - 1) // (8 * experts_all)
    info_away = info_all[away]
    order_all = info_away[:, 2]
    routed_here = jnp.any(info_away[:, 3 : 3 + TOP] == me, axis=1)
    earlier = (order_all[:, None, :] < order_all[:, :, None]) & routed_here[:, None, :]
    slots = jnp.sum(earlier.astype(jnp.int32), axis=2)
    slots = jnp.where(routed_here, slots, capacity)
    chosen = slots[:, None, :] == jnp.arange(capacity, dtype=jnp.int32)[None, :, None]
    onehot = chosen.astype(jnp.bfloat16)

    def rows_of(values):
        got = lax.dot_general(
            onehot,
            values.reshape(plane, tokens, width),
            (((2,), (1,)), ((0,), (0,))),
            preferred_element_type=jnp.float32,
        )
        return got.reshape(plane * capacity, width)

    slot_gates = jnp.sum(
        jnp.where(chosen, expert_gate.reshape(plane, 1, tokens), 0.0), axis=2
    ).reshape(plane * capacity, 1)
    expert_rows = low(rows_of(n2_all))
    gate_pre = mm(sh_gate_t, n2_all, ((1,), (1,)))
    up_pre = mm(sh_up_t, n2_all, ((1,), (1,)))
    gate_act = gate_pre * jax.nn.sigmoid(gate_pre)
    shared_hidden = low(gate_act * up_pre)
    expert_rows = after(expert_rows, (shared_hidden, sh_down))
    gate_e = mm(expert_rows, ex_gate)
    up_e = mm(expert_rows, ex_up)
    act_e = gate_e * jax.nn.sigmoid(gate_e)
    hidden_e = low(act_e * up_e)
    cot_near = jnp.concatenate([cot_own] + [after(v, gate_e) for v in cot_got])
    cot_all = jnp.concatenate([cot_near, twin(cot_near)])
    row_cots = low(rows_of(cot_all))
    row_grads = low(row_cots.astype(jnp.float32) * slot_gates)

    shared_grads = low(sg_all * cot_all.astype(jnp.float32))
    shared_hgrad = mm(sh_down, shared_grads, ((1,), (1,)))
    gate_grad_s = low(shared_hgrad * up_pre * silu_grad(gate_pre))
    up_grad_s = low(shared_hgrad * gate_act)
    rows_out = width // (halves * depth)

    def shared_scatter(total):
        first, second = total[:, :, :rows_out], total[:, :, rows_out:]
        keep = jnp.where(core == 0, first, second)
        got = twin(jnp.where(core == 0, second, first))
        both = [v.reshape(3, depth, part, rows_out) for v in (keep, got)]
        both = jnp.where(core == 0, jnp.stack(both, axis=2), jnp.stack(both[::-1], axis=2))
        return both.reshape(3, units, rows_out).astype(jnp.float32)

    scatter = lambda v, dim: lax.psum_scatter(v, DP, scatter_dimension=dim, tiled=True)
    shared_sums = unit_grads(
        shared_hidden, gate_grad_s, up_grad_s, shared_grads, n2_all, depth, halves
    )
    shared_sums = scatter(shared_sums.reshape(3 * depth * depth * part, -1), 0)
    result_e = low(mm(hidden_e, ex_down))
    hgrad_e = mm(row_grads, ex_down, ((1,), (1,)))
    gate_grad_e = low(hgrad_e * up_e * silu_grad(gate_e))
    up_grad_e = low(hgrad_e * act_e)

    grad_ex_down = low(mm(hidden_e, row_grads, ((0,), (0,))))
    slots = slots.reshape(all_tokens, 1)
    *out_near, dots = output_parts(
        shared_hidden,
        sh_down,
        result_e.reshape(plane, capacity, width),
        slots,
        sg_all,
        expert_gate,
        cot_all,
    )
    expert_rows = after(expert_rows, out_near)
    grad_ex_gate = low(mm(expert_rows, gate_grad_e, ((0,), (0,))))
    grad_ex_up = low(mm(expert_rows, up_grad_e, ((0,), (0,))))
    grads_made = (grad_ex_down, grad_ex_gate, grad_ex_up)
    grads = [scatter(v, dim) for v, dim in zip(grads_made, (1, 0, 0))]
    rows_grad = low(
        mm(gate_grad_e, ex_gate, ((1,), (1,))) + mm(up_grad_e, ex_up, ((1,), (1,)))
    )

    out_got = hops(out_near)
    slots, out_got, _ = lax.optimization_barrier((slots, out_got, (shared_sums, grads_made)))
    n2_grad = n2_grad_sum(
        gate_grad_s,
        up_grad_s,
        sh_gate_t,
        sh_up_t,
        rows_grad.reshape(plane, capacity, width),
        slots,
    )

    dots = dots.reshape(plane, tokens, 128)[:, :, :2].transpose(0, 2, 1)
    back = jnp.arange(plane, dtype=jnp.int32) ^ me
    dots = dots[(back // 2) + 4 * (back % 2)]
    dots = lax.all_to_all(dots, PLANE, split_axis=0, concat_axis=0, tiled=True)
    probs_grad = dots[:, 0].T
    probs, sg = gates_of(n2)
    logit_grad = low(probs * (probs_grad - jnp.sum(probs * probs_grad, axis=1, keepdims=True)))
    sg_logit_grad = low(jnp.sum(dots[:, 1], axis=0)[:, None] * sg * (1.0 - sg))
    n2_grad = (
        n2_grad
        + mm(logit_grad, router_t)
        + sg_logit_grad.astype(jnp.float32) * gate_vec.astype(jnp.float32)[None]
    )
    residual_grad, grad_gain_two = norm_back(residual, inv_two, g_two, n2_grad)
    residual_grad = residual_grad + cot_rows
    low_residual = low(residual_grad)

    attended_grad = low(mm(low_residual, w_out_full, ((1,), (1,))))
    low_residual = after(low_residual, attended_grad)
    output = low(residual + sum_up(after(out_got, attended_grad)))
    attended_grad = to_columns(attended_grad)
    grad_out = low(mm(attended, low_residual, ((0,), (0,))))
    grad_out = grad_out.reshape(groups, halves, width // plane, width)
    block_of = lambda k, c: lax.dynamic_slice(
        grad_out, (place ^ k, c, 0, 0), (1, 1, width // plane, width)
    )[0, 0]
    out_grad_sums = twin_sums(
        [block_of(k, core) for k in range(4)],
        jnp.stack([block_of(k, 1 - core) for k in range(4)]),
    )
    dz_all = jnp.concatenate([logit_grad, sg_logit_grad], axis=1)
    dz_all = after(dz_all, out_grad_sums)
    small_grads = mm(n2, dz_all, ((0,), (0,)))
    small_grads = jnp.concatenate([small_grads, grad_gain_two[:, None]], axis=1).T
    small_grads = jnp.pad(small_grads, ((0, 14 - experts_all), (0, 0)))
    small_grads = small_grads.reshape(16, plane, width // plane).transpose(1, 0, 2)
    attended_grad, small_grads = lax.optimization_barrier((attended_grad, small_grads))
    attended_grad = after(attended_grad, (out_grad_sums, output, grads[0]))
    qkv_grad = attention_call(qkv, attended_grad, q_codes, k_codes, seq_len)
    out_grad_got = hops(out_grad_sums)
    qkv_grad, out_grad_got = lax.optimization_barrier((qkv_grad, out_grad_got))
    small_grads = after(small_grads, qkv_grad)
    small_grads = jnp.sum(
        lax.all_to_all(small_grads, PLANE, split_axis=0, concat_axis=0, tiled=True), axis=0
    )
    grad_qkv = low(mm(n1_all, qkv_grad, ((0,), (0,))))
    fine = shard // plane
    grad_qkv = (
        grad_qkv.reshape(plane, depth, fine, 3 * head_cols)
        .transpose(1, 0, 2, 3)
        .reshape(width, 3 * head_cols)
    )
    qkv_grad, small_grads, _ = lax.optimization_barrier(
        (qkv_grad, small_grads, (grad_qkv, grads[1]))
    )
    n1_near = n1_grad_parts(qkv_grad, w_qkv, plane)
    grad_out = low(sum_up(out_grad_got))
    grad_qkv = lax.psum_scatter(grad_qkv, DP, scatter_dimension=0, tiled=True)
    qkv_sum = grad_qkv
    w_rows = (
        w_qkv.reshape(plane, depth, fine, 3 * head_cols)
        .transpose(1, 0, 2, 3)
        .reshape(depth, plane * fine, 3 * head_cols)
    )
    w_rows = lax.dynamic_index_in_dim(w_rows, lax.axis_index(DP), axis=0, keepdims=False)
    gain_dots = jnp.sum(grad_qkv.astype(jnp.float32) * w_rows.astype(jnp.float32), axis=1)
    my_gain = lax.dynamic_slice(
        g_one, ((me * depth + lax.axis_index(DP)) * fine,), (fine,)
    )
    gain_dots = jnp.broadcast_to(low(gain_dots).reshape(plane, fine, 1), (plane, fine, 128))
    grad_qkv = lax.all_to_all(
        jnp.concatenate([grad_qkv.reshape(plane, fine, 3 * head_cols), gain_dots], axis=2),
        PLANE,
        split_axis=0,
        concat_axis=0,
        tiled=True,
    )
    gain_dots = grad_qkv[:, :, 3 * head_cols].astype(jnp.float32)
    grad_gain_one = jnp.sum(gain_dots, axis=0) / my_gain
    grad_qkv = (
        grad_qkv[:, :, : 3 * head_cols]
        .reshape(plane, fine, 3, head_cols)
        .transpose(2, 1, 0, 3)
        .reshape(3, fine, width)
        .astype(jnp.float32)
    )
    grad_ex_down, grad_ex_gate, grad_ex_up = [
        v.astype(jnp.float32)[None] for v in after(grads, n1_near)
    ]
    grad_out = scatter(after(grad_out, qkv_sum), 0).astype(jnp.float32)
    shared_sums = after(shared_sums, n1_near)
    shared_sums = shared_scatter(shared_sums.reshape(3, units // halves, -1))
    grad_sh_down, grad_sh_gate, grad_sh_up = [shared_sums[k] for k in range(3)]
    grad_sh_gate, grad_sh_up = grad_sh_gate.T, grad_sh_up.T
    small_grads = after(small_grads, n1_near)
    small_grads = small_grads.reshape(16, depth, shard // plane).transpose(1, 0, 2)
    small_grads = jnp.sum(
        lax.all_to_all(small_grads, DP, split_axis=0, concat_axis=0, tiled=True), axis=0
    )
    n1_grad = two_stage_sum(*n1_near, qkv_sum, grad_qkv)
    input_part, _ = norm_back(x_rows, inv_one, g_one, n1_grad)
    input_grad = low(residual_grad + input_part)
    return (
        output[None],
        input_grad[None],
        grad_gain_one,
        grad_qkv[0],
        grad_qkv[1],
        grad_qkv[2],
        grad_out,
        small_grads[experts_all + 1],
        small_grads[:experts_all].T,
        small_grads[experts_all],
        grad_sh_gate,
        grad_sh_up,
        grad_sh_down,
        grad_ex_gate,
        grad_ex_up,
        grad_ex_down,
    )


def solution(mesh):
    in_specs = (
        P((EXP, DP), CTX, None),
        P((EXP, DP), CTX, None),
        P((EXP, DP), CTX),
        P((EXP, DP), CTX),
        P((EXP, DP), CTX, None),
        P((EXP, DP), CTX, None),
        P(DP),
        P(DP, None),
        P(DP, None),
        P(DP, None),
        P(DP, None),
        P(DP),
        P(DP, None),
        P(DP),
        P(DP, EXP),
        P(DP, EXP),
        P((EXP, DP), None),
        P((EXP, CTX), DP, None),
        P((EXP, CTX), DP, None),
        P((EXP, CTX), None, DP),
    )
    out_specs = (
        P((EXP, DP), CTX, None),
        P((EXP, DP), CTX, None),
        P((EXP, CTX, DP)),
        P((EXP, CTX, DP), None),
        P((EXP, CTX, DP), None),
        P((EXP, CTX, DP), None),
        P((EXP, CTX, DP), None),
        P((EXP, CTX, DP)),
        P((EXP, CTX, DP), None),
        P((EXP, CTX, DP)),
        P((CTX, DP), EXP),
        P((CTX, DP), EXP),
        P(EXP, (CTX, DP)),
        P((EXP, CTX), DP, None),
        P((EXP, CTX), DP, None),
        P((EXP, CTX), None, DP),
    )
    plane = mesh.shape[EXP] * mesh.shape[CTX]

    def run(*args):
        square = mesh.shape[EXP] == 4 and mesh.shape[CTX] == 2 and mesh.shape[DP] == 4
        one_each = square and args[12].shape[1] == plane
        local = local_plane if one_each else local_general
        return jax.shard_map(
            local, mesh=mesh, in_specs=in_specs, out_specs=out_specs, check_vma=False
        )(*args)

    return run
```
